128 devices in a mesh: dp: 64 (over y, z_hi, x, core), tensor: 2 (over z_lo).
Axes of the slice: x: 4, y: 4, z: 4 (z_hi: 2, z_lo: 2; z = z_hi * 2 + z_lo), core: 2. Of those that a mesh axis runs over, the one named last changes fastest.
Arguments:
- layer_input: bfloat16 [32768, 1024], P('dp'), may hold values from -6 to 6
- segments: int32 [64, 512], P('dp'), may hold values from 0 to 3, never falling along the last dimension, each value on 1 to 256 neighbouring positions
- input_gain: float32 [1024], replicated, may hold values from 0.5 to 1.5
- mixer_proj: bfloat16 [1024, 2, 1536], P(None, None, 'tensor'), may hold values from -0.1875 to 0.1875
- state_proj: bfloat16 [1024, 256], replicated, may hold values from -0.1875 to 0.1875
- step_proj: bfloat16 [1024, 24], P(None, 'tensor'), may hold values from -0.1875 to 0.1875
- step_bias: float32 [24], P('tensor'), may hold values from -3 to -0.5
- decay_log: float32 [24], P('tensor'), may hold values from -6 to -1.5
- skip_gain: float32 [24], P('tensor'), may hold values from 0.5 to 1.5
- conv_kernel: float32 [4, 1536], P(None, 'tensor'), may hold values from -3 to 3
- conv_bias: float32 [1536], P('tensor'), may hold values from -3 to 3
- state_kernel: float32 [4, 256], replicated, may hold values from -3 to 3
- state_bias: float32 [256], replicated, may hold values from -3 to 3
- gated_gain: float32 [1536], P('tensor'), may hold values from 0.5 to 1.5
- mixer_out: bfloat16 [1536, 1024], P('tensor'), may hold values from -0.15625 to 0.15625
- query_proj: bfloat16 [1024, 512], P(None, 'tensor'), may hold values from -0.1875 to 0.1875
- key_value_weight: bfloat16 [1024, 2, 128], P(None, 'tensor'), may hold values from -0.1875 to 0.1875
- attn_out: bfloat16 [512, 1024], P('tensor'), may hold values from -0.75 to 0.75
- ffn_gain: float32 [1024], replicated, may hold values from 0.5 to 1.5
- ffn_gate: bfloat16 [1024, 2048], P(None, 'tensor'), may hold values from -0.1875 to 0.1875
- ffn_up: bfloat16 [1024, 2048], P(None, 'tensor'), may hold values from -0.1875 to 0.1875
- ffn_down: bfloat16 [2048, 1024], P('tensor'), may hold values from -0.125 to 0.125
- cotangent: bfloat16 [32768, 1024], P('dp'), may hold values from -6 to 6
Outputs:
- layer_output: bfloat16 [32768, 1024], P('dp')
- input_grad: float32 [32768, 1024], P('dp')
- grad_input_gain: float32 [1024], replicated
- grad_mixer_proj: float32 [1024, 2, 1536], P(None, None, 'tensor')
- grad_state_proj: float32 [1024, 256], replicated
- grad_step_proj: float32 [1024, 24], P(None, 'tensor')
- grad_step_bias: float32 [24], P('tensor')
- grad_decay_log: float32 [24], P('tensor')
- grad_skip_gain: float32 [24], P('tensor')
- grad_conv_kernel: float32 [4, 1536], P(None, 'tensor')
- grad_conv_bias: float32 [1536], P('tensor')
- grad_state_kernel: float32 [4, 256], replicated
- grad_state_bias: float32 [256], replicated
- grad_gated_gain: float32 [1536], P('tensor')
- grad_mixer_out: float32 [1536, 1024], P('tensor')
- grad_query_proj: float32 [1024, 512], P(None, 'tensor')
- grad_keyval_proj: float32 [1024, 2, 128], P(None, 'tensor')
- grad_attn_out: float32 [512, 1024], P('tensor')
- grad_ffn_gain: float32 [1024], replicated
- grad_ffn_gate: float32 [1024, 2048], P(None, 'tensor')
- grad_ffn_up: float32 [1024, 2048], P(None, 'tensor')
- grad_ffn_down: float32 [2048, 1024], P('tensor')
The draws below stay inside these ranges and needn't reach their ends.
Inputs may be any that keep to these rules, and one draw needn't show every extreme that they name: `segments`: along each row the numbers never fall; each number names one document of at most half of 512 tokens.
All inputs are finite; a program needn't handle non-finite values.
Results may differ from the reference program's by a relative error of at most 0.013.
Values sent between devices are 32-bit elements; how exact they have to be, the bound alone decides.
No kernel may reach another device: no remote copies, remote signals or barrier semaphores. Data moves between devices by JAX's collectives and lax.ppermute only.
A program may use at most 192 MiB of HBM per device.

```python
import math
import jax
import jax.numpy as jnp
import numpy as np
from jax import lax

MODEL_DIM = 1024
FF = 2048
QUERY_HEAD_COUNT = 8
KEY_VALUE_HEADS = 2
HEAD_DIM = 64
MH = 24
MD = 64
NST = 128
KCONV = 4
DSSM = 1536
SEQ = 512
SEQS = 64
TOKENS = 32768


def block_scale(own_key, dims, shards, smallest, largest):
    loudness = 1.0
    for axis_at, blocks in shards:
        draws = jax.random.uniform(jax.random.fold_in(jax.random.fold_in(own_key, 6), axis_at), (blocks,), jnp.float32, smallest / len(shards), largest / len(shards))
        loudness = loudness * jnp.repeat(jnp.exp(draws), dims[axis_at] // blocks).reshape((-1,) + (1,) * (len(dims) - 1 - axis_at))
    return loudness


def split_up(number_of, total, most, skew):
    weights = [(1 << 20) // math.isqrt(grade ** skew) + 1 for grade in range(2, number_of + 1)]
    surplus, counts = total - most - (number_of - 1), [1] * (number_of - 1)
    while surplus > 0:
        free = [i for i in range(number_of - 1) if counts[i] < most]
        whole, budget = sum([weights[i] for i in free]), surplus
        for i in free:
            extra = min(most - counts[i], max(1, budget * weights[i] // whole), surplus)
            counts[i] = counts[i] + extra
            surplus = surplus - extra
    return np.array([most] + counts)


def uneven(stream_key, count, total, reach, skew):
    if count == 2:
        one = jax.random.randint(stream_key, (), max(1, total - reach), min(reach, total - 1) + 1)
        return jnp.stack([one, total - one])
    sizes = jnp.asarray(split_up(count, total, reach, skew), jnp.int32)
    twos = (count - 1) // 2
    source_of, receiver = sizes[1:1 + 2 * twos:2], sizes[2:2 + 2 * twos:2]
    room = jnp.minimum(source_of - 1, reach - receiver)
    shifted = jax.random.randint(jax.random.fold_in(stream_key, 1), (twos,), 0, 1 << 20) % (room + 1)
    sizes = sizes.at[1:1 + 2 * twos:2].set(source_of - shifted).at[2:2 + 2 * twos:2].set(receiver + shifted)
    return sizes[jax.random.permutation(jax.random.fold_in(stream_key, 2), count)]


def gaussian(key, shape, scale, reach, cuts=(), held_as=jnp.bfloat16):
    level = block_scale(key, shape, cuts, -0.22, 0.18) if cuts else 1.0
    result = jax.random.normal(key, shape, jnp.float32) * scale * level
    return jnp.minimum(jnp.maximum(result, -reach), reach).astype(held_as)


def setup_inputs(seed: int = 0) -> dict:
    key_list = jax.random.split(jax.random.key(seed), 24)
    return {
        "layer_input": gaussian(key_list[0], (TOKENS, MODEL_DIM), 1.0, 6.0, ((0, 64),)),
        "segments": jax.vmap(lambda own: jnp.searchsorted(jnp.cumsum(uneven(own, 4, SEQ, SEQ // 2, 0)), jnp.arange(SEQ), side="right"))(jax.random.split(key_list[1], SEQS)).reshape((SEQS, SEQ)).astype(jnp.int32),
        "input_gain": jnp.clip(1.0 + 0.1 * jax.random.normal(key_list[2], (MODEL_DIM,), jnp.float32), 0.5, 1.5),
        "mixer_proj": gaussian(key_list[3], (MODEL_DIM, 2, DSSM), MODEL_DIM ** -0.5, 0.1875, ((2, 2),)),
        "state_proj": gaussian(key_list[4], (MODEL_DIM, 2 * NST), MODEL_DIM ** -0.5, 0.1875),
        "step_proj": gaussian(key_list[5], (MODEL_DIM, MH), MODEL_DIM ** -0.5, 0.1875, ((1, 2),)),
        "step_bias": jnp.clip(-3.0 + 2.5 * jax.random.uniform(key_list[6], (MH,), jnp.float32) ** block_scale(key_list[6], (MH,), ((0, 2),), -0.2, 0.2), -3.0, -0.5),
        "decay_log": jnp.clip(-6.0 + 4.5 * jax.random.uniform(key_list[7], (MH,), jnp.float32) ** block_scale(key_list[7], (MH,), ((0, 2),), -0.2, 0.2), -6.0, -1.5),
        "skip_gain": jnp.clip(0.5 + 1.0 * jax.random.uniform(key_list[8], (MH,), jnp.float32) ** block_scale(key_list[8], (MH,), ((0, 2),), -0.2, 0.2), 0.5, 1.5),
        "conv_kernel": gaussian(key_list[9], (KCONV, DSSM), KCONV ** -0.5, 3.0, ((1, 2),), jnp.float32),
        "conv_bias": gaussian(key_list[10], (DSSM,), 0.5, 3.0, ((0, 2),), jnp.float32),
        "state_kernel": gaussian(key_list[11], (KCONV, 2 * NST), KCONV ** -0.5, 3.0, (), jnp.float32),
        "state_bias": gaussian(key_list[12], (2 * NST,), 0.5, 3.0, (), jnp.float32),
        "gated_gain": jnp.clip(1.0 + 0.1 * jax.random.normal(key_list[13], (DSSM,), jnp.float32), 0.5, 1.5),
        "mixer_out": gaussian(key_list[14], (DSSM, MODEL_DIM), DSSM ** -0.5, 0.15625, ((0, 2),)),
        "query_proj": gaussian(key_list[15], (MODEL_DIM, QUERY_HEAD_COUNT * HEAD_DIM), MODEL_DIM ** -0.5, 0.1875, ((1, 2),)),
        "key_value_weight": gaussian(key_list[16], (MODEL_DIM, KEY_VALUE_HEADS, 2 * HEAD_DIM), MODEL_DIM ** -0.5, 0.1875, ((1, 2),)),
        "attn_out": gaussian(key_list[17], (QUERY_HEAD_COUNT * HEAD_DIM, MODEL_DIM), (QUERY_HEAD_COUNT * HEAD_DIM // 8) ** -0.5, 0.75, ((0, 2),)),
        "ffn_gain": jnp.clip(1.0 + 0.1 * jax.random.normal(key_list[18], (MODEL_DIM,), jnp.float32), 0.5, 1.5),
        "ffn_gate": gaussian(key_list[19], (MODEL_DIM, FF), MODEL_DIM ** -0.5, 0.1875, ((1, 2),)),
        "ffn_up": gaussian(key_list[20], (MODEL_DIM, FF), MODEL_DIM ** -0.5, 0.1875, ((1, 2),)),
        "ffn_down": gaussian(key_list[21], (FF, MODEL_DIM), FF ** -0.5, 0.125, ((0, 2),)),
        "cotangent": gaussian(key_list[22], (TOKENS, MODEL_DIM), 1.0, 6.0, ((0, 64),)),
    }


norm_eps = 1e-05
rope_base = 10000.0
masked_score = -1e+30
highest = lax.Precision.HIGHEST

@jax.custom_vjp
def low(v):
    return lax.optimization_barrier(v.astype(jnp.bfloat16)).astype(jnp.float32)

@jax.custom_vjp
def reduced_backward(v):
    return v

def low_keep(v):
    return (low(v), None)

def low_pass(kept, grad):
    return (grad,)

def back_keep(v):
    return (v, None)

def back_low(kept, grad):
    return (low(grad),)
low.defvjp(low_keep, low_pass)
reduced_backward.defvjp(back_keep, back_low)

def matrix_product(left, right):
    return jnp.dot(left, right, precision=highest)

def rms_norm(argument, gain):
    inv_rms = lax.rsqrt(lax.optimization_barrier(jnp.mean(argument * argument, axis=-1, keepdims=True)) + norm_eps)
    return argument * inv_rms * gain

def rope_tables(document_length, head_size):
    half_size = head_size // 2
    inverse = rope_base ** (-(2.0 * jnp.arange(half_size, dtype=jnp.float32)) / head_size)
    angles = jnp.arange(document_length, dtype=jnp.float32)[:, None] * inverse[None, :]
    return (jnp.cos(angles)[:, None, :], jnp.sin(angles)[:, None, :])

def rotate(argument, cosine, sine):
    half_size = argument.shape[-1] // 2
    first_half = argument[..., :half_size]
    second_half = argument[..., half_size:]
    return jnp.concatenate([first_half * cosine - second_half * sine, second_half * cosine + first_half * sine], axis=-1)

def shift_down(values, offset):
    return jnp.concatenate([jnp.zeros((offset, values.shape[1]), values.dtype), values[:-offset]], axis=0)

def lag_keep(segment, offset, dtype):
    previous = jnp.concatenate([jnp.full((offset,), -1, jnp.int32), segment[:-offset]])
    return (previous == segment).astype(dtype)[:, None]

def conv_forward(values, kernel, conv_shift, segment):
    tap_count = kernel.shape[0]
    summed = conv_shift[None, :] + kernel[tap_count - 1][None, :] * values
    for offset in range(1, tap_count):
        summed = summed + kernel[tap_count - 1 - offset][None, :] * shift_down(values, offset) * lag_keep(segment, offset, values.dtype)
    return summed

def decay_weights(step_size, decay_rate, segment):
    document_length = step_size.shape[0]
    cumulative = jnp.cumsum(step_size * decay_rate[None, :], axis=0).T
    positions = jnp.arange(document_length)
    allowed = (positions[:, None] >= positions[None, :]) & (segment[:, None] == segment[None, :])
    spread = cumulative[:, :, None] - cumulative[:, None, :]
    return jnp.where(allowed[None], jnp.exp(jnp.where(allowed[None], spread, 0.0)), 0.0)

def attention(query_matrix, key_rows, value_rows, segment):
    document_length = query_matrix.shape[0]
    group_width = QUERY_HEAD_COUNT // KEY_VALUE_HEADS
    grouped_rows = query_matrix.reshape(document_length, KEY_VALUE_HEADS, group_width, HEAD_DIM)
    scores = reduced_backward(jnp.einsum('tkgd,skd->kgts', grouped_rows, key_rows, precision=highest) * HEAD_DIM ** (-0.5))
    positions = jnp.arange(document_length)
    allowed = (positions[:, None] >= positions[None, :]) & (segment[:, None] == segment[None, :])
    scores = jnp.where(allowed[None, None], scores, masked_score)
    row_max = lax.optimization_barrier(jnp.max(scores, axis=-1, keepdims=True))
    weights = jnp.exp(scores - row_max)
    weights = low(weights / lax.optimization_barrier(jnp.sum(weights, axis=-1, keepdims=True)))
    attended = jnp.einsum('kgts,skd->tkgd', weights, value_rows, precision=highest)
    return attended.reshape(document_length, QUERY_HEAD_COUNT * HEAD_DIM)

def layer(tokens, segment, params):
    input_gain, mixer_proj, state_proj, step_proj, step_bias, decay_log, skip_gain, conv_kernel, conv_bias, state_kernel, state_bias, gated_gain, mixer_out, query_proj, key_value_weight, attn_out, ffn_gain, ffn_gate, ffn_up, ffn_down = params
    document_length = tokens.shape[0]
    normed_input = low(rms_norm(tokens, input_gain))
    gate_input = reduced_backward(matrix_product(normed_input, mixer_proj.reshape(MODEL_DIM, 2 * DSSM)))
    gate_branch = gate_input[:, :DSSM]
    conv_in = gate_input[:, DSSM:]
    state_in = reduced_backward(matrix_product(normed_input, state_proj))
    step_raw = reduced_backward(matrix_product(normed_input, step_proj))
    conv_out = jax.nn.silu(conv_forward(conv_in, conv_kernel, conv_bias, segment))
    state_conv = jax.nn.silu(conv_forward(state_in, state_kernel, state_bias, segment))
    in_state = state_conv[:, :NST]
    out_state = state_conv[:, NST:]
    step_size = jax.nn.softplus(step_raw + step_bias)
    decay_rate = -jnp.exp(decay_log)
    heads_in = conv_out.reshape(document_length, MH, MD)
    decay_mat = decay_weights(step_size, decay_rate, segment)
    intersection = matrix_product(out_state, in_state.T)
    mixing = decay_mat * intersection[None]
    scan_heads = jnp.einsum('hts,shd->thd', mixing, heads_in * step_size[:, :, None], precision=highest)
    scan_out = (scan_heads + skip_gain[None, :, None] * heads_in).reshape(document_length, DSSM)
    gated = scan_out * jax.nn.silu(gate_branch)
    mixer_rows = low(rms_norm(gated, gated_gain))
    cosine, sine = rope_tables(document_length, HEAD_DIM)
    query_matrix = reduced_backward(matrix_product(normed_input, query_proj)).reshape(document_length, QUERY_HEAD_COUNT, HEAD_DIM)
    pair_rows = reduced_backward(matrix_product(normed_input, key_value_weight.reshape(MODEL_DIM, KEY_VALUE_HEADS * 2 * HEAD_DIM))).reshape(document_length, KEY_VALUE_HEADS, 2, HEAD_DIM)
    query_matrix = low(rotate(query_matrix, cosine, sine))
    key_rows = low(rotate(pair_rows[:, :, 0], cosine, sine))
    value_rows = low(pair_rows[:, :, 1])
    attended = low(reduced_backward(attention(query_matrix, key_rows, value_rows, segment)))
    branch = reduced_backward(matrix_product(mixer_rows, mixer_out) + matrix_product(attended, attn_out))
    hidden = tokens + branch
    normed_ffn = low(rms_norm(hidden, ffn_gain))
    gate_rows = reduced_backward(matrix_product(normed_ffn, ffn_gate))
    up_rows = reduced_backward(matrix_product(normed_ffn, ffn_up))
    activated = low(jax.nn.silu(gate_rows) * up_rows)
    return hidden + matrix_product(activated, ffn_down)

def reference(layer_input, segments, input_gain, mixer_proj, state_proj, step_proj, step_bias, decay_log, skip_gain, conv_kernel, conv_bias, state_kernel, state_bias, gated_gain, mixer_out, query_proj, key_value_weight, attn_out, ffn_gain, ffn_gate, ffn_up, ffn_down, cotangent):
    params = tuple((weight.astype(jnp.float32) for weight in (input_gain, mixer_proj, state_proj, step_proj, step_bias, decay_log, skip_gain, conv_kernel, conv_bias, state_kernel, state_bias, gated_gain, mixer_out, query_proj, key_value_weight, attn_out, ffn_gain, ffn_gate, ffn_up, ffn_down)))
    tokens = layer_input.astype(jnp.float32).reshape(SEQS, SEQ, MODEL_DIM)

    def forward(token_rows, weights):
        return jax.vmap(lambda rows, segment: layer(rows, segment, weights))(token_rows, segments)
    output, pullback = jax.vjp(forward, tokens, params)
    grad_tokens, grads = pullback(cotangent.astype(jnp.float32).reshape(SEQS, SEQ, MODEL_DIM))
    return (output.reshape(TOKENS, MODEL_DIM).astype(jnp.bfloat16), grad_tokens.reshape(TOKENS, MODEL_DIM), grads[0], grads[1], grads[2], grads[3], grads[4], grads[5], grads[6], grads[7], grads[8], grads[9], grads[10], grads[11], grads[12], grads[13], grads[14], grads[15], grads[16], grads[17], grads[18], grads[19])
```

```python
import jax
import jax.numpy as jnp
from jax import lax
from jax.sharding import PartitionSpec as P

HEAD_DIM = 64
DSSM = 1536
DP = ("y", "zh", "x", "core")
PAIR = [(0, 1), (1, 0)]
LINKS = {
    "A": [(0, 1), (1, 0), (2, 3), (3, 2)],
    "B": [(1, 2), (2, 1), (3, 0), (0, 3)],
}


norm_eps = 1e-05
rope_base = 10000.0
masked_score = -1e30
highest = lax.Precision.HIGHEST


def silu_slope(argument):
    logistic = jax.nn.sigmoid(argument)
    return logistic * (1.0 + argument * (1.0 - logistic))


def rope_tables(document_length, head_size):
    half_size = head_size // 2
    inverse = rope_base ** (-(2.0 * jnp.arange(half_size, dtype=jnp.float32)) / head_size)
    angles = jnp.arange(document_length, dtype=jnp.float32)[:, None] * inverse[None, :]
    return (jnp.cos(angles)[:, None, :], jnp.sin(angles)[:, None, :])


def rotate(argument, cosine, sine):
    half_size = argument.shape[-1] // 2
    first_half = argument[..., :half_size]
    second_half = argument[..., half_size:]
    return jnp.concatenate(
        [first_half * cosine - second_half * sine, second_half * cosine + first_half * sine],
        axis=-1,
    )


def shift_down(values, offset):
    return jnp.concatenate(
        [jnp.zeros((offset, values.shape[1]), values.dtype), values[:-offset]], axis=0
    )


def shift_up(values, offset):
    return jnp.concatenate(
        [values[offset:], jnp.zeros((offset, values.shape[1]), values.dtype)], axis=0
    )


def lag_keep(segment, offset):
    previous = jnp.concatenate([jnp.full((offset,), -1, jnp.int32), segment[:-offset]])
    return (previous == segment).astype(jnp.float32)[:, None]


def conv_forward(values, kernel, conv_shift, segment):
    tap_count = kernel.shape[0]
    summed = conv_shift[None, :] + kernel[tap_count - 1][None, :] * values
    for offset in range(1, tap_count):
        summed = summed + kernel[tap_count - 1 - offset][None, :] * shift_down(
            values, offset
        ) * lag_keep(segment, offset)
    return summed


def conv_backward(grad_pre, values, kernel, segment):
    tap_count = kernel.shape[0]
    grad_values = kernel[tap_count - 1][None, :] * grad_pre
    kernel_rows = [jnp.sum(grad_pre * values, axis=0)]
    for offset in range(1, tap_count):
        masked = grad_pre * lag_keep(segment, offset)
        grad_values = grad_values + kernel[tap_count - 1 - offset][None, :] * shift_up(
            masked, offset
        )
        kernel_rows.append(jnp.sum(masked * shift_down(values, offset), axis=0))
    return (grad_values, jnp.stack(kernel_rows[::-1], axis=0), jnp.sum(grad_pre, axis=0))


def decay_weights(step_size, decay_rate, segment):
    document_length = step_size.shape[0]
    cumulative = jnp.cumsum(step_size * decay_rate[None, :], axis=0).T
    positions = jnp.arange(document_length)
    allowed = (positions[:, None] >= positions[None, :]) & (segment[:, None] == segment[None, :])
    spread = cumulative[:, :, None] - cumulative[:, None, :]
    return jnp.where(allowed[None], jnp.exp(jnp.where(allowed[None], spread, 0.0)), 0.0)


def norm_backward(grad_unit, unit_rows, inv_rms):
    return inv_rms * (
        grad_unit - unit_rows * jnp.mean(grad_unit * unit_rows, axis=-1, keepdims=True)
    )


def exchange(values, name):
    return values + lax.ppermute(values, name, PAIR)


def take(values, index, axis):
    return lax.dynamic_slice_in_dim(values, index, 1, axis)


def first_halving(values, name, axis, link):
    place = lax.axis_index(name)
    if link == "A":
        side = ((place + 1) // 2) % 2
        kept = jnp.concatenate([take(values, side, axis), take(values, 3 - side, axis)], axis)
        sent = jnp.concatenate([take(values, 1 - side, axis), take(values, 2 + side, axis)], axis)
    else:
        side = place // 2
        kept = lax.dynamic_slice_in_dim(values, 2 * side, 2, axis)
        sent = lax.dynamic_slice_in_dim(values, 2 - 2 * side, 2, axis)
    return kept + lax.ppermute(sent, name, LINKS[link])


def second_halving(values, name, axis, link):
    place = lax.axis_index(name)
    index = place // 2 if link == "B" else place % 2
    sent = take(values, 1 - index, axis)
    return take(values, index, axis) + lax.ppermute(sent, name, LINKS[link])


def reduce_blocks(values):
    count, rows, columns = values.shape
    blocks = values.reshape(count, 4, 2, 4, rows // 32, columns)
    tiles = columns // 128
    sizes = [128 * (tiles // 4 + (1 if k < tiles % 4 else 0)) for k in range(4)]
    orders = [
        (("x", "A"), ("x", "B"), ("y", "A"), ("y", "B")),
        (("x", "B"), ("y", "A"), ("y", "B"), ("x", "A")),
        (("y", "A"), ("y", "B"), ("x", "A"), ("x", "B")),
        (("y", "B"), ("x", "A"), ("x", "B"), ("y", "A")),
    ]
    parts, start = [], 0
    for size in sizes:
        parts.append(blocks[..., start : start + size])
        start += size
    seen = [set() for _ in range(4)]
    for step in range(4):
        for k in range(4):
            name, link = orders[k][step]
            axis = {"y": 1, "x": 3}[name]
            halving = second_halving if name in seen[k] else first_halving
            parts[k] = halving(parts[k], name, axis, link)
            seen[k].add(name)
    merged = jnp.concatenate(parts, axis=-1)
    place = lax.axis_index("zh")
    own = take(merged, place, 2) + lax.ppermute(take(merged, 1 - place, 2), "zh", PAIR)
    return own.reshape(count, rows // 32, columns)


def core_halves(left, right):
    place = lax.axis_index("core")
    half = left.shape[2] // 2

    def rows_of(index):
        part = lax.dynamic_slice_in_dim(left, index * half, half, 2)
        return jnp.einsum("btm,btn->bmn", part, right, preferred_element_type=jnp.float32)

    return rows_of(place) + lax.ppermute(rows_of(1 - place), "core", PAIR)


def gather_blocks(values):
    return lax.all_gather(values, ("core", "y", "zh", "x"), axis=1, tiled=True)


def on_device(
    layer_input,
    segments,
    input_gain,
    mixer_proj,
    state_proj,
    step_proj,
    step_bias,
    decay_log,
    skip_gain,
    conv_kernel,
    conv_bias,
    state_kernel,
    state_bias,
    gated_gain,
    mixer_out,
    query_proj,
    key_value_weight,
    attn_out,
    ffn_gain,
    ffn_gate,
    ffn_up,
    ffn_down,
    cotangent,
):
    segment = segments.reshape(-1)
    tokens = layer_input.astype(jnp.float32)
    document_length = tokens.shape[0]
    model_width = tokens.shape[1]
    width = mixer_proj.shape[2]
    heads = step_proj.shape[1]
    head_size = width // heads
    state_size = state_proj.shape[1] // 2
    kv_heads = key_value_weight.shape[1]
    query_heads = query_proj.shape[1] // HEAD_DIM
    group_width = query_heads // kv_heads
    score_scale = HEAD_DIM ** (-0.5)
    mixer_flat = mixer_proj.reshape(model_width, 2 * width)
    keyval_flat = key_value_weight.reshape(model_width, kv_heads * 2 * HEAD_DIM)
    inv_rms_in = lax.rsqrt(jnp.mean(tokens * tokens, axis=-1, keepdims=True) + norm_eps)
    unit_in = tokens * inv_rms_in
    normed_input = (unit_in * input_gain).astype(jnp.bfloat16)
    gate_input = jnp.dot(normed_input, mixer_flat, preferred_element_type=jnp.float32)
    gate_branch = gate_input[:, :width]
    conv_in = gate_input[:, width:]
    state_in = jnp.dot(normed_input, state_proj, preferred_element_type=jnp.float32)
    step_raw = jnp.dot(normed_input, step_proj, preferred_element_type=jnp.float32)
    conv_pre = conv_forward(conv_in, conv_kernel, conv_bias, segment)
    conv_out = jax.nn.silu(conv_pre)
    state_pre = conv_forward(state_in, state_kernel, state_bias, segment)
    state_conv = jax.nn.silu(state_pre)
    in_state = state_conv[:, :state_size]
    out_state = state_conv[:, state_size:]
    step_arg = step_raw + step_bias
    step_size = jax.nn.softplus(step_arg)
    decay_rate = -jnp.exp(decay_log)
    heads_in = conv_out.reshape(document_length, heads, head_size)
    decay_mat = decay_weights(step_size, decay_rate, segment)
    intersection = jnp.dot(out_state, in_state.T, precision=highest)
    mixing = decay_mat * intersection[None]
    scaled_in = heads_in * step_size[:, :, None]
    scan_heads = jnp.einsum("hts,shd->thd", mixing, scaled_in, precision=highest)
    scan_out = (scan_heads + skip_gain[None, :, None] * heads_in).reshape(document_length, width)
    gate_act = jax.nn.silu(gate_branch)
    gated = scan_out * gate_act
    squares = exchange(jnp.sum(gated * gated, axis=-1, keepdims=True), "tensor")
    inv_rms_gated = lax.rsqrt(squares / DSSM + norm_eps)
    unit_gated = gated * inv_rms_gated
    mixer_rows = (unit_gated * gated_gain).astype(jnp.bfloat16)
    cosine, sine = rope_tables(document_length, HEAD_DIM)
    query_raw = jnp.dot(normed_input, query_proj, preferred_element_type=jnp.float32).reshape(
        document_length, query_heads, HEAD_DIM
    )
    pair_rows = jnp.dot(normed_input, keyval_flat, preferred_element_type=jnp.float32).reshape(
        document_length, kv_heads, 2, HEAD_DIM
    )
    query_matrix = (
        rotate(query_raw, cosine, sine)
        .astype(jnp.bfloat16)
        .reshape(document_length, kv_heads, group_width, HEAD_DIM)
    )
    key_rows = rotate(pair_rows[:, :, 0], cosine, sine).astype(jnp.bfloat16)
    value_rows = pair_rows[:, :, 1].astype(jnp.bfloat16)
    positions = jnp.arange(document_length)
    allowed = ((positions[:, None] >= positions[None, :]) & (segment[:, None] == segment[None, :]))[
        None, None
    ]
    scores = jnp.where(
        allowed,
        jnp.einsum("tkgd,skd->kgts", query_matrix, key_rows, preferred_element_type=jnp.float32)
        * score_scale,
        masked_score,
    )
    row_max = jnp.max(scores, axis=-1, keepdims=True)
    log_total = row_max + jnp.log(jnp.sum(jnp.exp(scores - row_max), axis=-1, keepdims=True))
    prob_rows = jnp.exp(scores - log_total).astype(jnp.bfloat16)
    attended = jnp.einsum(
        "kgts,skd->tkgd", prob_rows, value_rows, preferred_element_type=jnp.float32
    )
    attended = attended.reshape(document_length, query_heads * HEAD_DIM).astype(jnp.bfloat16)
    partial_branch = jnp.dot(mixer_rows, mixer_out, preferred_element_type=jnp.float32) + jnp.dot(
        attended, attn_out, preferred_element_type=jnp.float32
    )
    branch = exchange(partial_branch, "tensor")
    hidden = tokens + branch
    inv_rms_ffn = lax.rsqrt(jnp.mean(hidden * hidden, axis=-1, keepdims=True) + norm_eps)
    unit_ffn = hidden * inv_rms_ffn
    normed_ffn = (unit_ffn * ffn_gain).astype(jnp.bfloat16)
    gate_rows = jnp.dot(normed_ffn, ffn_gate, preferred_element_type=jnp.float32)
    up_rows = jnp.dot(normed_ffn, ffn_up, preferred_element_type=jnp.float32)
    gate_silu = jax.nn.silu(gate_rows)
    activated = (gate_silu * up_rows).astype(jnp.bfloat16)
    down_rows = exchange(jnp.dot(activated, ffn_down, preferred_element_type=jnp.float32), "tensor")
    layer_output = (hidden + down_rows).astype(jnp.bfloat16)
    grad_out = cotangent.astype(jnp.float32)
    grad_activated = jnp.dot(cotangent, ffn_down.T, preferred_element_type=jnp.float32)
    grad_gate_rows = (grad_activated * up_rows * silu_slope(gate_rows)).astype(jnp.bfloat16)
    grad_up_rows = (grad_activated * gate_silu).astype(jnp.bfloat16)
    partial_ffn = jnp.dot(grad_gate_rows, ffn_gate.T, preferred_element_type=jnp.float32) + jnp.dot(
        grad_up_rows, ffn_up.T, preferred_element_type=jnp.float32
    )
    grad_normed_ffn = exchange(partial_ffn, "tensor")
    grad_ffn_gain = jnp.sum(grad_normed_ffn * unit_ffn, axis=0)
    grad_hidden = grad_out + norm_backward(grad_normed_ffn * ffn_gain, unit_ffn, inv_rms_ffn)
    grad_branch = grad_hidden.astype(jnp.bfloat16)
    grad_mixer_rows = jnp.dot(grad_branch, mixer_out.T, preferred_element_type=jnp.float32)
    grad_attended = jnp.dot(grad_branch, attn_out.T, preferred_element_type=jnp.float32).astype(
        jnp.bfloat16
    )
    grad_attended = grad_attended.reshape(document_length, kv_heads, group_width, HEAD_DIM)
    scores_again = jnp.where(
        allowed,
        jnp.einsum("tkgd,skd->kgts", query_matrix, key_rows, preferred_element_type=jnp.float32)
        * score_scale,
        masked_score,
    )
    probs = jnp.exp(scores_again - log_total)
    grad_probs = jnp.einsum(
        "tkgd,skd->kgts", grad_attended, value_rows, preferred_element_type=jnp.float32
    )
    grad_values = jnp.einsum(
        "kgts,tkgd->skd",
        probs.astype(jnp.bfloat16),
        grad_attended,
        preferred_element_type=jnp.float32,
    )
    row_dot = jnp.sum(probs * grad_probs, axis=-1, keepdims=True)
    grad_scores = (probs * (grad_probs - row_dot)).astype(jnp.bfloat16)
    grad_queries = (
        jnp.einsum("kgts,skd->tkgd", grad_scores, key_rows, preferred_element_type=jnp.float32)
        * score_scale
    )
    grad_keys = (
        jnp.einsum("kgts,tkgd->skd", grad_scores, query_matrix, preferred_element_type=jnp.float32)
        * score_scale
    )
    grad_queries = rotate(
        grad_queries.reshape(document_length, query_heads, HEAD_DIM), cosine, -sine
    )
    grad_queries = grad_queries.astype(jnp.bfloat16).reshape(
        document_length, query_heads * HEAD_DIM
    )
    grad_pairs = jnp.stack([rotate(grad_keys, cosine, -sine), grad_values], axis=2)
    grad_pairs = grad_pairs.astype(jnp.bfloat16).reshape(document_length, kv_heads * 2 * HEAD_DIM)
    grad_gated_gain = jnp.sum(grad_mixer_rows * unit_gated, axis=0)
    grad_unit_gated = grad_mixer_rows * gated_gain
    gated_dot = exchange(jnp.sum(grad_unit_gated * unit_gated, axis=-1, keepdims=True), "tensor")
    grad_gated = inv_rms_gated * (grad_unit_gated - unit_gated * gated_dot / DSSM)
    grad_scan = (grad_gated * gate_act).reshape(document_length, heads, head_size)
    grad_gate_branch = grad_gated * scan_out * silu_slope(gate_branch)
    grad_mix = jnp.einsum("thd,shd->hts", grad_scan, scaled_in, precision=highest)
    grad_scaled = jnp.einsum("hts,thd->shd", mixing, grad_scan, precision=highest)
    grad_skip_gain = jnp.sum(grad_scan * heads_in, axis=(0, 2))
    grad_heads = grad_scaled * step_size[:, :, None] + grad_scan * skip_gain[None, :, None]
    grad_intersection = jnp.sum(grad_mix * decay_mat, axis=0)
    decay_flow = grad_mix * mixing
    grad_cumulative = (jnp.sum(decay_flow, axis=2) - jnp.sum(decay_flow, axis=1)).T
    grad_log = jnp.cumsum(grad_cumulative[::-1], axis=0)[::-1]
    grad_step = jnp.sum(grad_scaled * heads_in, axis=-1) + grad_log * decay_rate[None, :]
    grad_decay_log = jnp.sum(grad_log * step_size, axis=0) * decay_rate
    grad_out_state = jnp.dot(grad_intersection, in_state, precision=highest)
    grad_in_state = jnp.dot(grad_intersection.T, out_state, precision=highest)
    grad_state = exchange(jnp.concatenate([grad_in_state, grad_out_state], axis=1), "tensor")
    grad_state_in, grad_state_kernel, grad_state_bias = conv_backward(
        grad_state * silu_slope(state_pre), state_in, state_kernel, segment
    )
    grad_state_rows = grad_state_in.astype(jnp.bfloat16)
    grad_step_arg = grad_step * jax.nn.sigmoid(step_arg)
    grad_step_bias = jnp.sum(grad_step_arg, axis=0)
    grad_step_rows = grad_step_arg.astype(jnp.bfloat16)
    grad_conv_in, grad_conv_kernel, grad_conv_bias = conv_backward(
        grad_heads.reshape(document_length, width) * silu_slope(conv_pre),
        conv_in,
        conv_kernel,
        segment,
    )
    grad_gate_input = jnp.concatenate([grad_gate_branch, grad_conv_in], axis=1).astype(jnp.bfloat16)
    partial_normed = jnp.dot(grad_gate_input, mixer_flat.T, preferred_element_type=jnp.float32)
    partial_normed = partial_normed + jnp.dot(
        grad_step_rows, step_proj.T, preferred_element_type=jnp.float32
    )
    partial_normed = partial_normed + jnp.dot(
        grad_queries, query_proj.T, preferred_element_type=jnp.float32
    )
    partial_normed = partial_normed + jnp.dot(
        grad_pairs, keyval_flat.T, preferred_element_type=jnp.float32
    )
    grad_normed = exchange(partial_normed, "tensor")
    grad_normed = grad_normed + jnp.dot(
        grad_state_rows, state_proj.T, preferred_element_type=jnp.float32
    )
    grad_input_gain = jnp.sum(grad_normed * unit_in, axis=0)
    input_grad = grad_hidden + norm_backward(grad_normed * input_gain, unit_in, inv_rms_in)
    first = core_halves(
        jnp.stack([normed_ffn, normed_ffn, activated, jnp.concatenate([mixer_rows, attended], axis=1)]),
        jnp.stack([grad_gate_rows, grad_up_rows, cotangent, grad_branch]),
    )
    first = gather_blocks(reduce_blocks(first))
    flat = [
        grad_input_gain,
        grad_step_bias,
        grad_decay_log,
        grad_skip_gain,
        grad_conv_kernel,
        grad_conv_bias,
        grad_state_kernel,
        grad_state_bias,
        grad_gated_gain,
        grad_ffn_gain,
    ]
    small = jnp.concatenate([part.reshape(-1) for part in flat])
    small = jnp.pad(small, (0, 16 * model_width - small.shape[0])).reshape(16, model_width).T
    right = jnp.concatenate(
        [
            grad_gate_input,
            grad_state_rows,
            grad_queries,
            grad_pairs,
            grad_step_rows,
            jnp.zeros((document_length, 128 - heads), jnp.bfloat16),
        ],
        axis=1,
    )
    second = core_halves(normed_input[None], right[None])
    place = lax.axis_index("core")
    half = model_width // 2
    small_kept = lax.dynamic_slice_in_dim(small, place * half, half, 0)
    small_sent = lax.dynamic_slice_in_dim(small, (1 - place) * half, half, 0)
    small_kept = small_kept + lax.ppermute(small_sent, "core", PAIR)
    width_in = right.shape[1]
    at_small = width_in - 128 + heads
    second = second + jnp.pad(small_kept, ((0, 0), (at_small, 128 - heads - 16)))[None]
    second = gather_blocks(reduce_blocks(second))[0]
    small = second[:, at_small : at_small + 16].T.reshape(-1)
    small_out, start = [], 0
    for part in flat:
        small_out.append(small[start : start + part.size].reshape(part.shape))
        start += part.size
    ends = [2 * width, 2 * state_size, query_heads * HEAD_DIM, kv_heads * 2 * HEAD_DIM, heads]
    big_out, start = [], 0
    for end in ends:
        big_out.append(second[:, start : start + end])
        start += end
    return (
        layer_output,
        input_grad,
        small_out[0],
        big_out[0].reshape(mixer_proj.shape),
        big_out[1],
        big_out[4],
        small_out[1],
        small_out[2],
        small_out[3],
        small_out[4],
        small_out[5],
        small_out[6],
        small_out[7],
        small_out[8],
        first[3, :width],
        big_out[2],
        big_out[3].reshape(key_value_weight.shape),
        first[3, width:],
        small_out[9],
        first[0],
        first[1],
        first[2],
    )


def solution(mesh):
    in_specs = (
        P(DP, None),
        P(DP, None),
        P(),
        P(None, None, "tensor"),
        P(),
        P(None, "tensor"),
        P("tensor"),
        P("tensor"),
        P("tensor"),
        P(None, "tensor"),
        P("tensor"),
        P(),
        P(),
        P("tensor"),
        P("tensor", None),
        P(None, "tensor"),
        P(None, "tensor", None),
        P("tensor", None),
        P(),
        P(None, "tensor"),
        P(None, "tensor"),
        P("tensor", None),
        P(DP, None),
    )
    out_specs = (
        P(DP, None),
        P(DP, None),
        P(),
        P(None, None, "tensor"),
        P(),
        P(None, "tensor"),
        P("tensor"),
        P("tensor"),
        P("tensor"),
        P(None, "tensor"),
        P("tensor"),
        P(),
        P(),
        P("tensor"),
        P("tensor", None),
        P(None, "tensor"),
        P(None, "tensor", None),
        P("tensor", None),
        P(),
        P(None, "tensor"),
        P(None, "tensor"),
        P("tensor", None),
    )
    mesh = jax.sharding.Mesh(
        mesh.devices.reshape(4, 2, 4, 2, 2), ("y", "zh", "x", "core", "tensor")
    )
    return jax.shard_map(
        on_device, mesh=mesh, in_specs=in_specs, out_specs=out_specs, check_vma=False
    )
```

```python
import functools

import jax
import jax.numpy as jnp
import numpy as np
from jax import lax
from jax.experimental import pallas as pl
from jax.experimental.pallas import tpu as pltpu
from jax.sharding import PartitionSpec as P

HEAD_DIM = 64
DSSM = 1536
DP = ("y", "zh", "x", "core")
PAIR = [(0, 1), (1, 0)]
LINKS = {
    "A": [(0, 1), (1, 0), (2, 3), (3, 2)],
    "B": [(1, 2), (2, 1), (3, 0), (0, 3)],
}
ORDERS = (
    (("x", "A"), ("x", "B"), ("y", "A"), ("y", "B")),
    (("x", "B"), ("y", "A"), ("y", "B"), ("x", "A")),
    (("y", "A"), ("y", "B"), ("x", "A"), ("x", "B")),
    (("y", "B"), ("x", "A"), ("x", "B"), ("y", "A")),
)
AXIS = {"y": 1, "x": 3}
LOG2E = 1.4426950408889634
hidden_bias = -1e30
norm_eps = 1e-05
rope_base = 10000.0
LEN = 128


def dot_nn(left, right):
    return lax.dot_general(
        left, right, (((1,), (0,)), ((), ())), preferred_element_type=jnp.float32
    )


def dot_nt(left, right):
    return lax.dot_general(
        left, right, (((1,), (1,)), ((), ())), preferred_element_type=jnp.float32
    )


def dot_tn(left, right):
    return lax.dot_general(
        left, right, (((0,), (0,)), ((), ())), preferred_element_type=jnp.float32
    )


def two_terms(v):
    high = v.astype(jnp.bfloat16)
    return high, (v - high.astype(jnp.float32)).astype(jnp.bfloat16)


def three_dots(dot, left, right):
    left_high, left_low = two_terms(left)
    right_high, right_low = two_terms(right)
    return dot(left_high, right_high) + dot(left_high, right_low) + dot(left_low, right_high)


def sigmoid(v):
    return 1.0 / (1.0 + jnp.exp(-v))


def block(index):
    return slice(index * LEN, (index + 1) * LEN)


def lane_iota(rows=LEN):
    return lax.broadcasted_iota(jnp.int32, (rows, LEN), 1)


def mask_ts(seg_col, seg_row, i, j):
    same = seg_col[block(i), :] == seg_row[:, block(j)]
    if i != j:
        return same
    down = lax.broadcasted_iota(jnp.int32, (LEN, LEN), 0)
    return same & (down >= lane_iota())


def mask_st(seg_col, seg_row, j, i):
    same = seg_col[block(j), :] == seg_row[:, block(i)]
    if i != j:
        return same
    down = lax.broadcasted_iota(jnp.int32, (LEN, LEN), 0)
    return same & (down <= lane_iota())


def conv_rows(pad_ref, keep_ref, kernel, bias, start, lanes):
    summed = bias + kernel[3:4] * pad_ref[8 + start : 8 + start + LEN, lanes]
    for lag in (1, 2, 3):
        moved = pad_ref[8 + start - lag : 8 + start - lag + LEN, lanes]
        summed = summed + kernel[3 - lag : 4 - lag] * (moved * keep_ref[lag - 1, start : start + LEN, :])
    return summed


def widen(keep_ref, wide_ref):
    rows = keep_ref.shape[0]
    for lag in (1, 2, 3):
        wide_ref[lag - 1, :, :] = jnp.broadcast_to(keep_ref[:, lag : lag + 1], (rows, LEN))


def prep_kernel(
    conv_ref,
    small_ref,
    cos_ref,
    sin_ref,
    keep_ref,
    conv_kernel_ref,
    conv_bias_ref,
    state_kernel_ref,
    state_bias_ref,
    step_bias_ref,
    rate_ref,
    x_ref,
    xb_ref,
    slope_ref,
    state_ref,
    state_slope_ref,
    cum_ref,
    lag_ref,
    cum_row_ref,
    lag_row_ref,
    step_row_ref,
    sig_row_ref,
    q_ref,
    kv_ref,
    pad_ref,
    state_pad_ref,
    wide_ref,
):
    rows = conv_ref.shape[0]
    blocks = rows // LEN
    pad_ref[0:8, :] = jnp.zeros((8, pad_ref.shape[1]), jnp.float32)
    pad_ref[8 : rows + 8, :] = conv_ref[...]
    state_pad_ref[0:8, :] = jnp.zeros((8, state_pad_ref.shape[1]), jnp.float32)
    state_pad_ref[8 : rows + 8, :] = small_ref[:, : 2 * LEN]
    widen(keep_ref, wide_ref)

    def channel_tile(c, _):
        lanes = pl.ds(pl.multiple_of(c * LEN, LEN), LEN)
        for i in range(blocks):
            pre = conv_rows(pad_ref, wide_ref, conv_kernel_ref[:, lanes], conv_bias_ref[:, lanes], i * LEN, lanes)
            sig = sigmoid(pre)
            x = pre * sig
            x_ref[block(i), lanes] = x
            xb_ref[block(i), lanes] = x.astype(jnp.bfloat16)
            slope_ref[block(i), lanes] = sig * (1.0 + pre * (1.0 - sig))
        return 0

    lax.fori_loop(0, conv_ref.shape[1] // LEN, channel_tile, 0)

    def state_tile(c, _):
        lanes = pl.ds(pl.multiple_of(c * LEN, LEN), LEN)
        for i in range(blocks):
            pre = conv_rows(
                state_pad_ref, wide_ref, state_kernel_ref[:, lanes], state_bias_ref[:, lanes], i * LEN, lanes
            )
            sig = sigmoid(pre)
            state_ref[block(i), lanes] = pre * sig
            state_slope_ref[block(i), lanes] = sig * (1.0 + pre * (1.0 - sig))
        return 0

    lax.fori_loop(0, 2, state_tile, 0)

    down = lax.broadcasted_iota(jnp.int32, (LEN, LEN), 0)
    lower = jnp.where(down >= lane_iota(), 1.0, 0.0).astype(jnp.bfloat16)
    left_half = lane_iota() < HEAD_DIM
    carry = jnp.zeros((1, LEN), jnp.float32)
    heads = cum_row_ref.shape[0]
    for i in range(blocks):
        argument = small_ref[block(i), block(5)] + step_bias_ref[...]
        tail = jnp.exp(-jnp.abs(argument))
        grown = jnp.where(tail < 1e-3, tail - 0.5 * tail * tail, jnp.log(1.0 + tail))
        step = jnp.maximum(argument, 0.0) + grown
        first, rest = two_terms(step * rate_ref[...] * LOG2E)
        last = step * rate_ref[...] * LOG2E - first.astype(jnp.float32) - rest.astype(jnp.float32)
        cum = dot_nn(lower, first) + dot_nn(lower, rest) + dot_nn(lower, last.astype(jnp.bfloat16)) + carry
        carry = cum[LEN - 1 : LEN, :]
        lag = cum - jnp.log(step) * LOG2E
        cum_ref[block(i), :] = cum
        lag_ref[block(i), :] = lag
        cum_t, lag_t = cum.T, lag.T
        step_row_ref[:, block(i)] = step.T[:heads]
        sig_row_ref[:, block(i)] = sigmoid(argument).T[:heads]
        for h in range(heads):
            cum_row_ref[h, :, block(i)] = cum_t[h : h + 1]
            lag_row_ref[h, :, block(i)] = lag_t[h : h + 1]
        cosine, sine = cos_ref[block(i), :], sin_ref[block(i), :]
        kv = small_ref[block(i), block(4)]
        kv_ref[block(i), :] = jnp.where(left_half, rotate_tile(kv, cosine, sine), kv).astype(jnp.bfloat16)
        for p in range(q_ref.shape[1] // LEN):
            q_ref[block(i), block(p)] = rotate_tile(small_ref[block(i), block(2 + p)], cosine, sine).astype(jnp.bfloat16)


def rotate_tile(v, cosine, sine):
    first = lax.rem(lane_iota(v.shape[0]), HEAD_DIM) < HEAD_DIM // 2
    swapped = jnp.where(first, pltpu.roll(v, LEN - HEAD_DIM // 2, 1), pltpu.roll(v, HEAD_DIM // 2, 1))
    return v * cosine + swapped * sine


def scan_kernel(
    chunks,
    heads,
    gate_ref,
    x_ref,
    xb_ref,
    state_ref,
    cum_ref,
    lag_row_ref,
    seg_col_ref,
    seg_row_ref,
    skip_ref,
    y_ref,
    gated_ref,
    row_ref,
    wide_ref,
    cross_ref,
    bias_ref,
    mix_ref,
    square_ref,
):
    first = chunks[0]
    for h in range(heads):
        for i in chunks:
            wide_ref[h, block(i - first), :] = jnp.broadcast_to(cum_ref[block(i), h : h + 1], (LEN, LEN))
    pairs = [(i, j) for i in chunks for j in range(max(0, i - 2), i + 1)]
    for i in chunks:
        low = max(0, i - 2)
        cross = three_dots(dot_nt, state_ref[block(i), LEN:], state_ref[low * LEN : (i + 1) * LEN, :LEN])
        for n, (i2, j) in enumerate(pairs):
            if i2 == i:
                cross_ref[n] = cross[:, block(j - low)]
                allowed = mask_ts(seg_col_ref, seg_row_ref, i, j)
                bias_ref[n] = jnp.where(allowed, 0.0, hidden_bias)
    left_half = lane_iota() < HEAD_DIM
    square_ref[...] = jnp.zeros(square_ref.shape, jnp.float32)

    def head_pair(hp, _):
        lanes = pl.ds(pl.multiple_of(hp * LEN, LEN), LEN)
        for i in chunks:
            at = block(i - first)
            low = max(0, i - 2)
            for n, (i2, j) in enumerate(pairs):
                if i2 != i:
                    continue
                for e in range(2):
                    spread = wide_ref[2 * hp + e, at, :] - lag_row_ref[2 * hp + e, :, block(j)]
                    decay = jnp.exp2(spread + bias_ref[n])
                    mix_ref[block(e), block(j - low)] = (decay * cross_ref[n]).astype(jnp.bfloat16)
            both = dot_nn(mix_ref[:, : (i + 1 - low) * LEN], xb_ref[low * LEN : (i + 1) * LEN, lanes])
            y = jnp.where(left_half, both[:LEN], both[LEN:])
            y_ref[at, lanes] = y
            gate = gate_ref[block(i), lanes]
            gated = (y + skip_ref[:, lanes] * x_ref[block(i), lanes]) * (gate * sigmoid(gate))
            gated_ref[at, lanes] = gated
            square_ref[at, :] = square_ref[at, :] + gated * gated
        return 0

    lax.fori_loop(0, heads // 2, head_pair, 0)
    for i in chunks:
        at = block(i - first)
        total = jnp.sum(square_ref[at, :], axis=1, keepdims=True)
        row_ref[0:1, at] = jnp.broadcast_to(total, (LEN, LEN)).T[0:1]


def attention_kernel(chunks, q_ref, kv_ref, seg_col_ref, seg_row_ref, out_ref, lse_ref):
    scale = HEAD_DIM ** (-0.5) * LOG2E
    first = chunks[0]
    left_half = lane_iota() < HEAD_DIM
    zero = jnp.zeros((LEN, LEN), jnp.bfloat16)
    lse_ref[...] = jnp.zeros(lse_ref.shape, jnp.float32)
    for i in chunks:
        at = block(i - first)
        low = max(0, i - 2) * LEN
        span = (i + 1) * LEN - low
        allowed = jnp.concatenate([mask_ts(seg_col_ref, seg_row_ref, i, j) for j in range(low // LEN, i + 1)], axis=1)
        keys = kv_ref[low : low + span, :]
        turned = pltpu.roll(keys.astype(jnp.float32), HEAD_DIM, 1).astype(jnp.bfloat16)
        for p in range(q_ref.shape[1] // LEN):
            queries = q_ref[block(i), block(p)]
            result = []
            for e in range(2):
                masked = jnp.where(left_half == (e == 0), queries, zero)
                scores = dot_nt(masked, keys if e == 0 else turned) * scale
                scores = jnp.where(allowed, scores, hidden_bias)
                top = jnp.max(scores, axis=1, keepdims=True)
                weights = jnp.exp2(scores - top)
                total = jnp.sum(weights, axis=1, keepdims=True)
                probs = (weights * (1.0 / total)).astype(jnp.bfloat16)
                result.append(dot_nn(probs, turned if e == 0 else keys))
                lse = jnp.broadcast_to(top + jnp.log(total) * LOG2E, (LEN, LEN))
                lse_ref[2 * p + e : 2 * p + e + 1, at] = lse.T[0:1]
            out_ref[at, block(p)] = jnp.where(left_half, result[0], result[1]).astype(jnp.bfloat16)


def attention_back_kernel(chunks, final, *refs):
    q_ref, kv_ref, do_ref, lse_ref, seg_col_ref, seg_row_ref, cos_ref, sin_ref = refs[:8]
    if final:
        dk_in_ref, dv_in_ref, dq_ref, dkv_ref, dk_ref, dv_ref, turned_ref, key_t_ref = refs[8:]
    else:
        dq_ref, dk_ref, dv_ref, turned_ref, key_t_ref = refs[8:]
    scale = HEAD_DIM ** (-0.5)
    blocks = q_ref.shape[0] // LEN
    first = chunks[0]
    left_half = lane_iota() < HEAD_DIM
    zero = jnp.zeros((LEN, LEN), jnp.bfloat16)
    for i in range(chunks[-1] + 1):
        kv = kv_ref[block(i), :].astype(jnp.float32)
        turned_ref[block(i), :] = pltpu.roll(kv, HEAD_DIM, 1).astype(jnp.bfloat16)
        key_t_ref[:, block(i)] = kv.T[:HEAD_DIM].astype(jnp.bfloat16)
    if final:
        dk_ref[...] = dk_in_ref[...]
        dv_ref[...] = dv_in_ref[...]
    else:
        dk_ref[...] = jnp.zeros(dk_ref.shape, jnp.float32)
        dv_ref[...] = jnp.zeros(dv_ref.shape, jnp.float32)
    for i in chunks:
        at = block(i - first)
        low = max(0, i - 2) * LEN
        span = (i + 1) * LEN - low
        window = slice(low, low + span)
        allowed = jnp.concatenate([mask_st(seg_col_ref, seg_row_ref, j, i) for j in range(low // LEN, i + 1)], axis=0)
        keys, turned = kv_ref[window, :], turned_ref[window, :]
        for p in range(q_ref.shape[1] // LEN):
            queries, douts = q_ref[block(i), block(p)], do_ref[at, block(p)]
            back = []
            for e in range(2):
                side = left_half == (e == 0)
                q_half = jnp.where(side, queries, zero)
                do_half = jnp.where(side, douts, zero)
                h = 2 * p + e
                scores = dot_nt(keys if e == 0 else turned, q_half) * (scale * LOG2E)
                probs = jnp.exp2(jnp.where(allowed, scores, hidden_bias) - lse_ref[h : h + 1, at])
                dprobs = dot_nt(turned if e == 0 else keys, do_half)
                inner = jnp.sum(probs * dprobs, axis=0, keepdims=True)
                dscores = (probs * (dprobs - inner)).astype(jnp.bfloat16)
                dv_ref[window, :] = dv_ref[window, :] + dot_nn(probs.astype(jnp.bfloat16), do_half)
                dk_ref[window, :] = dk_ref[window, :] + dot_nn(dscores, q_half)
                back.append(dot_nn(key_t_ref[:, window], dscores))
            dq = jnp.concatenate(back, axis=0).T * scale
            dq_ref[at, block(p)] = rotate_tile(dq, cos_ref[block(i), :], -sin_ref[block(i), :]).astype(jnp.bfloat16)
    if not final:
        return
    for i in range(blocks):
        dk = dk_ref[block(i), :]
        dk = (dk + pltpu.roll(dk, HEAD_DIM, 1)) * scale
        dk = rotate_tile(dk, cos_ref[block(i), :], -sin_ref[block(i), :])
        dv = dv_ref[block(i), :]
        dv = dv + pltpu.roll(dv, HEAD_DIM, 1)
        dkv_ref[block(i), :] = jnp.where(left_half, dk, dv).astype(jnp.bfloat16)


def scan_back_kernel(
    chunks,
    heads,
    gmr_ref,
    gated_ref,
    inv_ref,
    dot_ref,
    gain_ref,
    gate_ref,
    y_ref,
    x_ref,
    xb_ref,
    state_ref,
    lag_ref,
    cum_row_ref,
    skip_ref,
    seg_col_ref,
    seg_row_ref,
    select_ref,
    dgate_ref,
    gy_ref,
    dx_ref,
    p_ref,
    grad_in_ref,
    grad_out_ref,
    skip_sum_ref,
    gyb_ref,
    wide_ref,
    cross_ref,
    bias_ref,
    dcross_ref,
    high_ref,
    rest_ref,
    inv_wide_ref,
    dot_wide_ref,
    inner_ref,
    mix_ref,
):
    first = chunks[0]
    half = len(chunks) * LEN
    sources = chunks[-1] + 1
    left_half = lane_iota() < HEAD_DIM
    zero = jnp.zeros((LEN, LEN), jnp.bfloat16)
    inv_wide_ref[...] = jnp.broadcast_to(inv_ref[...], (half, LEN))
    dot_wide_ref[...] = jnp.broadcast_to(dot_ref[...], (half, LEN))
    for h in range(heads):
        wide_ref[h] = jnp.broadcast_to(lag_ref[: sources * LEN, h : h + 1], (sources * LEN, LEN))
    spans = [(j, max(j, first), min(j + 3, sources)) for j in range(sources)]
    pairs = [(j, i) for j, start, stop in spans for i in range(start, stop)]
    for j, start, stop in spans:
        cross = three_dots(dot_nt, state_ref[block(j), :LEN], state_ref[start * LEN : stop * LEN, LEN:])
        for n, (j2, i) in enumerate(pairs):
            if j2 == j:
                cross_ref[n] = cross[:, block(i - start)]
                allowed = mask_st(seg_col_ref, seg_row_ref, j, i)
                bias_ref[n] = jnp.where(allowed, 0.0, hidden_bias)
                dcross_ref[n] = jnp.zeros((LEN, LEN), jnp.float32)

    def prelude(hp, _):
        lanes = pl.ds(pl.multiple_of(hp * LEN, LEN), LEN)
        skip = skip_ref[:, lanes]
        gain = gain_ref[:, lanes]
        skip_sum = jnp.zeros((1, LEN), jnp.float32)
        gain_sum = jnp.zeros((1, LEN), jnp.float32)
        for i in chunks:
            at = block(i - first)
            inv = inv_wide_ref[at, :]
            unit = gated_ref[at, lanes] * inv
            grad = inv * (gmr_ref[at, lanes] * gain - unit * dot_wide_ref[at, :])
            gate = gate_ref[block(i), lanes]
            sig = sigmoid(gate)
            y = y_ref[at, lanes]
            x = x_ref[block(i), lanes]
            gy = grad * (gate * sig)
            dgate_ref[at, lanes] = (grad * (y + skip * x) * (sig * (1.0 + gate * (1.0 - sig)))).astype(jnp.bfloat16)
            gyb = gy.astype(jnp.bfloat16)
            gy_ref[at, lanes] = gy
            gyb_ref[at, lanes] = gyb
            high_ref[at, lanes], rest_ref[at, lanes] = two_terms(gyb.astype(jnp.float32) * y)
            skip_sum = skip_sum + jnp.sum(gy * x, axis=0, keepdims=True)
            gain_sum = gain_sum + jnp.sum(gmr_ref[at, lanes] * unit, axis=0, keepdims=True)
        skip_sum_ref[0:1, lanes] = skip_sum
        skip_sum_ref[1:2, lanes] = gain_sum
        return 0

    lax.fori_loop(0, heads // 2, prelude, 0)
    p_ref[...] = dot_nt(select_ref[...], high_ref[...]) + dot_nt(select_ref[...], rest_ref[...])

    def head_pair(hp, _):
        lanes = pl.ds(pl.multiple_of(hp * LEN, LEN), LEN)
        for j, start, stop in spans:
            x_pair = xb_ref[block(j), lanes]
            x_both = jnp.concatenate([jnp.where(left_half, x_pair, zero), jnp.where(left_half, zero, x_pair)], axis=0)
            wide = (stop - start) * LEN
            gy_rows = gyb_ref[(start - first) * LEN : (stop - first) * LEN, lanes]
            inner_ref[:, :wide] = dot_nt(x_both, gy_rows)
            for n, (j2, i) in enumerate(pairs):
                if j2 != j:
                    continue
                grown = dcross_ref[n]
                for e in range(2):
                    spread = cum_row_ref[2 * hp + e, :, block(i)] - wide_ref[2 * hp + e, block(j), :]
                    decay = jnp.exp2(spread + bias_ref[n])
                    grown = grown + inner_ref[block(e), block(i - start)] * decay
                    mix_ref[block(e), block(i - start)] = (decay * cross_ref[n]).astype(jnp.bfloat16)
                dcross_ref[n] = grown
            both = dot_nn(mix_ref[:, :wide], gy_rows)
            dx_ref[block(j), lanes] = jnp.where(left_half, both[:LEN], both[LEN:])
        return 0

    lax.fori_loop(0, heads // 2, head_pair, 0)

    grad_out = {i: jnp.zeros((LEN, LEN), jnp.float32) for i in chunks}
    for j in range(sources):
        grad_in = jnp.zeros((LEN, LEN), jnp.float32)
        for n, (j2, i) in enumerate(pairs):
            if j2 != j:
                continue
            high, rest = two_terms(dcross_ref[n])
            out_high, out_rest = two_terms(state_ref[block(i), LEN:])
            in_high, in_rest = two_terms(state_ref[block(j), :LEN])
            grad_in = grad_in + dot_nn(high, out_high) + dot_nn(high, out_rest) + dot_nn(rest, out_high)
            grad_out[i] = grad_out[i] + dot_tn(high, in_high) + dot_tn(high, in_rest) + dot_tn(rest, in_high)
        grad_in_ref[block(j), :] = grad_in
    for i in chunks:
        grad_out_ref[block(i - first), :] = grad_out[i]


def conv_back(grad_ref, value_pad_ref, keep_ref, kernel_ref, out_ref, kernel_grad_ref, bias_grad_ref, lanes, blocks):
    taps = kernel_ref[:, lanes]
    totals = [jnp.zeros((1, LEN), jnp.float32) for _ in range(5)]
    for i in range(blocks):
        here = grad_ref[i * LEN : (i + 1) * LEN, lanes]
        grad = taps[3:4] * here
        totals[4] = totals[4] + jnp.sum(here, axis=0, keepdims=True)
        totals[3] = totals[3] + jnp.sum(here * value_pad_ref[8 + i * LEN : 8 + (i + 1) * LEN, lanes], axis=0, keepdims=True)
        for lag in (1, 2, 3):
            ahead = grad_ref[i * LEN + lag : (i + 1) * LEN + lag, lanes]
            grad = grad + taps[3 - lag : 4 - lag] * (ahead * keep_ref[lag - 1, i * LEN + lag : (i + 1) * LEN + lag, :])
            moved = value_pad_ref[8 + i * LEN - lag : 8 + (i + 1) * LEN - lag, lanes]
            masked = here * keep_ref[lag - 1, i * LEN : (i + 1) * LEN, :]
            totals[3 - lag] = totals[3 - lag] + jnp.sum(masked * moved, axis=0, keepdims=True)
        out_ref[block(i), lanes] = grad.astype(jnp.bfloat16)
    for tap in range(4):
        kernel_grad_ref[tap : tap + 1, lanes] = totals[tap]
    bias_grad_ref[0:1, lanes] = totals[4]


def scan_end_kernel(
    heads,
    gy_a_ref,
    gy_b_ref,
    dx_a_ref,
    dx_b_ref,
    p_a_ref,
    p_b_ref,
    in_a_ref,
    in_b_ref,
    out_a_ref,
    out_b_ref,
    xb_ref,
    slope_ref,
    state_slope_ref,
    conv_ref,
    small_ref,
    step_row_ref,
    sig_row_ref,
    rate_ref,
    skip_ref,
    keep_ref,
    seg_col_ref,
    seg_row_ref,
    select_ref,
    conv_kernel_ref,
    state_kernel_ref,
    dconv_ref,
    dstate_ref,
    dstep_ref,
    conv_kernel_sum_ref,
    conv_bias_sum_ref,
    state_kernel_sum_ref,
    state_bias_sum_ref,
    step_sum_ref,
    grad_pad_ref,
    value_pad_ref,
    state_grad_ref,
    state_value_ref,
    wide_ref,
    high_ref,
    rest_ref,
    flow_ref,
):
    rows, width = conv_ref.shape
    blocks = rows // LEN
    half = rows // 2
    value_pad_ref[0:8, :] = jnp.zeros((8, width), jnp.float32)
    value_pad_ref[8 : rows + 8, :] = conv_ref[...]
    grad_pad_ref[rows : rows + 8, :] = jnp.zeros((8, width), jnp.float32)
    state_value_ref[0:8, :] = jnp.zeros((8, 2 * LEN), jnp.float32)
    state_value_ref[8 : rows + 8, :] = small_ref[:, : 2 * LEN]
    state_grad_ref[rows : rows + 8, :] = jnp.zeros((8, 2 * LEN), jnp.float32)
    widen(keep_ref, wide_ref)

    def epilogue(hp, _):
        lanes = pl.ds(pl.multiple_of(hp * LEN, LEN), LEN)
        for j in range(blocks):
            dx = dx_b_ref[block(j), lanes]
            if j < blocks // 2:
                dx = dx + dx_a_ref[block(j), lanes]
                gy = gy_a_ref[block(j), lanes]
            else:
                gy = gy_b_ref[block(j - blocks // 2), lanes]
            high_ref[block(j), lanes], rest_ref[block(j), lanes] = two_terms(
                dx * xb_ref[block(j), lanes].astype(jnp.float32)
            )
            grad_pad_ref[block(j), lanes] = (dx + gy * skip_ref[:, lanes]) * slope_ref[block(j), lanes]
        conv_back(
            grad_pad_ref,
            value_pad_ref,
            wide_ref,
            conv_kernel_ref,
            dconv_ref,
            conv_kernel_sum_ref,
            conv_bias_sum_ref,
            lanes,
            blocks,
        )
        return 0

    lax.fori_loop(0, heads // 2, epilogue, 0)

    state_grad_ref[0:half, 0:LEN] = (in_a_ref[...] + in_b_ref[0:half, :]) * state_slope_ref[0:half, 0:LEN]
    state_grad_ref[half:rows, 0:LEN] = in_b_ref[half:rows, :] * state_slope_ref[half:rows, 0:LEN]
    state_grad_ref[0:half, LEN:] = out_a_ref[...] * state_slope_ref[0:half, LEN:]
    state_grad_ref[half:rows, LEN:] = out_b_ref[...] * state_slope_ref[half:rows, LEN:]
    for c in range(2):
        conv_back(
            state_grad_ref,
            state_value_ref,
            wide_ref,
            state_kernel_ref,
            dstate_ref,
            state_kernel_sum_ref,
            state_bias_sum_ref,
            block(c),
            blocks,
        )

    q = dot_nt(select_ref[...], high_ref[...]) + dot_nt(select_ref[...], rest_ref[...])
    flow_ref[:, 0:half] = p_a_ref[...] - q[:, 0:half]
    flow_ref[:, half:rows] = p_b_ref[...] - q[:, half:rows]
    rate = jnp.broadcast_to(rate_ref[...], (LEN, LEN)).T[: flow_ref.shape[0]]
    bias_total = jnp.zeros((flow_ref.shape[0], LEN), jnp.float32)
    decay_total = jnp.zeros((flow_ref.shape[0], LEN), jnp.float32)
    step_sum_ref[...] = jnp.zeros(step_sum_ref.shape, jnp.float32)
    for j in range(blocks):
        log_grad = jnp.zeros((flow_ref.shape[0], LEN), jnp.float32)
        for i in range(j, min(j + 3, blocks)):
            chosen = jnp.where(mask_st(seg_col_ref, seg_row_ref, j, i), 1.0, 0.0).astype(jnp.bfloat16)
            high, rest = two_terms(flow_ref[:, block(i)])
            log_grad = log_grad + dot_nt(high, chosen) + dot_nt(rest, chosen)
        step = step_row_ref[:, block(j)]
        grad_step = jnp.where(step > 1e-30, q[:, block(j)] / step, 0.0) + log_grad * rate
        grad_arg = grad_step * sig_row_ref[:, block(j)]
        bias_total = bias_total + grad_arg
        decay_total = decay_total + log_grad * step
        tall = jnp.concatenate([grad_arg, jnp.zeros((LEN - grad_arg.shape[0], LEN), jnp.float32)], axis=0)
        dstep_ref[block(j), :] = tall.T.astype(jnp.bfloat16)
    count = flow_ref.shape[0]
    step_sum_ref[0:count, :] = jnp.broadcast_to(jnp.sum(bias_total, axis=1, keepdims=True), (count, LEN))
    step_sum_ref[count : 2 * count, :] = jnp.broadcast_to(
        jnp.sum(decay_total * rate, axis=1, keepdims=True), (count, LEN)
    )


def vmem(count):
    return [pl.BlockSpec(memory_space=pltpu.VMEM)] * count


def call(kernel, out_shape, scratch, operands, flops):
    moved = sum(o.size * o.dtype.itemsize for o in operands) + sum(o.size * o.dtype.itemsize for o in out_shape)
    return pl.pallas_call(
        kernel,
        out_shape=out_shape,
        in_specs=vmem(len(operands)),
        out_specs=vmem(len(out_shape)),
        scratch_shapes=scratch,
        compiler_params=pltpu.CompilerParams(vmem_limit_bytes=40 * 1024 * 1024),
        cost_estimate=pl.CostEstimate(flops=flops, bytes_accessed=moved, transcendentals=0),
    )(*operands)


def f32(*shape):
    return jax.ShapeDtypeStruct(shape, jnp.float32)


def b16(*shape):
    return jax.ShapeDtypeStruct(shape, jnp.bfloat16)


HEAD_ROWS = 16


def scan_prep(conv_in, small, *rest):
    rows, width = conv_in.shape
    outs = [
        f32(rows, width),
        b16(rows, width),
        f32(rows, width),
        f32(rows, 2 * LEN),
        f32(rows, 2 * LEN),
        f32(rows, LEN),
        f32(rows, LEN),
        f32(HEAD_ROWS, 1, rows),
        f32(HEAD_ROWS, 1, rows),
        f32(HEAD_ROWS, rows),
        f32(HEAD_ROWS, rows),
        b16(rows, 2 * LEN),
        b16(rows, LEN),
    ]
    scratch = [
        pltpu.VMEM((rows + 8, width), jnp.float32),
        pltpu.VMEM((rows + 8, 2 * LEN), jnp.float32),
        pltpu.VMEM((3, rows + 8, LEN), jnp.float32),
    ]
    return call(prep_kernel, outs, scratch, (conv_in, small, *rest), 10**9)


def scan_forward(chunks, heads, *operands):
    width = operands[0].shape[1]
    rows = LEN * len(chunks)
    count = sum(min(i, 2) + 1 for i in chunks)
    outs = [f32(rows, width), f32(rows, width), f32(1, rows)]
    scratch = [
        pltpu.VMEM((heads, rows, LEN), jnp.float32),
        pltpu.VMEM((count, LEN, LEN), jnp.float32),
        pltpu.VMEM((count, LEN, LEN), jnp.float32),
        pltpu.VMEM((2 * LEN, 3 * LEN), jnp.bfloat16),
        pltpu.VMEM((rows, LEN), jnp.float32),
    ]
    return call(functools.partial(scan_kernel, chunks, heads), outs, scratch, operands, 2 * 10**9)


def attention_forward(chunks, q, kv, seg_col, seg_row):
    rows = LEN * len(chunks)
    outs = [b16(rows, q.shape[1]), f32(8, rows)]
    return call(functools.partial(attention_kernel, chunks), outs, [], (q, kv, seg_col, seg_row), 10**9)


def attention_backward(chunks, final, *operands):
    q = operands[0]
    rows = q.shape[0]
    partial = [f32(rows, LEN), f32(rows, LEN)]
    sums = [pltpu.VMEM((rows, LEN), jnp.float32)] * 2
    outs = [b16(LEN * len(chunks), q.shape[1])] + ([b16(rows, LEN)] if final else partial)
    scratch = (sums if final else []) + [
        pltpu.VMEM((rows, LEN), jnp.bfloat16),
        pltpu.VMEM((HEAD_DIM, rows), jnp.bfloat16),
    ]
    return call(functools.partial(attention_back_kernel, chunks, final), outs, scratch, operands, 2 * 10**9)


def scan_backward(chunks, heads, *operands):
    rows, width = operands[0].shape
    sources = (chunks[-1] + 1) * LEN
    count = sum(min(i, 2) + 1 for i in chunks)
    outs = [
        b16(rows, width),
        f32(rows, width),
        f32(sources, width),
        f32(HEAD_ROWS, rows),
        f32(sources, LEN),
        f32(rows, LEN),
        f32(8, width),
    ]
    scratch = [
        pltpu.VMEM((rows, width), jnp.bfloat16),
        pltpu.VMEM((heads, sources, LEN), jnp.float32),
        pltpu.VMEM((count, LEN, LEN), jnp.float32),
        pltpu.VMEM((count, LEN, LEN), jnp.float32),
        pltpu.VMEM((count, LEN, LEN), jnp.float32),
        pltpu.VMEM((rows, width), jnp.bfloat16),
        pltpu.VMEM((rows, width), jnp.bfloat16),
        pltpu.VMEM((rows, LEN), jnp.float32),
        pltpu.VMEM((rows, LEN), jnp.float32),
        pltpu.VMEM((2 * LEN, 3 * LEN), jnp.float32),
        pltpu.VMEM((2 * LEN, 3 * LEN), jnp.bfloat16),
    ]
    return call(functools.partial(scan_back_kernel, chunks, heads), outs, scratch, operands, 4 * 10**9)


def scan_end(heads, *operands):
    gy = operands[0]
    rows, width = 2 * gy.shape[0], gy.shape[1]
    outs = [
        b16(rows, width),
        b16(rows, 2 * LEN),
        b16(rows, LEN),
        f32(8, width),
        f32(8, width),
        f32(8, 2 * LEN),
        f32(8, 2 * LEN),
        f32(2 * HEAD_ROWS, LEN),
    ]
    scratch = [
        pltpu.VMEM((rows + 8, width), jnp.float32),
        pltpu.VMEM((rows + 8, width), jnp.float32),
        pltpu.VMEM((rows + 8, 2 * LEN), jnp.float32),
        pltpu.VMEM((rows + 8, 2 * LEN), jnp.float32),
        pltpu.VMEM((3, rows + 8, LEN), jnp.float32),
        pltpu.VMEM((rows, width), jnp.bfloat16),
        pltpu.VMEM((rows, width), jnp.bfloat16),
        pltpu.VMEM((HEAD_ROWS, rows), jnp.float32),
    ]
    return call(functools.partial(scan_end_kernel, heads), outs, scratch, operands, 2 * 10**9)


def silu_slope(argument):
    logistic = jax.nn.sigmoid(argument)
    return logistic * (1.0 + argument * (1.0 - logistic))


def rope_tables(rows):
    half_size = HEAD_DIM // 2
    inverse = np.float32(rope_base) ** (-(2.0 * np.arange(half_size, dtype=np.float32)) / HEAD_DIM)
    angles = np.arange(rows, dtype=np.float32)[:, None] * inverse.astype(np.float32)[None, :]
    cosine, sine = np.cos(angles), np.sin(angles)
    return (
        np.concatenate([cosine] * 4, axis=1).astype(np.float32),
        np.concatenate([-sine, sine, -sine, sine], axis=1).astype(np.float32),
    )


def norm_backward(grad_unit, unit_rows, inv_rms):
    return inv_rms * (grad_unit - unit_rows * jnp.mean(grad_unit * unit_rows, axis=-1, keepdims=True))


def dot32(left, right):
    return jnp.dot(left, right, preferred_element_type=jnp.float32)


def swap(values, name):
    return lax.ppermute(values, name, PAIR)


def exchange(values, name):
    return values + swap(values, name)


def take(values, index, axis):
    return lax.dynamic_slice_in_dim(values, index, 1, axis)


def first_halving(values, name, axis, link):
    place = lax.axis_index(name)
    if link == "A":
        side = ((place + 1) // 2) % 2
        kept = jnp.concatenate([take(values, side, axis), take(values, 3 - side, axis)], axis)
        sent = jnp.concatenate([take(values, 1 - side, axis), take(values, 2 + side, axis)], axis)
    else:
        side = place // 2
        kept = lax.dynamic_slice_in_dim(values, 2 * side, 2, axis)
        sent = lax.dynamic_slice_in_dim(values, 2 - 2 * side, 2, axis)
    return kept + lax.ppermute(sent, name, LINKS[link])


def second_halving(values, name, axis, link):
    place = lax.axis_index(name)
    index = place // 2 if link == "B" else place % 2
    sent = take(values, 1 - index, axis)
    return take(values, index, axis) + lax.ppermute(sent, name, LINKS[link])


def either(chosen, first, second, axis):
    return jnp.where(chosen, jnp.concatenate([first, second], axis), jnp.concatenate([second, first], axis))


def second_doubling(values, name, axis, link):
    place = lax.axis_index(name)
    index = place // 2 if link == "B" else place % 2
    return either(index == 0, values, lax.ppermute(values, name, LINKS[link]), axis)


def first_doubling(values, name, axis, link):
    place = lax.axis_index(name)
    other = lax.ppermute(values, name, LINKS[link])
    if link == "B":
        return either(place // 2 == 0, values, other, axis)
    side = ((place + 1) // 2) % 2 == 0
    own = [lax.slice_in_dim(values, k, k + 1, axis=axis) for k in range(2)]
    far = [lax.slice_in_dim(other, k, k + 1, axis=axis) for k in range(2)]
    return jnp.where(
        side,
        jnp.concatenate([own[0], far[0], far[1], own[1]], axis),
        jnp.concatenate([far[0], own[0], own[1], far[1]], axis),
    )


def part_sizes(columns):
    tiles = columns // LEN
    return [LEN * (tiles // 4 + (1 if k < tiles % 4 else 0)) for k in range(4)]


def split_columns(values):
    parts, start = [], 0
    for size in part_sizes(values.shape[-1]):
        parts.append(values[..., start : start + size])
        start += size
    return parts


def reduce_blocks(values):
    count, rows, columns = values.shape
    parts = split_columns(values.reshape(count, 4, 2, 4, rows // 32, columns))
    for step in range(4):
        for k in range(4):
            name, link = ORDERS[k][step]
            seen = [n for n, _ in ORDERS[k][:step]]
            halving = second_halving if name in seen else first_halving
            parts[k] = halving(parts[k], name, AXIS[name], link)
    merged = jnp.concatenate(parts, axis=-1)
    place = lax.axis_index("zh")
    own = take(merged, place, 2) + swap(take(merged, 1 - place, 2), "zh")
    return own.reshape(count, rows // 32, columns)


def gather_rows(values):
    rows, columns = values.shape
    merged = values.reshape(1, 1, 1, 1, rows, columns)
    merged = either(lax.axis_index("zh") == 0, merged, swap(merged, "zh"), 2)
    parts = split_columns(merged)
    for step in reversed(range(4)):
        for k in range(4):
            name, link = ORDERS[k][step]
            seen = [n for n, _ in ORDERS[k][:step]]
            doubling = second_doubling if name in seen else first_doubling
            parts[k] = doubling(parts[k], name, AXIS[name], link)
    merged = jnp.concatenate(parts, axis=-1).reshape(32 * rows, columns)
    return either(lax.axis_index("core") == 0, merged, swap(merged, "core"), 0)


def core_rows(values, index):
    half = values.shape[1] // 2
    return lax.dynamic_slice_in_dim(values, index * half, half, 1)


def core_dot(left, right):
    place = lax.axis_index("core")

    def rows_of(index):
        return lax.dot_general(
            core_rows(left, index), right, (((0,), (0,)), ((), ())), preferred_element_type=jnp.float32
        )

    return rows_of(place) + swap(rows_of(1 - place), "core")


def on_device(
    layer_input,
    segments,
    input_gain,
    mixer_proj,
    state_proj,
    step_proj,
    step_bias,
    decay_log,
    skip_gain,
    conv_kernel,
    conv_bias,
    state_kernel,
    state_bias,
    gated_gain,
    mixer_out,
    query_proj,
    key_value_weight,
    attn_out,
    ffn_gain,
    ffn_gate,
    ffn_up,
    ffn_down,
    cotangent,
):
    segment = segments.reshape(-1)
    rows, model_width = layer_input.shape
    width = mixer_proj.shape[2]
    heads = step_proj.shape[1]
    state_size = state_proj.shape[1] // 2
    query_width = query_proj.shape[1]
    pair_width = key_value_weight.shape[2]
    cosine, sine = rope_tables(rows)
    select = np.arange(HEAD_ROWS)[:, None] == np.arange(width)[None, :] // HEAD_DIM
    select = jnp.asarray(select.astype(np.float32)).astype(jnp.bfloat16)
    seg_col, seg_row = segment[:, None], segment[None, :]
    keep = [jnp.ones((rows,), jnp.float32)]
    for lag in (1, 2, 3):
        previous = jnp.concatenate([jnp.full((lag,), -1, jnp.int32), segment[:-lag]])
        keep.append((previous == segment).astype(jnp.float32))
    keep = jnp.pad(jnp.stack(keep, axis=1), ((0, 8), (0, 4)))
    pad_heads = ((0, 0), (0, LEN - heads))
    rate_row = jnp.pad(-jnp.exp(decay_log)[None, :], pad_heads)
    step_bias_row = jnp.pad(step_bias[None, :], pad_heads)
    skip_row = jnp.repeat(skip_gain, HEAD_DIM)[None, :]
    gain_row = gated_gain[None, :]
    gate_proj, channel_proj = mixer_proj[:, 0, :], mixer_proj[:, 1, :]
    small_proj = jnp.concatenate(
        [
            state_proj,
            query_proj,
            key_value_weight.reshape(model_width, pair_width),
            step_proj,
            jnp.zeros((model_width, LEN - heads), jnp.bfloat16),
        ],
        axis=1,
    )

    tokens = layer_input.astype(jnp.float32)
    inv_rms_in = lax.rsqrt(jnp.mean(tokens * tokens, axis=-1, keepdims=True) + norm_eps)
    unit_in = tokens * inv_rms_in
    normed_input = (unit_in * input_gain).astype(jnp.bfloat16)
    small_in = dot32(normed_input, small_proj)
    conv_in = dot32(normed_input, channel_proj)
    gate_branch = dot32(normed_input, gate_proj)
    x, xb, slope, state, state_slope, cum, lag, cum_row, lag_row, step_row, sig_row, queries, pairs = scan_prep(
        conv_in,
        small_in,
        cosine,
        sine,
        keep,
        conv_kernel,
        conv_bias[None, :],
        state_kernel,
        state_bias[None, :],
        step_bias_row,
        rate_row,
    )

    blocks = rows // LEN
    late = tuple(range(blocks // 2, blocks))
    early = tuple(range(blocks // 2))
    half = {}
    for chunks in (late, early):
        span = slice(chunks[0] * LEN, (chunks[-1] + 1) * LEN)
        h = {"span": span}
        h["y"], h["gated"], squares = scan_forward(
            chunks, heads, gate_branch, x, xb, state, cum, lag_row, seg_col, seg_row, skip_row
        )
        h["attended"], h["lse"] = attention_forward(chunks, queries, pairs, seg_col, seg_row)
        squares = exchange(squares, "tensor")
        h["inv_gated"] = lax.rsqrt(squares.reshape(-1, 1) / DSSM + norm_eps)
        h["mixer_rows"] = (h["gated"] * h["inv_gated"] * gated_gain).astype(jnp.bfloat16)
        h["branch"] = exchange(dot32(h["mixer_rows"], mixer_out) + dot32(h["attended"], attn_out), "tensor")
        half[chunks] = h

    for chunks in (late, early):
        h = half[chunks]
        span = h["span"]
        hidden = tokens[span] + h["branch"]
        inv_rms_ffn = lax.rsqrt(jnp.mean(hidden * hidden, axis=-1, keepdims=True) + norm_eps)
        unit_ffn = hidden * inv_rms_ffn
        normed_ffn = (unit_ffn * ffn_gain).astype(jnp.bfloat16)
        gate_rows = dot32(normed_ffn, ffn_gate)
        up_rows = dot32(normed_ffn, ffn_up)
        gate_silu = jax.nn.silu(gate_rows)
        activated = (gate_silu * up_rows).astype(jnp.bfloat16)
        grad_activated = dot32(cotangent[span], ffn_down.T)
        grad_gate_rows = (grad_activated * up_rows * silu_slope(gate_rows)).astype(jnp.bfloat16)
        grad_up_rows = (grad_activated * gate_silu).astype(jnp.bfloat16)
        partial_ffn = dot32(grad_gate_rows, ffn_gate.T) + dot32(grad_up_rows, ffn_up.T)
        h["grad_normed_ffn"] = exchange(partial_ffn, "tensor")
        h["down"] = dot32(activated, ffn_down)
        h.update(
            hidden=hidden,
            unit_ffn=unit_ffn,
            inv_rms_ffn=inv_rms_ffn,
            normed_ffn=normed_ffn,
            activated=activated,
            grad_gate_rows=grad_gate_rows,
            grad_up_rows=grad_up_rows,
        )

    def whole(name):
        return jnp.concatenate([half[early][name], half[late][name]], axis=0)

    normed_ffn = whole("normed_ffn")
    first = reduce_blocks(
        jnp.stack(
            [
                core_dot(normed_ffn, whole("grad_gate_rows")),
                core_dot(normed_ffn, whole("grad_up_rows")),
                core_dot(whole("activated"), cotangent),
            ]
        )
    )
    first = lax.all_gather(first, ("core", "y", "zh", "x"), axis=1, tiled=True)

    grad_ffn_gain = 0.0
    for chunks in (late, early):
        h = half[chunks]
        span = h["span"]
        grad_ffn_gain = grad_ffn_gain + jnp.sum(h["grad_normed_ffn"] * h["unit_ffn"], axis=0)
        h["grad_hidden"] = cotangent[span].astype(jnp.float32) + norm_backward(
            h["grad_normed_ffn"] * ffn_gain, h["unit_ffn"], h["inv_rms_ffn"]
        )
        grad_branch = h["grad_hidden"].astype(jnp.bfloat16)
        h["grad_branch"] = grad_branch
        grad_mixer_rows = dot32(grad_branch, mixer_out.T)
        unit_gated = h["gated"] * h["inv_gated"]
        gated_dot = exchange(jnp.sum(grad_mixer_rows * gated_gain * unit_gated, axis=-1)[None, :], "tensor")
        grad_attended = dot32(grad_branch, attn_out.T).astype(jnp.bfloat16)
        operands = (queries, pairs, grad_attended, h["lse"], seg_col, seg_row, cosine, sine)
        if chunks == late:
            h["grad_queries"], grad_keys, grad_values = attention_backward(chunks, False, *operands)
        else:
            h["grad_queries"], grad_pairs = attention_backward(chunks, True, *operands, grad_keys, grad_values)
        h["grad_gate"], h["gy"], h["dx"], h["p"], h["grad_in"], h["grad_out"], h["sums"] = scan_backward(
            chunks,
            heads,
            grad_mixer_rows,
            h["gated"],
            h["inv_gated"],
            gated_dot.reshape(-1, 1) / DSSM,
            gain_row,
            gate_branch,
            h["y"],
            x,
            xb,
            state,
            lag,
            cum_row,
            skip_row,
            seg_col,
            seg_row,
            select,
        )
    ends = []
    for name in ("gy", "dx", "p", "grad_in", "grad_out"):
        ends += [half[early][name], half[late][name]]
    grad_conv, grad_state, grad_step, conv_kernel_sum, conv_bias_sum, state_kernel_sum, state_bias_sum, step_sum = scan_end(
        heads,
        *ends,
        xb,
        slope,
        state_slope,
        conv_in,
        small_in,
        step_row,
        sig_row,
        rate_row,
        skip_row,
        keep,
        seg_col,
        seg_row,
        select,
        conv_kernel,
        state_kernel,
    )

    left = jnp.concatenate([whole("mixer_rows"), whole("attended")], axis=1)
    right = jnp.concatenate([whole("grad_gate"), whole("grad_queries"), grad_pairs], axis=1)
    second = jnp.concatenate([core_dot(left, whole("grad_branch")), core_dot(normed_input, right)], axis=1)
    second = gather_rows(reduce_blocks(second[None])[0])

    grad_small = jnp.concatenate([grad_state, whole("grad_queries"), grad_pairs, grad_step], axis=1)
    partial_normed = (
        dot32(whole("grad_gate"), gate_proj.T) + dot32(grad_small, small_proj.T) + dot32(grad_conv, channel_proj.T)
    )
    sums = half[early]["sums"] + half[late]["sums"]
    over_tensor = [jnp.sum(partial_normed * unit_in, axis=0), state_kernel_sum[:4], state_bias_sum[0]]
    alone = [
        step_sum[:heads, 0],
        step_sum[HEAD_ROWS : HEAD_ROWS + heads, 0],
        jnp.sum(sums[0].reshape(heads, HEAD_DIM), axis=1),
        conv_kernel_sum[:4],
        conv_bias_sum[0],
        sums[1],
        grad_ffn_gain,
    ]

    def packed(values):
        flat = jnp.concatenate([v.reshape(-1) for v in values])
        count = -(-flat.shape[0] // model_width)
        return jnp.pad(flat, (0, count * model_width - flat.shape[0])).reshape(count, model_width)

    def unpacked(table, values):
        flat, result, start = table.T.reshape(-1), [], 0
        for v in values:
            result.append(flat[start : start + v.size].reshape(v.shape))
            start += v.size
        return result

    tables = [packed(over_tensor), packed(alone)]
    shared_end = heads + tables[0].shape[0]
    table = jnp.concatenate(tables, axis=0)
    table_end = heads + table.shape[0]
    place = lax.axis_index("core")
    table = (core_rows(table, place) + swap(core_rows(table, 1 - place), "core")).T
    third = core_dot(normed_input, jnp.concatenate([grad_conv, grad_state, grad_step], axis=1))
    at_state, at_step = width, width + 2 * state_size
    third = third + jnp.pad(table, ((0, 0), (at_step + heads, LEN - table_end)))
    third = reduce_blocks(third[None])[0]
    both = third[:, at_state:]
    summed = exchange(both, "tensor")
    lane = np.arange(both.shape[1]) - 2 * state_size
    is_shared = (lane < 0) | ((lane >= heads) & (lane < shared_end))
    third = jnp.concatenate([third[:, :at_state], jnp.where(is_shared[None, :], summed, both)], axis=1)
    third = gather_rows(third)

    grad_normed = exchange(partial_normed, "tensor")
    grad_hidden = whole("grad_hidden")
    input_grad = grad_hidden + norm_backward(grad_normed * input_gain, unit_in, inv_rms_in)
    layer_output = (whole("hidden") + exchange(whole("down"), "tensor")).astype(jnp.bfloat16)

    small_shared = unpacked(third[:, at_step + heads : at_step + shared_end], over_tensor)
    small_alone = unpacked(third[:, at_step + shared_end : at_step + table_end], alone)
    at_gate = model_width
    at_query = at_gate + width
    at_pair = at_query + query_width
    return (
        layer_output,
        input_grad,
        small_shared[0],
        jnp.stack([second[:, at_gate:at_query], third[:, :width]], axis=1),
        third[:, at_state:at_step],
        third[:, at_step : at_step + heads],
        small_alone[0],
        small_alone[1],
        small_alone[2],
        small_alone[3],
        small_alone[4],
        small_shared[1],
        small_shared[2],
        small_alone[5],
        second[:width, :model_width],
        second[:, at_query:at_pair],
        second[:, at_pair:].reshape(key_value_weight.shape),
        second[width:, :model_width],
        small_alone[6],
        first[0],
        first[1],
        first[2],
    )


def solution(mesh):
    dp, whole_spec, columns = P(DP, None), P(), P(None, "tensor")
    per_channel, middle = P("tensor"), P(None, "tensor", None)
    last, by_rows = P(None, None, "tensor"), P("tensor", None)
    weights = (
        whole_spec,
        last,
        whole_spec,
        columns,
        per_channel,
        per_channel,
        per_channel,
        columns,
        per_channel,
        whole_spec,
        whole_spec,
        per_channel,
        by_rows,
        columns,
        middle,
        by_rows,
        whole_spec,
        columns,
        columns,
        by_rows,
    )
    mesh = jax.sharding.Mesh(mesh.devices.reshape(4, 2, 4, 2, 2), (*DP, "tensor"))
    return jax.shard_map(
        on_device, mesh=mesh, in_specs=(dp, dp, *weights, dp), out_specs=(dp, dp, *weights), check_vma=False
    )
```

```python
import functools

import jax
import jax.numpy as jnp
import numpy as np
from jax import lax
from jax.experimental import pallas as pl
from jax.experimental.pallas import tpu as pltpu
from jax.sharding import PartitionSpec as P

HEAD_DIM = 64
DSSM = 1536
DP = ("y", "zh", "x", "core")
PAIR = [(0, 1), (1, 0)]
LOG2E = 1.4426950408889634
hidden_bias = -1e30
norm_eps = 1e-05
rope_base = 10000.0
LEN = 128


def dot_nn(left, right):
    return lax.dot_general(
        left, right, (((1,), (0,)), ((), ())), preferred_element_type=jnp.float32
    )


def dot_nt(left, right):
    return lax.dot_general(
        left, right, (((1,), (1,)), ((), ())), preferred_element_type=jnp.float32
    )


def dot_tn(left, right):
    return lax.dot_general(
        left, right, (((0,), (0,)), ((), ())), preferred_element_type=jnp.float32
    )


def two_terms(v):
    high = v.astype(jnp.bfloat16)
    return high, (v - high.astype(jnp.float32)).astype(jnp.bfloat16)


def three_dots(dot, left, right):
    left_high, left_low = two_terms(left)
    right_high, right_low = two_terms(right)
    return dot(left_high, right_high) + dot(left_high, right_low) + dot(left_low, right_high)


def sigmoid(v):
    return 1.0 / (1.0 + jnp.exp(-v))


def block(index):
    return slice(index * LEN, (index + 1) * LEN)


def lane_iota(rows=LEN):
    return lax.broadcasted_iota(jnp.int32, (rows, LEN), 1)


def mask_ts(seg_col, seg_row, i, j):
    same = seg_col[block(i), :] == seg_row[:, block(j)]
    if i != j:
        return same
    down = lax.broadcasted_iota(jnp.int32, (LEN, LEN), 0)
    return same & (down >= lane_iota())


def mask_st(seg_col, seg_row, j, i):
    same = seg_col[block(j), :] == seg_row[:, block(i)]
    if i != j:
        return same
    down = lax.broadcasted_iota(jnp.int32, (LEN, LEN), 0)
    return same & (down <= lane_iota())


def conv_rows(pad_ref, keep_ref, kernel, bias, start, lanes):
    summed = bias + kernel[3:4] * pad_ref[8 + start : 8 + start + LEN, lanes]
    for lag in (1, 2, 3):
        moved = pad_ref[8 + start - lag : 8 + start - lag + LEN, lanes]
        summed = summed + kernel[3 - lag : 4 - lag] * (moved * keep_ref[lag - 1, start : start + LEN, :])
    return summed


def widen(keep_ref, wide_ref):
    rows = keep_ref.shape[0]
    for lag in (1, 2, 3):
        wide_ref[lag - 1, :, :] = jnp.broadcast_to(keep_ref[:, lag : lag + 1], (rows, LEN))


def prep_kernel(
    conv_ref,
    small_ref,
    cos_ref,
    sin_ref,
    keep_ref,
    conv_kernel_ref,
    conv_bias_ref,
    state_kernel_ref,
    state_bias_ref,
    step_bias_ref,
    rate_ref,
    x_ref,
    xb_ref,
    slope_ref,
    state_ref,
    state_slope_ref,
    cum_ref,
    lag_ref,
    cum_row_ref,
    lag_row_ref,
    step_row_ref,
    sig_row_ref,
    q_ref,
    kv_ref,
    pad_ref,
    wide_ref,
):
    rows = conv_ref.shape[0]
    blocks = rows // LEN

    @pl.when(pl.program_id(0) == 0)
    def _():
        pad_ref[0:8, :] = jnp.zeros((8, LEN), jnp.float32)
        widen(keep_ref, wide_ref)
        for c in range(2):
            pad_ref[8 : rows + 8, :] = small_ref[:, block(c)]
            for i in range(blocks):
                pre = conv_rows(
                    pad_ref, wide_ref, state_kernel_ref[:, block(c)], state_bias_ref[:, block(c)], i * LEN, slice(0, LEN)
                )
                sig = sigmoid(pre)
                state_ref[block(i), block(c)] = pre * sig
                state_slope_ref[block(i), block(c)] = sig * (1.0 + pre * (1.0 - sig))

    @pl.when(pl.program_id(0) == 1)
    def _():
        down = lax.broadcasted_iota(jnp.int32, (LEN, LEN), 0)
        lower = jnp.where(down >= lane_iota(), 1.0, 0.0).astype(jnp.bfloat16)
        left_half = lane_iota() < HEAD_DIM
        carry = jnp.zeros((1, LEN), jnp.float32)
        heads = cum_row_ref.shape[0]
        for i in range(blocks):
            argument = small_ref[block(i), block(5)] + step_bias_ref[...]
            tail = jnp.exp(-jnp.abs(argument))
            grown = jnp.where(tail < 1e-3, tail - 0.5 * tail * tail, jnp.log(1.0 + tail))
            step = jnp.maximum(argument, 0.0) + grown
            scaled = step * rate_ref[...] * LOG2E
            first, rest = two_terms(scaled)
            last = scaled - first.astype(jnp.float32) - rest.astype(jnp.float32)
            cum = dot_nn(lower, first) + dot_nn(lower, rest) + dot_nn(lower, last.astype(jnp.bfloat16)) + carry
            carry = cum[LEN - 1 : LEN, :]
            lag = cum - jnp.log(step) * LOG2E
            cum_ref[block(i), :] = cum
            lag_ref[block(i), :] = lag
            cum_t, lag_t = cum.T, lag.T
            step_row_ref[:, block(i)] = step.T[:heads]
            sig_row_ref[:, block(i)] = sigmoid(argument).T[:heads]
            for h in range(heads):
                cum_row_ref[h, :, block(i)] = cum_t[h : h + 1]
                lag_row_ref[h, :, block(i)] = lag_t[h : h + 1]
            cosine, sine = cos_ref[block(i), :], sin_ref[block(i), :]
            kv = small_ref[block(i), block(4)]
            kv_ref[block(i), :] = jnp.where(left_half, rotate_tile(kv, cosine, sine), kv).astype(jnp.bfloat16)
            for p in range(q_ref.shape[1] // LEN):
                q_ref[block(i), block(p)] = rotate_tile(small_ref[block(i), block(2 + p)], cosine, sine).astype(
                    jnp.bfloat16
                )

    for sub in range(GROUP):
        lanes = block(sub)
        pad_ref[8 : rows + 8, :] = conv_ref[:, lanes]
        for i in range(blocks):
            pre = conv_rows(pad_ref, wide_ref, conv_kernel_ref[:, lanes], conv_bias_ref[:, lanes], i * LEN, slice(0, LEN))
            sig = sigmoid(pre)
            x = pre * sig
            x_ref[block(i), lanes] = x
            xb_ref[block(i), lanes] = x.astype(jnp.bfloat16)
            slope_ref[block(i), lanes] = sig * (1.0 + pre * (1.0 - sig))


def rotate_tile(v, cosine, sine):
    first = lax.rem(lane_iota(v.shape[0]), HEAD_DIM) < HEAD_DIM // 2
    swapped = jnp.where(first, pltpu.roll(v, LEN - HEAD_DIM // 2, 1), pltpu.roll(v, HEAD_DIM // 2, 1))
    return v * cosine + swapped * sine


def scan_kernel(
    chunks,
    heads,
    gate_ref,
    x_ref,
    xb_ref,
    state_ref,
    cum_ref,
    lag_row_ref,
    seg_col_ref,
    seg_row_ref,
    skip_ref,
    y_ref,
    gated_ref,
    row_ref,
    wide_ref,
    cross_ref,
    bias_ref,
    mix_ref,
    square_ref,
):
    step = pl.program_id(0)
    first = chunks[0]
    pairs = [(i, j) for i in chunks for j in range(max(0, i - 2), i + 1)]
    left_half = lane_iota() < HEAD_DIM

    @pl.when(step == 0)
    def _():
        for h in range(heads):
            for i in chunks:
                wide_ref[h, block(i - first), :] = jnp.broadcast_to(cum_ref[block(i), h : h + 1], (LEN, LEN))
        for i in chunks:
            low = max(0, i - 2)
            cross = three_dots(dot_nt, state_ref[block(i), LEN:], state_ref[low * LEN : (i + 1) * LEN, :LEN])
            for n, (i2, j) in enumerate(pairs):
                if i2 == i:
                    cross_ref[n] = cross[:, block(j - low)]
                    allowed = mask_ts(seg_col_ref, seg_row_ref, i, j)
                    bias_ref[n] = jnp.where(allowed, 0.0, hidden_bias)
        square_ref[...] = jnp.zeros(square_ref.shape, jnp.float32)

    tiles = (gate_ref, x_ref, xb_ref, skip_ref, y_ref, gated_ref)

    def head_pair(hp, gate_ref, x_ref, xb_ref, skip_ref, y_ref, gated_ref):
        for i in chunks:
            at = block(i - first)
            low = max(0, i - 2)
            for n, (i2, j) in enumerate(pairs):
                if i2 != i:
                    continue
                for e in range(2):
                    spread = wide_ref[2 * hp + e, at, :] - lag_row_ref[2 * hp + e, :, block(j)]
                    decay = jnp.exp2(spread + bias_ref[n])
                    mix_ref[i - first, block(e), block(j - low)] = (decay * cross_ref[n]).astype(jnp.bfloat16)
            both = dot_nn(mix_ref[i - first, :, : (i + 1 - low) * LEN], xb_ref[low * LEN : (i + 1) * LEN, :])
            y = jnp.where(left_half, both[:LEN], both[LEN:])
            y_ref[at, :] = y
            gate = gate_ref[at, :]
            gated = (y + skip_ref[...] * x_ref[at, :]) * (gate * sigmoid(gate))
            gated_ref[at, :] = gated
            square_ref[at, :] = square_ref[at, :] + gated * gated

    for sub in range(GROUP):
        head_pair(GROUP * step + sub, *[t.at[:, block(sub)] for t in tiles])

    @pl.when(step == pl.num_programs(0) - 1)
    def _():
        for i in chunks:
            at = block(i - first)
            total = jnp.sum(square_ref[at, :], axis=1, keepdims=True)
            row_ref[0:1, at] = jnp.broadcast_to(total, (LEN, LEN)).T[0:1]


def attention_kernel(chunks, q_ref, kv_ref, seg_col_ref, seg_row_ref, out_ref, lse_ref):
    scale = HEAD_DIM ** (-0.5) * LOG2E
    first = chunks[0]
    left_half = lane_iota() < HEAD_DIM
    zero = jnp.zeros((LEN, LEN), jnp.bfloat16)
    lse_ref[...] = jnp.zeros(lse_ref.shape, jnp.float32)
    for i in chunks:
        at = block(i - first)
        low = max(0, i - 2) * LEN
        span = (i + 1) * LEN - low
        allowed = jnp.concatenate([mask_ts(seg_col_ref, seg_row_ref, i, j) for j in range(low // LEN, i + 1)], axis=1)
        keys = kv_ref[low : low + span, :]
        turned = pltpu.roll(keys.astype(jnp.float32), HEAD_DIM, 1).astype(jnp.bfloat16)
        for p in range(q_ref.shape[1] // LEN):
            queries = q_ref[block(i), block(p)]
            result = []
            for e in range(2):
                masked = jnp.where(left_half == (e == 0), queries, zero)
                scores = dot_nt(masked, keys if e == 0 else turned) * scale
                scores = jnp.where(allowed, scores, hidden_bias)
                top = jnp.max(scores, axis=1, keepdims=True)
                weights = jnp.exp2(scores - top)
                total = jnp.sum(weights, axis=1, keepdims=True)
                probs = (weights * (1.0 / total)).astype(jnp.bfloat16)
                result.append(dot_nn(probs, turned if e == 0 else keys))
                lse = jnp.broadcast_to(top + jnp.log(total) * LOG2E, (LEN, LEN))
                lse_ref[2 * p + e : 2 * p + e + 1, at] = lse.T[0:1]
            out_ref[at, block(p)] = jnp.where(left_half, result[0], result[1]).astype(jnp.bfloat16)


def attention_back_kernel(chunks, final, *refs):
    q_ref, kv_ref, do_ref, lse_ref, seg_col_ref, seg_row_ref, cos_ref, sin_ref = refs[:8]
    if final:
        dk_in_ref, dv_in_ref, dq_ref, dkv_ref, dk_ref, dv_ref, turned_ref, key_t_ref = refs[8:]
    else:
        dq_ref, dk_ref, dv_ref, turned_ref, key_t_ref = refs[8:]
    scale = HEAD_DIM ** (-0.5)
    blocks = q_ref.shape[0] // LEN
    first = chunks[0]
    left_half = lane_iota() < HEAD_DIM
    zero = jnp.zeros((LEN, LEN), jnp.bfloat16)
    for i in range(chunks[-1] + 1):
        kv = kv_ref[block(i), :].astype(jnp.float32)
        turned_ref[block(i), :] = pltpu.roll(kv, HEAD_DIM, 1).astype(jnp.bfloat16)
        key_t_ref[:, block(i)] = kv.T[:HEAD_DIM].astype(jnp.bfloat16)
    if final:
        dk_ref[...] = dk_in_ref[...]
        dv_ref[...] = dv_in_ref[...]
    else:
        dk_ref[...] = jnp.zeros(dk_ref.shape, jnp.float32)
        dv_ref[...] = jnp.zeros(dv_ref.shape, jnp.float32)
    for i in chunks:
        at = block(i - first)
        low = max(0, i - 2) * LEN
        span = (i + 1) * LEN - low
        window = slice(low, low + span)
        allowed = jnp.concatenate([mask_st(seg_col_ref, seg_row_ref, j, i) for j in range(low // LEN, i + 1)], axis=0)
        keys, turned = kv_ref[window, :], turned_ref[window, :]
        for p in range(q_ref.shape[1] // LEN):
            queries, douts = q_ref[block(i), block(p)], do_ref[at, block(p)]
            back = []
            for e in range(2):
                side = left_half == (e == 0)
                q_half = jnp.where(side, queries, zero)
                do_half = jnp.where(side, douts, zero)
                h = 2 * p + e
                scores = dot_nt(keys if e == 0 else turned, q_half) * (scale * LOG2E)
                probs = jnp.exp2(jnp.where(allowed, scores, hidden_bias) - lse_ref[h : h + 1, at])
                dprobs = dot_nt(turned if e == 0 else keys, do_half)
                inner = jnp.sum(probs * dprobs, axis=0, keepdims=True)
                dscores = (probs * (dprobs - inner)).astype(jnp.bfloat16)
                dv_ref[window, :] = dv_ref[window, :] + dot_nn(probs.astype(jnp.bfloat16), do_half)
                dk_ref[window, :] = dk_ref[window, :] + dot_nn(dscores, q_half)
                back.append(dot_nn(key_t_ref[:, window], dscores))
            dq = jnp.concatenate(back, axis=0).T * scale
            dq_ref[at, block(p)] = rotate_tile(dq, cos_ref[block(i), :], -sin_ref[block(i), :]).astype(jnp.bfloat16)
    if not final:
        return
    for i in range(blocks):
        dk = dk_ref[block(i), :]
        dk = (dk + pltpu.roll(dk, HEAD_DIM, 1)) * scale
        dk = rotate_tile(dk, cos_ref[block(i), :], -sin_ref[block(i), :])
        dv = dv_ref[block(i), :]
        dv = dv + pltpu.roll(dv, HEAD_DIM, 1)
        dkv_ref[block(i), :] = jnp.where(left_half, dk, dv).astype(jnp.bfloat16)


def scan_back_kernel(
    chunks,
    heads,
    gmr_ref,
    gated_ref,
    square_a_ref,
    square_b_ref,
    dot_a_ref,
    dot_b_ref,
    gain_ref,
    gate_ref,
    y_ref,
    x_ref,
    xb_ref,
    state_ref,
    lag_ref,
    cum_row_ref,
    skip_ref,
    seg_col_ref,
    seg_row_ref,
    select_ref,
    dgate_ref,
    gy_ref,
    dx_ref,
    p_ref,
    grad_in_ref,
    grad_out_ref,
    sums_ref,
    gyb_ref,
    wide_ref,
    cross_ref,
    bias_ref,
    dcross_ref,
    inv_wide_ref,
    dot_wide_ref,
    inner_ref,
    mix_ref,
):
    step = pl.program_id(0)
    first = chunks[0]
    sources = chunks[-1] + 1
    left_half = lane_iota() < HEAD_DIM
    zero = jnp.zeros((LEN, LEN), jnp.bfloat16)
    spans = [(j, max(j, first), min(j + 3, sources)) for j in range(sources)]
    pairs = [(j, i) for j, start, stop in spans for i in range(start, stop)]

    @pl.when(step == 0)
    def _():
        for i in chunks:
            at = block(i - first)
            square = (square_a_ref[:, at] + square_b_ref[:, at]) / DSSM
            inv = lax.rsqrt(square + norm_eps)
            inv_wide_ref[at, :] = jnp.broadcast_to(inv, (LEN, LEN)).T
            dot = (dot_a_ref[:, at] + dot_b_ref[:, at]) / DSSM
            dot_wide_ref[at, :] = jnp.broadcast_to(dot, (LEN, LEN)).T
        p_ref[...] = jnp.zeros(p_ref.shape, jnp.float32)
        for h in range(heads):
            wide_ref[h] = jnp.broadcast_to(lag_ref[: sources * LEN, h : h + 1], (sources * LEN, LEN))
        for j, start, stop in spans:
            cross = three_dots(dot_nt, state_ref[block(j), :LEN], state_ref[start * LEN : stop * LEN, LEN:])
            for n, (j2, i) in enumerate(pairs):
                if j2 == j:
                    cross_ref[n] = cross[:, block(i - start)]
                    allowed = mask_st(seg_col_ref, seg_row_ref, j, i)
                    bias_ref[n] = jnp.where(allowed, 0.0, hidden_bias)
                    dcross_ref[n] = jnp.zeros((LEN, LEN), jnp.float32)

    tiles = (
        gmr_ref, gated_ref, gain_ref, gate_ref, y_ref, x_ref, xb_ref, skip_ref, dgate_ref, gy_ref, dx_ref, sums_ref
    )

    def head_pair(
        hp,
        select,
        gmr_ref,
        gated_ref,
        gain_ref,
        gate_ref,
        y_ref,
        x_ref,
        xb_ref,
        skip_ref,
        dgate_ref,
        gy_ref,
        dx_ref,
        sums_ref,
    ):
        skip = skip_ref[...]
        gain = gain_ref[...]
        skip_sum = jnp.zeros((1, LEN), jnp.float32)
        gain_sum = jnp.zeros((1, LEN), jnp.float32)
        for i in chunks:
            at = block(i - first)
            inv = inv_wide_ref[at, :]
            unit = gated_ref[at, :] * inv
            rows_grad = gmr_ref[at, :]
            grad = inv * (rows_grad * gain - unit * dot_wide_ref[at, :])
            gate = gate_ref[at, :]
            sig = sigmoid(gate)
            y = y_ref[at, :]
            x = x_ref[at, :]
            gy = grad * (gate * sig)
            dgate_ref[at, :] = (grad * (y + skip * x) * (sig * (1.0 + gate * (1.0 - sig)))).astype(jnp.bfloat16)
            gyb = gy.astype(jnp.bfloat16)
            gy_ref[at, :] = gy
            gyb_ref[at, :] = gyb
            high, rest = two_terms(gyb.astype(jnp.float32) * y)
            p_ref[:, at] = p_ref[:, at] + dot_nt(select, high) + dot_nt(select, rest)
            skip_sum = skip_sum + jnp.sum(gy * x, axis=0, keepdims=True)
            gain_sum = gain_sum + jnp.sum(rows_grad * unit, axis=0, keepdims=True)
        sums_ref[0:1, :] = skip_sum
        sums_ref[1:2, :] = gain_sum

        for j, start, stop in spans:
            x_pair = xb_ref[block(j), :]
            x_both = jnp.concatenate([jnp.where(left_half, x_pair, zero), jnp.where(left_half, zero, x_pair)], axis=0)
            wide = (stop - start) * LEN
            gy_rows = gyb_ref[(start - first) * LEN : (stop - first) * LEN, :]
            inner_ref[:, :wide] = dot_nt(x_both, gy_rows)
            for n, (j2, i) in enumerate(pairs):
                if j2 != j:
                    continue
                grown = dcross_ref[n]
                for e in range(2):
                    spread = cum_row_ref[2 * hp + e, :, block(i)] - wide_ref[2 * hp + e, block(j), :]
                    decay = jnp.exp2(spread + bias_ref[n])
                    grown = grown + inner_ref[block(e), block(i - start)] * decay
                    mix_ref[block(e), block(i - start)] = (decay * cross_ref[n]).astype(jnp.bfloat16)
                dcross_ref[n] = grown
            both = dot_nn(mix_ref[:, :wide], gy_rows)
            dx_ref[block(j), :] = jnp.where(left_half, both[:LEN], both[LEN:])

    for sub in range(GROUP):
        head_pair(GROUP * step + sub, select_ref[:, block(sub)], *[t.at[:, block(sub)] for t in tiles])

    @pl.when(step == pl.num_programs(0) - 1)
    def _():
        grad_out = {i: jnp.zeros((LEN, LEN), jnp.float32) for i in chunks}
        for j in range(sources):
            grad_in = jnp.zeros((LEN, LEN), jnp.float32)
            for n, (j2, i) in enumerate(pairs):
                if j2 != j:
                    continue
                high, rest = two_terms(dcross_ref[n])
                out_high, out_rest = two_terms(state_ref[block(i), LEN:])
                in_high, in_rest = two_terms(state_ref[block(j), :LEN])
                grad_in = grad_in + dot_nn(high, out_high) + dot_nn(high, out_rest) + dot_nn(rest, out_high)
                grad_out[i] = grad_out[i] + dot_tn(high, in_high) + dot_tn(high, in_rest) + dot_tn(rest, in_high)
            grad_in_ref[block(j), :] = grad_in
        for i in chunks:
            grad_out_ref[block(i - first), :] = grad_out[i]


def conv_back(grad_ref, value_ref, keep_ref, kernel_ref, out_ref, sum_ref, lanes, blocks):
    taps = kernel_ref[:, lanes]
    totals = [jnp.zeros((1, LEN), jnp.float32) for _ in range(5)]
    for i in range(blocks):
        here = grad_ref[i * LEN : (i + 1) * LEN, :]
        grad = taps[3:4] * here
        totals[4] = totals[4] + jnp.sum(here, axis=0, keepdims=True)
        totals[3] = totals[3] + jnp.sum(here * value_ref[8 + i * LEN : 8 + (i + 1) * LEN, :], axis=0, keepdims=True)
        for lag in (1, 2, 3):
            ahead = grad_ref[i * LEN + lag : (i + 1) * LEN + lag, :]
            grad = grad + taps[3 - lag : 4 - lag] * (ahead * keep_ref[lag - 1, i * LEN + lag : (i + 1) * LEN + lag, :])
            moved = value_ref[8 + i * LEN - lag : 8 + (i + 1) * LEN - lag, :]
            masked = here * keep_ref[lag - 1, i * LEN : (i + 1) * LEN, :]
            totals[3 - lag] = totals[3 - lag] + jnp.sum(masked * moved, axis=0, keepdims=True)
        out_ref[block(i), lanes] = grad.astype(jnp.bfloat16)
    for tap in range(5):
        sum_ref[tap : tap + 1, lanes] = totals[tap]


def scan_end_kernel(
    heads,
    gy_a_ref,
    gy_b_ref,
    dx_a_ref,
    dx_b_ref,
    p_a_ref,
    p_b_ref,
    in_a_ref,
    in_b_ref,
    out_a_ref,
    out_b_ref,
    xb_ref,
    slope_ref,
    state_slope_ref,
    conv_ref,
    small_ref,
    step_row_ref,
    sig_row_ref,
    rate_ref,
    skip_ref,
    keep_ref,
    seg_col_ref,
    seg_row_ref,
    select_ref,
    conv_kernel_ref,
    state_kernel_ref,
    dconv_ref,
    dstate_ref,
    dstep_ref,
    conv_sum_ref,
    state_sum_ref,
    step_sum_ref,
    grad_pad_ref,
    value_pad_ref,
    wide_ref,
    q_ref,
    flow_ref,
):
    step = pl.program_id(0)
    rows = conv_ref.shape[0]
    blocks = rows // LEN
    half = rows // 2
    count = flow_ref.shape[0]

    @pl.when(step == 0)
    def _():
        value_pad_ref[0:8, :] = jnp.zeros((8, LEN), jnp.float32)
        grad_pad_ref[rows : rows + 8, :] = jnp.zeros((8, LEN), jnp.float32)
        widen(keep_ref, wide_ref)
        q_ref[...] = jnp.zeros(q_ref.shape, jnp.float32)
        for c in range(2):
            if c == 0:
                grad_pad_ref[0:half, :] = (in_a_ref[...] + in_b_ref[0:half, :]) * state_slope_ref[0:half, block(c)]
                grad_pad_ref[half:rows, :] = in_b_ref[half:rows, :] * state_slope_ref[half:rows, block(c)]
            else:
                grad_pad_ref[0:half, :] = out_a_ref[...] * state_slope_ref[0:half, block(c)]
                grad_pad_ref[half:rows, :] = out_b_ref[...] * state_slope_ref[half:rows, block(c)]
            value_pad_ref[8 : rows + 8, :] = small_ref[:, block(c)]
            conv_back(grad_pad_ref, value_pad_ref, wide_ref, state_kernel_ref, dstate_ref, state_sum_ref, block(c), blocks)

    tiles = (
        gy_a_ref, gy_b_ref, dx_a_ref, dx_b_ref, xb_ref, slope_ref, conv_ref, skip_ref, conv_kernel_ref, dconv_ref, conv_sum_ref
    )

    def head_pair(
        select,
        gy_a_ref,
        gy_b_ref,
        dx_a_ref,
        dx_b_ref,
        xb_ref,
        slope_ref,
        conv_ref,
        skip_ref,
        conv_kernel_ref,
        dconv_ref,
        conv_sum_ref,
    ):
        for j in range(blocks):
            dx = dx_b_ref[block(j), :]
            if j < blocks // 2:
                dx = dx + dx_a_ref[block(j), :]
                gy = gy_a_ref[block(j), :]
            else:
                gy = gy_b_ref[block(j - blocks // 2), :]
            high, rest = two_terms(dx * xb_ref[block(j), :].astype(jnp.float32))
            q_ref[:, block(j)] = q_ref[:, block(j)] + dot_nt(select, high) + dot_nt(select, rest)
            grad_pad_ref[block(j), :] = (dx + gy * skip_ref[...]) * slope_ref[block(j), :]
        value_pad_ref[8 : rows + 8, :] = conv_ref[...]
        conv_back(
            grad_pad_ref, value_pad_ref, wide_ref, conv_kernel_ref, dconv_ref, conv_sum_ref, slice(0, LEN), blocks
        )

    for sub in range(GROUP):
        head_pair(select_ref[:, block(sub)], *[t.at[:, block(sub)] for t in tiles])

    @pl.when(step == pl.num_programs(0) - 1)
    def _():
        q = q_ref[...]
        flow_ref[:, 0:half] = p_a_ref[...] - q[:, 0:half]
        flow_ref[:, half:rows] = p_b_ref[...] - q[:, half:rows]
        rate = jnp.broadcast_to(rate_ref[...], (LEN, LEN)).T[:count]
        bias_total = jnp.zeros((count, LEN), jnp.float32)
        decay_total = jnp.zeros((count, LEN), jnp.float32)
        for j in range(blocks):
            log_grad = jnp.zeros((count, LEN), jnp.float32)
            for i in range(j, min(j + 3, blocks)):
                chosen = jnp.where(mask_st(seg_col_ref, seg_row_ref, j, i), 1.0, 0.0).astype(jnp.bfloat16)
                high, rest = two_terms(flow_ref[:, block(i)])
                log_grad = log_grad + dot_nt(high, chosen) + dot_nt(rest, chosen)
            step = step_row_ref[:, block(j)]
            grad_step = jnp.where(step > 1e-30, q[:, block(j)] / step, 0.0) + log_grad * rate
            grad_arg = grad_step * sig_row_ref[:, block(j)]
            bias_total = bias_total + grad_arg
            decay_total = decay_total + log_grad * step
            tall = jnp.concatenate([grad_arg, jnp.zeros((LEN - count, LEN), jnp.float32)], axis=0)
            dstep_ref[block(j), :] = tall.T.astype(jnp.bfloat16)
        step_sum_ref[0:count, :] = jnp.broadcast_to(jnp.sum(bias_total, axis=1, keepdims=True), (count, LEN))
        step_sum_ref[count : 2 * count, :] = jnp.broadcast_to(
            jnp.sum(decay_total * rate, axis=1, keepdims=True), (count, LEN)
        )


def whole_block(shape):
    return pl.BlockSpec(shape, lambda step: (0,) * len(shape), pipeline_mode=pl.Buffered(1))


def tile(rows, row_block=0, first=0):
    return pl.BlockSpec((rows, GROUP * LEN), lambda step: (row_block, first + step))


def call(kernel, steps, out_shape, out_specs, scratch, operands, specs, flops):
    moved = sum(o.size * o.dtype.itemsize for o in operands) + sum(o.size * o.dtype.itemsize for o in out_shape)
    return pl.pallas_call(
        kernel,
        grid=(steps,),
        out_shape=out_shape,
        in_specs=[s or whole_block(o.shape) for o, s in zip(operands, specs)],
        out_specs=[s or whole_block(o.shape) for o, s in zip(out_shape, out_specs)],
        scratch_shapes=scratch,
        compiler_params=pltpu.CompilerParams(vmem_limit_bytes=VMEM_BYTES),
        cost_estimate=pl.CostEstimate(flops=flops, bytes_accessed=moved, transcendentals=0),
    )(*operands)


def f32(*shape):
    return jax.ShapeDtypeStruct(shape, jnp.float32)


def b16(*shape):
    return jax.ShapeDtypeStruct(shape, jnp.bfloat16)


HEAD_ROWS = 16
GROUP = 3
VMEM_BYTES = 60 * 1024 * 1024


def scan_prep(width, wide_in, small, cosine, sine, keep, conv_kernel, conv_bias, *rest):
    rows = wide_in.shape[0]
    steps = width // LEN // GROUP
    outs = [
        f32(rows, width),
        b16(rows, width),
        f32(rows, width),
        f32(rows, 2 * LEN),
        f32(rows, 2 * LEN),
        f32(rows, LEN),
        f32(rows, LEN),
        f32(HEAD_ROWS, 1, rows),
        f32(HEAD_ROWS, 1, rows),
        f32(HEAD_ROWS, rows),
        f32(HEAD_ROWS, rows),
        b16(rows, 2 * LEN),
        b16(rows, LEN),
    ]
    scratch = [pltpu.VMEM((rows + 8, LEN), jnp.float32), pltpu.VMEM((3, rows + 8, LEN), jnp.float32)]
    operands = (wide_in, small, cosine, sine, keep, conv_kernel, conv_bias, *rest)
    specs = [tile(rows, 0, steps), None, None, None, None, tile(4), tile(1)] + [None] * len(rest)
    return call(prep_kernel, steps, outs, [tile(rows)] * 3 + [None] * 10, scratch, operands, specs, 10**9)


def scan_forward(chunks, heads, wide_in, x, xb, *rest):
    width = x.shape[1]
    rows = LEN * len(chunks)
    at = chunks[0] // len(chunks)
    count = sum(min(i, 2) + 1 for i in chunks)
    outs = [f32(rows, width), f32(rows, width), f32(1, rows)]
    scratch = [
        pltpu.VMEM((heads, rows, LEN), jnp.float32),
        pltpu.VMEM((count, LEN, LEN), jnp.float32),
        pltpu.VMEM((count, LEN, LEN), jnp.float32),
        pltpu.VMEM((len(chunks), 2 * LEN, 3 * LEN), jnp.bfloat16),
        pltpu.VMEM((rows, LEN), jnp.float32),
    ]
    specs = [tile(rows, at), tile(rows, at), tile((chunks[-1] + 1) * LEN)] + [None] * (len(rest) - 1) + [tile(1)]
    kernel = functools.partial(scan_kernel, chunks, heads)
    operands = (wide_in, x, xb, *rest)
    return call(kernel, heads // 2 // GROUP, outs, [tile(rows), tile(rows), None], scratch, operands, specs, 2 * 10**9)


def attention_forward(chunks, q, kv, seg_col, seg_row):
    rows = LEN * len(chunks)
    outs = [b16(rows, q.shape[1]), f32(8, rows)]
    kernel = functools.partial(attention_kernel, chunks)
    return call(kernel, 1, outs, [None] * 2, [], (q, kv, seg_col, seg_row), [None] * 4, 10**9)


def attention_backward(chunks, final, *operands):
    q = operands[0]
    rows = q.shape[0]
    partial = [f32(rows, LEN), f32(rows, LEN)]
    sums = [pltpu.VMEM((rows, LEN), jnp.float32)] * 2
    outs = [b16(LEN * len(chunks), q.shape[1])] + ([b16(rows, LEN)] if final else partial)
    scratch = (sums if final else []) + [
        pltpu.VMEM((rows, LEN), jnp.bfloat16),
        pltpu.VMEM((HEAD_DIM, rows), jnp.bfloat16),
    ]
    kernel = functools.partial(attention_back_kernel, chunks, final)
    return call(kernel, 1, outs, [None] * len(outs), scratch, operands, [None] * len(operands), 2 * 10**9)


def scan_backward(chunks, heads, *operands):
    rows, width = operands[0].shape
    at = chunks[0] // len(chunks)
    sources = (chunks[-1] + 1) * LEN
    count = sum(min(i, 2) + 1 for i in chunks)
    outs = [
        b16(rows, width),
        f32(rows, width),
        f32(sources, width),
        f32(HEAD_ROWS, rows),
        f32(sources, LEN),
        f32(rows, LEN),
        f32(8, width),
    ]
    scratch = [
        pltpu.VMEM((rows, LEN), jnp.bfloat16),
        pltpu.VMEM((heads, sources, LEN), jnp.float32),
        pltpu.VMEM((count, LEN, LEN), jnp.float32),
        pltpu.VMEM((count, LEN, LEN), jnp.float32),
        pltpu.VMEM((count, LEN, LEN), jnp.float32),
        pltpu.VMEM((rows, LEN), jnp.float32),
        pltpu.VMEM((rows, LEN), jnp.float32),
        pltpu.VMEM((2 * LEN, 3 * LEN), jnp.float32),
        pltpu.VMEM((2 * LEN, 3 * LEN), jnp.bfloat16),
    ]
    specs = [tile(rows), tile(rows), None, None, None, None, tile(1), tile(rows, at), tile(rows), tile(rows, at), tile(sources)]
    specs += [None, None, None, tile(1), None, None, tile(HEAD_ROWS)]
    out_specs = [tile(rows), tile(rows), tile(sources), None, None, None, tile(8)]
    kernel = functools.partial(scan_back_kernel, chunks, heads)
    return call(kernel, heads // 2 // GROUP, outs, out_specs, scratch, operands, specs, 4 * 10**9)


def scan_end(heads, *operands):
    rows, width = 2 * operands[0].shape[0], operands[0].shape[1]
    steps = heads // 2 // GROUP
    outs = [
        b16(rows, width),
        b16(rows, 2 * LEN),
        b16(rows, LEN),
        f32(8, width),
        f32(8, 2 * LEN),
        f32(2 * HEAD_ROWS, LEN),
    ]
    scratch = [
        pltpu.VMEM((rows + 8, LEN), jnp.float32),
        pltpu.VMEM((rows + 8, LEN), jnp.float32),
        pltpu.VMEM((3, rows + 8, LEN), jnp.float32),
        pltpu.VMEM((HEAD_ROWS, rows), jnp.float32),
        pltpu.VMEM((HEAD_ROWS, rows), jnp.float32),
    ]
    half = rows // 2
    specs = [tile(half), tile(half), tile(half), tile(rows)] + [None] * 6 + [tile(rows), tile(rows), None]
    specs += [tile(rows, 0, steps)] + [None] * 4 + [tile(1), None, None, None, tile(HEAD_ROWS), tile(4), None]
    out_specs = [tile(rows), None, None, tile(8), None, None]
    kernel = functools.partial(scan_end_kernel, heads)
    return call(kernel, steps, outs, out_specs, scratch, operands, specs, 2 * 10**9)


def assemble_kernel(
    core_ref, own_ref, far_ref, mixer_out_ref, attn_out_ref, mixer_proj_ref, query_ref, pair_ref, state_ref, step_ref
):
    at = pl.program_id(0)
    count = pl.num_programs(0)
    width = mixer_proj_ref.shape[2]
    model_width = mixer_out_ref.shape[1]
    split = mixer_out_count(width)

    def write(source):
        @pl.when(at < split)
        def _():
            mixer_out_ref[...] = source[:, :model_width]

        @pl.when(at >= split)
        def _():
            attn_out_ref[...] = source[:, :model_width]

        start = model_width
        mixer_proj_ref[:, 0, :] = source[:, start : start + width]
        start += width
        query_ref[...] = source[:, start : start + query_ref.shape[1]]
        start += query_ref.shape[1]
        pair_ref[:, 0, :] = source[:, start : start + LEN]
        start += LEN
        mixer_proj_ref[:, 1, :] = source[:, start : start + width]
        start += width
        state_ref[...] = source[:, start : start + 2 * LEN]
        step_ref[...] = source[:, start + 2 * LEN :]

    mine = at // (count // 2) == core_ref[0]

    @pl.when(mine)
    def _():
        write(own_ref)

    @pl.when(jnp.logical_not(mine))
    def _():
        write(far_ref)


def mixer_out_count(width):
    return width // LEN


def assemble(own, far, width, query_width):
    half, columns = own.shape
    rows = 2 * half
    blocks = rows // LEN
    split = mixer_out_count(width)
    core = lax.axis_index("core").astype(jnp.int32).reshape(1)

    def source(flip):
        def index(at, core_ref):
            first = (blocks // 2) * jnp.where(flip, 1 - core_ref[0], core_ref[0])
            return (jnp.clip(at - first, 0, blocks // 2 - 1), 0)

        return pl.BlockSpec((LEN, columns), index)

    def plain(count):
        return pl.BlockSpec((LEN, count), lambda at, core_ref: (at, 0))

    out_specs = [
        pl.BlockSpec((LEN, rows), lambda at, core_ref: (jnp.minimum(at, split - 1), 0)),
        pl.BlockSpec((LEN, rows), lambda at, core_ref: (jnp.maximum(at - split, 0), 0)),
        pl.BlockSpec((LEN, 2, width), lambda at, core_ref: (at, 0, 0)),
        plain(query_width),
        pl.BlockSpec((LEN, 1, LEN), lambda at, core_ref: (at, 0, 0)),
        plain(2 * LEN),
        plain(LEN),
    ]
    out_shape = [
        f32(width, rows),
        f32(rows - width, rows),
        f32(rows, 2, width),
        f32(rows, query_width),
        f32(rows, 1, LEN),
        f32(rows, 2 * LEN),
        f32(rows, LEN),
    ]
    return pl.pallas_call(
        assemble_kernel,
        grid_spec=pltpu.PrefetchScalarGridSpec(
            num_scalar_prefetch=1, grid=(blocks,), in_specs=[source(False), source(True)], out_specs=out_specs
        ),
        out_shape=out_shape,
        compiler_params=pltpu.CompilerParams(vmem_limit_bytes=VMEM_BYTES),
        cost_estimate=pl.CostEstimate(flops=0, bytes_accessed=16 * own.size, transcendentals=0),
    )(core, own, far)


def silu_slope(argument):
    logistic = jax.nn.sigmoid(argument)
    return logistic * (1.0 + argument * (1.0 - logistic))


def rope_tables(rows):
    half_size = HEAD_DIM // 2
    inverse = np.float32(rope_base) ** (-(2.0 * np.arange(half_size, dtype=np.float32)) / HEAD_DIM)
    angles = np.arange(rows, dtype=np.float32)[:, None] * inverse.astype(np.float32)[None, :]
    cosine, sine = np.cos(angles), np.sin(angles)
    return (
        np.concatenate([cosine] * 4, axis=1).astype(np.float32),
        np.concatenate([-sine, sine, -sine, sine], axis=1).astype(np.float32),
    )


def norm_backward(grad_unit, unit_rows, inv_rms):
    return inv_rms * (grad_unit - unit_rows * jnp.mean(grad_unit * unit_rows, axis=-1, keepdims=True))


def dot32(left, right):
    return jnp.dot(left, right, preferred_element_type=jnp.float32)


def after(value, *others):
    return lax.optimization_barrier((value, *others))[0]


def swap(values, name):
    return lax.ppermute(values, name, PAIR)


def exchange(values, name):
    return values + swap(values, name)


def core_rows(values, index):
    half = values.shape[1] // 2
    return lax.dynamic_slice_in_dim(values, index * half, half, 1)


def rows_dot(left, right, index):
    return lax.dot_general(core_rows(left, index), right, (((0,), (0,)), ((), ())), preferred_element_type=jnp.float32)


def on_device(
    layer_input,
    segments,
    input_gain,
    mixer_proj,
    state_proj,
    step_proj,
    step_bias,
    decay_log,
    skip_gain,
    conv_kernel,
    conv_bias,
    state_kernel,
    state_bias,
    gated_gain,
    mixer_out,
    query_proj,
    key_value_weight,
    attn_out,
    ffn_gain,
    ffn_gate,
    ffn_up,
    ffn_down,
    cotangent,
):
    segment = segments.reshape(-1)
    rows, model_width = layer_input.shape
    width = mixer_proj.shape[2]
    heads = step_proj.shape[1]
    state_size = state_proj.shape[1] // 2
    query_width = query_proj.shape[1]
    pair_width = key_value_weight.shape[2]
    place = lax.axis_index("core")
    cosine, sine = rope_tables(rows)
    select = np.arange(HEAD_ROWS)[:, None] == np.arange(width)[None, :] // HEAD_DIM
    select = jnp.asarray(select.astype(np.float32)).astype(jnp.bfloat16)
    seg_col, seg_row = segment[:, None], segment[None, :]
    keep = [jnp.ones((rows,), jnp.float32)]
    for lag in (1, 2, 3):
        previous = jnp.concatenate([jnp.full((lag,), -1, jnp.int32), segment[:-lag]])
        keep.append((previous == segment).astype(jnp.float32))
    keep = jnp.pad(jnp.stack(keep, axis=1), ((0, 8), (0, 4)))
    pad_heads = ((0, 0), (0, LEN - heads))
    rate_row = jnp.pad(-jnp.exp(decay_log)[None, :], pad_heads)
    step_bias_row = jnp.pad(step_bias[None, :], pad_heads)
    skip_row = jnp.repeat(skip_gain, HEAD_DIM)[None, :]
    gain_row = gated_gain[None, :]
    wide_proj = mixer_proj.reshape(model_width, 2 * width)
    small_proj = jnp.concatenate(
        [
            state_proj,
            query_proj,
            key_value_weight.reshape(model_width, pair_width),
            jnp.pad(step_proj, pad_heads),
        ],
        axis=1,
    )

    tokens = layer_input.astype(jnp.float32)
    inv_rms_in = lax.rsqrt(jnp.mean(tokens * tokens, axis=-1, keepdims=True) + norm_eps)
    unit_in = tokens * inv_rms_in
    normed_input = (unit_in * input_gain).astype(jnp.bfloat16)
    small_in = dot32(normed_input, small_proj)
    wide_in = dot32(normed_input, wide_proj)
    x, xb, slope, state, state_slope, cum, lag, cum_row, lag_row, step_row, sig_row, queries, pairs = scan_prep(
        width,
        wide_in,
        small_in,
        cosine,
        sine,
        keep,
        conv_kernel,
        conv_bias[None, :],
        state_kernel,
        state_bias[None, :],
        step_bias_row,
        rate_row,
    )

    blocks = rows // LEN
    late = tuple(range(blocks // 2, blocks))
    early = tuple(range(blocks // 2))
    half = {}
    ready = None
    for chunks in (late, early):
        span = slice(chunks[0] * LEN, (chunks[-1] + 1) * LEN)
        h = {"span": span}
        lag_now = lag_row if ready is None else after(lag_row, ready)
        h["y"], h["gated"], h["square"] = scan_forward(
            chunks, heads, wide_in, x, xb, state, cum, lag_now, seg_col, seg_row, skip_row
        )
        h["attended"], h["lse"] = attention_forward(chunks, after(queries, h["square"]), pairs, seg_col, seg_row)
        h["square_far"] = swap(h["square"], "tensor")
        squares = after(h["square"] + h["square_far"], h["lse"])
        h["inv_gated"] = lax.rsqrt(squares.reshape(-1, 1) / DSSM + norm_eps)
        h["mixer_rows"] = (h["gated"] * h["inv_gated"] * gated_gain).astype(jnp.bfloat16)
        h["part"] = dot32(h["mixer_rows"], mixer_out) + dot32(h["attended"], attn_out)
        h["branch_far"] = swap(h["part"], "tensor")
        ready = h["part"]
        half[chunks] = h

    ready = None
    for chunks in (late, early):
        h = half[chunks]
        span = h["span"]
        far = h["branch_far"] if ready is None else after(h["branch_far"], ready)
        hidden = tokens[span] + (h["part"] + far)
        inv_rms_ffn = lax.rsqrt(jnp.mean(hidden * hidden, axis=-1, keepdims=True) + norm_eps)
        unit_ffn = hidden * inv_rms_ffn
        normed_ffn = (unit_ffn * ffn_gain).astype(jnp.bfloat16)
        gate_rows = dot32(normed_ffn, ffn_gate)
        up_rows = dot32(normed_ffn, ffn_up)
        gate_silu = jax.nn.silu(gate_rows)
        activated = (gate_silu * up_rows).astype(jnp.bfloat16)
        grad_activated = dot32(cotangent[span], ffn_down.T)
        grad_gate_rows = (grad_activated * up_rows * silu_slope(gate_rows)).astype(jnp.bfloat16)
        grad_up_rows = (grad_activated * gate_silu).astype(jnp.bfloat16)
        partial_ffn = dot32(grad_gate_rows, ffn_gate.T) + dot32(grad_up_rows, ffn_up.T)
        h["part_ffn"] = partial_ffn
        h["ffn_far"] = swap(partial_ffn, "tensor")
        ready = partial_ffn
        h.update(
            hidden=hidden,
            unit_ffn=unit_ffn,
            inv_rms_ffn=inv_rms_ffn,
            normed_ffn=normed_ffn,
            activated=activated,
            grad_gate_rows=grad_gate_rows,
            grad_up_rows=grad_up_rows,
        )

    def whole(name):
        return jnp.concatenate([half[early][name], half[late][name]], axis=0)

    normed_ffn = whole("normed_ffn")
    sides = [
        (normed_ffn, whole("grad_gate_rows")),
        (normed_ffn, whole("grad_up_rows")),
        (whole("activated"), cotangent),
    ]
    sent = [swap(rows_dot(left, right, 1 - place), "core") for left, right in sides]
    kept = [rows_dot(left, right, place) for left, right in sides]
    first = jnp.concatenate([a + b for a, b in zip(kept, sent)], axis=1)
    first_sum = lax.psum_scatter(first, ("y", "x"), scatter_dimension=0, tiled=True)
    depth = first_sum.shape[0] // 2
    zh = lax.axis_index("zh")
    first_own = lax.dynamic_slice_in_dim(first_sum, zh * depth, depth, 0) + swap(
        lax.dynamic_slice_in_dim(first_sum, (1 - zh) * depth, depth, 0), "zh"
    )
    first_all = lax.all_gather(first_own, ("core", "y", "x", "zh"), axis=0, tiled=True)

    grad_ffn_gain = 0.0
    ready = first
    for chunks in (late, early):
        h = half[chunks]
        span = h["span"]
        grad_normed_ffn = h["part_ffn"] + after(h["ffn_far"], ready)
        grad_ffn_gain = grad_ffn_gain + jnp.sum(grad_normed_ffn * h["unit_ffn"], axis=0)
        h["grad_hidden"] = cotangent[span].astype(jnp.float32) + norm_backward(
            grad_normed_ffn * ffn_gain, h["unit_ffn"], h["inv_rms_ffn"]
        )
        grad_branch = h["grad_hidden"].astype(jnp.bfloat16)
        h["grad_branch"] = grad_branch
        grad_mixer_rows = dot32(grad_branch, mixer_out.T)
        unit_gated = h["gated"] * h["inv_gated"]
        gated_dot = jnp.sum(grad_mixer_rows * gated_gain * unit_gated, axis=-1)[None, :]
        dot_far = swap(gated_dot, "tensor")
        grad_attended = dot32(after(grad_branch, gated_dot), attn_out.T).astype(jnp.bfloat16)
        operands = (queries, pairs, grad_attended, h["lse"], seg_col, seg_row, cosine, sine)
        if chunks == late:
            h["grad_queries"], grad_keys, grad_values = attention_backward(chunks, False, *operands)
        else:
            h["grad_queries"], grad_pairs = attention_backward(chunks, True, *operands, grad_keys, grad_values)
        h["grad_gate"], h["gy"], h["dx"], h["p"], h["grad_in"], h["grad_out"], h["sums"] = scan_backward(
            chunks,
            heads,
            grad_mixer_rows,
            h["gated"],
            h["square"],
            h["square_far"],
            gated_dot,
            after(dot_far, h["grad_queries"]),
            gain_row,
            wide_in,
            h["y"],
            x,
            xb,
            state,
            lag,
            cum_row,
            skip_row,
            seg_col,
            seg_row,
            select,
        )
        ready = h["p"]
    down = dot32(whole("activated"), ffn_down)
    down_far = swap(after(down, dot_far), "tensor")
    ends = []
    for name in ("gy", "dx", "p", "grad_in", "grad_out"):
        ends += [half[early][name], half[late][name]]
    grad_conv, grad_state, grad_step, conv_sum, state_sum, step_sum = scan_end(
        heads,
        *ends,
        xb,
        slope,
        state_slope,
        wide_in,
        small_in,
        step_row,
        sig_row,
        rate_row,
        skip_row,
        keep,
        seg_col,
        seg_row,
        select,
        conv_kernel,
        state_kernel,
    )

    grad_queries, grad_gate = whole("grad_queries"), whole("grad_gate")
    outer = jnp.concatenate([whole("mixer_rows"), whole("attended")], axis=1)
    grad_branch = whole("grad_branch")
    right = jnp.concatenate([grad_gate, grad_queries, grad_pairs, grad_conv, grad_state, grad_step], axis=1)
    far_outer = swap(rows_dot(outer, grad_branch, 1 - place), "core")
    far_inner = swap(rows_dot(normed_input, right, 1 - place), "core")

    wide_grad = jnp.concatenate([grad_gate, grad_conv], axis=1)
    small_grad = jnp.concatenate([grad_state, grad_queries, grad_pairs, grad_step], axis=1)
    partial_normed = dot32(wide_grad, wide_proj.T) + dot32(small_grad, small_proj.T)
    normed_far = swap(partial_normed, "tensor")
    sums = half[early]["sums"] + half[late]["sums"]
    over_tensor = [jnp.sum(partial_normed * unit_in, axis=0), state_sum[:4], state_sum[4]]
    alone = [
        step_sum[:heads, 0],
        step_sum[HEAD_ROWS : HEAD_ROWS + heads, 0],
        jnp.sum(sums[0].reshape(heads, HEAD_DIM), axis=1),
        conv_sum[:4],
        conv_sum[4],
        sums[1],
        grad_ffn_gain,
    ]

    def packed(values):
        flat = jnp.concatenate([v.reshape(-1) for v in values])
        count = -(-flat.shape[0] // model_width)
        return jnp.pad(flat, (0, count * model_width - flat.shape[0])).reshape(count, model_width)

    def unpacked(table, values):
        flat, result, start = table.T.reshape(-1), [], 0
        for v in values:
            result.append(flat[start : start + v.size].reshape(v.shape))
            start += v.size
        return result

    tables = [packed(over_tensor), packed(alone)]
    shared_end = heads + tables[0].shape[0]
    table = jnp.concatenate(tables, axis=0)
    table_end = heads + table.shape[0]
    table = (core_rows(table, place) + swap(core_rows(table, 1 - place), "core")).T
    table = jnp.pad(table, ((0, 0), (heads, LEN - table_end)))
    kept_outer, kept_inner = rows_dot(outer, grad_branch, place), rows_dot(normed_input, right, place)
    at_step = model_width + 2 * width + query_width + pair_width + 2 * state_size
    inner = kept_inner + far_inner
    inner_end = at_step - model_width
    second = jnp.concatenate([kept_outer + far_outer, inner[:, :inner_end], inner[:, inner_end:] + table], axis=1)
    devices = 32
    own_rows = second.shape[0] // devices
    columns = second.shape[1]
    second = after(second, first_own)
    second = lax.all_to_all(second.reshape(devices, own_rows, columns), ("y", "zh", "x"), 0, 0, tiled=True)
    second = jnp.sum(second, axis=0)
    at_state = at_step - 2 * state_size
    both = second[:, at_state:]
    summed = exchange(both, "tensor")
    lane = np.arange(both.shape[1]) - 2 * state_size
    is_shared = (lane < 0) | ((lane >= heads) & (lane < shared_end))
    second = jnp.concatenate([second[:, :at_state], jnp.where(is_shared[None, :], summed, both)], axis=1)
    second = jnp.broadcast_to(second[None], (devices, own_rows, columns))
    second = lax.all_to_all(second, ("y", "zh", "x"), 0, 0, tiled=True).reshape(devices * own_rows, columns)
    second_far = swap(second, "core")
    grad_mixer_out, grad_attn_out, grad_mixer_proj, grad_query_proj, grad_keyval, grad_state_proj, step_block = assemble(
        second, second_far, width, query_width
    )

    grad_hidden = whole("grad_hidden")
    grad_normed = partial_normed + normed_far
    input_grad = grad_hidden + norm_backward(grad_normed * input_gain, unit_in, inv_rms_in)
    layer_output = (whole("hidden") + (down + down_far)).astype(jnp.bfloat16)

    small_shared = unpacked(step_block[:, heads:shared_end], over_tensor)
    small_alone = unpacked(step_block[:, shared_end:table_end], alone)
    return (
        layer_output,
        input_grad,
        small_shared[0],
        grad_mixer_proj,
        grad_state_proj,
        step_block[:, :heads],
        small_alone[0],
        small_alone[1],
        small_alone[2],
        small_alone[3],
        small_alone[4],
        small_shared[1],
        small_shared[2],
        small_alone[5],
        grad_mixer_out,
        grad_query_proj,
        grad_keyval,
        grad_attn_out,
        small_alone[6],
        first_all[:, :model_width],
        first_all[:, model_width : 2 * model_width],
        first_all[:, 2 * model_width :],
    )


def solution(mesh):
    dp, whole_spec, columns = P(DP, None), P(), P(None, "tensor")
    per_channel, middle = P("tensor"), P(None, "tensor", None)
    last, by_rows = P(None, None, "tensor"), P("tensor", None)
    weights = (
        whole_spec,
        last,
        whole_spec,
        columns,
        per_channel,
        per_channel,
        per_channel,
        columns,
        per_channel,
        whole_spec,
        whole_spec,
        per_channel,
        by_rows,
        columns,
        middle,
        by_rows,
        whole_spec,
        columns,
        columns,
        by_rows,
    )
    mesh = jax.sharding.Mesh(mesh.devices.reshape(4, 2, 4, 2, 2), (*DP, "tensor"))
    return jax.shard_map(
        on_device, mesh=mesh, in_specs=(dp, dp, *weights, dp), out_specs=(dp, dp, *weights), check_vma=False
    )
```

```python
import functools

import jax
import jax.numpy as jnp
import numpy as np
from jax import lax
from jax.experimental import pallas as pl
from jax.experimental.pallas import tpu as pltpu
from jax.sharding import PartitionSpec as P

HEAD_DIM = 64
DSSM = 1536
DP = ("y", "zh", "x", "core")
PAIR = [(0, 1), (1, 0)]
LOG2E = 1.4426950408889634
hidden_bias = -1e30
norm_eps = 1e-05
rope_base = 10000.0
LEN = 128


def dot_nn(left, right):
    return lax.dot_general(
        left, right, (((1,), (0,)), ((), ())), preferred_element_type=jnp.float32
    )


def dot_nt(left, right):
    return lax.dot_general(
        left, right, (((1,), (1,)), ((), ())), preferred_element_type=jnp.float32
    )


def dot_tn(left, right):
    return lax.dot_general(
        left, right, (((0,), (0,)), ((), ())), preferred_element_type=jnp.float32
    )


def two_terms(v):
    high = v.astype(jnp.bfloat16)
    return high, (v - high.astype(jnp.float32)).astype(jnp.bfloat16)


def three_dots(dot, left, right):
    left_high, left_low = two_terms(left)
    right_high, right_low = two_terms(right)
    return dot(left_high, right_high) + dot(left_high, right_low) + dot(left_low, right_high)


def sigmoid(v):
    return 1.0 / (1.0 + jnp.exp(-v))


def block(index):
    return slice(index * LEN, (index + 1) * LEN)


def lane_iota(rows=LEN):
    return lax.broadcasted_iota(jnp.int32, (rows, LEN), 1)


def mask_ts(seg_col, seg_row, i, j):
    same = seg_col[block(i), :] == seg_row[:, block(j)]
    if i != j:
        return same
    down = lax.broadcasted_iota(jnp.int32, (LEN, LEN), 0)
    return same & (down >= lane_iota())


def mask_st(seg_col, seg_row, j, i):
    same = seg_col[block(j), :] == seg_row[:, block(i)]
    if i != j:
        return same
    down = lax.broadcasted_iota(jnp.int32, (LEN, LEN), 0)
    return same & (down <= lane_iota())


def conv_rows(pad_ref, keep_ref, kernel, bias, start, lanes):
    summed = bias + kernel[3:4] * pad_ref[8 + start : 8 + start + LEN, lanes]
    for lag in (1, 2, 3):
        moved = pad_ref[8 + start - lag : 8 + start - lag + LEN, lanes]
        summed = summed + kernel[3 - lag : 4 - lag] * (moved * keep_ref[lag - 1, start : start + LEN, :])
    return summed


def widen(keep_ref, wide_ref):
    rows = keep_ref.shape[0]
    for lag in (1, 2, 3):
        wide_ref[lag - 1, :, :] = jnp.broadcast_to(keep_ref[:, lag : lag + 1], (rows, LEN))


def prep_kernel(
    conv_ref,
    small_ref,
    cos_ref,
    sin_ref,
    keep_ref,
    conv_kernel_ref,
    conv_bias_ref,
    state_kernel_ref,
    state_bias_ref,
    step_bias_ref,
    rate_ref,
    x_ref,
    xb_ref,
    slope_ref,
    state_ref,
    state_slope_ref,
    cum_ref,
    lag_ref,
    cum_row_ref,
    lag_row_ref,
    step_row_ref,
    sig_row_ref,
    q_ref,
    kv_ref,
    pad_ref,
    wide_ref,
):
    rows = conv_ref.shape[0]
    blocks = rows // LEN

    @pl.when(pl.program_id(0) == 0)
    def _():
        pad_ref[0:8, :] = jnp.zeros((8, LEN), jnp.float32)
        widen(keep_ref, wide_ref)
        for c in range(2):
            pad_ref[8 : rows + 8, :] = small_ref[:, block(c)]
            for i in range(blocks):
                pre = conv_rows(
                    pad_ref, wide_ref, state_kernel_ref[:, block(c)], state_bias_ref[:, block(c)], i * LEN, slice(0, LEN)
                )
                sig = sigmoid(pre)
                state_ref[block(i), block(c)] = pre * sig
                state_slope_ref[block(i), block(c)] = sig * (1.0 + pre * (1.0 - sig))

    @pl.when(pl.program_id(0) == 1)
    def _():
        down = lax.broadcasted_iota(jnp.int32, (LEN, LEN), 0)
        lower = jnp.where(down >= lane_iota(), 1.0, 0.0).astype(jnp.bfloat16)
        left_half = lane_iota() < HEAD_DIM
        carry = jnp.zeros((1, LEN), jnp.float32)
        heads = cum_row_ref.shape[0]
        for i in range(blocks):
            argument = small_ref[block(i), block(5)] + step_bias_ref[...]
            tail = jnp.exp(-jnp.abs(argument))
            grown = jnp.where(tail < 1e-3, tail - 0.5 * tail * tail, jnp.log(1.0 + tail))
            step = jnp.maximum(argument, 0.0) + grown
            scaled = step * rate_ref[...] * LOG2E
            first, rest = two_terms(scaled)
            last = scaled - first.astype(jnp.float32) - rest.astype(jnp.float32)
            cum = dot_nn(lower, first) + dot_nn(lower, rest) + dot_nn(lower, last.astype(jnp.bfloat16)) + carry
            carry = cum[LEN - 1 : LEN, :]
            lag = cum - jnp.log(step) * LOG2E
            cum_ref[block(i), :] = cum
            lag_ref[block(i), :] = lag
            cum_t, lag_t = cum.T, lag.T
            step_row_ref[:, block(i)] = step.T[:heads]
            sig_row_ref[:, block(i)] = sigmoid(argument).T[:heads]
            for h in range(heads):
                cum_row_ref[h, :, block(i)] = cum_t[h : h + 1]
                lag_row_ref[h, :, block(i)] = lag_t[h : h + 1]
            cosine, sine = cos_ref[block(i), :], sin_ref[block(i), :]
            kv = small_ref[block(i), block(4)]
            kv_ref[block(i), :] = jnp.where(left_half, rotate_tile(kv, cosine, sine), kv).astype(jnp.bfloat16)
            for p in range(q_ref.shape[1] // LEN):
                q_ref[block(i), block(p)] = rotate_tile(small_ref[block(i), block(2 + p)], cosine, sine).astype(
                    jnp.bfloat16
                )

    for sub in range(GROUP):
        lanes = block(sub)
        pad_ref[8 : rows + 8, :] = conv_ref[:, lanes]
        for i in range(blocks):
            pre = conv_rows(pad_ref, wide_ref, conv_kernel_ref[:, lanes], conv_bias_ref[:, lanes], i * LEN, slice(0, LEN))
            sig = sigmoid(pre)
            x = pre * sig
            x_ref[block(i), lanes] = x
            xb_ref[block(i), lanes] = x.astype(jnp.bfloat16)
            slope_ref[block(i), lanes] = sig * (1.0 + pre * (1.0 - sig))


def rotate_tile(v, cosine, sine):
    first = lax.rem(lane_iota(v.shape[0]), HEAD_DIM) < HEAD_DIM // 2
    swapped = jnp.where(first, pltpu.roll(v, LEN - HEAD_DIM // 2, 1), pltpu.roll(v, HEAD_DIM // 2, 1))
    return v * cosine + swapped * sine


def scan_kernel(
    chunks,
    heads,
    gate_ref,
    x_ref,
    xb_ref,
    state_ref,
    cum_ref,
    lag_row_ref,
    seg_col_ref,
    seg_row_ref,
    skip_ref,
    y_ref,
    gated_ref,
    row_ref,
    wide_ref,
    cross_ref,
    bias_ref,
    mix_ref,
    square_ref,
):
    step = pl.program_id(0)
    first = chunks[0]
    pairs = [(i, j) for i in chunks for j in range(max(0, i - 2), i + 1)]
    left_half = lane_iota() < HEAD_DIM

    @pl.when(step == 0)
    def _():
        for h in range(heads):
            for i in chunks:
                wide_ref[h, block(i - first), :] = jnp.broadcast_to(cum_ref[block(i), h : h + 1], (LEN, LEN))
        for i in chunks:
            low = max(0, i - 2)
            cross = three_dots(dot_nt, state_ref[block(i), LEN:], state_ref[low * LEN : (i + 1) * LEN, :LEN])
            for n, (i2, j) in enumerate(pairs):
                if i2 == i:
                    cross_ref[n] = cross[:, block(j - low)]
                    allowed = mask_ts(seg_col_ref, seg_row_ref, i, j)
                    bias_ref[n] = jnp.where(allowed, 0.0, hidden_bias)
        square_ref[...] = jnp.zeros(square_ref.shape, jnp.float32)

    tiles = (gate_ref, x_ref, xb_ref, skip_ref, y_ref, gated_ref)

    def head_pair(hp, gate_ref, x_ref, xb_ref, skip_ref, y_ref, gated_ref):
        for i in chunks:
            at = block(i - first)
            low = max(0, i - 2)
            for n, (i2, j) in enumerate(pairs):
                if i2 != i:
                    continue
                for e in range(2):
                    spread = wide_ref[2 * hp + e, at, :] - lag_row_ref[2 * hp + e, :, block(j)]
                    decay = jnp.exp2(spread + bias_ref[n])
                    mix_ref[i - first, block(e), block(j - low)] = (decay * cross_ref[n]).astype(jnp.bfloat16)
            both = dot_nn(mix_ref[i - first, :, : (i + 1 - low) * LEN], xb_ref[low * LEN : (i + 1) * LEN, :])
            y = jnp.where(left_half, both[:LEN], both[LEN:])
            y_ref[at, :] = y
            gate = gate_ref[at, :]
            gated = (y + skip_ref[...] * x_ref[at, :]) * (gate * sigmoid(gate))
            gated_ref[at, :] = gated
            square_ref[at, :] = square_ref[at, :] + gated * gated

    for sub in range(GROUP):
        head_pair(GROUP * step + sub, *[t.at[:, block(sub)] for t in tiles])

    @pl.when(step == pl.num_programs(0) - 1)
    def _():
        for i in chunks:
            at = block(i - first)
            total = jnp.sum(square_ref[at, :], axis=1, keepdims=True)
            row_ref[0:1, at] = jnp.broadcast_to(total, (LEN, LEN)).T[0:1]


def attention_kernel(chunks, q_ref, kv_ref, seg_col_ref, seg_row_ref, out_ref, lse_ref):
    scale = HEAD_DIM ** (-0.5) * LOG2E
    first = chunks[0]
    left_half = lane_iota() < HEAD_DIM
    zero = jnp.zeros((LEN, LEN), jnp.bfloat16)
    lse_ref[...] = jnp.zeros(lse_ref.shape, jnp.float32)
    for i in chunks:
        at = block(i - first)
        low = max(0, i - 2) * LEN
        span = (i + 1) * LEN - low
        allowed = jnp.concatenate([mask_ts(seg_col_ref, seg_row_ref, i, j) for j in range(low // LEN, i + 1)], axis=1)
        keys = kv_ref[low : low + span, :]
        turned = pltpu.roll(keys.astype(jnp.float32), HEAD_DIM, 1).astype(jnp.bfloat16)
        for p in range(q_ref.shape[1] // LEN):
            queries = q_ref[block(i), block(p)]
            result = []
            for e in range(2):
                masked = jnp.where(left_half == (e == 0), queries, zero)
                scores = dot_nt(masked, keys if e == 0 else turned) * scale
                scores = jnp.where(allowed, scores, hidden_bias)
                top = jnp.max(scores, axis=1, keepdims=True)
                weights = jnp.exp2(scores - top)
                total = jnp.sum(weights, axis=1, keepdims=True)
                probs = (weights * (1.0 / total)).astype(jnp.bfloat16)
                result.append(dot_nn(probs, turned if e == 0 else keys))
                lse = jnp.broadcast_to(top + jnp.log(total) * LOG2E, (LEN, LEN))
                lse_ref[2 * p + e : 2 * p + e + 1, at] = lse.T[0:1]
            out_ref[at, block(p)] = jnp.where(left_half, result[0], result[1]).astype(jnp.bfloat16)


def attention_back_kernel(chunks, final, *refs):
    q_ref, kv_ref, do_ref, lse_ref, seg_col_ref, seg_row_ref, cos_ref, sin_ref = refs[:8]
    if final:
        dk_in_ref, dv_in_ref, dq_ref, dkv_ref, dk_ref, dv_ref, turned_ref, key_t_ref = refs[8:]
    else:
        dq_ref, dk_ref, dv_ref, turned_ref, key_t_ref = refs[8:]
    scale = HEAD_DIM ** (-0.5)
    blocks = q_ref.shape[0] // LEN
    first = chunks[0]
    left_half = lane_iota() < HEAD_DIM
    zero = jnp.zeros((LEN, LEN), jnp.bfloat16)
    for i in range(chunks[-1] + 1):
        kv = kv_ref[block(i), :].astype(jnp.float32)
        turned_ref[block(i), :] = pltpu.roll(kv, HEAD_DIM, 1).astype(jnp.bfloat16)
        key_t_ref[:, block(i)] = kv.T[:HEAD_DIM].astype(jnp.bfloat16)
    if final:
        dk_ref[...] = dk_in_ref[...]
        dv_ref[...] = dv_in_ref[...]
    else:
        dk_ref[...] = jnp.zeros(dk_ref.shape, jnp.float32)
        dv_ref[...] = jnp.zeros(dv_ref.shape, jnp.float32)
    for i in chunks:
        at = block(i - first)
        low = max(0, i - 2) * LEN
        span = (i + 1) * LEN - low
        window = slice(low, low + span)
        allowed = jnp.concatenate([mask_st(seg_col_ref, seg_row_ref, j, i) for j in range(low // LEN, i + 1)], axis=0)
        keys, turned = kv_ref[window, :], turned_ref[window, :]
        for p in range(q_ref.shape[1] // LEN):
            queries, douts = q_ref[block(i), block(p)], do_ref[at, block(p)]
            back = []
            for e in range(2):
                side = left_half == (e == 0)
                q_half = jnp.where(side, queries, zero)
                do_half = jnp.where(side, douts, zero)
                h = 2 * p + e
                scores = dot_nt(keys if e == 0 else turned, q_half) * (scale * LOG2E)
                probs = jnp.exp2(jnp.where(allowed, scores, hidden_bias) - lse_ref[h : h + 1, at])
                dprobs = dot_nt(turned if e == 0 else keys, do_half)
                inner = jnp.sum(probs * dprobs, axis=0, keepdims=True)
                dscores = (probs * (dprobs - inner)).astype(jnp.bfloat16)
                dv_ref[window, :] = dv_ref[window, :] + dot_nn(probs.astype(jnp.bfloat16), do_half)
                dk_ref[window, :] = dk_ref[window, :] + dot_nn(dscores, q_half)
                back.append(dot_nn(key_t_ref[:, window], dscores))
            dq = jnp.concatenate(back, axis=0).T * scale
            dq_ref[at, block(p)] = rotate_tile(dq, cos_ref[block(i), :], -sin_ref[block(i), :]).astype(jnp.bfloat16)
    if not final:
        return
    for i in range(blocks):
        dk = dk_ref[block(i), :]
        dk = (dk + pltpu.roll(dk, HEAD_DIM, 1)) * scale
        dk = rotate_tile(dk, cos_ref[block(i), :], -sin_ref[block(i), :])
        dv = dv_ref[block(i), :]
        dv = dv + pltpu.roll(dv, HEAD_DIM, 1)
        dkv_ref[block(i), :] = jnp.where(left_half, dk, dv).astype(jnp.bfloat16)


def scan_back_kernel(
    chunks,
    heads,
    gmr_ref,
    gated_ref,
    square_a_ref,
    square_b_ref,
    dot_a_ref,
    dot_b_ref,
    gain_ref,
    gate_ref,
    y_ref,
    x_ref,
    xb_ref,
    state_ref,
    lag_ref,
    cum_row_ref,
    skip_ref,
    seg_col_ref,
    seg_row_ref,
    select_ref,
    dgate_ref,
    gy_ref,
    dx_ref,
    p_ref,
    grad_in_ref,
    grad_out_ref,
    sums_ref,
    gyb_ref,
    wide_ref,
    cross_ref,
    bias_ref,
    dcross_ref,
    inv_wide_ref,
    dot_wide_ref,
    inner_ref,
    mix_ref,
):
    step = pl.program_id(0)
    first = chunks[0]
    sources = chunks[-1] + 1
    left_half = lane_iota() < HEAD_DIM
    zero = jnp.zeros((LEN, LEN), jnp.bfloat16)
    spans = [(j, max(j, first), min(j + 3, sources)) for j in range(sources)]
    pairs = [(j, i) for j, start, stop in spans for i in range(start, stop)]

    @pl.when(step == 0)
    def _():
        for i in chunks:
            at = block(i - first)
            square = (square_a_ref[:, at] + square_b_ref[:, at]) / DSSM
            inv = lax.rsqrt(square + norm_eps)
            inv_wide_ref[at, :] = jnp.broadcast_to(inv, (LEN, LEN)).T
            dot = (dot_a_ref[:, at] + dot_b_ref[:, at]) / DSSM
            dot_wide_ref[at, :] = jnp.broadcast_to(dot, (LEN, LEN)).T
        p_ref[...] = jnp.zeros(p_ref.shape, jnp.float32)
        for h in range(heads):
            wide_ref[h] = jnp.broadcast_to(lag_ref[: sources * LEN, h : h + 1], (sources * LEN, LEN))
        for j, start, stop in spans:
            cross = three_dots(dot_nt, state_ref[block(j), :LEN], state_ref[start * LEN : stop * LEN, LEN:])
            for n, (j2, i) in enumerate(pairs):
                if j2 == j:
                    cross_ref[n] = cross[:, block(i - start)]
                    allowed = mask_st(seg_col_ref, seg_row_ref, j, i)
                    bias_ref[n] = jnp.where(allowed, 0.0, hidden_bias)
                    dcross_ref[n] = jnp.zeros((LEN, LEN), jnp.float32)

    tiles = (
        gmr_ref, gated_ref, gain_ref, gate_ref, y_ref, x_ref, xb_ref, skip_ref, dgate_ref, gy_ref, dx_ref, sums_ref
    )

    def head_pair(
        hp,
        select,
        gmr_ref,
        gated_ref,
        gain_ref,
        gate_ref,
        y_ref,
        x_ref,
        xb_ref,
        skip_ref,
        dgate_ref,
        gy_ref,
        dx_ref,
        sums_ref,
    ):
        skip = skip_ref[...]
        gain = gain_ref[...]
        skip_sum = jnp.zeros((1, LEN), jnp.float32)
        gain_sum = jnp.zeros((1, LEN), jnp.float32)
        for i in chunks:
            at = block(i - first)
            inv = inv_wide_ref[at, :]
            unit = gated_ref[at, :] * inv
            rows_grad = gmr_ref[at, :]
            grad = inv * (rows_grad * gain - unit * dot_wide_ref[at, :])
            gate = gate_ref[at, :]
            sig = sigmoid(gate)
            y = y_ref[at, :]
            x = x_ref[at, :]
            gy = grad * (gate * sig)
            dgate_ref[at, :] = (grad * (y + skip * x) * (sig * (1.0 + gate * (1.0 - sig)))).astype(jnp.bfloat16)
            gyb = gy.astype(jnp.bfloat16)
            gy_ref[at, :] = gy
            gyb_ref[at, :] = gyb
            high, rest = two_terms(gyb.astype(jnp.float32) * y)
            p_ref[:, at] = p_ref[:, at] + dot_nt(select, high) + dot_nt(select, rest)
            skip_sum = skip_sum + jnp.sum(gy * x, axis=0, keepdims=True)
            gain_sum = gain_sum + jnp.sum(rows_grad * unit, axis=0, keepdims=True)
        sums_ref[0:1, :] = skip_sum
        sums_ref[1:2, :] = gain_sum

        for j, start, stop in spans:
            x_pair = xb_ref[block(j), :]
            x_both = jnp.concatenate([jnp.where(left_half, x_pair, zero), jnp.where(left_half, zero, x_pair)], axis=0)
            wide = (stop - start) * LEN
            gy_rows = gyb_ref[(start - first) * LEN : (stop - first) * LEN, :]
            inner_ref[:, :wide] = dot_nt(x_both, gy_rows)
            for n, (j2, i) in enumerate(pairs):
                if j2 != j:
                    continue
                grown = dcross_ref[n]
                for e in range(2):
                    spread = cum_row_ref[2 * hp + e, :, block(i)] - wide_ref[2 * hp + e, block(j), :]
                    decay = jnp.exp2(spread + bias_ref[n])
                    grown = grown + inner_ref[block(e), block(i - start)] * decay
                    mix_ref[block(e), block(i - start)] = (decay * cross_ref[n]).astype(jnp.bfloat16)
                dcross_ref[n] = grown
            both = dot_nn(mix_ref[:, :wide], gy_rows)
            dx_ref[block(j), :] = jnp.where(left_half, both[:LEN], both[LEN:])

    for sub in range(GROUP):
        head_pair(GROUP * step + sub, select_ref[:, block(sub)], *[t.at[:, block(sub)] for t in tiles])

    @pl.when(step == pl.num_programs(0) - 1)
    def _():
        grad_out = {i: jnp.zeros((LEN, LEN), jnp.float32) for i in chunks}
        for j in range(sources):
            grad_in = jnp.zeros((LEN, LEN), jnp.float32)
            for n, (j2, i) in enumerate(pairs):
                if j2 != j:
                    continue
                high, rest = two_terms(dcross_ref[n])
                out_high, out_rest = two_terms(state_ref[block(i), LEN:])
                in_high, in_rest = two_terms(state_ref[block(j), :LEN])
                grad_in = grad_in + dot_nn(high, out_high) + dot_nn(high, out_rest) + dot_nn(rest, out_high)
                grad_out[i] = grad_out[i] + dot_tn(high, in_high) + dot_tn(high, in_rest) + dot_tn(rest, in_high)
            grad_in_ref[block(j), :] = grad_in
        for i in chunks:
            grad_out_ref[block(i - first), :] = grad_out[i]


def conv_back(grad_ref, value_ref, keep_ref, kernel_ref, out_ref, sum_ref, lanes, blocks):
    taps = kernel_ref[:, lanes]
    totals = [jnp.zeros((1, LEN), jnp.float32) for _ in range(5)]
    for i in range(blocks):
        here = grad_ref[i * LEN : (i + 1) * LEN, :]
        grad = taps[3:4] * here
        totals[4] = totals[4] + jnp.sum(here, axis=0, keepdims=True)
        totals[3] = totals[3] + jnp.sum(here * value_ref[8 + i * LEN : 8 + (i + 1) * LEN, :], axis=0, keepdims=True)
        for lag in (1, 2, 3):
            ahead = grad_ref[i * LEN + lag : (i + 1) * LEN + lag, :]
            grad = grad + taps[3 - lag : 4 - lag] * (ahead * keep_ref[lag - 1, i * LEN + lag : (i + 1) * LEN + lag, :])
            moved = value_ref[8 + i * LEN - lag : 8 + (i + 1) * LEN - lag, :]
            masked = here * keep_ref[lag - 1, i * LEN : (i + 1) * LEN, :]
            totals[3 - lag] = totals[3 - lag] + jnp.sum(masked * moved, axis=0, keepdims=True)
        out_ref[block(i), lanes] = grad.astype(jnp.bfloat16)
    for tap in range(5):
        sum_ref[tap : tap + 1, lanes] = totals[tap]


def scan_end_kernel(
    heads,
    gy_a_ref,
    gy_b_ref,
    dx_a_ref,
    dx_b_ref,
    p_a_ref,
    p_b_ref,
    in_a_ref,
    in_b_ref,
    out_a_ref,
    out_b_ref,
    xb_ref,
    slope_ref,
    state_slope_ref,
    conv_ref,
    small_ref,
    step_row_ref,
    sig_row_ref,
    rate_ref,
    skip_ref,
    keep_ref,
    seg_col_ref,
    seg_row_ref,
    select_ref,
    conv_kernel_ref,
    state_kernel_ref,
    dconv_ref,
    dstate_ref,
    dstep_ref,
    conv_sum_ref,
    state_sum_ref,
    step_sum_ref,
    grad_pad_ref,
    value_pad_ref,
    wide_ref,
    q_ref,
    flow_ref,
):
    step = pl.program_id(0)
    rows = conv_ref.shape[0]
    blocks = rows // LEN
    half = rows // 2
    count = flow_ref.shape[0]

    @pl.when(step == 0)
    def _():
        value_pad_ref[0:8, :] = jnp.zeros((8, LEN), jnp.float32)
        grad_pad_ref[rows : rows + 8, :] = jnp.zeros((8, LEN), jnp.float32)
        widen(keep_ref, wide_ref)
        q_ref[...] = jnp.zeros(q_ref.shape, jnp.float32)
        for c in range(2):
            if c == 0:
                grad_pad_ref[0:half, :] = (in_a_ref[...] + in_b_ref[0:half, :]) * state_slope_ref[0:half, block(c)]
                grad_pad_ref[half:rows, :] = in_b_ref[half:rows, :] * state_slope_ref[half:rows, block(c)]
            else:
                grad_pad_ref[0:half, :] = out_a_ref[...] * state_slope_ref[0:half, block(c)]
                grad_pad_ref[half:rows, :] = out_b_ref[...] * state_slope_ref[half:rows, block(c)]
            value_pad_ref[8 : rows + 8, :] = small_ref[:, block(c)]
            conv_back(grad_pad_ref, value_pad_ref, wide_ref, state_kernel_ref, dstate_ref, state_sum_ref, block(c), blocks)

    tiles = (
        gy_a_ref, gy_b_ref, dx_a_ref, dx_b_ref, xb_ref, slope_ref, conv_ref, skip_ref, conv_kernel_ref, dconv_ref, conv_sum_ref
    )

    def head_pair(
        select,
        gy_a_ref,
        gy_b_ref,
        dx_a_ref,
        dx_b_ref,
        xb_ref,
        slope_ref,
        conv_ref,
        skip_ref,
        conv_kernel_ref,
        dconv_ref,
        conv_sum_ref,
    ):
        for j in range(blocks):
            dx = dx_b_ref[block(j), :]
            if j < blocks // 2:
                dx = dx + dx_a_ref[block(j), :]
                gy = gy_a_ref[block(j), :]
            else:
                gy = gy_b_ref[block(j - blocks // 2), :]
            high, rest = two_terms(dx * xb_ref[block(j), :].astype(jnp.float32))
            q_ref[:, block(j)] = q_ref[:, block(j)] + dot_nt(select, high) + dot_nt(select, rest)
            grad_pad_ref[block(j), :] = (dx + gy * skip_ref[...]) * slope_ref[block(j), :]
        value_pad_ref[8 : rows + 8, :] = conv_ref[...]
        conv_back(
            grad_pad_ref, value_pad_ref, wide_ref, conv_kernel_ref, dconv_ref, conv_sum_ref, slice(0, LEN), blocks
        )

    for sub in range(GROUP):
        head_pair(select_ref[:, block(sub)], *[t.at[:, block(sub)] for t in tiles])

    @pl.when(step == pl.num_programs(0) - 1)
    def _():
        q = q_ref[...]
        flow_ref[:, 0:half] = p_a_ref[...] - q[:, 0:half]
        flow_ref[:, half:rows] = p_b_ref[...] - q[:, half:rows]
        rate = jnp.broadcast_to(rate_ref[...], (LEN, LEN)).T[:count]
        bias_total = jnp.zeros((count, LEN), jnp.float32)
        decay_total = jnp.zeros((count, LEN), jnp.float32)
        for j in range(blocks):
            log_grad = jnp.zeros((count, LEN), jnp.float32)
            for i in range(j, min(j + 3, blocks)):
                chosen = jnp.where(mask_st(seg_col_ref, seg_row_ref, j, i), 1.0, 0.0).astype(jnp.bfloat16)
                high, rest = two_terms(flow_ref[:, block(i)])
                log_grad = log_grad + dot_nt(high, chosen) + dot_nt(rest, chosen)
            step = step_row_ref[:, block(j)]
            grad_step = jnp.where(step > 1e-30, q[:, block(j)] / step, 0.0) + log_grad * rate
            grad_arg = grad_step * sig_row_ref[:, block(j)]
            bias_total = bias_total + grad_arg
            decay_total = decay_total + log_grad * step
            tall = jnp.concatenate([grad_arg, jnp.zeros((LEN - count, LEN), jnp.float32)], axis=0)
            dstep_ref[block(j), :] = tall.T.astype(jnp.bfloat16)
        step_sum_ref[0:count, :] = jnp.broadcast_to(jnp.sum(bias_total, axis=1, keepdims=True), (count, LEN))
        step_sum_ref[count : 2 * count, :] = jnp.broadcast_to(
            jnp.sum(decay_total * rate, axis=1, keepdims=True), (count, LEN)
        )


def whole_block(shape):
    return pl.BlockSpec(shape, lambda step: (0,) * len(shape), pipeline_mode=pl.Buffered(1))


def tile(rows, row_block=0, first=0):
    return pl.BlockSpec((rows, GROUP * LEN), lambda step: (row_block, first + step))


def call(kernel, steps, out_shape, out_specs, scratch, operands, specs, flops):
    moved = sum(o.size * o.dtype.itemsize for o in operands) + sum(o.size * o.dtype.itemsize for o in out_shape)
    return pl.pallas_call(
        kernel,
        grid=(steps,),
        out_shape=out_shape,
        in_specs=[s or whole_block(o.shape) for o, s in zip(operands, specs)],
        out_specs=[s or whole_block(o.shape) for o, s in zip(out_shape, out_specs)],
        scratch_shapes=scratch,
        compiler_params=pltpu.CompilerParams(vmem_limit_bytes=VMEM_BYTES),
        cost_estimate=pl.CostEstimate(flops=flops, bytes_accessed=moved, transcendentals=0),
    )(*operands)


def f32(*shape):
    return jax.ShapeDtypeStruct(shape, jnp.float32)


def b16(*shape):
    return jax.ShapeDtypeStruct(shape, jnp.bfloat16)


HEAD_ROWS = 16
GROUP = 3
VMEM_BYTES = 60 * 1024 * 1024


def scan_prep(width, wide_in, small, cosine, sine, keep, conv_kernel, conv_bias, *rest):
    rows = wide_in.shape[0]
    steps = width // LEN // GROUP
    outs = [
        f32(rows, width),
        b16(rows, width),
        f32(rows, width),
        f32(rows, 2 * LEN),
        f32(rows, 2 * LEN),
        f32(rows, LEN),
        f32(rows, LEN),
        f32(HEAD_ROWS, 1, rows),
        f32(HEAD_ROWS, 1, rows),
        f32(HEAD_ROWS, rows),
        f32(HEAD_ROWS, rows),
        b16(rows, 2 * LEN),
        b16(rows, LEN),
    ]
    scratch = [pltpu.VMEM((rows + 8, LEN), jnp.float32), pltpu.VMEM((3, rows + 8, LEN), jnp.float32)]
    operands = (wide_in, small, cosine, sine, keep, conv_kernel, conv_bias, *rest)
    specs = [tile(rows, 0, steps), None, None, None, None, tile(4), tile(1)] + [None] * len(rest)
    return call(prep_kernel, steps, outs, [tile(rows)] * 3 + [None] * 10, scratch, operands, specs, 10**9)


def scan_forward(chunks, heads, wide_in, x, xb, *rest):
    width = x.shape[1]
    rows = LEN * len(chunks)
    at = chunks[0] // len(chunks)
    count = sum(min(i, 2) + 1 for i in chunks)
    outs = [f32(rows, width), f32(rows, width), f32(1, rows)]
    scratch = [
        pltpu.VMEM((heads, rows, LEN), jnp.float32),
        pltpu.VMEM((count, LEN, LEN), jnp.float32),
        pltpu.VMEM((count, LEN, LEN), jnp.float32),
        pltpu.VMEM((len(chunks), 2 * LEN, 3 * LEN), jnp.bfloat16),
        pltpu.VMEM((rows, LEN), jnp.float32),
    ]
    specs = [tile(rows, at), tile(rows, at), tile((chunks[-1] + 1) * LEN)] + [None] * (len(rest) - 1) + [tile(1)]
    kernel = functools.partial(scan_kernel, chunks, heads)
    operands = (wide_in, x, xb, *rest)
    return call(kernel, heads // 2 // GROUP, outs, [tile(rows), tile(rows), None], scratch, operands, specs, 2 * 10**9)


def attention_forward(chunks, q, kv, seg_col, seg_row):
    rows = LEN * len(chunks)
    outs = [b16(rows, q.shape[1]), f32(8, rows)]
    kernel = functools.partial(attention_kernel, chunks)
    return call(kernel, 1, outs, [None] * 2, [], (q, kv, seg_col, seg_row), [None] * 4, 10**9)


def attention_backward(chunks, final, *operands):
    q = operands[0]
    rows = q.shape[0]
    partial = [f32(rows, LEN), f32(rows, LEN)]
    sums = [pltpu.VMEM((rows, LEN), jnp.float32)] * 2
    outs = [b16(LEN * len(chunks), q.shape[1])] + ([b16(rows, LEN)] if final else partial)
    scratch = (sums if final else []) + [
        pltpu.VMEM((rows, LEN), jnp.bfloat16),
        pltpu.VMEM((HEAD_DIM, rows), jnp.bfloat16),
    ]
    kernel = functools.partial(attention_back_kernel, chunks, final)
    return call(kernel, 1, outs, [None] * len(outs), scratch, operands, [None] * len(operands), 2 * 10**9)


def scan_backward(chunks, heads, *operands):
    rows, width = operands[0].shape
    at = chunks[0] // len(chunks)
    sources = (chunks[-1] + 1) * LEN
    count = sum(min(i, 2) + 1 for i in chunks)
    outs = [
        b16(rows, width),
        f32(rows, width),
        f32(sources, width),
        f32(HEAD_ROWS, rows),
        f32(sources, LEN),
        f32(rows, LEN),
        f32(8, width),
    ]
    scratch = [
        pltpu.VMEM((rows, LEN), jnp.bfloat16),
        pltpu.VMEM((heads, sources, LEN), jnp.float32),
        pltpu.VMEM((count, LEN, LEN), jnp.float32),
        pltpu.VMEM((count, LEN, LEN), jnp.float32),
        pltpu.VMEM((count, LEN, LEN), jnp.float32),
        pltpu.VMEM((rows, LEN), jnp.float32),
        pltpu.VMEM((rows, LEN), jnp.float32),
        pltpu.VMEM((2 * LEN, 3 * LEN), jnp.float32),
        pltpu.VMEM((2 * LEN, 3 * LEN), jnp.bfloat16),
    ]
    specs = [tile(rows), tile(rows), None, None, None, None, tile(1), tile(rows, at), tile(rows), tile(rows, at), tile(sources)]
    specs += [None, None, None, tile(1), None, None, tile(HEAD_ROWS)]
    out_specs = [tile(rows), tile(rows), tile(sources), None, None, None, tile(8)]
    kernel = functools.partial(scan_back_kernel, chunks, heads)
    return call(kernel, heads // 2 // GROUP, outs, out_specs, scratch, operands, specs, 4 * 10**9)


def scan_end(heads, *operands):
    rows, width = 2 * operands[0].shape[0], operands[0].shape[1]
    steps = heads // 2 // GROUP
    outs = [
        b16(rows, width),
        b16(rows, 2 * LEN),
        b16(rows, LEN),
        f32(8, width),
        f32(8, 2 * LEN),
        f32(2 * HEAD_ROWS, LEN),
    ]
    scratch = [
        pltpu.VMEM((rows + 8, LEN), jnp.float32),
        pltpu.VMEM((rows + 8, LEN), jnp.float32),
        pltpu.VMEM((3, rows + 8, LEN), jnp.float32),
        pltpu.VMEM((HEAD_ROWS, rows), jnp.float32),
        pltpu.VMEM((HEAD_ROWS, rows), jnp.float32),
    ]
    half = rows // 2
    specs = [tile(half), tile(half), tile(half), tile(rows)] + [None] * 6 + [tile(rows), tile(rows), None]
    specs += [tile(rows, 0, steps)] + [None] * 4 + [tile(1), None, None, None, tile(HEAD_ROWS), tile(4), None]
    out_specs = [tile(rows), None, None, tile(8), None, None]
    kernel = functools.partial(scan_end_kernel, heads)
    return call(kernel, steps, outs, out_specs, scratch, operands, specs, 2 * 10**9)


def assemble_kernel(
    core_ref, own_ref, far_ref, mixer_out_ref, attn_out_ref, mixer_proj_ref, query_ref, pair_ref, state_ref, step_ref
):
    at = pl.program_id(0)
    count = pl.num_programs(0)
    width = mixer_proj_ref.shape[2]
    model_width = mixer_out_ref.shape[1]
    split = mixer_out_count(width)

    def write(source):
        @pl.when(at < split)
        def _():
            mixer_out_ref[...] = source[:, :model_width]

        @pl.when(at >= split)
        def _():
            attn_out_ref[...] = source[:, :model_width]

        start = model_width
        mixer_proj_ref[:, 0, :] = source[:, start : start + width]
        start += width
        query_ref[...] = source[:, start : start + query_ref.shape[1]]
        start += query_ref.shape[1]
        pair_ref[:, 0, :] = source[:, start : start + LEN]
        start += LEN
        mixer_proj_ref[:, 1, :] = source[:, start : start + width]
        start += width
        state_ref[...] = source[:, start : start + 2 * LEN]
        step_ref[...] = source[:, start + 2 * LEN :]

    mine = at // (count // 2) == core_ref[0]

    @pl.when(mine)
    def _():
        write(own_ref)

    @pl.when(jnp.logical_not(mine))
    def _():
        write(far_ref)


def mixer_out_count(width):
    return width // LEN


def assemble(own, far, width, query_width):
    half, columns = own.shape
    rows = 2 * half
    blocks = rows // LEN
    split = mixer_out_count(width)
    core = lax.axis_index("core").astype(jnp.int32).reshape(1)

    def source(flip):
        def index(at, core_ref):
            first = (blocks // 2) * jnp.where(flip, 1 - core_ref[0], core_ref[0])
            return (jnp.clip(at - first, 0, blocks // 2 - 1), 0)

        return pl.BlockSpec((LEN, columns), index)

    def plain(count):
        return pl.BlockSpec((LEN, count), lambda at, core_ref: (at, 0))

    out_specs = [
        pl.BlockSpec((LEN, rows), lambda at, core_ref: (jnp.minimum(at, split - 1), 0)),
        pl.BlockSpec((LEN, rows), lambda at, core_ref: (jnp.maximum(at - split, 0), 0)),
        pl.BlockSpec((LEN, 2, width), lambda at, core_ref: (at, 0, 0)),
        plain(query_width),
        pl.BlockSpec((LEN, 1, LEN), lambda at, core_ref: (at, 0, 0)),
        plain(2 * LEN),
        plain(LEN),
    ]
    out_shape = [
        f32(width, rows),
        f32(rows - width, rows),
        f32(rows, 2, width),
        f32(rows, query_width),
        f32(rows, 1, LEN),
        f32(rows, 2 * LEN),
        f32(rows, LEN),
    ]
    return pl.pallas_call(
        assemble_kernel,
        grid_spec=pltpu.PrefetchScalarGridSpec(
            num_scalar_prefetch=1, grid=(blocks,), in_specs=[source(False), source(True)], out_specs=out_specs
        ),
        out_shape=out_shape,
        compiler_params=pltpu.CompilerParams(vmem_limit_bytes=VMEM_BYTES),
        cost_estimate=pl.CostEstimate(flops=0, bytes_accessed=16 * own.size, transcendentals=0),
    )(core, own, far)


def silu_slope(argument):
    logistic = jax.nn.sigmoid(argument)
    return logistic * (1.0 + argument * (1.0 - logistic))


def rope_tables(rows):
    half_size = HEAD_DIM // 2
    inverse = np.float32(rope_base) ** (-(2.0 * np.arange(half_size, dtype=np.float32)) / HEAD_DIM)
    angles = np.arange(rows, dtype=np.float32)[:, None] * inverse.astype(np.float32)[None, :]
    cosine, sine = np.cos(angles), np.sin(angles)
    return (
        np.concatenate([cosine] * 4, axis=1).astype(np.float32),
        np.concatenate([-sine, sine, -sine, sine], axis=1).astype(np.float32),
    )


def norm_backward(grad_unit, unit_rows, inv_rms):
    return inv_rms * (grad_unit - unit_rows * jnp.mean(grad_unit * unit_rows, axis=-1, keepdims=True))


def dot32(left, right):
    return jnp.dot(left, right, preferred_element_type=jnp.float32)


def after(value, *others):
    return lax.optimization_barrier((value, *others))[0]


def swap(values, name):
    return lax.ppermute(values, name, PAIR)


def exchange(values, name):
    return values + swap(values, name)


def core_rows(values, index):
    half = values.shape[1] // 2
    return lax.dynamic_slice_in_dim(values, index * half, half, 1)


def rows_dot(left, right, index):
    return lax.dot_general(core_rows(left, index), right, (((0,), (0,)), ((), ())), preferred_element_type=jnp.float32)


def on_device(
    layer_input,
    segments,
    input_gain,
    mixer_proj,
    state_proj,
    step_proj,
    step_bias,
    decay_log,
    skip_gain,
    conv_kernel,
    conv_bias,
    state_kernel,
    state_bias,
    gated_gain,
    mixer_out,
    query_proj,
    key_value_weight,
    attn_out,
    ffn_gain,
    ffn_gate,
    ffn_up,
    ffn_down,
    cotangent,
):
    segment = segments.reshape(-1)
    rows, model_width = layer_input.shape
    width = mixer_proj.shape[2]
    heads = step_proj.shape[1]
    state_size = state_proj.shape[1] // 2
    query_width = query_proj.shape[1]
    pair_width = key_value_weight.shape[2]
    place = lax.axis_index("core")
    cosine, sine = rope_tables(rows)
    select = np.arange(HEAD_ROWS)[:, None] == np.arange(width)[None, :] // HEAD_DIM
    select = jnp.asarray(select.astype(np.float32)).astype(jnp.bfloat16)
    seg_col, seg_row = segment[:, None], segment[None, :]
    keep = [jnp.ones((rows,), jnp.float32)]
    for lag in (1, 2, 3):
        previous = jnp.concatenate([jnp.full((lag,), -1, jnp.int32), segment[:-lag]])
        keep.append((previous == segment).astype(jnp.float32))
    keep = jnp.pad(jnp.stack(keep, axis=1), ((0, 8), (0, 4)))
    pad_heads = ((0, 0), (0, LEN - heads))
    rate_row = jnp.pad(-jnp.exp(decay_log)[None, :], pad_heads)
    step_bias_row = jnp.pad(step_bias[None, :], pad_heads)
    skip_row = jnp.repeat(skip_gain, HEAD_DIM)[None, :]
    gain_row = gated_gain[None, :]
    wide_proj = mixer_proj.reshape(model_width, 2 * width)
    small_proj = jnp.concatenate(
        [
            state_proj,
            query_proj,
            key_value_weight.reshape(model_width, pair_width),
            jnp.pad(step_proj, pad_heads),
        ],
        axis=1,
    )

    tokens = layer_input.astype(jnp.float32)
    inv_rms_in = lax.rsqrt(jnp.mean(tokens * tokens, axis=-1, keepdims=True) + norm_eps)
    unit_in = tokens * inv_rms_in
    normed_input = (unit_in * input_gain).astype(jnp.bfloat16)
    small_in = dot32(normed_input, small_proj)
    wide_in = dot32(normed_input, wide_proj)
    x, xb, slope, state, state_slope, cum, lag, cum_row, lag_row, step_row, sig_row, queries, pairs = scan_prep(
        width,
        wide_in,
        small_in,
        cosine,
        sine,
        keep,
        conv_kernel,
        conv_bias[None, :],
        state_kernel,
        state_bias[None, :],
        step_bias_row,
        rate_row,
    )

    blocks = rows // LEN
    late = tuple(range(blocks // 2, blocks))
    early = tuple(range(blocks // 2))
    half = {}
    for chunks in (late, early):
        h = {"span": slice(chunks[0] * LEN, (chunks[-1] + 1) * LEN)}
        h["y"], h["gated"], h["square"] = scan_forward(
            chunks, heads, wide_in, x, xb, state, cum, lag_row, seg_col, seg_row, skip_row
        )
        half[chunks] = h
    squares = jnp.concatenate([half[early]["square"], half[late]["square"]], axis=1)
    squares_far = swap(squares, "tensor")
    ready = squares
    for chunks in (late, early):
        h = half[chunks]
        h["attended"], h["lse"] = attention_forward(chunks, after(queries, ready), pairs, seg_col, seg_row)
        if chunks == late:
            squares_far = after(squares_far, h["lse"])
            squares_all = squares + squares_far
        h["square"], h["square_far"] = squares[:, h["span"]], squares_far[:, h["span"]]
        h["inv_gated"] = lax.rsqrt(squares_all[:, h["span"]].reshape(-1, 1) / DSSM + norm_eps)
        h["mixer_rows"] = (h["gated"] * h["inv_gated"] * gated_gain).astype(jnp.bfloat16)
        h["part"] = dot32(h["mixer_rows"], mixer_out) + dot32(h["attended"], attn_out)
        h["branch_far"] = swap(h["part"], "tensor")
        ready = h["part"]

    ready = None
    for chunks in (late, early):
        h = half[chunks]
        span = h["span"]
        far = h["branch_far"] if ready is None else after(h["branch_far"], ready)
        hidden = tokens[span] + (h["part"] + far)
        inv_rms_ffn = lax.rsqrt(jnp.mean(hidden * hidden, axis=-1, keepdims=True) + norm_eps)
        unit_ffn = hidden * inv_rms_ffn
        normed_ffn = (unit_ffn * ffn_gain).astype(jnp.bfloat16)
        gate_rows = dot32(normed_ffn, ffn_gate)
        up_rows = dot32(normed_ffn, ffn_up)
        gate_silu = jax.nn.silu(gate_rows)
        activated = (gate_silu * up_rows).astype(jnp.bfloat16)
        grad_activated = dot32(cotangent[span], ffn_down.T)
        grad_gate_rows = (grad_activated * up_rows * silu_slope(gate_rows)).astype(jnp.bfloat16)
        grad_up_rows = (grad_activated * gate_silu).astype(jnp.bfloat16)
        partial_ffn = dot32(grad_gate_rows, ffn_gate.T) + dot32(grad_up_rows, ffn_up.T)
        h["part_ffn"] = partial_ffn
        h["ffn_far"] = swap(partial_ffn, "tensor")
        ready = partial_ffn
        h.update(
            hidden=hidden,
            unit_ffn=unit_ffn,
            inv_rms_ffn=inv_rms_ffn,
            normed_ffn=normed_ffn,
            activated=activated,
            grad_gate_rows=grad_gate_rows,
            grad_up_rows=grad_up_rows,
        )

    def whole(name):
        return jnp.concatenate([half[early][name], half[late][name]], axis=0)

    grad_ffn_gain = 0.0
    ready = half[early]["part_ffn"]
    for chunks in (late, early):
        h = half[chunks]
        span = h["span"]
        grad_normed_ffn = h["part_ffn"] + after(h["ffn_far"], ready)
        grad_ffn_gain = grad_ffn_gain + jnp.sum(grad_normed_ffn * h["unit_ffn"], axis=0)
        h["grad_hidden"] = cotangent[span].astype(jnp.float32) + norm_backward(
            grad_normed_ffn * ffn_gain, h["unit_ffn"], h["inv_rms_ffn"]
        )
        grad_branch = h["grad_hidden"].astype(jnp.bfloat16)
        h["grad_branch"] = grad_branch
        grad_mixer_rows = dot32(grad_branch, mixer_out.T)
        unit_gated = h["gated"] * h["inv_gated"]
        gated_dot = jnp.sum(grad_mixer_rows * gated_gain * unit_gated, axis=-1)[None, :]
        dot_far = swap(gated_dot, "tensor")
        grad_attended = dot32(after(grad_branch, gated_dot), attn_out.T).astype(jnp.bfloat16)
        operands = (queries, pairs, grad_attended, h["lse"], seg_col, seg_row, cosine, sine)
        if chunks == late:
            h["grad_queries"], grad_keys, grad_values = attention_backward(chunks, False, *operands)
            normed_ffn = after(whole("normed_ffn"), grad_keys)
            sides = [
                (normed_ffn, whole("grad_gate_rows")),
                (normed_ffn, whole("grad_up_rows")),
                (after(whole("activated"), grad_keys), cotangent),
            ]
            sent = [swap(rows_dot(left, right, 1 - place), "core") for left, right in sides]
            kept = [rows_dot(left, right, place) for left, right in sides]
            first = jnp.concatenate([a + b for a, b in zip(kept, sent)], axis=1)
            first_sum = lax.psum_scatter(first, ("y", "x"), scatter_dimension=0, tiled=True)
            depth = first_sum.shape[0] // 2
            zh = lax.axis_index("zh")
            first_own = lax.dynamic_slice_in_dim(first_sum, zh * depth, depth, 0) + swap(
                lax.dynamic_slice_in_dim(first_sum, (1 - zh) * depth, depth, 0), "zh"
            )
            first_all = lax.all_gather(first_own, ("core", "y", "x", "zh"), axis=0, tiled=True)
            dot_far = after(dot_far, first)
        else:
            h["grad_queries"], grad_pairs = attention_backward(chunks, True, *operands, grad_keys, grad_values)
        h["grad_gate"], h["gy"], h["dx"], h["p"], h["grad_in"], h["grad_out"], h["sums"] = scan_backward(
            chunks,
            heads,
            grad_mixer_rows,
            h["gated"],
            h["square"],
            h["square_far"],
            gated_dot,
            after(dot_far, h["grad_queries"]),
            gain_row,
            wide_in,
            h["y"],
            x,
            xb,
            state,
            lag,
            cum_row,
            skip_row,
            seg_col,
            seg_row,
            select,
        )
        ready = h["p"]
    ends = []
    for name in ("gy", "dx", "p", "grad_in", "grad_out"):
        ends += [half[early][name], half[late][name]]
    grad_conv, grad_state, grad_step, conv_sum, state_sum, step_sum = scan_end(
        heads,
        *ends,
        xb,
        slope,
        state_slope,
        wide_in,
        small_in,
        step_row,
        sig_row,
        rate_row,
        skip_row,
        keep,
        seg_col,
        seg_row,
        select,
        conv_kernel,
        state_kernel,
    )

    grad_queries, grad_gate = whole("grad_queries"), whole("grad_gate")
    outer = jnp.concatenate([whole("mixer_rows"), whole("attended")], axis=1)
    grad_branch = whole("grad_branch")
    right = jnp.concatenate([grad_gate, grad_queries, grad_pairs, grad_conv, grad_state, grad_step], axis=1)
    far_outer = swap(rows_dot(outer, grad_branch, 1 - place), "core")
    far_inner = swap(rows_dot(normed_input, right, 1 - place), "core")

    wide_grad = jnp.concatenate([grad_gate, grad_conv], axis=1)
    small_grad = jnp.concatenate([grad_state, grad_queries, grad_pairs, grad_step], axis=1)
    partial_normed = dot32(wide_grad, wide_proj.T) + dot32(small_grad, small_proj.T)
    normed_far = swap(after(partial_normed, first_own), "tensor")
    sums = half[early]["sums"] + half[late]["sums"]
    over_tensor = [jnp.sum(partial_normed * unit_in, axis=0), state_sum[:4], state_sum[4]]
    alone = [
        step_sum[:heads, 0],
        step_sum[HEAD_ROWS : HEAD_ROWS + heads, 0],
        jnp.sum(sums[0].reshape(heads, HEAD_DIM), axis=1),
        conv_sum[:4],
        conv_sum[4],
        sums[1],
        grad_ffn_gain,
    ]

    def packed(values):
        flat = jnp.concatenate([v.reshape(-1) for v in values])
        count = -(-flat.shape[0] // model_width)
        return jnp.pad(flat, (0, count * model_width - flat.shape[0])).reshape(count, model_width)

    def unpacked(table, values):
        flat, result, start = table.T.reshape(-1), [], 0
        for v in values:
            result.append(flat[start : start + v.size].reshape(v.shape))
            start += v.size
        return result

    tables = [packed(over_tensor), packed(alone)]
    shared_end = heads + tables[0].shape[0]
    table = jnp.concatenate(tables, axis=0)
    table_end = heads + table.shape[0]
    table = (core_rows(table, place) + swap(core_rows(table, 1 - place), "core")).T
    table = jnp.pad(table, ((0, 0), (heads, LEN - table_end)))
    kept_outer, kept_inner = rows_dot(outer, grad_branch, place), rows_dot(normed_input, right, place)
    at_step = model_width + 2 * width + query_width + pair_width + 2 * state_size
    inner = kept_inner + far_inner
    inner_end = at_step - model_width
    second = jnp.concatenate([kept_outer + far_outer, inner[:, :inner_end], inner[:, inner_end:] + table], axis=1)
    peers = 16
    peer_rows = second.shape[0] // peers
    columns = second.shape[1]
    second = after(second, first_own)
    second = lax.all_to_all(second.reshape(peers, peer_rows, columns), ("y", "x"), 0, 0, tiled=True)
    second = after(second, normed_far)
    second = jnp.sum(second, axis=0)
    depth = peer_rows // 2
    second = lax.dynamic_slice_in_dim(second, zh * depth, depth, 0) + swap(
        lax.dynamic_slice_in_dim(second, (1 - zh) * depth, depth, 0), "zh"
    )
    at_state = at_step - 2 * state_size
    both = second[:, at_state:]
    summed = exchange(both, "tensor")
    lane = np.arange(both.shape[1]) - 2 * state_size
    is_shared = (lane < 0) | ((lane >= heads) & (lane < shared_end))
    second = jnp.concatenate([second[:, :at_state], jnp.where(is_shared[None, :], summed, both)], axis=1)
    other = swap(second, "zh")
    second = jnp.where(
        zh == 0, jnp.concatenate([second, other], axis=0), jnp.concatenate([other, second], axis=0)
    )
    down = dot32(whole("activated"), ffn_down)
    down_far = swap(after(down, second), "tensor")
    second = jnp.broadcast_to(after(second, first_all)[None], (peers, peer_rows, columns))
    second = lax.all_to_all(second, ("y", "x"), 0, 0, tiled=True)
    second = after(second, down_far).reshape(peers * peer_rows, columns)
    second_far = swap(second, "core")
    grad_mixer_out, grad_attn_out, grad_mixer_proj, grad_query_proj, grad_keyval, grad_state_proj, step_block = assemble(
        second, second_far, width, query_width
    )

    grad_hidden = whole("grad_hidden")
    grad_normed = partial_normed + normed_far
    input_grad = grad_hidden + norm_backward(grad_normed * input_gain, unit_in, inv_rms_in)
    layer_output = (whole("hidden") + (down + down_far)).astype(jnp.bfloat16)

    small_shared = unpacked(step_block[:, heads:shared_end], over_tensor)
    small_alone = unpacked(step_block[:, shared_end:table_end], alone)
    return (
        layer_output,
        input_grad,
        small_shared[0],
        grad_mixer_proj,
        grad_state_proj,
        step_block[:, :heads],
        small_alone[0],
        small_alone[1],
        small_alone[2],
        small_alone[3],
        small_alone[4],
        small_shared[1],
        small_shared[2],
        small_alone[5],
        grad_mixer_out,
        grad_query_proj,
        grad_keyval,
        grad_attn_out,
        small_alone[6],
        first_all[:, :model_width],
        first_all[:, model_width : 2 * model_width],
        first_all[:, 2 * model_width :],
    )


def solution(mesh):
    dp, whole_spec, columns = P(DP, None), P(), P(None, "tensor")
    per_channel, middle = P("tensor"), P(None, "tensor", None)
    last, by_rows = P(None, None, "tensor"), P("tensor", None)
    weights = (
        whole_spec,
        last,
        whole_spec,
        columns,
        per_channel,
        per_channel,
        per_channel,
        columns,
        per_channel,
        whole_spec,
        whole_spec,
        per_channel,
        by_rows,
        columns,
        middle,
        by_rows,
        whole_spec,
        columns,
        columns,
        by_rows,
    )
    mesh = jax.sharding.Mesh(mesh.devices.reshape(4, 2, 4, 2, 2), (*DP, "tensor"))
    return jax.shard_map(
        on_device, mesh=mesh, in_specs=(dp, dp, *weights, dp), out_specs=(dp, dp, *weights), check_vma=False
    )
```

```python
import functools

import jax
import jax.numpy as jnp
import numpy as np
from jax import lax
from jax.experimental import pallas as pl
from jax.experimental.pallas import tpu as pltpu
from jax.sharding import PartitionSpec as P

HEAD_DIM = 64
DSSM = 1536
DP = ("y", "zh", "x", "core")
PAIR = [(0, 1), (1, 0)]
LOG2E = 1.4426950408889634
hidden_bias = -1e30
norm_eps = 1e-05
rope_base = 10000.0
LEN = 128


def dot_nn(left, right):
    return lax.dot_general(
        left, right, (((1,), (0,)), ((), ())), preferred_element_type=jnp.float32
    )


def dot_nt(left, right):
    return lax.dot_general(
        left, right, (((1,), (1,)), ((), ())), preferred_element_type=jnp.float32
    )


def dot_tn(left, right):
    return lax.dot_general(
        left, right, (((0,), (0,)), ((), ())), preferred_element_type=jnp.float32
    )


def two_terms(v):
    high = v.astype(jnp.bfloat16)
    return high, (v - high.astype(jnp.float32)).astype(jnp.bfloat16)


def three_dots(dot, left, right):
    left_high, left_low = two_terms(left)
    right_high, right_low = two_terms(right)
    return dot(left_high, right_high) + dot(left_high, right_low) + dot(left_low, right_high)


def sigmoid(v):
    return 1.0 / (1.0 + jnp.exp(-v))


def block(index):
    return slice(index * LEN, (index + 1) * LEN)


def lane_iota(rows=LEN):
    return lax.broadcasted_iota(jnp.int32, (rows, LEN), 1)


def mask_ts(seg_col, seg_row, i, j):
    same = seg_col[block(i), :] == seg_row[:, block(j)]
    if i != j:
        return same
    down = lax.broadcasted_iota(jnp.int32, (LEN, LEN), 0)
    return same & (down >= lane_iota())


def mask_st(seg_col, seg_row, j, i):
    same = seg_col[block(j), :] == seg_row[:, block(i)]
    if i != j:
        return same
    down = lax.broadcasted_iota(jnp.int32, (LEN, LEN), 0)
    return same & (down <= lane_iota())


def conv_rows(pad_ref, keep_ref, kernel, bias, start, lanes):
    summed = bias + kernel[3:4] * pad_ref[8 + start : 8 + start + LEN, lanes]
    for lag in (1, 2, 3):
        moved = pad_ref[8 + start - lag : 8 + start - lag + LEN, lanes]
        summed = summed + kernel[3 - lag : 4 - lag] * (moved * keep_ref[lag - 1, start : start + LEN, :])
    return summed


def widen(keep_ref, wide_ref):
    rows = keep_ref.shape[0]
    for lag in (1, 2, 3):
        wide_ref[lag - 1, :, :] = jnp.broadcast_to(keep_ref[:, lag : lag + 1], (rows, LEN))


def prep_kernel(
    conv_ref,
    small_ref,
    cos_ref,
    sin_ref,
    keep_ref,
    conv_kernel_ref,
    conv_bias_ref,
    state_kernel_ref,
    state_bias_ref,
    step_bias_ref,
    rate_ref,
    x_ref,
    xb_ref,
    slope_ref,
    state_ref,
    state_slope_ref,
    cum_ref,
    lag_ref,
    cum_row_ref,
    lag_row_ref,
    step_row_ref,
    sig_row_ref,
    q_ref,
    kv_ref,
    pad_ref,
    wide_ref,
):
    rows = conv_ref.shape[0]
    blocks = rows // LEN

    @pl.when(pl.program_id(0) == 0)
    def _():
        pad_ref[0:8, :] = jnp.zeros((8, LEN), jnp.float32)
        widen(keep_ref, wide_ref)
        for c in range(2):
            pad_ref[8 : rows + 8, :] = small_ref[:, block(c)]
            for i in range(blocks):
                pre = conv_rows(
                    pad_ref, wide_ref, state_kernel_ref[:, block(c)], state_bias_ref[:, block(c)], i * LEN, slice(0, LEN)
                )
                sig = sigmoid(pre)
                state_ref[block(i), block(c)] = pre * sig
                state_slope_ref[block(i), block(c)] = sig * (1.0 + pre * (1.0 - sig))

    @pl.when(pl.program_id(0) == 1)
    def _():
        down = lax.broadcasted_iota(jnp.int32, (LEN, LEN), 0)
        lower = jnp.where(down >= lane_iota(), 1.0, 0.0).astype(jnp.bfloat16)
        left_half = lane_iota() < HEAD_DIM
        carry = jnp.zeros((1, LEN), jnp.float32)
        heads = cum_row_ref.shape[0]
        for i in range(blocks):
            argument = small_ref[block(i), block(5)] + step_bias_ref[...]
            tail = jnp.exp(-jnp.abs(argument))
            grown = jnp.where(tail < 1e-3, tail - 0.5 * tail * tail, jnp.log(1.0 + tail))
            step = jnp.maximum(argument, 0.0) + grown
            scaled = step * rate_ref[...] * LOG2E
            first, rest = two_terms(scaled)
            last = scaled - first.astype(jnp.float32) - rest.astype(jnp.float32)
            cum = dot_nn(lower, first) + dot_nn(lower, rest) + dot_nn(lower, last.astype(jnp.bfloat16)) + carry
            carry = cum[LEN - 1 : LEN, :]
            lag = cum - jnp.log(step) * LOG2E
            cum_ref[block(i), :] = cum
            lag_ref[block(i), :] = lag
            cum_t, lag_t = cum.T, lag.T
            step_row_ref[:, block(i)] = step.T[:heads]
            sig_row_ref[:, block(i)] = sigmoid(argument).T[:heads]
            for h in range(heads):
                cum_row_ref[h, :, block(i)] = cum_t[h : h + 1]
                lag_row_ref[h, :, block(i)] = lag_t[h : h + 1]
            cosine, sine = cos_ref[block(i), :], sin_ref[block(i), :]
            kv = small_ref[block(i), block(4)]
            kv_ref[block(i), :] = jnp.where(left_half, rotate_tile(kv, cosine, sine), kv).astype(jnp.bfloat16)
            for p in range(q_ref.shape[1] // LEN):
                q_ref[block(i), block(p)] = rotate_tile(small_ref[block(i), block(2 + p)], cosine, sine).astype(
                    jnp.bfloat16
                )

    for sub in range(GROUP):
        lanes = block(sub)
        pad_ref[8 : rows + 8, :] = conv_ref[:, lanes]
        for i in range(blocks):
            pre = conv_rows(pad_ref, wide_ref, conv_kernel_ref[:, lanes], conv_bias_ref[:, lanes], i * LEN, slice(0, LEN))
            sig = sigmoid(pre)
            x = pre * sig
            x_ref[block(i), lanes] = x
            xb_ref[block(i), lanes] = x.astype(jnp.bfloat16)
            slope_ref[block(i), lanes] = sig * (1.0 + pre * (1.0 - sig))


def rotate_tile(v, cosine, sine):
    first = lax.rem(lane_iota(v.shape[0]), HEAD_DIM) < HEAD_DIM // 2
    swapped = jnp.where(first, pltpu.roll(v, LEN - HEAD_DIM // 2, 1), pltpu.roll(v, HEAD_DIM // 2, 1))
    return v * cosine + swapped * sine


def scan_kernel(
    chunks,
    heads,
    gate_ref,
    x_ref,
    xb_ref,
    state_ref,
    cum_ref,
    lag_row_ref,
    seg_col_ref,
    seg_row_ref,
    skip_ref,
    y_ref,
    gated_ref,
    row_ref,
    wide_ref,
    cross_ref,
    bias_ref,
    mix_ref,
    square_ref,
):
    step = pl.program_id(0)
    first = chunks[0]
    pairs = [(i, j) for i in chunks for j in range(max(0, i - 2), i + 1)]
    left_half = lane_iota() < HEAD_DIM

    @pl.when(step == 0)
    def _():
        for h in range(heads):
            for i in chunks:
                wide_ref[h, block(i - first), :] = jnp.broadcast_to(cum_ref[block(i), h : h + 1], (LEN, LEN))
        for i in chunks:
            low = max(0, i - 2)
            cross = three_dots(dot_nt, state_ref[block(i), LEN:], state_ref[low * LEN : (i + 1) * LEN, :LEN])
            for n, (i2, j) in enumerate(pairs):
                if i2 == i:
                    cross_ref[n] = cross[:, block(j - low)]
                    allowed = mask_ts(seg_col_ref, seg_row_ref, i, j)
                    bias_ref[n] = jnp.where(allowed, 0.0, hidden_bias)
        square_ref[...] = jnp.zeros(square_ref.shape, jnp.float32)

    tiles = (gate_ref, x_ref, xb_ref, skip_ref, y_ref, gated_ref)

    def head_pair(hp, gate_ref, x_ref, xb_ref, skip_ref, y_ref, gated_ref):
        for i in chunks:
            at = block(i - first)
            low = max(0, i - 2)
            for n, (i2, j) in enumerate(pairs):
                if i2 != i:
                    continue
                for e in range(2):
                    spread = wide_ref[2 * hp + e, at, :] - lag_row_ref[2 * hp + e, :, block(j)]
                    decay = jnp.exp2(spread + bias_ref[n])
                    mix_ref[i - first, block(e), block(j - low)] = (decay * cross_ref[n]).astype(jnp.bfloat16)
            both = dot_nn(mix_ref[i - first, :, : (i + 1 - low) * LEN], xb_ref[low * LEN : (i + 1) * LEN, :])
            y = jnp.where(left_half, both[:LEN], both[LEN:])
            y_ref[at, :] = y
            gate = gate_ref[at, :]
            gated = (y + skip_ref[...] * x_ref[at, :]) * (gate * sigmoid(gate))
            gated_ref[at, :] = gated
            square_ref[at, :] = square_ref[at, :] + gated * gated

    for sub in range(GROUP):
        head_pair(GROUP * step + sub, *[t.at[:, block(sub)] for t in tiles])

    @pl.when(step == pl.num_programs(0) - 1)
    def _():
        for i in chunks:
            at = block(i - first)
            total = jnp.sum(square_ref[at, :], axis=1, keepdims=True)
            row_ref[0:1, at] = jnp.broadcast_to(total, (LEN, LEN)).T[0:1]


def attention_kernel(chunks, q_ref, kv_ref, seg_col_ref, seg_row_ref, out_ref, lse_ref):
    scale = HEAD_DIM ** (-0.5) * LOG2E
    first = chunks[0]
    left_half = lane_iota() < HEAD_DIM
    zero = jnp.zeros((LEN, LEN), jnp.bfloat16)
    lse_ref[...] = jnp.zeros(lse_ref.shape, jnp.float32)
    for i in chunks:
        at = block(i - first)
        low = max(0, i - 2) * LEN
        span = (i + 1) * LEN - low
        allowed = jnp.concatenate([mask_ts(seg_col_ref, seg_row_ref, i, j) for j in range(low // LEN, i + 1)], axis=1)
        keys = kv_ref[low : low + span, :]
        turned = pltpu.roll(keys.astype(jnp.float32), HEAD_DIM, 1).astype(jnp.bfloat16)
        for p in range(q_ref.shape[1] // LEN):
            queries = q_ref[block(i), block(p)]
            result = []
            for e in range(2):
                masked = jnp.where(left_half == (e == 0), queries, zero)
                scores = dot_nt(masked, keys if e == 0 else turned) * scale
                scores = jnp.where(allowed, scores, hidden_bias)
                top = jnp.max(scores, axis=1, keepdims=True)
                weights = jnp.exp2(scores - top)
                total = jnp.sum(weights, axis=1, keepdims=True)
                probs = (weights * (1.0 / total)).astype(jnp.bfloat16)
                result.append(dot_nn(probs, turned if e == 0 else keys))
                lse = jnp.broadcast_to(top + jnp.log(total) * LOG2E, (LEN, LEN))
                lse_ref[2 * p + e : 2 * p + e + 1, at] = lse.T[0:1]
            out_ref[at, block(p)] = jnp.where(left_half, result[0], result[1]).astype(jnp.bfloat16)


def attention_back_kernel(chunks, final, *refs):
    q_ref, kv_ref, do_ref, lse_ref, seg_col_ref, seg_row_ref, cos_ref, sin_ref = refs[:8]
    if final:
        dk_in_ref, dv_in_ref, dq_ref, dkv_ref, dk_ref, dv_ref, turned_ref, key_t_ref = refs[8:]
    else:
        dq_ref, dk_ref, dv_ref, turned_ref, key_t_ref = refs[8:]
    scale = HEAD_DIM ** (-0.5)
    blocks = q_ref.shape[0] // LEN
    first = chunks[0]
    left_half = lane_iota() < HEAD_DIM
    zero = jnp.zeros((LEN, LEN), jnp.bfloat16)
    for i in range(chunks[-1] + 1):
        kv = kv_ref[block(i), :].astype(jnp.float32)
        turned_ref[block(i), :] = pltpu.roll(kv, HEAD_DIM, 1).astype(jnp.bfloat16)
        key_t_ref[:, block(i)] = kv.T[:HEAD_DIM].astype(jnp.bfloat16)
    if final:
        dk_ref[...] = dk_in_ref[...]
        dv_ref[...] = dv_in_ref[...]
    else:
        dk_ref[...] = jnp.zeros(dk_ref.shape, jnp.float32)
        dv_ref[...] = jnp.zeros(dv_ref.shape, jnp.float32)
    for i in chunks:
        at = block(i - first)
        low = max(0, i - 2) * LEN
        span = (i + 1) * LEN - low
        window = slice(low, low + span)
        allowed = jnp.concatenate([mask_st(seg_col_ref, seg_row_ref, j, i) for j in range(low // LEN, i + 1)], axis=0)
        keys, turned = kv_ref[window, :], turned_ref[window, :]
        for p in range(q_ref.shape[1] // LEN):
            queries, douts = q_ref[block(i), block(p)], do_ref[at, block(p)]
            back = []
            for e in range(2):
                side = left_half == (e == 0)
                q_half = jnp.where(side, queries, zero)
                do_half = jnp.where(side, douts, zero)
                h = 2 * p + e
                scores = dot_nt(keys if e == 0 else turned, q_half) * (scale * LOG2E)
                probs = jnp.exp2(jnp.where(allowed, scores, hidden_bias) - lse_ref[h : h + 1, at])
                dprobs = dot_nt(turned if e == 0 else keys, do_half)
                inner = jnp.sum(probs * dprobs, axis=0, keepdims=True)
                dscores = (probs * (dprobs - inner)).astype(jnp.bfloat16)
                dv_ref[window, :] = dv_ref[window, :] + dot_nn(probs.astype(jnp.bfloat16), do_half)
                dk_ref[window, :] = dk_ref[window, :] + dot_nn(dscores, q_half)
                back.append(dot_nn(key_t_ref[:, window], dscores))
            dq = jnp.concatenate(back, axis=0).T * scale
            dq_ref[at, block(p)] = rotate_tile(dq, cos_ref[block(i), :], -sin_ref[block(i), :]).astype(jnp.bfloat16)
    if not final:
        return
    for i in range(blocks):
        dk = dk_ref[block(i), :]
        dk = (dk + pltpu.roll(dk, HEAD_DIM, 1)) * scale
        dk = rotate_tile(dk, cos_ref[block(i), :], -sin_ref[block(i), :])
        dv = dv_ref[block(i), :]
        dv = dv + pltpu.roll(dv, HEAD_DIM, 1)
        dkv_ref[block(i), :] = jnp.where(left_half, dk, dv).astype(jnp.bfloat16)


def scan_back_kernel(
    chunks,
    heads,
    gmr_ref,
    gated_ref,
    square_a_ref,
    square_b_ref,
    dot_a_ref,
    dot_b_ref,
    gain_ref,
    gate_ref,
    y_ref,
    x_ref,
    xb_ref,
    state_ref,
    lag_ref,
    cum_row_ref,
    skip_ref,
    seg_col_ref,
    seg_row_ref,
    select_ref,
    dgate_ref,
    gy_ref,
    dx_ref,
    p_ref,
    grad_in_ref,
    grad_out_ref,
    sums_ref,
    gyb_ref,
    wide_ref,
    cross_ref,
    bias_ref,
    dcross_ref,
    inv_wide_ref,
    dot_wide_ref,
    inner_ref,
    mix_ref,
):
    step = pl.program_id(0)
    first = chunks[0]
    sources = chunks[-1] + 1
    left_half = lane_iota() < HEAD_DIM
    zero = jnp.zeros((LEN, LEN), jnp.bfloat16)
    spans = [(j, max(j, first), min(j + 3, sources)) for j in range(sources)]
    pairs = [(j, i) for j, start, stop in spans for i in range(start, stop)]

    @pl.when(step == 0)
    def _():
        for i in chunks:
            at = block(i - first)
            square = (square_a_ref[:, at] + square_b_ref[:, at]) / DSSM
            inv = lax.rsqrt(square + norm_eps)
            inv_wide_ref[at, :] = jnp.broadcast_to(inv, (LEN, LEN)).T
            dot = (dot_a_ref[:, at] + dot_b_ref[:, at]) / DSSM
            dot_wide_ref[at, :] = jnp.broadcast_to(dot, (LEN, LEN)).T
        p_ref[...] = jnp.zeros(p_ref.shape, jnp.float32)
        for h in range(heads):
            wide_ref[h] = jnp.broadcast_to(lag_ref[: sources * LEN, h : h + 1], (sources * LEN, LEN))
        for j, start, stop in spans:
            cross = three_dots(dot_nt, state_ref[block(j), :LEN], state_ref[start * LEN : stop * LEN, LEN:])
            for n, (j2, i) in enumerate(pairs):
                if j2 == j:
                    cross_ref[n] = cross[:, block(i - start)]
                    allowed = mask_st(seg_col_ref, seg_row_ref, j, i)
                    bias_ref[n] = jnp.where(allowed, 0.0, hidden_bias)
                    dcross_ref[n] = jnp.zeros((LEN, LEN), jnp.float32)

    tiles = (
        gmr_ref, gated_ref, gain_ref, gate_ref, y_ref, x_ref, xb_ref, skip_ref, dgate_ref, gy_ref, dx_ref, sums_ref
    )

    def head_pair(
        hp,
        select,
        gmr_ref,
        gated_ref,
        gain_ref,
        gate_ref,
        y_ref,
        x_ref,
        xb_ref,
        skip_ref,
        dgate_ref,
        gy_ref,
        dx_ref,
        sums_ref,
    ):
        skip = skip_ref[...]
        gain = gain_ref[...]
        skip_sum = jnp.zeros((1, LEN), jnp.float32)
        gain_sum = jnp.zeros((1, LEN), jnp.float32)
        for i in chunks:
            at = block(i - first)
            inv = inv_wide_ref[at, :]
            unit = gated_ref[at, :] * inv
            rows_grad = gmr_ref[at, :]
            grad = inv * (rows_grad * gain - unit * dot_wide_ref[at, :])
            gate = gate_ref[at, :]
            sig = sigmoid(gate)
            y = y_ref[at, :]
            x = x_ref[at, :]
            gy = grad * (gate * sig)
            dgate_ref[at, :] = (grad * (y + skip * x) * (sig * (1.0 + gate * (1.0 - sig)))).astype(jnp.bfloat16)
            gyb = gy.astype(jnp.bfloat16)
            gy_ref[at, :] = gy
            gyb_ref[at, :] = gyb
            high, rest = two_terms(gyb.astype(jnp.float32) * y)
            p_ref[:, at] = p_ref[:, at] + dot_nt(select, high) + dot_nt(select, rest)
            skip_sum = skip_sum + jnp.sum(gy * x, axis=0, keepdims=True)
            gain_sum = gain_sum + jnp.sum(rows_grad * unit, axis=0, keepdims=True)
        sums_ref[0:1, :] = skip_sum
        sums_ref[1:2, :] = gain_sum

        for j, start, stop in spans:
            x_pair = xb_ref[block(j), :]
            x_both = jnp.concatenate([jnp.where(left_half, x_pair, zero), jnp.where(left_half, zero, x_pair)], axis=0)
            wide = (stop - start) * LEN
            gy_rows = gyb_ref[(start - first) * LEN : (stop - first) * LEN, :]
            inner_ref[:, :wide] = dot_nt(x_both, gy_rows)
            for n, (j2, i) in enumerate(pairs):
                if j2 != j:
                    continue
                grown = dcross_ref[n]
                for e in range(2):
                    spread = cum_row_ref[2 * hp + e, :, block(i)] - wide_ref[2 * hp + e, block(j), :]
                    decay = jnp.exp2(spread + bias_ref[n])
                    grown = grown + inner_ref[block(e), block(i - start)] * decay
                    mix_ref[block(e), block(i - start)] = (decay * cross_ref[n]).astype(jnp.bfloat16)
                dcross_ref[n] = grown
            both = dot_nn(mix_ref[:, :wide], gy_rows)
            dx_ref[block(j), :] = jnp.where(left_half, both[:LEN], both[LEN:])

    for sub in range(GROUP):
        head_pair(GROUP * step + sub, select_ref[:, block(sub)], *[t.at[:, block(sub)] for t in tiles])

    @pl.when(step == pl.num_programs(0) - 1)
    def _():
        grad_out = {i: jnp.zeros((LEN, LEN), jnp.float32) for i in chunks}
        for j in range(sources):
            grad_in = jnp.zeros((LEN, LEN), jnp.float32)
            for n, (j2, i) in enumerate(pairs):
                if j2 != j:
                    continue
                high, rest = two_terms(dcross_ref[n])
                out_high, out_rest = two_terms(state_ref[block(i), LEN:])
                in_high, in_rest = two_terms(state_ref[block(j), :LEN])
                grad_in = grad_in + dot_nn(high, out_high) + dot_nn(high, out_rest) + dot_nn(rest, out_high)
                grad_out[i] = grad_out[i] + dot_tn(high, in_high) + dot_tn(high, in_rest) + dot_tn(rest, in_high)
            grad_in_ref[block(j), :] = grad_in
        for i in chunks:
            grad_out_ref[block(i - first), :] = grad_out[i]


def conv_back(grad_ref, value_ref, keep_ref, kernel_ref, out_ref, sum_ref, lanes, blocks):
    taps = kernel_ref[:, lanes]
    totals = [jnp.zeros((1, LEN), jnp.float32) for _ in range(5)]
    for i in range(blocks):
        here = grad_ref[i * LEN : (i + 1) * LEN, :]
        grad = taps[3:4] * here
        totals[4] = totals[4] + jnp.sum(here, axis=0, keepdims=True)
        totals[3] = totals[3] + jnp.sum(here * value_ref[8 + i * LEN : 8 + (i + 1) * LEN, :], axis=0, keepdims=True)
        for lag in (1, 2, 3):
            ahead = grad_ref[i * LEN + lag : (i + 1) * LEN + lag, :]
            grad = grad + taps[3 - lag : 4 - lag] * (ahead * keep_ref[lag - 1, i * LEN + lag : (i + 1) * LEN + lag, :])
            moved = value_ref[8 + i * LEN - lag : 8 + (i + 1) * LEN - lag, :]
            masked = here * keep_ref[lag - 1, i * LEN : (i + 1) * LEN, :]
            totals[3 - lag] = totals[3 - lag] + jnp.sum(masked * moved, axis=0, keepdims=True)
        out_ref[block(i), lanes] = grad.astype(jnp.bfloat16)
    for tap in range(5):
        sum_ref[tap : tap + 1, lanes] = totals[tap]


def scan_end_kernel(
    heads,
    gy_a_ref,
    gy_b_ref,
    dx_a_ref,
    dx_b_ref,
    p_a_ref,
    p_b_ref,
    in_a_ref,
    in_b_ref,
    out_a_ref,
    out_b_ref,
    xb_ref,
    slope_ref,
    state_slope_ref,
    conv_ref,
    small_ref,
    step_row_ref,
    sig_row_ref,
    rate_ref,
    skip_ref,
    keep_ref,
    seg_col_ref,
    seg_row_ref,
    select_ref,
    conv_kernel_ref,
    state_kernel_ref,
    dconv_ref,
    dstate_ref,
    dstep_ref,
    conv_sum_ref,
    state_sum_ref,
    step_sum_ref,
    grad_pad_ref,
    value_pad_ref,
    wide_ref,
    q_ref,
    flow_ref,
):
    step = pl.program_id(0)
    rows = conv_ref.shape[0]
    blocks = rows // LEN
    half = rows // 2
    count = flow_ref.shape[0]

    @pl.when(step == 0)
    def _():
        value_pad_ref[0:8, :] = jnp.zeros((8, LEN), jnp.float32)
        grad_pad_ref[rows : rows + 8, :] = jnp.zeros((8, LEN), jnp.float32)
        widen(keep_ref, wide_ref)
        q_ref[...] = jnp.zeros(q_ref.shape, jnp.float32)
        for c in range(2):
            if c == 0:
                grad_pad_ref[0:half, :] = (in_a_ref[...] + in_b_ref[0:half, :]) * state_slope_ref[0:half, block(c)]
                grad_pad_ref[half:rows, :] = in_b_ref[half:rows, :] * state_slope_ref[half:rows, block(c)]
            else:
                grad_pad_ref[0:half, :] = out_a_ref[...] * state_slope_ref[0:half, block(c)]
                grad_pad_ref[half:rows, :] = out_b_ref[...] * state_slope_ref[half:rows, block(c)]
            value_pad_ref[8 : rows + 8, :] = small_ref[:, block(c)]
            conv_back(grad_pad_ref, value_pad_ref, wide_ref, state_kernel_ref, dstate_ref, state_sum_ref, block(c), blocks)

    tiles = (
        gy_a_ref, gy_b_ref, dx_a_ref, dx_b_ref, xb_ref, slope_ref, conv_ref, skip_ref, conv_kernel_ref, dconv_ref, conv_sum_ref
    )

    def head_pair(
        select,
        gy_a_ref,
        gy_b_ref,
        dx_a_ref,
        dx_b_ref,
        xb_ref,
        slope_ref,
        conv_ref,
        skip_ref,
        conv_kernel_ref,
        dconv_ref,
        conv_sum_ref,
    ):
        for j in range(blocks):
            dx = dx_b_ref[block(j), :]
            if j < blocks // 2:
                dx = dx + dx_a_ref[block(j), :]
                gy = gy_a_ref[block(j), :]
            else:
                gy = gy_b_ref[block(j - blocks // 2), :]
            high, rest = two_terms(dx * xb_ref[block(j), :].astype(jnp.float32))
            q_ref[:, block(j)] = q_ref[:, block(j)] + dot_nt(select, high) + dot_nt(select, rest)
            grad_pad_ref[block(j), :] = (dx + gy * skip_ref[...]) * slope_ref[block(j), :]
        value_pad_ref[8 : rows + 8, :] = conv_ref[...]
        conv_back(
            grad_pad_ref, value_pad_ref, wide_ref, conv_kernel_ref, dconv_ref, conv_sum_ref, slice(0, LEN), blocks
        )

    for sub in range(GROUP):
        head_pair(select_ref[:, block(sub)], *[t.at[:, block(sub)] for t in tiles])

    @pl.when(step == pl.num_programs(0) - 1)
    def _():
        q = q_ref[...]
        flow_ref[:, 0:half] = p_a_ref[...] - q[:, 0:half]
        flow_ref[:, half:rows] = p_b_ref[...] - q[:, half:rows]
        rate = jnp.broadcast_to(rate_ref[...], (LEN, LEN)).T[:count]
        bias_total = jnp.zeros((count, LEN), jnp.float32)
        decay_total = jnp.zeros((count, LEN), jnp.float32)
        for j in range(blocks):
            log_grad = jnp.zeros((count, LEN), jnp.float32)
            for i in range(j, min(j + 3, blocks)):
                chosen = jnp.where(mask_st(seg_col_ref, seg_row_ref, j, i), 1.0, 0.0).astype(jnp.bfloat16)
                high, rest = two_terms(flow_ref[:, block(i)])
                log_grad = log_grad + dot_nt(high, chosen) + dot_nt(rest, chosen)
            step = step_row_ref[:, block(j)]
            grad_step = jnp.where(step > 1e-30, q[:, block(j)] / step, 0.0) + log_grad * rate
            grad_arg = grad_step * sig_row_ref[:, block(j)]
            bias_total = bias_total + grad_arg
            decay_total = decay_total + log_grad * step
            tall = jnp.concatenate([grad_arg, jnp.zeros((LEN - count, LEN), jnp.float32)], axis=0)
            dstep_ref[block(j), :] = tall.T.astype(jnp.bfloat16)
        step_sum_ref[0:count, :] = jnp.broadcast_to(jnp.sum(bias_total, axis=1, keepdims=True), (count, LEN))
        step_sum_ref[count : 2 * count, :] = jnp.broadcast_to(
            jnp.sum(decay_total * rate, axis=1, keepdims=True), (count, LEN)
        )


def whole_block(shape):
    return pl.BlockSpec(shape, lambda step: (0,) * len(shape), pipeline_mode=pl.Buffered(1))


def tile(rows, row_block=0, first=0):
    return pl.BlockSpec((rows, GROUP * LEN), lambda step: (row_block, first + step))


def call(kernel, steps, out_shape, out_specs, scratch, operands, specs, flops):
    return pl.pallas_call(
        kernel,
        grid=(steps,),
        out_shape=out_shape,
        in_specs=[s or whole_block(o.shape) for o, s in zip(operands, specs)],
        out_specs=[s or whole_block(o.shape) for o, s in zip(out_shape, out_specs)],
        scratch_shapes=scratch,
        compiler_params=pltpu.CompilerParams(vmem_limit_bytes=VMEM_BYTES),
        cost_estimate=pl.CostEstimate(flops=flops, bytes_accessed=0, transcendentals=0),
    )(*operands)


def f32(*shape):
    return jax.ShapeDtypeStruct(shape, jnp.float32)


def b16(*shape):
    return jax.ShapeDtypeStruct(shape, jnp.bfloat16)


HEAD_ROWS = 16
GROUP = 3
VMEM_BYTES = 60 * 1024 * 1024


def scan_prep(width, wide_in, small, cosine, sine, keep, conv_kernel, conv_bias, *rest):
    rows = wide_in.shape[0]
    steps = width // LEN // GROUP
    outs = [
        f32(rows, width),
        b16(rows, width),
        f32(rows, width),
        f32(rows, 2 * LEN),
        f32(rows, 2 * LEN),
        f32(rows, LEN),
        f32(rows, LEN),
        f32(HEAD_ROWS, 1, rows),
        f32(HEAD_ROWS, 1, rows),
        f32(HEAD_ROWS, rows),
        f32(HEAD_ROWS, rows),
        b16(rows, 2 * LEN),
        b16(rows, LEN),
    ]
    scratch = [pltpu.VMEM((rows + 8, LEN), jnp.float32), pltpu.VMEM((3, rows + 8, LEN), jnp.float32)]
    operands = (wide_in, small, cosine, sine, keep, conv_kernel, conv_bias, *rest)
    specs = [tile(rows, 0, steps), None, None, None, None, tile(4), tile(1)] + [None] * len(rest)
    return call(prep_kernel, steps, outs, [tile(rows)] * 3 + [None] * 10, scratch, operands, specs, 0 * 10**9)


def scan_forward(chunks, heads, wide_in, x, xb, *rest):
    width = x.shape[1]
    rows = LEN * len(chunks)
    at = chunks[0] // len(chunks)
    count = sum(min(i, 2) + 1 for i in chunks)
    outs = [f32(rows, width), f32(rows, width), f32(1, rows)]
    scratch = [
        pltpu.VMEM((heads, rows, LEN), jnp.float32),
        pltpu.VMEM((count, LEN, LEN), jnp.float32),
        pltpu.VMEM((count, LEN, LEN), jnp.float32),
        pltpu.VMEM((len(chunks), 2 * LEN, 3 * LEN), jnp.bfloat16),
        pltpu.VMEM((rows, LEN), jnp.float32),
    ]
    specs = [tile(rows, at), tile(rows, at), tile((chunks[-1] + 1) * LEN)] + [None] * (len(rest) - 1) + [tile(1)]
    kernel = functools.partial(scan_kernel, chunks, heads)
    operands = (wide_in, x, xb, *rest)
    return call(kernel, heads // 2 // GROUP, outs, [tile(rows), tile(rows), None], scratch, operands, specs, 0 * 10**9)


def attention_forward(chunks, q, kv, seg_col, seg_row):
    rows = LEN * len(chunks)
    outs = [b16(rows, q.shape[1]), f32(8, rows)]
    kernel = functools.partial(attention_kernel, chunks)
    return call(kernel, 1, outs, [None] * 2, [], (q, kv, seg_col, seg_row), [None] * 4, 0 * 10**9)


def attention_backward(chunks, final, *operands):
    q = operands[0]
    rows = q.shape[0]
    partial = [f32(rows, LEN), f32(rows, LEN)]
    sums = [pltpu.VMEM((rows, LEN), jnp.float32)] * 2
    outs = [b16(LEN * len(chunks), q.shape[1])] + ([b16(rows, LEN)] if final else partial)
    scratch = (sums if final else []) + [
        pltpu.VMEM((rows, LEN), jnp.bfloat16),
        pltpu.VMEM((HEAD_DIM, rows), jnp.bfloat16),
    ]
    kernel = functools.partial(attention_back_kernel, chunks, final)
    return call(kernel, 1, outs, [None] * len(outs), scratch, operands, [None] * len(operands), 0 * 10**9)


def scan_backward(chunks, heads, *operands):
    rows, width = operands[0].shape
    at = chunks[0] // len(chunks)
    sources = (chunks[-1] + 1) * LEN
    count = sum(min(i, 2) + 1 for i in chunks)
    outs = [
        b16(rows, width),
        f32(rows, width),
        f32(sources, width),
        f32(HEAD_ROWS, rows),
        f32(sources, LEN),
        f32(rows, LEN),
        f32(8, width),
    ]
    scratch = [
        pltpu.VMEM((rows, LEN), jnp.bfloat16),
        pltpu.VMEM((heads, sources, LEN), jnp.float32),
        pltpu.VMEM((count, LEN, LEN), jnp.float32),
        pltpu.VMEM((count, LEN, LEN), jnp.float32),
        pltpu.VMEM((count, LEN, LEN), jnp.float32),
        pltpu.VMEM((rows, LEN), jnp.float32),
        pltpu.VMEM((rows, LEN), jnp.float32),
        pltpu.VMEM((2 * LEN, 3 * LEN), jnp.float32),
        pltpu.VMEM((2 * LEN, 3 * LEN), jnp.bfloat16),
    ]
    specs = [tile(rows), tile(rows), None, None, None, None, tile(1), tile(rows, at), tile(rows), tile(rows, at), tile(sources)]
    specs += [None, None, None, tile(1), None, None, tile(HEAD_ROWS)]
    out_specs = [tile(rows), tile(rows), tile(sources), None, None, None, tile(8)]
    kernel = functools.partial(scan_back_kernel, chunks, heads)
    return call(kernel, heads // 2 // GROUP, outs, out_specs, scratch, operands, specs, 30 * 10**9)


def scan_end(heads, *operands):
    rows, width = 2 * operands[0].shape[0], operands[0].shape[1]
    steps = heads // 2 // GROUP
    outs = [
        b16(rows, width),
        b16(rows, 2 * LEN),
        b16(rows, LEN),
        f32(8, width),
        f32(8, 2 * LEN),
        f32(2 * HEAD_ROWS, LEN),
    ]
    scratch = [
        pltpu.VMEM((rows + 8, LEN), jnp.float32),
        pltpu.VMEM((rows + 8, LEN), jnp.float32),
        pltpu.VMEM((3, rows + 8, LEN), jnp.float32),
        pltpu.VMEM((HEAD_ROWS, rows), jnp.float32),
        pltpu.VMEM((HEAD_ROWS, rows), jnp.float32),
    ]
    half = rows // 2
    specs = [tile(half), tile(half), tile(half), tile(rows)] + [None] * 6 + [tile(rows), tile(rows), None]
    specs += [tile(rows, 0, steps)] + [None] * 4 + [tile(1), None, None, None, tile(HEAD_ROWS), tile(4), None]
    out_specs = [tile(rows), None, None, tile(8), None, None]
    kernel = functools.partial(scan_end_kernel, heads)
    return call(kernel, steps, outs, out_specs, scratch, operands, specs, 30 * 10**9)


def inverse_rms(rows):
    return lax.rsqrt(jnp.mean(rows * rows, axis=-1, keepdims=True) + norm_eps)


def ffn_kernel(
    tokens_ref,
    part_ref,
    far_ref,
    gain_ref,
    gate_ref,
    up_ref,
    down_ref,
    cotangent_ref,
    hidden_ref,
    normed_ref,
    activated_ref,
    grad_gate_ref,
    grad_up_ref,
    back_ref,
    out_ref,
):
    @pl.when(pl.program_id(0) == 0)
    def _():
        hidden = tokens_ref[...].astype(jnp.float32) + (part_ref[...] + far_ref[...])
        hidden_ref[...] = hidden
        normed_ref[...] = (hidden * inverse_rms(hidden) * gain_ref[...]).astype(jnp.bfloat16)
        back_ref[...] = jnp.zeros(back_ref.shape, jnp.float32)
        out_ref[...] = jnp.zeros(out_ref.shape, jnp.float32)

    normed = normed_ref[...]
    gate = dot_nn(normed, gate_ref[...])
    up = dot_nn(normed, up_ref[...])
    sig = sigmoid(gate)
    act = gate * sig
    activated = (act * up).astype(jnp.bfloat16)
    activated_ref[...] = activated
    grad = dot_nt(cotangent_ref[...], down_ref[...])
    grad_gate = (grad * up * (sig * (1.0 + gate * (1.0 - sig)))).astype(jnp.bfloat16)
    grad_up = (grad * act).astype(jnp.bfloat16)
    grad_gate_ref[...] = grad_gate
    grad_up_ref[...] = grad_up
    back_ref[...] = back_ref[...] + (dot_nt(grad_gate, gate_ref[...]) + dot_nt(grad_up, up_ref[...]))
    out_ref[...] = out_ref[...] + dot_nn(activated, down_ref[...])


def ffn(chunks, tokens, part, far, gain, gate, up, down, cotangent):
    rows, model_width = part.shape
    at = chunks[0] // len(chunks)
    hidden_width = gate.shape[1]
    steps = hidden_width // 256
    outs = [f32(rows, model_width), b16(rows, model_width)] + [b16(rows, hidden_width)] * 3
    outs += [f32(rows, model_width)] * 2
    rows_of = pl.BlockSpec((rows, model_width), lambda step: (at, 0), pipeline_mode=pl.Buffered(1))
    columns = pl.BlockSpec((model_width, 256), lambda step: (0, step))
    tiles = pl.BlockSpec((rows, 256), lambda step: (0, step))
    specs = [rows_of, None, None, None, columns, columns]
    specs += [pl.BlockSpec((256, model_width), lambda step: (step, 0)), rows_of]
    operands = (tokens, part, far, gain, gate, up, down, cotangent)
    return call(ffn_kernel, steps, outs, [None, None, tiles, tiles, tiles, None, None], [], operands, specs, 0 * 10**9)


def middle_kernel(
    hidden_ref,
    part_ref,
    far_ref,
    cotangent_ref,
    gain_ref,
    gated_ref,
    square_a_ref,
    square_b_ref,
    gated_gain_ref,
    mixer_out_ref,
    attn_out_ref,
    grad_hidden_ref,
    grad_branch_ref,
    grad_rows_ref,
    grad_attended_ref,
    dot_ref,
    gain_sum_ref,
):
    hidden = hidden_ref[...]
    inv = inverse_rms(hidden)
    unit = hidden * inv
    grad_normed = part_ref[...] + far_ref[...]
    gain_sum_ref[0:1, :] = jnp.sum(grad_normed * unit, axis=0, keepdims=True)
    grad_unit = grad_normed * gain_ref[...]
    inner = jnp.mean(grad_unit * unit, axis=-1, keepdims=True)
    grad_hidden = cotangent_ref[...].astype(jnp.float32) + inv * (grad_unit - unit * inner)
    grad_hidden_ref[...] = grad_hidden
    grad_branch = grad_hidden.astype(jnp.bfloat16)
    grad_branch_ref[...] = grad_branch
    grad_rows = dot_nt(grad_branch, mixer_out_ref[...])
    grad_rows_ref[...] = grad_rows
    grad_attended_ref[...] = dot_nt(grad_branch, attn_out_ref[...]).astype(jnp.bfloat16)
    total = jnp.sum(grad_rows * gated_gain_ref[...] * gated_ref[...], axis=-1, keepdims=True)
    for i in range(hidden.shape[0] // LEN):
        at = block(i)
        inv_gated = lax.rsqrt((square_a_ref[:, at] + square_b_ref[:, at]) / DSSM + norm_eps)
        dot_ref[0:1, at] = jnp.broadcast_to(total[at], (LEN, LEN)).T[0:1] * inv_gated


def middle(chunks, hidden, part, far, cotangent, gain, gated, square_a, square_b, gated_gain, mixer_out, attn_out):
    rows, model_width = part.shape
    at = chunks[0] // len(chunks)
    width, inner = mixer_out.shape[0], attn_out.shape[0]
    outs = [
        f32(rows, model_width),
        b16(rows, model_width),
        f32(rows, width),
        b16(rows, inner),
        f32(1, rows),
        f32(8, model_width),
    ]
    rows_of = pl.BlockSpec((rows, model_width), lambda step: (at, 0), pipeline_mode=pl.Buffered(1))
    specs = [None, None, None, rows_of] + [None] * 7
    operands = (hidden, part, far, cotangent, gain, gated, square_a, square_b, gated_gain, mixer_out, attn_out)
    return call(middle_kernel, 1, outs, [None] * 6, [], operands, specs, 0 * 10**9)


def core_call(kernel, steps, core, out_shape, out_spec, scratch, operands, specs, flops):
    return pl.pallas_call(
        kernel,
        grid_spec=pltpu.PrefetchScalarGridSpec(
            num_scalar_prefetch=1, grid=(steps,), in_specs=specs, out_specs=out_spec, scratch_shapes=scratch
        ),
        out_shape=out_shape,
        compiler_params=pltpu.CompilerParams(vmem_limit_bytes=VMEM_BYTES),
        cost_estimate=pl.CostEstimate(flops=flops, bytes_accessed=0, transcendentals=0),
    )(core, *operands)


def clip_tile(rows, columns, first, last):
    return pl.BlockSpec((rows, columns), lambda step, core_ref: (0, jnp.clip(step - first, 0, last - first - 1)))


def ffn_weights_kernel(add, core_ref, *refs):
    refs = list(refs)
    normed_a, normed_b, act_a, act_b, gate_a, gate_b, up_a, up_b, cot_a, cot_b = refs[:10]
    far_ref = refs[10] if add else None
    out_ref, left_ref = refs[-2:]
    step = pl.program_id(0)
    third = pl.num_programs(0) // 3
    half = normed_a.shape[0]

    def turn(first, second):
        left_ref[:, :half] = first[...].T
        left_ref[:, half:] = second[...].T

    @pl.when(step == 0)
    def _():
        turn(normed_a, normed_b)

    @pl.when(step == 2 * third)
    def _():
        turn(act_a, act_b)

    def product(first, second):
        result = dot_nn(left_ref[:, :half], first[...]) + dot_nn(left_ref[:, half:], second[...])
        out_ref[...] = result + far_ref[...] if add else result

    @pl.when(step < third)
    def _():
        product(gate_a, gate_b)

    @pl.when((step >= third) & (step < 2 * third))
    def _():
        product(up_a, up_b)

    @pl.when(step >= 2 * third)
    def _():
        product(cot_a, cot_b)


def ffn_weights(core, far, normed_a, normed_b, act_a, act_b, gate_a, gate_b, up_a, up_b, cotangent):
    half, columns = normed_a.shape
    kept = columns // 2
    tile_width = 512
    third = columns // tile_width
    left = pl.BlockSpec((half, kept), lambda step, core_ref: (0, core_ref[0]), pipeline_mode=pl.Buffered(1))
    specs = [left] * 4 + [clip_tile(half, tile_width, 0, third)] * 2
    specs += [clip_tile(half, tile_width, third, 2 * third)] * 2

    def cot_rows(at):
        return pl.BlockSpec(
            (half, tile_width), lambda step, core_ref: (at, jnp.clip(step - 2 * third, 0, third - 1))
        )

    specs += [cot_rows(0), cot_rows(1)]
    out = pl.BlockSpec((kept, tile_width), lambda step, core_ref: (0, step))
    operands = [normed_a, normed_b, act_a, act_b, gate_a, gate_b, up_a, up_b, cotangent, cotangent]
    if far is not None:
        operands.append(far)
        specs.append(out)
    return core_call(
        functools.partial(ffn_weights_kernel, far is not None),
        3 * third,
        core,
        f32(kept, 3 * columns),
        out,
        [pltpu.VMEM((kept, 2 * half), jnp.bfloat16)],
        operands,
        specs,
        0 * 10**9,
    )


def mixer_weights_kernel(add, core_ref, *refs):
    refs = list(refs)
    (
        rows_a,
        rows_b,
        edge_a,
        edge_b,
        att_a,
        att_b,
        normed_ref,
        branch_a,
        branch_b,
        gate_a,
        gate_b,
        conv_ref,
        query_a,
        query_b,
        state_ref,
        pair_ref,
        step_ref,
    ) = refs[:17]
    far_ref = refs[17] if add else None
    table_ref = refs[18] if add else None
    out_ref, left_ref = refs[-2:]
    step = pl.program_id(0)
    half = rows_a.shape[0]
    kept = left_ref.shape[0]
    middle_row = kept // 2

    @pl.when((step == 0) & (core_ref[0] == 0))
    def _():
        left_ref[:, :half] = rows_a[...].T
        left_ref[:, half:] = rows_b[...].T

    @pl.when((step == 0) & (core_ref[0] == 1))
    def _():
        left_ref[:middle_row, :half] = edge_a[...].T
        left_ref[:middle_row, half:] = edge_b[...].T
        left_ref[middle_row:, :half] = att_a[...].T
        left_ref[middle_row:, half:] = att_b[...].T

    @pl.when(step == 4)
    def _():
        left_ref[...] = normed_ref[...].T

    def write(value, lanes=slice(None)):
        out_ref[:, lanes] = value + far_ref[:, lanes] if add else value

    def two(first, second):
        write(dot_nn(left_ref[:, :half], first[...]) + dot_nn(left_ref[:, half:], second[...]))

    @pl.when(step < 4)
    def _():
        two(branch_a, branch_b)

    @pl.when((step >= 4) & (step < 7))
    def _():
        two(gate_a, gate_b)

    @pl.when((step >= 7) & (step < 10))
    def _():
        write(dot_nn(left_ref[...], conv_ref[...]))

    @pl.when(step == 10)
    def _():
        two(query_a, query_b)

    @pl.when(step == 11)
    def _():
        write(dot_nn(left_ref[...], state_ref[...]))

    @pl.when(step == 12)
    def _():
        write(dot_nn(left_ref[...], pair_ref[...]), slice(0, LEN))
        steps = dot_nn(left_ref[...], step_ref[...])
        write(steps + table_ref[...] if add else steps, slice(LEN, 2 * LEN))


def mixer_weights(core, far, table, rows_a, rows_b, att_a, att_b, normed, branch_a, branch_b, gate_a, gate_b, conv, query_a, query_b, state, pair, step):
    half, width = rows_a.shape
    rows, model_width = normed.shape
    kept = model_width // 2
    tile_width = 256
    steps = 13

    def fixed(shape, column=0):
        return pl.BlockSpec(shape, lambda step, core_ref: (0, column), pipeline_mode=pl.Buffered(1))

    specs = [fixed((half, kept))] * 2
    specs += [fixed((half, width - kept), kept // (width - kept))] * 2
    specs += [fixed(att_a.shape)] * 2
    specs += [pl.BlockSpec((rows, kept), lambda step, core_ref: (0, core_ref[0]), pipeline_mode=pl.Buffered(1))]
    specs += [clip_tile(half, tile_width, 0, 4)] * 2
    specs += [clip_tile(half, tile_width, 4, 7)] * 2
    specs += [clip_tile(rows, tile_width, 7, 10)]
    specs += [fixed(query_a.shape)] * 2 + [fixed(state.shape), fixed(pair.shape), fixed(step.shape)]
    operands = [rows_a, rows_b, rows_a, rows_b, att_a, att_b, normed, branch_a, branch_b, gate_a, gate_b, conv]
    operands += [query_a, query_b, state, pair, step]
    out = pl.BlockSpec((kept, tile_width), lambda step, core_ref: (0, step))
    if far is not None:
        operands += [far, table]
        specs += [out, fixed(table.shape)]
    return core_call(
        functools.partial(mixer_weights_kernel, far is not None),
        steps,
        core,
        f32(kept, steps * tile_width),
        out,
        [pltpu.VMEM((kept, rows), jnp.bfloat16)],
        operands,
        specs,
        0 * 10**9,
    )


def normed_back_kernel(
    gate_a,
    gate_b,
    conv_ref,
    query_a,
    query_b,
    state_ref,
    pair_ref,
    step_ref,
    wide_ref,
    small_ref,
    tokens_ref,
    inv_ref,
    out_ref,
    sum_ref,
):
    half, width = gate_a.shape
    query_width = query_a.shape[1]
    gate_w, conv_w = wide_ref[:, :width], wide_ref[:, width:]
    state_w = small_ref[:, : 2 * LEN]
    query_w = small_ref[:, 2 * LEN : 2 * LEN + query_width]
    pair_w = small_ref[:, 2 * LEN + query_width : 3 * LEN + query_width]
    step_w = small_ref[:, 3 * LEN + query_width :]
    total = jnp.zeros((1, out_ref.shape[1]), jnp.float32)
    for k, (gate, query) in enumerate(((gate_a, query_a), (gate_b, query_b))):
        at = slice(k * half, (k + 1) * half)
        grad = dot_nt(gate[...], gate_w) + dot_nt(conv_ref[at, :], conv_w) + dot_nt(query[...], query_w)
        grad = grad + dot_nt(state_ref[at, :], state_w) + dot_nt(pair_ref[at, :], pair_w) + dot_nt(step_ref[at, :], step_w)
        out_ref[at, :] = grad
        unit = tokens_ref[at, :].astype(jnp.float32) * inv_ref[at, :]
        total = total + jnp.sum(grad * unit, axis=0, keepdims=True)
    sum_ref[0:1, :] = total


def normed_back(gate_a, gate_b, conv, query_a, query_b, state, pair, step, wide_proj, small_proj, tokens, inv):
    rows, model_width = tokens.shape
    tile_width = 256
    operands = (gate_a, gate_b, conv, query_a, query_b, state, pair, step, wide_proj, small_proj, tokens, inv)

    def weights(count):
        return pl.BlockSpec((tile_width, count), lambda step: (step, 0))

    columns = pl.BlockSpec((rows, tile_width), lambda step: (0, step))
    specs = [None] * 8 + [weights(wide_proj.shape[1]), weights(small_proj.shape[1]), columns, None]
    out_specs = [columns, pl.BlockSpec((8, tile_width), lambda step: (0, step))]
    outs = [f32(rows, model_width), f32(8, model_width)]
    return call(normed_back_kernel, model_width // tile_width, outs, out_specs, [], operands, specs, 0 * 10**9)


def assemble_kernel(
    source, mixer_out_ref, attn_out_ref, mixer_proj_ref, query_ref, pair_ref, state_ref, step_ref
):
    width = mixer_proj_ref.shape[2]
    model_width = mixer_out_ref.shape[1]
    split = width // LEN

    @pl.when(pl.program_id(0) < split)
    def _():
        mixer_out_ref[...] = source[:, :model_width]

    @pl.when(pl.program_id(0) >= split)
    def _():
        attn_out_ref[...] = source[:, :model_width]

    start = model_width
    mixer_proj_ref[:, 0, :] = source[:, start : start + width]
    start += width
    mixer_proj_ref[:, 1, :] = source[:, start : start + width]
    start += width
    query_ref[...] = source[:, start : start + query_ref.shape[1]]
    start += query_ref.shape[1]
    state_ref[...] = source[:, start : start + 2 * LEN]
    start += 2 * LEN
    pair_ref[:, 0, :] = source[:, start : start + LEN]
    step_ref[...] = source[:, start + LEN :]


def assemble(values, width, query_width):
    rows, columns = values.shape
    split = width // LEN

    def plain(count):
        return pl.BlockSpec((LEN, count), lambda at: (at, 0))

    out_specs = [
        pl.BlockSpec((LEN, rows), lambda at: (jnp.minimum(at, split - 1), 0)),
        pl.BlockSpec((LEN, rows), lambda at: (jnp.maximum(at - split, 0), 0)),
        pl.BlockSpec((LEN, 2, width), lambda at: (at, 0, 0)),
        plain(query_width),
        pl.BlockSpec((LEN, 1, LEN), lambda at: (at, 0, 0)),
        plain(2 * LEN),
        plain(LEN),
    ]
    out_shape = [
        f32(width, rows),
        f32(rows - width, rows),
        f32(rows, 2, width),
        f32(rows, query_width),
        f32(rows, 1, LEN),
        f32(rows, 2 * LEN),
        f32(rows, LEN),
    ]
    return call(assemble_kernel, rows // LEN, out_shape, out_specs, [], (values,), [plain(columns)], 0)


def rope_tables(rows):
    half_size = HEAD_DIM // 2
    inverse = np.float32(rope_base) ** (-(2.0 * np.arange(half_size, dtype=np.float32)) / HEAD_DIM)
    angles = np.arange(rows, dtype=np.float32)[:, None] * inverse.astype(np.float32)[None, :]
    cosine, sine = np.cos(angles), np.sin(angles)
    return (
        np.concatenate([cosine] * 4, axis=1).astype(np.float32),
        np.concatenate([-sine, sine, -sine, sine], axis=1).astype(np.float32),
    )


def norm_backward(grad_unit, unit_rows, inv_rms):
    return inv_rms * (grad_unit - unit_rows * jnp.mean(grad_unit * unit_rows, axis=-1, keepdims=True))


def dot32(left, right):
    return jnp.dot(left, right, preferred_element_type=jnp.float32)


def after(value, *others):
    return lax.optimization_barrier((value, *others))[0]


def swap(values, name):
    return lax.ppermute(values, name, PAIR)


def exchange(values, name):
    return values + swap(values, name)


def core_rows(values, index):
    half = values.shape[1] // 2
    return lax.dynamic_slice_in_dim(values, index * half, half, 1)


def on_device(
    layer_input,
    segments,
    input_gain,
    mixer_proj,
    state_proj,
    step_proj,
    step_bias,
    decay_log,
    skip_gain,
    conv_kernel,
    conv_bias,
    state_kernel,
    state_bias,
    gated_gain,
    mixer_out,
    query_proj,
    key_value_weight,
    attn_out,
    ffn_gain,
    ffn_gate,
    ffn_up,
    ffn_down,
    cotangent,
):
    segment = segments.reshape(-1)
    rows, model_width = layer_input.shape
    width = mixer_proj.shape[2]
    heads = step_proj.shape[1]
    state_size = state_proj.shape[1] // 2
    query_width = query_proj.shape[1]
    pair_width = key_value_weight.shape[2]
    place = lax.axis_index("core")
    zh = lax.axis_index("zh")
    core = place.astype(jnp.int32).reshape(1)
    far_core = 1 - core
    cosine, sine = rope_tables(rows)
    select = np.arange(HEAD_ROWS)[:, None] == np.arange(width)[None, :] // HEAD_DIM
    select = jnp.asarray(select.astype(np.float32)).astype(jnp.bfloat16)
    seg_col, seg_row = segment[:, None], segment[None, :]
    keep = [jnp.ones((rows,), jnp.float32)]
    for lag in (1, 2, 3):
        previous = jnp.concatenate([jnp.full((lag,), -1, jnp.int32), segment[:-lag]])
        keep.append((previous == segment).astype(jnp.float32))
    keep = jnp.pad(jnp.stack(keep, axis=1), ((0, 8), (0, 4)))
    pad_heads = ((0, 0), (0, LEN - heads))
    rate_row = jnp.pad(-jnp.exp(decay_log)[None, :], pad_heads)
    step_bias_row = jnp.pad(step_bias[None, :], pad_heads)
    skip_row = jnp.repeat(skip_gain, HEAD_DIM)[None, :]
    gain_row = gated_gain[None, :]
    wide_proj = mixer_proj.reshape(model_width, 2 * width)
    small_proj = jnp.concatenate(
        [
            state_proj,
            query_proj,
            key_value_weight.reshape(model_width, pair_width),
            jnp.pad(step_proj, pad_heads),
        ],
        axis=1,
    )

    tokens = layer_input.astype(jnp.float32)
    inv_rms_in = lax.rsqrt(jnp.mean(tokens * tokens, axis=-1, keepdims=True) + norm_eps)
    unit_in = tokens * inv_rms_in
    normed_input = (unit_in * input_gain).astype(jnp.bfloat16)
    small_in = dot32(normed_input, small_proj)
    wide_in = dot32(normed_input, wide_proj)
    x, xb, slope, state, state_slope, cum, lag, cum_row, lag_row, step_row, sig_row, queries, pairs = scan_prep(
        width,
        wide_in,
        small_in,
        cosine,
        sine,
        keep,
        conv_kernel,
        conv_bias[None, :],
        state_kernel,
        state_bias[None, :],
        step_bias_row,
        rate_row,
    )

    blocks = rows // LEN
    late = tuple(range(blocks // 2, blocks))
    early = tuple(range(blocks // 2))
    half = {}
    for chunks in (late, early):
        h = {"span": slice(chunks[0] * LEN, (chunks[-1] + 1) * LEN)}
        h["y"], h["gated"], h["square"] = scan_forward(
            chunks, heads, wide_in, x, xb, state, cum, lag_row, seg_col, seg_row, skip_row
        )
        half[chunks] = h
    squares = jnp.concatenate([half[early]["square"], half[late]["square"]], axis=1)
    squares_far = swap(squares, "tensor")
    ready = squares
    for chunks in (late, early):
        h = half[chunks]
        h["attended"], h["lse"] = attention_forward(chunks, after(queries, ready), pairs, seg_col, seg_row)
        if chunks == late:
            squares_far = after(squares_far, h["lse"])
            squares_all = squares + squares_far
        h["square"], h["square_far"] = squares[:, h["span"]], squares_far[:, h["span"]]
        h["inv_gated"] = lax.rsqrt(squares_all[:, h["span"]].reshape(-1, 1) / DSSM + norm_eps)
        h["mixer_rows"] = (h["gated"] * h["inv_gated"] * gated_gain).astype(jnp.bfloat16)
        h["part"] = dot32(h["mixer_rows"], mixer_out) + dot32(h["attended"], attn_out)
        h["branch_far"] = swap(h["part"], "tensor")
        ready = h["part"]

    a, b = half[early], half[late]
    gain_ffn = ffn_gain[None, :]
    names = ("hidden", "normed", "activated", "grad_gate_rows", "grad_up_rows", "back", "down")
    for chunks in (late, early):
        h = half[chunks]
        far = h["branch_far"] if chunks == late else after(h["branch_far"], b["back"])
        operands = (layer_input, h["part"], far, gain_ffn, ffn_gate, ffn_up, ffn_down, cotangent)
        h.update(zip(names, ffn(chunks, *operands)))
        h["back_far"] = swap(h["back"], "tensor")

    sides = (after(a["normed"], b["back_far"]), b["normed"], a["activated"], b["activated"])
    sides += (a["grad_gate_rows"], b["grad_gate_rows"], a["grad_up_rows"], b["grad_up_rows"], cotangent)
    first = swap(ffn_weights(far_core, None, *sides), "core")

    for chunks in (late, early):
        h = half[chunks]
        far = h["back_far"] if chunks == late else after(h["back_far"], first)
        h["grad_hidden"], h["grad_branch"], h["grad_rows"], grad_attended, h["dot"], h["gain_sum"] = middle(
            chunks,
            h["hidden"],
            h["back"],
            far,
            cotangent,
            gain_ffn,
            h["gated"],
            h["square"],
            h["square_far"],
            gain_row,
            mixer_out,
            attn_out,
        )
        operands = (queries, pairs, grad_attended, h["lse"], seg_col, seg_row, cosine, sine)
        if chunks == late:
            h["grad_queries"], grad_keys, grad_values = attention_backward(chunks, False, *operands)
            first = ffn_weights(core, after(first, grad_keys), *sides)
            first_sum = lax.psum_scatter(first, ("y", "x"), scatter_dimension=0, tiled=True)
        else:
            dots = jnp.concatenate([a["dot"], b["dot"]], axis=1)
            dots_far = swap(dots, "tensor")
            h["grad_queries"], grad_pairs = attention_backward(chunks, True, *operands, grad_keys, grad_values)
    dots_far = after(dots_far, grad_pairs)
    for chunks in (late, early):
        h = half[chunks]
        h["grad_gate"], h["gy"], h["dx"], h["p"], h["grad_in"], h["grad_out"], h["sums"] = scan_backward(
            chunks,
            heads,
            h["grad_rows"],
            h["gated"],
            h["square"],
            h["square_far"],
            h["dot"],
            dots_far[:, h["span"]],
            gain_row,
            wide_in,
            h["y"],
            x,
            xb,
            state,
            lag,
            cum_row,
            skip_row,
            seg_col,
            seg_row,
            select,
        )
    down = jnp.concatenate([a["down"], b["down"]], axis=0)
    ends = []
    for name in ("gy", "dx", "p", "grad_in", "grad_out"):
        ends += [a[name], b[name]]
    grad_conv, grad_state, grad_step, conv_sum, state_sum, step_sum = scan_end(
        heads,
        *ends,
        xb,
        slope,
        state_slope,
        wide_in,
        small_in,
        step_row,
        sig_row,
        rate_row,
        skip_row,
        keep,
        seg_col,
        seg_row,
        select,
        conv_kernel,
        state_kernel,
    )

    grads = (a["grad_gate"], b["grad_gate"], grad_conv, a["grad_queries"], b["grad_queries"])
    grads += (grad_state, grad_pairs, grad_step)
    sides = (a["mixer_rows"], b["mixer_rows"], a["attended"], b["attended"], normed_input)
    sides += (a["grad_branch"], b["grad_branch"], *grads)
    second_far = swap(mixer_weights(far_core, None, None, *sides), "core")
    partial_normed, input_gain_sum = normed_back(*grads, wide_proj, small_proj, layer_input, inv_rms_in)

    sums = a["sums"] + b["sums"]
    over_tensor = [input_gain_sum[0], state_sum[:4], state_sum[4]]
    alone = [
        step_sum[:heads, 0],
        step_sum[HEAD_ROWS : HEAD_ROWS + heads, 0],
        jnp.sum(sums[0].reshape(heads, HEAD_DIM), axis=1),
        conv_sum[:4],
        conv_sum[4],
        sums[1],
        a["gain_sum"][0] + b["gain_sum"][0],
    ]

    def packed(values):
        flat = jnp.concatenate([v.reshape(-1) for v in values])
        count = -(-flat.shape[0] // model_width)
        return jnp.pad(flat, (0, count * model_width - flat.shape[0])).reshape(count, model_width)

    def unpacked(table, values):
        flat, result, start = table.T.reshape(-1), [], 0
        for v in values:
            result.append(flat[start : start + v.size].reshape(v.shape))
            start += v.size
        return result

    tables = [packed(over_tensor), packed(alone)]
    shared_end = heads + tables[0].shape[0]
    table = jnp.concatenate(tables, axis=0)
    table_end = heads + table.shape[0]
    table = (core_rows(table, place) + swap(core_rows(table, 1 - place), "core")).T
    table = jnp.pad(table, ((0, 0), (heads, LEN - table_end)))
    second = mixer_weights(core, second_far, table, *sides)
    first_own = exchange(after(first_sum, second), "zh")
    first_all = lax.all_gather(first_own, ("core", "y", "x"), axis=0, tiled=True)
    down_far = swap(after(down, first_own), "tensor")
    at_state = model_width + 2 * width + query_width
    at_step = at_state + 2 * state_size + pair_width
    peers = 16
    peer_rows = second.shape[0] // peers
    columns = second.shape[1]
    second = after(second, first_own)
    second = lax.all_to_all(second.reshape(peers, peer_rows, columns), ("y", "x"), 0, 0, tiled=True)

    second = jnp.sum(after(second, down_far), axis=0)
    both = second[:, at_state:]
    summed = exchange(both, "tensor")
    lane = np.arange(both.shape[1])
    in_table = lane - 2 * state_size - pair_width
    is_shared = (lane < 2 * state_size) | ((in_table >= heads) & (in_table < shared_end))
    second = jnp.concatenate([second[:, :at_state], jnp.where(is_shared[None, :], summed, both)], axis=1)
    second = exchange(second, "zh")
    second = after(second, first_all)
    normed_far = swap(after(partial_normed, second), "tensor")
    second = lax.all_gather(second, ("core", "y", "x"), axis=0, tiled=True)
    grad_mixer_out, grad_attn_out, grad_mixer_proj, grad_query_proj, grad_keyval, grad_state_proj, step_block = assemble(
        second, width, query_width
    )

    def whole(name):
        return jnp.concatenate([a[name], b[name]], axis=0)

    grad_hidden = whole("grad_hidden")
    grad_normed = partial_normed + normed_far
    input_grad = grad_hidden + norm_backward(grad_normed * input_gain, unit_in, inv_rms_in)
    layer_output = (whole("hidden") + (down + down_far)).astype(jnp.bfloat16)

    small_shared = unpacked(step_block[:, heads:shared_end], over_tensor)
    small_alone = unpacked(step_block[:, shared_end:table_end], alone)
    return (
        layer_output,
        input_grad,
        small_shared[0],
        grad_mixer_proj,
        grad_state_proj,
        step_block[:, :heads],
        small_alone[0],
        small_alone[1],
        small_alone[2],
        small_alone[3],
        small_alone[4],
        small_shared[1],
        small_shared[2],
        small_alone[5],
        grad_mixer_out,
        grad_query_proj,
        grad_keyval,
        grad_attn_out,
        small_alone[6],
        first_all[:, :model_width],
        first_all[:, model_width : 2 * model_width],
        first_all[:, 2 * model_width :],
    )


def solution(mesh):
    dp, whole_spec, columns = P(DP, None), P(), P(None, "tensor")
    per_channel, middle = P("tensor"), P(None, "tensor", None)
    last, by_rows = P(None, None, "tensor"), P("tensor", None)
    weights = (
        whole_spec,
        last,
        whole_spec,
        columns,
        per_channel,
        per_channel,
        per_channel,
        columns,
        per_channel,
        whole_spec,
        whole_spec,
        per_channel,
        by_rows,
        columns,
        middle,
        by_rows,
        whole_spec,
        columns,
        columns,
        by_rows,
    )
    mesh = jax.sharding.Mesh(mesh.devices.reshape(4, 2, 4, 2, 2), (*DP, "tensor"))
    return jax.shard_map(
        on_device, mesh=mesh, in_specs=(dp, dp, *weights, dp), out_specs=(dp, dp, *weights), check_vma=False
    )
```

```python
import functools

import jax
import jax.numpy as jnp
import numpy as np
from jax import lax
from jax.experimental import pallas as pl
from jax.experimental.pallas import tpu as pltpu
from jax.sharding import PartitionSpec as P

HEAD_DIM = 64
DSSM = 1536
DP = ("y", "zh", "x", "core")
PAIR = [(0, 1), (1, 0)]
LOG2E = 1.4426950408889634
hidden_bias = -1e30
norm_eps = 1e-05
rope_base = 10000.0
LEN = 128


def dot_nn(left, right):
    return lax.dot_general(
        left, right, (((1,), (0,)), ((), ())), preferred_element_type=jnp.float32
    )


def dot_nt(left, right):
    return lax.dot_general(
        left, right, (((1,), (1,)), ((), ())), preferred_element_type=jnp.float32
    )


def dot_tn(left, right):
    return lax.dot_general(
        left, right, (((0,), (0,)), ((), ())), preferred_element_type=jnp.float32
    )


def two_terms(v):
    high = v.astype(jnp.bfloat16)
    return high, (v - high.astype(jnp.float32)).astype(jnp.bfloat16)


def three_dots(dot, left, right):
    left_high, left_low = two_terms(left)
    right_high, right_low = two_terms(right)
    return dot(left_high, right_high) + dot(left_high, right_low) + dot(left_low, right_high)


def sigmoid(v):
    return 1.0 / (1.0 + jnp.exp(-v))


def block(index):
    return slice(index * LEN, (index + 1) * LEN)


def lane_iota(rows=LEN):
    return lax.broadcasted_iota(jnp.int32, (rows, LEN), 1)


def mask_ts(seg_col, seg_row, i, j):
    same = seg_col[block(i), :] == seg_row[:, block(j)]
    if i != j:
        return same
    down = lax.broadcasted_iota(jnp.int32, (LEN, LEN), 0)
    return same & (down >= lane_iota())


def mask_st(seg_col, seg_row, j, i):
    same = seg_col[block(j), :] == seg_row[:, block(i)]
    if i != j:
        return same
    down = lax.broadcasted_iota(jnp.int32, (LEN, LEN), 0)
    return same & (down <= lane_iota())


def conv_rows(pad_ref, keep_ref, kernel, bias, start, lanes):
    summed = bias + kernel[3:4] * pad_ref[8 + start : 8 + start + LEN, lanes]
    for lag in (1, 2, 3):
        moved = pad_ref[8 + start - lag : 8 + start - lag + LEN, lanes]
        summed = summed + kernel[3 - lag : 4 - lag] * (moved * keep_ref[lag - 1, start : start + LEN, :])
    return summed


def widen(keep_ref, wide_ref):
    rows = keep_ref.shape[0]
    for lag in (1, 2, 3):
        wide_ref[lag - 1, :, :] = jnp.broadcast_to(keep_ref[:, lag : lag + 1], (rows, LEN))


def prep_kernel(
    conv_ref,
    small_ref,
    cos_ref,
    sin_ref,
    keep_ref,
    conv_kernel_ref,
    conv_bias_ref,
    state_kernel_ref,
    state_bias_ref,
    step_bias_ref,
    rate_ref,
    x_ref,
    xb_ref,
    slope_ref,
    state_ref,
    state_slope_ref,
    cum_ref,
    lag_ref,
    cum_row_ref,
    lag_row_ref,
    step_row_ref,
    sig_row_ref,
    q_ref,
    kv_ref,
    pad_ref,
    wide_ref,
):
    rows = conv_ref.shape[0]
    blocks = rows // LEN

    @pl.when(pl.program_id(0) == 0)
    def _():
        pad_ref[0:8, :] = jnp.zeros((8, LEN), jnp.float32)
        widen(keep_ref, wide_ref)
        for c in range(2):
            pad_ref[8 : rows + 8, :] = small_ref[:, block(c)]
            for i in range(blocks):
                pre = conv_rows(
                    pad_ref, wide_ref, state_kernel_ref[:, block(c)], state_bias_ref[:, block(c)], i * LEN, slice(0, LEN)
                )
                sig = sigmoid(pre)
                state_ref[block(i), block(c)] = pre * sig
                state_slope_ref[block(i), block(c)] = sig * (1.0 + pre * (1.0 - sig))

    @pl.when(pl.program_id(0) == 1)
    def _():
        down = lax.broadcasted_iota(jnp.int32, (LEN, LEN), 0)
        lower = jnp.where(down >= lane_iota(), 1.0, 0.0).astype(jnp.bfloat16)
        left_half = lane_iota() < HEAD_DIM
        carry = jnp.zeros((1, LEN), jnp.float32)
        heads = cum_row_ref.shape[0]
        for i in range(blocks):
            argument = small_ref[block(i), block(5)] + step_bias_ref[...]
            tail = jnp.exp(-jnp.abs(argument))
            grown = jnp.where(tail < 1e-3, tail - 0.5 * tail * tail, jnp.log(1.0 + tail))
            step = jnp.maximum(argument, 0.0) + grown
            scaled = step * rate_ref[...] * LOG2E
            first, rest = two_terms(scaled)
            last = scaled - first.astype(jnp.float32) - rest.astype(jnp.float32)
            cum = dot_nn(lower, first) + dot_nn(lower, rest) + dot_nn(lower, last.astype(jnp.bfloat16)) + carry
            carry = cum[LEN - 1 : LEN, :]
            lag = cum - jnp.log(step) * LOG2E
            cum_ref[block(i), :] = cum
            lag_ref[block(i), :] = lag
            cum_t, lag_t = cum.T, lag.T
            step_row_ref[:, block(i)] = step.T[:heads]
            sig_row_ref[:, block(i)] = sigmoid(argument).T[:heads]
            for h in range(heads):
                cum_row_ref[h, :, block(i)] = cum_t[h : h + 1]
                lag_row_ref[h, :, block(i)] = lag_t[h : h + 1]
            cosine, sine = cos_ref[block(i), :], sin_ref[block(i), :]
            kv = small_ref[block(i), block(4)]
            kv_ref[block(i), :] = jnp.where(left_half, rotate_tile(kv, cosine, sine), kv).astype(jnp.bfloat16)
            for p in range(q_ref.shape[1] // LEN):
                q_ref[block(i), block(p)] = rotate_tile(small_ref[block(i), block(2 + p)], cosine, sine).astype(
                    jnp.bfloat16
                )

    for sub in range(GROUP):
        lanes = block(sub)
        pad_ref[8 : rows + 8, :] = conv_ref[:, lanes]
        for i in range(blocks):
            pre = conv_rows(pad_ref, wide_ref, conv_kernel_ref[:, lanes], conv_bias_ref[:, lanes], i * LEN, slice(0, LEN))
            sig = sigmoid(pre)
            x = pre * sig
            x_ref[block(i), lanes] = x
            xb_ref[block(i), lanes] = x.astype(jnp.bfloat16)
            slope_ref[block(i), lanes] = sig * (1.0 + pre * (1.0 - sig))


def rotate_tile(v, cosine, sine):
    first = lax.rem(lane_iota(v.shape[0]), HEAD_DIM) < HEAD_DIM // 2
    swapped = jnp.where(first, pltpu.roll(v, LEN - HEAD_DIM // 2, 1), pltpu.roll(v, HEAD_DIM // 2, 1))
    return v * cosine + swapped * sine


def scan_kernel(
    chunks,
    heads,
    gate_ref,
    x_ref,
    xb_ref,
    state_ref,
    cum_ref,
    lag_row_ref,
    seg_col_ref,
    seg_row_ref,
    skip_ref,
    y_ref,
    gated_ref,
    row_ref,
    wide_ref,
    cross_ref,
    bias_ref,
    mix_ref,
    square_ref,
):
    step = pl.program_id(0)
    first = chunks[0]
    pairs = [(i, j) for i in chunks for j in range(max(0, i - 2), i + 1)]
    left_half = lane_iota() < HEAD_DIM

    @pl.when(step == 0)
    def _():
        for h in range(heads):
            for i in chunks:
                wide_ref[h, block(i - first), :] = jnp.broadcast_to(cum_ref[block(i), h : h + 1], (LEN, LEN))
        for i in chunks:
            low = max(0, i - 2)
            cross = three_dots(dot_nt, state_ref[block(i), LEN:], state_ref[low * LEN : (i + 1) * LEN, :LEN])
            for n, (i2, j) in enumerate(pairs):
                if i2 == i:
                    cross_ref[n] = cross[:, block(j - low)]
                    allowed = mask_ts(seg_col_ref, seg_row_ref, i, j)
                    bias_ref[n] = jnp.where(allowed, 0.0, hidden_bias)
        square_ref[...] = jnp.zeros(square_ref.shape, jnp.float32)

    tiles = (gate_ref, x_ref, xb_ref, skip_ref, y_ref, gated_ref)

    def head_pair(hp, gate_ref, x_ref, xb_ref, skip_ref, y_ref, gated_ref):
        for i in chunks:
            at = block(i - first)
            low = max(0, i - 2)
            for n, (i2, j) in enumerate(pairs):
                if i2 != i:
                    continue
                for e in range(2):
                    spread = wide_ref[2 * hp + e, at, :] - lag_row_ref[2 * hp + e, :, block(j)]
                    decay = jnp.exp2(spread + bias_ref[n])
                    mix_ref[i - first, block(e), block(j - low)] = (decay * cross_ref[n]).astype(jnp.bfloat16)
            both = dot_nn(mix_ref[i - first, :, : (i + 1 - low) * LEN], xb_ref[low * LEN : (i + 1) * LEN, :])
            y = jnp.where(left_half, both[:LEN], both[LEN:])
            y_ref[at, :] = y
            gate = gate_ref[at, :]
            gated = (y + skip_ref[...] * x_ref[at, :]) * (gate * sigmoid(gate))
            gated_ref[at, :] = gated
            square_ref[at, :] = square_ref[at, :] + gated * gated

    for sub in range(GROUP):
        head_pair(GROUP * step + sub, *[t.at[:, block(sub)] for t in tiles])

    @pl.when(step == pl.num_programs(0) - 1)
    def _():
        for i in chunks:
            at = block(i - first)
            total = jnp.sum(square_ref[at, :], axis=1, keepdims=True)
            row_ref[0:1, at] = jnp.broadcast_to(total, (LEN, LEN)).T[0:1]


def attention_kernel(chunks, q_ref, kv_ref, seg_col_ref, seg_row_ref, out_ref, lse_ref):
    scale = HEAD_DIM ** (-0.5) * LOG2E
    first = chunks[0]
    left_half = lane_iota() < HEAD_DIM
    zero = jnp.zeros((LEN, LEN), jnp.bfloat16)
    lse_ref[...] = jnp.zeros(lse_ref.shape, jnp.float32)
    for i in chunks:
        at = block(i - first)
        low = max(0, i - 2) * LEN
        span = (i + 1) * LEN - low
        allowed = jnp.concatenate([mask_ts(seg_col_ref, seg_row_ref, i, j) for j in range(low // LEN, i + 1)], axis=1)
        keys = kv_ref[low : low + span, :]
        turned = pltpu.roll(keys.astype(jnp.float32), HEAD_DIM, 1).astype(jnp.bfloat16)
        for p in range(q_ref.shape[1] // LEN):
            queries = q_ref[block(i), block(p)]
            result = []
            for e in range(2):
                masked = jnp.where(left_half == (e == 0), queries, zero)
                scores = dot_nt(masked, keys if e == 0 else turned) * scale
                scores = jnp.where(allowed, scores, hidden_bias)
                top = jnp.max(scores, axis=1, keepdims=True)
                weights = jnp.exp2(scores - top)
                total = jnp.sum(weights, axis=1, keepdims=True)
                probs = (weights * (1.0 / total)).astype(jnp.bfloat16)
                result.append(dot_nn(probs, turned if e == 0 else keys))
                lse = jnp.broadcast_to(top + jnp.log(total) * LOG2E, (LEN, LEN))
                lse_ref[2 * p + e : 2 * p + e + 1, at] = lse.T[0:1]
            out_ref[at, block(p)] = jnp.where(left_half, result[0], result[1]).astype(jnp.bfloat16)


def attention_back_kernel(chunks, final, *refs):
    q_ref, kv_ref, do_ref, lse_ref, seg_col_ref, seg_row_ref, cos_ref, sin_ref = refs[:8]
    if final:
        dk_in_ref, dv_in_ref, dq_ref, dkv_ref, dk_ref, dv_ref, turned_ref, key_t_ref = refs[8:]
    else:
        dq_ref, dk_ref, dv_ref, turned_ref, key_t_ref = refs[8:]
    scale = HEAD_DIM ** (-0.5)
    blocks = q_ref.shape[0] // LEN
    first = chunks[0]
    left_half = lane_iota() < HEAD_DIM
    zero = jnp.zeros((LEN, LEN), jnp.bfloat16)
    for i in range(chunks[-1] + 1):
        kv = kv_ref[block(i), :].astype(jnp.float32)
        turned_ref[block(i), :] = pltpu.roll(kv, HEAD_DIM, 1).astype(jnp.bfloat16)
        key_t_ref[:, block(i)] = kv.T[:HEAD_DIM].astype(jnp.bfloat16)
    if final:
        dk_ref[...] = dk_in_ref[...]
        dv_ref[...] = dv_in_ref[...]
    else:
        dk_ref[...] = jnp.zeros(dk_ref.shape, jnp.float32)
        dv_ref[...] = jnp.zeros(dv_ref.shape, jnp.float32)
    for i in chunks:
        at = block(i - first)
        low = max(0, i - 2) * LEN
        span = (i + 1) * LEN - low
        window = slice(low, low + span)
        allowed = jnp.concatenate([mask_st(seg_col_ref, seg_row_ref, j, i) for j in range(low // LEN, i + 1)], axis=0)
        keys, turned = kv_ref[window, :], turned_ref[window, :]
        for p in range(q_ref.shape[1] // LEN):
            queries, douts = q_ref[block(i), block(p)], do_ref[at, block(p)]
            back = []
            for e in range(2):
                side = left_half == (e == 0)
                q_half = jnp.where(side, queries, zero)
                do_half = jnp.where(side, douts, zero)
                h = 2 * p + e
                scores = dot_nt(keys if e == 0 else turned, q_half) * (scale * LOG2E)
                probs = jnp.exp2(jnp.where(allowed, scores, hidden_bias) - lse_ref[h : h + 1, at])
                dprobs = dot_nt(turned if e == 0 else keys, do_half)
                inner = jnp.sum(probs * dprobs, axis=0, keepdims=True)
                dscores = (probs * (dprobs - inner)).astype(jnp.bfloat16)
                dv_ref[window, :] = dv_ref[window, :] + dot_nn(probs.astype(jnp.bfloat16), do_half)
                dk_ref[window, :] = dk_ref[window, :] + dot_nn(dscores, q_half)
                back.append(dot_nn(key_t_ref[:, window], dscores))
            dq = jnp.concatenate(back, axis=0).T * scale
            dq_ref[at, block(p)] = rotate_tile(dq, cos_ref[block(i), :], -sin_ref[block(i), :]).astype(jnp.bfloat16)
    if not final:
        return
    for i in range(blocks):
        dk = dk_ref[block(i), :]
        dk = (dk + pltpu.roll(dk, HEAD_DIM, 1)) * scale
        dk = rotate_tile(dk, cos_ref[block(i), :], -sin_ref[block(i), :])
        dv = dv_ref[block(i), :]
        dv = dv + pltpu.roll(dv, HEAD_DIM, 1)
        dkv_ref[block(i), :] = jnp.where(left_half, dk, dv).astype(jnp.bfloat16)


def scan_back_kernel(
    chunks,
    heads,
    gmr_ref,
    gated_ref,
    square_a_ref,
    square_b_ref,
    dot_a_ref,
    dot_b_ref,
    gain_ref,
    gate_ref,
    y_ref,
    x_ref,
    xb_ref,
    state_ref,
    lag_ref,
    cum_row_ref,
    skip_ref,
    seg_col_ref,
    seg_row_ref,
    select_ref,
    dgate_ref,
    gy_ref,
    dx_ref,
    p_ref,
    grad_in_ref,
    grad_out_ref,
    sums_ref,
    gyb_ref,
    wide_ref,
    cross_ref,
    bias_ref,
    dcross_ref,
    inv_wide_ref,
    dot_wide_ref,
    inner_ref,
    mix_ref,
):
    step = pl.program_id(0)
    first = chunks[0]
    sources = chunks[-1] + 1
    left_half = lane_iota() < HEAD_DIM
    zero = jnp.zeros((LEN, LEN), jnp.bfloat16)
    spans = [(j, max(j, first), min(j + 3, sources)) for j in range(sources)]
    pairs = [(j, i) for j, start, stop in spans for i in range(start, stop)]

    @pl.when(step == 0)
    def _():
        for i in chunks:
            at = block(i - first)
            square = (square_a_ref[:, at] + square_b_ref[:, at]) / DSSM
            inv = lax.rsqrt(square + norm_eps)
            inv_wide_ref[at, :] = jnp.broadcast_to(inv, (LEN, LEN)).T
            dot = (dot_a_ref[:, at] + dot_b_ref[:, at]) / DSSM
            dot_wide_ref[at, :] = jnp.broadcast_to(dot, (LEN, LEN)).T
        p_ref[...] = jnp.zeros(p_ref.shape, jnp.float32)
        for h in range(heads):
            wide_ref[h] = jnp.broadcast_to(lag_ref[: sources * LEN, h : h + 1], (sources * LEN, LEN))
        for j, start, stop in spans:
            cross = three_dots(dot_nt, state_ref[block(j), :LEN], state_ref[start * LEN : stop * LEN, LEN:])
            for n, (j2, i) in enumerate(pairs):
                if j2 == j:
                    cross_ref[n] = cross[:, block(i - start)]
                    allowed = mask_st(seg_col_ref, seg_row_ref, j, i)
                    bias_ref[n] = jnp.where(allowed, 0.0, hidden_bias)
                    dcross_ref[n] = jnp.zeros((LEN, LEN), jnp.float32)

    tiles = (
        gmr_ref, gated_ref, gain_ref, gate_ref, y_ref, x_ref, xb_ref, skip_ref, dgate_ref, gy_ref, dx_ref, sums_ref
    )

    def head_pair(
        hp,
        select,
        gmr_ref,
        gated_ref,
        gain_ref,
        gate_ref,
        y_ref,
        x_ref,
        xb_ref,
        skip_ref,
        dgate_ref,
        gy_ref,
        dx_ref,
        sums_ref,
    ):
        skip = skip_ref[...]
        gain = gain_ref[...]
        skip_sum = jnp.zeros((1, LEN), jnp.float32)
        gain_sum = jnp.zeros((1, LEN), jnp.float32)
        for i in chunks:
            at = block(i - first)
            inv = inv_wide_ref[at, :]
            unit = gated_ref[at, :] * inv
            rows_grad = gmr_ref[at, :]
            grad = inv * (rows_grad * gain - unit * dot_wide_ref[at, :])
            gate = gate_ref[at, :]
            sig = sigmoid(gate)
            y = y_ref[at, :]
            x = x_ref[at, :]
            gy = grad * (gate * sig)
            dgate_ref[at, :] = (grad * (y + skip * x) * (sig * (1.0 + gate * (1.0 - sig)))).astype(jnp.bfloat16)
            gyb = gy.astype(jnp.bfloat16)
            gy_ref[at, :] = gy
            gyb_ref[at, :] = gyb
            high, rest = two_terms(gyb.astype(jnp.float32) * y)
            p_ref[:, at] = p_ref[:, at] + dot_nt(select, high) + dot_nt(select, rest)
            skip_sum = skip_sum + jnp.sum(gy * x, axis=0, keepdims=True)
            gain_sum = gain_sum + jnp.sum(rows_grad * unit, axis=0, keepdims=True)
        sums_ref[0:1, :] = skip_sum
        sums_ref[1:2, :] = gain_sum

        for j, start, stop in spans:
            x_pair = xb_ref[block(j), :]
            x_both = jnp.concatenate([jnp.where(left_half, x_pair, zero), jnp.where(left_half, zero, x_pair)], axis=0)
            wide = (stop - start) * LEN
            gy_rows = gyb_ref[(start - first) * LEN : (stop - first) * LEN, :]
            inner_ref[:, :wide] = dot_nt(x_both, gy_rows)
            for n, (j2, i) in enumerate(pairs):
                if j2 != j:
                    continue
                grown = dcross_ref[n]
                for e in range(2):
                    spread = cum_row_ref[2 * hp + e, :, block(i)] - wide_ref[2 * hp + e, block(j), :]
                    decay = jnp.exp2(spread + bias_ref[n])
                    grown = grown + inner_ref[block(e), block(i - start)] * decay
                    mix_ref[block(e), block(i - start)] = (decay * cross_ref[n]).astype(jnp.bfloat16)
                dcross_ref[n] = grown
            both = dot_nn(mix_ref[:, :wide], gy_rows)
            dx_ref[block(j), :] = jnp.where(left_half, both[:LEN], both[LEN:])

    for sub in range(GROUP):
        head_pair(GROUP * step + sub, select_ref[:, block(sub)], *[t.at[:, block(sub)] for t in tiles])

    @pl.when(step == pl.num_programs(0) - 1)
    def _():
        grad_out = {i: jnp.zeros((LEN, LEN), jnp.float32) for i in chunks}
        for j in range(sources):
            grad_in = jnp.zeros((LEN, LEN), jnp.float32)
            for n, (j2, i) in enumerate(pairs):
                if j2 != j:
                    continue
                high, rest = two_terms(dcross_ref[n])
                out_high, out_rest = two_terms(state_ref[block(i), LEN:])
                in_high, in_rest = two_terms(state_ref[block(j), :LEN])
                grad_in = grad_in + dot_nn(high, out_high) + dot_nn(high, out_rest) + dot_nn(rest, out_high)
                grad_out[i] = grad_out[i] + dot_tn(high, in_high) + dot_tn(high, in_rest) + dot_tn(rest, in_high)
            grad_in_ref[block(j), :] = grad_in
        for i in chunks:
            grad_out_ref[block(i - first), :] = grad_out[i]


def conv_back(grad_ref, value_ref, keep_ref, kernel_ref, out_ref, sum_ref, lanes, blocks):
    taps = kernel_ref[:, lanes]
    totals = [jnp.zeros((1, LEN), jnp.float32) for _ in range(5)]
    for i in range(blocks):
        here = grad_ref[i * LEN : (i + 1) * LEN, :]
        grad = taps[3:4] * here
        totals[4] = totals[4] + jnp.sum(here, axis=0, keepdims=True)
        totals[3] = totals[3] + jnp.sum(here * value_ref[8 + i * LEN : 8 + (i + 1) * LEN, :], axis=0, keepdims=True)
        for lag in (1, 2, 3):
            ahead = grad_ref[i * LEN + lag : (i + 1) * LEN + lag, :]
            grad = grad + taps[3 - lag : 4 - lag] * (ahead * keep_ref[lag - 1, i * LEN + lag : (i + 1) * LEN + lag, :])
            moved = value_ref[8 + i * LEN - lag : 8 + (i + 1) * LEN - lag, :]
            masked = here * keep_ref[lag - 1, i * LEN : (i + 1) * LEN, :]
            totals[3 - lag] = totals[3 - lag] + jnp.sum(masked * moved, axis=0, keepdims=True)
        out_ref[block(i), lanes] = grad.astype(jnp.bfloat16)
    for tap in range(5):
        sum_ref[tap : tap + 1, lanes] = totals[tap]


def scan_end_kernel(
    heads,
    gy_a_ref,
    gy_b_ref,
    dx_a_ref,
    dx_b_ref,
    p_a_ref,
    p_b_ref,
    in_a_ref,
    in_b_ref,
    out_a_ref,
    out_b_ref,
    xb_ref,
    slope_ref,
    state_slope_ref,
    conv_ref,
    small_ref,
    step_row_ref,
    sig_row_ref,
    rate_ref,
    skip_ref,
    keep_ref,
    seg_col_ref,
    seg_row_ref,
    select_ref,
    conv_kernel_ref,
    state_kernel_ref,
    dconv_ref,
    dstate_ref,
    dstep_ref,
    conv_sum_ref,
    state_sum_ref,
    step_sum_ref,
    grad_pad_ref,
    value_pad_ref,
    wide_ref,
    q_ref,
    flow_ref,
):
    step = pl.program_id(0)
    rows = conv_ref.shape[0]
    blocks = rows // LEN
    half = rows // 2
    count = flow_ref.shape[0]

    @pl.when(step == 0)
    def _():
        value_pad_ref[0:8, :] = jnp.zeros((8, LEN), jnp.float32)
        grad_pad_ref[rows : rows + 8, :] = jnp.zeros((8, LEN), jnp.float32)
        widen(keep_ref, wide_ref)
        q_ref[...] = jnp.zeros(q_ref.shape, jnp.float32)
        for c in range(2):
            if c == 0:
                grad_pad_ref[0:half, :] = (in_a_ref[...] + in_b_ref[0:half, :]) * state_slope_ref[0:half, block(c)]
                grad_pad_ref[half:rows, :] = in_b_ref[half:rows, :] * state_slope_ref[half:rows, block(c)]
            else:
                grad_pad_ref[0:half, :] = out_a_ref[...] * state_slope_ref[0:half, block(c)]
                grad_pad_ref[half:rows, :] = out_b_ref[...] * state_slope_ref[half:rows, block(c)]
            value_pad_ref[8 : rows + 8, :] = small_ref[:, block(c)]
            conv_back(grad_pad_ref, value_pad_ref, wide_ref, state_kernel_ref, dstate_ref, state_sum_ref, block(c), blocks)

    tiles = (
        gy_a_ref, gy_b_ref, dx_a_ref, dx_b_ref, xb_ref, slope_ref, conv_ref, skip_ref, conv_kernel_ref, dconv_ref, conv_sum_ref
    )

    def head_pair(
        select,
        gy_a_ref,
        gy_b_ref,
        dx_a_ref,
        dx_b_ref,
        xb_ref,
        slope_ref,
        conv_ref,
        skip_ref,
        conv_kernel_ref,
        dconv_ref,
        conv_sum_ref,
    ):
        for j in range(blocks):
            dx = dx_b_ref[block(j), :]
            if j < blocks // 2:
                dx = dx + dx_a_ref[block(j), :]
                gy = gy_a_ref[block(j), :]
            else:
                gy = gy_b_ref[block(j - blocks // 2), :]
            high, rest = two_terms(dx * xb_ref[block(j), :].astype(jnp.float32))
            q_ref[:, block(j)] = q_ref[:, block(j)] + dot_nt(select, high) + dot_nt(select, rest)
            grad_pad_ref[block(j), :] = (dx + gy * skip_ref[...]) * slope_ref[block(j), :]
        value_pad_ref[8 : rows + 8, :] = conv_ref[...]
        conv_back(
            grad_pad_ref, value_pad_ref, wide_ref, conv_kernel_ref, dconv_ref, conv_sum_ref, slice(0, LEN), blocks
        )

    for sub in range(GROUP):
        head_pair(select_ref[:, block(sub)], *[t.at[:, block(sub)] for t in tiles])

    @pl.when(step == pl.num_programs(0) - 1)
    def _():
        q = q_ref[...]
        flow_ref[:, 0:half] = p_a_ref[...] - q[:, 0:half]
        flow_ref[:, half:rows] = p_b_ref[...] - q[:, half:rows]
        rate = jnp.broadcast_to(rate_ref[...], (LEN, LEN)).T[:count]
        bias_total = jnp.zeros((count, LEN), jnp.float32)
        decay_total = jnp.zeros((count, LEN), jnp.float32)
        for j in range(blocks):
            log_grad = jnp.zeros((count, LEN), jnp.float32)
            for i in range(j, min(j + 3, blocks)):
                chosen = jnp.where(mask_st(seg_col_ref, seg_row_ref, j, i), 1.0, 0.0).astype(jnp.bfloat16)
                high, rest = two_terms(flow_ref[:, block(i)])
                log_grad = log_grad + dot_nt(high, chosen) + dot_nt(rest, chosen)
            step = step_row_ref[:, block(j)]
            grad_step = jnp.where(step > 1e-30, q[:, block(j)] / step, 0.0) + log_grad * rate
            grad_arg = grad_step * sig_row_ref[:, block(j)]
            bias_total = bias_total + grad_arg
            decay_total = decay_total + log_grad * step
            tall = jnp.concatenate([grad_arg, jnp.zeros((LEN - count, LEN), jnp.float32)], axis=0)
            dstep_ref[block(j), :] = tall.T.astype(jnp.bfloat16)
        step_sum_ref[0:count, :] = jnp.broadcast_to(jnp.sum(bias_total, axis=1, keepdims=True), (count, LEN))
        step_sum_ref[count : 2 * count, :] = jnp.broadcast_to(
            jnp.sum(decay_total * rate, axis=1, keepdims=True), (count, LEN)
        )


def whole_block(shape):
    return pl.BlockSpec(shape, lambda step: (0,) * len(shape), pipeline_mode=pl.Buffered(1))


def tile(rows, row_block=0, first=0):
    return pl.BlockSpec((rows, GROUP * LEN), lambda step: (row_block, first + step))


def call(kernel, steps, out_shape, out_specs, scratch, operands, specs, flops):
    return pl.pallas_call(
        kernel,
        grid=(steps,),
        out_shape=out_shape,
        in_specs=[s or whole_block(o.shape) for o, s in zip(operands, specs)],
        out_specs=[s or whole_block(o.shape) for o, s in zip(out_shape, out_specs)],
        scratch_shapes=scratch,
        compiler_params=pltpu.CompilerParams(vmem_limit_bytes=VMEM_BYTES),
        cost_estimate=pl.CostEstimate(flops=flops, bytes_accessed=0, transcendentals=0),
    )(*operands)


def f32(*shape):
    return jax.ShapeDtypeStruct(shape, jnp.float32)


def b16(*shape):
    return jax.ShapeDtypeStruct(shape, jnp.bfloat16)


HEAD_ROWS = 16
GROUP = 3
VMEM_BYTES = 60 * 1024 * 1024


def scan_prep(width, wide_in, small, cosine, sine, keep, conv_kernel, conv_bias, *rest):
    rows = wide_in.shape[0]
    steps = width // LEN // GROUP
    outs = [
        f32(rows, width),
        b16(rows, width),
        f32(rows, width),
        f32(rows, 2 * LEN),
        f32(rows, 2 * LEN),
        f32(rows, LEN),
        f32(rows, LEN),
        f32(HEAD_ROWS, 1, rows),
        f32(HEAD_ROWS, 1, rows),
        f32(HEAD_ROWS, rows),
        f32(HEAD_ROWS, rows),
        b16(rows, 2 * LEN),
        b16(rows, LEN),
    ]
    scratch = [pltpu.VMEM((rows + 8, LEN), jnp.float32), pltpu.VMEM((3, rows + 8, LEN), jnp.float32)]
    operands = (wide_in, small, cosine, sine, keep, conv_kernel, conv_bias, *rest)
    specs = [tile(rows, 0, steps), None, None, None, None, tile(4), tile(1)] + [None] * len(rest)
    return call(prep_kernel, steps, outs, [tile(rows)] * 3 + [None] * 10, scratch, operands, specs, 0 * 10**9)


def scan_forward(chunks, heads, wide_in, x, xb, *rest):
    width = x.shape[1]
    rows = LEN * len(chunks)
    at = chunks[0] // len(chunks)
    count = sum(min(i, 2) + 1 for i in chunks)
    outs = [f32(rows, width), f32(rows, width), f32(1, rows)]
    scratch = [
        pltpu.VMEM((heads, rows, LEN), jnp.float32),
        pltpu.VMEM((count, LEN, LEN), jnp.float32),
        pltpu.VMEM((count, LEN, LEN), jnp.float32),
        pltpu.VMEM((len(chunks), 2 * LEN, 3 * LEN), jnp.bfloat16),
        pltpu.VMEM((rows, LEN), jnp.float32),
    ]
    specs = [tile(rows, at), tile(rows, at), tile((chunks[-1] + 1) * LEN)] + [None] * (len(rest) - 1) + [tile(1)]
    kernel = functools.partial(scan_kernel, chunks, heads)
    operands = (wide_in, x, xb, *rest)
    return call(kernel, heads // 2 // GROUP, outs, [tile(rows), tile(rows), None], scratch, operands, specs, 0 * 10**9)


def attention_forward(chunks, q, kv, seg_col, seg_row):
    rows = LEN * len(chunks)
    outs = [b16(rows, q.shape[1]), f32(8, rows)]
    kernel = functools.partial(attention_kernel, chunks)
    return call(kernel, 1, outs, [None] * 2, [], (q, kv, seg_col, seg_row), [None] * 4, 0 * 10**9)


def attention_backward(chunks, final, *operands):
    q = operands[0]
    rows = q.shape[0]
    partial = [f32(rows, LEN), f32(rows, LEN)]
    sums = [pltpu.VMEM((rows, LEN), jnp.float32)] * 2
    outs = [b16(LEN * len(chunks), q.shape[1])] + ([b16(rows, LEN)] if final else partial)
    scratch = (sums if final else []) + [
        pltpu.VMEM((rows, LEN), jnp.bfloat16),
        pltpu.VMEM((HEAD_DIM, rows), jnp.bfloat16),
    ]
    kernel = functools.partial(attention_back_kernel, chunks, final)
    return call(kernel, 1, outs, [None] * len(outs), scratch, operands, [None] * len(operands), 0 * 10**9)


def scan_backward(chunks, heads, *operands):
    rows, width = operands[0].shape
    at = chunks[0] // len(chunks)
    sources = (chunks[-1] + 1) * LEN
    count = sum(min(i, 2) + 1 for i in chunks)
    outs = [
        b16(rows, width),
        f32(rows, width),
        f32(sources, width),
        f32(HEAD_ROWS, rows),
        f32(sources, LEN),
        f32(rows, LEN),
        f32(8, width),
    ]
    scratch = [
        pltpu.VMEM((rows, LEN), jnp.bfloat16),
        pltpu.VMEM((heads, sources, LEN), jnp.float32),
        pltpu.VMEM((count, LEN, LEN), jnp.float32),
        pltpu.VMEM((count, LEN, LEN), jnp.float32),
        pltpu.VMEM((count, LEN, LEN), jnp.float32),
        pltpu.VMEM((rows, LEN), jnp.float32),
        pltpu.VMEM((rows, LEN), jnp.float32),
        pltpu.VMEM((2 * LEN, 3 * LEN), jnp.float32),
        pltpu.VMEM((2 * LEN, 3 * LEN), jnp.bfloat16),
    ]
    specs = [tile(rows), tile(rows), None, None, None, None, tile(1), tile(rows, at), tile(rows), tile(rows, at), tile(sources)]
    specs += [None, None, None, tile(1), None, None, tile(HEAD_ROWS)]
    out_specs = [tile(rows), tile(rows), tile(sources), None, None, None, tile(8)]
    kernel = functools.partial(scan_back_kernel, chunks, heads)
    return call(kernel, heads // 2 // GROUP, outs, out_specs, scratch, operands, specs, 30 * 10**9)


def scan_end(heads, *operands):
    rows, width = 2 * operands[0].shape[0], operands[0].shape[1]
    steps = heads // 2 // GROUP
    outs = [
        b16(rows, width),
        b16(rows, 2 * LEN),
        b16(rows, LEN),
        f32(8, width),
        f32(8, 2 * LEN),
        f32(2 * HEAD_ROWS, LEN),
    ]
    scratch = [
        pltpu.VMEM((rows + 8, LEN), jnp.float32),
        pltpu.VMEM((rows + 8, LEN), jnp.float32),
        pltpu.VMEM((3, rows + 8, LEN), jnp.float32),
        pltpu.VMEM((HEAD_ROWS, rows), jnp.float32),
        pltpu.VMEM((HEAD_ROWS, rows), jnp.float32),
    ]
    half = rows // 2
    specs = [tile(half), tile(half), tile(half), tile(rows)] + [None] * 6 + [tile(rows), tile(rows), None]
    specs += [tile(rows, 0, steps)] + [None] * 4 + [tile(1), None, None, None, tile(HEAD_ROWS), tile(4), None]
    out_specs = [tile(rows), None, None, tile(8), None, None]
    kernel = functools.partial(scan_end_kernel, heads)
    return call(kernel, steps, outs, out_specs, scratch, operands, specs, 30 * 10**9)


def inverse_rms(rows):
    return lax.rsqrt(jnp.mean(rows * rows, axis=-1, keepdims=True) + norm_eps)


def ffn_kernel(
    tokens_ref,
    part_ref,
    far_ref,
    gain_ref,
    gate_ref,
    up_ref,
    down_ref,
    cotangent_ref,
    hidden_ref,
    normed_ref,
    activated_ref,
    grad_gate_ref,
    grad_up_ref,
    back_ref,
    out_ref,
):
    @pl.when(pl.program_id(0) == 0)
    def _():
        hidden = tokens_ref[...].astype(jnp.float32) + (part_ref[...] + far_ref[...])
        hidden_ref[...] = hidden
        normed_ref[...] = (hidden * inverse_rms(hidden) * gain_ref[...]).astype(jnp.bfloat16)
        back_ref[...] = jnp.zeros(back_ref.shape, jnp.float32)
        out_ref[...] = jnp.zeros(out_ref.shape, jnp.float32)

    normed = normed_ref[...]
    gate = dot_nn(normed, gate_ref[...])
    up = dot_nn(normed, up_ref[...])
    sig = sigmoid(gate)
    act = gate * sig
    activated = (act * up).astype(jnp.bfloat16)
    activated_ref[...] = activated
    grad = dot_nt(cotangent_ref[...], down_ref[...])
    grad_gate = (grad * up * (sig * (1.0 + gate * (1.0 - sig)))).astype(jnp.bfloat16)
    grad_up = (grad * act).astype(jnp.bfloat16)
    grad_gate_ref[...] = grad_gate
    grad_up_ref[...] = grad_up
    back_ref[...] = back_ref[...] + (dot_nt(grad_gate, gate_ref[...]) + dot_nt(grad_up, up_ref[...]))
    out_ref[...] = out_ref[...] + dot_nn(activated, down_ref[...])


def ffn(chunks, tokens, part, far, gain, gate, up, down, cotangent):
    rows, model_width = part.shape
    at = chunks[0] // len(chunks)
    hidden_width = gate.shape[1]
    steps = hidden_width // 256
    outs = [f32(rows, model_width), b16(rows, model_width)] + [b16(rows, hidden_width)] * 3
    outs += [f32(rows, model_width)] * 2
    rows_of = pl.BlockSpec((rows, model_width), lambda step: (at, 0), pipeline_mode=pl.Buffered(1))
    columns = pl.BlockSpec((model_width, 256), lambda step: (0, step))
    tiles = pl.BlockSpec((rows, 256), lambda step: (0, step))
    specs = [rows_of, None, None, None, columns, columns]
    specs += [pl.BlockSpec((256, model_width), lambda step: (step, 0)), rows_of]
    operands = (tokens, part, far, gain, gate, up, down, cotangent)
    return call(ffn_kernel, steps, outs, [None, None, tiles, tiles, tiles, None, None], [], operands, specs, 0 * 10**9)


def middle_kernel(
    hidden_ref,
    part_ref,
    far_ref,
    cotangent_ref,
    gain_ref,
    gated_ref,
    square_a_ref,
    square_b_ref,
    gated_gain_ref,
    mixer_out_ref,
    attn_out_ref,
    grad_hidden_ref,
    grad_branch_ref,
    grad_rows_ref,
    grad_attended_ref,
    dot_ref,
    gain_sum_ref,
):
    hidden = hidden_ref[...]
    inv = inverse_rms(hidden)
    unit = hidden * inv
    grad_normed = part_ref[...] + far_ref[...]
    gain_sum_ref[0:1, :] = jnp.sum(grad_normed * unit, axis=0, keepdims=True)
    grad_unit = grad_normed * gain_ref[...]
    inner = jnp.mean(grad_unit * unit, axis=-1, keepdims=True)
    grad_hidden = cotangent_ref[...].astype(jnp.float32) + inv * (grad_unit - unit * inner)
    grad_hidden_ref[...] = grad_hidden
    grad_branch = grad_hidden.astype(jnp.bfloat16)
    grad_branch_ref[...] = grad_branch
    grad_rows = dot_nt(grad_branch, mixer_out_ref[...])
    grad_rows_ref[...] = grad_rows
    grad_attended_ref[...] = dot_nt(grad_branch, attn_out_ref[...]).astype(jnp.bfloat16)
    total = jnp.sum(grad_rows * gated_gain_ref[...] * gated_ref[...], axis=-1, keepdims=True)
    for i in range(hidden.shape[0] // LEN):
        at = block(i)
        inv_gated = lax.rsqrt((square_a_ref[:, at] + square_b_ref[:, at]) / DSSM + norm_eps)
        dot_ref[0:1, at] = jnp.broadcast_to(total[at], (LEN, LEN)).T[0:1] * inv_gated


def middle(chunks, hidden, part, far, cotangent, gain, gated, square_a, square_b, gated_gain, mixer_out, attn_out):
    rows, model_width = part.shape
    at = chunks[0] // len(chunks)
    width, inner = mixer_out.shape[0], attn_out.shape[0]
    outs = [
        f32(rows, model_width),
        b16(rows, model_width),
        f32(rows, width),
        b16(rows, inner),
        f32(1, rows),
        f32(8, model_width),
    ]
    rows_of = pl.BlockSpec((rows, model_width), lambda step: (at, 0), pipeline_mode=pl.Buffered(1))
    specs = [None, None, None, rows_of] + [None] * 7
    operands = (hidden, part, far, cotangent, gain, gated, square_a, square_b, gated_gain, mixer_out, attn_out)
    return call(middle_kernel, 1, outs, [None] * 6, [], operands, specs, 0 * 10**9)


def core_call(kernel, steps, core, out_shape, out_spec, scratch, operands, specs, flops):
    return pl.pallas_call(
        kernel,
        grid_spec=pltpu.PrefetchScalarGridSpec(
            num_scalar_prefetch=1, grid=(steps,), in_specs=specs, out_specs=out_spec, scratch_shapes=scratch
        ),
        out_shape=out_shape,
        compiler_params=pltpu.CompilerParams(vmem_limit_bytes=VMEM_BYTES),
        cost_estimate=pl.CostEstimate(flops=flops, bytes_accessed=0, transcendentals=0),
    )(core, *operands)


def clip_tile(rows, columns, first, last):
    return pl.BlockSpec((rows, columns), lambda step, core_ref: (0, jnp.clip(step - first, 0, last - first - 1)))


def ffn_weights_kernel(add, core_ref, *refs):
    refs = list(refs)
    normed_a, normed_b, act_a, act_b, gate_a, gate_b, up_a, up_b, cot_a, cot_b = refs[:10]
    far_ref = refs[10] if add else None
    out_ref, left_ref = refs[-2:]
    step = pl.program_id(0)
    third = pl.num_programs(0) // 3
    half = normed_a.shape[0]

    def turn(first, second):
        left_ref[:, :half] = first[...].T
        left_ref[:, half:] = second[...].T

    @pl.when(step == 0)
    def _():
        turn(normed_a, normed_b)

    @pl.when(step == 2 * third)
    def _():
        turn(act_a, act_b)

    def product(first, second):
        result = dot_nn(left_ref[:, :half], first[...]) + dot_nn(left_ref[:, half:], second[...])
        out_ref[...] = result + far_ref[...] if add else result

    @pl.when(step < third)
    def _():
        product(gate_a, gate_b)

    @pl.when((step >= third) & (step < 2 * third))
    def _():
        product(up_a, up_b)

    @pl.when(step >= 2 * third)
    def _():
        product(cot_a, cot_b)


def ffn_weights(core, far, normed_a, normed_b, act_a, act_b, gate_a, gate_b, up_a, up_b, cotangent):
    half, columns = normed_a.shape
    kept = columns // 2
    tile_width = 512
    third = columns // tile_width
    left = pl.BlockSpec((half, kept), lambda step, core_ref: (0, core_ref[0]), pipeline_mode=pl.Buffered(1))
    specs = [left] * 4 + [clip_tile(half, tile_width, 0, third)] * 2
    specs += [clip_tile(half, tile_width, third, 2 * third)] * 2

    def cot_rows(at):
        return pl.BlockSpec(
            (half, tile_width), lambda step, core_ref: (at, jnp.clip(step - 2 * third, 0, third - 1))
        )

    specs += [cot_rows(0), cot_rows(1)]
    out = pl.BlockSpec((kept, tile_width), lambda step, core_ref: (0, step))
    operands = [normed_a, normed_b, act_a, act_b, gate_a, gate_b, up_a, up_b, cotangent, cotangent]
    if far is not None:
        operands.append(far)
        specs.append(out)
    return core_call(
        functools.partial(ffn_weights_kernel, far is not None),
        3 * third,
        core,
        f32(kept, 3 * columns),
        out,
        [pltpu.VMEM((kept, 2 * half), jnp.bfloat16)],
        operands,
        specs,
        0 * 10**9,
    )


def mixer_weights_kernel(add, core_ref, *refs):
    refs = list(refs)
    (
        rows_a,
        rows_b,
        edge_a,
        edge_b,
        att_a,
        att_b,
        normed_ref,
        branch_a,
        branch_b,
        gate_a,
        gate_b,
        conv_ref,
        query_a,
        query_b,
        state_ref,
        pair_ref,
        step_ref,
    ) = refs[:17]
    far_ref = refs[17] if add else None
    table_ref = refs[18] if add else None
    out_ref, left_ref = refs[-2:]
    step = pl.program_id(0)
    half = rows_a.shape[0]
    kept = left_ref.shape[0]
    middle_row = kept // 2

    @pl.when((step == 0) & (core_ref[0] == 0))
    def _():
        left_ref[:, :half] = rows_a[...].T
        left_ref[:, half:] = rows_b[...].T

    @pl.when((step == 0) & (core_ref[0] == 1))
    def _():
        left_ref[:middle_row, :half] = edge_a[...].T
        left_ref[:middle_row, half:] = edge_b[...].T
        left_ref[middle_row:, :half] = att_a[...].T
        left_ref[middle_row:, half:] = att_b[...].T

    @pl.when(step == 4)
    def _():
        left_ref[...] = normed_ref[...].T

    def write(value, lanes=slice(None)):
        out_ref[:, lanes] = value + far_ref[:, lanes] if add else value

    def two(first, second):
        write(dot_nn(left_ref[:, :half], first[...]) + dot_nn(left_ref[:, half:], second[...]))

    @pl.when(step < 4)
    def _():
        two(branch_a, branch_b)

    @pl.when((step >= 4) & (step < 7))
    def _():
        two(gate_a, gate_b)

    @pl.when((step >= 7) & (step < 10))
    def _():
        write(dot_nn(left_ref[...], conv_ref[...]))

    @pl.when(step == 10)
    def _():
        two(query_a, query_b)

    @pl.when(step == 11)
    def _():
        write(dot_nn(left_ref[...], state_ref[...]))

    @pl.when(step == 12)
    def _():
        write(dot_nn(left_ref[...], pair_ref[...]), slice(0, LEN))
        steps = dot_nn(left_ref[...], step_ref[...])
        write(steps + table_ref[...] if add else steps, slice(LEN, 2 * LEN))


def mixer_weights(core, far, table, rows_a, rows_b, att_a, att_b, normed, branch_a, branch_b, gate_a, gate_b, conv, query_a, query_b, state, pair, step):
    half, width = rows_a.shape
    rows, model_width = normed.shape
    kept = model_width // 2
    tile_width = 256
    steps = 13

    def fixed(shape, column=0):
        return pl.BlockSpec(shape, lambda step, core_ref: (0, column), pipeline_mode=pl.Buffered(1))

    specs = [fixed((half, kept))] * 2
    specs += [fixed((half, width - kept), kept // (width - kept))] * 2
    specs += [fixed(att_a.shape)] * 2
    specs += [pl.BlockSpec((rows, kept), lambda step, core_ref: (0, core_ref[0]), pipeline_mode=pl.Buffered(1))]
    specs += [clip_tile(half, tile_width, 0, 4)] * 2
    specs += [clip_tile(half, tile_width, 4, 7)] * 2
    specs += [clip_tile(rows, tile_width, 7, 10)]
    specs += [fixed(query_a.shape)] * 2 + [fixed(state.shape), fixed(pair.shape), fixed(step.shape)]
    operands = [rows_a, rows_b, rows_a, rows_b, att_a, att_b, normed, branch_a, branch_b, gate_a, gate_b, conv]
    operands += [query_a, query_b, state, pair, step]
    out = pl.BlockSpec((kept, tile_width), lambda step, core_ref: (0, step))
    if far is not None:
        operands += [far, table]
        specs += [out, fixed(table.shape)]
    return core_call(
        functools.partial(mixer_weights_kernel, far is not None),
        steps,
        core,
        f32(kept, steps * tile_width),
        out,
        [pltpu.VMEM((kept, rows), jnp.bfloat16)],
        operands,
        specs,
        30 * 10**9,
    )


def normed_back_kernel(
    gate_a,
    gate_b,
    conv_ref,
    query_a,
    query_b,
    state_ref,
    pair_ref,
    step_ref,
    wide_ref,
    small_ref,
    tokens_ref,
    inv_ref,
    out_ref,
    sum_ref,
):
    half, width = gate_a.shape
    query_width = query_a.shape[1]
    gate_w, conv_w = wide_ref[:, :width], wide_ref[:, width:]
    state_w = small_ref[:, : 2 * LEN]
    query_w = small_ref[:, 2 * LEN : 2 * LEN + query_width]
    pair_w = small_ref[:, 2 * LEN + query_width : 3 * LEN + query_width]
    step_w = small_ref[:, 3 * LEN + query_width :]
    total = jnp.zeros((1, out_ref.shape[1]), jnp.float32)
    for k, (gate, query) in enumerate(((gate_a, query_a), (gate_b, query_b))):
        at = slice(k * half, (k + 1) * half)
        grad = dot_nt(gate[...], gate_w) + dot_nt(conv_ref[at, :], conv_w) + dot_nt(query[...], query_w)
        grad = grad + dot_nt(state_ref[at, :], state_w) + dot_nt(pair_ref[at, :], pair_w) + dot_nt(step_ref[at, :], step_w)
        out_ref[at, :] = grad
        unit = tokens_ref[at, :].astype(jnp.float32) * inv_ref[at, :]
        total = total + jnp.sum(grad * unit, axis=0, keepdims=True)
    sum_ref[0:1, :] = total


def normed_back(gate_a, gate_b, conv, query_a, query_b, state, pair, step, wide_proj, small_proj, tokens, inv):
    rows, model_width = tokens.shape
    tile_width = 256
    operands = (gate_a, gate_b, conv, query_a, query_b, state, pair, step, wide_proj, small_proj, tokens, inv)

    def weights(count):
        return pl.BlockSpec((tile_width, count), lambda step: (step, 0))

    columns = pl.BlockSpec((rows, tile_width), lambda step: (0, step))
    specs = [None] * 8 + [weights(wide_proj.shape[1]), weights(small_proj.shape[1]), columns, None]
    out_specs = [columns, pl.BlockSpec((8, tile_width), lambda step: (0, step))]
    outs = [f32(rows, model_width), f32(8, model_width)]
    return call(normed_back_kernel, model_width // tile_width, outs, out_specs, [], operands, specs, 30 * 10**9)


def assemble_kernel(
    source, mixer_out_ref, attn_out_ref, mixer_proj_ref, query_ref, pair_ref, state_ref, step_ref
):
    width = mixer_proj_ref.shape[2]
    model_width = mixer_out_ref.shape[1]
    split = width // LEN

    @pl.when(pl.program_id(0) < split)
    def _():
        mixer_out_ref[...] = source[:, :model_width]

    @pl.when(pl.program_id(0) >= split)
    def _():
        attn_out_ref[...] = source[:, :model_width]

    start = model_width
    mixer_proj_ref[:, 0, :] = source[:, start : start + width]
    start += width
    mixer_proj_ref[:, 1, :] = source[:, start : start + width]
    start += width
    query_ref[...] = source[:, start : start + query_ref.shape[1]]
    start += query_ref.shape[1]
    state_ref[...] = source[:, start : start + 2 * LEN]
    start += 2 * LEN
    pair_ref[:, 0, :] = source[:, start : start + LEN]
    step_ref[...] = source[:, start + LEN :]


def assemble(values, width, query_width):
    rows, columns = values.shape
    split = width // LEN

    def plain(count):
        return pl.BlockSpec((LEN, count), lambda at: (at, 0))

    out_specs = [
        pl.BlockSpec((LEN, rows), lambda at: (jnp.minimum(at, split - 1), 0)),
        pl.BlockSpec((LEN, rows), lambda at: (jnp.maximum(at - split, 0), 0)),
        pl.BlockSpec((LEN, 2, width), lambda at: (at, 0, 0)),
        plain(query_width),
        pl.BlockSpec((LEN, 1, LEN), lambda at: (at, 0, 0)),
        plain(2 * LEN),
        plain(LEN),
    ]
    out_shape = [
        f32(width, rows),
        f32(rows - width, rows),
        f32(rows, 2, width),
        f32(rows, query_width),
        f32(rows, 1, LEN),
        f32(rows, 2 * LEN),
        f32(rows, LEN),
    ]
    return call(assemble_kernel, rows // LEN, out_shape, out_specs, [], (values,), [plain(columns)], 0)


LINKS = {
    "A": [(0, 1), (1, 0), (2, 3), (3, 2)],
    "B": [(1, 2), (2, 1), (3, 0), (0, 3)],
}
ORDERS = (
    (("x", "A"), ("x", "B"), ("y", "A"), ("y", "B")),
    (("x", "B"), ("y", "A"), ("y", "B"), ("x", "A")),
    (("y", "A"), ("y", "B"), ("x", "A"), ("x", "B")),
    (("y", "B"), ("x", "A"), ("x", "B"), ("y", "A")),
)
AXIS = {"y": 0, "x": 1}


def take(values, index, axis):
    return lax.dynamic_slice_in_dim(values, index, 1, axis)


def halves(values, name, link, again):
    place, axis = lax.axis_index(name), AXIS[name]
    if again:
        index = place // 2 if link == "B" else place % 2
        return take(values, index, axis), take(values, 1 - index, axis)
    if link == "B":
        side = place // 2
        kept = lax.dynamic_slice_in_dim(values, 2 * side, 2, axis)
        return kept, lax.dynamic_slice_in_dim(values, 2 - 2 * side, 2, axis)
    side = ((place + 1) // 2) % 2
    kept = jnp.concatenate([take(values, side, axis), take(values, 3 - side, axis)], axis)
    return kept, jnp.concatenate([take(values, 1 - side, axis), take(values, 2 + side, axis)], axis)


def reduce_rows(values):
    rows, columns = values.shape
    tiles = columns // LEN
    sizes = [LEN * (tiles // 4 + (1 if k < tiles % 4 else 0)) for k in range(4)]
    blocks = values.reshape(4, 4, rows // 16, columns)
    parts = [blocks[..., sum(sizes[:k]) : sum(sizes[: k + 1])] for k in range(4)]
    for step in range(4):
        kept, sent = [], []
        for k in range(4):
            name, link = ORDERS[k][step]
            again = name in [n for n, _ in ORDERS[k][:step]]
            stays, goes = halves(parts[k], name, link, again)
            kept.append(stays)
            sent.append(goes)
        sent = lax.optimization_barrier(tuple(sent))
        come = [lax.ppermute(sent[k], ORDERS[k][step][0], LINKS[ORDERS[k][step][1]]) for k in range(4)]
        come = lax.optimization_barrier(tuple(come))
        parts = [stays + more for stays, more in zip(kept, come)]
    return jnp.concatenate(parts, axis=-1).reshape(rows // 16, columns)


def rope_tables(rows):
    half_size = HEAD_DIM // 2
    inverse = np.float32(rope_base) ** (-(2.0 * np.arange(half_size, dtype=np.float32)) / HEAD_DIM)
    angles = np.arange(rows, dtype=np.float32)[:, None] * inverse.astype(np.float32)[None, :]
    cosine, sine = np.cos(angles), np.sin(angles)
    return (
        np.concatenate([cosine] * 4, axis=1).astype(np.float32),
        np.concatenate([-sine, sine, -sine, sine], axis=1).astype(np.float32),
    )


def norm_backward(grad_unit, unit_rows, inv_rms):
    return inv_rms * (grad_unit - unit_rows * jnp.mean(grad_unit * unit_rows, axis=-1, keepdims=True))


def dot32(left, right):
    return jnp.dot(left, right, preferred_element_type=jnp.float32)


def after(value, *others):
    return lax.optimization_barrier((value, *others))[0]


def swap(values, name):
    return lax.ppermute(values, name, PAIR)


def exchange(values, name):
    return values + swap(values, name)


def core_rows(values, index):
    half = values.shape[1] // 2
    return lax.dynamic_slice_in_dim(values, index * half, half, 1)


def on_device(
    layer_input,
    segments,
    input_gain,
    mixer_proj,
    state_proj,
    step_proj,
    step_bias,
    decay_log,
    skip_gain,
    conv_kernel,
    conv_bias,
    state_kernel,
    state_bias,
    gated_gain,
    mixer_out,
    query_proj,
    key_value_weight,
    attn_out,
    ffn_gain,
    ffn_gate,
    ffn_up,
    ffn_down,
    cotangent,
):
    segment = segments.reshape(-1)
    rows, model_width = layer_input.shape
    width = mixer_proj.shape[2]
    heads = step_proj.shape[1]
    state_size = state_proj.shape[1] // 2
    query_width = query_proj.shape[1]
    pair_width = key_value_weight.shape[2]
    place = lax.axis_index("core")
    zh = lax.axis_index("zh")
    core = place.astype(jnp.int32).reshape(1)
    far_core = 1 - core
    cosine, sine = rope_tables(rows)
    select = np.arange(HEAD_ROWS)[:, None] == np.arange(width)[None, :] // HEAD_DIM
    select = jnp.asarray(select.astype(np.float32)).astype(jnp.bfloat16)
    seg_col, seg_row = segment[:, None], segment[None, :]
    keep = [jnp.ones((rows,), jnp.float32)]
    for lag in (1, 2, 3):
        previous = jnp.concatenate([jnp.full((lag,), -1, jnp.int32), segment[:-lag]])
        keep.append((previous == segment).astype(jnp.float32))
    keep = jnp.pad(jnp.stack(keep, axis=1), ((0, 8), (0, 4)))
    pad_heads = ((0, 0), (0, LEN - heads))
    rate_row = jnp.pad(-jnp.exp(decay_log)[None, :], pad_heads)
    step_bias_row = jnp.pad(step_bias[None, :], pad_heads)
    skip_row = jnp.repeat(skip_gain, HEAD_DIM)[None, :]
    gain_row = gated_gain[None, :]
    wide_proj = mixer_proj.reshape(model_width, 2 * width)
    small_proj = jnp.concatenate(
        [
            state_proj,
            query_proj,
            key_value_weight.reshape(model_width, pair_width),
            jnp.pad(step_proj, pad_heads),
        ],
        axis=1,
    )

    tokens = layer_input.astype(jnp.float32)
    inv_rms_in = lax.rsqrt(jnp.mean(tokens * tokens, axis=-1, keepdims=True) + norm_eps)
    unit_in = tokens * inv_rms_in
    normed_input = (unit_in * input_gain).astype(jnp.bfloat16)
    small_in = dot32(normed_input, small_proj)
    wide_in = dot32(normed_input, wide_proj)
    x, xb, slope, state, state_slope, cum, lag, cum_row, lag_row, step_row, sig_row, queries, pairs = scan_prep(
        width,
        wide_in,
        small_in,
        cosine,
        sine,
        keep,
        conv_kernel,
        conv_bias[None, :],
        state_kernel,
        state_bias[None, :],
        step_bias_row,
        rate_row,
    )

    blocks = rows // LEN
    late = tuple(range(blocks // 2, blocks))
    early = tuple(range(blocks // 2))
    half = {}
    for chunks in (late, early):
        h = {"span": slice(chunks[0] * LEN, (chunks[-1] + 1) * LEN)}
        h["y"], h["gated"], h["square"] = scan_forward(
            chunks, heads, wide_in, x, xb, state, cum, lag_row, seg_col, seg_row, skip_row
        )
        half[chunks] = h
    squares = jnp.concatenate([half[early]["square"], half[late]["square"]], axis=1)
    squares_far = swap(squares, "tensor")
    ready = squares
    for chunks in (late, early):
        h = half[chunks]
        h["attended"], h["lse"] = attention_forward(chunks, after(queries, ready), pairs, seg_col, seg_row)
        if chunks == late:
            squares_far = after(squares_far, h["lse"])
            squares_all = squares + squares_far
        h["square"], h["square_far"] = squares[:, h["span"]], squares_far[:, h["span"]]
        h["inv_gated"] = lax.rsqrt(squares_all[:, h["span"]].reshape(-1, 1) / DSSM + norm_eps)
        h["mixer_rows"] = (h["gated"] * h["inv_gated"] * gated_gain).astype(jnp.bfloat16)
        h["part"] = dot32(h["mixer_rows"], mixer_out) + dot32(h["attended"], attn_out)
        h["branch_far"] = swap(h["part"], "tensor")
        ready = h["part"]

    a, b = half[early], half[late]
    gain_ffn = ffn_gain[None, :]
    names = ("hidden", "normed", "activated", "grad_gate_rows", "grad_up_rows", "back", "down")
    for chunks in (late, early):
        h = half[chunks]
        far = h["branch_far"] if chunks == late else after(h["branch_far"], b["back"])
        operands = (layer_input, h["part"], far, gain_ffn, ffn_gate, ffn_up, ffn_down, cotangent)
        h.update(zip(names, ffn(chunks, *operands)))
        h["back_far"] = swap(h["back"], "tensor")

    sides = (after(a["normed"], b["back_far"]), b["normed"], a["activated"], b["activated"])
    sides += (a["grad_gate_rows"], b["grad_gate_rows"], a["grad_up_rows"], b["grad_up_rows"], cotangent)
    first = swap(ffn_weights(far_core, None, *sides), "core")

    for chunks in (late, early):
        h = half[chunks]
        far = h["back_far"] if chunks == late else after(h["back_far"], first)
        h["grad_hidden"], h["grad_branch"], h["grad_rows"], grad_attended, h["dot"], h["gain_sum"] = middle(
            chunks,
            h["hidden"],
            h["back"],
            far,
            cotangent,
            gain_ffn,
            h["gated"],
            h["square"],
            h["square_far"],
            gain_row,
            mixer_out,
            attn_out,
        )
        operands = (queries, pairs, grad_attended, h["lse"], seg_col, seg_row, cosine, sine)
        if chunks == late:
            h["grad_queries"], grad_keys, grad_values = attention_backward(chunks, False, *operands)
            first = ffn_weights(core, after(first, grad_keys), *sides)
            first_sum = lax.psum_scatter(first, ("y", "x"), scatter_dimension=0, tiled=True)
        else:
            dots = jnp.concatenate([a["dot"], b["dot"]], axis=1)
            dots_far = swap(dots, "tensor")
            h["grad_queries"], grad_pairs = attention_backward(chunks, True, *operands, grad_keys, grad_values)
    dots_far = after(dots_far, grad_pairs)
    for chunks in (late, early):
        h = half[chunks]
        h["grad_gate"], h["gy"], h["dx"], h["p"], h["grad_in"], h["grad_out"], h["sums"] = scan_backward(
            chunks,
            heads,
            h["grad_rows"],
            h["gated"],
            h["square"],
            h["square_far"],
            h["dot"],
            dots_far[:, h["span"]],
            gain_row,
            wide_in,
            h["y"],
            x,
            xb,
            state,
            lag,
            cum_row,
            skip_row,
            seg_col,
            seg_row,
            select,
        )
    pieces = [b["down"][:LEN], b["down"][LEN:], a["down"][:LEN], a["down"][LEN:]]
    pieces_far = [swap(after(piece, dots_far), "tensor") for piece in pieces]
    down = jnp.concatenate([a["down"], b["down"]], axis=0)
    ends = []
    for name in ("gy", "dx", "p", "grad_in", "grad_out"):
        ends += [a[name], b[name]]
    grad_conv, grad_state, grad_step, conv_sum, state_sum, step_sum = scan_end(
        heads,
        *ends,
        after(xb, pieces_far[0]),
        slope,
        state_slope,
        wide_in,
        small_in,
        step_row,
        sig_row,
        rate_row,
        skip_row,
        keep,
        seg_col,
        seg_row,
        select,
        conv_kernel,
        state_kernel,
    )

    grads = (a["grad_gate"], b["grad_gate"], grad_conv, a["grad_queries"], b["grad_queries"])
    grads += (grad_state, grad_pairs, grad_step)
    sides = (a["mixer_rows"], b["mixer_rows"], a["attended"], b["attended"], after(normed_input, pieces_far[1], pieces_far[2]))
    sides += (a["grad_branch"], b["grad_branch"], *grads)
    second_far = swap(mixer_weights(far_core, None, None, *sides), "core")
    partial_normed, input_gain_sum = normed_back(*grads, wide_proj, small_proj, layer_input, inv_rms_in)

    sums = a["sums"] + b["sums"]
    over_tensor = [input_gain_sum[0], state_sum[:4], state_sum[4]]
    alone = [
        step_sum[:heads, 0],
        step_sum[HEAD_ROWS : HEAD_ROWS + heads, 0],
        jnp.sum(sums[0].reshape(heads, HEAD_DIM), axis=1),
        conv_sum[:4],
        conv_sum[4],
        sums[1],
        a["gain_sum"][0] + b["gain_sum"][0],
    ]

    def packed(values):
        flat = jnp.concatenate([v.reshape(-1) for v in values])
        count = -(-flat.shape[0] // model_width)
        return jnp.pad(flat, (0, count * model_width - flat.shape[0])).reshape(count, model_width)

    def unpacked(table, values):
        flat, result, start = table.T.reshape(-1), [], 0
        for v in values:
            result.append(flat[start : start + v.size].reshape(v.shape))
            start += v.size
        return result

    tables = [packed(over_tensor), packed(alone)]
    shared_end = heads + tables[0].shape[0]
    table = jnp.concatenate(tables, axis=0)
    table_end = heads + table.shape[0]
    table = (core_rows(table, place) + swap(core_rows(table, 1 - place), "core")).T
    table = jnp.pad(table, ((0, 0), (heads, LEN - table_end)))
    second = mixer_weights(core, after(second_far, pieces_far[3]), table, *sides)
    first_own = exchange(after(first_sum, second), "zh")
    first_all = lax.all_gather(first_own, ("core", "y", "x"), axis=0, tiled=True)
    at_state = model_width + 2 * width + query_width
    at_step = at_state + 2 * state_size + pair_width
    second = reduce_rows(second)
    both = second[:, at_state:]
    lane = np.arange(both.shape[1])
    in_table = lane - 2 * state_size - pair_width
    is_shared = (lane < 2 * state_size) | ((in_table >= heads) & (in_table < shared_end))
    diagonal = [(0, 3), (3, 0), (1, 2), (2, 1)]
    more = swap(both, "tensor") + lax.ppermute(both, ("zh", "tensor"), diagonal)
    second = exchange(second, "zh")
    summed = second[:, at_state:] + jnp.where(is_shared[None, :], more, 0.0)
    second = jnp.concatenate([second[:, :at_state], summed], axis=1)
    second = after(second, first_all)
    normed_far = swap(after(partial_normed, second), "tensor")
    second = lax.all_gather(second, ("core", "y", "x"), axis=0, tiled=True)
    grad_mixer_out, grad_attn_out, grad_mixer_proj, grad_query_proj, grad_keyval, grad_state_proj, step_block = assemble(
        second, width, query_width
    )

    def whole(name):
        return jnp.concatenate([a[name], b[name]], axis=0)

    grad_hidden = whole("grad_hidden")
    grad_normed = partial_normed + normed_far
    input_grad = grad_hidden + norm_backward(grad_normed * input_gain, unit_in, inv_rms_in)
    down_far = jnp.concatenate([pieces_far[2], pieces_far[3], pieces_far[0], pieces_far[1]], axis=0)
    layer_output = (whole("hidden") + (down + down_far)).astype(jnp.bfloat16)

    small_shared = unpacked(step_block[:, heads:shared_end], over_tensor)
    small_alone = unpacked(step_block[:, shared_end:table_end], alone)
    return (
        layer_output,
        input_grad,
        small_shared[0],
        grad_mixer_proj,
        grad_state_proj,
        step_block[:, :heads],
        small_alone[0],
        small_alone[1],
        small_alone[2],
        small_alone[3],
        small_alone[4],
        small_shared[1],
        small_shared[2],
        small_alone[5],
        grad_mixer_out,
        grad_query_proj,
        grad_keyval,
        grad_attn_out,
        small_alone[6],
        first_all[:, :model_width],
        first_all[:, model_width : 2 * model_width],
        first_all[:, 2 * model_width :],
    )


def solution(mesh):
    dp, whole_spec, columns = P(DP, None), P(), P(None, "tensor")
    per_channel, middle = P("tensor"), P(None, "tensor", None)
    last, by_rows = P(None, None, "tensor"), P("tensor", None)
    weights = (
        whole_spec,
        last,
        whole_spec,
        columns,
        per_channel,
        per_channel,
        per_channel,
        columns,
        per_channel,
        whole_spec,
        whole_spec,
        per_channel,
        by_rows,
        columns,
        middle,
        by_rows,
        whole_spec,
        columns,
        columns,
        by_rows,
    )
    mesh = jax.sharding.Mesh(mesh.devices.reshape(4, 2, 4, 2, 2), (*DP, "tensor"))
    return jax.shard_map(
        on_device, mesh=mesh, in_specs=(dp, dp, *weights, dp), out_specs=(dp, dp, *weights), check_vma=False
    )
```

```python
import functools

import jax
import jax.numpy as jnp
import numpy as np
from jax import lax
from jax.experimental import pallas as pl
from jax.experimental.pallas import tpu as pltpu
from jax.sharding import PartitionSpec as P

HEAD_DIM = 64
DSSM = 1536
DP = ("y", "zh", "x", "core")
PAIR = [(0, 1), (1, 0)]
LOG2E = 1.4426950408889634
hidden_bias = -1e30
norm_eps = 1e-05
rope_base = 10000.0
LEN = 128


def dot_nn(left, right):
    return lax.dot_general(
        left, right, (((1,), (0,)), ((), ())), preferred_element_type=jnp.float32
    )


def dot_nt(left, right):
    return lax.dot_general(
        left, right, (((1,), (1,)), ((), ())), preferred_element_type=jnp.float32
    )


def dot_tn(left, right):
    return lax.dot_general(
        left, right, (((0,), (0,)), ((), ())), preferred_element_type=jnp.float32
    )


def two_terms(v):
    high = v.astype(jnp.bfloat16)
    return high, (v - high.astype(jnp.float32)).astype(jnp.bfloat16)


def three_dots(dot, left, right):
    left_high, left_low = two_terms(left)
    right_high, right_low = two_terms(right)
    return dot(left_high, right_high) + dot(left_high, right_low) + dot(left_low, right_high)


def sigmoid(v):
    return 1.0 / (1.0 + jnp.exp(-v))


def block(index):
    return slice(index * LEN, (index + 1) * LEN)


def lane_iota(rows=LEN):
    return lax.broadcasted_iota(jnp.int32, (rows, LEN), 1)


def mask_ts(seg_col, seg_row, i, j):
    same = seg_col[block(i), :] == seg_row[:, block(j)]
    if i != j:
        return same
    down = lax.broadcasted_iota(jnp.int32, (LEN, LEN), 0)
    return same & (down >= lane_iota())


def mask_st(seg_col, seg_row, j, i):
    same = seg_col[block(j), :] == seg_row[:, block(i)]
    if i != j:
        return same
    down = lax.broadcasted_iota(jnp.int32, (LEN, LEN), 0)
    return same & (down <= lane_iota())


def conv_rows(pad_ref, keep_ref, kernel, bias, start, lanes):
    summed = bias + kernel[3:4] * pad_ref[8 + start : 8 + start + LEN, lanes]
    for lag in (1, 2, 3):
        moved = pad_ref[8 + start - lag : 8 + start - lag + LEN, lanes]
        summed = summed + kernel[3 - lag : 4 - lag] * (moved * keep_ref[lag - 1, start : start + LEN, :])
    return summed


def widen(keep_ref, wide_ref):
    rows = keep_ref.shape[0]
    for lag in (1, 2, 3):
        wide_ref[lag - 1, :, :] = jnp.broadcast_to(keep_ref[:, lag : lag + 1], (rows, LEN))


def prep_kernel(
    conv_ref,
    small_ref,
    cos_ref,
    sin_ref,
    keep_ref,
    conv_kernel_ref,
    conv_bias_ref,
    state_kernel_ref,
    state_bias_ref,
    step_bias_ref,
    rate_ref,
    x_ref,
    xb_ref,
    slope_ref,
    state_ref,
    state_slope_ref,
    cum_ref,
    lag_ref,
    cum_row_ref,
    lag_row_ref,
    step_row_ref,
    sig_row_ref,
    q_ref,
    kv_ref,
    pad_ref,
    wide_ref,
):
    rows = conv_ref.shape[0]
    blocks = rows // LEN

    @pl.when(pl.program_id(0) == 0)
    def _():
        pad_ref[0:8, :] = jnp.zeros((8, LEN), jnp.float32)
        widen(keep_ref, wide_ref)
        for c in range(2):
            pad_ref[8 : rows + 8, :] = small_ref[:, block(c)]
            for i in range(blocks):
                pre = conv_rows(
                    pad_ref, wide_ref, state_kernel_ref[:, block(c)], state_bias_ref[:, block(c)], i * LEN, slice(0, LEN)
                )
                sig = sigmoid(pre)
                state_ref[block(i), block(c)] = pre * sig
                state_slope_ref[block(i), block(c)] = sig * (1.0 + pre * (1.0 - sig))

    @pl.when(pl.program_id(0) == 1)
    def _():
        down = lax.broadcasted_iota(jnp.int32, (LEN, LEN), 0)
        lower = jnp.where(down >= lane_iota(), 1.0, 0.0).astype(jnp.bfloat16)
        left_half = lane_iota() < HEAD_DIM
        carry = jnp.zeros((1, LEN), jnp.float32)
        heads = cum_row_ref.shape[0]
        for i in range(blocks):
            argument = small_ref[block(i), block(5)] + step_bias_ref[...]
            tail = jnp.exp(-jnp.abs(argument))
            grown = jnp.where(tail < 1e-3, tail - 0.5 * tail * tail, jnp.log(1.0 + tail))
            step = jnp.maximum(argument, 0.0) + grown
            scaled = step * rate_ref[...] * LOG2E
            first, rest = two_terms(scaled)
            last = scaled - first.astype(jnp.float32) - rest.astype(jnp.float32)
            cum = dot_nn(lower, first) + dot_nn(lower, rest) + dot_nn(lower, last.astype(jnp.bfloat16)) + carry
            carry = cum[LEN - 1 : LEN, :]
            lag = cum - jnp.log(step) * LOG2E
            cum_ref[block(i), :] = cum
            lag_ref[block(i), :] = lag
            cum_t, lag_t = cum.T, lag.T
            step_row_ref[:, block(i)] = step.T[:heads]
            sig_row_ref[:, block(i)] = sigmoid(argument).T[:heads]
            for h in range(heads):
                cum_row_ref[h, :, block(i)] = cum_t[h : h + 1]
                lag_row_ref[h, :, block(i)] = lag_t[h : h + 1]
            cosine, sine = cos_ref[block(i), :], sin_ref[block(i), :]
            kv = small_ref[block(i), block(4)]
            kv_ref[block(i), :] = jnp.where(left_half, rotate_tile(kv, cosine, sine), kv).astype(jnp.bfloat16)
            for p in range(q_ref.shape[1] // LEN):
                q_ref[block(i), block(p)] = rotate_tile(small_ref[block(i), block(2 + p)], cosine, sine).astype(
                    jnp.bfloat16
                )

    for sub in range(GROUP):
        lanes = block(sub)
        pad_ref[8 : rows + 8, :] = conv_ref[:, lanes]
        for i in range(blocks):
            pre = conv_rows(pad_ref, wide_ref, conv_kernel_ref[:, lanes], conv_bias_ref[:, lanes], i * LEN, slice(0, LEN))
            sig = sigmoid(pre)
            x = pre * sig
            x_ref[block(i), lanes] = x
            xb_ref[block(i), lanes] = x.astype(jnp.bfloat16)
            slope_ref[block(i), lanes] = sig * (1.0 + pre * (1.0 - sig))


def rotate_tile(v, cosine, sine):
    first = lax.rem(lane_iota(v.shape[0]), HEAD_DIM) < HEAD_DIM // 2
    swapped = jnp.where(first, pltpu.roll(v, LEN - HEAD_DIM // 2, 1), pltpu.roll(v, HEAD_DIM // 2, 1))
    return v * cosine + swapped * sine


def scan_kernel(
    chunks,
    heads,
    gate_ref,
    x_ref,
    xb_ref,
    state_ref,
    cum_ref,
    lag_row_ref,
    seg_col_ref,
    seg_row_ref,
    skip_ref,
    y_ref,
    gated_ref,
    row_ref,
    wide_ref,
    cross_ref,
    bias_ref,
    mix_ref,
    square_ref,
):
    step = pl.program_id(0)
    first = chunks[0]
    pairs = [(i, j) for i in chunks for j in range(max(0, i - 2), i + 1)]
    left_half = lane_iota() < HEAD_DIM

    @pl.when(step == 0)
    def _():
        for h in range(heads):
            for i in chunks:
                wide_ref[h, block(i - first), :] = jnp.broadcast_to(cum_ref[block(i), h : h + 1], (LEN, LEN))
        for i in chunks:
            low = max(0, i - 2)
            cross = three_dots(dot_nt, state_ref[block(i), LEN:], state_ref[low * LEN : (i + 1) * LEN, :LEN])
            for n, (i2, j) in enumerate(pairs):
                if i2 == i:
                    cross_ref[n] = cross[:, block(j - low)]
                    allowed = mask_ts(seg_col_ref, seg_row_ref, i, j)
                    bias_ref[n] = jnp.where(allowed, 0.0, hidden_bias)
        square_ref[...] = jnp.zeros(square_ref.shape, jnp.float32)

    tiles = (gate_ref, x_ref, xb_ref, skip_ref, y_ref, gated_ref)

    def head_pair(hp, gate_ref, x_ref, xb_ref, skip_ref, y_ref, gated_ref):
        for i in chunks:
            at = block(i - first)
            low = max(0, i - 2)
            for n, (i2, j) in enumerate(pairs):
                if i2 != i:
                    continue
                for e in range(2):
                    spread = wide_ref[2 * hp + e, at, :] - lag_row_ref[2 * hp + e, :, block(j)]
                    decay = jnp.exp2(spread + bias_ref[n])
                    mix_ref[i - first, block(e), block(j - low)] = (decay * cross_ref[n]).astype(jnp.bfloat16)
            both = dot_nn(mix_ref[i - first, :, : (i + 1 - low) * LEN], xb_ref[low * LEN : (i + 1) * LEN, :])
            y = jnp.where(left_half, both[:LEN], both[LEN:])
            y_ref[at, :] = y
            gate = gate_ref[at, :]
            gated = (y + skip_ref[...] * x_ref[at, :]) * (gate * sigmoid(gate))
            gated_ref[at, :] = gated
            square_ref[at, :] = square_ref[at, :] + gated * gated

    for sub in range(GROUP):
        head_pair(GROUP * step + sub, *[t.at[:, block(sub)] for t in tiles])

    @pl.when(step == pl.num_programs(0) - 1)
    def _():
        for i in chunks:
            at = block(i - first)
            total = jnp.sum(square_ref[at, :], axis=1, keepdims=True)
            row_ref[0:1, at] = jnp.broadcast_to(total, (LEN, LEN)).T[0:1]


def attention_kernel(chunks, q_ref, kv_ref, seg_col_ref, seg_row_ref, out_ref, lse_ref):
    scale = HEAD_DIM ** (-0.5) * LOG2E
    first = chunks[0]
    left_half = lane_iota() < HEAD_DIM
    zero = jnp.zeros((LEN, LEN), jnp.bfloat16)
    lse_ref[...] = jnp.zeros(lse_ref.shape, jnp.float32)
    for i in chunks:
        at = block(i - first)
        low = max(0, i - 2) * LEN
        span = (i + 1) * LEN - low
        allowed = jnp.concatenate([mask_ts(seg_col_ref, seg_row_ref, i, j) for j in range(low // LEN, i + 1)], axis=1)
        keys = kv_ref[low : low + span, :]
        turned = pltpu.roll(keys.astype(jnp.float32), HEAD_DIM, 1).astype(jnp.bfloat16)
        for p in range(q_ref.shape[1] // LEN):
            queries = q_ref[block(i), block(p)]
            result = []
            for e in range(2):
                masked = jnp.where(left_half == (e == 0), queries, zero)
                scores = dot_nt(masked, keys if e == 0 else turned) * scale
                scores = jnp.where(allowed, scores, hidden_bias)
                top = jnp.max(scores, axis=1, keepdims=True)
                weights = jnp.exp2(scores - top)
                total = jnp.sum(weights, axis=1, keepdims=True)
                probs = (weights * (1.0 / total)).astype(jnp.bfloat16)
                result.append(dot_nn(probs, turned if e == 0 else keys))
                lse = jnp.broadcast_to(top + jnp.log(total) * LOG2E, (LEN, LEN))
                lse_ref[2 * p + e : 2 * p + e + 1, at] = lse.T[0:1]
            out_ref[at, block(p)] = jnp.where(left_half, result[0], result[1]).astype(jnp.bfloat16)


def attention_back_kernel(chunks, final, *refs):
    q_ref, kv_ref, do_ref, lse_ref, seg_col_ref, seg_row_ref, cos_ref, sin_ref = refs[:8]
    if final:
        dk_in_ref, dv_in_ref, dq_ref, dkv_ref, dk_ref, dv_ref, turned_ref, key_t_ref = refs[8:]
    else:
        dq_ref, dk_ref, dv_ref, turned_ref, key_t_ref = refs[8:]
    scale = HEAD_DIM ** (-0.5)
    blocks = q_ref.shape[0] // LEN
    first = chunks[0]
    left_half = lane_iota() < HEAD_DIM
    zero = jnp.zeros((LEN, LEN), jnp.bfloat16)
    for i in range(chunks[-1] + 1):
        kv = kv_ref[block(i), :].astype(jnp.float32)
        turned_ref[block(i), :] = pltpu.roll(kv, HEAD_DIM, 1).astype(jnp.bfloat16)
        key_t_ref[:, block(i)] = kv.T[:HEAD_DIM].astype(jnp.bfloat16)
    if final:
        dk_ref[...] = dk_in_ref[...]
        dv_ref[...] = dv_in_ref[...]
    else:
        dk_ref[...] = jnp.zeros(dk_ref.shape, jnp.float32)
        dv_ref[...] = jnp.zeros(dv_ref.shape, jnp.float32)
    for i in chunks:
        at = block(i - first)
        low = max(0, i - 2) * LEN
        span = (i + 1) * LEN - low
        window = slice(low, low + span)
        allowed = jnp.concatenate([mask_st(seg_col_ref, seg_row_ref, j, i) for j in range(low // LEN, i + 1)], axis=0)
        keys, turned = kv_ref[window, :], turned_ref[window, :]
        for p in range(q_ref.shape[1] // LEN):
            queries, douts = q_ref[block(i), block(p)], do_ref[at, block(p)]
            back = []
            for e in range(2):
                side = left_half == (e == 0)
                q_half = jnp.where(side, queries, zero)
                do_half = jnp.where(side, douts, zero)
                h = 2 * p + e
                scores = dot_nt(keys if e == 0 else turned, q_half) * (scale * LOG2E)
                probs = jnp.exp2(jnp.where(allowed, scores, hidden_bias) - lse_ref[h : h + 1, at])
                dprobs = dot_nt(turned if e == 0 else keys, do_half)
                inner = jnp.sum(probs * dprobs, axis=0, keepdims=True)
                dscores = (probs * (dprobs - inner)).astype(jnp.bfloat16)
                dv_ref[window, :] = dv_ref[window, :] + dot_nn(probs.astype(jnp.bfloat16), do_half)
                dk_ref[window, :] = dk_ref[window, :] + dot_nn(dscores, q_half)
                back.append(dot_nn(key_t_ref[:, window], dscores))
            dq = jnp.concatenate(back, axis=0).T * scale
            dq_ref[at, block(p)] = rotate_tile(dq, cos_ref[block(i), :], -sin_ref[block(i), :]).astype(jnp.bfloat16)
    if not final:
        return
    for i in range(blocks):
        dk = dk_ref[block(i), :]
        dk = (dk + pltpu.roll(dk, HEAD_DIM, 1)) * scale
        dk = rotate_tile(dk, cos_ref[block(i), :], -sin_ref[block(i), :])
        dv = dv_ref[block(i), :]
        dv = dv + pltpu.roll(dv, HEAD_DIM, 1)
        dkv_ref[block(i), :] = jnp.where(left_half, dk, dv).astype(jnp.bfloat16)


def scan_back_kernel(
    chunks,
    heads,
    gmr_ref,
    gated_ref,
    square_a_ref,
    square_b_ref,
    dot_a_ref,
    dot_b_ref,
    gain_ref,
    gate_ref,
    y_ref,
    x_ref,
    xb_ref,
    state_ref,
    lag_ref,
    cum_row_ref,
    skip_ref,
    seg_col_ref,
    seg_row_ref,
    select_ref,
    dgate_ref,
    gy_ref,
    dx_ref,
    p_ref,
    grad_in_ref,
    grad_out_ref,
    sums_ref,
    gyb_ref,
    wide_ref,
    cross_ref,
    bias_ref,
    dcross_ref,
    inv_wide_ref,
    dot_wide_ref,
    inner_ref,
    mix_ref,
):
    step = pl.program_id(0)
    first = chunks[0]
    sources = chunks[-1] + 1
    left_half = lane_iota() < HEAD_DIM
    zero = jnp.zeros((LEN, LEN), jnp.bfloat16)
    spans = [(j, max(j, first), min(j + 3, sources)) for j in range(sources)]
    pairs = [(j, i) for j, start, stop in spans for i in range(start, stop)]

    @pl.when(step == 0)
    def _():
        for i in chunks:
            at = block(i - first)
            square = (square_a_ref[:, at] + square_b_ref[:, at]) / DSSM
            inv = lax.rsqrt(square + norm_eps)
            inv_wide_ref[at, :] = jnp.broadcast_to(inv, (LEN, LEN)).T
            dot = (dot_a_ref[:, at] + dot_b_ref[:, at]) / DSSM
            dot_wide_ref[at, :] = jnp.broadcast_to(dot, (LEN, LEN)).T
        p_ref[...] = jnp.zeros(p_ref.shape, jnp.float32)
        for h in range(heads):
            wide_ref[h] = jnp.broadcast_to(lag_ref[: sources * LEN, h : h + 1], (sources * LEN, LEN))
        for j, start, stop in spans:
            cross = three_dots(dot_nt, state_ref[block(j), :LEN], state_ref[start * LEN : stop * LEN, LEN:])
            for n, (j2, i) in enumerate(pairs):
                if j2 == j:
                    cross_ref[n] = cross[:, block(i - start)]
                    allowed = mask_st(seg_col_ref, seg_row_ref, j, i)
                    bias_ref[n] = jnp.where(allowed, 0.0, hidden_bias)
                    dcross_ref[n] = jnp.zeros((LEN, LEN), jnp.float32)

    tiles = (
        gmr_ref, gated_ref, gain_ref, gate_ref, y_ref, x_ref, xb_ref, skip_ref, dgate_ref, gy_ref, dx_ref, sums_ref
    )

    def head_pair(
        hp,
        select,
        gmr_ref,
        gated_ref,
        gain_ref,
        gate_ref,
        y_ref,
        x_ref,
        xb_ref,
        skip_ref,
        dgate_ref,
        gy_ref,
        dx_ref,
        sums_ref,
    ):
        skip = skip_ref[...]
        gain = gain_ref[...]
        skip_sum = jnp.zeros((1, LEN), jnp.float32)
        gain_sum = jnp.zeros((1, LEN), jnp.float32)
        for i in chunks:
            at = block(i - first)
            inv = inv_wide_ref[at, :]
            unit = gated_ref[at, :] * inv
            rows_grad = gmr_ref[at, :]
            grad = inv * (rows_grad * gain - unit * dot_wide_ref[at, :])
            gate = gate_ref[at, :]
            sig = sigmoid(gate)
            y = y_ref[at, :]
            x = x_ref[at, :]
            gy = grad * (gate * sig)
            dgate_ref[at, :] = (grad * (y + skip * x) * (sig * (1.0 + gate * (1.0 - sig)))).astype(jnp.bfloat16)
            gyb = gy.astype(jnp.bfloat16)
            gy_ref[at, :] = gy
            gyb_ref[at, :] = gyb
            high, rest = two_terms(gyb.astype(jnp.float32) * y)
            p_ref[:, at] = p_ref[:, at] + dot_nt(select, high) + dot_nt(select, rest)
            skip_sum = skip_sum + jnp.sum(gy * x, axis=0, keepdims=True)
            gain_sum = gain_sum + jnp.sum(rows_grad * unit, axis=0, keepdims=True)
        sums_ref[0:1, :] = skip_sum
        sums_ref[1:2, :] = gain_sum

        for j, start, stop in spans:
            x_pair = xb_ref[block(j), :]
            x_both = jnp.concatenate([jnp.where(left_half, x_pair, zero), jnp.where(left_half, zero, x_pair)], axis=0)
            wide = (stop - start) * LEN
            gy_rows = gyb_ref[(start - first) * LEN : (stop - first) * LEN, :]
            inner_ref[:, :wide] = dot_nt(x_both, gy_rows)
            for n, (j2, i) in enumerate(pairs):
                if j2 != j:
                    continue
                grown = dcross_ref[n]
                for e in range(2):
                    spread = cum_row_ref[2 * hp + e, :, block(i)] - wide_ref[2 * hp + e, block(j), :]
                    decay = jnp.exp2(spread + bias_ref[n])
                    grown = grown + inner_ref[block(e), block(i - start)] * decay
                    mix_ref[block(e), block(i - start)] = (decay * cross_ref[n]).astype(jnp.bfloat16)
                dcross_ref[n] = grown
            both = dot_nn(mix_ref[:, :wide], gy_rows)
            dx_ref[block(j), :] = jnp.where(left_half, both[:LEN], both[LEN:])

    for sub in range(GROUP):
        head_pair(GROUP * step + sub, select_ref[:, block(sub)], *[t.at[:, block(sub)] for t in tiles])

    @pl.when(step == pl.num_programs(0) - 1)
    def _():
        grad_out = {i: jnp.zeros((LEN, LEN), jnp.float32) for i in chunks}
        for j in range(sources):
            grad_in = jnp.zeros((LEN, LEN), jnp.float32)
            for n, (j2, i) in enumerate(pairs):
                if j2 != j:
                    continue
                high, rest = two_terms(dcross_ref[n])
                out_high, out_rest = two_terms(state_ref[block(i), LEN:])
                in_high, in_rest = two_terms(state_ref[block(j), :LEN])
                grad_in = grad_in + dot_nn(high, out_high) + dot_nn(high, out_rest) + dot_nn(rest, out_high)
                grad_out[i] = grad_out[i] + dot_tn(high, in_high) + dot_tn(high, in_rest) + dot_tn(rest, in_high)
            grad_in_ref[block(j), :] = grad_in
        for i in chunks:
            grad_out_ref[block(i - first), :] = grad_out[i]


def conv_back(grad_ref, value_ref, keep_ref, kernel_ref, out_ref, sum_ref, lanes, blocks):
    taps = kernel_ref[:, lanes]
    totals = [jnp.zeros((1, LEN), jnp.float32) for _ in range(5)]
    for i in range(blocks):
        here = grad_ref[i * LEN : (i + 1) * LEN, :]
        grad = taps[3:4] * here
        totals[4] = totals[4] + jnp.sum(here, axis=0, keepdims=True)
        totals[3] = totals[3] + jnp.sum(here * value_ref[8 + i * LEN : 8 + (i + 1) * LEN, :], axis=0, keepdims=True)
        for lag in (1, 2, 3):
            ahead = grad_ref[i * LEN + lag : (i + 1) * LEN + lag, :]
            grad = grad + taps[3 - lag : 4 - lag] * (ahead * keep_ref[lag - 1, i * LEN + lag : (i + 1) * LEN + lag, :])
            moved = value_ref[8 + i * LEN - lag : 8 + (i + 1) * LEN - lag, :]
            masked = here * keep_ref[lag - 1, i * LEN : (i + 1) * LEN, :]
            totals[3 - lag] = totals[3 - lag] + jnp.sum(masked * moved, axis=0, keepdims=True)
        out_ref[block(i), lanes] = grad.astype(jnp.bfloat16)
    for tap in range(5):
        sum_ref[tap : tap + 1, lanes] = totals[tap]


def scan_end_kernel(
    heads,
    gy_a_ref,
    gy_b_ref,
    dx_a_ref,
    dx_b_ref,
    p_a_ref,
    p_b_ref,
    in_a_ref,
    in_b_ref,
    out_a_ref,
    out_b_ref,
    xb_ref,
    slope_ref,
    state_slope_ref,
    conv_ref,
    small_ref,
    step_row_ref,
    sig_row_ref,
    rate_ref,
    skip_ref,
    keep_ref,
    seg_col_ref,
    seg_row_ref,
    select_ref,
    conv_kernel_ref,
    state_kernel_ref,
    dconv_ref,
    dstate_ref,
    dstep_ref,
    conv_sum_ref,
    state_sum_ref,
    step_sum_ref,
    grad_pad_ref,
    value_pad_ref,
    wide_ref,
    q_ref,
    flow_ref,
):
    step = pl.program_id(0)
    rows = conv_ref.shape[0]
    blocks = rows // LEN
    half = rows // 2
    count = flow_ref.shape[0]

    @pl.when(step == 0)
    def _():
        value_pad_ref[0:8, :] = jnp.zeros((8, LEN), jnp.float32)
        grad_pad_ref[rows : rows + 8, :] = jnp.zeros((8, LEN), jnp.float32)
        widen(keep_ref, wide_ref)
        q_ref[...] = jnp.zeros(q_ref.shape, jnp.float32)
        for c in range(2):
            if c == 0:
                grad_pad_ref[0:half, :] = (in_a_ref[...] + in_b_ref[0:half, :]) * state_slope_ref[0:half, block(c)]
                grad_pad_ref[half:rows, :] = in_b_ref[half:rows, :] * state_slope_ref[half:rows, block(c)]
            else:
                grad_pad_ref[0:half, :] = out_a_ref[...] * state_slope_ref[0:half, block(c)]
                grad_pad_ref[half:rows, :] = out_b_ref[...] * state_slope_ref[half:rows, block(c)]
            value_pad_ref[8 : rows + 8, :] = small_ref[:, block(c)]
            conv_back(grad_pad_ref, value_pad_ref, wide_ref, state_kernel_ref, dstate_ref, state_sum_ref, block(c), blocks)

    tiles = (
        gy_a_ref, gy_b_ref, dx_a_ref, dx_b_ref, xb_ref, slope_ref, conv_ref, skip_ref, conv_kernel_ref, dconv_ref, conv_sum_ref
    )

    def head_pair(
        select,
        gy_a_ref,
        gy_b_ref,
        dx_a_ref,
        dx_b_ref,
        xb_ref,
        slope_ref,
        conv_ref,
        skip_ref,
        conv_kernel_ref,
        dconv_ref,
        conv_sum_ref,
    ):
        for j in range(blocks):
            dx = dx_b_ref[block(j), :]
            if j < blocks // 2:
                dx = dx + dx_a_ref[block(j), :]
                gy = gy_a_ref[block(j), :]
            else:
                gy = gy_b_ref[block(j - blocks // 2), :]
            high, rest = two_terms(dx * xb_ref[block(j), :].astype(jnp.float32))
            q_ref[:, block(j)] = q_ref[:, block(j)] + dot_nt(select, high) + dot_nt(select, rest)
            grad_pad_ref[block(j), :] = (dx + gy * skip_ref[...]) * slope_ref[block(j), :]
        value_pad_ref[8 : rows + 8, :] = conv_ref[...]
        conv_back(
            grad_pad_ref, value_pad_ref, wide_ref, conv_kernel_ref, dconv_ref, conv_sum_ref, slice(0, LEN), blocks
        )

    for sub in range(GROUP):
        head_pair(select_ref[:, block(sub)], *[t.at[:, block(sub)] for t in tiles])

    @pl.when(step == pl.num_programs(0) - 1)
    def _():
        q = q_ref[...]
        flow_ref[:, 0:half] = p_a_ref[...] - q[:, 0:half]
        flow_ref[:, half:rows] = p_b_ref[...] - q[:, half:rows]
        rate = jnp.broadcast_to(rate_ref[...], (LEN, LEN)).T[:count]
        bias_total = jnp.zeros((count, LEN), jnp.float32)
        decay_total = jnp.zeros((count, LEN), jnp.float32)
        for j in range(blocks):
            log_grad = jnp.zeros((count, LEN), jnp.float32)
            for i in range(j, min(j + 3, blocks)):
                chosen = jnp.where(mask_st(seg_col_ref, seg_row_ref, j, i), 1.0, 0.0).astype(jnp.bfloat16)
                high, rest = two_terms(flow_ref[:, block(i)])
                log_grad = log_grad + dot_nt(high, chosen) + dot_nt(rest, chosen)
            step = step_row_ref[:, block(j)]
            grad_step = jnp.where(step > 1e-30, q[:, block(j)] / step, 0.0) + log_grad * rate
            grad_arg = grad_step * sig_row_ref[:, block(j)]
            bias_total = bias_total + grad_arg
            decay_total = decay_total + log_grad * step
            tall = jnp.concatenate([grad_arg, jnp.zeros((LEN - count, LEN), jnp.float32)], axis=0)
            dstep_ref[block(j), :] = tall.T.astype(jnp.bfloat16)
        step_sum_ref[0:count, :] = jnp.broadcast_to(jnp.sum(bias_total, axis=1, keepdims=True), (count, LEN))
        step_sum_ref[count : 2 * count, :] = jnp.broadcast_to(
            jnp.sum(decay_total * rate, axis=1, keepdims=True), (count, LEN)
        )


def whole_block(shape):
    return pl.BlockSpec(shape, lambda step: (0,) * len(shape), pipeline_mode=pl.Buffered(1))


def tile(rows, row_block=0, first=0):
    return pl.BlockSpec((rows, GROUP * LEN), lambda step: (row_block, first + step))


def call(kernel, steps, out_shape, out_specs, scratch, operands, specs, flops):
    return pl.pallas_call(
        kernel,
        grid=(steps,),
        out_shape=out_shape,
        in_specs=[s or whole_block(o.shape) for o, s in zip(operands, specs)],
        out_specs=[s or whole_block(o.shape) for o, s in zip(out_shape, out_specs)],
        scratch_shapes=scratch,
        compiler_params=pltpu.CompilerParams(vmem_limit_bytes=VMEM_BYTES),
        cost_estimate=pl.CostEstimate(flops=flops, bytes_accessed=0, transcendentals=0),
    )(*operands)


def f32(*shape):
    return jax.ShapeDtypeStruct(shape, jnp.float32)


def b16(*shape):
    return jax.ShapeDtypeStruct(shape, jnp.bfloat16)


HEAD_ROWS = 16
GROUP = 3
VMEM_BYTES = 60 * 1024 * 1024


def scan_prep(width, wide_in, small, cosine, sine, keep, conv_kernel, conv_bias, *rest):
    rows = wide_in.shape[0]
    steps = width // LEN // GROUP
    outs = [
        f32(rows, width),
        b16(rows, width),
        f32(rows, width),
        f32(rows, 2 * LEN),
        f32(rows, 2 * LEN),
        f32(rows, LEN),
        f32(rows, LEN),
        f32(HEAD_ROWS, 1, rows),
        f32(HEAD_ROWS, 1, rows),
        f32(HEAD_ROWS, rows),
        f32(HEAD_ROWS, rows),
        b16(rows, 2 * LEN),
        b16(rows, LEN),
    ]
    scratch = [pltpu.VMEM((rows + 8, LEN), jnp.float32), pltpu.VMEM((3, rows + 8, LEN), jnp.float32)]
    operands = (wide_in, small, cosine, sine, keep, conv_kernel, conv_bias, *rest)
    specs = [tile(rows, 0, steps), None, None, None, None, tile(4), tile(1)] + [None] * len(rest)
    return call(prep_kernel, steps, outs, [tile(rows)] * 3 + [None] * 10, scratch, operands, specs, 0 * 10**9)


def scan_forward(chunks, heads, wide_in, x, xb, *rest):
    width = x.shape[1]
    rows = LEN * len(chunks)
    at = chunks[0] // len(chunks)
    count = sum(min(i, 2) + 1 for i in chunks)
    outs = [f32(rows, width), f32(rows, width), f32(1, rows)]
    scratch = [
        pltpu.VMEM((heads, rows, LEN), jnp.float32),
        pltpu.VMEM((count, LEN, LEN), jnp.float32),
        pltpu.VMEM((count, LEN, LEN), jnp.float32),
        pltpu.VMEM((len(chunks), 2 * LEN, 3 * LEN), jnp.bfloat16),
        pltpu.VMEM((rows, LEN), jnp.float32),
    ]
    specs = [tile(rows, at), tile(rows, at), tile((chunks[-1] + 1) * LEN)] + [None] * (len(rest) - 1) + [tile(1)]
    kernel = functools.partial(scan_kernel, chunks, heads)
    operands = (wide_in, x, xb, *rest)
    return call(kernel, heads // 2 // GROUP, outs, [tile(rows), tile(rows), None], scratch, operands, specs, 0 * 10**9)


def attention_forward(chunks, q, kv, seg_col, seg_row):
    rows = LEN * len(chunks)
    outs = [b16(rows, q.shape[1]), f32(8, rows)]
    kernel = functools.partial(attention_kernel, chunks)
    return call(kernel, 1, outs, [None] * 2, [], (q, kv, seg_col, seg_row), [None] * 4, 0 * 10**9)


def attention_backward(chunks, final, *operands):
    q = operands[0]
    rows = q.shape[0]
    partial = [f32(rows, LEN), f32(rows, LEN)]
    sums = [pltpu.VMEM((rows, LEN), jnp.float32)] * 2
    outs = [b16(LEN * len(chunks), q.shape[1])] + ([b16(rows, LEN)] if final else partial)
    scratch = (sums if final else []) + [
        pltpu.VMEM((rows, LEN), jnp.bfloat16),
        pltpu.VMEM((HEAD_DIM, rows), jnp.bfloat16),
    ]
    kernel = functools.partial(attention_back_kernel, chunks, final)
    return call(kernel, 1, outs, [None] * len(outs), scratch, operands, [None] * len(operands), 0 * 10**9)


def scan_backward(chunks, heads, *operands):
    rows, width = operands[0].shape
    at = chunks[0] // len(chunks)
    sources = (chunks[-1] + 1) * LEN
    count = sum(min(i, 2) + 1 for i in chunks)
    outs = [
        b16(rows, width),
        f32(rows, width),
        f32(sources, width),
        f32(HEAD_ROWS, rows),
        f32(sources, LEN),
        f32(rows, LEN),
        f32(8, width),
    ]
    scratch = [
        pltpu.VMEM((rows, LEN), jnp.bfloat16),
        pltpu.VMEM((heads, sources, LEN), jnp.float32),
        pltpu.VMEM((count, LEN, LEN), jnp.float32),
        pltpu.VMEM((count, LEN, LEN), jnp.float32),
        pltpu.VMEM((count, LEN, LEN), jnp.float32),
        pltpu.VMEM((rows, LEN), jnp.float32),
        pltpu.VMEM((rows, LEN), jnp.float32),
        pltpu.VMEM((2 * LEN, 3 * LEN), jnp.float32),
        pltpu.VMEM((2 * LEN, 3 * LEN), jnp.bfloat16),
    ]
    specs = [tile(rows), tile(rows), None, None, None, None, tile(1), tile(rows, at), tile(rows), tile(rows, at), tile(sources)]
    specs += [None, None, None, tile(1), None, None, tile(HEAD_ROWS)]
    out_specs = [tile(rows), tile(rows), tile(sources), None, None, None, tile(8)]
    kernel = functools.partial(scan_back_kernel, chunks, heads)
    return call(kernel, heads // 2 // GROUP, outs, out_specs, scratch, operands, specs, 30 * 10**9)


def scan_end(heads, *operands):
    rows, width = 2 * operands[0].shape[0], operands[0].shape[1]
    steps = heads // 2 // GROUP
    outs = [
        b16(rows, width),
        b16(rows, 2 * LEN),
        b16(rows, LEN),
        f32(8, width),
        f32(8, 2 * LEN),
        f32(2 * HEAD_ROWS, LEN),
    ]
    scratch = [
        pltpu.VMEM((rows + 8, LEN), jnp.float32),
        pltpu.VMEM((rows + 8, LEN), jnp.float32),
        pltpu.VMEM((3, rows + 8, LEN), jnp.float32),
        pltpu.VMEM((HEAD_ROWS, rows), jnp.float32),
        pltpu.VMEM((HEAD_ROWS, rows), jnp.float32),
    ]
    half = rows // 2
    specs = [tile(half), tile(half), tile(half), tile(rows)] + [None] * 6 + [tile(rows), tile(rows), None]
    specs += [tile(rows, 0, steps)] + [None] * 4 + [tile(1), None, None, None, tile(HEAD_ROWS), tile(4), None]
    out_specs = [tile(rows), None, None, tile(8), None, None]
    kernel = functools.partial(scan_end_kernel, heads)
    return call(kernel, steps, outs, out_specs, scratch, operands, specs, 30 * 10**9)


def inverse_rms(rows):
    return lax.rsqrt(jnp.mean(rows * rows, axis=-1, keepdims=True) + norm_eps)


def ffn_kernel(
    tokens_ref,
    part_ref,
    far_ref,
    gain_ref,
    gate_ref,
    up_ref,
    down_ref,
    cotangent_ref,
    hidden_ref,
    normed_ref,
    activated_ref,
    grad_gate_ref,
    grad_up_ref,
    back_ref,
    out_ref,
):
    @pl.when(pl.program_id(0) == 0)
    def _():
        hidden = tokens_ref[...].astype(jnp.float32) + (part_ref[...] + far_ref[...])
        hidden_ref[...] = hidden
        normed_ref[...] = (hidden * inverse_rms(hidden) * gain_ref[...]).astype(jnp.bfloat16)
        back_ref[...] = jnp.zeros(back_ref.shape, jnp.float32)
        out_ref[...] = jnp.zeros(out_ref.shape, jnp.float32)

    normed = normed_ref[...]
    gate = dot_nn(normed, gate_ref[...])
    up = dot_nn(normed, up_ref[...])
    sig = sigmoid(gate)
    act = gate * sig
    activated = (act * up).astype(jnp.bfloat16)
    activated_ref[...] = activated
    grad = dot_nt(cotangent_ref[...], down_ref[...])
    grad_gate = (grad * up * (sig * (1.0 + gate * (1.0 - sig)))).astype(jnp.bfloat16)
    grad_up = (grad * act).astype(jnp.bfloat16)
    grad_gate_ref[...] = grad_gate
    grad_up_ref[...] = grad_up
    back_ref[...] = back_ref[...] + (dot_nt(grad_gate, gate_ref[...]) + dot_nt(grad_up, up_ref[...]))
    out_ref[...] = out_ref[...] + dot_nn(activated, down_ref[...])


def ffn(chunks, tokens, part, far, gain, gate, up, down, cotangent):
    rows, model_width = part.shape
    at = chunks[0] // len(chunks)
    hidden_width = gate.shape[1]
    steps = hidden_width // 256
    outs = [f32(rows, model_width), b16(rows, model_width)] + [b16(rows, hidden_width)] * 3
    outs += [f32(rows, model_width)] * 2
    rows_of = pl.BlockSpec((rows, model_width), lambda step: (at, 0), pipeline_mode=pl.Buffered(1))
    columns = pl.BlockSpec((model_width, 256), lambda step: (0, step))
    tiles = pl.BlockSpec((rows, 256), lambda step: (0, step))
    specs = [rows_of, None, None, None, columns, columns]
    specs += [pl.BlockSpec((256, model_width), lambda step: (step, 0)), rows_of]
    operands = (tokens, part, far, gain, gate, up, down, cotangent)
    return call(ffn_kernel, steps, outs, [None, None, tiles, tiles, tiles, None, None], [], operands, specs, 0 * 10**9)


def middle_kernel(
    hidden_ref,
    part_ref,
    far_ref,
    cotangent_ref,
    gain_ref,
    gated_ref,
    square_a_ref,
    square_b_ref,
    gated_gain_ref,
    mixer_out_ref,
    attn_out_ref,
    grad_hidden_ref,
    grad_branch_ref,
    grad_rows_ref,
    grad_attended_ref,
    dot_ref,
    gain_sum_ref,
):
    hidden = hidden_ref[...]
    inv = inverse_rms(hidden)
    unit = hidden * inv
    grad_normed = part_ref[...] + far_ref[...]
    gain_sum_ref[0:1, :] = jnp.sum(grad_normed * unit, axis=0, keepdims=True)
    grad_unit = grad_normed * gain_ref[...]
    inner = jnp.mean(grad_unit * unit, axis=-1, keepdims=True)
    grad_hidden = cotangent_ref[...].astype(jnp.float32) + inv * (grad_unit - unit * inner)
    grad_hidden_ref[...] = grad_hidden
    grad_branch = grad_hidden.astype(jnp.bfloat16)
    grad_branch_ref[...] = grad_branch
    grad_rows = dot_nt(grad_branch, mixer_out_ref[...])
    grad_rows_ref[...] = grad_rows
    grad_attended_ref[...] = dot_nt(grad_branch, attn_out_ref[...]).astype(jnp.bfloat16)
    total = jnp.sum(grad_rows * gated_gain_ref[...] * gated_ref[...], axis=-1, keepdims=True)
    for i in range(hidden.shape[0] // LEN):
        at = block(i)
        inv_gated = lax.rsqrt((square_a_ref[:, at] + square_b_ref[:, at]) / DSSM + norm_eps)
        dot_ref[0:1, at] = jnp.broadcast_to(total[at], (LEN, LEN)).T[0:1] * inv_gated


def middle(chunks, hidden, part, far, cotangent, gain, gated, square_a, square_b, gated_gain, mixer_out, attn_out):
    rows, model_width = part.shape
    at = chunks[0] // len(chunks)
    width, inner = mixer_out.shape[0], attn_out.shape[0]
    outs = [
        f32(rows, model_width),
        b16(rows, model_width),
        f32(rows, width),
        b16(rows, inner),
        f32(1, rows),
        f32(8, model_width),
    ]
    rows_of = pl.BlockSpec((rows, model_width), lambda step: (at, 0), pipeline_mode=pl.Buffered(1))
    specs = [None, None, None, rows_of] + [None] * 7
    operands = (hidden, part, far, cotangent, gain, gated, square_a, square_b, gated_gain, mixer_out, attn_out)
    return call(middle_kernel, 1, outs, [None] * 6, [], operands, specs, 0 * 10**9)


def core_call(kernel, steps, core, out_shape, out_spec, scratch, operands, specs, flops, aliases=None):
    return pl.pallas_call(
        kernel,
        grid_spec=pltpu.PrefetchScalarGridSpec(
            num_scalar_prefetch=1, grid=(steps,), in_specs=specs, out_specs=out_spec, scratch_shapes=scratch
        ),
        out_shape=out_shape,
        compiler_params=pltpu.CompilerParams(vmem_limit_bytes=VMEM_BYTES),
        cost_estimate=pl.CostEstimate(flops=flops, bytes_accessed=0, transcendentals=0),
        input_output_aliases=aliases or {},
    )(core, *operands)


def clip_tile(rows, columns, first, last):
    return pl.BlockSpec((rows, columns), lambda step, core_ref: (0, jnp.clip(step - first, 0, last - first - 1)))


def ffn_weights_kernel(add, core_ref, *refs):
    refs = list(refs)
    normed_a, normed_b, act_a, act_b, gate_a, gate_b, up_a, up_b, cot_a, cot_b = refs[:10]
    far_ref = refs[10] if add else None
    out_ref, left_ref = refs[-2:]
    step = pl.program_id(0)
    third = pl.num_programs(0) // 3
    half = normed_a.shape[0]

    def turn(first, second):
        left_ref[:, :half] = first[...].T
        left_ref[:, half:] = second[...].T

    @pl.when(step == 0)
    def _():
        turn(normed_a, normed_b)

    @pl.when(step == 2 * third)
    def _():
        turn(act_a, act_b)

    def product(first, second):
        result = dot_nn(left_ref[:, :half], first[...]) + dot_nn(left_ref[:, half:], second[...])
        out_ref[...] = result + far_ref[...] if add else result

    @pl.when(step < third)
    def _():
        product(gate_a, gate_b)

    @pl.when((step >= third) & (step < 2 * third))
    def _():
        product(up_a, up_b)

    @pl.when(step >= 2 * third)
    def _():
        product(cot_a, cot_b)


def ffn_weights(core, far, normed_a, normed_b, act_a, act_b, gate_a, gate_b, up_a, up_b, cotangent):
    half, columns = normed_a.shape
    kept = columns // 2
    tile_width = 512
    third = columns // tile_width
    left = pl.BlockSpec((half, kept), lambda step, core_ref: (0, core_ref[0]), pipeline_mode=pl.Buffered(1))
    specs = [left] * 4 + [clip_tile(half, tile_width, 0, third)] * 2
    specs += [clip_tile(half, tile_width, third, 2 * third)] * 2

    def cot_rows(at):
        return pl.BlockSpec(
            (half, tile_width), lambda step, core_ref: (at, jnp.clip(step - 2 * third, 0, third - 1))
        )

    specs += [cot_rows(0), cot_rows(1)]
    out = pl.BlockSpec((kept, tile_width), lambda step, core_ref: (0, step))
    operands = [normed_a, normed_b, act_a, act_b, gate_a, gate_b, up_a, up_b, cotangent, cotangent]
    if far is not None:
        operands.append(far)
        specs.append(out)
    return core_call(
        functools.partial(ffn_weights_kernel, far is not None),
        3 * third,
        core,
        f32(kept, (3 if far is None else 4) * columns),
        out,
        [pltpu.VMEM((kept, 2 * half), jnp.bfloat16)],
        operands,
        specs,
        0 * 10**9,
    )


def outer_weights_kernel(add, core_ref, *refs):
    refs = list(refs)
    rows_a, rows_b, edge_a, edge_b, att_a, att_b, branch_a, branch_b = refs[:8]
    out_ref, left_ref = refs[-2:]
    half = rows_a.shape[0]
    middle_row = left_ref.shape[0] // 2

    @pl.when((pl.program_id(0) == 0) & (core_ref[0] == 0))
    def _():
        left_ref[:, :half] = rows_a[...].T
        left_ref[:, half:] = rows_b[...].T

    @pl.when((pl.program_id(0) == 0) & (core_ref[0] == 1))
    def _():
        left_ref[:middle_row, :half] = edge_a[...].T
        left_ref[:middle_row, half:] = edge_b[...].T
        left_ref[middle_row:, :half] = att_a[...].T
        left_ref[middle_row:, half:] = att_b[...].T

    result = dot_nn(left_ref[:, :half], branch_a[...]) + dot_nn(left_ref[:, half:], branch_b[...])
    out_ref[...] = result + refs[8][...] if add else result


def outer_weights(core, far, buffer, rows_a, rows_b, att_a, att_b, branch_a, branch_b):
    half, width = rows_a.shape
    model_width = branch_a.shape[1]
    kept = model_width // 2
    tile_width = 512
    steps = model_width // tile_width

    def fixed(shape, column=0):
        return pl.BlockSpec(shape, lambda step, core_ref: (0, column), pipeline_mode=pl.Buffered(1))

    specs = [fixed((half, kept))] * 2
    specs += [fixed((half, width - kept), kept // (width - kept))] * 2
    specs += [fixed(att_a.shape)] * 2 + [clip_tile(half, tile_width, 0, steps)] * 2
    operands = [rows_a, rows_b, rows_a, rows_b, att_a, att_b, branch_a, branch_b]
    out = pl.BlockSpec((kept, tile_width), lambda step, core_ref: (0, step))
    columns, aliases = model_width, {}
    if far is not None:
        operands += [far, buffer]
        specs += [out, pl.BlockSpec(memory_space=pl.ANY)]
        columns = buffer.shape[1]
        first = columns // tile_width - steps
        out = pl.BlockSpec((kept, tile_width), lambda step, core_ref: (0, first + step))
        aliases = {len(operands): 0}
    return core_call(
        functools.partial(outer_weights_kernel, far is not None),
        steps,
        core,
        f32(kept, columns),
        out,
        [pltpu.VMEM((kept, 2 * half), jnp.bfloat16)],
        operands,
        specs,
        0,
        aliases,
    )


PARTS = ((0, 3), (3, 5), (5, 7), (7, 9))


def mixer_weights_kernel(add, core_ref, *refs):
    refs = list(refs)
    normed_ref, gate_a, gate_b, conv_ref, query_a, query_b, state_ref, pair_ref, step_ref = refs[:9]
    far_ref, table_ref = refs[9:11] if add else (None, None)
    outs = refs[11:19] if add else refs[9:10]
    left_ref, result_ref = refs[-2:]
    step = pl.program_id(0)
    half = gate_a.shape[0]

    @pl.when(step == 0)
    def _():
        left_ref[...] = normed_ref[...].T

    def two(first, second):
        result_ref[...] = dot_nn(left_ref[:, :half], first[...]) + dot_nn(left_ref[:, half:], second[...])

    @pl.when(step < 3)
    def _():
        two(gate_a, gate_b)

    @pl.when((step >= 3) & (step < 6))
    def _():
        result_ref[...] = dot_nn(left_ref[...], conv_ref[...])

    @pl.when(step == 6)
    def _():
        two(query_a, query_b)

    @pl.when(step == 7)
    def _():
        result_ref[...] = dot_nn(left_ref[...], state_ref[...])

    @pl.when(step == 8)
    def _():
        result_ref[:, :LEN] = dot_nn(left_ref[...], pair_ref[...])
        steps = dot_nn(left_ref[...], step_ref[...])
        result_ref[:, LEN:] = steps + table_ref[...] if add else steps

    if not add:
        outs[0][...] = result_ref[...]
        return
    result_ref[...] = result_ref[...] + far_ref[...]
    for k, (first, last) in enumerate(PARTS):

        @pl.when((step >= first) & (step < last))
        def _():
            for side in range(2):
                out_ref = outs[2 * k + side]
                for q in range(2):
                    index = core_ref[1 + 4 * k + 2 * side + q]
                    if k < 2:
                        for y in range(4):
                            start = pl.multiple_of((4 * y + index) * 32, 32)
                            out_ref[(2 * y + q) * 32 : (2 * y + q + 1) * 32, :] = result_ref[pl.ds(start, 32), :]
                    else:
                        start = pl.multiple_of(index * LEN, LEN)
                        out_ref[q * LEN : (q + 1) * LEN, :] = result_ref[pl.ds(start, LEN), :]


def mixer_weights(core, far, table, normed, gate_a, gate_b, conv, query_a, query_b, state, pair, step):
    half = gate_a.shape[0]
    rows, model_width = normed.shape
    kept = model_width // 2
    tile_width = 256
    steps = 9

    def fixed(shape, column=0):
        return pl.BlockSpec(shape, lambda step, core_ref: (0, column), pipeline_mode=pl.Buffered(1))

    specs = [pl.BlockSpec((rows, kept), lambda step, core_ref: (0, core_ref[0]), pipeline_mode=pl.Buffered(1))]
    specs += [clip_tile(half, tile_width, 0, 3)] * 2 + [clip_tile(rows, tile_width, 3, 6)]
    specs += [fixed(query_a.shape)] * 2 + [fixed(state.shape), fixed(pair.shape), fixed(step.shape)]
    operands = [normed, gate_a, gate_b, conv, query_a, query_b, state, pair, step]
    out = pl.BlockSpec((kept, tile_width), lambda step, core_ref: (0, step))
    shape = f32(kept, steps * tile_width)
    if far is not None:
        operands += [far, table]
        specs += [out, fixed(table.shape)]
        out, shape = [], []
        for first, last in PARTS:
            out += [clip_tile(kept // 2, tile_width, first, last)] * 2
            shape += [f32(kept // 2, (last - first) * tile_width)] * 2
    return core_call(
        functools.partial(mixer_weights_kernel, far is not None),
        steps,
        core,
        shape,
        out,
        [pltpu.VMEM((kept, rows), jnp.bfloat16), pltpu.VMEM((kept, tile_width), jnp.float32)],
        operands,
        specs,
        30 * 10**9,
    )


def normed_back_kernel(
    gate_a,
    gate_b,
    conv_ref,
    query_a,
    query_b,
    state_ref,
    pair_ref,
    step_ref,
    wide_ref,
    small_ref,
    tokens_ref,
    inv_ref,
    out_ref,
    sum_ref,
):
    half, width = gate_a.shape
    query_width = query_a.shape[1]
    gate_w, conv_w = wide_ref[:, :width], wide_ref[:, width:]
    state_w = small_ref[:, : 2 * LEN]
    query_w = small_ref[:, 2 * LEN : 2 * LEN + query_width]
    pair_w = small_ref[:, 2 * LEN + query_width : 3 * LEN + query_width]
    step_w = small_ref[:, 3 * LEN + query_width :]
    total = jnp.zeros((1, out_ref.shape[1]), jnp.float32)
    for k, (gate, query) in enumerate(((gate_a, query_a), (gate_b, query_b))):
        at = slice(k * half, (k + 1) * half)
        grad = dot_nt(gate[...], gate_w) + dot_nt(conv_ref[at, :], conv_w) + dot_nt(query[...], query_w)
        grad = grad + dot_nt(state_ref[at, :], state_w) + dot_nt(pair_ref[at, :], pair_w) + dot_nt(step_ref[at, :], step_w)
        out_ref[at, :] = grad
        unit = tokens_ref[at, :].astype(jnp.float32) * inv_ref[at, :]
        total = total + jnp.sum(grad * unit, axis=0, keepdims=True)
    sum_ref[0:1, :] = total


def normed_back(gate_a, gate_b, conv, query_a, query_b, state, pair, step, wide_proj, small_proj, tokens, inv):
    rows, model_width = tokens.shape
    tile_width = 256
    operands = (gate_a, gate_b, conv, query_a, query_b, state, pair, step, wide_proj, small_proj, tokens, inv)

    def weights(count):
        return pl.BlockSpec((tile_width, count), lambda step: (step, 0))

    columns = pl.BlockSpec((rows, tile_width), lambda step: (0, step))
    specs = [None] * 8 + [weights(wide_proj.shape[1]), weights(small_proj.shape[1]), columns, None]
    out_specs = [columns, pl.BlockSpec((8, tile_width), lambda step: (0, step))]
    outs = [f32(rows, model_width), f32(8, model_width)]
    return call(normed_back_kernel, model_width // tile_width, outs, out_specs, [], operands, specs, 30 * 10**9)


def assemble_kernel(source, mixer_proj_ref, query_ref, pair_ref, state_ref, step_ref):
    width = mixer_proj_ref.shape[2]
    start = 0
    mixer_proj_ref[:, 0, :] = source[:, start : start + width]
    start += width
    mixer_proj_ref[:, 1, :] = source[:, start : start + width]
    start += width
    query_ref[...] = source[:, start : start + query_ref.shape[1]]
    start += query_ref.shape[1]
    state_ref[...] = source[:, start : start + 2 * LEN]
    start += 2 * LEN
    pair_ref[:, 0, :] = source[:, start : start + LEN]
    step_ref[...] = source[:, start + LEN :]


def assemble(values, width, query_width):
    rows, columns = values.shape

    def plain(count):
        return pl.BlockSpec((LEN, count), lambda at: (at, 0))

    out_specs = [
        pl.BlockSpec((LEN, 2, width), lambda at: (at, 0, 0)),
        plain(query_width),
        pl.BlockSpec((LEN, 1, LEN), lambda at: (at, 0, 0)),
        plain(2 * LEN),
        plain(LEN),
    ]
    out_shape = [
        f32(rows, 2, width),
        f32(rows, query_width),
        f32(rows, 1, LEN),
        f32(rows, 2 * LEN),
        f32(rows, LEN),
    ]
    return call(assemble_kernel, rows // LEN, out_shape, out_specs, [], (values,), [plain(columns)], 0)


LINKS = {
    "A": [(0, 1), (1, 0), (2, 3), (3, 2)],
    "B": [(1, 2), (2, 1), (3, 0), (0, 3)],
}
ORDERS = (
    (("x", "A"), ("x", "B"), ("y", "A"), ("y", "B")),
    (("x", "B"), ("y", "A"), ("y", "B"), ("x", "A")),
    (("y", "A"), ("y", "B"), ("x", "A"), ("x", "B")),
    (("y", "B"), ("x", "A"), ("x", "B"), ("y", "A")),
)
AXIS = {"y": 0, "x": 1}


def take(values, index, axis):
    return lax.dynamic_slice_in_dim(values, index, 1, axis)


def halves(values, name, link, again):
    place, axis = lax.axis_index(name), AXIS[name]
    if again:
        index = place // 2 if link == "B" else place % 2
        return take(values, index, axis), take(values, 1 - index, axis)
    if link == "B":
        side = place // 2
        kept = lax.dynamic_slice_in_dim(values, 2 * side, 2, axis)
        return kept, lax.dynamic_slice_in_dim(values, 2 - 2 * side, 2, axis)
    side = ((place + 1) // 2) % 2
    kept = jnp.concatenate([take(values, side, axis), take(values, 3 - side, axis)], axis)
    return kept, jnp.concatenate([take(values, 1 - side, axis), take(values, 2 + side, axis)], axis)


def reduce_rows(pairs, steps):
    kept, sent, parts = [], [], pairs
    if steps[0] == 0:
        for k, (stays, goes) in enumerate(pairs):
            shape = (4, 2, 32, stays.shape[1]) if ORDERS[k][0][0] == "x" else (2, 4, 32, stays.shape[1])
            kept.append(stays.reshape(shape))
            sent.append(goes.reshape(shape))
    for step in steps:
        if step:
            kept, sent = [], []
            for k in range(4):
                name, link = ORDERS[k][step]
                again = name in [n for n, _ in ORDERS[k][:step]]
                stays, goes = halves(parts[k], name, link, again)
                kept.append(stays)
                sent.append(goes)
        sent = lax.optimization_barrier(tuple(sent))
        come = [lax.ppermute(sent[k], ORDERS[k][step][0], LINKS[ORDERS[k][step][1]]) for k in range(4)]
        come = lax.optimization_barrier(tuple(come))
        parts = [stays + more for stays, more in zip(kept, come)]
    return parts


def rope_tables(rows):
    half_size = HEAD_DIM // 2
    inverse = np.float32(rope_base) ** (-(2.0 * np.arange(half_size, dtype=np.float32)) / HEAD_DIM)
    angles = np.arange(rows, dtype=np.float32)[:, None] * inverse.astype(np.float32)[None, :]
    cosine, sine = np.cos(angles), np.sin(angles)
    return (
        np.concatenate([cosine] * 4, axis=1).astype(np.float32),
        np.concatenate([-sine, sine, -sine, sine], axis=1).astype(np.float32),
    )


def norm_backward(grad_unit, unit_rows, inv_rms):
    return inv_rms * (grad_unit - unit_rows * jnp.mean(grad_unit * unit_rows, axis=-1, keepdims=True))


def dot32(left, right):
    return jnp.dot(left, right, preferred_element_type=jnp.float32)


def after(value, *others):
    return lax.optimization_barrier((value, *others))[0]


def swap(values, name):
    return lax.ppermute(values, name, PAIR)


def exchange(values, name):
    return values + swap(values, name)


def core_rows(values, index):
    half = values.shape[1] // 2
    return lax.dynamic_slice_in_dim(values, index * half, half, 1)


def on_device(
    layer_input,
    segments,
    input_gain,
    mixer_proj,
    state_proj,
    step_proj,
    step_bias,
    decay_log,
    skip_gain,
    conv_kernel,
    conv_bias,
    state_kernel,
    state_bias,
    gated_gain,
    mixer_out,
    query_proj,
    key_value_weight,
    attn_out,
    ffn_gain,
    ffn_gate,
    ffn_up,
    ffn_down,
    cotangent,
):
    segment = segments.reshape(-1)
    rows, model_width = layer_input.shape
    width = mixer_proj.shape[2]
    heads = step_proj.shape[1]
    state_size = state_proj.shape[1] // 2
    query_width = query_proj.shape[1]
    pair_width = key_value_weight.shape[2]
    place = lax.axis_index("core")
    zh = lax.axis_index("zh")
    core = place.astype(jnp.int32).reshape(1)
    far_core = 1 - core
    cosine, sine = rope_tables(rows)
    select = np.arange(HEAD_ROWS)[:, None] == np.arange(width)[None, :] // HEAD_DIM
    select = jnp.asarray(select.astype(np.float32)).astype(jnp.bfloat16)
    seg_col, seg_row = segment[:, None], segment[None, :]
    keep = [jnp.ones((rows,), jnp.float32)]
    for lag in (1, 2, 3):
        previous = jnp.concatenate([jnp.full((lag,), -1, jnp.int32), segment[:-lag]])
        keep.append((previous == segment).astype(jnp.float32))
    keep = jnp.pad(jnp.stack(keep, axis=1), ((0, 8), (0, 4)))
    pad_heads = ((0, 0), (0, LEN - heads))
    rate_row = jnp.pad(-jnp.exp(decay_log)[None, :], pad_heads)
    step_bias_row = jnp.pad(step_bias[None, :], pad_heads)
    skip_row = jnp.repeat(skip_gain, HEAD_DIM)[None, :]
    gain_row = gated_gain[None, :]
    wide_proj = mixer_proj.reshape(model_width, 2 * width)
    small_proj = jnp.concatenate(
        [
            state_proj,
            query_proj,
            key_value_weight.reshape(model_width, pair_width),
            jnp.pad(step_proj, pad_heads),
        ],
        axis=1,
    )

    tokens = layer_input.astype(jnp.float32)
    inv_rms_in = lax.rsqrt(jnp.mean(tokens * tokens, axis=-1, keepdims=True) + norm_eps)
    unit_in = tokens * inv_rms_in
    normed_input = (unit_in * input_gain).astype(jnp.bfloat16)
    small_in = dot32(normed_input, small_proj)
    wide_in = dot32(normed_input, wide_proj)
    x, xb, slope, state, state_slope, cum, lag, cum_row, lag_row, step_row, sig_row, queries, pairs = scan_prep(
        width,
        wide_in,
        small_in,
        cosine,
        sine,
        keep,
        conv_kernel,
        conv_bias[None, :],
        state_kernel,
        state_bias[None, :],
        step_bias_row,
        rate_row,
    )

    blocks = rows // LEN
    late = tuple(range(blocks // 2, blocks))
    early = tuple(range(blocks // 2))
    half = {}
    for chunks in (late, early):
        h = {"span": slice(chunks[0] * LEN, (chunks[-1] + 1) * LEN)}
        h["y"], h["gated"], h["square"] = scan_forward(
            chunks, heads, wide_in, x, xb, state, cum, lag_row, seg_col, seg_row, skip_row
        )
        half[chunks] = h
    squares = jnp.concatenate([half[early]["square"], half[late]["square"]], axis=1)
    squares_far = swap(squares, "tensor")
    ready = squares
    for chunks in (late, early):
        h = half[chunks]
        h["attended"], h["lse"] = attention_forward(chunks, after(queries, ready), pairs, seg_col, seg_row)
        if chunks == late:
            squares_far = after(squares_far, h["lse"])
            squares_all = squares + squares_far
        h["square"], h["square_far"] = squares[:, h["span"]], squares_far[:, h["span"]]
        h["inv_gated"] = lax.rsqrt(squares_all[:, h["span"]].reshape(-1, 1) / DSSM + norm_eps)
        h["mixer_rows"] = (h["gated"] * h["inv_gated"] * gated_gain).astype(jnp.bfloat16)
        h["part"] = dot32(h["mixer_rows"], mixer_out) + dot32(h["attended"], attn_out)
        h["branch_far"] = swap(h["part"], "tensor")
        ready = h["part"]

    a, b = half[early], half[late]
    gain_ffn = ffn_gain[None, :]
    names = ("hidden", "normed", "activated", "grad_gate_rows", "grad_up_rows", "back", "down")
    for chunks in (late, early):
        h = half[chunks]
        far = h["branch_far"] if chunks == late else after(h["branch_far"], b["back"])
        operands = (layer_input, h["part"], far, gain_ffn, ffn_gate, ffn_up, ffn_down, cotangent)
        h.update(zip(names, ffn(chunks, *operands)))
        h["back_far"] = swap(h["back"], "tensor")

    sides = (after(a["normed"], b["back_far"]), b["normed"], a["activated"], b["activated"])
    sides += (a["grad_gate_rows"], b["grad_gate_rows"], a["grad_up_rows"], b["grad_up_rows"], cotangent)
    first = swap(ffn_weights(far_core, None, *sides), "core")

    for chunks in (late, early):
        h = half[chunks]
        far = h["back_far"] if chunks == late else after(h["back_far"], first)
        h["grad_hidden"], h["grad_branch"], h["grad_rows"], grad_attended, h["dot"], h["gain_sum"] = middle(
            chunks,
            h["hidden"],
            h["back"],
            far,
            cotangent,
            gain_ffn,
            h["gated"],
            h["square"],
            h["square_far"],
            gain_row,
            mixer_out,
            attn_out,
        )
        operands = (queries, pairs, grad_attended, h["lse"], seg_col, seg_row, cosine, sine)
        if chunks == late:
            h["grad_queries"], grad_keys, grad_values = attention_backward(chunks, False, *operands)
            first = ffn_weights(core, after(first, grad_keys), *sides)
        else:
            dots = jnp.concatenate([a["dot"], b["dot"]], axis=1)
            dots_far = swap(dots, "tensor")
            outer = (a["mixer_rows"], b["mixer_rows"], a["attended"], b["attended"])
            outer += (a["grad_branch"], b["grad_branch"])
            outer_far = swap(outer_weights(far_core, None, None, *outer), "core")
            h["grad_queries"], grad_pairs = attention_backward(chunks, True, *operands, grad_keys, grad_values)
    first = outer_weights(core, after(outer_far, grad_pairs), first, *outer)
    first_sum = lax.psum_scatter(first, ("y", "x"), scatter_dimension=0, tiled=True)
    dots_far = after(dots_far, first)
    for chunks in (late, early):
        h = half[chunks]
        h["grad_gate"], h["gy"], h["dx"], h["p"], h["grad_in"], h["grad_out"], h["sums"] = scan_backward(
            chunks,
            heads,
            h["grad_rows"],
            h["gated"],
            h["square"],
            h["square_far"],
            h["dot"],
            dots_far[:, h["span"]],
            gain_row,
            wide_in,
            h["y"],
            x,
            xb,
            state,
            lag,
            cum_row,
            skip_row,
            seg_col,
            seg_row,
            select,
        )
    pieces = [b["down"][:LEN], b["down"][LEN:], a["down"][:LEN], a["down"][LEN:]]
    pieces_far = [swap(after(piece, dots_far), "tensor") for piece in pieces]
    down = jnp.concatenate([a["down"], b["down"]], axis=0)
    ends = []
    for name in ("gy", "dx", "p", "grad_in", "grad_out"):
        ends += [a[name], b[name]]
    grad_conv, grad_state, grad_step, conv_sum, state_sum, step_sum = scan_end(
        heads,
        *ends,
        xb,
        slope,
        state_slope,
        wide_in,
        small_in,
        step_row,
        sig_row,
        rate_row,
        skip_row,
        keep,
        seg_col,
        seg_row,
        select,
        conv_kernel,
        state_kernel,
    )

    grads = (a["grad_gate"], b["grad_gate"], grad_conv, a["grad_queries"], b["grad_queries"])
    grads += (grad_state, grad_pairs, grad_step)
    tied = after(normed_input, *pieces_far[:3])
    second_far = swap(mixer_weights(far_core, None, None, tied, *grads), "core")
    partial_normed, input_gain_sum = normed_back(*grads, wide_proj, small_proj, layer_input, inv_rms_in)

    sums = a["sums"] + b["sums"]
    over_tensor = [input_gain_sum[0], state_sum[:4], state_sum[4]]
    alone = [
        step_sum[:heads, 0],
        step_sum[HEAD_ROWS : HEAD_ROWS + heads, 0],
        jnp.sum(sums[0].reshape(heads, HEAD_DIM), axis=1),
        conv_sum[:4],
        conv_sum[4],
        sums[1],
        a["gain_sum"][0] + b["gain_sum"][0],
    ]

    def packed(values):
        flat = jnp.concatenate([v.reshape(-1) for v in values])
        count = -(-flat.shape[0] // model_width)
        return jnp.pad(flat, (0, count * model_width - flat.shape[0])).reshape(count, model_width)

    def unpacked(table, values):
        flat, result, start = table.T.reshape(-1), [], 0
        for v in values:
            result.append(flat[start : start + v.size].reshape(v.shape))
            start += v.size
        return result

    tables = [packed(over_tensor), packed(alone)]
    shared_end = heads + tables[0].shape[0]
    table = jnp.concatenate(tables, axis=0)
    table_end = heads + table.shape[0]
    table = (core_rows(table, place) + swap(core_rows(table, 1 - place), "core")).T
    table = jnp.pad(table, ((0, 0), (heads, LEN - table_end)))
    spots = [core]
    for name, link in [order[0] for order in ORDERS]:
        at = lax.axis_index(name).astype(jnp.int32)
        side = ((at + 1) // 2) % 2 if link == "A" else at // 2
        spots.append(jnp.stack([side, 3 - side, 1 - side, 2 + side] if link == "A" else [2 * side, 2 * side + 1, 2 - 2 * side, 3 - 2 * side]))
    second = mixer_weights(jnp.concatenate(spots), after(second_far, pieces_far[3]), table, normed_input, *grads)
    at_state = 2 * width + query_width
    parts = reduce_rows([(second[2 * k], second[2 * k + 1]) for k in range(4)], (0, 1))
    first_own = exchange(after(first_sum, parts[0]), "zh")
    first_all = lax.all_gather(first_own, ("core", "y", "x"), axis=0, tiled=True)
    parts = reduce_rows(parts, (2, 3))
    second = jnp.concatenate([p.reshape(32, -1) for p in parts], axis=1)
    both = second[:, at_state:]
    lane = np.arange(both.shape[1])
    in_table = lane - 2 * state_size - pair_width
    is_shared = (lane < 2 * state_size) | ((in_table >= heads) & (in_table < shared_end))
    diagonal = [(0, 3), (3, 0), (1, 2), (2, 1)]
    more = swap(both, "tensor") + lax.ppermute(both, ("zh", "tensor"), diagonal)
    second = exchange(second, "zh")
    summed = second[:, at_state:] + jnp.where(is_shared[None, :], more, 0.0)
    second = jnp.concatenate([second[:, :at_state], summed], axis=1)
    second = after(second, first_all)
    normed_far = swap(after(partial_normed, second), "tensor")
    second = lax.all_gather(second, ("core", "y", "x"), axis=0, tiled=True)
    grad_mixer_proj, grad_query_proj, grad_keyval, grad_state_proj, step_block = assemble(second, width, query_width)

    def whole(name):
        return jnp.concatenate([a[name], b[name]], axis=0)

    grad_hidden = whole("grad_hidden")
    grad_normed = partial_normed + normed_far
    input_grad = grad_hidden + norm_backward(grad_normed * input_gain, unit_in, inv_rms_in)
    down_far = jnp.concatenate([pieces_far[2], pieces_far[3], pieces_far[0], pieces_far[1]], axis=0)
    layer_output = (whole("hidden") + (down + down_far)).astype(jnp.bfloat16)

    small_shared = unpacked(step_block[:, heads:shared_end], over_tensor)
    small_alone = unpacked(step_block[:, shared_end:table_end], alone)
    return (
        layer_output,
        input_grad,
        small_shared[0],
        grad_mixer_proj,
        grad_state_proj,
        step_block[:, :heads],
        small_alone[0],
        small_alone[1],
        small_alone[2],
        small_alone[3],
        small_alone[4],
        small_shared[1],
        small_shared[2],
        small_alone[5],
        first_all[:width, 3 * model_width :],
        grad_query_proj,
        grad_keyval,
        first_all[width:, 3 * model_width :],
        small_alone[6],
        first_all[:, :model_width],
        first_all[:, model_width : 2 * model_width],
        first_all[:, 2 * model_width : 3 * model_width],
    )


def solution(mesh):
    dp, whole_spec, columns = P(DP, None), P(), P(None, "tensor")
    per_channel, middle = P("tensor"), P(None, "tensor", None)
    last, by_rows = P(None, None, "tensor"), P("tensor", None)
    weights = (
        whole_spec,
        last,
        whole_spec,
        columns,
        per_channel,
        per_channel,
        per_channel,
        columns,
        per_channel,
        whole_spec,
        whole_spec,
        per_channel,
        by_rows,
        columns,
        middle,
        by_rows,
        whole_spec,
        columns,
        columns,
        by_rows,
    )
    mesh = jax.sharding.Mesh(mesh.devices.reshape(4, 2, 4, 2, 2), (*DP, "tensor"))
    return jax.shard_map(
        on_device, mesh=mesh, in_specs=(dp, dp, *weights, dp), out_specs=(dp, dp, *weights), check_vma=False
    )
```

```python
import functools

import jax
import jax.numpy as jnp
import numpy as np
from jax import lax
from jax.experimental import pallas as pl
from jax.experimental.pallas import tpu as pltpu
from jax.sharding import PartitionSpec as P

HEAD_DIM = 64
DSSM = 1536
DP = ("y", "zh", "x", "core")
PAIR = [(0, 1), (1, 0)]
LOG2E = 1.4426950408889634
hidden_bias = -1e30
norm_eps = 1e-05
rope_base = 10000.0
LEN = 128


def dot_nn(left, right):
    return lax.dot_general(
        left, right, (((1,), (0,)), ((), ())), preferred_element_type=jnp.float32
    )


def dot_nt(left, right):
    return lax.dot_general(
        left, right, (((1,), (1,)), ((), ())), preferred_element_type=jnp.float32
    )


def dot_tn(left, right):
    return lax.dot_general(
        left, right, (((0,), (0,)), ((), ())), preferred_element_type=jnp.float32
    )


def two_terms(v):
    high = v.astype(jnp.bfloat16)
    return high, (v - high.astype(jnp.float32)).astype(jnp.bfloat16)


def three_dots(dot, left, right):
    left_high, left_low = two_terms(left)
    right_high, right_low = two_terms(right)
    return dot(left_high, right_high) + dot(left_high, right_low) + dot(left_low, right_high)


def sigmoid(v):
    return 1.0 / (1.0 + jnp.exp(-v))


def block(index):
    return slice(index * LEN, (index + 1) * LEN)


def lane_iota(rows=LEN):
    return lax.broadcasted_iota(jnp.int32, (rows, LEN), 1)


def mask_ts(seg_col, seg_row, i, j):
    same = seg_col[block(i), :] == seg_row[:, block(j)]
    if i != j:
        return same
    down = lax.broadcasted_iota(jnp.int32, (LEN, LEN), 0)
    return same & (down >= lane_iota())


def mask_st(seg_col, seg_row, j, i):
    same = seg_col[block(j), :] == seg_row[:, block(i)]
    if i != j:
        return same
    down = lax.broadcasted_iota(jnp.int32, (LEN, LEN), 0)
    return same & (down <= lane_iota())


def conv_rows(pad_ref, keep_ref, kernel, bias, start, lanes):
    summed = bias + kernel[3:4] * pad_ref[8 + start : 8 + start + LEN, lanes]
    for lag in (1, 2, 3):
        moved = pad_ref[8 + start - lag : 8 + start - lag + LEN, lanes]
        summed = summed + kernel[3 - lag : 4 - lag] * (moved * keep_ref[lag - 1, start : start + LEN, :])
    return summed


def widen(keep_ref, wide_ref):
    rows = keep_ref.shape[0]
    for lag in (1, 2, 3):
        wide_ref[lag - 1, :, :] = jnp.broadcast_to(keep_ref[:, lag : lag + 1], (rows, LEN))


def prep_kernel(
    conv_ref,
    small_ref,
    cos_ref,
    sin_ref,
    keep_ref,
    conv_kernel_ref,
    conv_bias_ref,
    state_kernel_ref,
    state_bias_ref,
    step_bias_ref,
    rate_ref,
    x_ref,
    xb_ref,
    slope_ref,
    state_ref,
    state_slope_ref,
    cum_ref,
    lag_ref,
    cum_row_ref,
    lag_row_ref,
    step_row_ref,
    sig_row_ref,
    q_ref,
    kv_ref,
    pad_ref,
    wide_ref,
):
    rows = conv_ref.shape[0]
    blocks = rows // LEN

    @pl.when(pl.program_id(0) == 0)
    def _():
        pad_ref[0:8, :] = jnp.zeros((8, LEN), jnp.float32)
        widen(keep_ref, wide_ref)
        for c in range(2):
            pad_ref[8 : rows + 8, :] = small_ref[:, block(c)]
            for i in range(blocks):
                pre = conv_rows(
                    pad_ref, wide_ref, state_kernel_ref[:, block(c)], state_bias_ref[:, block(c)], i * LEN, slice(0, LEN)
                )
                sig = sigmoid(pre)
                state_ref[block(i), block(c)] = pre * sig
                state_slope_ref[block(i), block(c)] = sig * (1.0 + pre * (1.0 - sig))

    @pl.when(pl.program_id(0) == 1)
    def _():
        down = lax.broadcasted_iota(jnp.int32, (LEN, LEN), 0)
        lower = jnp.where(down >= lane_iota(), 1.0, 0.0).astype(jnp.bfloat16)
        left_half = lane_iota() < HEAD_DIM
        carry = jnp.zeros((1, LEN), jnp.float32)
        heads = cum_row_ref.shape[0]
        for i in range(blocks):
            argument = small_ref[block(i), block(5)] + step_bias_ref[...]
            tail = jnp.exp(-jnp.abs(argument))
            grown = jnp.where(tail < 1e-3, tail - 0.5 * tail * tail, jnp.log(1.0 + tail))
            step = jnp.maximum(argument, 0.0) + grown
            scaled = step * rate_ref[...] * LOG2E
            first, rest = two_terms(scaled)
            last = scaled - first.astype(jnp.float32) - rest.astype(jnp.float32)
            cum = dot_nn(lower, first) + dot_nn(lower, rest) + dot_nn(lower, last.astype(jnp.bfloat16)) + carry
            carry = cum[LEN - 1 : LEN, :]
            lag = cum - jnp.log(step) * LOG2E
            cum_ref[block(i), :] = cum
            lag_ref[block(i), :] = lag
            cum_t, lag_t = cum.T, lag.T
            step_row_ref[:, block(i)] = step.T[:heads]
            sig_row_ref[:, block(i)] = sigmoid(argument).T[:heads]
            for h in range(heads):
                cum_row_ref[h, :, block(i)] = cum_t[h : h + 1]
                lag_row_ref[h, :, block(i)] = lag_t[h : h + 1]
            cosine, sine = cos_ref[block(i), :], sin_ref[block(i), :]
            kv = small_ref[block(i), block(4)]
            kv_ref[block(i), :] = jnp.where(left_half, rotate_tile(kv, cosine, sine), kv).astype(jnp.bfloat16)
            for p in range(q_ref.shape[1] // LEN):
                q_ref[block(i), block(p)] = rotate_tile(small_ref[block(i), block(2 + p)], cosine, sine).astype(
                    jnp.bfloat16
                )

    for sub in range(GROUP):
        lanes = block(sub)
        pad_ref[8 : rows + 8, :] = conv_ref[:, lanes]
        for i in range(blocks):
            pre = conv_rows(pad_ref, wide_ref, conv_kernel_ref[:, lanes], conv_bias_ref[:, lanes], i * LEN, slice(0, LEN))
            sig = sigmoid(pre)
            x = pre * sig
            x_ref[block(i), lanes] = x
            xb_ref[block(i), lanes] = x.astype(jnp.bfloat16)
            slope_ref[block(i), lanes] = sig * (1.0 + pre * (1.0 - sig))


def rotate_tile(v, cosine, sine):
    first = lax.rem(lane_iota(v.shape[0]), HEAD_DIM) < HEAD_DIM // 2
    swapped = jnp.where(first, pltpu.roll(v, LEN - HEAD_DIM // 2, 1), pltpu.roll(v, HEAD_DIM // 2, 1))
    return v * cosine + swapped * sine


def scan_kernel(
    chunks,
    heads,
    gate_ref,
    x_ref,
    xb_ref,
    state_ref,
    cum_ref,
    lag_row_ref,
    seg_col_ref,
    seg_row_ref,
    skip_ref,
    y_ref,
    gated_ref,
    row_ref,
    wide_ref,
    cross_ref,
    bias_ref,
    mix_ref,
    square_ref,
):
    step = pl.program_id(0)
    first = chunks[0]
    pairs = [(i, j) for i in chunks for j in range(max(0, i - 2), i + 1)]
    left_half = lane_iota() < HEAD_DIM

    @pl.when(step == 0)
    def _():
        for h in range(heads):
            for i in chunks:
                wide_ref[h, block(i - first), :] = jnp.broadcast_to(cum_ref[block(i), h : h + 1], (LEN, LEN))
        for i in chunks:
            low = max(0, i - 2)
            cross = three_dots(dot_nt, state_ref[block(i), LEN:], state_ref[low * LEN : (i + 1) * LEN, :LEN])
            for n, (i2, j) in enumerate(pairs):
                if i2 == i:
                    cross_ref[n] = cross[:, block(j - low)]
                    allowed = mask_ts(seg_col_ref, seg_row_ref, i, j)
                    bias_ref[n] = jnp.where(allowed, 0.0, hidden_bias)
        square_ref[...] = jnp.zeros(square_ref.shape, jnp.float32)

    tiles = (gate_ref, x_ref, xb_ref, skip_ref, y_ref, gated_ref)

    def head_pair(hp, gate_ref, x_ref, xb_ref, skip_ref, y_ref, gated_ref):
        for i in chunks:
            at = block(i - first)
            low = max(0, i - 2)
            for n, (i2, j) in enumerate(pairs):
                if i2 != i:
                    continue
                for e in range(2):
                    spread = wide_ref[2 * hp + e, at, :] - lag_row_ref[2 * hp + e, :, block(j)]
                    decay = jnp.exp2(spread + bias_ref[n])
                    mix_ref[i - first, block(e), block(j - low)] = (decay * cross_ref[n]).astype(jnp.bfloat16)
            both = dot_nn(mix_ref[i - first, :, : (i + 1 - low) * LEN], xb_ref[low * LEN : (i + 1) * LEN, :])
            y = jnp.where(left_half, both[:LEN], both[LEN:])
            y_ref[at, :] = y
            gate = gate_ref[at, :]
            gated = (y + skip_ref[...] * x_ref[at, :]) * (gate * sigmoid(gate))
            gated_ref[at, :] = gated
            square_ref[at, :] = square_ref[at, :] + gated * gated

    for sub in range(GROUP):
        head_pair(GROUP * step + sub, *[t.at[:, block(sub)] for t in tiles])

    @pl.when(step == pl.num_programs(0) - 1)
    def _():
        for i in chunks:
            at = block(i - first)
            total = jnp.sum(square_ref[at, :], axis=1, keepdims=True)
            row_ref[0:1, at] = jnp.broadcast_to(total, (LEN, LEN)).T[0:1]


def attention_kernel(chunks, q_ref, kv_ref, seg_col_ref, seg_row_ref, out_ref, lse_ref):
    scale = HEAD_DIM ** (-0.5) * LOG2E
    first = chunks[0]
    left_half = lane_iota() < HEAD_DIM
    zero = jnp.zeros((LEN, LEN), jnp.bfloat16)
    lse_ref[...] = jnp.zeros(lse_ref.shape, jnp.float32)
    for i in chunks:
        at = block(i - first)
        low = max(0, i - 2) * LEN
        span = (i + 1) * LEN - low
        allowed = jnp.concatenate([mask_ts(seg_col_ref, seg_row_ref, i, j) for j in range(low // LEN, i + 1)], axis=1)
        keys = kv_ref[low : low + span, :]
        turned = pltpu.roll(keys.astype(jnp.float32), HEAD_DIM, 1).astype(jnp.bfloat16)
        for p in range(q_ref.shape[1] // LEN):
            queries = q_ref[block(i), block(p)]
            result = []
            for e in range(2):
                masked = jnp.where(left_half == (e == 0), queries, zero)
                scores = dot_nt(masked, keys if e == 0 else turned) * scale
                scores = jnp.where(allowed, scores, hidden_bias)
                top = jnp.max(scores, axis=1, keepdims=True)
                weights = jnp.exp2(scores - top)
                total = jnp.sum(weights, axis=1, keepdims=True)
                probs = (weights * (1.0 / total)).astype(jnp.bfloat16)
                result.append(dot_nn(probs, turned if e == 0 else keys))
                lse = jnp.broadcast_to(top + jnp.log(total) * LOG2E, (LEN, LEN))
                lse_ref[2 * p + e : 2 * p + e + 1, at] = lse.T[0:1]
            out_ref[at, block(p)] = jnp.where(left_half, result[0], result[1]).astype(jnp.bfloat16)


def attention_back_kernel(chunks, final, *refs):
    q_ref, kv_ref, do_ref, lse_ref, seg_col_ref, seg_row_ref, cos_ref, sin_ref = refs[:8]
    if final:
        dk_in_ref, dv_in_ref, dq_ref, dkv_ref, dk_ref, dv_ref, turned_ref, key_t_ref = refs[8:]
    else:
        dq_ref, dk_ref, dv_ref, turned_ref, key_t_ref = refs[8:]
    scale = HEAD_DIM ** (-0.5)
    blocks = q_ref.shape[0] // LEN
    first = chunks[0]
    left_half = lane_iota() < HEAD_DIM
    zero = jnp.zeros((LEN, LEN), jnp.bfloat16)
    for i in range(chunks[-1] + 1):
        kv = kv_ref[block(i), :].astype(jnp.float32)
        turned_ref[block(i), :] = pltpu.roll(kv, HEAD_DIM, 1).astype(jnp.bfloat16)
        key_t_ref[:, block(i)] = kv.T[:HEAD_DIM].astype(jnp.bfloat16)
    if final:
        dk_ref[...] = dk_in_ref[...]
        dv_ref[...] = dv_in_ref[...]
    else:
        dk_ref[...] = jnp.zeros(dk_ref.shape, jnp.float32)
        dv_ref[...] = jnp.zeros(dv_ref.shape, jnp.float32)
    for i in chunks:
        at = block(i - first)
        low = max(0, i - 2) * LEN
        span = (i + 1) * LEN - low
        window = slice(low, low + span)
        allowed = jnp.concatenate([mask_st(seg_col_ref, seg_row_ref, j, i) for j in range(low // LEN, i + 1)], axis=0)
        keys, turned = kv_ref[window, :], turned_ref[window, :]
        for p in range(q_ref.shape[1] // LEN):
            queries, douts = q_ref[block(i), block(p)], do_ref[at, block(p)]
            back = []
            for e in range(2):
                side = left_half == (e == 0)
                q_half = jnp.where(side, queries, zero)
                do_half = jnp.where(side, douts, zero)
                h = 2 * p + e
                scores = dot_nt(keys if e == 0 else turned, q_half) * (scale * LOG2E)
                probs = jnp.exp2(jnp.where(allowed, scores, hidden_bias) - lse_ref[h : h + 1, at])
                dprobs = dot_nt(turned if e == 0 else keys, do_half)
                inner = jnp.sum(probs * dprobs, axis=0, keepdims=True)
                dscores = (probs * (dprobs - inner)).astype(jnp.bfloat16)
                dv_ref[window, :] = dv_ref[window, :] + dot_nn(probs.astype(jnp.bfloat16), do_half)
                dk_ref[window, :] = dk_ref[window, :] + dot_nn(dscores, q_half)
                back.append(dot_nn(key_t_ref[:, window], dscores))
            dq = jnp.concatenate(back, axis=0).T * scale
            dq_ref[at, block(p)] = rotate_tile(dq, cos_ref[block(i), :], -sin_ref[block(i), :]).astype(jnp.bfloat16)
    if not final:
        return
    for i in range(blocks):
        dk = dk_ref[block(i), :]
        dk = (dk + pltpu.roll(dk, HEAD_DIM, 1)) * scale
        dk = rotate_tile(dk, cos_ref[block(i), :], -sin_ref[block(i), :])
        dv = dv_ref[block(i), :]
        dv = dv + pltpu.roll(dv, HEAD_DIM, 1)
        dkv_ref[block(i), :] = jnp.where(left_half, dk, dv).astype(jnp.bfloat16)


def scan_back_kernel(
    chunks,
    heads,
    gmr_ref,
    gated_ref,
    square_a_ref,
    square_b_ref,
    dot_a_ref,
    dot_b_ref,
    gain_ref,
    gate_ref,
    y_ref,
    x_ref,
    xb_ref,
    state_ref,
    lag_ref,
    cum_row_ref,
    skip_ref,
    seg_col_ref,
    seg_row_ref,
    select_ref,
    dgate_ref,
    gy_ref,
    dx_ref,
    p_ref,
    grad_in_ref,
    grad_out_ref,
    sums_ref,
    gyb_ref,
    wide_ref,
    cross_ref,
    bias_ref,
    dcross_ref,
    inv_wide_ref,
    dot_wide_ref,
    inner_ref,
    mix_ref,
):
    step = pl.program_id(0)
    first = chunks[0]
    sources = chunks[-1] + 1
    left_half = lane_iota() < HEAD_DIM
    zero = jnp.zeros((LEN, LEN), jnp.bfloat16)
    spans = [(j, max(j, first), min(j + 3, sources)) for j in range(sources)]
    pairs = [(j, i) for j, start, stop in spans for i in range(start, stop)]

    @pl.when(step == 0)
    def _():
        for i in chunks:
            at = block(i - first)
            square = (square_a_ref[:, at] + square_b_ref[:, at]) / DSSM
            inv = lax.rsqrt(square + norm_eps)
            inv_wide_ref[at, :] = jnp.broadcast_to(inv, (LEN, LEN)).T
            dot = (dot_a_ref[:, at] + dot_b_ref[:, at]) / DSSM
            dot_wide_ref[at, :] = jnp.broadcast_to(dot, (LEN, LEN)).T
        p_ref[...] = jnp.zeros(p_ref.shape, jnp.float32)
        for h in range(heads):
            wide_ref[h] = jnp.broadcast_to(lag_ref[: sources * LEN, h : h + 1], (sources * LEN, LEN))
        for j, start, stop in spans:
            cross = three_dots(dot_nt, state_ref[block(j), :LEN], state_ref[start * LEN : stop * LEN, LEN:])
            for n, (j2, i) in enumerate(pairs):
                if j2 == j:
                    cross_ref[n] = cross[:, block(i - start)]
                    allowed = mask_st(seg_col_ref, seg_row_ref, j, i)
                    bias_ref[n] = jnp.where(allowed, 0.0, hidden_bias)
                    dcross_ref[n] = jnp.zeros((LEN, LEN), jnp.float32)

    tiles = (
        gmr_ref, gated_ref, gain_ref, gate_ref, y_ref, x_ref, xb_ref, skip_ref, dgate_ref, gy_ref, dx_ref, sums_ref
    )

    def head_pair(
        hp,
        select,
        gmr_ref,
        gated_ref,
        gain_ref,
        gate_ref,
        y_ref,
        x_ref,
        xb_ref,
        skip_ref,
        dgate_ref,
        gy_ref,
        dx_ref,
        sums_ref,
    ):
        skip = skip_ref[...]
        gain = gain_ref[...]
        skip_sum = jnp.zeros((1, LEN), jnp.float32)
        gain_sum = jnp.zeros((1, LEN), jnp.float32)
        for i in chunks:
            at = block(i - first)
            inv = inv_wide_ref[at, :]
            unit = gated_ref[at, :] * inv
            rows_grad = gmr_ref[at, :]
            grad = inv * (rows_grad * gain - unit * dot_wide_ref[at, :])
            gate = gate_ref[at, :]
            sig = sigmoid(gate)
            y = y_ref[at, :]
            x = x_ref[at, :]
            gy = grad * (gate * sig)
            dgate_ref[at, :] = (grad * (y + skip * x) * (sig * (1.0 + gate * (1.0 - sig)))).astype(jnp.bfloat16)
            gyb = gy.astype(jnp.bfloat16)
            gy_ref[at, :] = gy
            gyb_ref[at, :] = gyb
            high, rest = two_terms(gyb.astype(jnp.float32) * y)
            p_ref[:, at] = p_ref[:, at] + dot_nt(select, high) + dot_nt(select, rest)
            skip_sum = skip_sum + jnp.sum(gy * x, axis=0, keepdims=True)
            gain_sum = gain_sum + jnp.sum(rows_grad * unit, axis=0, keepdims=True)
        sums_ref[0:1, :] = skip_sum
        sums_ref[1:2, :] = gain_sum

        for j, start, stop in spans:
            x_pair = xb_ref[block(j), :]
            x_both = jnp.concatenate([jnp.where(left_half, x_pair, zero), jnp.where(left_half, zero, x_pair)], axis=0)
            wide = (stop - start) * LEN
            gy_rows = gyb_ref[(start - first) * LEN : (stop - first) * LEN, :]
            inner_ref[:, :wide] = dot_nt(x_both, gy_rows)
            for n, (j2, i) in enumerate(pairs):
                if j2 != j:
                    continue
                grown = dcross_ref[n]
                for e in range(2):
                    spread = cum_row_ref[2 * hp + e, :, block(i)] - wide_ref[2 * hp + e, block(j), :]
                    decay = jnp.exp2(spread + bias_ref[n])
                    grown = grown + inner_ref[block(e), block(i - start)] * decay
                    mix_ref[block(e), block(i - start)] = (decay * cross_ref[n]).astype(jnp.bfloat16)
                dcross_ref[n] = grown
            both = dot_nn(mix_ref[:, :wide], gy_rows)
            dx_ref[block(j), :] = jnp.where(left_half, both[:LEN], both[LEN:])

    for sub in range(GROUP):
        head_pair(GROUP * step + sub, select_ref[:, block(sub)], *[t.at[:, block(sub)] for t in tiles])

    @pl.when(step == pl.num_programs(0) - 1)
    def _():
        grad_out = {i: jnp.zeros((LEN, LEN), jnp.float32) for i in chunks}
        for j in range(sources):
            grad_in = jnp.zeros((LEN, LEN), jnp.float32)
            for n, (j2, i) in enumerate(pairs):
                if j2 != j:
                    continue
                high, rest = two_terms(dcross_ref[n])
                out_high, out_rest = two_terms(state_ref[block(i), LEN:])
                in_high, in_rest = two_terms(state_ref[block(j), :LEN])
                grad_in = grad_in + dot_nn(high, out_high) + dot_nn(high, out_rest) + dot_nn(rest, out_high)
                grad_out[i] = grad_out[i] + dot_tn(high, in_high) + dot_tn(high, in_rest) + dot_tn(rest, in_high)
            grad_in_ref[block(j), :] = grad_in
        for i in chunks:
            grad_out_ref[block(i - first), :] = grad_out[i]


def conv_back(grad_ref, value_ref, keep_ref, kernel_ref, out_ref, sum_ref, lanes, blocks):
    taps = kernel_ref[:, lanes]
    totals = [jnp.zeros((1, LEN), jnp.float32) for _ in range(5)]
    for i in range(blocks):
        here = grad_ref[i * LEN : (i + 1) * LEN, :]
        grad = taps[3:4] * here
        totals[4] = totals[4] + jnp.sum(here, axis=0, keepdims=True)
        totals[3] = totals[3] + jnp.sum(here * value_ref[8 + i * LEN : 8 + (i + 1) * LEN, :], axis=0, keepdims=True)
        for lag in (1, 2, 3):
            ahead = grad_ref[i * LEN + lag : (i + 1) * LEN + lag, :]
            grad = grad + taps[3 - lag : 4 - lag] * (ahead * keep_ref[lag - 1, i * LEN + lag : (i + 1) * LEN + lag, :])
            moved = value_ref[8 + i * LEN - lag : 8 + (i + 1) * LEN - lag, :]
            masked = here * keep_ref[lag - 1, i * LEN : (i + 1) * LEN, :]
            totals[3 - lag] = totals[3 - lag] + jnp.sum(masked * moved, axis=0, keepdims=True)
        out_ref[block(i), lanes] = grad.astype(jnp.bfloat16)
    for tap in range(5):
        sum_ref[tap : tap + 1, lanes] = totals[tap]


def scan_end_kernel(
    heads,
    gy_a_ref,
    gy_b_ref,
    dx_a_ref,
    dx_b_ref,
    p_a_ref,
    p_b_ref,
    in_a_ref,
    in_b_ref,
    out_a_ref,
    out_b_ref,
    xb_ref,
    slope_ref,
    state_slope_ref,
    conv_ref,
    small_ref,
    step_row_ref,
    sig_row_ref,
    rate_ref,
    skip_ref,
    keep_ref,
    seg_col_ref,
    seg_row_ref,
    select_ref,
    conv_kernel_ref,
    state_kernel_ref,
    dconv_ref,
    dstate_ref,
    dstep_ref,
    conv_sum_ref,
    state_sum_ref,
    step_sum_ref,
    grad_pad_ref,
    value_pad_ref,
    wide_ref,
    q_ref,
    flow_ref,
):
    step = pl.program_id(0)
    rows = conv_ref.shape[0]
    blocks = rows // LEN
    half = rows // 2
    count = flow_ref.shape[0]

    @pl.when(step == 0)
    def _():
        value_pad_ref[0:8, :] = jnp.zeros((8, LEN), jnp.float32)
        grad_pad_ref[rows : rows + 8, :] = jnp.zeros((8, LEN), jnp.float32)
        widen(keep_ref, wide_ref)
        q_ref[...] = jnp.zeros(q_ref.shape, jnp.float32)
        for c in range(2):
            if c == 0:
                grad_pad_ref[0:half, :] = (in_a_ref[...] + in_b_ref[0:half, :]) * state_slope_ref[0:half, block(c)]
                grad_pad_ref[half:rows, :] = in_b_ref[half:rows, :] * state_slope_ref[half:rows, block(c)]
            else:
                grad_pad_ref[0:half, :] = out_a_ref[...] * state_slope_ref[0:half, block(c)]
                grad_pad_ref[half:rows, :] = out_b_ref[...] * state_slope_ref[half:rows, block(c)]
            value_pad_ref[8 : rows + 8, :] = small_ref[:, block(c)]
            conv_back(grad_pad_ref, value_pad_ref, wide_ref, state_kernel_ref, dstate_ref, state_sum_ref, block(c), blocks)

    tiles = (
        gy_a_ref, gy_b_ref, dx_a_ref, dx_b_ref, xb_ref, slope_ref, conv_ref, skip_ref, conv_kernel_ref, dconv_ref, conv_sum_ref
    )

    def head_pair(
        select,
        gy_a_ref,
        gy_b_ref,
        dx_a_ref,
        dx_b_ref,
        xb_ref,
        slope_ref,
        conv_ref,
        skip_ref,
        conv_kernel_ref,
        dconv_ref,
        conv_sum_ref,
    ):
        for j in range(blocks):
            dx = dx_b_ref[block(j), :]
            if j < blocks // 2:
                dx = dx + dx_a_ref[block(j), :]
                gy = gy_a_ref[block(j), :]
            else:
                gy = gy_b_ref[block(j - blocks // 2), :]
            high, rest = two_terms(dx * xb_ref[block(j), :].astype(jnp.float32))
            q_ref[:, block(j)] = q_ref[:, block(j)] + dot_nt(select, high) + dot_nt(select, rest)
            grad_pad_ref[block(j), :] = (dx + gy * skip_ref[...]) * slope_ref[block(j), :]
        value_pad_ref[8 : rows + 8, :] = conv_ref[...]
        conv_back(
            grad_pad_ref, value_pad_ref, wide_ref, conv_kernel_ref, dconv_ref, conv_sum_ref, slice(0, LEN), blocks
        )

    for sub in range(GROUP):
        head_pair(select_ref[:, block(sub)], *[t.at[:, block(sub)] for t in tiles])

    @pl.when(step == pl.num_programs(0) - 1)
    def _():
        q = q_ref[...]
        flow_ref[:, 0:half] = p_a_ref[...] - q[:, 0:half]
        flow_ref[:, half:rows] = p_b_ref[...] - q[:, half:rows]
        rate = jnp.broadcast_to(rate_ref[...], (LEN, LEN)).T[:count]
        bias_total = jnp.zeros((count, LEN), jnp.float32)
        decay_total = jnp.zeros((count, LEN), jnp.float32)
        for j in range(blocks):
            log_grad = jnp.zeros((count, LEN), jnp.float32)
            for i in range(j, min(j + 3, blocks)):
                chosen = jnp.where(mask_st(seg_col_ref, seg_row_ref, j, i), 1.0, 0.0).astype(jnp.bfloat16)
                high, rest = two_terms(flow_ref[:, block(i)])
                log_grad = log_grad + dot_nt(high, chosen) + dot_nt(rest, chosen)
            step = step_row_ref[:, block(j)]
            grad_step = jnp.where(step > 1e-30, q[:, block(j)] / step, 0.0) + log_grad * rate
            grad_arg = grad_step * sig_row_ref[:, block(j)]
            bias_total = bias_total + grad_arg
            decay_total = decay_total + log_grad * step
            tall = jnp.concatenate([grad_arg, jnp.zeros((LEN - count, LEN), jnp.float32)], axis=0)
            dstep_ref[block(j), :] = tall.T.astype(jnp.bfloat16)
        step_sum_ref[0:count, :] = jnp.broadcast_to(jnp.sum(bias_total, axis=1, keepdims=True), (count, LEN))
        step_sum_ref[count : 2 * count, :] = jnp.broadcast_to(
            jnp.sum(decay_total * rate, axis=1, keepdims=True), (count, LEN)
        )


def whole_block(shape):
    return pl.BlockSpec(shape, lambda step: (0,) * len(shape), pipeline_mode=pl.Buffered(1))


def tile(rows, row_block=0, first=0):
    return pl.BlockSpec((rows, GROUP * LEN), lambda step: (row_block, first + step))


def call(kernel, steps, out_shape, out_specs, scratch, operands, specs, flops):
    return pl.pallas_call(
        kernel,
        grid=(steps,),
        out_shape=out_shape,
        in_specs=[s or whole_block(o.shape) for o, s in zip(operands, specs)],
        out_specs=[s or whole_block(o.shape) for o, s in zip(out_shape, out_specs)],
        scratch_shapes=scratch,
        compiler_params=pltpu.CompilerParams(vmem_limit_bytes=VMEM_BYTES),
        cost_estimate=pl.CostEstimate(flops=flops, bytes_accessed=0, transcendentals=0),
    )(*operands)


def f32(*shape):
    return jax.ShapeDtypeStruct(shape, jnp.float32)


def b16(*shape):
    return jax.ShapeDtypeStruct(shape, jnp.bfloat16)


HEAD_ROWS = 16
GROUP = 3
VMEM_BYTES = 60 * 1024 * 1024


def scan_prep(width, wide_in, small, cosine, sine, keep, conv_kernel, conv_bias, *rest):
    rows = wide_in.shape[0]
    steps = width // LEN // GROUP
    outs = [
        f32(rows, width),
        b16(rows, width),
        f32(rows, width),
        f32(rows, 2 * LEN),
        f32(rows, 2 * LEN),
        f32(rows, LEN),
        f32(rows, LEN),
        f32(HEAD_ROWS, 1, rows),
        f32(HEAD_ROWS, 1, rows),
        f32(HEAD_ROWS, rows),
        f32(HEAD_ROWS, rows),
        b16(rows, 2 * LEN),
        b16(rows, LEN),
    ]
    scratch = [pltpu.VMEM((rows + 8, LEN), jnp.float32), pltpu.VMEM((3, rows + 8, LEN), jnp.float32)]
    operands = (wide_in, small, cosine, sine, keep, conv_kernel, conv_bias, *rest)
    specs = [tile(rows, 0, steps), None, None, None, None, tile(4), tile(1)] + [None] * len(rest)
    return call(prep_kernel, steps, outs, [tile(rows)] * 3 + [None] * 10, scratch, operands, specs, 0 * 10**9)


def scan_forward(chunks, heads, wide_in, x, xb, *rest):
    width = x.shape[1]
    rows = LEN * len(chunks)
    at = chunks[0] // len(chunks)
    count = sum(min(i, 2) + 1 for i in chunks)
    outs = [f32(rows, width), f32(rows, width), f32(1, rows)]
    scratch = [
        pltpu.VMEM((heads, rows, LEN), jnp.float32),
        pltpu.VMEM((count, LEN, LEN), jnp.float32),
        pltpu.VMEM((count, LEN, LEN), jnp.float32),
        pltpu.VMEM((len(chunks), 2 * LEN, 3 * LEN), jnp.bfloat16),
        pltpu.VMEM((rows, LEN), jnp.float32),
    ]
    specs = [tile(rows, at), tile(rows, at), tile((chunks[-1] + 1) * LEN)] + [None] * (len(rest) - 1) + [tile(1)]
    kernel = functools.partial(scan_kernel, chunks, heads)
    operands = (wide_in, x, xb, *rest)
    return call(kernel, heads // 2 // GROUP, outs, [tile(rows), tile(rows), None], scratch, operands, specs, 0 * 10**9)


def attention_forward(chunks, q, kv, seg_col, seg_row):
    rows = LEN * len(chunks)
    outs = [b16(rows, q.shape[1]), f32(8, rows)]
    kernel = functools.partial(attention_kernel, chunks)
    return call(kernel, 1, outs, [None] * 2, [], (q, kv, seg_col, seg_row), [None] * 4, 0 * 10**9)


def attention_backward(chunks, final, *operands):
    q = operands[0]
    rows = q.shape[0]
    partial = [f32(rows, LEN), f32(rows, LEN)]
    sums = [pltpu.VMEM((rows, LEN), jnp.float32)] * 2
    outs = [b16(LEN * len(chunks), q.shape[1])] + ([b16(rows, LEN)] if final else partial)
    scratch = (sums if final else []) + [
        pltpu.VMEM((rows, LEN), jnp.bfloat16),
        pltpu.VMEM((HEAD_DIM, rows), jnp.bfloat16),
    ]
    kernel = functools.partial(attention_back_kernel, chunks, final)
    return call(kernel, 1, outs, [None] * len(outs), scratch, operands, [None] * len(operands), (0 if chunks[0] else 30) * 10**9)


def scan_backward(chunks, heads, *operands):
    rows, width = operands[0].shape
    at = chunks[0] // len(chunks)
    sources = (chunks[-1] + 1) * LEN
    count = sum(min(i, 2) + 1 for i in chunks)
    outs = [
        b16(rows, width),
        f32(rows, width),
        f32(sources, width),
        f32(HEAD_ROWS, rows),
        f32(sources, LEN),
        f32(rows, LEN),
        f32(8, width),
    ]
    scratch = [
        pltpu.VMEM((rows, LEN), jnp.bfloat16),
        pltpu.VMEM((heads, sources, LEN), jnp.float32),
        pltpu.VMEM((count, LEN, LEN), jnp.float32),
        pltpu.VMEM((count, LEN, LEN), jnp.float32),
        pltpu.VMEM((count, LEN, LEN), jnp.float32),
        pltpu.VMEM((rows, LEN), jnp.float32),
        pltpu.VMEM((rows, LEN), jnp.float32),
        pltpu.VMEM((2 * LEN, 3 * LEN), jnp.float32),
        pltpu.VMEM((2 * LEN, 3 * LEN), jnp.bfloat16),
    ]
    specs = [tile(rows), tile(rows), None, None, None, None, tile(1), tile(rows, at), tile(rows), tile(rows, at), tile(sources)]
    specs += [None, None, None, tile(1), None, None, tile(HEAD_ROWS)]
    out_specs = [tile(rows), tile(rows), tile(sources), None, None, None, tile(8)]
    kernel = functools.partial(scan_back_kernel, chunks, heads)
    return call(kernel, heads // 2 // GROUP, outs, out_specs, scratch, operands, specs, 30 * 10**9)


def scan_end(heads, *operands):
    rows, width = 2 * operands[0].shape[0], operands[0].shape[1]
    steps = heads // 2 // GROUP
    outs = [
        b16(rows, width),
        b16(rows, 2 * LEN),
        b16(rows, LEN),
        f32(8, width),
        f32(8, 2 * LEN),
        f32(2 * HEAD_ROWS, LEN),
    ]
    scratch = [
        pltpu.VMEM((rows + 8, LEN), jnp.float32),
        pltpu.VMEM((rows + 8, LEN), jnp.float32),
        pltpu.VMEM((3, rows + 8, LEN), jnp.float32),
        pltpu.VMEM((HEAD_ROWS, rows), jnp.float32),
        pltpu.VMEM((HEAD_ROWS, rows), jnp.float32),
    ]
    half = rows // 2
    specs = [tile(half), tile(half), tile(half), tile(rows)] + [None] * 6 + [tile(rows), tile(rows), None]
    specs += [tile(rows, 0, steps)] + [None] * 4 + [tile(1), None, None, None, tile(HEAD_ROWS), tile(4), None]
    out_specs = [tile(rows), None, None, tile(8), None, None]
    kernel = functools.partial(scan_end_kernel, heads)
    return call(kernel, steps, outs, out_specs, scratch, operands, specs, 30 * 10**9)


def inverse_rms(rows):
    return lax.rsqrt(jnp.mean(rows * rows, axis=-1, keepdims=True) + norm_eps)


def ffn_kernel(
    tokens_ref,
    part_ref,
    far_ref,
    gain_ref,
    gate_ref,
    up_ref,
    down_ref,
    cotangent_ref,
    hidden_ref,
    normed_ref,
    activated_ref,
    grad_gate_ref,
    grad_up_ref,
    back_ref,
    out_ref,
):
    @pl.when(pl.program_id(0) == 0)
    def _():
        hidden = tokens_ref[...].astype(jnp.float32) + (part_ref[...] + far_ref[...])
        hidden_ref[...] = hidden
        normed_ref[...] = (hidden * inverse_rms(hidden) * gain_ref[...]).astype(jnp.bfloat16)
        back_ref[...] = jnp.zeros(back_ref.shape, jnp.float32)
        out_ref[...] = jnp.zeros(out_ref.shape, jnp.float32)

    normed = normed_ref[...]
    gate = dot_nn(normed, gate_ref[...])
    up = dot_nn(normed, up_ref[...])
    sig = sigmoid(gate)
    act = gate * sig
    activated = (act * up).astype(jnp.bfloat16)
    activated_ref[...] = activated
    grad = dot_nt(cotangent_ref[...], down_ref[...])
    grad_gate = (grad * up * (sig * (1.0 + gate * (1.0 - sig)))).astype(jnp.bfloat16)
    grad_up = (grad * act).astype(jnp.bfloat16)
    grad_gate_ref[...] = grad_gate
    grad_up_ref[...] = grad_up
    back_ref[...] = back_ref[...] + (dot_nt(grad_gate, gate_ref[...]) + dot_nt(grad_up, up_ref[...]))
    out_ref[...] = out_ref[...] + dot_nn(activated, down_ref[...])


def ffn(chunks, tokens, part, far, gain, gate, up, down, cotangent):
    rows, model_width = part.shape
    at = chunks[0] // len(chunks)
    hidden_width = gate.shape[1]
    steps = hidden_width // 256
    outs = [f32(rows, model_width), b16(rows, model_width)] + [b16(rows, hidden_width)] * 3
    outs += [f32(rows, model_width)] * 2
    rows_of = pl.BlockSpec((rows, model_width), lambda step: (at, 0), pipeline_mode=pl.Buffered(1))
    columns = pl.BlockSpec((model_width, 256), lambda step: (0, step))
    tiles = pl.BlockSpec((rows, 256), lambda step: (0, step))
    specs = [rows_of, None, None, None, columns, columns]
    specs += [pl.BlockSpec((256, model_width), lambda step: (step, 0)), rows_of]
    operands = (tokens, part, far, gain, gate, up, down, cotangent)
    return call(ffn_kernel, steps, outs, [None, None, tiles, tiles, tiles, None, None], [], operands, specs, 0 * 10**9)


def middle_kernel(
    hidden_ref,
    part_ref,
    far_ref,
    cotangent_ref,
    gain_ref,
    gated_ref,
    square_a_ref,
    square_b_ref,
    gated_gain_ref,
    mixer_out_ref,
    attn_out_ref,
    grad_hidden_ref,
    grad_branch_ref,
    grad_rows_ref,
    grad_attended_ref,
    dot_ref,
    gain_sum_ref,
):
    hidden = hidden_ref[...]
    inv = inverse_rms(hidden)
    unit = hidden * inv
    grad_normed = part_ref[...] + far_ref[...]
    gain_sum_ref[0:1, :] = jnp.sum(grad_normed * unit, axis=0, keepdims=True)
    grad_unit = grad_normed * gain_ref[...]
    inner = jnp.mean(grad_unit * unit, axis=-1, keepdims=True)
    grad_hidden = cotangent_ref[...].astype(jnp.float32) + inv * (grad_unit - unit * inner)
    grad_hidden_ref[...] = grad_hidden
    grad_branch = grad_hidden.astype(jnp.bfloat16)
    grad_branch_ref[...] = grad_branch
    grad_rows = dot_nt(grad_branch, mixer_out_ref[...])
    grad_rows_ref[...] = grad_rows
    grad_attended_ref[...] = dot_nt(grad_branch, attn_out_ref[...]).astype(jnp.bfloat16)
    total = jnp.sum(grad_rows * gated_gain_ref[...] * gated_ref[...], axis=-1, keepdims=True)
    for i in range(hidden.shape[0] // LEN):
        at = block(i)
        inv_gated = lax.rsqrt((square_a_ref[:, at] + square_b_ref[:, at]) / DSSM + norm_eps)
        dot_ref[0:1, at] = jnp.broadcast_to(total[at], (LEN, LEN)).T[0:1] * inv_gated


def middle(chunks, hidden, part, far, cotangent, gain, gated, square_a, square_b, gated_gain, mixer_out, attn_out):
    rows, model_width = part.shape
    at = chunks[0] // len(chunks)
    width, inner = mixer_out.shape[0], attn_out.shape[0]
    outs = [
        f32(rows, model_width),
        b16(rows, model_width),
        f32(rows, width),
        b16(rows, inner),
        f32(1, rows),
        f32(8, model_width),
    ]
    rows_of = pl.BlockSpec((rows, model_width), lambda step: (at, 0), pipeline_mode=pl.Buffered(1))
    specs = [None, None, None, rows_of] + [None] * 7
    operands = (hidden, part, far, cotangent, gain, gated, square_a, square_b, gated_gain, mixer_out, attn_out)
    return call(middle_kernel, 1, outs, [None] * 6, [], operands, specs, (0 if chunks[0] else 30) * 10**9)


def core_call(kernel, steps, core, out_shape, out_spec, scratch, operands, specs, flops, aliases=None):
    return pl.pallas_call(
        kernel,
        grid_spec=pltpu.PrefetchScalarGridSpec(
            num_scalar_prefetch=1, grid=(steps,), in_specs=specs, out_specs=out_spec, scratch_shapes=scratch
        ),
        out_shape=out_shape,
        compiler_params=pltpu.CompilerParams(vmem_limit_bytes=VMEM_BYTES),
        cost_estimate=pl.CostEstimate(flops=flops, bytes_accessed=0, transcendentals=0),
        input_output_aliases=aliases or {},
    )(core, *operands)


def clip_tile(rows, columns, first, last):
    return pl.BlockSpec((rows, columns), lambda step, core_ref: (0, jnp.clip(step - first, 0, last - first - 1)))


def ffn_weights_kernel(add, core_ref, *refs):
    refs = list(refs)
    normed_a, normed_b, act_a, act_b, gate_a, gate_b, up_a, up_b, cot_a, cot_b = refs[:10]
    far_ref = refs[10] if add else None
    out_ref, left_ref = refs[-2:]
    step = pl.program_id(0)
    third = pl.num_programs(0) // 3
    half = normed_a.shape[0]

    def turn(first, second):
        left_ref[:, :half] = first[...].T
        left_ref[:, half:] = second[...].T

    @pl.when(step == 0)
    def _():
        turn(normed_a, normed_b)

    @pl.when(step == 2 * third)
    def _():
        turn(act_a, act_b)

    def product(first, second):
        result = dot_nn(left_ref[:, :half], first[...]) + dot_nn(left_ref[:, half:], second[...])
        out_ref[...] = result + far_ref[...] if add else result

    @pl.when(step < third)
    def _():
        product(gate_a, gate_b)

    @pl.when((step >= third) & (step < 2 * third))
    def _():
        product(up_a, up_b)

    @pl.when(step >= 2 * third)
    def _():
        product(cot_a, cot_b)


def ffn_weights(core, far, normed_a, normed_b, act_a, act_b, gate_a, gate_b, up_a, up_b, cotangent):
    half, columns = normed_a.shape
    kept = columns // 2
    tile_width = 512
    third = columns // tile_width
    left = pl.BlockSpec((half, kept), lambda step, core_ref: (0, core_ref[0]), pipeline_mode=pl.Buffered(1))
    specs = [left] * 4 + [clip_tile(half, tile_width, 0, third)] * 2
    specs += [clip_tile(half, tile_width, third, 2 * third)] * 2

    def cot_rows(at):
        return pl.BlockSpec(
            (half, tile_width), lambda step, core_ref: (at, jnp.clip(step - 2 * third, 0, third - 1))
        )

    specs += [cot_rows(0), cot_rows(1)]
    out = pl.BlockSpec((kept, tile_width), lambda step, core_ref: (0, step))
    operands = [normed_a, normed_b, act_a, act_b, gate_a, gate_b, up_a, up_b, cotangent, cotangent]
    if far is not None:
        operands.append(far)
        specs.append(out)
    return core_call(
        functools.partial(ffn_weights_kernel, far is not None),
        3 * third,
        core,
        f32(kept, (3 if far is None else 4) * columns),
        out,
        [pltpu.VMEM((kept, 2 * half), jnp.bfloat16)],
        operands,
        specs,
        0 * 10**9,
    )


def outer_weights_kernel(add, core_ref, *refs):
    refs = list(refs)
    rows_a, rows_b, edge_a, edge_b, att_a, att_b, branch_a, branch_b = refs[:8]
    out_ref, left_ref = refs[-2:]
    half = rows_a.shape[0]
    middle_row = left_ref.shape[0] // 2

    @pl.when((pl.program_id(0) == 0) & (core_ref[0] == 0))
    def _():
        left_ref[:, :half] = rows_a[...].T
        left_ref[:, half:] = rows_b[...].T

    @pl.when((pl.program_id(0) == 0) & (core_ref[0] == 1))
    def _():
        left_ref[:middle_row, :half] = edge_a[...].T
        left_ref[:middle_row, half:] = edge_b[...].T
        left_ref[middle_row:, :half] = att_a[...].T
        left_ref[middle_row:, half:] = att_b[...].T

    result = dot_nn(left_ref[:, :half], branch_a[...]) + dot_nn(left_ref[:, half:], branch_b[...])
    out_ref[...] = result + refs[8][...] if add else result


def outer_weights(core, far, buffer, rows_a, rows_b, att_a, att_b, branch_a, branch_b):
    half, width = rows_a.shape
    model_width = branch_a.shape[1]
    kept = model_width // 2
    tile_width = 512
    steps = model_width // tile_width

    def fixed(shape, column=0):
        return pl.BlockSpec(shape, lambda step, core_ref: (0, column), pipeline_mode=pl.Buffered(1))

    specs = [fixed((half, kept))] * 2
    specs += [fixed((half, width - kept), kept // (width - kept))] * 2
    specs += [fixed(att_a.shape)] * 2 + [clip_tile(half, tile_width, 0, steps)] * 2
    operands = [rows_a, rows_b, rows_a, rows_b, att_a, att_b, branch_a, branch_b]
    out = pl.BlockSpec((kept, tile_width), lambda step, core_ref: (0, step))
    columns, aliases = model_width, {}
    if far is not None:
        operands += [far, buffer]
        specs += [out, pl.BlockSpec(memory_space=pl.ANY)]
        columns = buffer.shape[1]
        first = columns // tile_width - steps
        out = pl.BlockSpec((kept, tile_width), lambda step, core_ref: (0, first + step))
        aliases = {len(operands): 0}
    return core_call(
        functools.partial(outer_weights_kernel, far is not None),
        steps,
        core,
        f32(kept, columns),
        out,
        [pltpu.VMEM((kept, 2 * half), jnp.bfloat16)],
        operands,
        specs,
        0,
        aliases,
    )


PARTS = ((0, 3), (3, 5), (5, 7), (7, 9))


def mixer_weights_kernel(add, core_ref, *refs):
    refs = list(refs)
    normed_ref, gate_a, gate_b, conv_ref, query_a, query_b, state_ref, pair_ref, step_ref = refs[:9]
    far_ref, table_ref = refs[9:11] if add else (None, None)
    outs = refs[11:19] if add else refs[9:10]
    left_ref, result_ref = refs[-2:]
    step = pl.program_id(0)
    half = gate_a.shape[0]

    @pl.when(step == 0)
    def _():
        left_ref[...] = normed_ref[...].T

    def two(first, second):
        result_ref[...] = dot_nn(left_ref[:, :half], first[...]) + dot_nn(left_ref[:, half:], second[...])

    @pl.when(step < 3)
    def _():
        two(gate_a, gate_b)

    @pl.when((step >= 3) & (step < 6))
    def _():
        result_ref[...] = dot_nn(left_ref[...], conv_ref[...])

    @pl.when(step == 6)
    def _():
        two(query_a, query_b)

    @pl.when(step == 7)
    def _():
        result_ref[...] = dot_nn(left_ref[...], state_ref[...])

    @pl.when(step == 8)
    def _():
        result_ref[:, :LEN] = dot_nn(left_ref[...], pair_ref[...])
        steps = dot_nn(left_ref[...], step_ref[...])
        result_ref[:, LEN:] = steps + table_ref[...] if add else steps

    if not add:
        outs[0][...] = result_ref[...]
        return
    result_ref[...] = result_ref[...] + far_ref[...]
    for k, (first, last) in enumerate(PARTS):

        @pl.when((step >= first) & (step < last))
        def _():
            for side in range(2):
                out_ref = outs[2 * k + side]
                for q in range(2):
                    index = core_ref[1 + 4 * k + 2 * side + q]
                    if k < 2:
                        for y in range(4):
                            start = pl.multiple_of((4 * y + index) * 32, 32)
                            out_ref[(2 * y + q) * 32 : (2 * y + q + 1) * 32, :] = result_ref[pl.ds(start, 32), :]
                    else:
                        start = pl.multiple_of(index * LEN, LEN)
                        out_ref[q * LEN : (q + 1) * LEN, :] = result_ref[pl.ds(start, LEN), :]


def mixer_weights(core, far, table, normed, gate_a, gate_b, conv, query_a, query_b, state, pair, step):
    half = gate_a.shape[0]
    rows, model_width = normed.shape
    kept = model_width // 2
    tile_width = 256
    steps = 9

    def fixed(shape, column=0):
        return pl.BlockSpec(shape, lambda step, core_ref: (0, column), pipeline_mode=pl.Buffered(1))

    specs = [pl.BlockSpec((rows, kept), lambda step, core_ref: (0, core_ref[0]), pipeline_mode=pl.Buffered(1))]
    specs += [clip_tile(half, tile_width, 0, 3)] * 2 + [clip_tile(rows, tile_width, 3, 6)]
    specs += [fixed(query_a.shape)] * 2 + [fixed(state.shape), fixed(pair.shape), fixed(step.shape)]
    operands = [normed, gate_a, gate_b, conv, query_a, query_b, state, pair, step]
    out = pl.BlockSpec((kept, tile_width), lambda step, core_ref: (0, step))
    shape = f32(kept, steps * tile_width)
    if far is not None:
        operands += [far, table]
        specs += [out, fixed(table.shape)]
        out, shape = [], []
        for first, last in PARTS:
            out += [clip_tile(kept // 2, tile_width, first, last)] * 2
            shape += [f32(kept // 2, (last - first) * tile_width)] * 2
    return core_call(
        functools.partial(mixer_weights_kernel, far is not None),
        steps,
        core,
        shape,
        out,
        [pltpu.VMEM((kept, rows), jnp.bfloat16), pltpu.VMEM((kept, tile_width), jnp.float32)],
        operands,
        specs,
        30 * 10**9,
    )


def normed_back_kernel(
    gate_a,
    gate_b,
    conv_ref,
    query_a,
    query_b,
    state_ref,
    pair_ref,
    step_ref,
    wide_ref,
    small_ref,
    tokens_ref,
    inv_ref,
    out_ref,
    sum_ref,
):
    half, width = gate_a.shape
    query_width = query_a.shape[1]
    gate_w, conv_w = wide_ref[:, :width], wide_ref[:, width:]
    state_w = small_ref[:, : 2 * LEN]
    query_w = small_ref[:, 2 * LEN : 2 * LEN + query_width]
    pair_w = small_ref[:, 2 * LEN + query_width : 3 * LEN + query_width]
    step_w = small_ref[:, 3 * LEN + query_width :]
    total = jnp.zeros((1, out_ref.shape[1]), jnp.float32)
    for k, (gate, query) in enumerate(((gate_a, query_a), (gate_b, query_b))):
        at = slice(k * half, (k + 1) * half)
        grad = dot_nt(gate[...], gate_w) + dot_nt(conv_ref[at, :], conv_w) + dot_nt(query[...], query_w)
        grad = grad + dot_nt(state_ref[at, :], state_w) + dot_nt(pair_ref[at, :], pair_w) + dot_nt(step_ref[at, :], step_w)
        out_ref[at, :] = grad
        unit = tokens_ref[at, :].astype(jnp.float32) * inv_ref[at, :]
        total = total + jnp.sum(grad * unit, axis=0, keepdims=True)
    sum_ref[0:1, :] = total


def normed_back(gate_a, gate_b, conv, query_a, query_b, state, pair, step, wide_proj, small_proj, tokens, inv):
    rows, model_width = tokens.shape
    tile_width = 256
    operands = (gate_a, gate_b, conv, query_a, query_b, state, pair, step, wide_proj, small_proj, tokens, inv)

    def weights(count):
        return pl.BlockSpec((tile_width, count), lambda step: (step, 0))

    columns = pl.BlockSpec((rows, tile_width), lambda step: (0, step))
    specs = [None] * 8 + [weights(wide_proj.shape[1]), weights(small_proj.shape[1]), columns, None]
    out_specs = [columns, pl.BlockSpec((8, tile_width), lambda step: (0, step))]
    outs = [f32(rows, model_width), f32(8, model_width)]
    return call(normed_back_kernel, model_width // tile_width, outs, out_specs, [], operands, specs, 30 * 10**9)


def assemble_kernel(source, mixer_proj_ref, query_ref, pair_ref, state_ref, step_ref):
    width = mixer_proj_ref.shape[2]
    start = 0
    mixer_proj_ref[:, 0, :] = source[:, start : start + width]
    start += width
    mixer_proj_ref[:, 1, :] = source[:, start : start + width]
    start += width
    query_ref[...] = source[:, start : start + query_ref.shape[1]]
    start += query_ref.shape[1]
    state_ref[...] = source[:, start : start + 2 * LEN]
    start += 2 * LEN
    pair_ref[:, 0, :] = source[:, start : start + LEN]
    step_ref[...] = source[:, start + LEN :]


def assemble(values, width, query_width):
    rows, columns = values.shape

    def plain(count):
        return pl.BlockSpec((LEN, count), lambda at: (at, 0))

    out_specs = [
        pl.BlockSpec((LEN, 2, width), lambda at: (at, 0, 0)),
        plain(query_width),
        pl.BlockSpec((LEN, 1, LEN), lambda at: (at, 0, 0)),
        plain(2 * LEN),
        plain(LEN),
    ]
    out_shape = [
        f32(rows, 2, width),
        f32(rows, query_width),
        f32(rows, 1, LEN),
        f32(rows, 2 * LEN),
        f32(rows, LEN),
    ]
    return call(assemble_kernel, rows // LEN, out_shape, out_specs, [], (values,), [plain(columns)], 0)


LINKS = {
    "A": [(0, 1), (1, 0), (2, 3), (3, 2)],
    "B": [(1, 2), (2, 1), (3, 0), (0, 3)],
}
ORDERS = (
    (("x", "A"), ("x", "B"), ("y", "A"), ("y", "B")),
    (("x", "B"), ("y", "A"), ("y", "B"), ("x", "A")),
    (("y", "A"), ("y", "B"), ("x", "A"), ("x", "B")),
    (("y", "B"), ("x", "A"), ("x", "B"), ("y", "A")),
)
AXIS = {"y": 0, "x": 1}


def take(values, index, axis):
    return lax.dynamic_slice_in_dim(values, index, 1, axis)


def halves(values, name, link, again):
    place, axis = lax.axis_index(name), AXIS[name]
    if again:
        index = place // 2 if link == "B" else place % 2
        return take(values, index, axis), take(values, 1 - index, axis)
    if link == "B":
        side = place // 2
        kept = lax.dynamic_slice_in_dim(values, 2 * side, 2, axis)
        return kept, lax.dynamic_slice_in_dim(values, 2 - 2 * side, 2, axis)
    side = ((place + 1) // 2) % 2
    kept = jnp.concatenate([take(values, side, axis), take(values, 3 - side, axis)], axis)
    return kept, jnp.concatenate([take(values, 1 - side, axis), take(values, 2 + side, axis)], axis)


def reduce_rows(pairs, steps):
    kept, sent, parts = [], [], pairs
    if steps[0] == 0:
        for k, (stays, goes) in enumerate(pairs):
            shape = (4, 2, 32, stays.shape[1]) if ORDERS[k][0][0] == "x" else (2, 4, 32, stays.shape[1])
            kept.append(stays.reshape(shape))
            sent.append(goes.reshape(shape))
    for step in steps:
        if step:
            kept, sent = [], []
            for k in range(4):
                name, link = ORDERS[k][step]
                again = name in [n for n, _ in ORDERS[k][:step]]
                stays, goes = halves(parts[k], name, link, again)
                kept.append(stays)
                sent.append(goes)
        sent = lax.optimization_barrier(tuple(sent))
        come = [lax.ppermute(sent[k], ORDERS[k][step][0], LINKS[ORDERS[k][step][1]]) for k in range(4)]
        come = lax.optimization_barrier(tuple(come))
        parts = [stays + more for stays, more in zip(kept, come)]
    return parts


def rope_tables(rows):
    half_size = HEAD_DIM // 2
    inverse = np.float32(rope_base) ** (-(2.0 * np.arange(half_size, dtype=np.float32)) / HEAD_DIM)
    angles = np.arange(rows, dtype=np.float32)[:, None] * inverse.astype(np.float32)[None, :]
    cosine, sine = np.cos(angles), np.sin(angles)
    return (
        np.concatenate([cosine] * 4, axis=1).astype(np.float32),
        np.concatenate([-sine, sine, -sine, sine], axis=1).astype(np.float32),
    )


def norm_backward(grad_unit, unit_rows, inv_rms):
    return inv_rms * (grad_unit - unit_rows * jnp.mean(grad_unit * unit_rows, axis=-1, keepdims=True))


def dot32(left, right):
    return jnp.dot(left, right, preferred_element_type=jnp.float32)


def after(value, *others):
    return lax.optimization_barrier((value, *others))[0]


def swap(values, name):
    return lax.ppermute(values, name, PAIR)


def exchange(values, name):
    return values + swap(values, name)


def core_rows(values, index):
    half = values.shape[1] // 2
    return lax.dynamic_slice_in_dim(values, index * half, half, 1)


def on_device(
    layer_input,
    segments,
    input_gain,
    mixer_proj,
    state_proj,
    step_proj,
    step_bias,
    decay_log,
    skip_gain,
    conv_kernel,
    conv_bias,
    state_kernel,
    state_bias,
    gated_gain,
    mixer_out,
    query_proj,
    key_value_weight,
    attn_out,
    ffn_gain,
    ffn_gate,
    ffn_up,
    ffn_down,
    cotangent,
):
    segment = segments.reshape(-1)
    rows, model_width = layer_input.shape
    width = mixer_proj.shape[2]
    heads = step_proj.shape[1]
    state_size = state_proj.shape[1] // 2
    query_width = query_proj.shape[1]
    pair_width = key_value_weight.shape[2]
    place = lax.axis_index("core")
    zh = lax.axis_index("zh")
    core = place.astype(jnp.int32).reshape(1)
    far_core = 1 - core
    cosine, sine = rope_tables(rows)
    select = np.arange(HEAD_ROWS)[:, None] == np.arange(width)[None, :] // HEAD_DIM
    select = jnp.asarray(select.astype(np.float32)).astype(jnp.bfloat16)
    seg_col, seg_row = segment[:, None], segment[None, :]
    keep = [jnp.ones((rows,), jnp.float32)]
    for lag in (1, 2, 3):
        previous = jnp.concatenate([jnp.full((lag,), -1, jnp.int32), segment[:-lag]])
        keep.append((previous == segment).astype(jnp.float32))
    keep = jnp.pad(jnp.stack(keep, axis=1), ((0, 8), (0, 4)))
    pad_heads = ((0, 0), (0, LEN - heads))
    rate_row = jnp.pad(-jnp.exp(decay_log)[None, :], pad_heads)
    step_bias_row = jnp.pad(step_bias[None, :], pad_heads)
    skip_row = jnp.repeat(skip_gain, HEAD_DIM)[None, :]
    gain_row = gated_gain[None, :]
    wide_proj = mixer_proj.reshape(model_width, 2 * width)
    small_proj = jnp.concatenate(
        [
            state_proj,
            query_proj,
            key_value_weight.reshape(model_width, pair_width),
            jnp.pad(step_proj, pad_heads),
        ],
        axis=1,
    )

    tokens = layer_input.astype(jnp.float32)
    inv_rms_in = lax.rsqrt(jnp.mean(tokens * tokens, axis=-1, keepdims=True) + norm_eps)
    unit_in = tokens * inv_rms_in
    normed_input = (unit_in * input_gain).astype(jnp.bfloat16)
    small_in = dot32(normed_input, small_proj)
    wide_in = dot32(normed_input, wide_proj)
    x, xb, slope, state, state_slope, cum, lag, cum_row, lag_row, step_row, sig_row, queries, pairs = scan_prep(
        width,
        wide_in,
        small_in,
        cosine,
        sine,
        keep,
        conv_kernel,
        conv_bias[None, :],
        state_kernel,
        state_bias[None, :],
        step_bias_row,
        rate_row,
    )

    blocks = rows // LEN
    late = tuple(range(blocks // 2, blocks))
    early = tuple(range(blocks // 2))
    half = {}
    for chunks in (late, early):
        h = {"span": slice(chunks[0] * LEN, (chunks[-1] + 1) * LEN)}
        h["y"], h["gated"], h["square"] = scan_forward(
            chunks, heads, wide_in, x, xb, state, cum, lag_row, seg_col, seg_row, skip_row
        )
        half[chunks] = h
    squares = jnp.concatenate([half[early]["square"], half[late]["square"]], axis=1)
    squares_far = swap(squares, "tensor")
    ready = squares
    for chunks in (late, early):
        h = half[chunks]
        h["attended"], h["lse"] = attention_forward(chunks, after(queries, ready), pairs, seg_col, seg_row)
        if chunks == late:
            squares_far = after(squares_far, h["lse"])
            squares_all = squares + squares_far
        h["square"], h["square_far"] = squares[:, h["span"]], squares_far[:, h["span"]]
        h["inv_gated"] = lax.rsqrt(squares_all[:, h["span"]].reshape(-1, 1) / DSSM + norm_eps)
        h["mixer_rows"] = (h["gated"] * h["inv_gated"] * gated_gain).astype(jnp.bfloat16)
        h["part"] = dot32(h["mixer_rows"], mixer_out) + dot32(h["attended"], attn_out)
        h["branch_far"] = swap(h["part"], "tensor")
        ready = h["part"]

    a, b = half[early], half[late]
    gain_ffn = ffn_gain[None, :]
    names = ("hidden", "normed", "activated", "grad_gate_rows", "grad_up_rows", "back", "down")
    for chunks in (late, early):
        h = half[chunks]
        far = h["branch_far"] if chunks == late else after(h["branch_far"], b["back"])
        operands = (layer_input, h["part"], far, gain_ffn, ffn_gate, ffn_up, ffn_down, cotangent)
        h.update(zip(names, ffn(chunks, *operands)))
        h["back_far"] = swap(h["back"], "tensor")

    for chunks in (late, early):
        h = half[chunks]
        far = h["back_far"] if chunks == late else after(h["back_far"], first)
        h["grad_hidden"], h["grad_branch"], h["grad_rows"], grad_attended, h["dot"], h["gain_sum"] = middle(
            chunks,
            h["hidden"],
            h["back"],
            far,
            cotangent,
            gain_ffn,
            h["gated"],
            h["square"],
            h["square_far"],
            gain_row,
            mixer_out,
            attn_out,
        )
        operands = (queries, pairs, grad_attended, h["lse"], seg_col, seg_row, cosine, sine)
        if chunks == late:
            h["grad_queries"], grad_keys, grad_values = attention_backward(chunks, False, *operands)
            sides = (after(a["normed"], grad_keys), b["normed"], a["activated"], b["activated"])
            sides += (a["grad_gate_rows"], b["grad_gate_rows"], a["grad_up_rows"], b["grad_up_rows"], cotangent)
            first = ffn_weights(far_core, None, *sides)
            first_far = swap(first, "core")
        else:
            dots = jnp.concatenate([a["dot"], b["dot"]], axis=1)
            dots_far = swap(dots, "tensor")
            outer = (a["mixer_rows"], b["mixer_rows"], a["attended"], b["attended"])
            outer += (a["grad_branch"], b["grad_branch"])
            outer_far = swap(outer_weights(far_core, None, None, *outer), "core")
            h["grad_queries"], grad_pairs = attention_backward(chunks, True, *operands, grad_keys, grad_values)
    first = ffn_weights(core, after(first_far, grad_pairs), *sides)
    first = outer_weights(core, outer_far, first, *outer)
    first_sum = lax.psum_scatter(first, ("y", "x"), scatter_dimension=0, tiled=True)
    dots_far = after(dots_far, first)
    for chunks in (late, early):
        h = half[chunks]
        h["grad_gate"], h["gy"], h["dx"], h["p"], h["grad_in"], h["grad_out"], h["sums"] = scan_backward(
            chunks,
            heads,
            h["grad_rows"],
            h["gated"],
            h["square"],
            h["square_far"],
            h["dot"],
            dots_far[:, h["span"]],
            gain_row,
            wide_in,
            h["y"],
            x,
            xb,
            state,
            lag,
            cum_row,
            skip_row,
            seg_col,
            seg_row,
            select,
        )
    pieces = [b["down"][:LEN], b["down"][LEN:], a["down"][:LEN], a["down"][LEN:]]
    pieces_far = [swap(after(piece, dots_far), "tensor") for piece in pieces[:3]]
    down = jnp.concatenate([a["down"], b["down"]], axis=0)
    ends = []
    for name in ("gy", "dx", "p", "grad_in", "grad_out"):
        ends += [a[name], b[name]]
    grad_conv, grad_state, grad_step, conv_sum, state_sum, step_sum = scan_end(
        heads,
        *ends,
        after(xb, pieces_far[0]),
        slope,
        state_slope,
        wide_in,
        small_in,
        step_row,
        sig_row,
        rate_row,
        skip_row,
        keep,
        seg_col,
        seg_row,
        select,
        conv_kernel,
        state_kernel,
    )

    grads = (a["grad_gate"], b["grad_gate"], grad_conv, a["grad_queries"], b["grad_queries"])
    grads += (grad_state, grad_pairs, grad_step)
    tied = after(normed_input, pieces_far[1])
    second_far = swap(mixer_weights(far_core, None, None, tied, *grads), "core")
    partial_normed, input_gain_sum = normed_back(*grads, wide_proj, small_proj, layer_input, inv_rms_in)

    sums = a["sums"] + b["sums"]
    over_tensor = [input_gain_sum[0], state_sum[:4], state_sum[4]]
    alone = [
        step_sum[:heads, 0],
        step_sum[HEAD_ROWS : HEAD_ROWS + heads, 0],
        jnp.sum(sums[0].reshape(heads, HEAD_DIM), axis=1),
        conv_sum[:4],
        conv_sum[4],
        sums[1],
        a["gain_sum"][0] + b["gain_sum"][0],
    ]

    def packed(values):
        flat = jnp.concatenate([v.reshape(-1) for v in values])
        count = -(-flat.shape[0] // model_width)
        return jnp.pad(flat, (0, count * model_width - flat.shape[0])).reshape(count, model_width)

    def unpacked(table, values):
        flat, result, start = table.T.reshape(-1), [], 0
        for v in values:
            result.append(flat[start : start + v.size].reshape(v.shape))
            start += v.size
        return result

    tables = [packed(over_tensor), packed(alone)]
    shared_end = heads + tables[0].shape[0]
    table = jnp.concatenate(tables, axis=0)
    table_end = heads + table.shape[0]
    table = (core_rows(table, place) + swap(core_rows(table, 1 - place), "core")).T
    table = jnp.pad(table, ((0, 0), (heads, LEN - table_end)))
    spots = [core]
    for name, link in [order[0] for order in ORDERS]:
        at = lax.axis_index(name).astype(jnp.int32)
        side = ((at + 1) // 2) % 2 if link == "A" else at // 2
        spots.append(jnp.stack([side, 3 - side, 1 - side, 2 + side] if link == "A" else [2 * side, 2 * side + 1, 2 - 2 * side, 3 - 2 * side]))
    second = mixer_weights(jnp.concatenate(spots), after(second_far, pieces_far[2]), table, normed_input, *grads)
    at_state = 2 * width + query_width
    parts = reduce_rows([(second[2 * k], second[2 * k + 1]) for k in range(4)], (0,))
    first_own = exchange(after(first_sum, parts[0]), "zh")
    first_all = lax.all_gather(first_own, ("core", "y", "x"), axis=0, tiled=True)
    parts = reduce_rows(parts, (1, 2, 3))
    second = jnp.concatenate([p.reshape(32, -1) for p in parts], axis=1)
    both = second[:, at_state:]
    lane = np.arange(both.shape[1])
    in_table = lane - 2 * state_size - pair_width
    is_shared = (lane < 2 * state_size) | ((in_table >= heads) & (in_table < shared_end))
    diagonal = [(0, 3), (3, 0), (1, 2), (2, 1)]
    more = swap(both, "tensor") + lax.ppermute(both, ("zh", "tensor"), diagonal)
    second = exchange(second, "zh")
    summed = second[:, at_state:] + jnp.where(is_shared[None, :], more, 0.0)
    second = jnp.concatenate([second[:, :at_state], summed], axis=1)
    second = after(second, first_all)
    normed_far = swap(after(partial_normed, second), "tensor")
    pieces_far.append(swap(after(pieces[3], second), "tensor"))
    second = lax.all_gather(second, ("core", "y", "x"), axis=0, tiled=True)
    grad_mixer_proj, grad_query_proj, grad_keyval, grad_state_proj, step_block = assemble(second, width, query_width)

    def whole(name):
        return jnp.concatenate([a[name], b[name]], axis=0)

    grad_hidden = whole("grad_hidden")
    grad_normed = partial_normed + normed_far
    input_grad = grad_hidden + norm_backward(grad_normed * input_gain, unit_in, inv_rms_in)
    down_far = jnp.concatenate([pieces_far[2], pieces_far[3], pieces_far[0], pieces_far[1]], axis=0)
    layer_output = (whole("hidden") + (down + down_far)).astype(jnp.bfloat16)

    small_shared = unpacked(step_block[:, heads:shared_end], over_tensor)
    small_alone = unpacked(step_block[:, shared_end:table_end], alone)
    return (
        layer_output,
        input_grad,
        small_shared[0],
        grad_mixer_proj,
        grad_state_proj,
        step_block[:, :heads],
        small_alone[0],
        small_alone[1],
        small_alone[2],
        small_alone[3],
        small_alone[4],
        small_shared[1],
        small_shared[2],
        small_alone[5],
        first_all[:width, 3 * model_width :],
        grad_query_proj,
        grad_keyval,
        first_all[width:, 3 * model_width :],
        small_alone[6],
        first_all[:, :model_width],
        first_all[:, model_width : 2 * model_width],
        first_all[:, 2 * model_width : 3 * model_width],
    )


def solution(mesh):
    dp, whole_spec, columns = P(DP, None), P(), P(None, "tensor")
    per_channel, middle = P("tensor"), P(None, "tensor", None)
    last, by_rows = P(None, None, "tensor"), P("tensor", None)
    weights = (
        whole_spec,
        last,
        whole_spec,
        columns,
        per_channel,
        per_channel,
        per_channel,
        columns,
        per_channel,
        whole_spec,
        whole_spec,
        per_channel,
        by_rows,
        columns,
        middle,
        by_rows,
        whole_spec,
        columns,
        columns,
        by_rows,
    )
    mesh = jax.sharding.Mesh(mesh.devices.reshape(4, 2, 4, 2, 2), (*DP, "tensor"))
    return jax.shard_map(
        on_device, mesh=mesh, in_specs=(dp, dp, *weights, dp), out_specs=(dp, dp, *weights), check_vma=False
    )
```

```python
import functools

import jax
import jax.numpy as jnp
import numpy as np
from jax import lax
from jax.experimental import pallas as pl
from jax.experimental.pallas import tpu as pltpu
from jax.sharding import PartitionSpec as P

HEAD_DIM = 64
DSSM = 1536
DP = ("y", "zh", "x", "core")
PAIR = [(0, 1), (1, 0)]
LOG2E = 1.4426950408889634
hidden_bias = -1e30
norm_eps = 1e-05
rope_base = 10000.0
LEN = 128


def dot_nn(left, right):
    return lax.dot_general(
        left, right, (((1,), (0,)), ((), ())), preferred_element_type=jnp.float32
    )


def dot_nt(left, right):
    return lax.dot_general(
        left, right, (((1,), (1,)), ((), ())), preferred_element_type=jnp.float32
    )


def dot_tn(left, right):
    return lax.dot_general(
        left, right, (((0,), (0,)), ((), ())), preferred_element_type=jnp.float32
    )


def two_terms(v):
    high = v.astype(jnp.bfloat16)
    return high, (v - high.astype(jnp.float32)).astype(jnp.bfloat16)


def three_dots(dot, left, right):
    left_high, left_low = two_terms(left)
    right_high, right_low = two_terms(right)
    return dot(left_high, right_high) + dot(left_high, right_low) + dot(left_low, right_high)


def sigmoid(v):
    return 1.0 / (1.0 + jnp.exp(-v))


def block(index):
    return slice(index * LEN, (index + 1) * LEN)


def lane_iota(rows=LEN):
    return lax.broadcasted_iota(jnp.int32, (rows, LEN), 1)


def mask_ts(seg_col, seg_row, i, j):
    same = seg_col[block(i), :] == seg_row[:, block(j)]
    if i != j:
        return same
    down = lax.broadcasted_iota(jnp.int32, (LEN, LEN), 0)
    return same & (down >= lane_iota())


def mask_st(seg_col, seg_row, j, i):
    same = seg_col[block(j), :] == seg_row[:, block(i)]
    if i != j:
        return same
    down = lax.broadcasted_iota(jnp.int32, (LEN, LEN), 0)
    return same & (down <= lane_iota())


def conv_rows(pad_ref, keep_ref, kernel, bias, start, lanes):
    summed = bias + kernel[3:4] * pad_ref[8 + start : 8 + start + LEN, lanes]
    for lag in (1, 2, 3):
        moved = pad_ref[8 + start - lag : 8 + start - lag + LEN, lanes]
        summed = summed + kernel[3 - lag : 4 - lag] * (moved * keep_ref[lag - 1, start : start + LEN, :])
    return summed


def widen(keep_ref, wide_ref):
    rows = keep_ref.shape[0]
    for lag in (1, 2, 3):
        wide_ref[lag - 1, :, :] = jnp.broadcast_to(keep_ref[:, lag : lag + 1], (rows, LEN))


def prep_kernel(
    conv_ref,
    small_ref,
    cos_ref,
    sin_ref,
    keep_ref,
    conv_kernel_ref,
    conv_bias_ref,
    state_kernel_ref,
    state_bias_ref,
    step_bias_ref,
    rate_ref,
    x_ref,
    xb_ref,
    slope_ref,
    state_ref,
    state_slope_ref,
    cum_ref,
    lag_ref,
    cum_row_ref,
    lag_row_ref,
    step_row_ref,
    sig_row_ref,
    q_ref,
    kv_ref,
    pad_ref,
    wide_ref,
):
    rows = conv_ref.shape[0]
    blocks = rows // LEN

    @pl.when(pl.program_id(0) == 0)
    def _():
        pad_ref[0:8, :] = jnp.zeros((8, LEN), jnp.float32)
        widen(keep_ref, wide_ref)
        for c in range(2):
            pad_ref[8 : rows + 8, :] = small_ref[:, block(c)]
            for i in range(blocks):
                pre = conv_rows(
                    pad_ref, wide_ref, state_kernel_ref[:, block(c)], state_bias_ref[:, block(c)], i * LEN, slice(0, LEN)
                )
                sig = sigmoid(pre)
                state_ref[block(i), block(c)] = pre * sig
                state_slope_ref[block(i), block(c)] = sig * (1.0 + pre * (1.0 - sig))

    @pl.when(pl.program_id(0) == 1)
    def _():
        down = lax.broadcasted_iota(jnp.int32, (LEN, LEN), 0)
        lower = jnp.where(down >= lane_iota(), 1.0, 0.0).astype(jnp.bfloat16)
        left_half = lane_iota() < HEAD_DIM
        carry = jnp.zeros((1, LEN), jnp.float32)
        heads = cum_row_ref.shape[0]
        for i in range(blocks):
            argument = small_ref[block(i), block(5)] + step_bias_ref[...]
            tail = jnp.exp(-jnp.abs(argument))
            grown = jnp.where(tail < 1e-3, tail - 0.5 * tail * tail, jnp.log(1.0 + tail))
            step = jnp.maximum(argument, 0.0) + grown
            scaled = step * rate_ref[...] * LOG2E
            first, rest = two_terms(scaled)
            last = scaled - first.astype(jnp.float32) - rest.astype(jnp.float32)
            cum = dot_nn(lower, first) + dot_nn(lower, rest) + dot_nn(lower, last.astype(jnp.bfloat16)) + carry
            carry = cum[LEN - 1 : LEN, :]
            lag = cum - jnp.log(step) * LOG2E
            cum_ref[block(i), :] = cum
            lag_ref[block(i), :] = lag
            cum_t, lag_t = cum.T, lag.T
            step_row_ref[:, block(i)] = step.T[:heads]
            sig_row_ref[:, block(i)] = sigmoid(argument).T[:heads]
            for h in range(heads):
                cum_row_ref[h, :, block(i)] = cum_t[h : h + 1]
                lag_row_ref[h, :, block(i)] = lag_t[h : h + 1]
            cosine, sine = cos_ref[block(i), :], sin_ref[block(i), :]
            kv = small_ref[block(i), block(4)]
            kv_ref[block(i), :] = jnp.where(left_half, rotate_tile(kv, cosine, sine), kv).astype(jnp.bfloat16)
            for p in range(q_ref.shape[1] // LEN):
                q_ref[block(i), block(p)] = rotate_tile(small_ref[block(i), block(2 + p)], cosine, sine).astype(
                    jnp.bfloat16
                )

    for sub in range(GROUP):
        lanes = block(sub)
        pad_ref[8 : rows + 8, :] = conv_ref[:, lanes]
        for i in range(blocks):
            pre = conv_rows(pad_ref, wide_ref, conv_kernel_ref[:, lanes], conv_bias_ref[:, lanes], i * LEN, slice(0, LEN))
            sig = sigmoid(pre)
            x = pre * sig
            x_ref[block(i), lanes] = x
            xb_ref[block(i), lanes] = x.astype(jnp.bfloat16)
            slope_ref[block(i), lanes] = sig * (1.0 + pre * (1.0 - sig))


def rotate_tile(v, cosine, sine):
    first = lax.rem(lane_iota(v.shape[0]), HEAD_DIM) < HEAD_DIM // 2
    swapped = jnp.where(first, pltpu.roll(v, LEN - HEAD_DIM // 2, 1), pltpu.roll(v, HEAD_DIM // 2, 1))
    return v * cosine + swapped * sine


def scan_kernel(
    chunks,
    heads,
    gate_ref,
    x_ref,
    xb_ref,
    state_ref,
    cum_ref,
    lag_row_ref,
    seg_col_ref,
    seg_row_ref,
    skip_ref,
    y_ref,
    gated_ref,
    row_ref,
    wide_ref,
    cross_ref,
    bias_ref,
    mix_ref,
    square_ref,
):
    step = pl.program_id(0)
    first = chunks[0]
    pairs = [(i, j) for i in chunks for j in range(max(0, i - 2), i + 1)]
    left_half = lane_iota() < HEAD_DIM

    @pl.when(step == 0)
    def _():
        for h in range(heads):
            for i in chunks:
                wide_ref[h, block(i - first), :] = jnp.broadcast_to(cum_ref[block(i), h : h + 1], (LEN, LEN))
        for i in chunks:
            low = max(0, i - 2)
            cross = three_dots(dot_nt, state_ref[block(i), LEN:], state_ref[low * LEN : (i + 1) * LEN, :LEN])
            for n, (i2, j) in enumerate(pairs):
                if i2 == i:
                    cross_ref[n] = cross[:, block(j - low)]
                    allowed = mask_ts(seg_col_ref, seg_row_ref, i, j)
                    bias_ref[n] = jnp.where(allowed, 0.0, hidden_bias)
        square_ref[...] = jnp.zeros(square_ref.shape, jnp.float32)

    tiles = (gate_ref, x_ref, xb_ref, skip_ref, y_ref, gated_ref)

    def head_pair(hp, gate_ref, x_ref, xb_ref, skip_ref, y_ref, gated_ref):
        for i in chunks:
            at = block(i - first)
            low = max(0, i - 2)
            for n, (i2, j) in enumerate(pairs):
                if i2 != i:
                    continue
                for e in range(2):
                    spread = wide_ref[2 * hp + e, at, :] - lag_row_ref[2 * hp + e, :, block(j)]
                    decay = jnp.exp2(spread + bias_ref[n])
                    mix_ref[i - first, block(e), block(j - low)] = (decay * cross_ref[n]).astype(jnp.bfloat16)
            both = dot_nn(mix_ref[i - first, :, : (i + 1 - low) * LEN], xb_ref[low * LEN : (i + 1) * LEN, :])
            y = jnp.where(left_half, both[:LEN], both[LEN:])
            y_ref[at, :] = y
            gate = gate_ref[at, :]
            gated = (y + skip_ref[...] * x_ref[at, :]) * (gate * sigmoid(gate))
            gated_ref[at, :] = gated
            square_ref[at, :] = square_ref[at, :] + gated * gated

    for sub in range(GROUP):
        head_pair(GROUP * step + sub, *[t.at[:, block(sub)] for t in tiles])

    @pl.when(step == pl.num_programs(0) - 1)
    def _():
        for i in chunks:
            at = block(i - first)
            total = jnp.sum(square_ref[at, :], axis=1, keepdims=True)
            row_ref[0:1, at] = jnp.broadcast_to(total, (LEN, LEN)).T[0:1]


def attention_kernel(chunks, q_ref, kv_ref, seg_col_ref, seg_row_ref, out_ref, lse_ref):
    scale = HEAD_DIM ** (-0.5) * LOG2E
    first = chunks[0]
    left_half = lane_iota() < HEAD_DIM
    zero = jnp.zeros((LEN, LEN), jnp.bfloat16)
    lse_ref[...] = jnp.zeros(lse_ref.shape, jnp.float32)
    for i in chunks:
        at = block(i - first)
        low = max(0, i - 2) * LEN
        span = (i + 1) * LEN - low
        allowed = jnp.concatenate([mask_ts(seg_col_ref, seg_row_ref, i, j) for j in range(low // LEN, i + 1)], axis=1)
        keys = kv_ref[low : low + span, :]
        turned = pltpu.roll(keys.astype(jnp.float32), HEAD_DIM, 1).astype(jnp.bfloat16)
        for p in range(q_ref.shape[1] // LEN):
            queries = q_ref[block(i), block(p)]
            result = []
            for e in range(2):
                masked = jnp.where(left_half == (e == 0), queries, zero)
                scores = dot_nt(masked, keys if e == 0 else turned) * scale
                scores = jnp.where(allowed, scores, hidden_bias)
                top = jnp.max(scores, axis=1, keepdims=True)
                weights = jnp.exp2(scores - top)
                total = jnp.sum(weights, axis=1, keepdims=True)
                probs = (weights * (1.0 / total)).astype(jnp.bfloat16)
                result.append(dot_nn(probs, turned if e == 0 else keys))
                lse = jnp.broadcast_to(top + jnp.log(total) * LOG2E, (LEN, LEN))
                lse_ref[2 * p + e : 2 * p + e + 1, at] = lse.T[0:1]
            out_ref[at, block(p)] = jnp.where(left_half, result[0], result[1]).astype(jnp.bfloat16)


def attention_back_kernel(chunks, final, *refs):
    q_ref, kv_ref, do_ref, lse_ref, seg_col_ref, seg_row_ref, cos_ref, sin_ref = refs[:8]
    if final:
        dk_in_ref, dv_in_ref, dq_ref, dkv_ref, dk_ref, dv_ref, turned_ref, key_t_ref = refs[8:]
    else:
        dq_ref, dk_ref, dv_ref, turned_ref, key_t_ref = refs[8:]
    scale = HEAD_DIM ** (-0.5)
    blocks = q_ref.shape[0] // LEN
    first = chunks[0]
    left_half = lane_iota() < HEAD_DIM
    zero = jnp.zeros((LEN, LEN), jnp.bfloat16)
    for i in range(chunks[-1] + 1):
        kv = kv_ref[block(i), :].astype(jnp.float32)
        turned_ref[block(i), :] = pltpu.roll(kv, HEAD_DIM, 1).astype(jnp.bfloat16)
        key_t_ref[:, block(i)] = kv.T[:HEAD_DIM].astype(jnp.bfloat16)
    if final:
        dk_ref[...] = dk_in_ref[...]
        dv_ref[...] = dv_in_ref[...]
    else:
        dk_ref[...] = jnp.zeros(dk_ref.shape, jnp.float32)
        dv_ref[...] = jnp.zeros(dv_ref.shape, jnp.float32)
    for i in chunks:
        at = block(i - first)
        low = max(0, i - 2) * LEN
        span = (i + 1) * LEN - low
        window = slice(low, low + span)
        allowed = jnp.concatenate([mask_st(seg_col_ref, seg_row_ref, j, i) for j in range(low // LEN, i + 1)], axis=0)
        keys, turned = kv_ref[window, :], turned_ref[window, :]
        for p in range(q_ref.shape[1] // LEN):
            queries, douts = q_ref[block(i), block(p)], do_ref[at, block(p)]
            back = []
            for e in range(2):
                side = left_half == (e == 0)
                q_half = jnp.where(side, queries, zero)
                do_half = jnp.where(side, douts, zero)
                h = 2 * p + e
                scores = dot_nt(keys if e == 0 else turned, q_half) * (scale * LOG2E)
                probs = jnp.exp2(jnp.where(allowed, scores, hidden_bias) - lse_ref[h : h + 1, at])
                dprobs = dot_nt(turned if e == 0 else keys, do_half)
                inner = jnp.sum(probs * dprobs, axis=0, keepdims=True)
                dscores = (probs * (dprobs - inner)).astype(jnp.bfloat16)
                dv_ref[window, :] = dv_ref[window, :] + dot_nn(probs.astype(jnp.bfloat16), do_half)
                dk_ref[window, :] = dk_ref[window, :] + dot_nn(dscores, q_half)
                back.append(dot_nn(key_t_ref[:, window], dscores))
            dq = jnp.concatenate(back, axis=0).T * scale
            dq_ref[at, block(p)] = rotate_tile(dq, cos_ref[block(i), :], -sin_ref[block(i), :]).astype(jnp.bfloat16)
    if not final:
        return
    for i in range(blocks):
        dk = dk_ref[block(i), :]
        dk = (dk + pltpu.roll(dk, HEAD_DIM, 1)) * scale
        dk = rotate_tile(dk, cos_ref[block(i), :], -sin_ref[block(i), :])
        dv = dv_ref[block(i), :]
        dv = dv + pltpu.roll(dv, HEAD_DIM, 1)
        dkv_ref[block(i), :] = jnp.where(left_half, dk, dv).astype(jnp.bfloat16)


def scan_back_kernel(
    chunks,
    heads,
    gmr_ref,
    gated_ref,
    square_a_ref,
    square_b_ref,
    dot_a_ref,
    dot_b_ref,
    gain_ref,
    gate_ref,
    y_ref,
    x_ref,
    xb_ref,
    state_ref,
    lag_ref,
    cum_row_ref,
    skip_ref,
    seg_col_ref,
    seg_row_ref,
    select_ref,
    dgate_ref,
    gy_ref,
    dx_ref,
    p_ref,
    grad_in_ref,
    grad_out_ref,
    sums_ref,
    gyb_ref,
    wide_ref,
    cross_ref,
    bias_ref,
    dcross_ref,
    inv_wide_ref,
    dot_wide_ref,
    inner_ref,
    mix_ref,
):
    step = pl.program_id(0)
    first = chunks[0]
    sources = chunks[-1] + 1
    left_half = lane_iota() < HEAD_DIM
    zero = jnp.zeros((LEN, LEN), jnp.bfloat16)
    spans = [(j, max(j, first), min(j + 3, sources)) for j in range(sources)]
    pairs = [(j, i) for j, start, stop in spans for i in range(start, stop)]

    @pl.when(step == 0)
    def _():
        for i in chunks:
            at = block(i - first)
            square = (square_a_ref[:, at] + square_b_ref[:, at]) / DSSM
            inv = lax.rsqrt(square + norm_eps)
            inv_wide_ref[at, :] = jnp.broadcast_to(inv, (LEN, LEN)).T
            dot = (dot_a_ref[:, at] + dot_b_ref[:, at]) / DSSM
            dot_wide_ref[at, :] = jnp.broadcast_to(dot, (LEN, LEN)).T
        p_ref[...] = jnp.zeros(p_ref.shape, jnp.float32)
        for h in range(heads):
            wide_ref[h] = jnp.broadcast_to(lag_ref[: sources * LEN, h : h + 1], (sources * LEN, LEN))
        for j, start, stop in spans:
            cross = three_dots(dot_nt, state_ref[block(j), :LEN], state_ref[start * LEN : stop * LEN, LEN:])
            for n, (j2, i) in enumerate(pairs):
                if j2 == j:
                    cross_ref[n] = cross[:, block(i - start)]
                    allowed = mask_st(seg_col_ref, seg_row_ref, j, i)
                    bias_ref[n] = jnp.where(allowed, 0.0, hidden_bias)
                    dcross_ref[n] = jnp.zeros((LEN, LEN), jnp.float32)

    tiles = (
        gmr_ref, gated_ref, gain_ref, gate_ref, y_ref, x_ref, xb_ref, skip_ref, dgate_ref, gy_ref, dx_ref, sums_ref
    )

    def head_pair(
        hp,
        select,
        gmr_ref,
        gated_ref,
        gain_ref,
        gate_ref,
        y_ref,
        x_ref,
        xb_ref,
        skip_ref,
        dgate_ref,
        gy_ref,
        dx_ref,
        sums_ref,
    ):
        skip = skip_ref[...]
        gain = gain_ref[...]
        skip_sum = jnp.zeros((1, LEN), jnp.float32)
        gain_sum = jnp.zeros((1, LEN), jnp.float32)
        for i in chunks:
            at = block(i - first)
            inv = inv_wide_ref[at, :]
            unit = gated_ref[at, :] * inv
            rows_grad = gmr_ref[at, :]
            grad = inv * (rows_grad * gain - unit * dot_wide_ref[at, :])
            gate = gate_ref[at, :]
            sig = sigmoid(gate)
            y = y_ref[at, :]
            x = x_ref[at, :]
            gy = grad * (gate * sig)
            dgate_ref[at, :] = (grad * (y + skip * x) * (sig * (1.0 + gate * (1.0 - sig)))).astype(jnp.bfloat16)
            gyb = gy.astype(jnp.bfloat16)
            gy_ref[at, :] = gy
            gyb_ref[at, :] = gyb
            high, rest = two_terms(gyb.astype(jnp.float32) * y)
            p_ref[:, at] = p_ref[:, at] + dot_nt(select, high) + dot_nt(select, rest)
            skip_sum = skip_sum + jnp.sum(gy * x, axis=0, keepdims=True)
            gain_sum = gain_sum + jnp.sum(rows_grad * unit, axis=0, keepdims=True)
        sums_ref[0:1, :] = skip_sum
        sums_ref[1:2, :] = gain_sum

        for j, start, stop in spans:
            x_pair = xb_ref[block(j), :]
            x_both = jnp.concatenate([jnp.where(left_half, x_pair, zero), jnp.where(left_half, zero, x_pair)], axis=0)
            wide = (stop - start) * LEN
            gy_rows = gyb_ref[(start - first) * LEN : (stop - first) * LEN, :]
            inner_ref[:, :wide] = dot_nt(x_both, gy_rows)
            for n, (j2, i) in enumerate(pairs):
                if j2 != j:
                    continue
                grown = dcross_ref[n]
                for e in range(2):
                    spread = cum_row_ref[2 * hp + e, :, block(i)] - wide_ref[2 * hp + e, block(j), :]
                    decay = jnp.exp2(spread + bias_ref[n])
                    grown = grown + inner_ref[block(e), block(i - start)] * decay
                    mix_ref[block(e), block(i - start)] = (decay * cross_ref[n]).astype(jnp.bfloat16)
                dcross_ref[n] = grown
            both = dot_nn(mix_ref[:, :wide], gy_rows)
            dx_ref[block(j), :] = jnp.where(left_half, both[:LEN], both[LEN:])

    for sub in range(GROUP):
        head_pair(GROUP * step + sub, select_ref[:, block(sub)], *[t.at[:, block(sub)] for t in tiles])

    @pl.when(step == pl.num_programs(0) - 1)
    def _():
        grad_out = {i: jnp.zeros((LEN, LEN), jnp.float32) for i in chunks}
        for j in range(sources):
            grad_in = jnp.zeros((LEN, LEN), jnp.float32)
            for n, (j2, i) in enumerate(pairs):
                if j2 != j:
                    continue
                high, rest = two_terms(dcross_ref[n])
                out_high, out_rest = two_terms(state_ref[block(i), LEN:])
                in_high, in_rest = two_terms(state_ref[block(j), :LEN])
                grad_in = grad_in + dot_nn(high, out_high) + dot_nn(high, out_rest) + dot_nn(rest, out_high)
                grad_out[i] = grad_out[i] + dot_tn(high, in_high) + dot_tn(high, in_rest) + dot_tn(rest, in_high)
            grad_in_ref[block(j), :] = grad_in
        for i in chunks:
            grad_out_ref[block(i - first), :] = grad_out[i]


def conv_back(grad_ref, value_ref, keep_ref, kernel_ref, out_ref, sum_ref, lanes, blocks):
    taps = kernel_ref[:, lanes]
    totals = [jnp.zeros((1, LEN), jnp.float32) for _ in range(5)]
    for i in range(blocks):
        here = grad_ref[i * LEN : (i + 1) * LEN, :]
        grad = taps[3:4] * here
        totals[4] = totals[4] + jnp.sum(here, axis=0, keepdims=True)
        totals[3] = totals[3] + jnp.sum(here * value_ref[8 + i * LEN : 8 + (i + 1) * LEN, :], axis=0, keepdims=True)
        for lag in (1, 2, 3):
            ahead = grad_ref[i * LEN + lag : (i + 1) * LEN + lag, :]
            grad = grad + taps[3 - lag : 4 - lag] * (ahead * keep_ref[lag - 1, i * LEN + lag : (i + 1) * LEN + lag, :])
            moved = value_ref[8 + i * LEN - lag : 8 + (i + 1) * LEN - lag, :]
            masked = here * keep_ref[lag - 1, i * LEN : (i + 1) * LEN, :]
            totals[3 - lag] = totals[3 - lag] + jnp.sum(masked * moved, axis=0, keepdims=True)
        out_ref[block(i), lanes] = grad.astype(jnp.bfloat16)
    for tap in range(5):
        sum_ref[tap : tap + 1, lanes] = totals[tap]


def scan_end_kernel(
    heads,
    gy_a_ref,
    gy_b_ref,
    dx_a_ref,
    dx_b_ref,
    p_a_ref,
    p_b_ref,
    in_a_ref,
    in_b_ref,
    out_a_ref,
    out_b_ref,
    xb_ref,
    slope_ref,
    state_slope_ref,
    conv_ref,
    small_ref,
    step_row_ref,
    sig_row_ref,
    rate_ref,
    skip_ref,
    keep_ref,
    seg_col_ref,
    seg_row_ref,
    select_ref,
    conv_kernel_ref,
    state_kernel_ref,
    dconv_ref,
    dstate_ref,
    dstep_ref,
    conv_sum_ref,
    state_sum_ref,
    step_sum_ref,
    grad_pad_ref,
    value_pad_ref,
    wide_ref,
    q_ref,
    flow_ref,
):
    step = pl.program_id(0)
    rows = conv_ref.shape[0]
    blocks = rows // LEN
    half = rows // 2
    count = flow_ref.shape[0]

    @pl.when(step == 0)
    def _():
        value_pad_ref[0:8, :] = jnp.zeros((8, LEN), jnp.float32)
        grad_pad_ref[rows : rows + 8, :] = jnp.zeros((8, LEN), jnp.float32)
        widen(keep_ref, wide_ref)
        q_ref[...] = jnp.zeros(q_ref.shape, jnp.float32)
        for c in range(2):
            if c == 0:
                grad_pad_ref[0:half, :] = (in_a_ref[...] + in_b_ref[0:half, :]) * state_slope_ref[0:half, block(c)]
                grad_pad_ref[half:rows, :] = in_b_ref[half:rows, :] * state_slope_ref[half:rows, block(c)]
            else:
                grad_pad_ref[0:half, :] = out_a_ref[...] * state_slope_ref[0:half, block(c)]
                grad_pad_ref[half:rows, :] = out_b_ref[...] * state_slope_ref[half:rows, block(c)]
            value_pad_ref[8 : rows + 8, :] = small_ref[:, block(c)]
            conv_back(grad_pad_ref, value_pad_ref, wide_ref, state_kernel_ref, dstate_ref, state_sum_ref, block(c), blocks)

    tiles = (
        gy_a_ref, gy_b_ref, dx_a_ref, dx_b_ref, xb_ref, slope_ref, conv_ref, skip_ref, conv_kernel_ref, dconv_ref, conv_sum_ref
    )

    def head_pair(
        select,
        gy_a_ref,
        gy_b_ref,
        dx_a_ref,
        dx_b_ref,
        xb_ref,
        slope_ref,
        conv_ref,
        skip_ref,
        conv_kernel_ref,
        dconv_ref,
        conv_sum_ref,
    ):
        for j in range(blocks):
            dx = dx_b_ref[block(j), :]
            if j < blocks // 2:
                dx = dx + dx_a_ref[block(j), :]
                gy = gy_a_ref[block(j), :]
            else:
                gy = gy_b_ref[block(j - blocks // 2), :]
            high, rest = two_terms(dx * xb_ref[block(j), :].astype(jnp.float32))
            q_ref[:, block(j)] = q_ref[:, block(j)] + dot_nt(select, high) + dot_nt(select, rest)
            grad_pad_ref[block(j), :] = (dx + gy * skip_ref[...]) * slope_ref[block(j), :]
        value_pad_ref[8 : rows + 8, :] = conv_ref[...]
        conv_back(
            grad_pad_ref, value_pad_ref, wide_ref, conv_kernel_ref, dconv_ref, conv_sum_ref, slice(0, LEN), blocks
        )

    for sub in range(GROUP):
        head_pair(select_ref[:, block(sub)], *[t.at[:, block(sub)] for t in tiles])

    @pl.when(step == pl.num_programs(0) - 1)
    def _():
        q = q_ref[...]
        flow_ref[:, 0:half] = p_a_ref[...] - q[:, 0:half]
        flow_ref[:, half:rows] = p_b_ref[...] - q[:, half:rows]
        rate = jnp.broadcast_to(rate_ref[...], (LEN, LEN)).T[:count]
        bias_total = jnp.zeros((count, LEN), jnp.float32)
        decay_total = jnp.zeros((count, LEN), jnp.float32)
        for j in range(blocks):
            log_grad = jnp.zeros((count, LEN), jnp.float32)
            for i in range(j, min(j + 3, blocks)):
                chosen = jnp.where(mask_st(seg_col_ref, seg_row_ref, j, i), 1.0, 0.0).astype(jnp.bfloat16)
                high, rest = two_terms(flow_ref[:, block(i)])
                log_grad = log_grad + dot_nt(high, chosen) + dot_nt(rest, chosen)
            step = step_row_ref[:, block(j)]
            grad_step = jnp.where(step > 1e-30, q[:, block(j)] / step, 0.0) + log_grad * rate
            grad_arg = grad_step * sig_row_ref[:, block(j)]
            bias_total = bias_total + grad_arg
            decay_total = decay_total + log_grad * step
            tall = jnp.concatenate([grad_arg, jnp.zeros((LEN - count, LEN), jnp.float32)], axis=0)
            dstep_ref[block(j), :] = tall.T.astype(jnp.bfloat16)
        step_sum_ref[0:count, :] = jnp.broadcast_to(jnp.sum(bias_total, axis=1, keepdims=True), (count, LEN))
        step_sum_ref[count : 2 * count, :] = jnp.broadcast_to(
            jnp.sum(decay_total * rate, axis=1, keepdims=True), (count, LEN)
        )


def whole_block(shape):
    return pl.BlockSpec(shape, lambda step: (0,) * len(shape), pipeline_mode=pl.Buffered(1))


def tile(rows, row_block=0, first=0):
    return pl.BlockSpec((rows, GROUP * LEN), lambda step: (row_block, first + step))


def small_block(rows, width):
    return pl.BlockSpec((rows, width), lambda step: (0, 2), pipeline_mode=pl.Buffered(1))


def call(kernel, steps, out_shape, out_specs, scratch, operands, specs, flops):
    return pl.pallas_call(
        kernel,
        grid=(steps,),
        out_shape=out_shape,
        in_specs=[s or whole_block(o.shape) for o, s in zip(operands, specs)],
        out_specs=[s or whole_block(o.shape) for o, s in zip(out_shape, out_specs)],
        scratch_shapes=scratch,
        compiler_params=pltpu.CompilerParams(vmem_limit_bytes=VMEM_BYTES),
        cost_estimate=pl.CostEstimate(flops=flops, bytes_accessed=0, transcendentals=0),
    )(*operands)


def f32(*shape):
    return jax.ShapeDtypeStruct(shape, jnp.float32)


def b16(*shape):
    return jax.ShapeDtypeStruct(shape, jnp.bfloat16)


HEAD_ROWS = 16
GROUP = 3
VMEM_BYTES = 60 * 1024 * 1024


def scan_prep(width, wide_in, cosine, sine, keep, conv_kernel, conv_bias, *rest):
    rows = wide_in.shape[0]
    steps = width // LEN // GROUP
    outs = [
        f32(rows, width),
        b16(rows, width),
        f32(rows, width),
        f32(rows, 2 * LEN),
        f32(rows, 2 * LEN),
        f32(rows, LEN),
        f32(rows, LEN),
        f32(HEAD_ROWS, 1, rows),
        f32(HEAD_ROWS, 1, rows),
        f32(HEAD_ROWS, rows),
        f32(HEAD_ROWS, rows),
        b16(rows, 2 * LEN),
        b16(rows, LEN),
    ]
    scratch = [pltpu.VMEM((rows + 8, LEN), jnp.float32), pltpu.VMEM((3, rows + 8, LEN), jnp.float32)]
    operands = (wide_in, wide_in, cosine, sine, keep, conv_kernel, conv_bias, *rest)
    specs = [tile(rows, 0, steps), small_block(rows, width), None, None, None, tile(4), tile(1)] + [None] * len(rest)
    return call(prep_kernel, steps, outs, [tile(rows)] * 3 + [None] * 10, scratch, operands, specs, 0 * 10**9)


def scan_forward(chunks, heads, wide_in, x, xb, *rest):
    width = x.shape[1]
    rows = LEN * len(chunks)
    at = chunks[0] // len(chunks)
    count = sum(min(i, 2) + 1 for i in chunks)
    outs = [f32(rows, width), f32(rows, width), f32(1, rows)]
    scratch = [
        pltpu.VMEM((heads, rows, LEN), jnp.float32),
        pltpu.VMEM((count, LEN, LEN), jnp.float32),
        pltpu.VMEM((count, LEN, LEN), jnp.float32),
        pltpu.VMEM((len(chunks), 2 * LEN, 3 * LEN), jnp.bfloat16),
        pltpu.VMEM((rows, LEN), jnp.float32),
    ]
    specs = [tile(rows, at), tile(rows, at), tile((chunks[-1] + 1) * LEN)] + [None] * (len(rest) - 1) + [tile(1)]
    kernel = functools.partial(scan_kernel, chunks, heads)
    operands = (wide_in, x, xb, *rest)
    return call(kernel, heads // 2 // GROUP, outs, [tile(rows), tile(rows), None], scratch, operands, specs, 0 * 10**9)


def attention_forward(chunks, q, kv, seg_col, seg_row):
    rows = LEN * len(chunks)
    outs = [b16(rows, q.shape[1]), f32(8, rows)]
    kernel = functools.partial(attention_kernel, chunks)
    return call(kernel, 1, outs, [None] * 2, [], (q, kv, seg_col, seg_row), [None] * 4, 0 * 10**9)


def attention_backward(chunks, final, *operands):
    q = operands[0]
    rows = q.shape[0]
    partial = [f32(rows, LEN), f32(rows, LEN)]
    sums = [pltpu.VMEM((rows, LEN), jnp.float32)] * 2
    outs = [b16(LEN * len(chunks), q.shape[1])] + ([b16(rows, LEN)] if final else partial)
    scratch = (sums if final else []) + [
        pltpu.VMEM((rows, LEN), jnp.bfloat16),
        pltpu.VMEM((HEAD_DIM, rows), jnp.bfloat16),
    ]
    kernel = functools.partial(attention_back_kernel, chunks, final)
    return call(kernel, 1, outs, [None] * len(outs), scratch, operands, [None] * len(operands), (0 if chunks[0] else 30) * 10**9)


def scan_backward(chunks, heads, *operands):
    rows, width = operands[0].shape
    at = chunks[0] // len(chunks)
    sources = (chunks[-1] + 1) * LEN
    count = sum(min(i, 2) + 1 for i in chunks)
    outs = [
        b16(rows, width),
        f32(rows, width),
        f32(sources, width),
        f32(HEAD_ROWS, rows),
        f32(sources, LEN),
        f32(rows, LEN),
        f32(8, width),
    ]
    scratch = [
        pltpu.VMEM((rows, LEN), jnp.bfloat16),
        pltpu.VMEM((heads, sources, LEN), jnp.float32),
        pltpu.VMEM((count, LEN, LEN), jnp.float32),
        pltpu.VMEM((count, LEN, LEN), jnp.float32),
        pltpu.VMEM((count, LEN, LEN), jnp.float32),
        pltpu.VMEM((rows, LEN), jnp.float32),
        pltpu.VMEM((rows, LEN), jnp.float32),
        pltpu.VMEM((2 * LEN, 3 * LEN), jnp.float32),
        pltpu.VMEM((2 * LEN, 3 * LEN), jnp.bfloat16),
    ]
    specs = [tile(rows), tile(rows), None, None, None, None, tile(1), tile(rows, at), tile(rows), tile(rows, at), tile(sources)]
    specs += [None, None, None, tile(1), None, None, tile(HEAD_ROWS)]
    out_specs = [tile(rows), tile(rows), tile(sources), None, None, None, tile(8)]
    kernel = functools.partial(scan_back_kernel, chunks, heads)
    return call(kernel, heads // 2 // GROUP, outs, out_specs, scratch, operands, specs, 30 * 10**9)


def scan_end(heads, *operands):
    rows, width = 2 * operands[0].shape[0], operands[0].shape[1]
    steps = heads // 2 // GROUP
    outs = [
        b16(rows, width),
        b16(rows, 2 * LEN),
        b16(rows, LEN),
        f32(8, width),
        f32(8, 2 * LEN),
        f32(2 * HEAD_ROWS, LEN),
    ]
    scratch = [
        pltpu.VMEM((rows + 8, LEN), jnp.float32),
        pltpu.VMEM((rows + 8, LEN), jnp.float32),
        pltpu.VMEM((3, rows + 8, LEN), jnp.float32),
        pltpu.VMEM((HEAD_ROWS, rows), jnp.float32),
        pltpu.VMEM((HEAD_ROWS, rows), jnp.float32),
    ]
    half = rows // 2
    specs = [tile(half), tile(half), tile(half), tile(rows)] + [None] * 6 + [tile(rows), tile(rows), None]
    specs += [tile(rows, 0, steps), small_block(rows, width)] + [None] * 3 + [tile(1), None, None, None, tile(HEAD_ROWS), tile(4), None]
    out_specs = [tile(rows), None, None, tile(8), None, None]
    kernel = functools.partial(scan_end_kernel, heads)
    return call(kernel, steps, outs, out_specs, scratch, operands, specs, 30 * 10**9)


def inverse_rms(rows):
    return lax.rsqrt(jnp.mean(rows * rows, axis=-1, keepdims=True) + norm_eps)


def ffn_kernel(
    tokens_ref,
    part_ref,
    far_ref,
    gain_ref,
    gate_ref,
    up_ref,
    down_ref,
    cotangent_ref,
    hidden_ref,
    normed_ref,
    activated_ref,
    grad_gate_ref,
    grad_up_ref,
    back_ref,
    out_ref,
):
    @pl.when(pl.program_id(0) == 0)
    def _():
        hidden = tokens_ref[...].astype(jnp.float32) + (part_ref[...] + far_ref[...])
        hidden_ref[...] = hidden
        normed_ref[...] = (hidden * inverse_rms(hidden) * gain_ref[...]).astype(jnp.bfloat16)
        back_ref[...] = jnp.zeros(back_ref.shape, jnp.float32)
        out_ref[...] = jnp.zeros(out_ref.shape, jnp.float32)

    normed = normed_ref[...]
    gate = dot_nn(normed, gate_ref[...])
    up = dot_nn(normed, up_ref[...])
    sig = sigmoid(gate)
    act = gate * sig
    activated = (act * up).astype(jnp.bfloat16)
    activated_ref[...] = activated
    grad = dot_nt(cotangent_ref[...], down_ref[...])
    grad_gate = (grad * up * (sig * (1.0 + gate * (1.0 - sig)))).astype(jnp.bfloat16)
    grad_up = (grad * act).astype(jnp.bfloat16)
    grad_gate_ref[...] = grad_gate
    grad_up_ref[...] = grad_up
    back_ref[...] = back_ref[...] + (dot_nt(grad_gate, gate_ref[...]) + dot_nt(grad_up, up_ref[...]))
    out_ref[...] = out_ref[...] + dot_nn(activated, down_ref[...])


def ffn(chunks, tokens, part, far, gain, gate, up, down, cotangent):
    rows, model_width = part.shape
    at = chunks[0] // len(chunks)
    hidden_width = gate.shape[1]
    steps = hidden_width // 256
    outs = [f32(rows, model_width), b16(rows, model_width)] + [b16(rows, hidden_width)] * 3
    outs += [f32(rows, model_width)] * 2
    rows_of = pl.BlockSpec((rows, model_width), lambda step: (at, 0), pipeline_mode=pl.Buffered(1))
    columns = pl.BlockSpec((model_width, 256), lambda step: (0, step))
    tiles = pl.BlockSpec((rows, 256), lambda step: (0, step))
    specs = [rows_of, None, None, None, columns, columns]
    specs += [pl.BlockSpec((256, model_width), lambda step: (step, 0)), rows_of]
    operands = (tokens, part, far, gain, gate, up, down, cotangent)
    return call(ffn_kernel, steps, outs, [None, None, tiles, tiles, tiles, None, None], [], operands, specs, 0 * 10**9)


def middle_kernel(
    hidden_ref,
    part_ref,
    far_ref,
    cotangent_ref,
    gain_ref,
    gated_ref,
    square_a_ref,
    square_b_ref,
    gated_gain_ref,
    mixer_out_ref,
    attn_out_ref,
    grad_hidden_ref,
    grad_branch_ref,
    grad_rows_ref,
    grad_attended_ref,
    dot_ref,
    gain_sum_ref,
):
    hidden = hidden_ref[...]
    inv = inverse_rms(hidden)
    unit = hidden * inv
    grad_normed = part_ref[...] + far_ref[...]
    gain_sum_ref[0:1, :] = jnp.sum(grad_normed * unit, axis=0, keepdims=True)
    grad_unit = grad_normed * gain_ref[...]
    inner = jnp.mean(grad_unit * unit, axis=-1, keepdims=True)
    grad_hidden = cotangent_ref[...].astype(jnp.float32) + inv * (grad_unit - unit * inner)
    grad_hidden_ref[...] = grad_hidden
    grad_branch = grad_hidden.astype(jnp.bfloat16)
    grad_branch_ref[...] = grad_branch
    grad_rows = dot_nt(grad_branch, mixer_out_ref[...])
    grad_rows_ref[...] = grad_rows
    grad_attended_ref[...] = dot_nt(grad_branch, attn_out_ref[...]).astype(jnp.bfloat16)
    total = jnp.sum(grad_rows * gated_gain_ref[...] * gated_ref[...], axis=-1, keepdims=True)
    for i in range(hidden.shape[0] // LEN):
        at = block(i)
        inv_gated = lax.rsqrt((square_a_ref[:, at] + square_b_ref[:, at]) / DSSM + norm_eps)
        dot_ref[0:1, at] = jnp.broadcast_to(total[at], (LEN, LEN)).T[0:1] * inv_gated


def middle(chunks, hidden, part, far, cotangent, gain, gated, square_a, square_b, gated_gain, mixer_out, attn_out):
    rows, model_width = part.shape
    at = chunks[0] // len(chunks)
    width, inner = mixer_out.shape[0], attn_out.shape[0]
    outs = [
        f32(rows, model_width),
        b16(rows, model_width),
        f32(rows, width),
        b16(rows, inner),
        f32(1, rows),
        f32(8, model_width),
    ]
    rows_of = pl.BlockSpec((rows, model_width), lambda step: (at, 0), pipeline_mode=pl.Buffered(1))
    specs = [None, None, None, rows_of] + [None] * 7
    operands = (hidden, part, far, cotangent, gain, gated, square_a, square_b, gated_gain, mixer_out, attn_out)
    return call(middle_kernel, 1, outs, [None] * 6, [], operands, specs, 30 * 10**9)


def core_call(kernel, steps, core, out_shape, out_spec, scratch, operands, specs, flops, aliases=None):
    return pl.pallas_call(
        kernel,
        grid_spec=pltpu.PrefetchScalarGridSpec(
            num_scalar_prefetch=1, grid=(steps,), in_specs=specs, out_specs=out_spec, scratch_shapes=scratch
        ),
        out_shape=out_shape,
        compiler_params=pltpu.CompilerParams(vmem_limit_bytes=VMEM_BYTES),
        cost_estimate=pl.CostEstimate(flops=flops, bytes_accessed=0, transcendentals=0),
        input_output_aliases=aliases or {},
    )(core, *operands)


def clip_tile(rows, columns, first, last):
    return pl.BlockSpec((rows, columns), lambda step, core_ref: (0, jnp.clip(step - first, 0, last - first - 1)))


def ffn_weights_kernel(add, core_ref, *refs):
    refs = list(refs)
    normed_a, normed_b, act_a, act_b, gate_a, gate_b, up_a, up_b, cot_a, cot_b = refs[:10]
    far_ref = refs[10] if add else None
    out_ref, left_ref = refs[-2:]
    step = pl.program_id(0)
    third = pl.num_programs(0) // 3
    half = normed_a.shape[0]

    def turn(first, second):
        left_ref[:, :half] = first[...].T
        left_ref[:, half:] = second[...].T

    @pl.when(step == 0)
    def _():
        turn(normed_a, normed_b)

    @pl.when(step == 2 * third)
    def _():
        turn(act_a, act_b)

    def product(first, second):
        result = dot_nn(left_ref[:, :half], first[...]) + dot_nn(left_ref[:, half:], second[...])
        out_ref[...] = result + far_ref[...] if add else result

    @pl.when(step < third)
    def _():
        product(gate_a, gate_b)

    @pl.when((step >= third) & (step < 2 * third))
    def _():
        product(up_a, up_b)

    @pl.when(step >= 2 * third)
    def _():
        product(cot_a, cot_b)


def ffn_weights(core, far, normed_a, normed_b, act_a, act_b, gate_a, gate_b, up_a, up_b, cotangent):
    half, columns = normed_a.shape
    kept = columns // 2
    tile_width = 512
    third = columns // tile_width
    left = pl.BlockSpec((half, kept), lambda step, core_ref: (0, core_ref[0]), pipeline_mode=pl.Buffered(1))
    specs = [left] * 4 + [clip_tile(half, tile_width, 0, third)] * 2
    specs += [clip_tile(half, tile_width, third, 2 * third)] * 2

    def cot_rows(at):
        return pl.BlockSpec(
            (half, tile_width), lambda step, core_ref: (at, jnp.clip(step - 2 * third, 0, third - 1))
        )

    specs += [cot_rows(0), cot_rows(1)]
    out = pl.BlockSpec((kept, tile_width), lambda step, core_ref: (0, step))
    operands = [normed_a, normed_b, act_a, act_b, gate_a, gate_b, up_a, up_b, cotangent, cotangent]
    if far is not None:
        operands.append(far)
        specs.append(out)
    return core_call(
        functools.partial(ffn_weights_kernel, far is not None),
        3 * third,
        core,
        f32(kept, (3 if far is None else 4) * columns),
        out,
        [pltpu.VMEM((kept, 2 * half), jnp.bfloat16)],
        operands,
        specs,
        0 * 10**9,
    )


def outer_weights_kernel(add, core_ref, *refs):
    refs = list(refs)
    rows_a, rows_b, edge_a, edge_b, att_a, att_b, branch_a, branch_b = refs[:8]
    out_ref, left_ref = refs[-2:]
    half = rows_a.shape[0]
    middle_row = left_ref.shape[0] // 2

    @pl.when((pl.program_id(0) == 0) & (core_ref[0] == 0))
    def _():
        left_ref[:, :half] = rows_a[...].T
        left_ref[:, half:] = rows_b[...].T

    @pl.when((pl.program_id(0) == 0) & (core_ref[0] == 1))
    def _():
        left_ref[:middle_row, :half] = edge_a[...].T
        left_ref[:middle_row, half:] = edge_b[...].T
        left_ref[middle_row:, :half] = att_a[...].T
        left_ref[middle_row:, half:] = att_b[...].T

    result = dot_nn(left_ref[:, :half], branch_a[...]) + dot_nn(left_ref[:, half:], branch_b[...])
    out_ref[...] = result + refs[8][...] if add else result


def outer_weights(core, far, buffer, rows_a, rows_b, att_a, att_b, branch_a, branch_b):
    half, width = rows_a.shape
    model_width = branch_a.shape[1]
    kept = model_width // 2
    tile_width = 512
    steps = model_width // tile_width

    def fixed(shape, column=0):
        return pl.BlockSpec(shape, lambda step, core_ref: (0, column), pipeline_mode=pl.Buffered(1))

    specs = [fixed((half, kept))] * 2
    specs += [fixed((half, width - kept), kept // (width - kept))] * 2
    specs += [fixed(att_a.shape)] * 2 + [clip_tile(half, tile_width, 0, steps)] * 2
    operands = [rows_a, rows_b, rows_a, rows_b, att_a, att_b, branch_a, branch_b]
    out = pl.BlockSpec((kept, tile_width), lambda step, core_ref: (0, step))
    columns, aliases = model_width, {}
    if far is not None:
        operands += [far, buffer]
        specs += [out, pl.BlockSpec(memory_space=pl.ANY)]
        columns = buffer.shape[1]
        first = columns // tile_width - steps
        out = pl.BlockSpec((kept, tile_width), lambda step, core_ref: (0, first + step))
        aliases = {len(operands): 0}
    return core_call(
        functools.partial(outer_weights_kernel, far is not None),
        steps,
        core,
        f32(kept, columns),
        out,
        [pltpu.VMEM((kept, 2 * half), jnp.bfloat16)],
        operands,
        specs,
        0,
        aliases,
    )


PARTS = ((0, 3), (3, 5), (5, 7), (7, 9))


def mixer_weights_kernel(add, core_ref, *refs):
    refs = list(refs)
    normed_ref, gate_a, gate_b, conv_ref, query_a, query_b, state_ref, pair_ref, step_ref = refs[:9]
    far_ref, table_ref = refs[9:11] if add else (None, None)
    outs = refs[11:19] if add else refs[9:10]
    left_ref, result_ref = refs[-2:]
    step = pl.program_id(0)
    half = gate_a.shape[0]

    @pl.when(step == 0)
    def _():
        left_ref[...] = normed_ref[...].T

    def two(first, second):
        result_ref[...] = dot_nn(left_ref[:, :half], first[...]) + dot_nn(left_ref[:, half:], second[...])

    @pl.when(step < 3)
    def _():
        two(gate_a, gate_b)

    @pl.when((step >= 3) & (step < 6))
    def _():
        result_ref[...] = dot_nn(left_ref[...], conv_ref[...])

    @pl.when(step == 6)
    def _():
        two(query_a, query_b)

    @pl.when(step == 7)
    def _():
        result_ref[...] = dot_nn(left_ref[...], state_ref[...])

    @pl.when(step == 8)
    def _():
        result_ref[:, :LEN] = dot_nn(left_ref[...], pair_ref[...])
        steps = dot_nn(left_ref[...], step_ref[...])
        result_ref[:, LEN:] = steps + table_ref[...] if add else steps

    if not add:
        outs[0][...] = result_ref[...]
        return
    result_ref[...] = result_ref[...] + far_ref[...]
    for k, (first, last) in enumerate(PARTS):

        @pl.when((step >= first) & (step < last))
        def _():
            for side in range(2):
                out_ref = outs[2 * k + side]
                for q in range(2):
                    index = core_ref[1 + 4 * k + 2 * side + q]
                    if k < 2:
                        for y in range(4):
                            start = pl.multiple_of((4 * y + index) * 32, 32)
                            out_ref[(2 * y + q) * 32 : (2 * y + q + 1) * 32, :] = result_ref[pl.ds(start, 32), :]
                    else:
                        start = pl.multiple_of(index * LEN, LEN)
                        out_ref[q * LEN : (q + 1) * LEN, :] = result_ref[pl.ds(start, LEN), :]


def mixer_weights(core, far, table, normed, gate_a, gate_b, conv, query_a, query_b, state, pair, step):
    half = gate_a.shape[0]
    rows, model_width = normed.shape
    kept = model_width // 2
    tile_width = 256
    steps = 9

    def fixed(shape, column=0):
        return pl.BlockSpec(shape, lambda step, core_ref: (0, column), pipeline_mode=pl.Buffered(1))

    specs = [pl.BlockSpec((rows, kept), lambda step, core_ref: (0, core_ref[0]), pipeline_mode=pl.Buffered(1))]
    specs += [clip_tile(half, tile_width, 0, 3)] * 2 + [clip_tile(rows, tile_width, 3, 6)]
    specs += [fixed(query_a.shape)] * 2 + [fixed(state.shape), fixed(pair.shape), fixed(step.shape)]
    operands = [normed, gate_a, gate_b, conv, query_a, query_b, state, pair, step]
    out = pl.BlockSpec((kept, tile_width), lambda step, core_ref: (0, step))
    shape = f32(kept, steps * tile_width)
    if far is not None:
        operands += [far, table]
        specs += [out, fixed(table.shape)]
        out, shape = [], []
        for first, last in PARTS:
            out += [clip_tile(kept // 2, tile_width, first, last)] * 2
            shape += [f32(kept // 2, (last - first) * tile_width)] * 2
    return core_call(
        functools.partial(mixer_weights_kernel, far is not None),
        steps,
        core,
        shape,
        out,
        [pltpu.VMEM((kept, rows), jnp.bfloat16), pltpu.VMEM((kept, tile_width), jnp.float32)],
        operands,
        specs,
        30 * 10**9,
    )


def normed_back_kernel(
    gate_a,
    gate_b,
    conv_ref,
    query_a,
    query_b,
    state_ref,
    pair_ref,
    step_ref,
    wide_ref,
    small_ref,
    tokens_ref,
    whole_ref,
    out_ref,
    sum_ref,
    inv_ref,
):
    @pl.when(pl.program_id(0) == 0)
    def _():
        inv_ref[...] = jnp.broadcast_to(inverse_rms(whole_ref[...].astype(jnp.float32)), inv_ref.shape)

    half, width = gate_a.shape
    query_width = query_a.shape[1]
    gate_w, conv_w = wide_ref[:, :width], wide_ref[:, width:]
    state_w = small_ref[:, : 2 * LEN]
    query_w = small_ref[:, 2 * LEN : 2 * LEN + query_width]
    pair_w = small_ref[:, 2 * LEN + query_width : 3 * LEN + query_width]
    step_w = small_ref[:, 3 * LEN + query_width :]
    total = jnp.zeros((1, out_ref.shape[1]), jnp.float32)
    for k, (gate, query) in enumerate(((gate_a, query_a), (gate_b, query_b))):
        at = slice(k * half, (k + 1) * half)
        grad = dot_nt(gate[...], gate_w) + dot_nt(conv_ref[at, :], conv_w) + dot_nt(query[...], query_w)
        grad = grad + dot_nt(state_ref[at, :], state_w) + dot_nt(pair_ref[at, :], pair_w) + dot_nt(step_ref[at, :], step_w)
        out_ref[at, :] = grad
        unit = tokens_ref[at, :].astype(jnp.float32) * jnp.concatenate([inv_ref[at, :]] * 2, axis=1)
        total = total + jnp.sum(grad * unit, axis=0, keepdims=True)
    sum_ref[0:1, :] = total


def normed_back(gate_a, gate_b, conv, query_a, query_b, state, pair, step, wide_proj, small_proj, tokens):
    rows, model_width = tokens.shape
    tile_width = 256
    operands = (gate_a, gate_b, conv, query_a, query_b, state, pair, step, wide_proj, small_proj, tokens, tokens)

    def weights(count):
        return pl.BlockSpec((tile_width, count), lambda step: (step, 0))

    columns = pl.BlockSpec((rows, tile_width), lambda step: (0, step))
    specs = [None] * 8 + [weights(wide_proj.shape[1]), weights(small_proj.shape[1]), columns, None]
    out_specs = [columns, pl.BlockSpec((8, tile_width), lambda step: (0, step))]
    outs = [f32(rows, model_width), f32(8, model_width)]
    return call(
        normed_back_kernel,
        model_width // tile_width,
        outs,
        out_specs,
        [pltpu.VMEM((rows, LEN), jnp.float32)],
        operands,
        specs, 30 * 10**9)


def project_kernel(tokens_ref, gain_ref, wide_ref, small_ref, out_ref, normed_ref):
    step = pl.program_id(0)

    @pl.when(step == 0)
    def _():
        tokens = tokens_ref[...].astype(jnp.float32)
        normed_ref[...] = (tokens * inverse_rms(tokens) * gain_ref[...]).astype(jnp.bfloat16)

    @pl.when(step < pl.num_programs(0) - 1)
    def _():
        out_ref[...] = dot_nn(normed_ref[...], wide_ref[...])

    @pl.when(step == pl.num_programs(0) - 1)
    def _():
        out_ref[...] = dot_nn(normed_ref[...], small_ref[...])


def project(tokens, gain, wide_proj, small_proj):
    rows, model_width = tokens.shape
    count = small_proj.shape[1]
    wide_steps = wide_proj.shape[1] // count
    outs = [f32(rows, wide_proj.shape[1] + count), b16(rows, model_width)]
    wide = pl.BlockSpec((model_width, count), lambda step: (0, jnp.minimum(step, wide_steps - 1)))
    out = pl.BlockSpec((rows, count), lambda step: (0, step))
    operands = (tokens, gain, wide_proj, small_proj)
    return call(project_kernel, wide_steps + 1, outs, [out, None], [], operands, [None, None, wide, None], 0)


def assemble_kernel(source, mixer_proj_ref, query_ref, pair_ref, state_ref, step_ref):
    width = mixer_proj_ref.shape[2]
    start = 0
    mixer_proj_ref[:, 0, :] = source[:, start : start + width]
    start += width
    mixer_proj_ref[:, 1, :] = source[:, start : start + width]
    start += width
    query_ref[...] = source[:, start : start + query_ref.shape[1]]
    start += query_ref.shape[1]
    state_ref[...] = source[:, start : start + 2 * LEN]
    start += 2 * LEN
    pair_ref[:, 0, :] = source[:, start : start + LEN]
    step_ref[...] = source[:, start + LEN :]


def assemble(values, width, query_width):
    rows, columns = values.shape

    def plain(count):
        return pl.BlockSpec((LEN, count), lambda at: (at, 0))

    out_specs = [
        pl.BlockSpec((LEN, 2, width), lambda at: (at, 0, 0)),
        plain(query_width),
        pl.BlockSpec((LEN, 1, LEN), lambda at: (at, 0, 0)),
        plain(2 * LEN),
        plain(LEN),
    ]
    out_shape = [
        f32(rows, 2, width),
        f32(rows, query_width),
        f32(rows, 1, LEN),
        f32(rows, 2 * LEN),
        f32(rows, LEN),
    ]
    return call(assemble_kernel, rows // LEN, out_shape, out_specs, [], (values,), [plain(columns)], 0)


LINKS = {
    "A": [(0, 1), (1, 0), (2, 3), (3, 2)],
    "B": [(1, 2), (2, 1), (3, 0), (0, 3)],
}
ORDERS = (
    (("x", "A"), ("x", "B"), ("y", "A"), ("y", "B")),
    (("x", "B"), ("y", "A"), ("y", "B"), ("x", "A")),
    (("y", "A"), ("y", "B"), ("x", "A"), ("x", "B")),
    (("y", "B"), ("x", "A"), ("x", "B"), ("y", "A")),
)
AXIS = {"y": 0, "x": 1}


def take(values, index, axis):
    return lax.dynamic_slice_in_dim(values, index, 1, axis)


def halves(values, name, link, again):
    place, axis = lax.axis_index(name), AXIS[name]
    if again:
        index = place // 2 if link == "B" else place % 2
        return take(values, index, axis), take(values, 1 - index, axis)
    if link == "B":
        side = place // 2
        kept = lax.dynamic_slice_in_dim(values, 2 * side, 2, axis)
        return kept, lax.dynamic_slice_in_dim(values, 2 - 2 * side, 2, axis)
    side = ((place + 1) // 2) % 2
    kept = jnp.concatenate([take(values, side, axis), take(values, 3 - side, axis)], axis)
    return kept, jnp.concatenate([take(values, 1 - side, axis), take(values, 2 + side, axis)], axis)


def reduce_rows(pairs, steps):
    kept, sent, parts = [], [], pairs
    if steps[0] == 0:
        for k, (stays, goes) in enumerate(pairs):
            shape = (4, 2, 32, stays.shape[1]) if ORDERS[k][0][0] == "x" else (2, 4, 32, stays.shape[1])
            kept.append(stays.reshape(shape))
            sent.append(goes.reshape(shape))
    for step in steps:
        if step:
            kept, sent = [], []
            for k in range(4):
                name, link = ORDERS[k][step]
                again = name in [n for n, _ in ORDERS[k][:step]]
                stays, goes = halves(parts[k], name, link, again)
                kept.append(stays)
                sent.append(goes)
        sent = lax.optimization_barrier(tuple(sent))
        come = [lax.ppermute(sent[k], ORDERS[k][step][0], LINKS[ORDERS[k][step][1]]) for k in range(4)]
        come = lax.optimization_barrier(tuple(come))
        parts = [stays + more for stays, more in zip(kept, come)]
    return parts


def rope_tables(rows):
    half_size = HEAD_DIM // 2
    inverse = np.float32(rope_base) ** (-(2.0 * np.arange(half_size, dtype=np.float32)) / HEAD_DIM)
    angles = np.arange(rows, dtype=np.float32)[:, None] * inverse.astype(np.float32)[None, :]
    cosine, sine = np.cos(angles), np.sin(angles)
    return (
        np.concatenate([cosine] * 4, axis=1).astype(np.float32),
        np.concatenate([-sine, sine, -sine, sine], axis=1).astype(np.float32),
    )


def norm_backward(grad_unit, unit_rows, inv_rms):
    return inv_rms * (grad_unit - unit_rows * jnp.mean(grad_unit * unit_rows, axis=-1, keepdims=True))


def dot32(left, right):
    return jnp.dot(left, right, preferred_element_type=jnp.float32)


def after(value, *others):
    return lax.optimization_barrier((value, *others))[0]


def swap(values, name):
    return lax.ppermute(values, name, PAIR)


def exchange(values, name):
    return values + swap(values, name)


def core_rows(values, index):
    half = values.shape[1] // 2
    return lax.dynamic_slice_in_dim(values, index * half, half, 1)


def on_device(
    layer_input,
    segments,
    input_gain,
    mixer_proj,
    state_proj,
    step_proj,
    step_bias,
    decay_log,
    skip_gain,
    conv_kernel,
    conv_bias,
    state_kernel,
    state_bias,
    gated_gain,
    mixer_out,
    query_proj,
    key_value_weight,
    attn_out,
    ffn_gain,
    ffn_gate,
    ffn_up,
    ffn_down,
    cotangent,
):
    segment = segments.reshape(-1)
    rows, model_width = layer_input.shape
    width = mixer_proj.shape[2]
    heads = step_proj.shape[1]
    state_size = state_proj.shape[1] // 2
    query_width = query_proj.shape[1]
    pair_width = key_value_weight.shape[2]
    place = lax.axis_index("core")
    zh = lax.axis_index("zh")
    core = place.astype(jnp.int32).reshape(1)
    far_core = 1 - core
    cosine, sine = rope_tables(rows)
    select = np.arange(HEAD_ROWS)[:, None] == np.arange(width)[None, :] // HEAD_DIM
    select = jnp.asarray(select.astype(np.float32)).astype(jnp.bfloat16)
    seg_col, seg_row = segment[:, None], segment[None, :]
    keep = [jnp.ones((rows,), jnp.float32)]
    for lag in (1, 2, 3):
        previous = jnp.concatenate([jnp.full((lag,), -1, jnp.int32), segment[:-lag]])
        keep.append((previous == segment).astype(jnp.float32))
    keep = jnp.pad(jnp.stack(keep, axis=1), ((0, 8), (0, 4)))
    pad_heads = ((0, 0), (0, LEN - heads))
    rate_row = jnp.pad(-jnp.exp(decay_log)[None, :], pad_heads)
    step_bias_row = jnp.pad(step_bias[None, :], pad_heads)
    skip_row = jnp.repeat(skip_gain, HEAD_DIM)[None, :]
    gain_row = gated_gain[None, :]
    wide_proj = mixer_proj.reshape(model_width, 2 * width)
    small_proj = jnp.concatenate(
        [
            state_proj,
            query_proj,
            key_value_weight.reshape(model_width, pair_width),
            jnp.pad(step_proj, pad_heads),
        ],
        axis=1,
    )
    tokens = layer_input.astype(jnp.float32)
    wide_in, normed_input = project(layer_input, input_gain[None, :], wide_proj, small_proj)
    x, xb, slope, state, state_slope, cum, lag, cum_row, lag_row, step_row, sig_row, queries, pairs = scan_prep(
        width,
        wide_in,
        cosine,
        sine,
        keep,
        conv_kernel,
        conv_bias[None, :],
        state_kernel,
        state_bias[None, :],
        step_bias_row,
        rate_row,
    )

    blocks = rows // LEN
    late = tuple(range(blocks // 2, blocks))
    early = tuple(range(blocks // 2))
    half = {}
    for chunks in (late, early):
        h = {"span": slice(chunks[0] * LEN, (chunks[-1] + 1) * LEN)}
        h["y"], h["gated"], h["square"] = scan_forward(
            chunks, heads, wide_in, x, xb, state, cum, lag_row, seg_col, seg_row, skip_row
        )
        half[chunks] = h
    squares = jnp.concatenate([half[early]["square"], half[late]["square"]], axis=1)
    squares_far = swap(squares, "tensor")
    ready = squares
    for chunks in (late, early):
        h = half[chunks]
        h["attended"], h["lse"] = attention_forward(chunks, after(queries, ready), pairs, seg_col, seg_row)
        if chunks == late:
            squares_far = after(squares_far, h["lse"])
            squares_all = squares + squares_far
        h["square"], h["square_far"] = squares[:, h["span"]], squares_far[:, h["span"]]
        h["inv_gated"] = lax.rsqrt(squares_all[:, h["span"]].reshape(-1, 1) / DSSM + norm_eps)
        h["mixer_rows"] = (h["gated"] * h["inv_gated"] * gated_gain).astype(jnp.bfloat16)
        h["part"] = dot32(h["mixer_rows"], mixer_out) + dot32(h["attended"], attn_out)
        h["branch_far"] = swap(h["part"], "tensor")
        ready = h["part"]

    a, b = half[early], half[late]
    gain_ffn = ffn_gain[None, :]
    names = ("hidden", "normed", "activated", "grad_gate_rows", "grad_up_rows", "back", "down")
    for chunks in (late, early):
        h = half[chunks]
        far = h["branch_far"] if chunks == late else after(h["branch_far"], b["back"])
        operands = (layer_input, h["part"], far, gain_ffn, ffn_gate, ffn_up, ffn_down, cotangent)
        h.update(zip(names, ffn(chunks, *operands)))
        h["back_far"] = swap(h["back"], "tensor")

    sides = (after(a["normed"], b["back_far"]), b["normed"], a["activated"], b["activated"])
    sides += (a["grad_gate_rows"], b["grad_gate_rows"], a["grad_up_rows"], b["grad_up_rows"], cotangent)
    first = ffn_weights(far_core, None, *sides)
    first_far = swap(first, "core")
    for chunks in (late, early):
        h = half[chunks]
        far = after(h["back_far"], first)
        h["grad_hidden"], h["grad_branch"], h["grad_rows"], grad_attended, h["dot"], h["gain_sum"] = middle(
            chunks,
            h["hidden"],
            h["back"],
            far,
            cotangent,
            gain_ffn,
            h["gated"],
            h["square"],
            h["square_far"],
            gain_row,
            mixer_out,
            attn_out,
        )
        operands = (queries, pairs, grad_attended, h["lse"], seg_col, seg_row, cosine, sine)
        if chunks == late:
            h["grad_queries"], grad_keys, grad_values = attention_backward(chunks, False, *operands)
            first = ffn_weights(core, after(first_far, grad_keys), *sides)
        else:
            dots = jnp.concatenate([a["dot"], b["dot"]], axis=1)
            dots_far = swap(dots, "tensor")
            outer = (a["mixer_rows"], b["mixer_rows"], a["attended"], b["attended"])
            outer += (a["grad_branch"], b["grad_branch"])
            outer_far = swap(outer_weights(far_core, None, None, *outer), "core")
            h["grad_queries"], grad_pairs = attention_backward(chunks, True, *operands, grad_keys, grad_values)
    first = outer_weights(core, after(outer_far, grad_pairs), first, *outer)
    first_sum = lax.psum_scatter(first, ("y", "x"), scatter_dimension=0, tiled=True)
    dots_far = after(dots_far, first)
    for chunks in (late, early):
        h = half[chunks]
        h["grad_gate"], h["gy"], h["dx"], h["p"], h["grad_in"], h["grad_out"], h["sums"] = scan_backward(
            chunks,
            heads,
            h["grad_rows"],
            h["gated"],
            h["square"],
            h["square_far"],
            h["dot"],
            dots_far[:, h["span"]],
            gain_row,
            wide_in,
            h["y"],
            x,
            xb,
            state,
            lag,
            cum_row,
            skip_row,
            seg_col,
            seg_row,
            select,
        )
    pieces = [b["down"][:LEN], b["down"][LEN:], a["down"][:LEN], a["down"][LEN:]]
    pieces_far = [swap(after(piece, dots_far), "tensor") for piece in pieces[:3]]
    down = jnp.concatenate([a["down"], b["down"]], axis=0)
    ends = []
    for name in ("gy", "dx", "p", "grad_in", "grad_out"):
        ends += [a[name], b[name]]
    grad_conv, grad_state, grad_step, conv_sum, state_sum, step_sum = scan_end(
        heads,
        *ends,
        after(xb, pieces_far[0]),
        slope,
        state_slope,
        wide_in,
        wide_in,
        step_row,
        sig_row,
        rate_row,
        skip_row,
        keep,
        seg_col,
        seg_row,
        select,
        conv_kernel,
        state_kernel,
    )

    grads = (a["grad_gate"], b["grad_gate"], grad_conv, a["grad_queries"], b["grad_queries"])
    grads += (grad_state, grad_pairs, grad_step)
    tied = after(normed_input, pieces_far[1])
    second_far = swap(mixer_weights(far_core, None, None, tied, *grads), "core")
    partial_normed, input_gain_sum = normed_back(*grads, wide_proj, small_proj, layer_input)

    sums = a["sums"] + b["sums"]
    over_tensor = [input_gain_sum[0], state_sum[:4], state_sum[4]]
    alone = [
        step_sum[:heads, 0],
        step_sum[HEAD_ROWS : HEAD_ROWS + heads, 0],
        jnp.sum(sums[0].reshape(heads, HEAD_DIM), axis=1),
        conv_sum[:4],
        conv_sum[4],
        sums[1],
        a["gain_sum"][0] + b["gain_sum"][0],
    ]

    def packed(values):
        flat = jnp.concatenate([v.reshape(-1) for v in values])
        count = -(-flat.shape[0] // model_width)
        return jnp.pad(flat, (0, count * model_width - flat.shape[0])).reshape(count, model_width)

    def unpacked(table, values):
        flat, result, start = table.T.reshape(-1), [], 0
        for v in values:
            result.append(flat[start : start + v.size].reshape(v.shape))
            start += v.size
        return result

    tables = [packed(over_tensor), packed(alone)]
    shared_end = heads + tables[0].shape[0]
    table = jnp.concatenate(tables, axis=0)
    table_end = heads + table.shape[0]
    table = (core_rows(table, place) + swap(core_rows(table, 1 - place), "core")).T
    table = jnp.pad(table, ((0, 0), (heads, LEN - table_end)))
    spots = [core]
    for name, link in [order[0] for order in ORDERS]:
        at = lax.axis_index(name).astype(jnp.int32)
        side = ((at + 1) // 2) % 2 if link == "A" else at // 2
        spots.append(jnp.stack([side, 3 - side, 1 - side, 2 + side] if link == "A" else [2 * side, 2 * side + 1, 2 - 2 * side, 3 - 2 * side]))
    second = mixer_weights(jnp.concatenate(spots), after(second_far, pieces_far[2]), table, normed_input, *grads)
    second = list(second)
    at_state = 2 * width + query_width
    normed_far = [swap(partial_normed[k * LEN : (k + 1) * LEN], "tensor") for k in range(rows // LEN)]
    second[1] = after(second[1], normed_far[0])
    parts = reduce_rows([(second[2 * k], second[2 * k + 1]) for k in range(4)], (0,))
    parts[0] = after(parts[0], normed_far[1])
    first_own = exchange(after(first_sum, parts[0]), "zh")
    first_all = lax.all_gather(first_own, ("core", "y", "x"), axis=0, tiled=True)
    parts = reduce_rows(parts, (1,))
    parts[0] = after(parts[0], normed_far[2])
    parts = reduce_rows(parts, (2,))
    parts[0] = after(parts[0], normed_far[3])
    parts = reduce_rows(parts, (3,))
    second = jnp.concatenate([p.reshape(32, -1) for p in parts], axis=1)
    both = second[:, at_state:]
    lane = np.arange(both.shape[1])
    in_table = lane - 2 * state_size - pair_width
    is_shared = (lane < 2 * state_size) | ((in_table >= heads) & (in_table < shared_end))
    diagonal = [(0, 3), (3, 0), (1, 2), (2, 1)]
    more = swap(both, "tensor") + lax.ppermute(both, ("zh", "tensor"), diagonal)
    second = exchange(second, "zh")
    summed = second[:, at_state:] + jnp.where(is_shared[None, :], more, 0.0)
    second = jnp.concatenate([second[:, :at_state], summed], axis=1)
    second = after(second, first_all)
    pieces_far.append(swap(after(pieces[3], second), "tensor"))
    second = lax.all_gather(second, ("core", "y", "x"), axis=0, tiled=True)
    grad_mixer_proj, grad_query_proj, grad_keyval, grad_state_proj, step_block = assemble(second, width, query_width)

    def whole(name):
        return jnp.concatenate([a[name], b[name]], axis=0)

    grad_hidden = whole("grad_hidden")
    grad_normed = partial_normed + jnp.concatenate(normed_far, axis=0)
    inv_rms_in = inverse_rms(tokens)
    unit_in = tokens * inv_rms_in
    input_grad = grad_hidden + norm_backward(grad_normed * input_gain, unit_in, inv_rms_in)
    down_far = jnp.concatenate([pieces_far[2], pieces_far[3], pieces_far[0], pieces_far[1]], axis=0)
    layer_output = (whole("hidden") + (down + down_far)).astype(jnp.bfloat16)

    small_shared = unpacked(step_block[:, heads:shared_end], over_tensor)
    small_alone = unpacked(step_block[:, shared_end:table_end], alone)
    return (
        layer_output,
        input_grad,
        small_shared[0],
        grad_mixer_proj,
        grad_state_proj,
        step_block[:, :heads],
        small_alone[0],
        small_alone[1],
        small_alone[2],
        small_alone[3],
        small_alone[4],
        small_shared[1],
        small_shared[2],
        small_alone[5],
        first_all[:width, 3 * model_width :],
        grad_query_proj,
        grad_keyval,
        first_all[width:, 3 * model_width :],
        small_alone[6],
        first_all[:, :model_width],
        first_all[:, model_width : 2 * model_width],
        first_all[:, 2 * model_width : 3 * model_width],
    )


def solution(mesh):
    dp, whole_spec, columns = P(DP, None), P(), P(None, "tensor")
    per_channel, middle = P("tensor"), P(None, "tensor", None)
    last, by_rows = P(None, None, "tensor"), P("tensor", None)
    weights = (
        whole_spec,
        last,
        whole_spec,
        columns,
        per_channel,
        per_channel,
        per_channel,
        columns,
        per_channel,
        whole_spec,
        whole_spec,
        per_channel,
        by_rows,
        columns,
        middle,
        by_rows,
        whole_spec,
        columns,
        columns,
        by_rows,
    )
    mesh = jax.sharding.Mesh(mesh.devices.reshape(4, 2, 4, 2, 2), (*DP, "tensor"))
    return jax.shard_map(
        on_device, mesh=mesh, in_specs=(dp, dp, *weights, dp), out_specs=(dp, dp, *weights), check_vma=False
    )
```

```python
import functools

import jax
import jax.numpy as jnp
import numpy as np
from jax import lax
from jax.experimental import pallas as pl
from jax.experimental.pallas import tpu as pltpu
from jax.sharding import PartitionSpec as P

HEAD_DIM = 64
DSSM = 1536
DP = ("y", "zh", "x", "core")
PAIR = [(0, 1), (1, 0)]
LOG2E = 1.4426950408889634
hidden_bias = -1e30
norm_eps = 1e-05
rope_base = 10000.0
LEN = 128


def dot_nn(left, right):
    return lax.dot_general(
        left, right, (((1,), (0,)), ((), ())), preferred_element_type=jnp.float32
    )


def dot_nt(left, right):
    return lax.dot_general(
        left, right, (((1,), (1,)), ((), ())), preferred_element_type=jnp.float32
    )


def dot_tn(left, right):
    return lax.dot_general(
        left, right, (((0,), (0,)), ((), ())), preferred_element_type=jnp.float32
    )


def two_terms(v):
    high = v.astype(jnp.bfloat16)
    return high, (v - high.astype(jnp.float32)).astype(jnp.bfloat16)


def three_dots(dot, left, right):
    left_high, left_low = two_terms(left)
    right_high, right_low = two_terms(right)
    return dot(left_high, right_high) + dot(left_high, right_low) + dot(left_low, right_high)


def sigmoid(v):
    return 1.0 / (1.0 + jnp.exp(-v))


def block(index):
    return slice(index * LEN, (index + 1) * LEN)


def lane_iota(rows=LEN):
    return lax.broadcasted_iota(jnp.int32, (rows, LEN), 1)


def turned(row):
    return jnp.broadcast_to(row, (LEN, LEN)).T


def mask_ts(seg_row, i, j):
    same = turned(seg_row[:, block(i)]) == seg_row[:, block(j)]
    if i != j:
        return same
    down = lax.broadcasted_iota(jnp.int32, (LEN, LEN), 0)
    return same & (down >= lane_iota())


def mask_st(seg_row, j, i):
    same = turned(seg_row[:, block(j)]) == seg_row[:, block(i)]
    if i != j:
        return same
    down = lax.broadcasted_iota(jnp.int32, (LEN, LEN), 0)
    return same & (down <= lane_iota())


def conv_rows(pad_ref, keep_ref, kernel, bias, start, lanes):
    summed = bias + kernel[3:4] * pad_ref[8 + start : 8 + start + LEN, lanes]
    for lag in (1, 2, 3):
        moved = pad_ref[8 + start - lag : 8 + start - lag + LEN, lanes]
        summed = summed + kernel[3 - lag : 4 - lag] * (moved * keep_ref[lag - 1, start : start + LEN, :])
    return summed


def widen(seg_row_ref, wide_ref, pad_ref):
    rows = seg_row_ref.shape[1]
    pad_ref[0:8, :] = jnp.full((8, LEN), -1.0, jnp.float32)
    for i in range(rows // LEN):
        pad_ref[8 + i * LEN : 8 + (i + 1) * LEN, :] = turned(seg_row_ref[:, block(i)])
    for lag in (1, 2, 3):
        same = pad_ref[8 : rows + 8, :] == pad_ref[8 - lag : rows + 8 - lag, :]
        wide_ref[lag - 1, 0:rows, :] = jnp.where(same, 1.0, 0.0)
        wide_ref[lag - 1, rows : rows + 8, :] = jnp.zeros((8, LEN), jnp.float32)


def prep_kernel(
    conv_ref,
    small_ref,
    cos_ref,
    sin_ref,
    seg_row_ref,
    table_ref,
    params_ref,
    x_ref,
    xb_ref,
    slope_ref,
    state_ref,
    state_slope_ref,
    cum_ref,
    lag_ref,
    cum_row_ref,
    lag_row_ref,
    step_row_ref,
    sig_row_ref,
    q_ref,
    kv_ref,
    pad_ref,
    wide_ref,
):
    rows = conv_ref.shape[0]
    blocks = rows // LEN

    @pl.when(pl.program_id(0) == 0)
    def _():
        widen(seg_row_ref, wide_ref, pad_ref)
        pad_ref[0:8, :] = jnp.zeros((8, LEN), jnp.float32)
        for c in range(2):
            pad_ref[8 : rows + 8, :] = small_ref[:, block(c)]
            for i in range(blocks):
                pre = conv_rows(
                    pad_ref, wide_ref, params_ref[8:12, block(c)], params_ref[12:13, block(c)], i * LEN, slice(0, LEN)
                )
                sig = sigmoid(pre)
                state_ref[block(i), block(c)] = pre * sig
                state_slope_ref[block(i), block(c)] = sig * (1.0 + pre * (1.0 - sig))

    @pl.when(pl.program_id(0) == 1)
    def _():
        down = lax.broadcasted_iota(jnp.int32, (LEN, LEN), 0)
        lower = jnp.where(down >= lane_iota(), 1.0, 0.0).astype(jnp.bfloat16)
        left_half = lane_iota() < HEAD_DIM
        carry = jnp.zeros((1, LEN), jnp.float32)
        heads = cum_row_ref.shape[0]
        for i in range(blocks):
            argument = small_ref[block(i), block(5)] + params_ref[13:14, :LEN]
            tail = jnp.exp(-jnp.abs(argument))
            grown = jnp.where(tail < 1e-3, tail - 0.5 * tail * tail, jnp.log(1.0 + tail))
            step = jnp.maximum(argument, 0.0) + grown
            scaled = step * params_ref[14:15, :LEN] * LOG2E
            first, rest = two_terms(scaled)
            last = scaled - first.astype(jnp.float32) - rest.astype(jnp.float32)
            cum = dot_nn(lower, first) + dot_nn(lower, rest) + dot_nn(lower, last.astype(jnp.bfloat16)) + carry
            carry = cum[LEN - 1 : LEN, :]
            lag = cum - jnp.log(step) * LOG2E
            cum_ref[block(i), :] = cum
            lag_ref[block(i), :] = lag
            cum_t, lag_t = cum.T, lag.T
            step_row_ref[:, block(i)] = step.T[:heads]
            sig_row_ref[:, block(i)] = sigmoid(argument).T[:heads]
            for h in range(heads):
                cum_row_ref[h, :, block(i)] = cum_t[h : h + 1]
                lag_row_ref[h, :, block(i)] = lag_t[h : h + 1]
            cosine, sine = cos_ref[block(i), :], sin_ref[block(i), :]
            kv = small_ref[block(i), block(4)]
            kv_ref[block(i), :] = jnp.where(left_half, rotate_tile(kv, cosine, sine), kv).astype(jnp.bfloat16)
            for p in range(q_ref.shape[1] // LEN):
                q_ref[block(i), block(p)] = rotate_tile(small_ref[block(i), block(2 + p)], cosine, sine).astype(
                    jnp.bfloat16
                )

    for sub in range(GROUP):
        lanes = block(sub)
        pad_ref[8 : rows + 8, :] = conv_ref[:, lanes]
        for i in range(blocks):
            pre = conv_rows(pad_ref, wide_ref, table_ref[0:4, lanes], table_ref[4:5, lanes], i * LEN, slice(0, LEN))
            sig = sigmoid(pre)
            x = pre * sig
            x_ref[block(i), lanes] = x
            xb_ref[block(i), lanes] = x.astype(jnp.bfloat16)
            slope_ref[block(i), lanes] = sig * (1.0 + pre * (1.0 - sig))


def rotate_tile(v, cosine, sine):
    first = lax.rem(lane_iota(v.shape[0]), HEAD_DIM) < HEAD_DIM // 2
    swapped = jnp.where(first, pltpu.roll(v, LEN - HEAD_DIM // 2, 1), pltpu.roll(v, HEAD_DIM // 2, 1))
    return v * cosine + swapped * sine


def scan_kernel(
    chunks,
    heads,
    gate_ref,
    x_ref,
    xb_ref,
    state_ref,
    cum_ref,
    lag_row_ref,
    seg_row_ref,
    table_ref,
    y_ref,
    gated_ref,
    row_ref,
    wide_ref,
    cross_ref,
    bias_ref,
    mix_ref,
    square_ref,
):
    step = pl.program_id(0)
    first = chunks[0]
    pairs = [(i, j) for i in chunks for j in range(max(0, i - 2), i + 1)]
    left_half = lane_iota() < HEAD_DIM

    @pl.when(step == 0)
    def _():
        for h in range(heads):
            for i in chunks:
                wide_ref[h, block(i - first), :] = jnp.broadcast_to(cum_ref[block(i), h : h + 1], (LEN, LEN))
        for i in chunks:
            low = max(0, i - 2)
            cross = three_dots(dot_nt, state_ref[block(i), LEN:], state_ref[low * LEN : (i + 1) * LEN, :LEN])
            for n, (i2, j) in enumerate(pairs):
                if i2 == i:
                    cross_ref[n] = cross[:, block(j - low)]
                    allowed = mask_ts(seg_row_ref, i, j)
                    bias_ref[n] = jnp.where(allowed, 0.0, hidden_bias)
        square_ref[...] = jnp.zeros(square_ref.shape, jnp.float32)

    tiles = (gate_ref, x_ref, xb_ref, table_ref.at[5:6], y_ref, gated_ref)

    def head_pair(hp, gate_ref, x_ref, xb_ref, skip_ref, y_ref, gated_ref):
        for i in chunks:
            at = block(i - first)
            low = max(0, i - 2)
            for n, (i2, j) in enumerate(pairs):
                if i2 != i:
                    continue
                for e in range(2):
                    spread = wide_ref[2 * hp + e, at, :] - lag_row_ref[2 * hp + e, :, block(j)]
                    decay = jnp.exp2(spread + bias_ref[n])
                    mix_ref[i - first, block(e), block(j - low)] = (decay * cross_ref[n]).astype(jnp.bfloat16)
            both = dot_nn(mix_ref[i - first, :, : (i + 1 - low) * LEN], xb_ref[low * LEN : (i + 1) * LEN, :])
            y = jnp.where(left_half, both[:LEN], both[LEN:])
            y_ref[at, :] = y
            gate = gate_ref[at, :]
            gated = (y + skip_ref[...] * x_ref[at, :]) * (gate * sigmoid(gate))
            gated_ref[at, :] = gated
            square_ref[at, :] = square_ref[at, :] + gated * gated

    for sub in range(GROUP):
        head_pair(GROUP * step + sub, *[t.at[:, block(sub)] for t in tiles])

    @pl.when(step == pl.num_programs(0) - 1)
    def _():
        for i in chunks:
            at = block(i - first)
            total = jnp.sum(square_ref[at, :], axis=1, keepdims=True)
            row_ref[0:1, at] = jnp.broadcast_to(total, (LEN, LEN)).T[0:1]


def attention_kernel(chunks, q_ref, kv_ref, seg_row_ref, out_ref, lse_ref):
    scale = HEAD_DIM ** (-0.5) * LOG2E
    first = chunks[0]
    left_half = lane_iota() < HEAD_DIM
    zero = jnp.zeros((LEN, LEN), jnp.bfloat16)
    lse_ref[...] = jnp.zeros(lse_ref.shape, jnp.float32)
    for i in chunks:
        at = block(i - first)
        low = max(0, i - 2) * LEN
        span = (i + 1) * LEN - low
        allowed = jnp.concatenate([mask_ts(seg_row_ref, i, j) for j in range(low // LEN, i + 1)], axis=1)
        keys = kv_ref[low : low + span, :]
        swapped = pltpu.roll(keys.astype(jnp.float32), HEAD_DIM, 1).astype(jnp.bfloat16)
        for p in range(q_ref.shape[1] // LEN):
            queries = q_ref[block(i), block(p)]
            result = []
            for e in range(2):
                masked = jnp.where(left_half == (e == 0), queries, zero)
                scores = dot_nt(masked, keys if e == 0 else swapped) * scale
                scores = jnp.where(allowed, scores, hidden_bias)
                top = jnp.max(scores, axis=1, keepdims=True)
                weights = jnp.exp2(scores - top)
                total = jnp.sum(weights, axis=1, keepdims=True)
                probs = (weights * (1.0 / total)).astype(jnp.bfloat16)
                result.append(dot_nn(probs, swapped if e == 0 else keys))
                lse = jnp.broadcast_to(top + jnp.log(total) * LOG2E, (LEN, LEN))
                lse_ref[2 * p + e : 2 * p + e + 1, at] = lse.T[0:1]
            out_ref[at, block(p)] = jnp.where(left_half, result[0], result[1]).astype(jnp.bfloat16)


def attention_back_kernel(chunks, final, *refs):
    q_ref, kv_ref, do_ref, lse_ref, seg_row_ref, cos_ref, sin_ref = refs[:7]
    if final:
        dk_in_ref, dv_in_ref, dq_ref, dkv_ref, dk_ref, dv_ref, turned_ref, key_t_ref = refs[7:]
    else:
        dq_ref, dk_ref, dv_ref, turned_ref, key_t_ref = refs[7:]
    scale = HEAD_DIM ** (-0.5)
    blocks = q_ref.shape[0] // LEN
    first = chunks[0]
    left_half = lane_iota() < HEAD_DIM
    zero = jnp.zeros((LEN, LEN), jnp.bfloat16)
    for i in range(chunks[-1] + 1):
        kv = kv_ref[block(i), :].astype(jnp.float32)
        turned_ref[block(i), :] = pltpu.roll(kv, HEAD_DIM, 1).astype(jnp.bfloat16)
        key_t_ref[:, block(i)] = kv.T[:HEAD_DIM].astype(jnp.bfloat16)
    if final:
        dk_ref[...] = dk_in_ref[...]
        dv_ref[...] = dv_in_ref[...]
    else:
        dk_ref[...] = jnp.zeros(dk_ref.shape, jnp.float32)
        dv_ref[...] = jnp.zeros(dv_ref.shape, jnp.float32)
    for i in chunks:
        at = block(i - first)
        low = max(0, i - 2) * LEN
        span = (i + 1) * LEN - low
        window = slice(low, low + span)
        allowed = jnp.concatenate([mask_st(seg_row_ref, j, i) for j in range(low // LEN, i + 1)], axis=0)
        keys, swapped = kv_ref[window, :], turned_ref[window, :]
        for p in range(q_ref.shape[1] // LEN):
            queries, douts = q_ref[block(i), block(p)], do_ref[at, block(p)]
            back = []
            for e in range(2):
                side = left_half == (e == 0)
                q_half = jnp.where(side, queries, zero)
                do_half = jnp.where(side, douts, zero)
                h = 2 * p + e
                scores = dot_nt(keys if e == 0 else swapped, q_half) * (scale * LOG2E)
                probs = jnp.exp2(jnp.where(allowed, scores, hidden_bias) - lse_ref[h : h + 1, at])
                dprobs = dot_nt(swapped if e == 0 else keys, do_half)
                inner = jnp.sum(probs * dprobs, axis=0, keepdims=True)
                dscores = (probs * (dprobs - inner)).astype(jnp.bfloat16)
                dv_ref[window, :] = dv_ref[window, :] + dot_nn(probs.astype(jnp.bfloat16), do_half)
                dk_ref[window, :] = dk_ref[window, :] + dot_nn(dscores, q_half)
                back.append(dot_nn(key_t_ref[:, window], dscores))
            dq = jnp.concatenate(back, axis=0).T * scale
            dq_ref[at, block(p)] = rotate_tile(dq, cos_ref[block(i), :], -sin_ref[block(i), :]).astype(jnp.bfloat16)
    if not final:
        return
    for i in range(blocks):
        dk = dk_ref[block(i), :]
        dk = (dk + pltpu.roll(dk, HEAD_DIM, 1)) * scale
        dk = rotate_tile(dk, cos_ref[block(i), :], -sin_ref[block(i), :])
        dv = dv_ref[block(i), :]
        dv = dv + pltpu.roll(dv, HEAD_DIM, 1)
        dkv_ref[block(i), :] = jnp.where(left_half, dk, dv).astype(jnp.bfloat16)


def scan_back_kernel(
    chunks,
    heads,
    gmr_ref,
    gated_ref,
    square_a_ref,
    square_b_ref,
    dot_a_ref,
    dot_b_ref,
    table_ref,
    gate_ref,
    y_ref,
    x_ref,
    xb_ref,
    state_ref,
    lag_ref,
    cum_row_ref,
    seg_row_ref,
    select_ref,
    dgate_ref,
    gy_ref,
    dx_ref,
    p_ref,
    grad_in_ref,
    grad_out_ref,
    sums_ref,
    gyb_ref,
    wide_ref,
    cross_ref,
    bias_ref,
    dcross_ref,
    inv_wide_ref,
    dot_wide_ref,
    inner_ref,
    mix_ref,
):
    step = pl.program_id(0)
    first = chunks[0]
    sources = chunks[-1] + 1
    left_half = lane_iota() < HEAD_DIM
    zero = jnp.zeros((LEN, LEN), jnp.bfloat16)
    spans = [(j, max(j, first), min(j + 3, sources)) for j in range(sources)]
    pairs = [(j, i) for j, start, stop in spans for i in range(start, stop)]

    @pl.when(step == 0)
    def _():
        for i in chunks:
            at = block(i - first)
            square = (square_a_ref[:, at] + square_b_ref[:, at]) / DSSM
            inv = lax.rsqrt(square + norm_eps)
            inv_wide_ref[at, :] = jnp.broadcast_to(inv, (LEN, LEN)).T
            dot = (dot_a_ref[:, at] + dot_b_ref[:, at]) / DSSM
            dot_wide_ref[at, :] = jnp.broadcast_to(dot, (LEN, LEN)).T
        p_ref[...] = jnp.zeros(p_ref.shape, jnp.float32)
        for h in range(heads):
            wide_ref[h] = jnp.broadcast_to(lag_ref[: sources * LEN, h : h + 1], (sources * LEN, LEN))
        for j, start, stop in spans:
            cross = three_dots(dot_nt, state_ref[block(j), :LEN], state_ref[start * LEN : stop * LEN, LEN:])
            for n, (j2, i) in enumerate(pairs):
                if j2 == j:
                    cross_ref[n] = cross[:, block(i - start)]
                    allowed = mask_st(seg_row_ref, j, i)
                    bias_ref[n] = jnp.where(allowed, 0.0, hidden_bias)
                    dcross_ref[n] = jnp.zeros((LEN, LEN), jnp.float32)

    tiles = (
        gmr_ref,
        gated_ref,
        table_ref.at[6:7],
        gate_ref,
        y_ref,
        x_ref,
        xb_ref,
        table_ref.at[5:6],
        dgate_ref,
        gy_ref,
        dx_ref,
        sums_ref,
    )

    def head_pair(
        hp,
        select,
        gmr_ref,
        gated_ref,
        gain_ref,
        gate_ref,
        y_ref,
        x_ref,
        xb_ref,
        skip_ref,
        dgate_ref,
        gy_ref,
        dx_ref,
        sums_ref,
    ):
        skip = skip_ref[...]
        gain = gain_ref[...]
        skip_sum = jnp.zeros((1, LEN), jnp.float32)
        gain_sum = jnp.zeros((1, LEN), jnp.float32)
        for i in chunks:
            at = block(i - first)
            inv = inv_wide_ref[at, :]
            unit = gated_ref[at, :] * inv
            rows_grad = gmr_ref[at, :]
            grad = inv * (rows_grad * gain - unit * dot_wide_ref[at, :])
            gate = gate_ref[at, :]
            sig = sigmoid(gate)
            y = y_ref[at, :]
            x = x_ref[at, :]
            gy = grad * (gate * sig)
            dgate_ref[at, :] = (grad * (y + skip * x) * (sig * (1.0 + gate * (1.0 - sig)))).astype(jnp.bfloat16)
            gyb = gy.astype(jnp.bfloat16)
            gy_ref[at, :] = gy
            gyb_ref[at, :] = gyb
            high, rest = two_terms(gyb.astype(jnp.float32) * y)
            p_ref[:, at] = p_ref[:, at] + dot_nt(select, high) + dot_nt(select, rest)
            skip_sum = skip_sum + jnp.sum(gy * x, axis=0, keepdims=True)
            gain_sum = gain_sum + jnp.sum(rows_grad * unit, axis=0, keepdims=True)
        sums_ref[0:1, :] = skip_sum
        sums_ref[1:2, :] = gain_sum

        for j, start, stop in spans:
            x_pair = xb_ref[block(j), :]
            x_both = jnp.concatenate([jnp.where(left_half, x_pair, zero), jnp.where(left_half, zero, x_pair)], axis=0)
            wide = (stop - start) * LEN
            gy_rows = gyb_ref[(start - first) * LEN : (stop - first) * LEN, :]
            inner_ref[:, :wide] = dot_nt(x_both, gy_rows)
            for n, (j2, i) in enumerate(pairs):
                if j2 != j:
                    continue
                grown = dcross_ref[n]
                for e in range(2):
                    spread = cum_row_ref[2 * hp + e, :, block(i)] - wide_ref[2 * hp + e, block(j), :]
                    decay = jnp.exp2(spread + bias_ref[n])
                    grown = grown + inner_ref[block(e), block(i - start)] * decay
                    mix_ref[block(e), block(i - start)] = (decay * cross_ref[n]).astype(jnp.bfloat16)
                dcross_ref[n] = grown
            both = dot_nn(mix_ref[:, :wide], gy_rows)
            dx_ref[block(j), :] = jnp.where(left_half, both[:LEN], both[LEN:])

    for sub in range(GROUP):
        head_pair(GROUP * step + sub, select_ref[:, block(sub)], *[t.at[:, block(sub)] for t in tiles])

    @pl.when(step == pl.num_programs(0) - 1)
    def _():
        grad_out = {i: jnp.zeros((LEN, LEN), jnp.float32) for i in chunks}
        for j in range(sources):
            grad_in = jnp.zeros((LEN, LEN), jnp.float32)
            for n, (j2, i) in enumerate(pairs):
                if j2 != j:
                    continue
                high, rest = two_terms(dcross_ref[n])
                out_high, out_rest = two_terms(state_ref[block(i), LEN:])
                in_high, in_rest = two_terms(state_ref[block(j), :LEN])
                grad_in = grad_in + dot_nn(high, out_high) + dot_nn(high, out_rest) + dot_nn(rest, out_high)
                grad_out[i] = grad_out[i] + dot_tn(high, in_high) + dot_tn(high, in_rest) + dot_tn(rest, in_high)
            grad_in_ref[block(j), :] = grad_in
        for i in chunks:
            grad_out_ref[block(i - first), :] = grad_out[i]


def conv_back(grad_ref, value_ref, keep_ref, taps, out_ref, sum_ref, lanes, blocks):
    totals = [jnp.zeros((1, LEN), jnp.float32) for _ in range(5)]
    for i in range(blocks):
        here = grad_ref[i * LEN : (i + 1) * LEN, :]
        grad = taps[3:4] * here
        totals[4] = totals[4] + jnp.sum(here, axis=0, keepdims=True)
        totals[3] = totals[3] + jnp.sum(here * value_ref[8 + i * LEN : 8 + (i + 1) * LEN, :], axis=0, keepdims=True)
        for lag in (1, 2, 3):
            ahead = grad_ref[i * LEN + lag : (i + 1) * LEN + lag, :]
            grad = grad + taps[3 - lag : 4 - lag] * (ahead * keep_ref[lag - 1, i * LEN + lag : (i + 1) * LEN + lag, :])
            moved = value_ref[8 + i * LEN - lag : 8 + (i + 1) * LEN - lag, :]
            masked = here * keep_ref[lag - 1, i * LEN : (i + 1) * LEN, :]
            totals[3 - lag] = totals[3 - lag] + jnp.sum(masked * moved, axis=0, keepdims=True)
        out_ref[block(i), lanes] = grad.astype(jnp.bfloat16)
    for tap in range(5):
        sum_ref[tap : tap + 1, lanes] = totals[tap]


def scan_end_kernel(
    heads,
    gy_a_ref,
    gy_b_ref,
    dx_a_ref,
    dx_b_ref,
    p_a_ref,
    p_b_ref,
    in_a_ref,
    in_b_ref,
    out_a_ref,
    out_b_ref,
    xb_ref,
    slope_ref,
    state_slope_ref,
    conv_ref,
    small_ref,
    step_row_ref,
    sig_row_ref,
    seg_row_ref,
    select_ref,
    table_ref,
    params_ref,
    dconv_ref,
    dstate_ref,
    dstep_ref,
    conv_sum_ref,
    state_sum_ref,
    step_sum_ref,
    grad_pad_ref,
    value_pad_ref,
    wide_ref,
    q_ref,
    flow_ref,
):
    step = pl.program_id(0)
    rows = conv_ref.shape[0]
    blocks = rows // LEN
    half = rows // 2
    count = flow_ref.shape[0]

    @pl.when(step == 0)
    def _():
        value_pad_ref[0:8, :] = jnp.zeros((8, LEN), jnp.float32)
        grad_pad_ref[rows : rows + 8, :] = jnp.zeros((8, LEN), jnp.float32)
        widen(seg_row_ref, wide_ref, value_pad_ref)
        value_pad_ref[0:8, :] = jnp.zeros((8, LEN), jnp.float32)
        q_ref[...] = jnp.zeros(q_ref.shape, jnp.float32)
        for c in range(2):
            if c == 0:
                grad_pad_ref[0:half, :] = (in_a_ref[...] + in_b_ref[0:half, :]) * state_slope_ref[0:half, block(c)]
                grad_pad_ref[half:rows, :] = in_b_ref[half:rows, :] * state_slope_ref[half:rows, block(c)]
            else:
                grad_pad_ref[0:half, :] = out_a_ref[...] * state_slope_ref[0:half, block(c)]
                grad_pad_ref[half:rows, :] = out_b_ref[...] * state_slope_ref[half:rows, block(c)]
            value_pad_ref[8 : rows + 8, :] = small_ref[:, block(c)]
            conv_back(
                grad_pad_ref,
                value_pad_ref,
                wide_ref,
                params_ref[8:12, block(c)],
                dstate_ref,
                state_sum_ref,
                block(c),
                blocks,
            )

    tiles = (
        gy_a_ref,
        gy_b_ref,
        dx_a_ref,
        dx_b_ref,
        xb_ref,
        slope_ref,
        conv_ref,
        table_ref.at[5:6],
        dconv_ref,
        conv_sum_ref,
    )

    def head_pair(
        select,
        taps,
        gy_a_ref,
        gy_b_ref,
        dx_a_ref,
        dx_b_ref,
        xb_ref,
        slope_ref,
        conv_ref,
        skip_ref,
        dconv_ref,
        conv_sum_ref,
    ):
        for j in range(blocks):
            dx = dx_b_ref[block(j), :]
            if j < blocks // 2:
                dx = dx + dx_a_ref[block(j), :]
                gy = gy_a_ref[block(j), :]
            else:
                gy = gy_b_ref[block(j - blocks // 2), :]
            high, rest = two_terms(dx * xb_ref[block(j), :].astype(jnp.float32))
            q_ref[:, block(j)] = q_ref[:, block(j)] + dot_nt(select, high) + dot_nt(select, rest)
            grad_pad_ref[block(j), :] = (dx + gy * skip_ref[...]) * slope_ref[block(j), :]
        value_pad_ref[8 : rows + 8, :] = conv_ref[...]
        conv_back(
            grad_pad_ref, value_pad_ref, wide_ref, taps, dconv_ref, conv_sum_ref, slice(0, LEN), blocks
        )

    for sub in range(GROUP):
        head_pair(select_ref[:, block(sub)], table_ref[0:4, block(sub)], *[t.at[:, block(sub)] for t in tiles])

    @pl.when(step == pl.num_programs(0) - 1)
    def _():
        q = q_ref[...]
        flow_ref[:, 0:half] = p_a_ref[...] - q[:, 0:half]
        flow_ref[:, half:rows] = p_b_ref[...] - q[:, half:rows]
        rate = turned(params_ref[14:15, :LEN])[:count]
        bias_total = jnp.zeros((count, LEN), jnp.float32)
        decay_total = jnp.zeros((count, LEN), jnp.float32)
        for j in range(blocks):
            log_grad = jnp.zeros((count, LEN), jnp.float32)
            for i in range(j, min(j + 3, blocks)):
                chosen = jnp.where(mask_st(seg_row_ref, j, i), 1.0, 0.0).astype(jnp.bfloat16)
                high, rest = two_terms(flow_ref[:, block(i)])
                log_grad = log_grad + dot_nt(high, chosen) + dot_nt(rest, chosen)
            step = step_row_ref[:, block(j)]
            grad_step = jnp.where(step > 1e-30, q[:, block(j)] / step, 0.0) + log_grad * rate
            grad_arg = grad_step * sig_row_ref[:, block(j)]
            bias_total = bias_total + grad_arg
            decay_total = decay_total + log_grad * step
            tall = jnp.concatenate([grad_arg, jnp.zeros((LEN - count, LEN), jnp.float32)], axis=0)
            dstep_ref[block(j), :] = tall.T.astype(jnp.bfloat16)
        step_sum_ref[0:count, :] = jnp.broadcast_to(jnp.sum(bias_total, axis=1, keepdims=True), (count, LEN))
        step_sum_ref[count : 2 * count, :] = jnp.broadcast_to(
            jnp.sum(decay_total * rate, axis=1, keepdims=True), (count, LEN)
        )


def whole_block(shape):
    return pl.BlockSpec(shape, lambda step: (0,) * len(shape), pipeline_mode=pl.Buffered(1))


def tile(rows, row_block=0, first=0):
    return pl.BlockSpec((rows, GROUP * LEN), lambda step: (row_block, first + step))


def small_block(rows, width):
    return pl.BlockSpec((rows, width), lambda step: (0, 2), pipeline_mode=pl.Buffered(1))


def call(kernel, steps, out_shape, out_specs, scratch, operands, specs, flops):
    return pl.pallas_call(
        kernel,
        grid=(steps,),
        out_shape=out_shape,
        in_specs=[s or whole_block(o.shape) for o, s in zip(operands, specs)],
        out_specs=[s or whole_block(o.shape) for o, s in zip(out_shape, out_specs)],
        scratch_shapes=scratch,
        compiler_params=pltpu.CompilerParams(vmem_limit_bytes=VMEM_BYTES),
        cost_estimate=pl.CostEstimate(flops=flops, bytes_accessed=0, transcendentals=0),
    )(*operands)


def f32(*shape):
    return jax.ShapeDtypeStruct(shape, jnp.float32)


def b16(*shape):
    return jax.ShapeDtypeStruct(shape, jnp.bfloat16)


HEAD_ROWS = 16
GROUP = 3
VMEM_BYTES = 60 * 1024 * 1024


def scan_prep(width, wide_in, cosine, sine, seg_row, params):
    rows = wide_in.shape[0]
    steps = width // LEN // GROUP
    outs = [
        f32(rows, width),
        b16(rows, width),
        f32(rows, width),
        f32(rows, 2 * LEN),
        f32(rows, 2 * LEN),
        f32(rows, LEN),
        f32(rows, LEN),
        f32(HEAD_ROWS, 1, rows),
        f32(HEAD_ROWS, 1, rows),
        f32(HEAD_ROWS, rows),
        f32(HEAD_ROWS, rows),
        b16(rows, 2 * LEN),
        b16(rows, LEN),
    ]
    scratch = [pltpu.VMEM((rows + 8, LEN), jnp.float32), pltpu.VMEM((3, rows + 8, LEN), jnp.float32)]
    operands = (wide_in, wide_in, cosine, sine, seg_row, params, params)
    specs = [tile(rows, 0, steps), small_block(rows, width), None, None, None, tile(16), None]
    return call(prep_kernel, steps, outs, [tile(rows)] * 3 + [None] * 10, scratch, operands, specs, 0 * 10**9)


def scan_forward(chunks, heads, wide_in, x, xb, *rest):
    width = x.shape[1]
    rows = LEN * len(chunks)
    at = chunks[0] // len(chunks)
    count = sum(min(i, 2) + 1 for i in chunks)
    outs = [f32(rows, width), f32(rows, width), f32(1, rows)]
    scratch = [
        pltpu.VMEM((heads, rows, LEN), jnp.float32),
        pltpu.VMEM((count, LEN, LEN), jnp.float32),
        pltpu.VMEM((count, LEN, LEN), jnp.float32),
        pltpu.VMEM((len(chunks), 2 * LEN, 3 * LEN), jnp.bfloat16),
        pltpu.VMEM((rows, LEN), jnp.float32),
    ]
    specs = [tile(rows, at), tile(rows, at), tile((chunks[-1] + 1) * LEN)] + [None] * (len(rest) - 1) + [tile(16)]
    kernel = functools.partial(scan_kernel, chunks, heads)
    operands = (wide_in, x, xb, *rest)
    return call(kernel, heads // 2 // GROUP, outs, [tile(rows), tile(rows), None], scratch, operands, specs, 0 * 10**9)


def attention_forward(chunks, q, kv, seg_row):
    rows = LEN * len(chunks)
    outs = [b16(rows, q.shape[1]), f32(8, rows)]
    kernel = functools.partial(attention_kernel, chunks)
    return call(kernel, 1, outs, [None] * 2, [], (q, kv, seg_row), [None] * 3, 0 * 10**9)


def attention_backward(chunks, final, *operands):
    q = operands[0]
    rows = q.shape[0]
    partial = [f32(rows, LEN), f32(rows, LEN)]
    sums = [pltpu.VMEM((rows, LEN), jnp.float32)] * 2
    outs = [b16(LEN * len(chunks), q.shape[1])] + ([b16(rows, LEN)] if final else partial)
    scratch = (sums if final else []) + [
        pltpu.VMEM((rows, LEN), jnp.bfloat16),
        pltpu.VMEM((HEAD_DIM, rows), jnp.bfloat16),
    ]
    kernel = functools.partial(attention_back_kernel, chunks, final)
    return call(kernel, 1, outs, [None] * len(outs), scratch, operands, [None] * len(operands), (0 if chunks[0] else 30) * 10**9)


def scan_backward(chunks, heads, *operands):
    rows, width = operands[0].shape
    at = chunks[0] // len(chunks)
    sources = (chunks[-1] + 1) * LEN
    count = sum(min(i, 2) + 1 for i in chunks)
    outs = [
        b16(rows, width),
        f32(rows, width),
        f32(sources, width),
        f32(HEAD_ROWS, rows),
        f32(sources, LEN),
        f32(rows, LEN),
        f32(8, width),
    ]
    scratch = [
        pltpu.VMEM((rows, LEN), jnp.bfloat16),
        pltpu.VMEM((heads, sources, LEN), jnp.float32),
        pltpu.VMEM((count, LEN, LEN), jnp.float32),
        pltpu.VMEM((count, LEN, LEN), jnp.float32),
        pltpu.VMEM((count, LEN, LEN), jnp.float32),
        pltpu.VMEM((rows, LEN), jnp.float32),
        pltpu.VMEM((rows, LEN), jnp.float32),
        pltpu.VMEM((2 * LEN, 3 * LEN), jnp.float32),
        pltpu.VMEM((2 * LEN, 3 * LEN), jnp.bfloat16),
    ]
    specs = [tile(rows), tile(rows), None, None, None, None, tile(16), tile(rows, at), tile(rows), tile(rows, at), tile(sources)]
    specs += [None, None, None, None, tile(HEAD_ROWS)]
    out_specs = [tile(rows), tile(rows), tile(sources), None, None, None, tile(8)]
    kernel = functools.partial(scan_back_kernel, chunks, heads)
    return call(kernel, heads // 2 // GROUP, outs, out_specs, scratch, operands, specs, 30 * 10**9)


def scan_end(heads, *operands):
    rows, width = 2 * operands[0].shape[0], operands[0].shape[1]
    steps = heads // 2 // GROUP
    outs = [
        b16(rows, width),
        b16(rows, 2 * LEN),
        b16(rows, LEN),
        f32(8, width),
        f32(8, 2 * LEN),
        f32(2 * HEAD_ROWS, LEN),
    ]
    scratch = [
        pltpu.VMEM((rows + 8, LEN), jnp.float32),
        pltpu.VMEM((rows + 8, LEN), jnp.float32),
        pltpu.VMEM((3, rows + 8, LEN), jnp.float32),
        pltpu.VMEM((HEAD_ROWS, rows), jnp.float32),
        pltpu.VMEM((HEAD_ROWS, rows), jnp.float32),
    ]
    half = rows // 2
    specs = [tile(half), tile(half), tile(half), tile(rows)] + [None] * 6 + [tile(rows), tile(rows), None]
    specs += [tile(rows, 0, steps), small_block(rows, width), None, None, None, tile(HEAD_ROWS), tile(16), None]
    out_specs = [tile(rows), None, None, tile(8), None, None]
    kernel = functools.partial(scan_end_kernel, heads)
    return call(kernel, steps, outs, out_specs, scratch, operands, specs, 30 * 10**9)


def inverse_rms(rows):
    return lax.rsqrt(jnp.mean(rows * rows, axis=-1, keepdims=True) + norm_eps)


def ffn_kernel(
    tokens_ref,
    part_ref,
    far_ref,
    gain_ref,
    gate_ref,
    up_ref,
    down_ref,
    cotangent_ref,
    hidden_ref,
    normed_ref,
    activated_ref,
    grad_gate_ref,
    grad_up_ref,
    back_ref,
    out_ref,
):
    @pl.when(pl.program_id(0) == 0)
    def _():
        hidden = tokens_ref[...].astype(jnp.float32) + (part_ref[...] + far_ref[...])
        hidden_ref[...] = hidden
        normed_ref[...] = (hidden * inverse_rms(hidden) * gain_ref[...]).astype(jnp.bfloat16)
        back_ref[...] = jnp.zeros(back_ref.shape, jnp.float32)
        out_ref[...] = jnp.zeros(out_ref.shape, jnp.float32)

    normed = normed_ref[...]
    gate = dot_nn(normed, gate_ref[...])
    up = dot_nn(normed, up_ref[...])
    sig = sigmoid(gate)
    act = gate * sig
    activated = (act * up).astype(jnp.bfloat16)
    activated_ref[...] = activated
    grad = dot_nt(cotangent_ref[...], down_ref[...])
    grad_gate = (grad * up * (sig * (1.0 + gate * (1.0 - sig)))).astype(jnp.bfloat16)
    grad_up = (grad * act).astype(jnp.bfloat16)
    grad_gate_ref[...] = grad_gate
    grad_up_ref[...] = grad_up
    back_ref[...] = back_ref[...] + (dot_nt(grad_gate, gate_ref[...]) + dot_nt(grad_up, up_ref[...]))
    out_ref[...] = out_ref[...] + dot_nn(activated, down_ref[...])


def ffn(chunks, tokens, part, far, gain, gate, up, down, cotangent):
    rows, model_width = part.shape
    at = chunks[0] // len(chunks)
    hidden_width = gate.shape[1]
    steps = hidden_width // 256
    outs = [f32(rows, model_width), b16(rows, model_width)] + [b16(rows, hidden_width)] * 3
    outs += [f32(rows, model_width)] * 2
    rows_of = pl.BlockSpec((rows, model_width), lambda step: (at, 0), pipeline_mode=pl.Buffered(1))
    columns = pl.BlockSpec((model_width, 256), lambda step: (0, step))
    tiles = pl.BlockSpec((rows, 256), lambda step: (0, step))
    specs = [rows_of, None, None, None, columns, columns]
    specs += [pl.BlockSpec((256, model_width), lambda step: (step, 0)), rows_of]
    operands = (tokens, part, far, gain, gate, up, down, cotangent)
    return call(ffn_kernel, steps, outs, [None, None, tiles, tiles, tiles, None, None], [], operands, specs, 0 * 10**9)


def middle_kernel(
    hidden_ref,
    part_ref,
    far_ref,
    cotangent_ref,
    gain_ref,
    gated_ref,
    square_a_ref,
    square_b_ref,
    params_ref,
    mixer_out_ref,
    attn_out_ref,
    grad_hidden_ref,
    grad_branch_ref,
    grad_rows_ref,
    grad_attended_ref,
    dot_ref,
    gain_sum_ref,
):
    hidden = hidden_ref[...]
    inv = inverse_rms(hidden)
    unit = hidden * inv
    grad_normed = part_ref[...] + far_ref[...]
    gain_sum_ref[0:1, :] = jnp.sum(grad_normed * unit, axis=0, keepdims=True)
    grad_unit = grad_normed * gain_ref[...]
    inner = jnp.mean(grad_unit * unit, axis=-1, keepdims=True)
    grad_hidden = cotangent_ref[...].astype(jnp.float32) + inv * (grad_unit - unit * inner)
    grad_hidden_ref[...] = grad_hidden
    grad_branch = grad_hidden.astype(jnp.bfloat16)
    grad_branch_ref[...] = grad_branch
    grad_rows = dot_nt(grad_branch, mixer_out_ref[...])
    grad_rows_ref[...] = grad_rows
    grad_attended_ref[...] = dot_nt(grad_branch, attn_out_ref[...]).astype(jnp.bfloat16)
    total = jnp.sum(grad_rows * params_ref[6:7, :] * gated_ref[...], axis=-1, keepdims=True)
    for i in range(hidden.shape[0] // LEN):
        at = block(i)
        inv_gated = lax.rsqrt((square_a_ref[:, at] + square_b_ref[:, at]) / DSSM + norm_eps)
        dot_ref[0:1, at] = jnp.broadcast_to(total[at], (LEN, LEN)).T[0:1] * inv_gated


def middle(chunks, hidden, part, far, cotangent, gain, gated, square_a, square_b, gated_gain, mixer_out, attn_out):
    rows, model_width = part.shape
    at = chunks[0] // len(chunks)
    width, inner = mixer_out.shape[0], attn_out.shape[0]
    outs = [
        f32(rows, model_width),
        b16(rows, model_width),
        f32(rows, width),
        b16(rows, inner),
        f32(1, rows),
        f32(8, model_width),
    ]
    rows_of = pl.BlockSpec((rows, model_width), lambda step: (at, 0), pipeline_mode=pl.Buffered(1))
    specs = [None, None, None, rows_of] + [None] * 7
    operands = (hidden, part, far, cotangent, gain, gated, square_a, square_b, gated_gain, mixer_out, attn_out)
    return call(middle_kernel, 1, outs, [None] * 6, [], operands, specs, 30 * 10**9)


def core_call(kernel, steps, core, out_shape, out_spec, scratch, operands, specs, flops, aliases=None):
    return pl.pallas_call(
        kernel,
        grid_spec=pltpu.PrefetchScalarGridSpec(
            num_scalar_prefetch=1, grid=(steps,), in_specs=specs, out_specs=out_spec, scratch_shapes=scratch
        ),
        out_shape=out_shape,
        compiler_params=pltpu.CompilerParams(vmem_limit_bytes=VMEM_BYTES),
        cost_estimate=pl.CostEstimate(flops=flops, bytes_accessed=0, transcendentals=0),
        input_output_aliases=aliases or {},
    )(core, *operands)


def clip_tile(rows, columns, first, last):
    return pl.BlockSpec((rows, columns), lambda step, core_ref: (0, jnp.clip(step - first, 0, last - first - 1)))


def ffn_weights_kernel(add, core_ref, *refs):
    refs = list(refs)
    normed_a, normed_b, act_a, act_b, gate_a, gate_b, up_a, up_b, cot_a, cot_b = refs[:10]
    far_ref = refs[10] if add else None
    out_ref, left_ref = refs[-2:]
    step = pl.program_id(0)
    third = pl.num_programs(0) // 3
    half = normed_a.shape[0]

    def turn(first, second):
        left_ref[:, :half] = first[...].T
        left_ref[:, half:] = second[...].T

    @pl.when(step == 0)
    def _():
        turn(normed_a, normed_b)

    @pl.when(step == 2 * third)
    def _():
        turn(act_a, act_b)

    def product(first, second):
        result = dot_nn(left_ref[:, :half], first[...]) + dot_nn(left_ref[:, half:], second[...])
        out_ref[...] = result + far_ref[...] if add else result

    @pl.when(step < third)
    def _():
        product(gate_a, gate_b)

    @pl.when((step >= third) & (step < 2 * third))
    def _():
        product(up_a, up_b)

    @pl.when(step >= 2 * third)
    def _():
        product(cot_a, cot_b)


def ffn_weights(core, far, normed_a, normed_b, act_a, act_b, gate_a, gate_b, up_a, up_b, cotangent):
    half, columns = normed_a.shape
    kept = columns // 2
    tile_width = 512
    third = columns // tile_width
    left = pl.BlockSpec((half, kept), lambda step, core_ref: (0, core_ref[0]), pipeline_mode=pl.Buffered(1))
    specs = [left] * 4 + [clip_tile(half, tile_width, 0, third)] * 2
    specs += [clip_tile(half, tile_width, third, 2 * third)] * 2

    def cot_rows(at):
        return pl.BlockSpec(
            (half, tile_width), lambda step, core_ref: (at, jnp.clip(step - 2 * third, 0, third - 1))
        )

    specs += [cot_rows(0), cot_rows(1)]
    out = pl.BlockSpec((kept, tile_width), lambda step, core_ref: (0, step))
    operands = [normed_a, normed_b, act_a, act_b, gate_a, gate_b, up_a, up_b, cotangent, cotangent]
    if far is not None:
        operands.append(far)
        specs.append(out)
    return core_call(
        functools.partial(ffn_weights_kernel, far is not None),
        3 * third,
        core,
        f32(kept, (3 if far is None else 4) * columns),
        out,
        [pltpu.VMEM((kept, 2 * half), jnp.bfloat16)],
        operands,
        specs,
        0 * 10**9,
    )


def outer_weights_kernel(add, core_ref, *refs):
    refs = list(refs)
    rows_a, rows_b, edge_a, edge_b, att_a, att_b, branch_a, branch_b = refs[:8]
    out_ref, left_ref = refs[-2:]
    half = rows_a.shape[0]
    middle_row = left_ref.shape[0] // 2

    @pl.when((pl.program_id(0) == 0) & (core_ref[0] == 0))
    def _():
        left_ref[:, :half] = rows_a[...].T
        left_ref[:, half:] = rows_b[...].T

    @pl.when((pl.program_id(0) == 0) & (core_ref[0] == 1))
    def _():
        left_ref[:middle_row, :half] = edge_a[...].T
        left_ref[:middle_row, half:] = edge_b[...].T
        left_ref[middle_row:, :half] = att_a[...].T
        left_ref[middle_row:, half:] = att_b[...].T

    result = dot_nn(left_ref[:, :half], branch_a[...]) + dot_nn(left_ref[:, half:], branch_b[...])
    out_ref[...] = result + refs[8][...] if add else result


def outer_weights(core, far, buffer, rows_a, rows_b, att_a, att_b, branch_a, branch_b):
    half, width = rows_a.shape
    model_width = branch_a.shape[1]
    kept = model_width // 2
    tile_width = 512
    steps = model_width // tile_width

    def fixed(shape, column=0):
        return pl.BlockSpec(shape, lambda step, core_ref: (0, column), pipeline_mode=pl.Buffered(1))

    specs = [fixed((half, kept))] * 2
    specs += [fixed((half, width - kept), kept // (width - kept))] * 2
    specs += [fixed(att_a.shape)] * 2 + [clip_tile(half, tile_width, 0, steps)] * 2
    operands = [rows_a, rows_b, rows_a, rows_b, att_a, att_b, branch_a, branch_b]
    out = pl.BlockSpec((kept, tile_width), lambda step, core_ref: (0, step))
    columns, aliases = model_width, {}
    if far is not None:
        operands += [far, buffer]
        specs += [out, pl.BlockSpec(memory_space=pl.ANY)]
        columns = buffer.shape[1]
        first = columns // tile_width - steps
        out = pl.BlockSpec((kept, tile_width), lambda step, core_ref: (0, first + step))
        aliases = {len(operands): 0}
    return core_call(
        functools.partial(outer_weights_kernel, far is not None),
        steps,
        core,
        f32(kept, columns),
        out,
        [pltpu.VMEM((kept, 2 * half), jnp.bfloat16)],
        operands,
        specs,
        0,
        aliases,
    )


PARTS = ((0, 3), (3, 5), (5, 7), (7, 9))


def mixer_weights_kernel(add, core_ref, *refs):
    refs = list(refs)
    normed_ref, gate_a, gate_b, conv_ref, query_a, query_b, state_ref, pair_ref, step_ref = refs[:9]
    far_ref, table_ref = refs[9:11] if add else (None, None)
    outs = refs[11:19] if add else refs[9:10]
    left_ref, result_ref = refs[-2:]
    step = pl.program_id(0)
    half = gate_a.shape[0]

    @pl.when(step == 0)
    def _():
        left_ref[...] = normed_ref[...].T

    def two(first, second):
        result_ref[...] = dot_nn(left_ref[:, :half], first[...]) + dot_nn(left_ref[:, half:], second[...])

    @pl.when(step < 3)
    def _():
        two(gate_a, gate_b)

    @pl.when((step >= 3) & (step < 6))
    def _():
        result_ref[...] = dot_nn(left_ref[...], conv_ref[...])

    @pl.when(step == 6)
    def _():
        two(query_a, query_b)

    @pl.when(step == 7)
    def _():
        result_ref[...] = dot_nn(left_ref[...], state_ref[...])

    @pl.when(step == 8)
    def _():
        result_ref[:, :LEN] = dot_nn(left_ref[...], pair_ref[...])
        steps = dot_nn(left_ref[...], step_ref[...])
        result_ref[:, LEN:] = steps + table_ref[...] if add else steps

    if not add:
        outs[0][...] = result_ref[...]
        return
    result_ref[...] = result_ref[...] + far_ref[...]
    for k, (first, last) in enumerate(PARTS):

        @pl.when((step >= first) & (step < last))
        def _():
            for side in range(2):
                out_ref = outs[2 * k + side]
                for q in range(2):
                    index = core_ref[1 + 4 * k + 2 * side + q]
                    if k < 2:
                        for y in range(4):
                            start = pl.multiple_of((4 * y + index) * 32, 32)
                            out_ref[(2 * y + q) * 32 : (2 * y + q + 1) * 32, :] = result_ref[pl.ds(start, 32), :]
                    else:
                        start = pl.multiple_of(index * LEN, LEN)
                        out_ref[q * LEN : (q + 1) * LEN, :] = result_ref[pl.ds(start, LEN), :]


def mixer_weights(core, far, table, normed, gate_a, gate_b, conv, query_a, query_b, state, pair, step):
    half = gate_a.shape[0]
    rows, model_width = normed.shape
    kept = model_width // 2
    tile_width = 256
    steps = 9

    def fixed(shape, column=0):
        return pl.BlockSpec(shape, lambda step, core_ref: (0, column), pipeline_mode=pl.Buffered(1))

    specs = [pl.BlockSpec((rows, kept), lambda step, core_ref: (0, core_ref[0]), pipeline_mode=pl.Buffered(1))]
    specs += [clip_tile(half, tile_width, 0, 3)] * 2 + [clip_tile(rows, tile_width, 3, 6)]
    specs += [fixed(query_a.shape)] * 2 + [fixed(state.shape), fixed(pair.shape), fixed(step.shape)]
    operands = [normed, gate_a, gate_b, conv, query_a, query_b, state, pair, step]
    out = pl.BlockSpec((kept, tile_width), lambda step, core_ref: (0, step))
    shape = f32(kept, steps * tile_width)
    if far is not None:
        operands += [far, table]
        specs += [out, fixed(table.shape)]
        out, shape = [], []
        for first, last in PARTS:
            out += [clip_tile(kept // 2, tile_width, first, last)] * 2
            shape += [f32(kept // 2, (last - first) * tile_width)] * 2
    return core_call(
        functools.partial(mixer_weights_kernel, far is not None),
        steps,
        core,
        shape,
        out,
        [pltpu.VMEM((kept, rows), jnp.bfloat16), pltpu.VMEM((kept, tile_width), jnp.float32)],
        operands,
        specs,
        30 * 10**9,
    )


def normed_back_kernel(
    gate_a,
    gate_b,
    conv_ref,
    query_a,
    query_b,
    state_ref,
    pair_ref,
    step_ref,
    wide_ref,
    small_ref,
    tokens_ref,
    whole_ref,
    out_ref,
    sum_ref,
    inv_ref,
):
    @pl.when(pl.program_id(0) == 0)
    def _():
        inv_ref[...] = jnp.broadcast_to(inverse_rms(whole_ref[...].astype(jnp.float32)), inv_ref.shape)

    half, width = gate_a.shape
    query_width = query_a.shape[1]
    gate_w, conv_w = wide_ref[:, :width], wide_ref[:, width:]
    state_w = small_ref[:, : 2 * LEN]
    query_w = small_ref[:, 2 * LEN : 2 * LEN + query_width]
    pair_w = small_ref[:, 2 * LEN + query_width : 3 * LEN + query_width]
    step_w = small_ref[:, 3 * LEN + query_width :]
    total = jnp.zeros((1, out_ref.shape[1]), jnp.float32)
    for k, (gate, query) in enumerate(((gate_a, query_a), (gate_b, query_b))):
        at = slice(k * half, (k + 1) * half)
        grad = dot_nt(gate[...], gate_w) + dot_nt(conv_ref[at, :], conv_w) + dot_nt(query[...], query_w)
        grad = grad + dot_nt(state_ref[at, :], state_w) + dot_nt(pair_ref[at, :], pair_w) + dot_nt(step_ref[at, :], step_w)
        out_ref[at, :] = grad
        unit = tokens_ref[at, :].astype(jnp.float32) * jnp.concatenate([inv_ref[at, :]] * 2, axis=1)
        total = total + jnp.sum(grad * unit, axis=0, keepdims=True)
    sum_ref[0:1, :] = total


def normed_back(gate_a, gate_b, conv, query_a, query_b, state, pair, step, wide_proj, small_proj, tokens):
    rows, model_width = tokens.shape
    tile_width = 256
    operands = (gate_a, gate_b, conv, query_a, query_b, state, pair, step, wide_proj, small_proj, tokens, tokens)

    def weights(count):
        return pl.BlockSpec((tile_width, count), lambda step: (step, 0))

    columns = pl.BlockSpec((rows, tile_width), lambda step: (0, step))
    specs = [None] * 8 + [weights(wide_proj.shape[1]), weights(small_proj.shape[1]), columns, None]
    out_specs = [columns, pl.BlockSpec((8, tile_width), lambda step: (0, step))]
    outs = [f32(rows, model_width), f32(8, model_width)]
    return call(
        normed_back_kernel,
        model_width // tile_width,
        outs,
        out_specs,
        [pltpu.VMEM((rows, LEN), jnp.float32)],
        operands,
        specs, 30 * 10**9)


def project_kernel(wide_steps, tokens_ref, gain_ref, wide_ref, small_ref, out_ref, normed_ref):
    step = pl.program_id(0)

    @pl.when(step == 0)
    def _():
        tokens = tokens_ref[...].astype(jnp.float32)
        normed_ref[...] = (tokens * inverse_rms(tokens) * gain_ref[...]).astype(jnp.bfloat16)

    @pl.when(step < wide_steps)
    def _():
        out_ref[...] = dot_nn(normed_ref[...], wide_ref[...])

    @pl.when(step >= wide_steps)
    def _():
        out_ref[...] = dot_nn(normed_ref[...], small_ref[...])


def project(tokens, gain, wide_proj, small_proj):
    rows, model_width = tokens.shape
    count = 384
    wide_steps = wide_proj.shape[1] // count
    steps = wide_steps + small_proj.shape[1] // count
    outs = [f32(rows, steps * count), b16(rows, model_width)]
    wide = pl.BlockSpec((model_width, count), lambda step: (0, jnp.minimum(step, wide_steps - 1)))
    small = pl.BlockSpec((model_width, count), lambda step: (0, jnp.maximum(step - wide_steps, 0)))
    out = pl.BlockSpec((rows, count), lambda step: (0, step))
    operands = (tokens, gain, wide_proj, small_proj)
    kernel = functools.partial(project_kernel, wide_steps)
    return call(kernel, steps, outs, [out, None], [], operands, [None, None, wide, small], 0)


def unpack_kernel(
    block_ref,
    step_ref,
    input_gain_ref,
    state_kernel_ref,
    state_bias_ref,
    step_bias_ref,
    decay_ref,
    skip_ref,
    conv_kernel_ref,
    conv_bias_ref,
    gated_gain_ref,
    ffn_gain_ref,
    turned_ref,
):
    heads = step_ref.shape[0]
    for i in range(block_ref.shape[0] // LEN):
        turned_ref[:, block(i)] = block_ref[block(i), :].T

    def row(index, count, start=0):
        return turned_ref[heads + index, start : start + count]

    step_ref[...] = turned_ref[0:heads, :]
    input_gain_ref[...] = row(0, input_gain_ref.shape[0])
    columns = state_kernel_ref.shape[1]
    for tap in range(4):
        state_kernel_ref[tap, :] = row(1, columns, tap * columns)
        conv_kernel_ref[tap, :] = row(4 + tap, conv_kernel_ref.shape[1])
    state_bias_ref[...] = row(2, columns)
    step_bias_ref[...] = row(3, heads)
    decay_ref[...] = row(3, heads, LEN)
    skip_ref[...] = row(3, heads, 2 * LEN)
    conv_bias_ref[...] = row(8, conv_bias_ref.shape[0])
    gated_gain_ref[...] = row(9, gated_gain_ref.shape[0])
    ffn_gain_ref[...] = row(10, ffn_gain_ref.shape[0])


def unpack(heads, width, states, values):
    rows = values.shape[0]
    outs = [f32(heads, rows), f32(rows), f32(4, states), f32(states), f32(heads), f32(heads), f32(heads)]
    outs += [f32(4, width), f32(width), f32(width), f32(rows)]
    scratch = [pltpu.VMEM((LEN, rows), jnp.float32)]
    return call(unpack_kernel, 1, outs, [None] * len(outs), scratch, (values,), [None], 0)


def assemble_kernel(source, mixer_proj_ref, query_ref, pair_ref, state_ref, step_ref):
    width = mixer_proj_ref.shape[2]
    start = 0
    mixer_proj_ref[:, 0, :] = source[:, start : start + width]
    start += width
    mixer_proj_ref[:, 1, :] = source[:, start : start + width]
    start += width
    query_ref[...] = source[:, start : start + query_ref.shape[1]]
    start += query_ref.shape[1]
    state_ref[...] = source[:, start : start + 2 * LEN]
    start += 2 * LEN
    pair_ref[:, 0, :] = source[:, start : start + LEN]
    step_ref[...] = source[:, start + LEN :]


def assemble(values, width, query_width):
    rows, columns = values.shape

    def plain(count):
        return pl.BlockSpec((LEN, count), lambda at: (at, 0))

    out_specs = [
        pl.BlockSpec((LEN, 2, width), lambda at: (at, 0, 0)),
        plain(query_width),
        pl.BlockSpec((LEN, 1, LEN), lambda at: (at, 0, 0)),
        plain(2 * LEN),
        plain(LEN),
    ]
    out_shape = [
        f32(rows, 2, width),
        f32(rows, query_width),
        f32(rows, 1, LEN),
        f32(rows, 2 * LEN),
        f32(rows, LEN),
    ]
    return call(assemble_kernel, rows // LEN, out_shape, out_specs, [], (values,), [plain(columns)], 0)


LINKS = {
    "A": [(0, 1), (1, 0), (2, 3), (3, 2)],
    "B": [(1, 2), (2, 1), (3, 0), (0, 3)],
}
ORDERS = (
    (("x", "A"), ("x", "B"), ("y", "A"), ("y", "B")),
    (("x", "B"), ("y", "A"), ("y", "B"), ("x", "A")),
    (("y", "A"), ("y", "B"), ("x", "A"), ("x", "B")),
    (("y", "B"), ("x", "A"), ("x", "B"), ("y", "A")),
)
AXIS = {"y": 0, "x": 1}


def take(values, index, axis):
    return lax.dynamic_slice_in_dim(values, index, 1, axis)


def halves(values, name, link, again):
    place, axis = lax.axis_index(name), AXIS[name]
    if again:
        index = place // 2 if link == "B" else place % 2
        return take(values, index, axis), take(values, 1 - index, axis)
    if link == "B":
        side = place // 2
        kept = lax.dynamic_slice_in_dim(values, 2 * side, 2, axis)
        return kept, lax.dynamic_slice_in_dim(values, 2 - 2 * side, 2, axis)
    side = ((place + 1) // 2) % 2
    kept = jnp.concatenate([take(values, side, axis), take(values, 3 - side, axis)], axis)
    return kept, jnp.concatenate([take(values, 1 - side, axis), take(values, 2 + side, axis)], axis)


def reduce_rows(pairs, steps):
    kept, sent, parts = [], [], pairs
    if steps[0] == 0:
        for k, (stays, goes) in enumerate(pairs):
            shape = (4, 2, 32, stays.shape[1]) if ORDERS[k][0][0] == "x" else (2, 4, 32, stays.shape[1])
            kept.append(stays.reshape(shape))
            sent.append(goes.reshape(shape))
    for step in steps:
        if step:
            kept, sent = [], []
            for k in range(4):
                name, link = ORDERS[k][step]
                again = name in [n for n, _ in ORDERS[k][:step]]
                stays, goes = halves(parts[k], name, link, again)
                kept.append(stays)
                sent.append(goes)
        sent = lax.optimization_barrier(tuple(sent))
        come = [lax.ppermute(sent[k], ORDERS[k][step][0], LINKS[ORDERS[k][step][1]]) for k in range(4)]
        come = lax.optimization_barrier(tuple(come))
        parts = [stays + more for stays, more in zip(kept, come)]
    return parts


def rope_tables(rows):
    half_size = HEAD_DIM // 2
    inverse = np.float32(rope_base) ** (-(2.0 * np.arange(half_size, dtype=np.float32)) / HEAD_DIM)
    angles = np.arange(rows, dtype=np.float32)[:, None] * inverse.astype(np.float32)[None, :]
    cosine, sine = np.cos(angles), np.sin(angles)
    return (
        np.concatenate([cosine] * 4, axis=1).astype(np.float32),
        np.concatenate([-sine, sine, -sine, sine], axis=1).astype(np.float32),
    )


def norm_backward(grad_unit, unit_rows, inv_rms):
    return inv_rms * (grad_unit - unit_rows * jnp.mean(grad_unit * unit_rows, axis=-1, keepdims=True))


def dot32(left, right):
    return jnp.dot(left, right, preferred_element_type=jnp.float32)


def after(value, *others):
    return lax.optimization_barrier((value, *others))[0]


def swap(values, name):
    return lax.ppermute(values, name, PAIR)


def exchange(values, name):
    return values + swap(values, name)


def core_rows(values, index):
    half = values.shape[1] // 2
    return lax.dynamic_slice_in_dim(values, index * half, half, 1)


def on_device(
    layer_input,
    segments,
    input_gain,
    mixer_proj,
    state_proj,
    step_proj,
    step_bias,
    decay_log,
    skip_gain,
    conv_kernel,
    conv_bias,
    state_kernel,
    state_bias,
    gated_gain,
    mixer_out,
    query_proj,
    key_value_weight,
    attn_out,
    ffn_gain,
    ffn_gate,
    ffn_up,
    ffn_down,
    cotangent,
):
    rows, model_width = layer_input.shape
    width = mixer_proj.shape[2]
    heads = step_proj.shape[1]
    state_size = state_proj.shape[1] // 2
    query_width = query_proj.shape[1]
    pair_width = key_value_weight.shape[2]
    place = lax.axis_index("core")
    zh = lax.axis_index("zh")
    core = place.astype(jnp.int32).reshape(1)
    far_core = 1 - core
    cosine, sine = rope_tables(rows)
    select = np.arange(HEAD_ROWS)[:, None] == np.arange(width)[None, :] // HEAD_DIM
    select = jnp.asarray(select.astype(np.float32)).astype(jnp.bfloat16)
    seg_row = segments.astype(jnp.float32)
    pad_heads = ((0, 0), (0, LEN - heads))

    def padded(values):
        return jnp.pad(values, ((0, 0), (0, width - values.shape[1])))

    params = jnp.concatenate(
        [
            conv_kernel,
            conv_bias[None, :],
            jnp.repeat(skip_gain, HEAD_DIM)[None, :],
            gated_gain[None, :],
            jnp.zeros((1, width), jnp.float32),
            padded(state_kernel),
            padded(state_bias[None, :]),
            padded(step_bias[None, :]),
            padded(-jnp.exp(decay_log)[None, :]),
            jnp.zeros((1, width), jnp.float32),
        ],
        axis=0,
    )
    wide_proj = mixer_proj.reshape(model_width, 2 * width)
    small_proj = jnp.concatenate(
        [
            state_proj,
            query_proj,
            key_value_weight.reshape(model_width, pair_width),
            jnp.pad(step_proj, pad_heads),
        ],
        axis=1,
    )
    tokens = layer_input.astype(jnp.float32)
    wide_in, normed_input = project(layer_input, input_gain[None, :], wide_proj, small_proj)
    x, xb, slope, state, state_slope, cum, lag, cum_row, lag_row, step_row, sig_row, queries, pairs = scan_prep(
        width,
        wide_in,
        cosine,
        sine,
        seg_row,
        params,
    )

    blocks = rows // LEN
    late = tuple(range(blocks // 2, blocks))
    early = tuple(range(blocks // 2))
    half = {}
    for chunks in (late, early):
        h = {"span": slice(chunks[0] * LEN, (chunks[-1] + 1) * LEN)}
        h["y"], h["gated"], h["square"] = scan_forward(
            chunks, heads, wide_in, x, xb, state, cum, lag_row, seg_row, params
        )
        half[chunks] = h
    squares = jnp.concatenate([half[early]["square"], half[late]["square"]], axis=1)
    squares_far = swap(squares, "tensor")
    ready = squares
    for chunks in (late, early):
        h = half[chunks]
        h["attended"], h["lse"] = attention_forward(chunks, after(queries, ready), pairs, seg_row)
        if chunks == late:
            squares_far = after(squares_far, h["lse"])
            squares_all = squares + squares_far
        h["square"], h["square_far"] = squares[:, h["span"]], squares_far[:, h["span"]]
        h["inv_gated"] = lax.rsqrt(squares_all[:, h["span"]].reshape(-1, 1) / DSSM + norm_eps)
        h["mixer_rows"] = (h["gated"] * h["inv_gated"] * gated_gain).astype(jnp.bfloat16)
        h["part"] = dot32(h["mixer_rows"], mixer_out) + dot32(h["attended"], attn_out)
        h["branch_far"] = swap(h["part"], "tensor")
        ready = h["part"]

    a, b = half[early], half[late]
    gain_ffn = ffn_gain[None, :]
    names = ("hidden", "normed", "activated", "grad_gate_rows", "grad_up_rows", "back", "down")
    for chunks in (late, early):
        h = half[chunks]
        far = h["branch_far"] if chunks == late else after(h["branch_far"], b["back"])
        operands = (layer_input, h["part"], far, gain_ffn, ffn_gate, ffn_up, ffn_down, cotangent)
        h.update(zip(names, ffn(chunks, *operands)))
        h["back_far"] = swap(h["back"], "tensor")

    sides = (after(a["normed"], b["back_far"]), b["normed"], a["activated"], b["activated"])
    sides += (a["grad_gate_rows"], b["grad_gate_rows"], a["grad_up_rows"], b["grad_up_rows"], cotangent)
    first = ffn_weights(far_core, None, *sides)
    first_far = swap(first, "core")
    for chunks in (late, early):
        h = half[chunks]
        far = after(h["back_far"], first)
        h["grad_hidden"], h["grad_branch"], h["grad_rows"], grad_attended, h["dot"], h["gain_sum"] = middle(
            chunks,
            h["hidden"],
            h["back"],
            far,
            cotangent,
            gain_ffn,
            h["gated"],
            h["square"],
            h["square_far"],
            params,
            mixer_out,
            attn_out,
        )
        operands = (queries, pairs, grad_attended, h["lse"], seg_row, cosine, sine)
        if chunks == late:
            h["grad_queries"], grad_keys, grad_values = attention_backward(chunks, False, *operands)
            first = ffn_weights(core, after(first_far, grad_keys), *sides)
        else:
            dots = jnp.concatenate([a["dot"], b["dot"]], axis=1)
            dots_far = swap(dots, "tensor")
            outer = (a["mixer_rows"], b["mixer_rows"], a["attended"], b["attended"])
            outer += (a["grad_branch"], b["grad_branch"])
            outer_far = swap(outer_weights(far_core, None, None, *outer), "core")
            h["grad_queries"], grad_pairs = attention_backward(chunks, True, *operands, grad_keys, grad_values)
    first = outer_weights(core, after(outer_far, grad_pairs), first, *outer)
    first_sum = lax.psum_scatter(first, ("y", "x"), scatter_dimension=0, tiled=True)
    dots_far = after(dots_far, first)
    for chunks in (late, early):
        h = half[chunks]
        h["grad_gate"], h["gy"], h["dx"], h["p"], h["grad_in"], h["grad_out"], h["sums"] = scan_backward(
            chunks,
            heads,
            h["grad_rows"],
            h["gated"],
            h["square"],
            h["square_far"],
            h["dot"],
            dots_far[:, h["span"]],
            params,
            wide_in,
            h["y"],
            x,
            xb,
            state,
            lag,
            cum_row,
            seg_row,
            select,
        )
    pieces = [b["down"][:LEN], b["down"][LEN:], a["down"][:LEN], a["down"][LEN:]]
    pieces_far = [swap(after(piece, dots_far), "tensor") for piece in pieces[:3]]
    down = jnp.concatenate([a["down"], b["down"]], axis=0)
    ends = []
    for name in ("gy", "dx", "p", "grad_in", "grad_out"):
        ends += [a[name], b[name]]
    grad_conv, grad_state, grad_step, conv_sum, state_sum, step_sum = scan_end(
        heads,
        *ends,
        xb,
        slope,
        state_slope,
        wide_in,
        wide_in,
        step_row,
        sig_row,
        seg_row,
        select,
        params,
        params,
    )

    grads = (a["grad_gate"], b["grad_gate"], grad_conv, a["grad_queries"], b["grad_queries"])
    grads += (grad_state, grad_pairs, grad_step)
    tied = after(normed_input, pieces_far[0], pieces_far[1])
    second_far = swap(mixer_weights(far_core, None, None, tied, *grads), "core")
    partial_normed, input_gain_sum = normed_back(*grads, wide_proj, small_proj, layer_input)

    sums = a["sums"] + b["sums"]
    def row(*values):
        flat = jnp.concatenate([jnp.pad(v, (0, LEN - v.shape[0])) for v in values]) if len(values) > 1 else values[0]
        return jnp.pad(flat.reshape(1, -1), ((0, 0), (0, model_width - flat.size)))

    by_head = jnp.sum(sums[0].reshape(heads, HEAD_DIM), axis=1)
    table = jnp.concatenate(
        [
            input_gain_sum[:1],
            row(state_sum[:4].reshape(-1)),
            row(state_sum[4]),
            row(step_sum[:heads, 0], step_sum[HEAD_ROWS : HEAD_ROWS + heads, 0], by_head),
            jnp.pad(conv_sum[:5], ((0, 0), (0, model_width - width))),
            row(sums[1]),
            a["gain_sum"][:1] + b["gain_sum"][:1],
        ],
        axis=0,
    )
    shared_end = heads + 3
    table_end = heads + table.shape[0]
    table = (core_rows(table, place) + swap(core_rows(table, 1 - place), "core")).T
    table = jnp.pad(table, ((0, 0), (heads, LEN - table_end)))
    spots = [core]
    for name, link in [order[0] for order in ORDERS]:
        at = lax.axis_index(name).astype(jnp.int32)
        side = ((at + 1) // 2) % 2 if link == "A" else at // 2
        spots.append(jnp.stack([side, 3 - side, 1 - side, 2 + side] if link == "A" else [2 * side, 2 * side + 1, 2 - 2 * side, 3 - 2 * side]))
    second = mixer_weights(jnp.concatenate(spots), after(second_far, pieces_far[2]), table, normed_input, *grads)
    second = list(second)
    at_state = 2 * width + query_width
    normed_far = [swap(partial_normed[k * LEN : (k + 1) * LEN], "tensor") for k in range(rows // LEN)]
    second[1] = after(second[1], normed_far[0])
    parts = reduce_rows([(second[2 * k], second[2 * k + 1]) for k in range(4)], (0,))
    parts[0] = after(parts[0], normed_far[1])
    first_own = exchange(after(first_sum, parts[0]), "zh")
    first_all = lax.all_gather(first_own, ("core", "y", "x"), axis=0, tiled=True)
    parts = reduce_rows(parts, (1,))
    parts[0] = after(parts[0], normed_far[2])
    parts = reduce_rows(parts, (2,))
    parts[0] = after(parts[0], normed_far[3])
    parts = reduce_rows(parts, (3,))
    second = jnp.concatenate([p.reshape(32, -1) for p in parts], axis=1)
    both = second[:, at_state:]
    lane = np.arange(both.shape[1])
    in_table = lane - 2 * state_size - pair_width
    is_shared = (lane < 2 * state_size) | ((in_table >= heads) & (in_table < shared_end))
    diagonal = [(0, 3), (3, 0), (1, 2), (2, 1)]
    more = swap(both, "tensor") + lax.ppermute(both, ("zh", "tensor"), diagonal)
    second = exchange(second, "zh")
    summed = second[:, at_state:] + jnp.where(is_shared[None, :], more, 0.0)
    second = jnp.concatenate([second[:, :at_state], summed], axis=1)
    second = after(second, first_all)
    pieces_far.append(swap(after(pieces[3], second), "tensor"))
    second = lax.all_gather(second, ("core", "y", "x"), axis=0, tiled=True)
    grad_mixer_proj, grad_query_proj, grad_keyval, grad_state_proj, step_block = assemble(second, width, query_width)

    def whole(name):
        return jnp.concatenate([a[name], b[name]], axis=0)

    grad_hidden = whole("grad_hidden")
    grad_normed = partial_normed + jnp.concatenate(normed_far, axis=0)
    inv_rms_in = inverse_rms(tokens)
    unit_in = tokens * inv_rms_in
    input_grad = grad_hidden + norm_backward(grad_normed * input_gain, unit_in, inv_rms_in)
    down_far = jnp.concatenate([pieces_far[2], pieces_far[3], pieces_far[0], pieces_far[1]], axis=0)
    layer_output = (whole("hidden") + (down + down_far)).astype(jnp.bfloat16)

    smalls = unpack(heads, width, 2 * state_size, step_block)
    return (
        layer_output,
        input_grad,
        smalls[1],
        grad_mixer_proj,
        grad_state_proj,
        smalls[0].T,
        smalls[4],
        smalls[5],
        smalls[6],
        smalls[7],
        smalls[8],
        smalls[2],
        smalls[3],
        smalls[9],
        first_all[:width, 3 * model_width :],
        grad_query_proj,
        grad_keyval,
        first_all[width:, 3 * model_width :],
        smalls[10],
        first_all[:, :model_width],
        first_all[:, model_width : 2 * model_width],
        first_all[:, 2 * model_width : 3 * model_width],
    )


def solution(mesh):
    dp, whole_spec, columns = P(DP, None), P(), P(None, "tensor")
    per_channel, middle = P("tensor"), P(None, "tensor", None)
    last, by_rows = P(None, None, "tensor"), P("tensor", None)
    weights = (
        whole_spec,
        last,
        whole_spec,
        columns,
        per_channel,
        per_channel,
        per_channel,
        columns,
        per_channel,
        whole_spec,
        whole_spec,
        per_channel,
        by_rows,
        columns,
        middle,
        by_rows,
        whole_spec,
        columns,
        columns,
        by_rows,
    )
    mesh = jax.sharding.Mesh(mesh.devices.reshape(4, 2, 4, 2, 2), (*DP, "tensor"))
    return jax.shard_map(
        on_device, mesh=mesh, in_specs=(dp, dp, *weights, dp), out_specs=(dp, dp, *weights), check_vma=False
    )
```

```python
import functools

import jax
import jax.numpy as jnp
import numpy as np
from jax import lax
from jax.experimental import pallas as pl
from jax.experimental.pallas import tpu as pltpu
from jax.sharding import PartitionSpec as P

HEAD_DIM = 64
DSSM = 1536
DP = ("y", "zh", "x", "core")
PAIR = [(0, 1), (1, 0)]
LOG2E = 1.4426950408889634
hidden_bias = -1e30
norm_eps = 1e-05
rope_base = 10000.0
LEN = 128


def dot_nn(left, right):
    return lax.dot_general(
        left, right, (((1,), (0,)), ((), ())), preferred_element_type=jnp.float32
    )


def dot_nt(left, right):
    return lax.dot_general(
        left, right, (((1,), (1,)), ((), ())), preferred_element_type=jnp.float32
    )


def dot_tn(left, right):
    return lax.dot_general(
        left, right, (((0,), (0,)), ((), ())), preferred_element_type=jnp.float32
    )


def two_terms(v):
    high = v.astype(jnp.bfloat16)
    return high, (v - high.astype(jnp.float32)).astype(jnp.bfloat16)


def three_dots(dot, left, right):
    left_high, left_low = two_terms(left)
    right_high, right_low = two_terms(right)
    return dot(left_high, right_high) + dot(left_high, right_low) + dot(left_low, right_high)


def sigmoid(v):
    return 1.0 / (1.0 + jnp.exp(-v))


def block(index):
    return slice(index * LEN, (index + 1) * LEN)


def lane_iota(rows=LEN):
    return lax.broadcasted_iota(jnp.int32, (rows, LEN), 1)


def turned(row):
    return jnp.broadcast_to(row, (LEN, LEN)).T


def mask_ts(seg_row, i, j):
    same = turned(seg_row[:, block(i)]) == seg_row[:, block(j)]
    if i != j:
        return same
    down = lax.broadcasted_iota(jnp.int32, (LEN, LEN), 0)
    return same & (down >= lane_iota())


def mask_st(seg_row, j, i):
    same = turned(seg_row[:, block(j)]) == seg_row[:, block(i)]
    if i != j:
        return same
    down = lax.broadcasted_iota(jnp.int32, (LEN, LEN), 0)
    return same & (down <= lane_iota())


def conv_rows(pad_ref, keep_ref, kernel, bias, start, lanes):
    summed = bias + kernel[3:4] * pad_ref[8 + start : 8 + start + LEN, lanes]
    for lag in (1, 2, 3):
        moved = pad_ref[8 + start - lag : 8 + start - lag + LEN, lanes]
        summed = summed + kernel[3 - lag : 4 - lag] * (moved * keep_ref[lag - 1, start : start + LEN, :])
    return summed


def widen(seg_row_ref, wide_ref, pad_ref):
    rows = seg_row_ref.shape[1]
    pad_ref[0:8, :] = jnp.full((8, LEN), -1.0, jnp.float32)
    for i in range(rows // LEN):
        pad_ref[8 + i * LEN : 8 + (i + 1) * LEN, :] = turned(seg_row_ref[:, block(i)])
    for lag in (1, 2, 3):
        same = pad_ref[8 : rows + 8, :] == pad_ref[8 - lag : rows + 8 - lag, :]
        wide_ref[lag - 1, 0:rows, :] = jnp.where(same, 1.0, 0.0)
        wide_ref[lag - 1, rows : rows + 8, :] = jnp.zeros((8, LEN), jnp.float32)


def prep_kernel(
    conv_ref,
    small_ref,
    cos_ref,
    sin_ref,
    seg_row_ref,
    table_ref,
    params_ref,
    x_ref,
    xb_ref,
    slope_ref,
    state_ref,
    state_slope_ref,
    cum_ref,
    lag_ref,
    cum_row_ref,
    lag_row_ref,
    step_row_ref,
    sig_row_ref,
    q_ref,
    kv_ref,
    pad_ref,
    wide_ref,
):
    rows = conv_ref.shape[0]
    blocks = rows // LEN

    @pl.when(pl.program_id(0) == 0)
    def _():
        widen(seg_row_ref, wide_ref, pad_ref)
        pad_ref[0:8, :] = jnp.zeros((8, LEN), jnp.float32)
        for c in range(2):
            pad_ref[8 : rows + 8, :] = small_ref[:, block(c)]
            for i in range(blocks):
                pre = conv_rows(
                    pad_ref, wide_ref, params_ref[8:12, block(c)], params_ref[12:13, block(c)], i * LEN, slice(0, LEN)
                )
                sig = sigmoid(pre)
                state_ref[block(i), block(c)] = pre * sig
                state_slope_ref[block(i), block(c)] = sig * (1.0 + pre * (1.0 - sig))

    @pl.when(pl.program_id(0) == 1)
    def _():
        down = lax.broadcasted_iota(jnp.int32, (LEN, LEN), 0)
        lower = jnp.where(down >= lane_iota(), 1.0, 0.0).astype(jnp.bfloat16)
        left_half = lane_iota() < HEAD_DIM
        carry = jnp.zeros((1, LEN), jnp.float32)
        heads = cum_row_ref.shape[0]
        for i in range(blocks):
            argument = small_ref[block(i), block(5)] + params_ref[13:14, :LEN]
            tail = jnp.exp(-jnp.abs(argument))
            grown = jnp.where(tail < 1e-3, tail - 0.5 * tail * tail, jnp.log(1.0 + tail))
            step = jnp.maximum(argument, 0.0) + grown
            scaled = step * params_ref[14:15, :LEN] * LOG2E
            first, rest = two_terms(scaled)
            last = scaled - first.astype(jnp.float32) - rest.astype(jnp.float32)
            cum = dot_nn(lower, first) + dot_nn(lower, rest) + dot_nn(lower, last.astype(jnp.bfloat16)) + carry
            carry = cum[LEN - 1 : LEN, :]
            lag = cum - jnp.log(step) * LOG2E
            cum_ref[block(i), :] = cum
            lag_ref[block(i), :] = lag
            cum_t, lag_t = cum.T, lag.T
            step_row_ref[:, block(i)] = step.T[:heads]
            sig_row_ref[:, block(i)] = sigmoid(argument).T[:heads]
            for h in range(heads):
                cum_row_ref[h, :, block(i)] = cum_t[h : h + 1]
                lag_row_ref[h, :, block(i)] = lag_t[h : h + 1]
            cosine, sine = cos_ref[block(i), :], sin_ref[block(i), :]
            kv = small_ref[block(i), block(4)]
            kv_ref[block(i), :] = jnp.where(left_half, rotate_tile(kv, cosine, sine), kv).astype(jnp.bfloat16)
            for p in range(q_ref.shape[1] // LEN):
                q_ref[block(i), block(p)] = rotate_tile(small_ref[block(i), block(2 + p)], cosine, sine).astype(
                    jnp.bfloat16
                )

    for sub in range(GROUP):
        lanes = block(sub)
        pad_ref[8 : rows + 8, :] = conv_ref[:, lanes]
        for i in range(blocks):
            pre = conv_rows(pad_ref, wide_ref, table_ref[0:4, lanes], table_ref[4:5, lanes], i * LEN, slice(0, LEN))
            sig = sigmoid(pre)
            x = pre * sig
            x_ref[block(i), lanes] = x
            xb_ref[block(i), lanes] = x.astype(jnp.bfloat16)
            slope_ref[block(i), lanes] = sig * (1.0 + pre * (1.0 - sig))


def rotate_tile(v, cosine, sine):
    first = lax.rem(lane_iota(v.shape[0]), HEAD_DIM) < HEAD_DIM // 2
    swapped = jnp.where(first, pltpu.roll(v, LEN - HEAD_DIM // 2, 1), pltpu.roll(v, HEAD_DIM // 2, 1))
    return v * cosine + swapped * sine


def scan_kernel(
    chunks,
    heads,
    gate_ref,
    x_ref,
    xb_ref,
    state_ref,
    cum_ref,
    lag_row_ref,
    seg_row_ref,
    table_ref,
    y_ref,
    gated_ref,
    row_ref,
    wide_ref,
    cross_ref,
    bias_ref,
    mix_ref,
    square_ref,
):
    step = pl.program_id(0)
    first = chunks[0]
    pairs = [(i, j) for i in chunks for j in range(max(0, i - 2), i + 1)]
    left_half = lane_iota() < HEAD_DIM

    @pl.when(step == 0)
    def _():
        for h in range(heads):
            for i in chunks:
                wide_ref[h, block(i - first), :] = jnp.broadcast_to(cum_ref[block(i), h : h + 1], (LEN, LEN))
        for i in chunks:
            low = max(0, i - 2)
            cross = three_dots(dot_nt, state_ref[block(i), LEN:], state_ref[low * LEN : (i + 1) * LEN, :LEN])
            for n, (i2, j) in enumerate(pairs):
                if i2 == i:
                    cross_ref[n] = cross[:, block(j - low)]
                    allowed = mask_ts(seg_row_ref, i, j)
                    bias_ref[n] = jnp.where(allowed, 0.0, hidden_bias)
        square_ref[...] = jnp.zeros(square_ref.shape, jnp.float32)

    tiles = (gate_ref, x_ref, xb_ref, table_ref.at[5:6], y_ref, gated_ref)

    def head_pair(hp, gate_ref, x_ref, xb_ref, skip_ref, y_ref, gated_ref):
        for i in chunks:
            at = block(i - first)
            low = max(0, i - 2)
            for n, (i2, j) in enumerate(pairs):
                if i2 != i:
                    continue
                for e in range(2):
                    spread = wide_ref[2 * hp + e, at, :] - lag_row_ref[2 * hp + e, :, block(j)]
                    decay = jnp.exp2(spread + bias_ref[n])
                    mix_ref[i - first, block(e), block(j - low)] = (decay * cross_ref[n]).astype(jnp.bfloat16)
            both = dot_nn(mix_ref[i - first, :, : (i + 1 - low) * LEN], xb_ref[low * LEN : (i + 1) * LEN, :])
            y = jnp.where(left_half, both[:LEN], both[LEN:])
            y_ref[at, :] = y
            gate = gate_ref[at, :]
            gated = (y + skip_ref[...] * x_ref[at, :]) * (gate * sigmoid(gate))
            gated_ref[at, :] = gated
            square_ref[at, :] = square_ref[at, :] + gated * gated

    for sub in range(GROUP):
        head_pair(GROUP * step + sub, *[t.at[:, block(sub)] for t in tiles])

    @pl.when(step == pl.num_programs(0) - 1)
    def _():
        for i in chunks:
            at = block(i - first)
            total = jnp.sum(square_ref[at, :], axis=1, keepdims=True)
            row_ref[0:1, at] = jnp.broadcast_to(total, (LEN, LEN)).T[0:1]


def attention_kernel(chunks, q_ref, kv_ref, seg_row_ref, out_ref, lse_ref):
    scale = HEAD_DIM ** (-0.5) * LOG2E
    first = chunks[0]
    left_half = lane_iota() < HEAD_DIM
    zero = jnp.zeros((LEN, LEN), jnp.bfloat16)
    lse_ref[...] = jnp.zeros(lse_ref.shape, jnp.float32)
    for i in chunks:
        at = block(i - first)
        low = max(0, i - 2) * LEN
        span = (i + 1) * LEN - low
        allowed = jnp.concatenate([mask_ts(seg_row_ref, i, j) for j in range(low // LEN, i + 1)], axis=1)
        keys = kv_ref[low : low + span, :]
        swapped = pltpu.roll(keys.astype(jnp.float32), HEAD_DIM, 1).astype(jnp.bfloat16)
        for p in range(q_ref.shape[1] // LEN):
            queries = q_ref[block(i), block(p)]
            result = []
            for e in range(2):
                masked = jnp.where(left_half == (e == 0), queries, zero)
                scores = dot_nt(masked, keys if e == 0 else swapped) * scale
                scores = jnp.where(allowed, scores, hidden_bias)
                top = jnp.max(scores, axis=1, keepdims=True)
                weights = jnp.exp2(scores - top)
                total = jnp.sum(weights, axis=1, keepdims=True)
                probs = (weights * (1.0 / total)).astype(jnp.bfloat16)
                result.append(dot_nn(probs, swapped if e == 0 else keys))
                lse = jnp.broadcast_to(top + jnp.log(total) * LOG2E, (LEN, LEN))
                lse_ref[2 * p + e : 2 * p + e + 1, at] = lse.T[0:1]
            out_ref[at, block(p)] = jnp.where(left_half, result[0], result[1]).astype(jnp.bfloat16)


def attention_back_kernel(chunks, final, *refs):
    q_ref, kv_ref, do_ref, lse_ref, seg_row_ref, cos_ref, sin_ref = refs[:7]
    if final:
        dk_in_ref, dv_in_ref, dq_ref, dkv_ref, dk_ref, dv_ref, turned_ref, key_t_ref = refs[7:]
    else:
        dq_ref, dk_ref, dv_ref, turned_ref, key_t_ref = refs[7:]
    scale = HEAD_DIM ** (-0.5)
    blocks = q_ref.shape[0] // LEN
    first = chunks[0]
    left_half = lane_iota() < HEAD_DIM
    zero = jnp.zeros((LEN, LEN), jnp.bfloat16)
    for i in range(chunks[-1] + 1):
        kv = kv_ref[block(i), :].astype(jnp.float32)
        turned_ref[block(i), :] = pltpu.roll(kv, HEAD_DIM, 1).astype(jnp.bfloat16)
        key_t_ref[:, block(i)] = kv.T[:HEAD_DIM].astype(jnp.bfloat16)
    if final:
        dk_ref[...] = dk_in_ref[...]
        dv_ref[...] = dv_in_ref[...]
    else:
        dk_ref[...] = jnp.zeros(dk_ref.shape, jnp.float32)
        dv_ref[...] = jnp.zeros(dv_ref.shape, jnp.float32)
    for i in chunks:
        at = block(i - first)
        low = max(0, i - 2) * LEN
        span = (i + 1) * LEN - low
        window = slice(low, low + span)
        allowed = jnp.concatenate([mask_st(seg_row_ref, j, i) for j in range(low // LEN, i + 1)], axis=0)
        keys, swapped = kv_ref[window, :], turned_ref[window, :]
        for p in range(q_ref.shape[1] // LEN):
            queries, douts = q_ref[block(i), block(p)], do_ref[at, block(p)]
            back = []
            for e in range(2):
                side = left_half == (e == 0)
                q_half = jnp.where(side, queries, zero)
                do_half = jnp.where(side, douts, zero)
                h = 2 * p + e
                scores = dot_nt(keys if e == 0 else swapped, q_half) * (scale * LOG2E)
                probs = jnp.exp2(jnp.where(allowed, scores, hidden_bias) - lse_ref[h : h + 1, at])
                dprobs = dot_nt(swapped if e == 0 else keys, do_half)
                inner = jnp.sum(probs * dprobs, axis=0, keepdims=True)
                dscores = (probs * (dprobs - inner)).astype(jnp.bfloat16)
                dv_ref[window, :] = dv_ref[window, :] + dot_nn(probs.astype(jnp.bfloat16), do_half)
                dk_ref[window, :] = dk_ref[window, :] + dot_nn(dscores, q_half)
                back.append(dot_nn(key_t_ref[:, window], dscores))
            dq = jnp.concatenate(back, axis=0).T * scale
            dq_ref[at, block(p)] = rotate_tile(dq, cos_ref[block(i), :], -sin_ref[block(i), :]).astype(jnp.bfloat16)
    if not final:
        return
    for i in range(blocks):
        dk = dk_ref[block(i), :]
        dk = (dk + pltpu.roll(dk, HEAD_DIM, 1)) * scale
        dk = rotate_tile(dk, cos_ref[block(i), :], -sin_ref[block(i), :])
        dv = dv_ref[block(i), :]
        dv = dv + pltpu.roll(dv, HEAD_DIM, 1)
        dkv_ref[block(i), :] = jnp.where(left_half, dk, dv).astype(jnp.bfloat16)


def scan_back_kernel(
    chunks,
    heads,
    gmr_ref,
    gated_ref,
    square_a_ref,
    square_b_ref,
    dot_a_ref,
    dot_b_ref,
    table_ref,
    gate_ref,
    y_ref,
    x_ref,
    xb_ref,
    state_ref,
    lag_ref,
    cum_row_ref,
    seg_row_ref,
    select_ref,
    dgate_ref,
    gy_ref,
    dx_ref,
    p_ref,
    grad_in_ref,
    grad_out_ref,
    sums_ref,
    gyb_ref,
    wide_ref,
    cross_ref,
    bias_ref,
    dcross_ref,
    inv_wide_ref,
    dot_wide_ref,
    inner_ref,
    mix_ref,
):
    step = pl.program_id(0)
    first = chunks[0]
    sources = chunks[-1] + 1
    left_half = lane_iota() < HEAD_DIM
    zero = jnp.zeros((LEN, LEN), jnp.bfloat16)
    spans = [(j, max(j, first), min(j + 3, sources)) for j in range(sources)]
    pairs = [(j, i) for j, start, stop in spans for i in range(start, stop)]

    @pl.when(step == 0)
    def _():
        for i in chunks:
            at = block(i - first)
            square = (square_a_ref[:, at] + square_b_ref[:, at]) / DSSM
            inv = lax.rsqrt(square + norm_eps)
            inv_wide_ref[at, :] = jnp.broadcast_to(inv, (LEN, LEN)).T
            dot = (dot_a_ref[:, at] + dot_b_ref[:, at]) / DSSM
            dot_wide_ref[at, :] = jnp.broadcast_to(dot, (LEN, LEN)).T
        p_ref[...] = jnp.zeros(p_ref.shape, jnp.float32)
        for h in range(heads):
            wide_ref[h] = jnp.broadcast_to(lag_ref[: sources * LEN, h : h + 1], (sources * LEN, LEN))
        for j, start, stop in spans:
            cross = three_dots(dot_nt, state_ref[block(j), :LEN], state_ref[start * LEN : stop * LEN, LEN:])
            for n, (j2, i) in enumerate(pairs):
                if j2 == j:
                    cross_ref[n] = cross[:, block(i - start)]
                    allowed = mask_st(seg_row_ref, j, i)
                    bias_ref[n] = jnp.where(allowed, 0.0, hidden_bias)
                    dcross_ref[n] = jnp.zeros((LEN, LEN), jnp.float32)

    tiles = (
        gmr_ref,
        gated_ref,
        table_ref.at[6:7],
        gate_ref,
        y_ref,
        x_ref,
        xb_ref,
        table_ref.at[5:6],
        dgate_ref,
        gy_ref,
        dx_ref,
        sums_ref,
    )

    def head_pair(
        hp,
        select,
        gmr_ref,
        gated_ref,
        gain_ref,
        gate_ref,
        y_ref,
        x_ref,
        xb_ref,
        skip_ref,
        dgate_ref,
        gy_ref,
        dx_ref,
        sums_ref,
    ):
        skip = skip_ref[...]
        gain = gain_ref[...]
        skip_sum = jnp.zeros((1, LEN), jnp.float32)
        gain_sum = jnp.zeros((1, LEN), jnp.float32)
        for i in chunks:
            at = block(i - first)
            inv = inv_wide_ref[at, :]
            unit = gated_ref[at, :] * inv
            rows_grad = gmr_ref[at, :]
            grad = inv * (rows_grad * gain - unit * dot_wide_ref[at, :])
            gate = gate_ref[at, :]
            sig = sigmoid(gate)
            y = y_ref[at, :]
            x = x_ref[at, :]
            gy = grad * (gate * sig)
            dgate_ref[at, :] = (grad * (y + skip * x) * (sig * (1.0 + gate * (1.0 - sig)))).astype(jnp.bfloat16)
            gyb = gy.astype(jnp.bfloat16)
            gy_ref[at, :] = gy
            gyb_ref[at, :] = gyb
            high, rest = two_terms(gyb.astype(jnp.float32) * y)
            p_ref[:, at] = p_ref[:, at] + dot_nt(select, high) + dot_nt(select, rest)
            skip_sum = skip_sum + jnp.sum(gy * x, axis=0, keepdims=True)
            gain_sum = gain_sum + jnp.sum(rows_grad * unit, axis=0, keepdims=True)
        sums_ref[0:1, :] = skip_sum
        sums_ref[1:2, :] = gain_sum

        for j, start, stop in spans:
            x_pair = xb_ref[block(j), :]
            x_both = jnp.concatenate([jnp.where(left_half, x_pair, zero), jnp.where(left_half, zero, x_pair)], axis=0)
            wide = (stop - start) * LEN
            gy_rows = gyb_ref[(start - first) * LEN : (stop - first) * LEN, :]
            inner_ref[:, :wide] = dot_nt(x_both, gy_rows)
            for n, (j2, i) in enumerate(pairs):
                if j2 != j:
                    continue
                grown = dcross_ref[n]
                for e in range(2):
                    spread = cum_row_ref[2 * hp + e, :, block(i)] - wide_ref[2 * hp + e, block(j), :]
                    decay = jnp.exp2(spread + bias_ref[n])
                    grown = grown + inner_ref[block(e), block(i - start)] * decay
                    mix_ref[block(e), block(i - start)] = (decay * cross_ref[n]).astype(jnp.bfloat16)
                dcross_ref[n] = grown
            both = dot_nn(mix_ref[:, :wide], gy_rows)
            dx_ref[block(j), :] = jnp.where(left_half, both[:LEN], both[LEN:])

    for sub in range(GROUP):
        head_pair(GROUP * step + sub, select_ref[:, block(sub)], *[t.at[:, block(sub)] for t in tiles])

    @pl.when(step == pl.num_programs(0) - 1)
    def _():
        grad_out = {i: jnp.zeros((LEN, LEN), jnp.float32) for i in chunks}
        for j in range(sources):
            grad_in = jnp.zeros((LEN, LEN), jnp.float32)
            for n, (j2, i) in enumerate(pairs):
                if j2 != j:
                    continue
                high, rest = two_terms(dcross_ref[n])
                out_high, out_rest = two_terms(state_ref[block(i), LEN:])
                in_high, in_rest = two_terms(state_ref[block(j), :LEN])
                grad_in = grad_in + dot_nn(high, out_high) + dot_nn(high, out_rest) + dot_nn(rest, out_high)
                grad_out[i] = grad_out[i] + dot_tn(high, in_high) + dot_tn(high, in_rest) + dot_tn(rest, in_high)
            grad_in_ref[block(j), :] = grad_in
        for i in chunks:
            grad_out_ref[block(i - first), :] = grad_out[i]


def conv_back(grad_ref, value_ref, keep_ref, taps, out_ref, sum_ref, lanes, blocks):
    totals = [jnp.zeros((1, LEN), jnp.float32) for _ in range(5)]
    for i in range(blocks):
        here = grad_ref[i * LEN : (i + 1) * LEN, :]
        grad = taps[3:4] * here
        totals[4] = totals[4] + jnp.sum(here, axis=0, keepdims=True)
        totals[3] = totals[3] + jnp.sum(here * value_ref[8 + i * LEN : 8 + (i + 1) * LEN, :], axis=0, keepdims=True)
        for lag in (1, 2, 3):
            ahead = grad_ref[i * LEN + lag : (i + 1) * LEN + lag, :]
            grad = grad + taps[3 - lag : 4 - lag] * (ahead * keep_ref[lag - 1, i * LEN + lag : (i + 1) * LEN + lag, :])
            moved = value_ref[8 + i * LEN - lag : 8 + (i + 1) * LEN - lag, :]
            masked = here * keep_ref[lag - 1, i * LEN : (i + 1) * LEN, :]
            totals[3 - lag] = totals[3 - lag] + jnp.sum(masked * moved, axis=0, keepdims=True)
        out_ref[block(i), lanes] = grad.astype(jnp.bfloat16)
    for tap in range(5):
        sum_ref[tap : tap + 1, lanes] = totals[tap]


def scan_end_kernel(
    heads,
    gy_a_ref,
    gy_b_ref,
    dx_a_ref,
    dx_b_ref,
    p_a_ref,
    p_b_ref,
    in_a_ref,
    in_b_ref,
    out_a_ref,
    out_b_ref,
    xb_ref,
    slope_ref,
    state_slope_ref,
    conv_ref,
    small_ref,
    step_row_ref,
    sig_row_ref,
    seg_row_ref,
    select_ref,
    table_ref,
    params_ref,
    dconv_ref,
    dstate_ref,
    dstep_ref,
    conv_sum_ref,
    state_sum_ref,
    step_sum_ref,
    grad_pad_ref,
    value_pad_ref,
    wide_ref,
    q_ref,
    flow_ref,
):
    step = pl.program_id(0)
    rows = conv_ref.shape[0]
    blocks = rows // LEN
    half = rows // 2
    count = flow_ref.shape[0]

    @pl.when(step == 0)
    def _():
        value_pad_ref[0:8, :] = jnp.zeros((8, LEN), jnp.float32)
        grad_pad_ref[rows : rows + 8, :] = jnp.zeros((8, LEN), jnp.float32)
        widen(seg_row_ref, wide_ref, value_pad_ref)
        value_pad_ref[0:8, :] = jnp.zeros((8, LEN), jnp.float32)
        q_ref[...] = jnp.zeros(q_ref.shape, jnp.float32)
        for c in range(2):
            if c == 0:
                grad_pad_ref[0:half, :] = (in_a_ref[...] + in_b_ref[0:half, :]) * state_slope_ref[0:half, block(c)]
                grad_pad_ref[half:rows, :] = in_b_ref[half:rows, :] * state_slope_ref[half:rows, block(c)]
            else:
                grad_pad_ref[0:half, :] = out_a_ref[...] * state_slope_ref[0:half, block(c)]
                grad_pad_ref[half:rows, :] = out_b_ref[...] * state_slope_ref[half:rows, block(c)]
            value_pad_ref[8 : rows + 8, :] = small_ref[:, block(c)]
            conv_back(
                grad_pad_ref,
                value_pad_ref,
                wide_ref,
                params_ref[8:12, block(c)],
                dstate_ref,
                state_sum_ref,
                block(c),
                blocks,
            )

    tiles = (
        gy_a_ref,
        gy_b_ref,
        dx_a_ref,
        dx_b_ref,
        xb_ref,
        slope_ref,
        conv_ref,
        table_ref.at[5:6],
        dconv_ref,
        conv_sum_ref,
    )

    def head_pair(
        select,
        taps,
        gy_a_ref,
        gy_b_ref,
        dx_a_ref,
        dx_b_ref,
        xb_ref,
        slope_ref,
        conv_ref,
        skip_ref,
        dconv_ref,
        conv_sum_ref,
    ):
        for j in range(blocks):
            dx = dx_b_ref[block(j), :]
            if j < blocks // 2:
                dx = dx + dx_a_ref[block(j), :]
                gy = gy_a_ref[block(j), :]
            else:
                gy = gy_b_ref[block(j - blocks // 2), :]
            high, rest = two_terms(dx * xb_ref[block(j), :].astype(jnp.float32))
            q_ref[:, block(j)] = q_ref[:, block(j)] + dot_nt(select, high) + dot_nt(select, rest)
            grad_pad_ref[block(j), :] = (dx + gy * skip_ref[...]) * slope_ref[block(j), :]
        value_pad_ref[8 : rows + 8, :] = conv_ref[...]
        conv_back(
            grad_pad_ref, value_pad_ref, wide_ref, taps, dconv_ref, conv_sum_ref, slice(0, LEN), blocks
        )

    for sub in range(GROUP):
        head_pair(select_ref[:, block(sub)], table_ref[0:4, block(sub)], *[t.at[:, block(sub)] for t in tiles])

    @pl.when(step == pl.num_programs(0) - 1)
    def _():
        q = q_ref[...]
        flow_ref[:, 0:half] = p_a_ref[...] - q[:, 0:half]
        flow_ref[:, half:rows] = p_b_ref[...] - q[:, half:rows]
        rate = turned(params_ref[14:15, :LEN])[:count]
        bias_total = jnp.zeros((count, LEN), jnp.float32)
        decay_total = jnp.zeros((count, LEN), jnp.float32)
        for j in range(blocks):
            log_grad = jnp.zeros((count, LEN), jnp.float32)
            for i in range(j, min(j + 3, blocks)):
                chosen = jnp.where(mask_st(seg_row_ref, j, i), 1.0, 0.0).astype(jnp.bfloat16)
                high, rest = two_terms(flow_ref[:, block(i)])
                log_grad = log_grad + dot_nt(high, chosen) + dot_nt(rest, chosen)
            step = step_row_ref[:, block(j)]
            grad_step = jnp.where(step > 1e-30, q[:, block(j)] / step, 0.0) + log_grad * rate
            grad_arg = grad_step * sig_row_ref[:, block(j)]
            bias_total = bias_total + grad_arg
            decay_total = decay_total + log_grad * step
            tall = jnp.concatenate([grad_arg, jnp.zeros((LEN - count, LEN), jnp.float32)], axis=0)
            dstep_ref[block(j), :] = tall.T.astype(jnp.bfloat16)
        step_sum_ref[0:count, :] = jnp.broadcast_to(jnp.sum(bias_total, axis=1, keepdims=True), (count, LEN))
        step_sum_ref[count : 2 * count, :] = jnp.broadcast_to(
            jnp.sum(decay_total * rate, axis=1, keepdims=True), (count, LEN)
        )


def whole_block(shape):
    return pl.BlockSpec(shape, lambda step: (0,) * len(shape), pipeline_mode=pl.Buffered(1))


def tile(rows, row_block=0, first=0):
    return pl.BlockSpec((rows, GROUP * LEN), lambda step: (row_block, first + step))


def small_block(rows, width):
    return pl.BlockSpec((rows, width), lambda step: (0, 2), pipeline_mode=pl.Buffered(1))


def call(kernel, steps, out_shape, out_specs, scratch, operands, specs, flops):
    return pl.pallas_call(
        kernel,
        grid=(steps,),
        out_shape=out_shape,
        in_specs=[s or whole_block(o.shape) for o, s in zip(operands, specs)],
        out_specs=[s or whole_block(o.shape) for o, s in zip(out_shape, out_specs)],
        scratch_shapes=scratch,
        compiler_params=pltpu.CompilerParams(vmem_limit_bytes=VMEM_BYTES),
        cost_estimate=pl.CostEstimate(flops=flops, bytes_accessed=0, transcendentals=0),
    )(*operands)


def f32(*shape):
    return jax.ShapeDtypeStruct(shape, jnp.float32)


def b16(*shape):
    return jax.ShapeDtypeStruct(shape, jnp.bfloat16)


HEAD_ROWS = 16
GROUP = 3
VMEM_BYTES = 60 * 1024 * 1024


def scan_prep(width, wide_in, cosine, sine, seg_row, params):
    rows = wide_in.shape[0]
    steps = width // LEN // GROUP
    outs = [
        f32(rows, width),
        b16(rows, width),
        f32(rows, width),
        f32(rows, 2 * LEN),
        f32(rows, 2 * LEN),
        f32(rows, LEN),
        f32(rows, LEN),
        f32(HEAD_ROWS, 1, rows),
        f32(HEAD_ROWS, 1, rows),
        f32(HEAD_ROWS, rows),
        f32(HEAD_ROWS, rows),
        b16(rows, 2 * LEN),
        b16(rows, LEN),
    ]
    scratch = [pltpu.VMEM((rows + 8, LEN), jnp.float32), pltpu.VMEM((3, rows + 8, LEN), jnp.float32)]
    operands = (wide_in, wide_in, cosine, sine, seg_row, params, params)
    specs = [tile(rows, 0, steps), small_block(rows, width), None, None, None, tile(16), None]
    return call(prep_kernel, steps, outs, [tile(rows)] * 3 + [None] * 10, scratch, operands, specs, 0 * 10**9)


def scan_forward(chunks, heads, wide_in, x, xb, *rest):
    width = x.shape[1]
    rows = LEN * len(chunks)
    at = chunks[0] // len(chunks)
    count = sum(min(i, 2) + 1 for i in chunks)
    outs = [f32(rows, width), f32(rows, width), f32(1, rows)]
    scratch = [
        pltpu.VMEM((heads, rows, LEN), jnp.float32),
        pltpu.VMEM((count, LEN, LEN), jnp.float32),
        pltpu.VMEM((count, LEN, LEN), jnp.float32),
        pltpu.VMEM((len(chunks), 2 * LEN, 3 * LEN), jnp.bfloat16),
        pltpu.VMEM((rows, LEN), jnp.float32),
    ]
    specs = [tile(rows, at), tile(rows, at), tile((chunks[-1] + 1) * LEN)] + [None] * (len(rest) - 1) + [tile(16)]
    kernel = functools.partial(scan_kernel, chunks, heads)
    operands = (wide_in, x, xb, *rest)
    return call(kernel, heads // 2 // GROUP, outs, [tile(rows), tile(rows), None], scratch, operands, specs, 0 * 10**9)


def attention_forward(chunks, q, kv, seg_row):
    rows = LEN * len(chunks)
    outs = [b16(rows, q.shape[1]), f32(8, rows)]
    kernel = functools.partial(attention_kernel, chunks)
    return call(kernel, 1, outs, [None] * 2, [], (q, kv, seg_row), [None] * 3, 0 * 10**9)


def attention_backward(chunks, final, *operands):
    q = operands[0]
    rows = q.shape[0]
    partial = [f32(rows, LEN), f32(rows, LEN)]
    sums = [pltpu.VMEM((rows, LEN), jnp.float32)] * 2
    outs = [b16(LEN * len(chunks), q.shape[1])] + ([b16(rows, LEN)] if final else partial)
    scratch = (sums if final else []) + [
        pltpu.VMEM((rows, LEN), jnp.bfloat16),
        pltpu.VMEM((HEAD_DIM, rows), jnp.bfloat16),
    ]
    kernel = functools.partial(attention_back_kernel, chunks, final)
    return call(kernel, 1, outs, [None] * len(outs), scratch, operands, [None] * len(operands), (0 if chunks[0] else 30) * 10**9)


def scan_backward(chunks, heads, *operands):
    rows, width = operands[0].shape
    at = chunks[0] // len(chunks)
    sources = (chunks[-1] + 1) * LEN
    count = sum(min(i, 2) + 1 for i in chunks)
    outs = [
        b16(rows, width),
        f32(rows, width),
        f32(sources, width),
        f32(HEAD_ROWS, rows),
        f32(sources, LEN),
        f32(rows, LEN),
        f32(8, width),
    ]
    scratch = [
        pltpu.VMEM((rows, LEN), jnp.bfloat16),
        pltpu.VMEM((heads, sources, LEN), jnp.float32),
        pltpu.VMEM((count, LEN, LEN), jnp.float32),
        pltpu.VMEM((count, LEN, LEN), jnp.float32),
        pltpu.VMEM((count, LEN, LEN), jnp.float32),
        pltpu.VMEM((rows, LEN), jnp.float32),
        pltpu.VMEM((rows, LEN), jnp.float32),
        pltpu.VMEM((2 * LEN, 3 * LEN), jnp.float32),
        pltpu.VMEM((2 * LEN, 3 * LEN), jnp.bfloat16),
    ]
    specs = [tile(rows), tile(rows), None, None, None, None, tile(16), tile(rows, at), tile(rows), tile(rows, at), tile(sources)]
    specs += [None, None, None, None, tile(HEAD_ROWS)]
    out_specs = [tile(rows), tile(rows), tile(sources), None, None, None, tile(8)]
    kernel = functools.partial(scan_back_kernel, chunks, heads)
    return call(kernel, heads // 2 // GROUP, outs, out_specs, scratch, operands, specs, 30 * 10**9)


def scan_end(heads, *operands):
    rows, width = 2 * operands[0].shape[0], operands[0].shape[1]
    steps = heads // 2 // GROUP
    outs = [
        b16(rows, width),
        b16(rows, 2 * LEN),
        b16(rows, LEN),
        f32(8, width),
        f32(8, 2 * LEN),
        f32(2 * HEAD_ROWS, LEN),
    ]
    scratch = [
        pltpu.VMEM((rows + 8, LEN), jnp.float32),
        pltpu.VMEM((rows + 8, LEN), jnp.float32),
        pltpu.VMEM((3, rows + 8, LEN), jnp.float32),
        pltpu.VMEM((HEAD_ROWS, rows), jnp.float32),
        pltpu.VMEM((HEAD_ROWS, rows), jnp.float32),
    ]
    half = rows // 2
    specs = [tile(half), tile(half), tile(half), tile(rows)] + [None] * 6 + [tile(rows), tile(rows), None]
    specs += [tile(rows, 0, steps), small_block(rows, width), None, None, None, tile(HEAD_ROWS), tile(16), None]
    out_specs = [tile(rows), None, None, tile(8), None, None]
    kernel = functools.partial(scan_end_kernel, heads)
    return call(kernel, steps, outs, out_specs, scratch, operands, specs, 30 * 10**9)


def inverse_rms(rows):
    return lax.rsqrt(jnp.mean(rows * rows, axis=-1, keepdims=True) + norm_eps)


def ffn_kernel(
    tokens_ref,
    part_ref,
    far_ref,
    gain_ref,
    gate_ref,
    up_ref,
    down_ref,
    cotangent_ref,
    hidden_ref,
    normed_ref,
    activated_ref,
    grad_gate_ref,
    grad_up_ref,
    back_ref,
    out_ref,
):
    @pl.when(pl.program_id(0) == 0)
    def _():
        hidden = tokens_ref[...].astype(jnp.float32) + (part_ref[...] + far_ref[...])
        hidden_ref[...] = hidden
        normed_ref[...] = (hidden * inverse_rms(hidden) * gain_ref[...]).astype(jnp.bfloat16)
        back_ref[...] = jnp.zeros(back_ref.shape, jnp.float32)
        out_ref[...] = jnp.zeros(out_ref.shape, jnp.float32)

    normed = normed_ref[...]
    gate = dot_nn(normed, gate_ref[...])
    up = dot_nn(normed, up_ref[...])
    sig = sigmoid(gate)
    act = gate * sig
    activated = (act * up).astype(jnp.bfloat16)
    activated_ref[...] = activated
    grad = dot_nt(cotangent_ref[...], down_ref[...])
    grad_gate = (grad * up * (sig * (1.0 + gate * (1.0 - sig)))).astype(jnp.bfloat16)
    grad_up = (grad * act).astype(jnp.bfloat16)
    grad_gate_ref[...] = grad_gate
    grad_up_ref[...] = grad_up
    back_ref[...] = back_ref[...] + (dot_nt(grad_gate, gate_ref[...]) + dot_nt(grad_up, up_ref[...]))
    out_ref[...] = out_ref[...] + dot_nn(activated, down_ref[...])


def ffn(chunks, tokens, part, far, gain, gate, up, down, cotangent):
    rows, model_width = part.shape
    at = chunks[0] // len(chunks)
    hidden_width = gate.shape[1]
    steps = hidden_width // 256
    outs = [f32(rows, model_width), b16(rows, model_width)] + [b16(rows, hidden_width)] * 3
    outs += [f32(rows, model_width)] * 2
    rows_of = pl.BlockSpec((rows, model_width), lambda step: (at, 0), pipeline_mode=pl.Buffered(1))
    columns = pl.BlockSpec((model_width, 256), lambda step: (0, step))
    tiles = pl.BlockSpec((rows, 256), lambda step: (0, step))
    specs = [rows_of, None, None, None, columns, columns]
    specs += [pl.BlockSpec((256, model_width), lambda step: (step, 0)), rows_of]
    operands = (tokens, part, far, gain, gate, up, down, cotangent)
    return call(ffn_kernel, steps, outs, [None, None, tiles, tiles, tiles, None, None], [], operands, specs, 0 * 10**9)


def middle_kernel(
    hidden_ref,
    part_ref,
    far_ref,
    cotangent_ref,
    gain_ref,
    gated_ref,
    square_a_ref,
    square_b_ref,
    params_ref,
    mixer_out_ref,
    attn_out_ref,
    grad_hidden_ref,
    grad_branch_ref,
    grad_rows_ref,
    grad_attended_ref,
    dot_ref,
    gain_sum_ref,
):
    hidden = hidden_ref[...]
    inv = inverse_rms(hidden)
    unit = hidden * inv
    grad_normed = part_ref[...] + far_ref[...]
    gain_sum_ref[0:1, :] = jnp.sum(grad_normed * unit, axis=0, keepdims=True)
    grad_unit = grad_normed * gain_ref[...]
    inner = jnp.mean(grad_unit * unit, axis=-1, keepdims=True)
    grad_hidden = cotangent_ref[...].astype(jnp.float32) + inv * (grad_unit - unit * inner)
    grad_hidden_ref[...] = grad_hidden
    grad_branch = grad_hidden.astype(jnp.bfloat16)
    grad_branch_ref[...] = grad_branch
    grad_rows = dot_nt(grad_branch, mixer_out_ref[...])
    grad_rows_ref[...] = grad_rows
    grad_attended_ref[...] = dot_nt(grad_branch, attn_out_ref[...]).astype(jnp.bfloat16)
    total = jnp.sum(grad_rows * params_ref[6:7, :] * gated_ref[...], axis=-1, keepdims=True)
    for i in range(hidden.shape[0] // LEN):
        at = block(i)
        inv_gated = lax.rsqrt((square_a_ref[:, at] + square_b_ref[:, at]) / DSSM + norm_eps)
        dot_ref[0:1, at] = jnp.broadcast_to(total[at], (LEN, LEN)).T[0:1] * inv_gated


def middle(chunks, hidden, part, far, cotangent, gain, gated, square_a, square_b, gated_gain, mixer_out, attn_out):
    rows, model_width = part.shape
    at = chunks[0] // len(chunks)
    width, inner = mixer_out.shape[0], attn_out.shape[0]
    outs = [
        f32(rows, model_width),
        b16(rows, model_width),
        f32(rows, width),
        b16(rows, inner),
        f32(1, rows),
        f32(8, model_width),
    ]
    rows_of = pl.BlockSpec((rows, model_width), lambda step: (at, 0), pipeline_mode=pl.Buffered(1))
    specs = [None, None, None, rows_of] + [None] * 7
    operands = (hidden, part, far, cotangent, gain, gated, square_a, square_b, gated_gain, mixer_out, attn_out)
    return call(middle_kernel, 1, outs, [None] * 6, [], operands, specs, (0 if chunks[0] else 90) * 10**9)


def core_call(kernel, steps, core, out_shape, out_spec, scratch, operands, specs, flops, aliases=None):
    return pl.pallas_call(
        kernel,
        grid_spec=pltpu.PrefetchScalarGridSpec(
            num_scalar_prefetch=1, grid=(steps,), in_specs=specs, out_specs=out_spec, scratch_shapes=scratch
        ),
        out_shape=out_shape,
        compiler_params=pltpu.CompilerParams(vmem_limit_bytes=VMEM_BYTES),
        cost_estimate=pl.CostEstimate(flops=flops, bytes_accessed=0, transcendentals=0),
        input_output_aliases=aliases or {},
    )(core, *operands)


def clip_tile(rows, columns, first, last):
    return pl.BlockSpec((rows, columns), lambda step, core_ref: (0, jnp.clip(step - first, 0, last - first - 1)))


def ffn_weights_kernel(add, core_ref, *refs):
    refs = list(refs)
    normed_a, normed_b, act_a, act_b, gate_a, gate_b, up_a, up_b, cot_a, cot_b = refs[:10]
    far_ref = refs[10] if add else None
    out_ref, left_ref = refs[-2:]
    step = pl.program_id(0)
    third = pl.num_programs(0) // 3
    half = normed_a.shape[0]

    def turn(first, second):
        left_ref[:, :half] = first[...].T
        left_ref[:, half:] = second[...].T

    @pl.when(step == 0)
    def _():
        turn(normed_a, normed_b)

    @pl.when(step == 2 * third)
    def _():
        turn(act_a, act_b)

    def product(first, second):
        result = dot_nn(left_ref[:, :half], first[...]) + dot_nn(left_ref[:, half:], second[...])
        out_ref[...] = result + far_ref[...] if add else result

    @pl.when(step < third)
    def _():
        product(gate_a, gate_b)

    @pl.when((step >= third) & (step < 2 * third))
    def _():
        product(up_a, up_b)

    @pl.when(step >= 2 * third)
    def _():
        product(cot_a, cot_b)


def ffn_weights(core, far, normed_a, normed_b, act_a, act_b, gate_a, gate_b, up_a, up_b, cotangent):
    half, columns = normed_a.shape
    kept = columns // 2
    tile_width = 512
    third = columns // tile_width
    left = pl.BlockSpec((half, kept), lambda step, core_ref: (0, core_ref[0]), pipeline_mode=pl.Buffered(1))
    specs = [left] * 4 + [clip_tile(half, tile_width, 0, third)] * 2
    specs += [clip_tile(half, tile_width, third, 2 * third)] * 2

    def cot_rows(at):
        return pl.BlockSpec(
            (half, tile_width), lambda step, core_ref: (at, jnp.clip(step - 2 * third, 0, third - 1))
        )

    specs += [cot_rows(0), cot_rows(1)]
    out = pl.BlockSpec((kept, tile_width), lambda step, core_ref: (0, step))
    operands = [normed_a, normed_b, act_a, act_b, gate_a, gate_b, up_a, up_b, cotangent, cotangent]
    if far is not None:
        operands.append(far)
        specs.append(out)
    return core_call(
        functools.partial(ffn_weights_kernel, far is not None),
        3 * third,
        core,
        f32(kept, (3 if far is None else 4) * columns),
        out,
        [pltpu.VMEM((kept, 2 * half), jnp.bfloat16)],
        operands,
        specs,
        0 * 10**9,
    )


def outer_weights_kernel(add, core_ref, *refs):
    refs = list(refs)
    rows_a, rows_b, edge_a, edge_b, att_a, att_b, branch_a, branch_b = refs[:8]
    out_ref, left_ref = refs[-2:]
    half = rows_a.shape[0]
    middle_row = left_ref.shape[0] // 2

    @pl.when((pl.program_id(0) == 0) & (core_ref[0] == 0))
    def _():
        left_ref[:, :half] = rows_a[...].T
        left_ref[:, half:] = rows_b[...].T

    @pl.when((pl.program_id(0) == 0) & (core_ref[0] == 1))
    def _():
        left_ref[:middle_row, :half] = edge_a[...].T
        left_ref[:middle_row, half:] = edge_b[...].T
        left_ref[middle_row:, :half] = att_a[...].T
        left_ref[middle_row:, half:] = att_b[...].T

    result = dot_nn(left_ref[:, :half], branch_a[...]) + dot_nn(left_ref[:, half:], branch_b[...])
    out_ref[...] = result + refs[8][...] if add else result


def outer_weights(core, far, buffer, rows_a, rows_b, att_a, att_b, branch_a, branch_b):
    half, width = rows_a.shape
    model_width = branch_a.shape[1]
    kept = model_width // 2
    tile_width = 512
    steps = model_width // tile_width

    def fixed(shape, column=0):
        return pl.BlockSpec(shape, lambda step, core_ref: (0, column), pipeline_mode=pl.Buffered(1))

    specs = [fixed((half, kept))] * 2
    specs += [fixed((half, width - kept), kept // (width - kept))] * 2
    specs += [fixed(att_a.shape)] * 2 + [clip_tile(half, tile_width, 0, steps)] * 2
    operands = [rows_a, rows_b, rows_a, rows_b, att_a, att_b, branch_a, branch_b]
    out = pl.BlockSpec((kept, tile_width), lambda step, core_ref: (0, step))
    columns, aliases = model_width, {}
    if far is not None:
        operands += [far, buffer]
        specs += [out, pl.BlockSpec(memory_space=pl.ANY)]
        columns = buffer.shape[1]
        first = columns // tile_width - steps
        out = pl.BlockSpec((kept, tile_width), lambda step, core_ref: (0, first + step))
        aliases = {len(operands): 0}
    return core_call(
        functools.partial(outer_weights_kernel, far is not None),
        steps,
        core,
        f32(kept, columns),
        out,
        [pltpu.VMEM((kept, 2 * half), jnp.bfloat16)],
        operands,
        specs,
        0,
        aliases,
    )


PARTS = ((0, 3), (3, 5), (5, 7), (7, 9))


def mixer_weights_kernel(add, core_ref, *refs):
    refs = list(refs)
    normed_ref, gate_a, gate_b, conv_ref, query_a, query_b, state_ref, pair_ref, step_ref = refs[:9]
    far_ref, table_ref = refs[9:11] if add else (None, None)
    outs = refs[11:19] if add else refs[9:10]
    left_ref, result_ref = refs[-2:]
    step = pl.program_id(0)
    half = gate_a.shape[0]

    @pl.when(step == 0)
    def _():
        left_ref[...] = normed_ref[...].T

    def two(first, second):
        result_ref[...] = dot_nn(left_ref[:, :half], first[...]) + dot_nn(left_ref[:, half:], second[...])

    @pl.when(step < 3)
    def _():
        two(gate_a, gate_b)

    @pl.when((step >= 3) & (step < 6))
    def _():
        result_ref[...] = dot_nn(left_ref[...], conv_ref[...])

    @pl.when(step == 6)
    def _():
        two(query_a, query_b)

    @pl.when(step == 7)
    def _():
        result_ref[...] = dot_nn(left_ref[...], state_ref[...])

    @pl.when(step == 8)
    def _():
        result_ref[:, :LEN] = dot_nn(left_ref[...], pair_ref[...])
        steps = dot_nn(left_ref[...], step_ref[...])
        result_ref[:, LEN:] = steps + table_ref[...] if add else steps

    if not add:
        outs[0][...] = result_ref[...]
        return
    result_ref[...] = result_ref[...] + far_ref[...]
    for k, (first, last) in enumerate(PARTS):

        @pl.when((step >= first) & (step < last))
        def _():
            for side in range(2):
                out_ref = outs[2 * k + side]
                for q in range(2):
                    index = core_ref[1 + 4 * k + 2 * side + q]
                    if k < 2:
                        for y in range(4):
                            start = pl.multiple_of((4 * y + index) * 32, 32)
                            out_ref[(2 * y + q) * 32 : (2 * y + q + 1) * 32, :] = result_ref[pl.ds(start, 32), :]
                    else:
                        start = pl.multiple_of(index * LEN, LEN)
                        out_ref[q * LEN : (q + 1) * LEN, :] = result_ref[pl.ds(start, LEN), :]


def mixer_weights(core, far, table, normed, gate_a, gate_b, conv, query_a, query_b, state, pair, step):
    half = gate_a.shape[0]
    rows, model_width = normed.shape
    kept = model_width // 2
    tile_width = 256
    steps = 9

    def fixed(shape, column=0):
        return pl.BlockSpec(shape, lambda step, core_ref: (0, column), pipeline_mode=pl.Buffered(1))

    specs = [pl.BlockSpec((rows, kept), lambda step, core_ref: (0, core_ref[0]), pipeline_mode=pl.Buffered(1))]
    specs += [clip_tile(half, tile_width, 0, 3)] * 2 + [clip_tile(rows, tile_width, 3, 6)]
    specs += [fixed(query_a.shape)] * 2 + [fixed(state.shape), fixed(pair.shape), fixed(step.shape)]
    operands = [normed, gate_a, gate_b, conv, query_a, query_b, state, pair, step]
    out = pl.BlockSpec((kept, tile_width), lambda step, core_ref: (0, step))
    shape = f32(kept, steps * tile_width)
    if far is not None:
        operands += [far, table]
        specs += [out, fixed(table.shape)]
        out, shape = [], []
        for first, last in PARTS:
            out += [clip_tile(kept // 2, tile_width, first, last)] * 2
            shape += [f32(kept // 2, (last - first) * tile_width)] * 2
    return core_call(
        functools.partial(mixer_weights_kernel, far is not None),
        steps,
        core,
        shape,
        out,
        [pltpu.VMEM((kept, rows), jnp.bfloat16), pltpu.VMEM((kept, tile_width), jnp.float32)],
        operands,
        specs,
        30 * 10**9,
    )


def normed_back_kernel(
    gate_a,
    gate_b,
    conv_ref,
    query_a,
    query_b,
    state_ref,
    pair_ref,
    step_ref,
    wide_ref,
    small_ref,
    tokens_ref,
    whole_ref,
    out_ref,
    sum_ref,
    inv_ref,
):
    @pl.when(pl.program_id(0) == 0)
    def _():
        inv_ref[...] = jnp.broadcast_to(inverse_rms(whole_ref[...].astype(jnp.float32)), inv_ref.shape)

    half, width = gate_a.shape
    query_width = query_a.shape[1]
    gate_w, conv_w = wide_ref[:, :width], wide_ref[:, width:]
    state_w = small_ref[:, : 2 * LEN]
    query_w = small_ref[:, 2 * LEN : 2 * LEN + query_width]
    pair_w = small_ref[:, 2 * LEN + query_width : 3 * LEN + query_width]
    step_w = small_ref[:, 3 * LEN + query_width :]
    total = jnp.zeros((1, out_ref.shape[1]), jnp.float32)
    for k, (gate, query) in enumerate(((gate_a, query_a), (gate_b, query_b))):
        at = slice(k * half, (k + 1) * half)
        grad = dot_nt(gate[...], gate_w) + dot_nt(conv_ref[at, :], conv_w) + dot_nt(query[...], query_w)
        grad = grad + dot_nt(state_ref[at, :], state_w) + dot_nt(pair_ref[at, :], pair_w) + dot_nt(step_ref[at, :], step_w)
        out_ref[at, :] = grad
        unit = tokens_ref[at, :].astype(jnp.float32) * jnp.concatenate([inv_ref[at, :]] * 2, axis=1)
        total = total + jnp.sum(grad * unit, axis=0, keepdims=True)
    sum_ref[0:1, :] = total


def normed_back(gate_a, gate_b, conv, query_a, query_b, state, pair, step, wide_proj, small_proj, tokens):
    rows, model_width = tokens.shape
    tile_width = 256
    operands = (gate_a, gate_b, conv, query_a, query_b, state, pair, step, wide_proj, small_proj, tokens, tokens)

    def weights(count):
        return pl.BlockSpec((tile_width, count), lambda step: (step, 0))

    columns = pl.BlockSpec((rows, tile_width), lambda step: (0, step))
    specs = [None] * 8 + [weights(wide_proj.shape[1]), weights(small_proj.shape[1]), columns, None]
    out_specs = [columns, pl.BlockSpec((8, tile_width), lambda step: (0, step))]
    outs = [f32(rows, model_width), f32(8, model_width)]
    return call(
        normed_back_kernel,
        model_width // tile_width,
        outs,
        out_specs,
        [pltpu.VMEM((rows, LEN), jnp.float32)],
        operands,
        specs, 30 * 10**9)


def project_kernel(wide_steps, tokens_ref, gain_ref, wide_ref, small_ref, out_ref, normed_ref):
    step = pl.program_id(0)

    @pl.when(step == 0)
    def _():
        tokens = tokens_ref[...].astype(jnp.float32)
        normed_ref[...] = (tokens * inverse_rms(tokens) * gain_ref[...]).astype(jnp.bfloat16)

    @pl.when(step < wide_steps)
    def _():
        out_ref[...] = dot_nn(normed_ref[...], wide_ref[...])

    @pl.when(step >= wide_steps)
    def _():
        out_ref[...] = dot_nn(normed_ref[...], small_ref[...])


def project(tokens, gain, wide_proj, small_proj):
    rows, model_width = tokens.shape
    count = 768
    wide_steps = wide_proj.shape[1] // count
    steps = wide_steps + small_proj.shape[1] // count
    outs = [f32(rows, steps * count), b16(rows, model_width)]
    wide = pl.BlockSpec((model_width, count), lambda step: (0, jnp.minimum(step, wide_steps - 1)))
    small = pl.BlockSpec((model_width, count), lambda step: (0, jnp.maximum(step - wide_steps, 0)))
    out = pl.BlockSpec((rows, count), lambda step: (0, step))
    operands = (tokens, gain, wide_proj, small_proj)
    kernel = functools.partial(project_kernel, wide_steps)
    return call(kernel, steps, outs, [out, None], [], operands, [None, None, wide, small], 0)


def unpack_kernel(
    block_ref,
    step_ref,
    input_gain_ref,
    state_kernel_ref,
    state_bias_ref,
    step_bias_ref,
    decay_ref,
    skip_ref,
    conv_kernel_ref,
    conv_bias_ref,
    gated_gain_ref,
    ffn_gain_ref,
    turned_ref,
):
    heads = step_ref.shape[0]
    for i in range(block_ref.shape[0] // LEN):
        turned_ref[:, block(i)] = block_ref[block(i), :].T

    def row(index, count, start=0):
        return turned_ref[heads + index, start : start + count]

    step_ref[...] = turned_ref[0:heads, :]
    input_gain_ref[...] = row(0, input_gain_ref.shape[0])
    columns = state_kernel_ref.shape[1]
    for tap in range(4):
        state_kernel_ref[tap, :] = row(1, columns, tap * columns)
        conv_kernel_ref[tap, :] = row(4 + tap, conv_kernel_ref.shape[1])
    state_bias_ref[...] = row(2, columns)
    step_bias_ref[...] = row(3, heads)
    decay_ref[...] = row(3, heads, LEN)
    skip_ref[...] = row(3, heads, 2 * LEN)
    conv_bias_ref[...] = row(8, conv_bias_ref.shape[0])
    gated_gain_ref[...] = row(9, gated_gain_ref.shape[0])
    ffn_gain_ref[...] = row(10, ffn_gain_ref.shape[0])


def unpack(heads, width, states, values):
    rows = values.shape[0]
    outs = [f32(heads, rows), f32(rows), f32(4, states), f32(states), f32(heads), f32(heads), f32(heads)]
    outs += [f32(4, width), f32(width), f32(width), f32(rows)]
    scratch = [pltpu.VMEM((LEN, rows), jnp.float32)]
    return call(unpack_kernel, 1, outs, [None] * len(outs), scratch, (values,), [None], 0)


def assemble_kernel(source, mixer_proj_ref, query_ref, pair_ref, state_ref, step_ref):
    width = mixer_proj_ref.shape[2]
    start = 0
    mixer_proj_ref[:, 0, :] = source[:, start : start + width]
    start += width
    mixer_proj_ref[:, 1, :] = source[:, start : start + width]
    start += width
    query_ref[...] = source[:, start : start + query_ref.shape[1]]
    start += query_ref.shape[1]
    state_ref[...] = source[:, start : start + 2 * LEN]
    start += 2 * LEN
    pair_ref[:, 0, :] = source[:, start : start + LEN]
    step_ref[...] = source[:, start + LEN :]


def assemble(values, width, query_width):
    rows, columns = values.shape

    def plain(count):
        return pl.BlockSpec((LEN, count), lambda at: (at, 0))

    out_specs = [
        pl.BlockSpec((LEN, 2, width), lambda at: (at, 0, 0)),
        plain(query_width),
        pl.BlockSpec((LEN, 1, LEN), lambda at: (at, 0, 0)),
        plain(2 * LEN),
        plain(LEN),
    ]
    out_shape = [
        f32(rows, 2, width),
        f32(rows, query_width),
        f32(rows, 1, LEN),
        f32(rows, 2 * LEN),
        f32(rows, LEN),
    ]
    return call(assemble_kernel, rows // LEN, out_shape, out_specs, [], (values,), [plain(columns)], 0)


LINKS = {
    "A": [(0, 1), (1, 0), (2, 3), (3, 2)],
    "B": [(1, 2), (2, 1), (3, 0), (0, 3)],
}
ORDERS = (
    (("x", "A"), ("x", "B"), ("y", "A"), ("y", "B")),
    (("x", "B"), ("y", "A"), ("y", "B"), ("x", "A")),
    (("y", "A"), ("y", "B"), ("x", "A"), ("x", "B")),
    (("y", "B"), ("x", "A"), ("x", "B"), ("y", "A")),
)
AXIS = {"y": 0, "x": 1}


def take(values, index, axis):
    return lax.dynamic_slice_in_dim(values, index, 1, axis)


def halves(values, name, link, again):
    place, axis = lax.axis_index(name), AXIS[name]
    if again:
        index = place // 2 if link == "B" else place % 2
        return take(values, index, axis), take(values, 1 - index, axis)
    if link == "B":
        side = place // 2
        kept = lax.dynamic_slice_in_dim(values, 2 * side, 2, axis)
        return kept, lax.dynamic_slice_in_dim(values, 2 - 2 * side, 2, axis)
    side = ((place + 1) // 2) % 2
    kept = jnp.concatenate([take(values, side, axis), take(values, 3 - side, axis)], axis)
    return kept, jnp.concatenate([take(values, 1 - side, axis), take(values, 2 + side, axis)], axis)


def reduce_rows(pairs, steps):
    kept, sent, parts = [], [], pairs
    if steps[0] == 0:
        for k, (stays, goes) in enumerate(pairs):
            shape = (4, 2, 32, stays.shape[1]) if ORDERS[k][0][0] == "x" else (2, 4, 32, stays.shape[1])
            kept.append(stays.reshape(shape))
            sent.append(goes.reshape(shape))
    for step in steps:
        if step:
            kept, sent = [], []
            for k in range(4):
                name, link = ORDERS[k][step]
                again = name in [n for n, _ in ORDERS[k][:step]]
                stays, goes = halves(parts[k], name, link, again)
                kept.append(stays)
                sent.append(goes)
        sent = lax.optimization_barrier(tuple(sent))
        come = [lax.ppermute(sent[k], ORDERS[k][step][0], LINKS[ORDERS[k][step][1]]) for k in range(4)]
        come = lax.optimization_barrier(tuple(come))
        parts = [stays + more for stays, more in zip(kept, come)]
    return parts


def rope_tables(rows):
    half_size = HEAD_DIM // 2
    inverse = np.float32(rope_base) ** (-(2.0 * np.arange(half_size, dtype=np.float32)) / HEAD_DIM)
    angles = np.arange(rows, dtype=np.float32)[:, None] * inverse.astype(np.float32)[None, :]
    cosine, sine = np.cos(angles), np.sin(angles)
    return (
        np.concatenate([cosine] * 4, axis=1).astype(np.float32),
        np.concatenate([-sine, sine, -sine, sine], axis=1).astype(np.float32),
    )


def norm_backward(grad_unit, unit_rows, inv_rms):
    return inv_rms * (grad_unit - unit_rows * jnp.mean(grad_unit * unit_rows, axis=-1, keepdims=True))


def dot32(left, right):
    return jnp.dot(left, right, preferred_element_type=jnp.float32)


def after(value, *others):
    return lax.optimization_barrier((value, *others))[0]


def swap(values, name):
    return lax.ppermute(values, name, PAIR)


def exchange(values, name):
    return values + swap(values, name)


def core_rows(values, index):
    half = values.shape[1] // 2
    return lax.dynamic_slice_in_dim(values, index * half, half, 1)


def on_device(
    layer_input,
    segments,
    input_gain,
    mixer_proj,
    state_proj,
    step_proj,
    step_bias,
    decay_log,
    skip_gain,
    conv_kernel,
    conv_bias,
    state_kernel,
    state_bias,
    gated_gain,
    mixer_out,
    query_proj,
    key_value_weight,
    attn_out,
    ffn_gain,
    ffn_gate,
    ffn_up,
    ffn_down,
    cotangent,
):
    rows, model_width = layer_input.shape
    width = mixer_proj.shape[2]
    heads = step_proj.shape[1]
    state_size = state_proj.shape[1] // 2
    query_width = query_proj.shape[1]
    pair_width = key_value_weight.shape[2]
    place = lax.axis_index("core")
    zh = lax.axis_index("zh")
    core = place.astype(jnp.int32).reshape(1)
    far_core = 1 - core
    cosine, sine = rope_tables(rows)
    select = np.arange(HEAD_ROWS)[:, None] == np.arange(width)[None, :] // HEAD_DIM
    select = jnp.asarray(select.astype(np.float32)).astype(jnp.bfloat16)
    seg_row = segments.astype(jnp.float32)
    pad_heads = ((0, 0), (0, LEN - heads))

    def padded(values):
        return jnp.pad(values, ((0, 0), (0, width - values.shape[1])))

    params = jnp.concatenate(
        [
            conv_kernel,
            conv_bias[None, :],
            jnp.repeat(skip_gain, HEAD_DIM)[None, :],
            gated_gain[None, :],
            jnp.zeros((1, width), jnp.float32),
            padded(state_kernel),
            padded(state_bias[None, :]),
            padded(step_bias[None, :]),
            padded(-jnp.exp(decay_log)[None, :]),
            jnp.zeros((1, width), jnp.float32),
        ],
        axis=0,
    )
    wide_proj = mixer_proj.reshape(model_width, 2 * width)
    small_proj = jnp.concatenate(
        [
            state_proj,
            query_proj,
            key_value_weight.reshape(model_width, pair_width),
            jnp.pad(step_proj, pad_heads),
        ],
        axis=1,
    )
    tokens = layer_input.astype(jnp.float32)
    wide_in, normed_input = project(layer_input, input_gain[None, :], wide_proj, small_proj)
    x, xb, slope, state, state_slope, cum, lag, cum_row, lag_row, step_row, sig_row, queries, pairs = scan_prep(
        width,
        wide_in,
        cosine,
        sine,
        seg_row,
        params,
    )

    blocks = rows // LEN
    late = tuple(range(blocks // 2, blocks))
    early = tuple(range(blocks // 2))
    half = {}
    for chunks in (late, early):
        h = {"span": slice(chunks[0] * LEN, (chunks[-1] + 1) * LEN)}
        h["y"], h["gated"], h["square"] = scan_forward(
            chunks, heads, wide_in, x, xb, state, cum, lag_row, seg_row, params
        )
        half[chunks] = h
    squares = jnp.concatenate([half[early]["square"], half[late]["square"]], axis=1)
    squares_far = swap(squares, "tensor")
    ready = squares
    for chunks in (late, early):
        h = half[chunks]
        h["attended"], h["lse"] = attention_forward(chunks, after(queries, ready), pairs, seg_row)
        if chunks == late:
            squares_far = after(squares_far, h["lse"])
            squares_all = squares + squares_far
        h["square"], h["square_far"] = squares[:, h["span"]], squares_far[:, h["span"]]
        h["inv_gated"] = lax.rsqrt(squares_all[:, h["span"]].reshape(-1, 1) / DSSM + norm_eps)
        h["mixer_rows"] = (h["gated"] * h["inv_gated"] * gated_gain).astype(jnp.bfloat16)
        h["part"] = dot32(h["mixer_rows"], mixer_out) + dot32(h["attended"], attn_out)
        h["branch_far"] = swap(h["part"], "tensor")
        ready = h["part"]

    a, b = half[early], half[late]
    gain_ffn = ffn_gain[None, :]
    names = ("hidden", "normed", "activated", "grad_gate_rows", "grad_up_rows", "back", "down")
    for chunks in (late, early):
        h = half[chunks]
        far = h["branch_far"] if chunks == late else after(h["branch_far"], b["back"])
        operands = (layer_input, h["part"], far, gain_ffn, ffn_gate, ffn_up, ffn_down, cotangent)
        h.update(zip(names, ffn(chunks, *operands)))
        h["back_far"] = swap(h["back"], "tensor")

    for chunks in (late, early):
        h = half[chunks]
        far = h["back_far"] if chunks == late else after(h["back_far"], first)
        h["grad_hidden"], h["grad_branch"], h["grad_rows"], grad_attended, h["dot"], h["gain_sum"] = middle(
            chunks,
            h["hidden"],
            h["back"],
            far,
            cotangent,
            gain_ffn,
            h["gated"],
            h["square"],
            h["square_far"],
            params,
            mixer_out,
            attn_out,
        )
        if chunks == early:
            dots = jnp.concatenate([a["dot"], b["dot"]], axis=1)
            outer = (a["mixer_rows"], b["mixer_rows"], a["attended"], b["attended"])
            outer += (a["grad_branch"], b["grad_branch"])
            outer_sent = outer_weights(far_core, None, None, *outer)
            outer_far = swap(outer_sent, "core")
            first = ffn_weights(core, after(first_far, outer_sent), *sides)
            dots_far = swap(after(dots, first), "tensor")
            grad_attended = after(grad_attended, first)
        operands = (queries, pairs, grad_attended, h["lse"], seg_row, cosine, sine)
        if chunks == late:
            h["grad_queries"], grad_keys, grad_values = attention_backward(chunks, False, *operands)
            sides = (after(a["normed"], grad_keys), b["normed"], a["activated"], b["activated"])
            sides += (a["grad_gate_rows"], b["grad_gate_rows"], a["grad_up_rows"], b["grad_up_rows"], cotangent)
            first = ffn_weights(far_core, None, *sides)
            first_far = swap(first, "core")
        else:
            h["grad_queries"], grad_pairs = attention_backward(chunks, True, *operands, grad_keys, grad_values)
    first = outer_weights(core, after(outer_far, grad_pairs), first, *outer)
    first_sum = lax.psum_scatter(first, ("y", "x"), scatter_dimension=0, tiled=True)
    dots_far = after(dots_far, first)
    for chunks in (late, early):
        h = half[chunks]
        h["grad_gate"], h["gy"], h["dx"], h["p"], h["grad_in"], h["grad_out"], h["sums"] = scan_backward(
            chunks,
            heads,
            h["grad_rows"],
            h["gated"],
            h["square"],
            h["square_far"],
            h["dot"],
            dots_far[:, h["span"]],
            params,
            wide_in,
            h["y"],
            x,
            xb,
            state,
            lag,
            cum_row,
            seg_row,
            select,
        )
    pieces = [b["down"][:LEN], b["down"][LEN:], a["down"][:LEN], a["down"][LEN:]]
    pieces_far = [swap(after(piece, dots_far), "tensor") for piece in pieces[:3]]
    down = jnp.concatenate([a["down"], b["down"]], axis=0)
    ends = []
    for name in ("gy", "dx", "p", "grad_in", "grad_out"):
        ends += [a[name], b[name]]
    grad_conv, grad_state, grad_step, conv_sum, state_sum, step_sum = scan_end(
        heads,
        *ends,
        xb,
        slope,
        state_slope,
        wide_in,
        wide_in,
        step_row,
        sig_row,
        seg_row,
        select,
        params,
        params,
    )

    grads = (a["grad_gate"], b["grad_gate"], grad_conv, a["grad_queries"], b["grad_queries"])
    grads += (grad_state, grad_pairs, grad_step)
    tied = after(normed_input, pieces_far[0], pieces_far[1])
    second_far = swap(mixer_weights(far_core, None, None, tied, *grads), "core")
    partial_normed, input_gain_sum = normed_back(*grads, wide_proj, small_proj, layer_input)

    sums = a["sums"] + b["sums"]
    def row(*values):
        flat = jnp.concatenate([jnp.pad(v, (0, LEN - v.shape[0])) for v in values]) if len(values) > 1 else values[0]
        return jnp.pad(flat.reshape(1, -1), ((0, 0), (0, model_width - flat.size)))

    by_head = jnp.sum(sums[0].reshape(heads, HEAD_DIM), axis=1)
    table = jnp.concatenate(
        [
            input_gain_sum[:1],
            row(state_sum[:4].reshape(-1)),
            row(state_sum[4]),
            row(step_sum[:heads, 0], step_sum[HEAD_ROWS : HEAD_ROWS + heads, 0], by_head),
            jnp.pad(conv_sum[:5], ((0, 0), (0, model_width - width))),
            row(sums[1]),
            a["gain_sum"][:1] + b["gain_sum"][:1],
        ],
        axis=0,
    )
    shared_end = heads + 3
    table_end = heads + table.shape[0]
    table = (core_rows(table, place) + swap(core_rows(table, 1 - place), "core")).T
    table = jnp.pad(table, ((0, 0), (heads, LEN - table_end)))
    spots = [core]
    for name, link in [order[0] for order in ORDERS]:
        at = lax.axis_index(name).astype(jnp.int32)
        side = ((at + 1) // 2) % 2 if link == "A" else at // 2
        spots.append(jnp.stack([side, 3 - side, 1 - side, 2 + side] if link == "A" else [2 * side, 2 * side + 1, 2 - 2 * side, 3 - 2 * side]))
    second = mixer_weights(jnp.concatenate(spots), after(second_far, pieces_far[2]), table, normed_input, *grads)
    second = list(second)
    at_state = 2 * width + query_width
    normed_far = [swap(partial_normed[k * LEN : (k + 1) * LEN], "tensor") for k in range(rows // LEN)]
    second[1] = after(second[1], normed_far[0])
    parts = reduce_rows([(second[2 * k], second[2 * k + 1]) for k in range(4)], (0,))
    parts[0] = after(parts[0], normed_far[1])
    first_own = exchange(after(first_sum, parts[0]), "zh")
    first_all = lax.all_gather(first_own, ("core", "y", "x"), axis=0, tiled=True)
    parts = reduce_rows(parts, (1,))
    parts[0] = after(parts[0], normed_far[2])
    parts = reduce_rows(parts, (2,))
    parts[0] = after(parts[0], normed_far[3])
    parts = reduce_rows(parts, (3,))
    second = jnp.concatenate([p.reshape(32, -1) for p in parts], axis=1)
    both = second[:, at_state:]
    lane = np.arange(both.shape[1])
    in_table = lane - 2 * state_size - pair_width
    is_shared = (lane < 2 * state_size) | ((in_table >= heads) & (in_table < shared_end))
    diagonal = [(0, 3), (3, 0), (1, 2), (2, 1)]
    more = swap(both, "tensor") + lax.ppermute(both, ("zh", "tensor"), diagonal)
    second = exchange(second, "zh")
    summed = second[:, at_state:] + jnp.where(is_shared[None, :], more, 0.0)
    second = jnp.concatenate([second[:, :at_state], summed], axis=1)
    second = after(second, first_all)
    pieces_far.append(swap(after(pieces[3], second), "tensor"))
    second = lax.all_gather(second, ("core", "y", "x"), axis=0, tiled=True)
    grad_mixer_proj, grad_query_proj, grad_keyval, grad_state_proj, step_block = assemble(second, width, query_width)

    def whole(name):
        return jnp.concatenate([a[name], b[name]], axis=0)

    grad_hidden = whole("grad_hidden")
    grad_normed = partial_normed + jnp.concatenate(normed_far, axis=0)
    inv_rms_in = inverse_rms(tokens)
    unit_in = tokens * inv_rms_in
    input_grad = grad_hidden + norm_backward(grad_normed * input_gain, unit_in, inv_rms_in)
    down_far = jnp.concatenate([pieces_far[2], pieces_far[3], pieces_far[0], pieces_far[1]], axis=0)
    layer_output = (whole("hidden") + (down + down_far)).astype(jnp.bfloat16)

    smalls = unpack(heads, width, 2 * state_size, step_block)
    return (
        layer_output,
        input_grad,
        smalls[1],
        grad_mixer_proj,
        grad_state_proj,
        smalls[0].T,
        smalls[4],
        smalls[5],
        smalls[6],
        smalls[7],
        smalls[8],
        smalls[2],
        smalls[3],
        smalls[9],
        first_all[:width, 3 * model_width :],
        grad_query_proj,
        grad_keyval,
        first_all[width:, 3 * model_width :],
        smalls[10],
        first_all[:, :model_width],
        first_all[:, model_width : 2 * model_width],
        first_all[:, 2 * model_width : 3 * model_width],
    )


def solution(mesh):
    dp, whole_spec, columns = P(DP, None), P(), P(None, "tensor")
    per_channel, middle = P("tensor"), P(None, "tensor", None)
    last, by_rows = P(None, None, "tensor"), P("tensor", None)
    weights = (
        whole_spec,
        last,
        whole_spec,
        columns,
        per_channel,
        per_channel,
        per_channel,
        columns,
        per_channel,
        whole_spec,
        whole_spec,
        per_channel,
        by_rows,
        columns,
        middle,
        by_rows,
        whole_spec,
        columns,
        columns,
        by_rows,
    )
    mesh = jax.sharding.Mesh(mesh.devices.reshape(4, 2, 4, 2, 2), (*DP, "tensor"))
    return jax.shard_map(
        on_device, mesh=mesh, in_specs=(dp, dp, *weights, dp), out_specs=(dp, dp, *weights), check_vma=False
    )
```

```python
import functools

import jax
import jax.numpy as jnp
import numpy as np
from jax import lax
from jax.experimental import pallas as pl
from jax.experimental.pallas import tpu as pltpu
from jax.sharding import PartitionSpec as P

HEAD_DIM = 64
DSSM = 1536
DP = ("y", "zh", "x", "core")
PAIR = [(0, 1), (1, 0)]
LOG2E = 1.4426950408889634
hidden_bias = -1e30
norm_eps = 1e-05
rope_base = 10000.0
LEN = 128


def dot_nn(left, right):
    return lax.dot_general(
        left, right, (((1,), (0,)), ((), ())), preferred_element_type=jnp.float32
    )


def dot_nt(left, right):
    return lax.dot_general(
        left, right, (((1,), (1,)), ((), ())), preferred_element_type=jnp.float32
    )


def dot_tn(left, right):
    return lax.dot_general(
        left, right, (((0,), (0,)), ((), ())), preferred_element_type=jnp.float32
    )


def two_terms(v):
    high = v.astype(jnp.bfloat16)
    return high, (v - high.astype(jnp.float32)).astype(jnp.bfloat16)


def three_dots(dot, left, right):
    left_high, left_low = two_terms(left)
    right_high, right_low = two_terms(right)
    return dot(left_high, right_high) + dot(left_high, right_low) + dot(left_low, right_high)


def sigmoid(v):
    return 1.0 / (1.0 + jnp.exp(-v))


def block(index):
    return slice(index * LEN, (index + 1) * LEN)


def lane_iota(rows=LEN):
    return lax.broadcasted_iota(jnp.int32, (rows, LEN), 1)


def turned(row):
    return jnp.broadcast_to(row, (LEN, LEN)).T


def mask_ts(seg_row, i, j):
    same = turned(seg_row[:, block(i)].astype(jnp.float32)) == seg_row[:, block(j)].astype(jnp.float32)
    if i != j:
        return same
    down = lax.broadcasted_iota(jnp.int32, (LEN, LEN), 0)
    return same & (down >= lane_iota())


def mask_st(seg_row, j, i):
    same = turned(seg_row[:, block(j)].astype(jnp.float32)) == seg_row[:, block(i)].astype(jnp.float32)
    if i != j:
        return same
    down = lax.broadcasted_iota(jnp.int32, (LEN, LEN), 0)
    return same & (down <= lane_iota())


def conv_rows(pad_ref, keep_ref, kernel, bias, start, lanes):
    summed = bias + kernel[3:4] * pad_ref[8 + start : 8 + start + LEN, lanes]
    for lag in (1, 2, 3):
        moved = pad_ref[8 + start - lag : 8 + start - lag + LEN, lanes]
        summed = summed + kernel[3 - lag : 4 - lag] * (moved * keep_ref[lag - 1, start : start + LEN, :])
    return summed


def widen(seg_row_ref, wide_ref, pad_ref):
    rows = seg_row_ref.shape[1]
    pad_ref[0:8, :] = jnp.full((8, LEN), -1.0, jnp.float32)
    for i in range(rows // LEN):
        pad_ref[8 + i * LEN : 8 + (i + 1) * LEN, :] = turned(seg_row_ref[:, block(i)].astype(jnp.float32))
    for lag in (1, 2, 3):
        same = pad_ref[8 : rows + 8, :] == pad_ref[8 - lag : rows + 8 - lag, :]
        wide_ref[lag - 1, 0:rows, :] = jnp.where(same, 1.0, 0.0)
        wide_ref[lag - 1, rows : rows + 8, :] = jnp.zeros((8, LEN), jnp.float32)


def prep_kernel(
    conv_ref,
    small_ref,
    cos_ref,
    sin_ref,
    seg_row_ref,
    table_ref,
    params_ref,
    x_ref,
    xb_ref,
    slope_ref,
    state_ref,
    state_slope_ref,
    cum_ref,
    lag_ref,
    cum_row_ref,
    lag_row_ref,
    step_row_ref,
    sig_row_ref,
    q_ref,
    kv_ref,
    pad_ref,
    wide_ref,
):
    rows = conv_ref.shape[0]
    blocks = rows // LEN

    @pl.when(pl.program_id(0) == 0)
    def _():
        widen(seg_row_ref, wide_ref, pad_ref)
        pad_ref[0:8, :] = jnp.zeros((8, LEN), jnp.float32)
        for c in range(2):
            pad_ref[8 : rows + 8, :] = small_ref[:, block(c)]
            for i in range(blocks):
                pre = conv_rows(
                    pad_ref, wide_ref, params_ref[8:12, block(c)], params_ref[12:13, block(c)], i * LEN, slice(0, LEN)
                )
                sig = sigmoid(pre)
                state_ref[block(i), block(c)] = pre * sig
                state_slope_ref[block(i), block(c)] = sig * (1.0 + pre * (1.0 - sig))

    @pl.when(pl.program_id(0) == 1)
    def _():
        down = lax.broadcasted_iota(jnp.int32, (LEN, LEN), 0)
        lower = jnp.where(down >= lane_iota(), 1.0, 0.0).astype(jnp.bfloat16)
        left_half = lane_iota() < HEAD_DIM
        carry = jnp.zeros((1, LEN), jnp.float32)
        heads = cum_row_ref.shape[0]
        for i in range(blocks):
            argument = small_ref[block(i), block(5)] + params_ref[13:14, :LEN]
            tail = jnp.exp(-jnp.abs(argument))
            grown = jnp.where(tail < 1e-3, tail - 0.5 * tail * tail, jnp.log(1.0 + tail))
            step = jnp.maximum(argument, 0.0) + grown
            scaled = step * params_ref[14:15, :LEN] * LOG2E
            first, rest = two_terms(scaled)
            last = scaled - first.astype(jnp.float32) - rest.astype(jnp.float32)
            cum = dot_nn(lower, first) + dot_nn(lower, rest) + dot_nn(lower, last.astype(jnp.bfloat16)) + carry
            carry = cum[LEN - 1 : LEN, :]
            lag = cum - jnp.log(step) * LOG2E
            cum_ref[block(i), :] = cum
            lag_ref[block(i), :] = lag
            cum_t, lag_t = cum.T, lag.T
            step_row_ref[:, block(i)] = step.T[:heads]
            sig_row_ref[:, block(i)] = sigmoid(argument).T[:heads]
            for h in range(heads):
                cum_row_ref[h, :, block(i)] = cum_t[h : h + 1]
                lag_row_ref[h, :, block(i)] = lag_t[h : h + 1]
            cosine, sine = cos_ref[block(i), :], sin_ref[block(i), :]
            kv = small_ref[block(i), block(4)]
            kv_ref[block(i), :] = jnp.where(left_half, rotate_tile(kv, cosine, sine), kv).astype(jnp.bfloat16)
            for p in range(q_ref.shape[1] // LEN):
                q_ref[block(i), block(p)] = rotate_tile(small_ref[block(i), block(2 + p)], cosine, sine).astype(
                    jnp.bfloat16
                )

    for sub in range(GROUP):
        lanes = block(sub)
        pad_ref[8 : rows + 8, :] = conv_ref[:, lanes]
        for i in range(blocks):
            pre = conv_rows(pad_ref, wide_ref, table_ref[0:4, lanes], table_ref[4:5, lanes], i * LEN, slice(0, LEN))
            sig = sigmoid(pre)
            x = pre * sig
            x_ref[block(i), lanes] = x
            xb_ref[block(i), lanes] = x.astype(jnp.bfloat16)
            slope_ref[block(i), lanes] = sig * (1.0 + pre * (1.0 - sig))


def rotate_tile(v, cosine, sine):
    first = lax.rem(lane_iota(v.shape[0]), HEAD_DIM) < HEAD_DIM // 2
    swapped = jnp.where(first, pltpu.roll(v, LEN - HEAD_DIM // 2, 1), pltpu.roll(v, HEAD_DIM // 2, 1))
    return v * cosine + swapped * sine


def scan_kernel(
    chunks,
    heads,
    gate_ref,
    x_ref,
    xb_ref,
    state_ref,
    cum_ref,
    lag_row_ref,
    seg_row_ref,
    table_ref,
    y_ref,
    gated_ref,
    row_ref,
    wide_ref,
    cross_ref,
    bias_ref,
    mix_ref,
    square_ref,
):
    step = pl.program_id(0)
    first = chunks[0]
    pairs = [(i, j) for i in chunks for j in range(max(0, i - 2), i + 1)]
    left_half = lane_iota() < HEAD_DIM

    @pl.when(step == 0)
    def _():
        for h in range(heads):
            for i in chunks:
                wide_ref[h, block(i - first), :] = jnp.broadcast_to(cum_ref[block(i), h : h + 1], (LEN, LEN))
        for i in chunks:
            low = max(0, i - 2)
            cross = three_dots(dot_nt, state_ref[block(i), LEN:], state_ref[low * LEN : (i + 1) * LEN, :LEN])
            for n, (i2, j) in enumerate(pairs):
                if i2 == i:
                    cross_ref[n] = cross[:, block(j - low)]
                    allowed = mask_ts(seg_row_ref, i, j)
                    bias_ref[n] = jnp.where(allowed, 0.0, hidden_bias)
        square_ref[...] = jnp.zeros(square_ref.shape, jnp.float32)

    tiles = (gate_ref, x_ref, xb_ref, table_ref.at[5:6], y_ref, gated_ref)

    def head_pair(hp, gate_ref, x_ref, xb_ref, skip_ref, y_ref, gated_ref):
        for i in chunks:
            at = block(i - first)
            low = max(0, i - 2)
            for n, (i2, j) in enumerate(pairs):
                if i2 != i:
                    continue
                for e in range(2):
                    spread = wide_ref[2 * hp + e, at, :] - lag_row_ref[2 * hp + e, :, block(j)]
                    decay = jnp.exp2(spread + bias_ref[n])
                    mix_ref[i - first, block(e), block(j - low)] = (decay * cross_ref[n]).astype(jnp.bfloat16)
            both = dot_nn(mix_ref[i - first, :, : (i + 1 - low) * LEN], xb_ref[low * LEN : (i + 1) * LEN, :])
            y = jnp.where(left_half, both[:LEN], both[LEN:])
            y_ref[at, :] = y
            gate = gate_ref[at, :]
            gated = (y + skip_ref[...] * x_ref[at, :]) * (gate * sigmoid(gate))
            gated_ref[at, :] = gated
            square_ref[at, :] = square_ref[at, :] + gated * gated

    for sub in range(GROUP):
        head_pair(GROUP * step + sub, *[t.at[:, block(sub)] for t in tiles])

    @pl.when(step == pl.num_programs(0) - 1)
    def _():
        for i in chunks:
            at = block(i - first)
            total = jnp.sum(square_ref[at, :], axis=1, keepdims=True)
            row_ref[0:1, at] = jnp.broadcast_to(total, (LEN, LEN)).T[0:1]


def attention_kernel(chunks, q_ref, kv_ref, seg_row_ref, out_ref, lse_ref):
    scale = HEAD_DIM ** (-0.5) * LOG2E
    first = chunks[0]
    left_half = lane_iota() < HEAD_DIM
    zero = jnp.zeros((LEN, LEN), jnp.bfloat16)
    lse_ref[...] = jnp.zeros(lse_ref.shape, jnp.float32)
    for i in chunks:
        at = block(i - first)
        low = max(0, i - 2) * LEN
        span = (i + 1) * LEN - low
        allowed = jnp.concatenate([mask_ts(seg_row_ref, i, j) for j in range(low // LEN, i + 1)], axis=1)
        keys = kv_ref[low : low + span, :]
        swapped = pltpu.roll(keys.astype(jnp.float32), HEAD_DIM, 1).astype(jnp.bfloat16)
        for p in range(q_ref.shape[1] // LEN):
            queries = q_ref[block(i), block(p)]
            result = []
            for e in range(2):
                masked = jnp.where(left_half == (e == 0), queries, zero)
                scores = dot_nt(masked, keys if e == 0 else swapped) * scale
                scores = jnp.where(allowed, scores, hidden_bias)
                top = jnp.max(scores, axis=1, keepdims=True)
                weights = jnp.exp2(scores - top)
                total = jnp.sum(weights, axis=1, keepdims=True)
                probs = (weights * (1.0 / total)).astype(jnp.bfloat16)
                result.append(dot_nn(probs, swapped if e == 0 else keys))
                lse = jnp.broadcast_to(top + jnp.log(total) * LOG2E, (LEN, LEN))
                lse_ref[2 * p + e : 2 * p + e + 1, at] = lse.T[0:1]
            out_ref[at, block(p)] = jnp.where(left_half, result[0], result[1]).astype(jnp.bfloat16)


def attention_back_kernel(chunks, final, *refs):
    q_ref, kv_ref, do_ref, lse_ref, seg_row_ref, cos_ref, sin_ref = refs[:7]
    if final:
        dk_in_ref, dv_in_ref, dq_ref, dkv_ref, dk_ref, dv_ref, turned_ref, key_t_ref = refs[7:]
    else:
        dq_ref, dk_ref, dv_ref, turned_ref, key_t_ref = refs[7:]
    scale = HEAD_DIM ** (-0.5)
    blocks = q_ref.shape[0] // LEN
    first = chunks[0]
    left_half = lane_iota() < HEAD_DIM
    zero = jnp.zeros((LEN, LEN), jnp.bfloat16)
    for i in range(chunks[-1] + 1):
        kv = kv_ref[block(i), :].astype(jnp.float32)
        turned_ref[block(i), :] = pltpu.roll(kv, HEAD_DIM, 1).astype(jnp.bfloat16)
        key_t_ref[:, block(i)] = kv.T[:HEAD_DIM].astype(jnp.bfloat16)
    if final:
        dk_ref[...] = dk_in_ref[...]
        dv_ref[...] = dv_in_ref[...]
    else:
        dk_ref[...] = jnp.zeros(dk_ref.shape, jnp.float32)
        dv_ref[...] = jnp.zeros(dv_ref.shape, jnp.float32)
    for i in chunks:
        at = block(i - first)
        low = max(0, i - 2) * LEN
        span = (i + 1) * LEN - low
        window = slice(low, low + span)
        allowed = jnp.concatenate([mask_st(seg_row_ref, j, i) for j in range(low // LEN, i + 1)], axis=0)
        keys, swapped = kv_ref[window, :], turned_ref[window, :]
        for p in range(q_ref.shape[1] // LEN):
            queries, douts = q_ref[block(i), block(p)], do_ref[at, block(p)]
            back = []
            for e in range(2):
                side = left_half == (e == 0)
                q_half = jnp.where(side, queries, zero)
                do_half = jnp.where(side, douts, zero)
                h = 2 * p + e
                scores = dot_nt(keys if e == 0 else swapped, q_half) * (scale * LOG2E)
                probs = jnp.exp2(jnp.where(allowed, scores, hidden_bias) - lse_ref[h : h + 1, at])
                dprobs = dot_nt(swapped if e == 0 else keys, do_half)
                inner = jnp.sum(probs * dprobs, axis=0, keepdims=True)
                dscores = (probs * (dprobs - inner)).astype(jnp.bfloat16)
                dv_ref[window, :] = dv_ref[window, :] + dot_nn(probs.astype(jnp.bfloat16), do_half)
                dk_ref[window, :] = dk_ref[window, :] + dot_nn(dscores, q_half)
                back.append(dot_nn(key_t_ref[:, window], dscores))
            dq = jnp.concatenate(back, axis=0).T * scale
            dq_ref[at, block(p)] = rotate_tile(dq, cos_ref[block(i), :], -sin_ref[block(i), :]).astype(jnp.bfloat16)
    if not final:
        return
    for i in range(blocks):
        dk = dk_ref[block(i), :]
        dk = (dk + pltpu.roll(dk, HEAD_DIM, 1)) * scale
        dk = rotate_tile(dk, cos_ref[block(i), :], -sin_ref[block(i), :])
        dv = dv_ref[block(i), :]
        dv = dv + pltpu.roll(dv, HEAD_DIM, 1)
        dkv_ref[block(i), :] = jnp.where(left_half, dk, dv).astype(jnp.bfloat16)


def scan_back_kernel(
    chunks,
    heads,
    gmr_ref,
    gated_ref,
    square_a_ref,
    square_b_ref,
    dot_a_ref,
    dot_b_ref,
    table_ref,
    gate_ref,
    y_ref,
    x_ref,
    xb_ref,
    state_ref,
    lag_ref,
    cum_row_ref,
    seg_row_ref,
    select_ref,
    dgate_ref,
    gy_ref,
    dx_ref,
    p_ref,
    grad_in_ref,
    grad_out_ref,
    sums_ref,
    gyb_ref,
    wide_ref,
    cross_ref,
    bias_ref,
    dcross_ref,
    inv_wide_ref,
    dot_wide_ref,
    inner_ref,
    mix_ref,
):
    step = pl.program_id(0)
    first = chunks[0]
    sources = chunks[-1] + 1
    left_half = lane_iota() < HEAD_DIM
    zero = jnp.zeros((LEN, LEN), jnp.bfloat16)
    spans = [(j, max(j, first), min(j + 3, sources)) for j in range(sources)]
    pairs = [(j, i) for j, start, stop in spans for i in range(start, stop)]

    @pl.when(step == 0)
    def _():
        for i in chunks:
            at = block(i - first)
            square = (square_a_ref[:, at] + square_b_ref[:, at]) / DSSM
            inv = lax.rsqrt(square + norm_eps)
            inv_wide_ref[at, :] = jnp.broadcast_to(inv, (LEN, LEN)).T
            dot = (dot_a_ref[:, at] + dot_b_ref[:, at]) / DSSM
            dot_wide_ref[at, :] = jnp.broadcast_to(dot, (LEN, LEN)).T
        p_ref[...] = jnp.zeros(p_ref.shape, jnp.float32)
        for h in range(heads):
            wide_ref[h] = jnp.broadcast_to(lag_ref[: sources * LEN, h : h + 1], (sources * LEN, LEN))
        for j, start, stop in spans:
            cross = three_dots(dot_nt, state_ref[block(j), :LEN], state_ref[start * LEN : stop * LEN, LEN:])
            for n, (j2, i) in enumerate(pairs):
                if j2 == j:
                    cross_ref[n] = cross[:, block(i - start)]
                    allowed = mask_st(seg_row_ref, j, i)
                    bias_ref[n] = jnp.where(allowed, 0.0, hidden_bias)
                    dcross_ref[n] = jnp.zeros((LEN, LEN), jnp.float32)

    tiles = (
        gmr_ref,
        gated_ref,
        table_ref.at[6:7],
        gate_ref,
        y_ref,
        x_ref,
        xb_ref,
        table_ref.at[5:6],
        dgate_ref,
        gy_ref,
        dx_ref,
        sums_ref,
    )

    def head_pair(
        hp,
        select,
        gmr_ref,
        gated_ref,
        gain_ref,
        gate_ref,
        y_ref,
        x_ref,
        xb_ref,
        skip_ref,
        dgate_ref,
        gy_ref,
        dx_ref,
        sums_ref,
    ):
        skip = skip_ref[...]
        gain = gain_ref[...]
        skip_sum = jnp.zeros((1, LEN), jnp.float32)
        gain_sum = jnp.zeros((1, LEN), jnp.float32)
        for i in chunks:
            at = block(i - first)
            inv = inv_wide_ref[at, :]
            unit = gated_ref[at, :] * inv
            rows_grad = gmr_ref[at, :]
            grad = inv * (rows_grad * gain - unit * dot_wide_ref[at, :])
            gate = gate_ref[at, :]
            sig = sigmoid(gate)
            y = y_ref[at, :]
            x = x_ref[at, :]
            gy = grad * (gate * sig)
            dgate_ref[at, :] = (grad * (y + skip * x) * (sig * (1.0 + gate * (1.0 - sig)))).astype(jnp.bfloat16)
            gyb = gy.astype(jnp.bfloat16)
            gy_ref[at, :] = gy
            gyb_ref[at, :] = gyb
            high, rest = two_terms(gyb.astype(jnp.float32) * y)
            p_ref[:, at] = p_ref[:, at] + dot_nt(select, high) + dot_nt(select, rest)
            skip_sum = skip_sum + jnp.sum(gy * x, axis=0, keepdims=True)
            gain_sum = gain_sum + jnp.sum(rows_grad * unit, axis=0, keepdims=True)
        sums_ref[0:1, :] = skip_sum
        sums_ref[1:2, :] = gain_sum

        for j, start, stop in spans:
            x_pair = xb_ref[block(j), :]
            x_both = jnp.concatenate([jnp.where(left_half, x_pair, zero), jnp.where(left_half, zero, x_pair)], axis=0)
            wide = (stop - start) * LEN
            gy_rows = gyb_ref[(start - first) * LEN : (stop - first) * LEN, :]
            inner_ref[:, :wide] = dot_nt(x_both, gy_rows)
            for n, (j2, i) in enumerate(pairs):
                if j2 != j:
                    continue
                grown = dcross_ref[n]
                for e in range(2):
                    spread = cum_row_ref[2 * hp + e, :, block(i)] - wide_ref[2 * hp + e, block(j), :]
                    decay = jnp.exp2(spread + bias_ref[n])
                    grown = grown + inner_ref[block(e), block(i - start)] * decay
                    mix_ref[block(e), block(i - start)] = (decay * cross_ref[n]).astype(jnp.bfloat16)
                dcross_ref[n] = grown
            both = dot_nn(mix_ref[:, :wide], gy_rows)
            dx_ref[block(j), :] = jnp.where(left_half, both[:LEN], both[LEN:])

    for sub in range(GROUP):
        head_pair(GROUP * step + sub, select_ref[:, block(sub)], *[t.at[:, block(sub)] for t in tiles])

    @pl.when(step == pl.num_programs(0) - 1)
    def _():
        grad_out = {i: jnp.zeros((LEN, LEN), jnp.float32) for i in chunks}
        for j in range(sources):
            grad_in = jnp.zeros((LEN, LEN), jnp.float32)
            for n, (j2, i) in enumerate(pairs):
                if j2 != j:
                    continue
                high, rest = two_terms(dcross_ref[n])
                out_high, out_rest = two_terms(state_ref[block(i), LEN:])
                in_high, in_rest = two_terms(state_ref[block(j), :LEN])
                grad_in = grad_in + dot_nn(high, out_high) + dot_nn(high, out_rest) + dot_nn(rest, out_high)
                grad_out[i] = grad_out[i] + dot_tn(high, in_high) + dot_tn(high, in_rest) + dot_tn(rest, in_high)
            grad_in_ref[block(j), :] = grad_in
        for i in chunks:
            grad_out_ref[block(i - first), :] = grad_out[i]


def conv_back(grad_ref, value_ref, keep_ref, taps, out_ref, sum_ref, lanes, blocks):
    totals = [jnp.zeros((1, LEN), jnp.float32) for _ in range(5)]
    for i in range(blocks):
        here = grad_ref[i * LEN : (i + 1) * LEN, :]
        grad = taps[3:4] * here
        totals[4] = totals[4] + jnp.sum(here, axis=0, keepdims=True)
        totals[3] = totals[3] + jnp.sum(here * value_ref[8 + i * LEN : 8 + (i + 1) * LEN, :], axis=0, keepdims=True)
        for lag in (1, 2, 3):
            ahead = grad_ref[i * LEN + lag : (i + 1) * LEN + lag, :]
            grad = grad + taps[3 - lag : 4 - lag] * (ahead * keep_ref[lag - 1, i * LEN + lag : (i + 1) * LEN + lag, :])
            moved = value_ref[8 + i * LEN - lag : 8 + (i + 1) * LEN - lag, :]
            masked = here * keep_ref[lag - 1, i * LEN : (i + 1) * LEN, :]
            totals[3 - lag] = totals[3 - lag] + jnp.sum(masked * moved, axis=0, keepdims=True)
        out_ref[block(i), lanes] = grad.astype(jnp.bfloat16)
    for tap in range(5):
        sum_ref[tap : tap + 1, lanes] = totals[tap]


def scan_end_kernel(
    heads,
    gy_a_ref,
    gy_b_ref,
    dx_a_ref,
    dx_b_ref,
    p_a_ref,
    p_b_ref,
    in_a_ref,
    in_b_ref,
    out_a_ref,
    out_b_ref,
    xb_ref,
    slope_ref,
    state_slope_ref,
    conv_ref,
    small_ref,
    step_row_ref,
    sig_row_ref,
    seg_row_ref,
    select_ref,
    table_ref,
    params_ref,
    dconv_ref,
    dstate_ref,
    dstep_ref,
    conv_sum_ref,
    state_sum_ref,
    step_sum_ref,
    grad_pad_ref,
    value_pad_ref,
    wide_ref,
    q_ref,
    flow_ref,
):
    step = pl.program_id(0)
    rows = conv_ref.shape[0]
    blocks = rows // LEN
    half = rows // 2
    count = flow_ref.shape[0]

    @pl.when(step == 0)
    def _():
        value_pad_ref[0:8, :] = jnp.zeros((8, LEN), jnp.float32)
        grad_pad_ref[rows : rows + 8, :] = jnp.zeros((8, LEN), jnp.float32)
        widen(seg_row_ref, wide_ref, value_pad_ref)
        value_pad_ref[0:8, :] = jnp.zeros((8, LEN), jnp.float32)
        q_ref[...] = jnp.zeros(q_ref.shape, jnp.float32)
        for c in range(2):
            if c == 0:
                grad_pad_ref[0:half, :] = (in_a_ref[...] + in_b_ref[0:half, :]) * state_slope_ref[0:half, block(c)]
                grad_pad_ref[half:rows, :] = in_b_ref[half:rows, :] * state_slope_ref[half:rows, block(c)]
            else:
                grad_pad_ref[0:half, :] = out_a_ref[...] * state_slope_ref[0:half, block(c)]
                grad_pad_ref[half:rows, :] = out_b_ref[...] * state_slope_ref[half:rows, block(c)]
            value_pad_ref[8 : rows + 8, :] = small_ref[:, block(c)]
            conv_back(
                grad_pad_ref,
                value_pad_ref,
                wide_ref,
                params_ref[8:12, block(c)],
                dstate_ref,
                state_sum_ref,
                block(c),
                blocks,
            )

    tiles = (
        gy_a_ref,
        gy_b_ref,
        dx_a_ref,
        dx_b_ref,
        xb_ref,
        slope_ref,
        conv_ref,
        table_ref.at[5:6],
        dconv_ref,
        conv_sum_ref,
    )

    def head_pair(
        select,
        taps,
        gy_a_ref,
        gy_b_ref,
        dx_a_ref,
        dx_b_ref,
        xb_ref,
        slope_ref,
        conv_ref,
        skip_ref,
        dconv_ref,
        conv_sum_ref,
    ):
        for j in range(blocks):
            dx = dx_b_ref[block(j), :]
            if j < blocks // 2:
                dx = dx + dx_a_ref[block(j), :]
                gy = gy_a_ref[block(j), :]
            else:
                gy = gy_b_ref[block(j - blocks // 2), :]
            high, rest = two_terms(dx * xb_ref[block(j), :].astype(jnp.float32))
            q_ref[:, block(j)] = q_ref[:, block(j)] + dot_nt(select, high) + dot_nt(select, rest)
            grad_pad_ref[block(j), :] = (dx + gy * skip_ref[...]) * slope_ref[block(j), :]
        value_pad_ref[8 : rows + 8, :] = conv_ref[...]
        conv_back(
            grad_pad_ref, value_pad_ref, wide_ref, taps, dconv_ref, conv_sum_ref, slice(0, LEN), blocks
        )

    for sub in range(GROUP):
        head_pair(select_ref[:, block(sub)], table_ref[0:4, block(sub)], *[t.at[:, block(sub)] for t in tiles])

    @pl.when(step == pl.num_programs(0) - 1)
    def _():
        q = q_ref[...]
        flow_ref[:, 0:half] = p_a_ref[...] - q[:, 0:half]
        flow_ref[:, half:rows] = p_b_ref[...] - q[:, half:rows]
        rate = turned(params_ref[14:15, :LEN])[:count]
        bias_total = jnp.zeros((count, LEN), jnp.float32)
        decay_total = jnp.zeros((count, LEN), jnp.float32)
        for j in range(blocks):
            log_grad = jnp.zeros((count, LEN), jnp.float32)
            for i in range(j, min(j + 3, blocks)):
                chosen = jnp.where(mask_st(seg_row_ref, j, i), 1.0, 0.0).astype(jnp.bfloat16)
                high, rest = two_terms(flow_ref[:, block(i)])
                log_grad = log_grad + dot_nt(high, chosen) + dot_nt(rest, chosen)
            step = step_row_ref[:, block(j)]
            grad_step = jnp.where(step > 1e-30, q[:, block(j)] / step, 0.0) + log_grad * rate
            grad_arg = grad_step * sig_row_ref[:, block(j)]
            bias_total = bias_total + grad_arg
            decay_total = decay_total + log_grad * step
            tall = jnp.concatenate([grad_arg, jnp.zeros((LEN - count, LEN), jnp.float32)], axis=0)
            dstep_ref[block(j), :] = tall.T.astype(jnp.bfloat16)
        step_sum_ref[0:count, :] = jnp.broadcast_to(jnp.sum(bias_total, axis=1, keepdims=True), (count, LEN))
        step_sum_ref[count : 2 * count, :] = jnp.broadcast_to(
            jnp.sum(decay_total * rate, axis=1, keepdims=True), (count, LEN)
        )


def whole_block(shape):
    return pl.BlockSpec(shape, lambda step: (0,) * len(shape), pipeline_mode=pl.Buffered(1))


def tile(rows, row_block=0, first=0):
    return pl.BlockSpec((rows, GROUP * LEN), lambda step: (row_block, first + step))


def small_block(rows, width):
    return pl.BlockSpec((rows, width), lambda step: (0, 2), pipeline_mode=pl.Buffered(1))


def call(kernel, steps, out_shape, out_specs, scratch, operands, specs, flops):
    return pl.pallas_call(
        kernel,
        grid=(steps,),
        out_shape=out_shape,
        in_specs=[s or whole_block(o.shape) for o, s in zip(operands, specs)],
        out_specs=[s or whole_block(o.shape) for o, s in zip(out_shape, out_specs)],
        scratch_shapes=scratch,
        compiler_params=pltpu.CompilerParams(vmem_limit_bytes=VMEM_BYTES),
        cost_estimate=pl.CostEstimate(flops=flops, bytes_accessed=0, transcendentals=0),
    )(*operands)


def f32(*shape):
    return jax.ShapeDtypeStruct(shape, jnp.float32)


def b16(*shape):
    return jax.ShapeDtypeStruct(shape, jnp.bfloat16)


HEAD_ROWS = 16
GROUP = 3
VMEM_BYTES = 60 * 1024 * 1024


def scan_prep(width, wide_in, cosine, sine, seg_row, params):
    rows = wide_in.shape[0]
    steps = width // LEN // GROUP
    outs = [
        f32(rows, width),
        b16(rows, width),
        f32(rows, width),
        f32(rows, 2 * LEN),
        f32(rows, 2 * LEN),
        f32(rows, LEN),
        f32(rows, LEN),
        f32(HEAD_ROWS, 1, rows),
        f32(HEAD_ROWS, 1, rows),
        f32(HEAD_ROWS, rows),
        f32(HEAD_ROWS, rows),
        b16(rows, 2 * LEN),
        b16(rows, LEN),
    ]
    scratch = [pltpu.VMEM((rows + 8, LEN), jnp.float32), pltpu.VMEM((3, rows + 8, LEN), jnp.float32)]
    operands = (wide_in, wide_in, cosine, sine, seg_row, params, params)
    specs = [tile(rows, 0, steps), small_block(rows, width), None, None, None, tile(16), None]
    return call(prep_kernel, steps, outs, [tile(rows)] * 3 + [None] * 10, scratch, operands, specs, 0 * 10**9)


def scan_forward(chunks, heads, wide_in, x, xb, *rest):
    width = x.shape[1]
    rows = LEN * len(chunks)
    at = chunks[0] // len(chunks)
    count = sum(min(i, 2) + 1 for i in chunks)
    outs = [f32(rows, width), f32(rows, width), f32(1, rows)]
    scratch = [
        pltpu.VMEM((heads, rows, LEN), jnp.float32),
        pltpu.VMEM((count, LEN, LEN), jnp.float32),
        pltpu.VMEM((count, LEN, LEN), jnp.float32),
        pltpu.VMEM((len(chunks), 2 * LEN, 3 * LEN), jnp.bfloat16),
        pltpu.VMEM((rows, LEN), jnp.float32),
    ]
    specs = [tile(rows, at), tile(rows, at), tile((chunks[-1] + 1) * LEN)] + [None] * (len(rest) - 1) + [tile(16)]
    kernel = functools.partial(scan_kernel, chunks, heads)
    operands = (wide_in, x, xb, *rest)
    return call(kernel, heads // 2 // GROUP, outs, [tile(rows), tile(rows), None], scratch, operands, specs, 0 * 10**9)


def attention_forward(chunks, q, kv, seg_row):
    rows = LEN * len(chunks)
    outs = [b16(rows, q.shape[1]), f32(8, rows)]
    kernel = functools.partial(attention_kernel, chunks)
    return call(kernel, 1, outs, [None] * 2, [], (q, kv, seg_row), [None] * 3, 0 * 10**9)


def attention_backward(chunks, final, *operands):
    q = operands[0]
    rows = q.shape[0]
    partial = [f32(rows, LEN), f32(rows, LEN)]
    sums = [pltpu.VMEM((rows, LEN), jnp.float32)] * 2
    outs = [b16(LEN * len(chunks), q.shape[1])] + ([b16(rows, LEN)] if final else partial)
    scratch = (sums if final else []) + [
        pltpu.VMEM((rows, LEN), jnp.bfloat16),
        pltpu.VMEM((HEAD_DIM, rows), jnp.bfloat16),
    ]
    kernel = functools.partial(attention_back_kernel, chunks, final)
    return call(kernel, 1, outs, [None] * len(outs), scratch, operands, [None] * len(operands), (0 if chunks[0] else 30) * 10**9)


def scan_backward(chunks, heads, *operands):
    rows, width = operands[0].shape
    at = chunks[0] // len(chunks)
    sources = (chunks[-1] + 1) * LEN
    count = sum(min(i, 2) + 1 for i in chunks)
    outs = [
        b16(rows, width),
        f32(rows, width),
        f32(sources, width),
        f32(HEAD_ROWS, rows),
        f32(sources, LEN),
        f32(rows, LEN),
        f32(8, width),
    ]
    scratch = [
        pltpu.VMEM((rows, LEN), jnp.bfloat16),
        pltpu.VMEM((heads, sources, LEN), jnp.float32),
        pltpu.VMEM((count, LEN, LEN), jnp.float32),
        pltpu.VMEM((count, LEN, LEN), jnp.float32),
        pltpu.VMEM((count, LEN, LEN), jnp.float32),
        pltpu.VMEM((rows, LEN), jnp.float32),
        pltpu.VMEM((rows, LEN), jnp.float32),
        pltpu.VMEM((2 * LEN, 3 * LEN), jnp.float32),
        pltpu.VMEM((2 * LEN, 3 * LEN), jnp.bfloat16),
    ]
    specs = [tile(rows), tile(rows), None, None, None, None, tile(16), tile(rows, at), tile(rows), tile(rows, at), tile(sources)]
    specs += [None, None, None, None, tile(HEAD_ROWS)]
    out_specs = [tile(rows), tile(rows), tile(sources), None, None, None, tile(8)]
    kernel = functools.partial(scan_back_kernel, chunks, heads)
    return call(kernel, heads // 2 // GROUP, outs, out_specs, scratch, operands, specs, 30 * 10**9)


def scan_end(heads, *operands):
    rows, width = 2 * operands[0].shape[0], operands[0].shape[1]
    steps = heads // 2 // GROUP
    outs = [
        b16(rows, width),
        b16(rows, 2 * LEN),
        b16(rows, LEN),
        f32(8, width),
        f32(8, 2 * LEN),
        f32(2 * HEAD_ROWS, LEN),
    ]
    scratch = [
        pltpu.VMEM((rows + 8, LEN), jnp.float32),
        pltpu.VMEM((rows + 8, LEN), jnp.float32),
        pltpu.VMEM((3, rows + 8, LEN), jnp.float32),
        pltpu.VMEM((HEAD_ROWS, rows), jnp.float32),
        pltpu.VMEM((HEAD_ROWS, rows), jnp.float32),
    ]
    half = rows // 2
    specs = [tile(half), tile(half), tile(half), tile(rows)] + [None] * 6 + [tile(rows), tile(rows), None]
    specs += [tile(rows, 0, steps), small_block(rows, width), None, None, None, tile(HEAD_ROWS), tile(16), None]
    out_specs = [tile(rows), None, None, tile(8), None, None]
    kernel = functools.partial(scan_end_kernel, heads)
    return call(kernel, steps, outs, out_specs, scratch, operands, specs, 30 * 10**9)


def inverse_rms(rows):
    return lax.rsqrt(jnp.mean(rows * rows, axis=-1, keepdims=True) + norm_eps)


def ffn_kernel(
    tokens_ref,
    part_ref,
    far_ref,
    gain_ref,
    gate_ref,
    up_ref,
    down_ref,
    cotangent_ref,
    hidden_ref,
    normed_ref,
    activated_ref,
    grad_gate_ref,
    grad_up_ref,
    back_ref,
    out_ref,
):
    @pl.when(pl.program_id(0) == 0)
    def _():
        hidden = tokens_ref[...].astype(jnp.float32) + (part_ref[...] + far_ref[...])
        hidden_ref[...] = hidden
        normed_ref[...] = (hidden * inverse_rms(hidden) * gain_ref[...]).astype(jnp.bfloat16)
        back_ref[...] = jnp.zeros(back_ref.shape, jnp.float32)
        out_ref[...] = jnp.zeros(out_ref.shape, jnp.float32)

    normed = normed_ref[...]
    gate = dot_nn(normed, gate_ref[...])
    up = dot_nn(normed, up_ref[...])
    sig = sigmoid(gate)
    act = gate * sig
    activated = (act * up).astype(jnp.bfloat16)
    activated_ref[...] = activated
    grad = dot_nt(cotangent_ref[...], down_ref[...])
    grad_gate = (grad * up * (sig * (1.0 + gate * (1.0 - sig)))).astype(jnp.bfloat16)
    grad_up = (grad * act).astype(jnp.bfloat16)
    grad_gate_ref[...] = grad_gate
    grad_up_ref[...] = grad_up
    back_ref[...] = back_ref[...] + (dot_nt(grad_gate, gate_ref[...]) + dot_nt(grad_up, up_ref[...]))
    out_ref[...] = out_ref[...] + dot_nn(activated, down_ref[...])


def ffn(chunks, tokens, part, far, gain, gate, up, down, cotangent):
    rows, model_width = part.shape
    at = chunks[0] // len(chunks)
    hidden_width = gate.shape[1]
    steps = hidden_width // 256
    outs = [f32(rows, model_width), b16(rows, model_width)] + [b16(rows, hidden_width)] * 3
    outs += [f32(rows, model_width)] * 2
    rows_of = pl.BlockSpec((rows, model_width), lambda step: (at, 0), pipeline_mode=pl.Buffered(1))
    columns = pl.BlockSpec((model_width, 256), lambda step: (0, step))
    tiles = pl.BlockSpec((rows, 256), lambda step: (0, step))
    specs = [rows_of, None, None, None, columns, columns]
    specs += [pl.BlockSpec((256, model_width), lambda step: (step, 0)), rows_of]
    operands = (tokens, part, far, gain, gate, up, down, cotangent)
    return call(ffn_kernel, steps, outs, [None, None, tiles, tiles, tiles, None, None], [], operands, specs, 0 * 10**9)


def middle_kernel(
    hidden_ref,
    part_ref,
    far_ref,
    cotangent_ref,
    gain_ref,
    gated_ref,
    square_a_ref,
    square_b_ref,
    params_ref,
    mixer_out_ref,
    attn_out_ref,
    grad_hidden_ref,
    grad_branch_ref,
    grad_rows_ref,
    grad_attended_ref,
    dot_ref,
    gain_sum_ref,
):
    hidden = hidden_ref[...]
    inv = inverse_rms(hidden)
    unit = hidden * inv
    grad_normed = part_ref[...] + far_ref[...]
    gain_sum_ref[0:1, :] = jnp.sum(grad_normed * unit, axis=0, keepdims=True)
    grad_unit = grad_normed * gain_ref[...]
    inner = jnp.mean(grad_unit * unit, axis=-1, keepdims=True)
    grad_hidden = cotangent_ref[...].astype(jnp.float32) + inv * (grad_unit - unit * inner)
    grad_hidden_ref[...] = grad_hidden
    grad_branch = grad_hidden.astype(jnp.bfloat16)
    grad_branch_ref[...] = grad_branch
    grad_rows = dot_nt(grad_branch, mixer_out_ref[...])
    grad_rows_ref[...] = grad_rows
    grad_attended_ref[...] = dot_nt(grad_branch, attn_out_ref[...]).astype(jnp.bfloat16)
    total = jnp.sum(grad_rows * params_ref[6:7, :] * gated_ref[...], axis=-1, keepdims=True)
    for i in range(hidden.shape[0] // LEN):
        at = block(i)
        inv_gated = lax.rsqrt((square_a_ref[:, at] + square_b_ref[:, at]) / DSSM + norm_eps)
        dot_ref[0:1, at] = jnp.broadcast_to(total[at], (LEN, LEN)).T[0:1] * inv_gated


def middle(chunks, hidden, part, far, cotangent, gain, gated, square_a, square_b, gated_gain, mixer_out, attn_out):
    rows, model_width = part.shape
    at = chunks[0] // len(chunks)
    width, inner = mixer_out.shape[0], attn_out.shape[0]
    outs = [
        f32(rows, model_width),
        b16(rows, model_width),
        f32(rows, width),
        b16(rows, inner),
        f32(1, rows),
        f32(8, model_width),
    ]
    rows_of = pl.BlockSpec((rows, model_width), lambda step: (at, 0), pipeline_mode=pl.Buffered(1))
    specs = [None, None, None, rows_of] + [None] * 7
    operands = (hidden, part, far, cotangent, gain, gated, square_a, square_b, gated_gain, mixer_out, attn_out)
    return call(middle_kernel, 1, outs, [None] * 6, [], operands, specs, (0 if chunks[0] else 90) * 10**9)


def core_call(kernel, steps, core, out_shape, out_spec, scratch, operands, specs, flops, aliases=None):
    return pl.pallas_call(
        kernel,
        grid_spec=pltpu.PrefetchScalarGridSpec(
            num_scalar_prefetch=1, grid=(steps,), in_specs=specs, out_specs=out_spec, scratch_shapes=scratch
        ),
        out_shape=out_shape,
        compiler_params=pltpu.CompilerParams(vmem_limit_bytes=VMEM_BYTES),
        cost_estimate=pl.CostEstimate(flops=flops, bytes_accessed=0, transcendentals=0),
        input_output_aliases=aliases or {},
    )(core, *operands)


def clip_tile(rows, columns, first, last):
    return pl.BlockSpec((rows, columns), lambda step, core_ref: (0, jnp.clip(step - first, 0, last - first - 1)))


def ffn_weights_kernel(add, core_ref, *refs):
    refs = list(refs)
    normed_a, normed_b, act_a, act_b, gate_a, gate_b, up_a, up_b, cot_a, cot_b = refs[:10]
    far_ref = refs[10] if add else None
    out_ref, left_ref = refs[-2:]
    step = pl.program_id(0)
    third = pl.num_programs(0) // 3
    half = normed_a.shape[0]

    def turn(first, second):
        left_ref[:, :half] = first[...].T
        left_ref[:, half:] = second[...].T

    @pl.when(step == 0)
    def _():
        turn(normed_a, normed_b)

    @pl.when(step == 2 * third)
    def _():
        turn(act_a, act_b)

    def product(first, second):
        result = dot_nn(left_ref[:, :half], first[...]) + dot_nn(left_ref[:, half:], second[...])
        out_ref[...] = result + far_ref[...] if add else result

    @pl.when(step < third)
    def _():
        product(gate_a, gate_b)

    @pl.when((step >= third) & (step < 2 * third))
    def _():
        product(up_a, up_b)

    @pl.when(step >= 2 * third)
    def _():
        product(cot_a, cot_b)


def ffn_weights(core, far, normed_a, normed_b, act_a, act_b, gate_a, gate_b, up_a, up_b, cotangent):
    half, columns = normed_a.shape
    kept = columns // 2
    tile_width = 512
    third = columns // tile_width
    left = pl.BlockSpec((half, kept), lambda step, core_ref: (0, core_ref[0]), pipeline_mode=pl.Buffered(1))
    specs = [left] * 4 + [clip_tile(half, tile_width, 0, third)] * 2
    specs += [clip_tile(half, tile_width, third, 2 * third)] * 2

    def cot_rows(at):
        return pl.BlockSpec(
            (half, tile_width), lambda step, core_ref: (at, jnp.clip(step - 2 * third, 0, third - 1))
        )

    specs += [cot_rows(0), cot_rows(1)]
    out = pl.BlockSpec((kept, tile_width), lambda step, core_ref: (0, step))
    operands = [normed_a, normed_b, act_a, act_b, gate_a, gate_b, up_a, up_b, cotangent, cotangent]
    if far is not None:
        operands.append(far)
        specs.append(out)
    return core_call(
        functools.partial(ffn_weights_kernel, far is not None),
        3 * third,
        core,
        f32(kept, (3 if far is None else 4) * columns),
        out,
        [pltpu.VMEM((kept, 2 * half), jnp.bfloat16)],
        operands,
        specs,
        0 * 10**9,
    )


def outer_weights_kernel(add, core_ref, *refs):
    refs = list(refs)
    rows_a, rows_b, edge_a, edge_b, att_a, att_b, branch_a, branch_b = refs[:8]
    out_ref, left_ref = refs[-2:]
    half = rows_a.shape[0]
    middle_row = left_ref.shape[0] // 2

    @pl.when((pl.program_id(0) == 0) & (core_ref[0] == 0))
    def _():
        left_ref[:, :half] = rows_a[...].T
        left_ref[:, half:] = rows_b[...].T

    @pl.when((pl.program_id(0) == 0) & (core_ref[0] == 1))
    def _():
        left_ref[:middle_row, :half] = edge_a[...].T
        left_ref[:middle_row, half:] = edge_b[...].T
        left_ref[middle_row:, :half] = att_a[...].T
        left_ref[middle_row:, half:] = att_b[...].T

    result = dot_nn(left_ref[:, :half], branch_a[...]) + dot_nn(left_ref[:, half:], branch_b[...])
    out_ref[...] = result + refs[8][...] if add else result


def outer_weights(core, far, buffer, rows_a, rows_b, att_a, att_b, branch_a, branch_b):
    half, width = rows_a.shape
    model_width = branch_a.shape[1]
    kept = model_width // 2
    tile_width = 512
    steps = model_width // tile_width

    def fixed(shape, column=0):
        return pl.BlockSpec(shape, lambda step, core_ref: (0, column), pipeline_mode=pl.Buffered(1))

    specs = [fixed((half, kept))] * 2
    specs += [fixed((half, width - kept), kept // (width - kept))] * 2
    specs += [fixed(att_a.shape)] * 2 + [clip_tile(half, tile_width, 0, steps)] * 2
    operands = [rows_a, rows_b, rows_a, rows_b, att_a, att_b, branch_a, branch_b]
    out = pl.BlockSpec((kept, tile_width), lambda step, core_ref: (0, step))
    columns, aliases = model_width, {}
    if far is not None:
        operands += [far, buffer]
        specs += [out, pl.BlockSpec(memory_space=pl.ANY)]
        columns = buffer.shape[1]
        first = columns // tile_width - steps
        out = pl.BlockSpec((kept, tile_width), lambda step, core_ref: (0, first + step))
        aliases = {len(operands): 0}
    return core_call(
        functools.partial(outer_weights_kernel, far is not None),
        steps,
        core,
        f32(kept, columns),
        out,
        [pltpu.VMEM((kept, 2 * half), jnp.bfloat16)],
        operands,
        specs,
        0,
        aliases,
    )


PARTS = ((0, 3), (3, 5), (5, 7), (7, 9))


def small_table(rows_ref, gain_ref, state_ref, step_ref, sums_a, sums_b, conv_ref, ffn_a, ffn_b, select_ref):
    kept = rows_ref.shape[1] // 2
    heads = 12
    rows_ref[...] = jnp.zeros(rows_ref.shape, jnp.float32)
    width = conv_ref.shape[1]
    states = state_ref.shape[1]
    rows_ref[0:1, :] = gain_ref[0:1, :]
    for tap in range(4):
        rows_ref[1:2, tap * states : (tap + 1) * states] = state_ref[tap : tap + 1, :]
    rows_ref[2:3, :states] = state_ref[4:5, :]
    sums = sums_a[...] + sums_b[...]
    high, rest = two_terms(sums)
    by_head = dot_nt(high, select_ref[...]) + dot_nt(rest, select_ref[...])
    count = by_head.shape[1]
    rows_ref[3:4, 0:count] = step_ref[0:count, :].T[0:1, :]
    rows_ref[3:4, LEN : LEN + count] = step_ref[count : 2 * count, :].T[0:1, :]
    rows_ref[3:4, 2 * LEN : 2 * LEN + count] = by_head[0:1, :]
    rows_ref[4:9, :width] = conv_ref[0:5, :]
    rows_ref[9:10, :width] = sums[1:2, :]
    rows_ref[10:11, :] = ffn_a[0:1, :] + ffn_b[0:1, :]
    stacked = []
    for index in range(11):
        stacked += [rows_ref[index : index + 1, :kept], rows_ref[index : index + 1, kept:]]
    before = jnp.zeros((heads, kept), jnp.float32)
    behind = jnp.zeros((LEN - heads - len(stacked), kept), jnp.float32)
    return jnp.concatenate([before, *stacked, behind], axis=0).T


def mixer_weights_kernel(add, core_ref, *refs):
    refs = list(refs)
    normed_ref, gate_a, gate_b, conv_ref, query_a, query_b, state_ref, pair_ref, step_ref = refs[:9]
    far_ref = refs[9] if add else None
    outs = refs[19:27] if add else refs[9:10]
    left_ref, result_ref = refs[-3:-1] if add else refs[-2:]
    step = pl.program_id(0)
    half = gate_a.shape[0]

    @pl.when(step == 0)
    def _():
        left_ref[...] = normed_ref[...].T

    def two(first, second):
        result_ref[...] = dot_nn(left_ref[:, :half], first[...]) + dot_nn(left_ref[:, half:], second[...])

    @pl.when(step < 3)
    def _():
        two(gate_a, gate_b)

    @pl.when((step >= 3) & (step < 6))
    def _():
        result_ref[...] = dot_nn(left_ref[...], conv_ref[...])

    @pl.when(step == 6)
    def _():
        two(query_a, query_b)

    @pl.when(step == 7)
    def _():
        result_ref[...] = dot_nn(left_ref[...], state_ref[...])

    @pl.when(step == 8)
    def _():
        result_ref[:, :LEN] = dot_nn(left_ref[...], pair_ref[...])
        steps = dot_nn(left_ref[...], step_ref[...])
        result_ref[:, LEN:] = steps + small_table(refs[-1], *refs[10:19]) if add else steps

    if not add:
        outs[0][...] = result_ref[...]
        return
    result_ref[...] = result_ref[...] + far_ref[...]
    for k, (first, last) in enumerate(PARTS):

        @pl.when((step >= first) & (step < last))
        def _():
            for side in range(2):
                out_ref = outs[2 * k + side]
                for q in range(2):
                    index = core_ref[1 + 4 * k + 2 * side + q]
                    if k < 2:
                        for y in range(4):
                            start = pl.multiple_of((4 * y + index) * 32, 32)
                            out_ref[(2 * y + q) * 32 : (2 * y + q + 1) * 32, :] = result_ref[pl.ds(start, 32), :]
                    else:
                        start = pl.multiple_of(index * LEN, LEN)
                        out_ref[q * LEN : (q + 1) * LEN, :] = result_ref[pl.ds(start, LEN), :]


def mixer_weights(core, far, smalls, normed, gate_a, gate_b, conv, query_a, query_b, state, pair, step):
    half = gate_a.shape[0]
    rows, model_width = normed.shape
    kept = model_width // 2
    tile_width = 256
    steps = 9

    def fixed(shape, column=0):
        return pl.BlockSpec(shape, lambda step, core_ref: (0, column), pipeline_mode=pl.Buffered(1))

    specs = [pl.BlockSpec((rows, kept), lambda step, core_ref: (0, core_ref[0]), pipeline_mode=pl.Buffered(1))]
    specs += [clip_tile(half, tile_width, 0, 3)] * 2 + [clip_tile(rows, tile_width, 3, 6)]
    specs += [fixed(query_a.shape)] * 2 + [fixed(state.shape), fixed(pair.shape), fixed(step.shape)]
    operands = [normed, gate_a, gate_b, conv, query_a, query_b, state, pair, step]
    out = pl.BlockSpec((kept, tile_width), lambda step, core_ref: (0, step))
    shape = f32(kept, steps * tile_width)
    if far is not None:
        operands += [far, *smalls]
        specs += [out] + [fixed(v.shape) for v in smalls]
        out, shape = [], []
        for first, last in PARTS:
            out += [clip_tile(kept // 2, tile_width, first, last)] * 2
            shape += [f32(kept // 2, (last - first) * tile_width)] * 2
    return core_call(
        functools.partial(mixer_weights_kernel, far is not None),
        steps,
        core,
        shape,
        out,
        [pltpu.VMEM((kept, rows), jnp.bfloat16), pltpu.VMEM((kept, tile_width), jnp.float32)]
        + ([pltpu.VMEM((16, model_width), jnp.float32)] if far is not None else []),
        operands,
        specs,
        30 * 10**9,
    )


def normed_back_kernel(
    gate_a,
    gate_b,
    conv_ref,
    query_a,
    query_b,
    state_ref,
    pair_ref,
    step_ref,
    wide_ref,
    small_ref,
    tokens_ref,
    whole_ref,
    out_ref,
    sum_ref,
    inv_ref,
):
    @pl.when(pl.program_id(0) == 0)
    def _():
        inv_ref[...] = jnp.broadcast_to(inverse_rms(whole_ref[...].astype(jnp.float32)), inv_ref.shape)

    half, width = gate_a.shape
    query_width = query_a.shape[1]
    gate_w, conv_w = wide_ref[:, :width], wide_ref[:, width:]
    state_w = small_ref[:, : 2 * LEN]
    query_w = small_ref[:, 2 * LEN : 2 * LEN + query_width]
    pair_w = small_ref[:, 2 * LEN + query_width : 3 * LEN + query_width]
    step_w = small_ref[:, 3 * LEN + query_width :]
    total = jnp.zeros((1, out_ref.shape[1]), jnp.float32)
    for k, (gate, query) in enumerate(((gate_a, query_a), (gate_b, query_b))):
        at = slice(k * half, (k + 1) * half)
        grad = dot_nt(gate[...], gate_w) + dot_nt(conv_ref[at, :], conv_w) + dot_nt(query[...], query_w)
        grad = grad + dot_nt(state_ref[at, :], state_w) + dot_nt(pair_ref[at, :], pair_w) + dot_nt(step_ref[at, :], step_w)
        out_ref[at, :] = grad
        unit = tokens_ref[at, :].astype(jnp.float32) * jnp.concatenate([inv_ref[at, :]] * 2, axis=1)
        total = total + jnp.sum(grad * unit, axis=0, keepdims=True)
    sum_ref[0:1, :] = total


def normed_back(gate_a, gate_b, conv, query_a, query_b, state, pair, step, wide_proj, small_proj, tokens):
    rows, model_width = tokens.shape
    tile_width = 256
    operands = (gate_a, gate_b, conv, query_a, query_b, state, pair, step, wide_proj, small_proj, tokens, tokens)

    def weights(count):
        return pl.BlockSpec((tile_width, count), lambda step: (step, 0))

    columns = pl.BlockSpec((rows, tile_width), lambda step: (0, step))
    specs = [None] * 8 + [weights(wide_proj.shape[1]), weights(small_proj.shape[1]), columns, None]
    out_specs = [columns, pl.BlockSpec((8, tile_width), lambda step: (0, step))]
    outs = [f32(rows, model_width), f32(8, model_width)]
    return call(
        normed_back_kernel,
        model_width // tile_width,
        outs,
        out_specs,
        [pltpu.VMEM((rows, LEN), jnp.float32)],
        operands,
        specs, 30 * 10**9)


def project_kernel(wide_steps, tokens_ref, gain_ref, wide_ref, small_ref, out_ref, normed_ref):
    step = pl.program_id(0)

    @pl.when(step == 0)
    def _():
        tokens = tokens_ref[...].astype(jnp.float32)
        normed_ref[...] = (tokens * inverse_rms(tokens) * gain_ref[...]).astype(jnp.bfloat16)

    @pl.when(step < wide_steps)
    def _():
        out_ref[...] = dot_nn(normed_ref[...], wide_ref[...])

    @pl.when(step >= wide_steps)
    def _():
        out_ref[...] = dot_nn(normed_ref[...], small_ref[...])


def project(tokens, gain, wide_proj, small_proj):
    rows, model_width = tokens.shape
    count = 768
    wide_steps = wide_proj.shape[1] // count
    steps = wide_steps + small_proj.shape[1] // count
    outs = [f32(rows, steps * count), b16(rows, model_width)]
    wide = pl.BlockSpec((model_width, count), lambda step: (0, jnp.minimum(step, wide_steps - 1)))
    small = pl.BlockSpec((model_width, count), lambda step: (0, jnp.maximum(step - wide_steps, 0)))
    out = pl.BlockSpec((rows, count), lambda step: (0, step))
    operands = (tokens, gain, wide_proj, small_proj)
    kernel = functools.partial(project_kernel, wide_steps)
    return call(kernel, steps, outs, [out, None], [], operands, [None, None, wide, small], 0)


def unpack_kernel(
    block_ref,
    step_ref,
    input_gain_ref,
    state_kernel_ref,
    state_bias_ref,
    step_bias_ref,
    decay_ref,
    skip_ref,
    conv_kernel_ref,
    conv_bias_ref,
    gated_gain_ref,
    ffn_gain_ref,
    turned_ref,
):
    heads = step_ref.shape[0]
    for i in range(block_ref.shape[0] // LEN):
        turned_ref[:, block(i)] = block_ref[block(i), :].T

    half = block_ref.shape[0] // 2

    def row(index, count, start=0):
        pieces = []
        for side in range(2):
            low, high = max(start, side * half), min(start + count, (side + 1) * half)
            if low < high:
                column, at = heads + 2 * index + side, low - side * half
                mine = turned_ref[column : column + 1, at : at + high - low]
                pieces.append(mine + turned_ref[column : column + 1, half + at : half + at + high - low])
        return (pieces[0] if len(pieces) == 1 else jnp.concatenate(pieces, axis=1))[0]

    step_ref[...] = turned_ref[0:heads, :]
    input_gain_ref[...] = row(0, input_gain_ref.shape[0])
    columns = state_kernel_ref.shape[1]
    for tap in range(4):
        state_kernel_ref[tap, :] = row(1, columns, tap * columns)
        conv_kernel_ref[tap, :] = row(4 + tap, conv_kernel_ref.shape[1])
    state_bias_ref[...] = row(2, columns)
    step_bias_ref[...] = row(3, heads)
    decay_ref[...] = row(3, heads, LEN)
    skip_ref[...] = row(3, heads, 2 * LEN)
    conv_bias_ref[...] = row(8, conv_bias_ref.shape[0])
    gated_gain_ref[...] = row(9, gated_gain_ref.shape[0])
    ffn_gain_ref[...] = row(10, ffn_gain_ref.shape[0])


def unpack(heads, width, states, values):
    rows = values.shape[0]
    outs = [f32(heads, rows), f32(rows), f32(4, states), f32(states), f32(heads), f32(heads), f32(heads)]
    outs += [f32(4, width), f32(width), f32(width), f32(rows)]
    scratch = [pltpu.VMEM((LEN, rows), jnp.float32)]
    return call(unpack_kernel, 1, outs, [None] * len(outs), scratch, (values,), [None], 0)


def assemble_kernel(source, mixer_proj_ref, query_ref, pair_ref, state_ref, step_ref):
    width = mixer_proj_ref.shape[2]
    start = 0
    mixer_proj_ref[:, 0, :] = source[:, start : start + width]
    start += width
    mixer_proj_ref[:, 1, :] = source[:, start : start + width]
    start += width
    query_ref[...] = source[:, start : start + query_ref.shape[1]]
    start += query_ref.shape[1]
    state_ref[...] = source[:, start : start + 2 * LEN]
    start += 2 * LEN
    pair_ref[:, 0, :] = source[:, start : start + LEN]
    step_ref[...] = source[:, start + LEN :]


def assemble(values, width, query_width):
    rows, columns = values.shape

    def plain(count):
        return pl.BlockSpec((LEN, count), lambda at: (at, 0))

    out_specs = [
        pl.BlockSpec((LEN, 2, width), lambda at: (at, 0, 0)),
        plain(query_width),
        pl.BlockSpec((LEN, 1, LEN), lambda at: (at, 0, 0)),
        plain(2 * LEN),
        plain(LEN),
    ]
    out_shape = [
        f32(rows, 2, width),
        f32(rows, query_width),
        f32(rows, 1, LEN),
        f32(rows, 2 * LEN),
        f32(rows, LEN),
    ]
    return call(assemble_kernel, rows // LEN, out_shape, out_specs, [], (values,), [plain(columns)], 0)


LINKS = {
    "A": [(0, 1), (1, 0), (2, 3), (3, 2)],
    "B": [(1, 2), (2, 1), (3, 0), (0, 3)],
}
ORDERS = (
    (("x", "A"), ("x", "B"), ("y", "A"), ("y", "B")),
    (("x", "B"), ("y", "A"), ("y", "B"), ("x", "A")),
    (("y", "A"), ("y", "B"), ("x", "A"), ("x", "B")),
    (("y", "B"), ("x", "A"), ("x", "B"), ("y", "A")),
)
AXIS = {"y": 0, "x": 1}


def take(values, index, axis):
    return lax.dynamic_slice_in_dim(values, index, 1, axis)


def halves(values, name, link, again):
    place, axis = lax.axis_index(name), AXIS[name]
    if again:
        index = place // 2 if link == "B" else place % 2
        return take(values, index, axis), take(values, 1 - index, axis)
    if link == "B":
        side = place // 2
        kept = lax.dynamic_slice_in_dim(values, 2 * side, 2, axis)
        return kept, lax.dynamic_slice_in_dim(values, 2 - 2 * side, 2, axis)
    side = ((place + 1) // 2) % 2
    kept = jnp.concatenate([take(values, side, axis), take(values, 3 - side, axis)], axis)
    return kept, jnp.concatenate([take(values, 1 - side, axis), take(values, 2 + side, axis)], axis)


def reduce_rows(pairs, steps):
    kept, sent, parts = [], [], pairs
    if steps[0] == 0:
        for k, (stays, goes) in enumerate(pairs):
            shape = (4, 2, 32, stays.shape[1]) if ORDERS[k][0][0] == "x" else (2, 4, 32, stays.shape[1])
            kept.append(stays.reshape(shape))
            sent.append(goes.reshape(shape))
    for step in steps:
        if step:
            kept, sent = [], []
            for k in range(4):
                name, link = ORDERS[k][step]
                again = name in [n for n, _ in ORDERS[k][:step]]
                stays, goes = halves(parts[k], name, link, again)
                kept.append(stays)
                sent.append(goes)
        sent = lax.optimization_barrier(tuple(sent))
        come = [lax.ppermute(sent[k], ORDERS[k][step][0], LINKS[ORDERS[k][step][1]]) for k in range(4)]
        come = lax.optimization_barrier(tuple(come))
        parts = [stays + more for stays, more in zip(kept, come)]
    return parts


def rope_tables(rows):
    half_size = HEAD_DIM // 2
    inverse = np.float32(rope_base) ** (-(2.0 * np.arange(half_size, dtype=np.float32)) / HEAD_DIM)
    angles = np.arange(rows, dtype=np.float32)[:, None] * inverse.astype(np.float32)[None, :]
    cosine, sine = np.cos(angles), np.sin(angles)
    return (
        np.concatenate([cosine] * 4, axis=1).astype(np.float32),
        np.concatenate([-sine, sine, -sine, sine], axis=1).astype(np.float32),
    )


def norm_backward(grad_unit, unit_rows, inv_rms):
    return inv_rms * (grad_unit - unit_rows * jnp.mean(grad_unit * unit_rows, axis=-1, keepdims=True))


def dot32(left, right):
    return jnp.dot(left, right, preferred_element_type=jnp.float32)


def after(value, *others):
    return lax.optimization_barrier((value, *others))[0]


def swap(values, name):
    return lax.ppermute(values, name, PAIR)


def exchange(values, name):
    return values + swap(values, name)


def core_rows(values, index):
    half = values.shape[1] // 2
    return lax.dynamic_slice_in_dim(values, index * half, half, 1)


def on_device(
    layer_input,
    segments,
    input_gain,
    mixer_proj,
    state_proj,
    step_proj,
    step_bias,
    decay_log,
    skip_gain,
    conv_kernel,
    conv_bias,
    state_kernel,
    state_bias,
    gated_gain,
    mixer_out,
    query_proj,
    key_value_weight,
    attn_out,
    ffn_gain,
    ffn_gate,
    ffn_up,
    ffn_down,
    cotangent,
):
    rows, model_width = layer_input.shape
    width = mixer_proj.shape[2]
    heads = step_proj.shape[1]
    state_size = state_proj.shape[1] // 2
    query_width = query_proj.shape[1]
    pair_width = key_value_weight.shape[2]
    place = lax.axis_index("core")
    zh = lax.axis_index("zh")
    core = place.astype(jnp.int32).reshape(1)
    far_core = 1 - core
    cosine, sine = rope_tables(rows)
    select = np.arange(HEAD_ROWS)[:, None] == np.arange(width)[None, :] // HEAD_DIM
    select = jnp.asarray(select.astype(np.float32)).astype(jnp.bfloat16)
    seg_row = segments
    pad_heads = ((0, 0), (0, LEN - heads))

    def padded(values):
        return jnp.pad(values, ((0, 0), (0, width - values.shape[1])))

    params = jnp.concatenate(
        [
            conv_kernel,
            conv_bias[None, :],
            jnp.repeat(skip_gain, HEAD_DIM)[None, :],
            gated_gain[None, :],
            jnp.zeros((1, width), jnp.float32),
            padded(state_kernel),
            padded(state_bias[None, :]),
            padded(step_bias[None, :]),
            padded(-jnp.exp(decay_log)[None, :]),
            jnp.zeros((1, width), jnp.float32),
        ],
        axis=0,
    )
    wide_proj = mixer_proj.reshape(model_width, 2 * width)
    small_proj = jnp.concatenate(
        [
            state_proj,
            query_proj,
            key_value_weight.reshape(model_width, pair_width),
            jnp.pad(step_proj, pad_heads),
        ],
        axis=1,
    )
    tokens = layer_input.astype(jnp.float32)
    wide_in, normed_input = project(layer_input, input_gain[None, :], wide_proj, small_proj)
    x, xb, slope, state, state_slope, cum, lag, cum_row, lag_row, step_row, sig_row, queries, pairs = scan_prep(
        width,
        wide_in,
        cosine,
        sine,
        seg_row,
        params,
    )

    blocks = rows // LEN
    late = tuple(range(blocks // 2, blocks))
    early = tuple(range(blocks // 2))
    half = {}
    for chunks in (late, early):
        h = {"span": slice(chunks[0] * LEN, (chunks[-1] + 1) * LEN)}
        h["y"], h["gated"], h["square"] = scan_forward(
            chunks, heads, wide_in, x, xb, state, cum, lag_row, seg_row, params
        )
        half[chunks] = h
    squares = jnp.concatenate([half[early]["square"], half[late]["square"]], axis=1)
    squares_far = swap(squares, "tensor")
    ready = squares
    for chunks in (late, early):
        h = half[chunks]
        h["attended"], h["lse"] = attention_forward(chunks, after(queries, ready), pairs, seg_row)
        if chunks == late:
            squares_far = after(squares_far, h["lse"])
            squares_all = squares + squares_far
        h["square"], h["square_far"] = squares[:, h["span"]], squares_far[:, h["span"]]
        h["inv_gated"] = lax.rsqrt(squares_all[:, h["span"]].reshape(-1, 1) / DSSM + norm_eps)
        h["mixer_rows"] = (h["gated"] * h["inv_gated"] * gated_gain).astype(jnp.bfloat16)
        h["part"] = dot32(h["mixer_rows"], mixer_out) + dot32(h["attended"], attn_out)
        h["branch_far"] = swap(h["part"], "tensor")
        ready = h["part"]

    a, b = half[early], half[late]
    gain_ffn = ffn_gain[None, :]
    names = ("hidden", "normed", "activated", "grad_gate_rows", "grad_up_rows", "back", "down")
    for chunks in (late, early):
        h = half[chunks]
        far = h["branch_far"] if chunks == late else after(h["branch_far"], b["back"])
        operands = (layer_input, h["part"], far, gain_ffn, ffn_gate, ffn_up, ffn_down, cotangent)
        h.update(zip(names, ffn(chunks, *operands)))
        h["back_far"] = swap(h["back"], "tensor")

    for chunks in (late, early):
        h = half[chunks]
        far = h["back_far"] if chunks == late else after(h["back_far"], first)
        h["grad_hidden"], h["grad_branch"], h["grad_rows"], grad_attended, h["dot"], h["gain_sum"] = middle(
            chunks,
            h["hidden"],
            h["back"],
            far,
            cotangent,
            gain_ffn,
            h["gated"],
            h["square"],
            h["square_far"],
            params,
            mixer_out,
            attn_out,
        )
        if chunks == early:
            dots = jnp.concatenate([a["dot"], b["dot"]], axis=1)
            outer = (a["mixer_rows"], b["mixer_rows"], a["attended"], b["attended"])
            outer += (a["grad_branch"], b["grad_branch"])
            outer_sent = outer_weights(far_core, None, None, *outer)
            outer_far = swap(outer_sent, "core")
            first = ffn_weights(core, after(first_far, outer_sent), *sides)
            dots_far = swap(after(dots, first), "tensor")
            first = outer_weights(core, outer_far, first, *outer)
            first_sum = lax.psum_scatter(first, ("y", "x"), scatter_dimension=0, tiled=True)
            grad_attended = after(grad_attended, first)
        operands = (queries, pairs, grad_attended, h["lse"], seg_row, cosine, sine)
        if chunks == late:
            h["grad_queries"], grad_keys, grad_values = attention_backward(chunks, False, *operands)
            sides = (after(a["normed"], grad_keys), b["normed"], a["activated"], b["activated"])
            sides += (a["grad_gate_rows"], b["grad_gate_rows"], a["grad_up_rows"], b["grad_up_rows"], cotangent)
            first = ffn_weights(far_core, None, *sides)
            first_far = swap(first, "core")
        else:
            h["grad_queries"], grad_pairs = attention_backward(chunks, True, *operands, grad_keys, grad_values)
    dots_far = after(dots_far, grad_pairs)
    for chunks in (late, early):
        h = half[chunks]
        h["grad_gate"], h["gy"], h["dx"], h["p"], h["grad_in"], h["grad_out"], h["sums"] = scan_backward(
            chunks,
            heads,
            h["grad_rows"],
            h["gated"],
            h["square"],
            h["square_far"],
            h["dot"],
            dots_far[:, h["span"]],
            params,
            wide_in,
            h["y"],
            x,
            xb,
            state,
            lag,
            cum_row,
            seg_row,
            select,
        )
    pieces = [b["down"][:LEN], b["down"][LEN:], a["down"][:LEN], a["down"][LEN:]]
    pieces_far = [swap(after(piece, dots_far), "tensor") for piece in pieces[:3]]
    down = jnp.concatenate([a["down"], b["down"]], axis=0)
    ends = []
    for name in ("gy", "dx", "p", "grad_in", "grad_out"):
        ends += [a[name], b[name]]
    grad_conv, grad_state, grad_step, conv_sum, state_sum, step_sum = scan_end(
        heads,
        *ends,
        xb,
        slope,
        state_slope,
        wide_in,
        wide_in,
        step_row,
        sig_row,
        seg_row,
        select,
        params,
        params,
    )

    grads = (a["grad_gate"], b["grad_gate"], grad_conv, a["grad_queries"], b["grad_queries"])
    grads += (grad_state, grad_pairs, grad_step)
    tied = after(normed_input, pieces_far[0], pieces_far[1])
    second_far = swap(mixer_weights(far_core, None, None, tied, *grads), "core")
    partial_normed, input_gain_sum = normed_back(*grads, wide_proj, small_proj, layer_input)

    smalls = (input_gain_sum, state_sum, step_sum, a["sums"], b["sums"], conv_sum, a["gain_sum"], b["gain_sum"], select)
    shared_end = heads + 6
    spots = [core]
    for name, link in [order[0] for order in ORDERS]:
        at = lax.axis_index(name).astype(jnp.int32)
        side = ((at + 1) // 2) % 2 if link == "A" else at // 2
        spots.append(jnp.stack([side, 3 - side, 1 - side, 2 + side] if link == "A" else [2 * side, 2 * side + 1, 2 - 2 * side, 3 - 2 * side]))
    second = mixer_weights(jnp.concatenate(spots), after(second_far, pieces_far[2]), smalls, normed_input, *grads)
    second = list(second)
    at_state = 2 * width + query_width
    normed_far = [swap(partial_normed[k * LEN : (k + 1) * LEN], "tensor") for k in range(rows // LEN)]
    second[1] = after(second[1], normed_far[0])
    parts = reduce_rows([(second[2 * k], second[2 * k + 1]) for k in range(4)], (0,))
    parts[0] = after(parts[0], normed_far[1])
    first_own = exchange(after(first_sum, parts[0]), "zh")
    first_all = lax.all_gather(first_own, ("core", "y", "x"), axis=0, tiled=True)
    parts = reduce_rows(parts, (1,))
    parts[0] = after(parts[0], normed_far[2])
    parts = reduce_rows(parts, (2,))
    parts[0] = after(parts[0], normed_far[3])
    parts = reduce_rows(parts, (3,))
    second = jnp.concatenate([p.reshape(32, -1) for p in parts], axis=1)
    both = second[:, at_state:]
    lane = np.arange(both.shape[1])
    in_table = lane - 2 * state_size - pair_width
    is_shared = (lane < 2 * state_size) | ((in_table >= heads) & (in_table < shared_end))
    diagonal = [(0, 3), (3, 0), (1, 2), (2, 1)]
    more = swap(both, "tensor") + lax.ppermute(both, ("zh", "tensor"), diagonal)
    second = exchange(second, "zh")
    summed = second[:, at_state:] + jnp.where(is_shared[None, :], more, 0.0)
    second = jnp.concatenate([second[:, :at_state], summed], axis=1)
    second = after(second, first_all)
    pieces_far.append(swap(after(pieces[3], second), "tensor"))
    second = lax.all_gather(second, ("core", "y", "x"), axis=0, tiled=True)
    grad_mixer_proj, grad_query_proj, grad_keyval, grad_state_proj, step_block = assemble(second, width, query_width)

    def whole(name):
        return jnp.concatenate([a[name], b[name]], axis=0)

    grad_hidden = whole("grad_hidden")
    grad_normed = partial_normed + jnp.concatenate(normed_far, axis=0)
    inv_rms_in = inverse_rms(tokens)
    unit_in = tokens * inv_rms_in
    input_grad = grad_hidden + norm_backward(grad_normed * input_gain, unit_in, inv_rms_in)
    down_far = jnp.concatenate([pieces_far[2], pieces_far[3], pieces_far[0], pieces_far[1]], axis=0)
    layer_output = (whole("hidden") + (down + down_far)).astype(jnp.bfloat16)

    smalls = unpack(heads, width, 2 * state_size, step_block)
    return (
        layer_output,
        input_grad,
        smalls[1],
        grad_mixer_proj,
        grad_state_proj,
        smalls[0].T,
        smalls[4],
        smalls[5],
        smalls[6],
        smalls[7],
        smalls[8],
        smalls[2],
        smalls[3],
        smalls[9],
        first_all[:width, 3 * model_width :],
        grad_query_proj,
        grad_keyval,
        first_all[width:, 3 * model_width :],
        smalls[10],
        first_all[:, :model_width],
        first_all[:, model_width : 2 * model_width],
        first_all[:, 2 * model_width : 3 * model_width],
    )


def solution(mesh):
    dp, whole_spec, columns = P(DP, None), P(), P(None, "tensor")
    per_channel, middle = P("tensor"), P(None, "tensor", None)
    last, by_rows = P(None, None, "tensor"), P("tensor", None)
    weights = (
        whole_spec,
        last,
        whole_spec,
        columns,
        per_channel,
        per_channel,
        per_channel,
        columns,
        per_channel,
        whole_spec,
        whole_spec,
        per_channel,
        by_rows,
        columns,
        middle,
        by_rows,
        whole_spec,
        columns,
        columns,
        by_rows,
    )
    mesh = jax.sharding.Mesh(mesh.devices.reshape(4, 2, 4, 2, 2), (*DP, "tensor"))
    return jax.shard_map(
        on_device, mesh=mesh, in_specs=(dp, dp, *weights, dp), out_specs=(dp, dp, *weights), check_vma=False
    )
```

```python
import functools

import jax
import jax.numpy as jnp
import numpy as np
from jax import lax
from jax.experimental import pallas as pl
from jax.experimental.pallas import tpu as pltpu
from jax.sharding import PartitionSpec as P

HEAD_DIM = 64
DSSM = 1536
DP = ("y", "zh", "x", "core")
PAIR = [(0, 1), (1, 0)]
LOG2E = 1.4426950408889634
hidden_bias = -1e30
norm_eps = 1e-05
rope_base = 10000.0
LEN = 128


def dot_nn(left, right):
    return lax.dot_general(
        left, right, (((1,), (0,)), ((), ())), preferred_element_type=jnp.float32
    )


def dot_nt(left, right):
    return lax.dot_general(
        left, right, (((1,), (1,)), ((), ())), preferred_element_type=jnp.float32
    )


def dot_tn(left, right):
    return lax.dot_general(
        left, right, (((0,), (0,)), ((), ())), preferred_element_type=jnp.float32
    )


def two_terms(v):
    high = v.astype(jnp.bfloat16)
    return high, (v - high.astype(jnp.float32)).astype(jnp.bfloat16)


def three_dots(dot, left, right):
    left_high, left_low = two_terms(left)
    right_high, right_low = two_terms(right)
    return dot(left_high, right_high) + dot(left_high, right_low) + dot(left_low, right_high)


def sigmoid(v):
    return 1.0 / (1.0 + jnp.exp(-v))


def block(index):
    return slice(index * LEN, (index + 1) * LEN)


def lane_iota(rows=LEN):
    return lax.broadcasted_iota(jnp.int32, (rows, LEN), 1)


def turned(row):
    return jnp.broadcast_to(row, (LEN, LEN)).T


def mask_ts(seg_row, i, j):
    same = turned(seg_row[:, block(i)].astype(jnp.float32)) == seg_row[:, block(j)].astype(jnp.float32)
    if i != j:
        return same
    down = lax.broadcasted_iota(jnp.int32, (LEN, LEN), 0)
    return same & (down >= lane_iota())


def mask_st(seg_row, j, i):
    same = turned(seg_row[:, block(j)].astype(jnp.float32)) == seg_row[:, block(i)].astype(jnp.float32)
    if i != j:
        return same
    down = lax.broadcasted_iota(jnp.int32, (LEN, LEN), 0)
    return same & (down <= lane_iota())


def conv_rows(pad_ref, keep_ref, kernel, bias, start, lanes):
    summed = bias + kernel[3:4] * pad_ref[8 + start : 8 + start + LEN, lanes]
    for lag in (1, 2, 3):
        moved = pad_ref[8 + start - lag : 8 + start - lag + LEN, lanes]
        summed = summed + kernel[3 - lag : 4 - lag] * (moved * keep_ref[lag - 1, start : start + LEN, :])
    return summed


def widen(seg_row_ref, wide_ref, pad_ref):
    rows = seg_row_ref.shape[1]
    pad_ref[0:8, :] = jnp.full((8, LEN), -1.0, jnp.float32)
    for i in range(rows // LEN):
        pad_ref[8 + i * LEN : 8 + (i + 1) * LEN, :] = turned(seg_row_ref[:, block(i)].astype(jnp.float32))
    for lag in (1, 2, 3):
        same = pad_ref[8 : rows + 8, :] == pad_ref[8 - lag : rows + 8 - lag, :]
        wide_ref[lag - 1, 0:rows, :] = jnp.where(same, 1.0, 0.0)
        wide_ref[lag - 1, rows : rows + 8, :] = jnp.zeros((8, LEN), jnp.float32)


def prep_kernel(
    conv_ref,
    small_ref,
    cos_ref,
    sin_ref,
    seg_row_ref,
    table_ref,
    params_ref,
    x_ref,
    xb_ref,
    slope_ref,
    state_ref,
    state_slope_ref,
    cum_ref,
    lag_ref,
    cum_row_ref,
    lag_row_ref,
    step_row_ref,
    sig_row_ref,
    q_ref,
    kv_ref,
    pad_ref,
    wide_ref,
):
    rows = conv_ref.shape[0]
    blocks = rows // LEN

    @pl.when(pl.program_id(0) == 0)
    def _():
        widen(seg_row_ref, wide_ref, pad_ref)
        pad_ref[0:8, :] = jnp.zeros((8, LEN), jnp.float32)
        for c in range(2):
            pad_ref[8 : rows + 8, :] = small_ref[:, block(c)]
            for i in range(blocks):
                pre = conv_rows(
                    pad_ref, wide_ref, params_ref[8:12, block(c)], params_ref[12:13, block(c)], i * LEN, slice(0, LEN)
                )
                sig = sigmoid(pre)
                state_ref[block(i), block(c)] = pre * sig
                state_slope_ref[block(i), block(c)] = sig * (1.0 + pre * (1.0 - sig))

    @pl.when(pl.program_id(0) == 1)
    def _():
        down = lax.broadcasted_iota(jnp.int32, (LEN, LEN), 0)
        lower = jnp.where(down >= lane_iota(), 1.0, 0.0).astype(jnp.bfloat16)
        left_half = lane_iota() < HEAD_DIM
        carry = jnp.zeros((1, LEN), jnp.float32)
        heads = cum_row_ref.shape[0]
        for i in range(blocks):
            argument = small_ref[block(i), block(5)] + params_ref[13:14, :LEN]
            tail = jnp.exp(-jnp.abs(argument))
            grown = jnp.where(tail < 1e-3, tail - 0.5 * tail * tail, jnp.log(1.0 + tail))
            step = jnp.maximum(argument, 0.0) + grown
            scaled = step * params_ref[14:15, :LEN] * LOG2E
            first, rest = two_terms(scaled)
            last = scaled - first.astype(jnp.float32) - rest.astype(jnp.float32)
            cum = dot_nn(lower, first) + dot_nn(lower, rest) + dot_nn(lower, last.astype(jnp.bfloat16)) + carry
            carry = cum[LEN - 1 : LEN, :]
            lag = cum - jnp.log(step) * LOG2E
            cum_ref[block(i), :] = cum
            lag_ref[block(i), :] = lag
            cum_t, lag_t = cum.T, lag.T
            step_row_ref[:, block(i)] = step.T[:heads]
            sig_row_ref[:, block(i)] = sigmoid(argument).T[:heads]
            for h in range(heads):
                cum_row_ref[h, :, block(i)] = cum_t[h : h + 1]
                lag_row_ref[h, :, block(i)] = lag_t[h : h + 1]
            cosine, sine = cos_ref[block(i), :], sin_ref[block(i), :]
            kv = small_ref[block(i), block(4)]
            kv_ref[block(i), :] = jnp.where(left_half, rotate_tile(kv, cosine, sine), kv).astype(jnp.bfloat16)
            for p in range(q_ref.shape[1] // LEN):
                q_ref[block(i), block(p)] = rotate_tile(small_ref[block(i), block(2 + p)], cosine, sine).astype(
                    jnp.bfloat16
                )

    for sub in range(GROUP):
        lanes = block(sub)
        pad_ref[8 : rows + 8, :] = conv_ref[:, lanes]
        for i in range(blocks):
            pre = conv_rows(pad_ref, wide_ref, table_ref[0:4, lanes], table_ref[4:5, lanes], i * LEN, slice(0, LEN))
            sig = sigmoid(pre)
            x = pre * sig
            x_ref[block(i), lanes] = x
            xb_ref[block(i), lanes] = x.astype(jnp.bfloat16)
            slope_ref[block(i), lanes] = sig * (1.0 + pre * (1.0 - sig))


def rotate_tile(v, cosine, sine):
    first = lax.rem(lane_iota(v.shape[0]), HEAD_DIM) < HEAD_DIM // 2
    swapped = jnp.where(first, pltpu.roll(v, LEN - HEAD_DIM // 2, 1), pltpu.roll(v, HEAD_DIM // 2, 1))
    return v * cosine + swapped * sine


def scan_kernel(
    chunks,
    heads,
    gate_ref,
    x_ref,
    xb_ref,
    state_ref,
    cum_ref,
    lag_row_ref,
    seg_row_ref,
    table_ref,
    y_ref,
    gated_ref,
    row_ref,
    wide_ref,
    cross_ref,
    bias_ref,
    mix_ref,
    square_ref,
):
    step = pl.program_id(0)
    first = chunks[0]
    pairs = [(i, j) for i in chunks for j in range(max(0, i - 2), i + 1)]
    left_half = lane_iota() < HEAD_DIM

    @pl.when(step == 0)
    def _():
        for h in range(heads):
            for i in chunks:
                wide_ref[h, block(i - first), :] = jnp.broadcast_to(cum_ref[block(i), h : h + 1], (LEN, LEN))
        for i in chunks:
            low = max(0, i - 2)
            cross = three_dots(dot_nt, state_ref[block(i), LEN:], state_ref[low * LEN : (i + 1) * LEN, :LEN])
            for n, (i2, j) in enumerate(pairs):
                if i2 == i:
                    cross_ref[n] = cross[:, block(j - low)]
                    allowed = mask_ts(seg_row_ref, i, j)
                    bias_ref[n] = jnp.where(allowed, 0.0, hidden_bias)
        square_ref[...] = jnp.zeros(square_ref.shape, jnp.float32)

    tiles = (gate_ref, x_ref, xb_ref, table_ref.at[5:6], y_ref, gated_ref)

    def head_pair(hp, gate_ref, x_ref, xb_ref, skip_ref, y_ref, gated_ref):
        for i in chunks:
            at = block(i - first)
            low = max(0, i - 2)
            for n, (i2, j) in enumerate(pairs):
                if i2 != i:
                    continue
                for e in range(2):
                    spread = wide_ref[2 * hp + e, at, :] - lag_row_ref[2 * hp + e, :, block(j)]
                    decay = jnp.exp2(spread + bias_ref[n])
                    mix_ref[i - first, block(e), block(j - low)] = (decay * cross_ref[n]).astype(jnp.bfloat16)
            both = dot_nn(mix_ref[i - first, :, : (i + 1 - low) * LEN], xb_ref[low * LEN : (i + 1) * LEN, :])
            y = jnp.where(left_half, both[:LEN], both[LEN:])
            y_ref[at, :] = y
            gate = gate_ref[at, :]
            gated = (y + skip_ref[...] * x_ref[at, :]) * (gate * sigmoid(gate))
            gated_ref[at, :] = gated
            square_ref[at, :] = square_ref[at, :] + gated * gated

    for sub in range(GROUP):
        head_pair(GROUP * step + sub, *[t.at[:, block(sub)] for t in tiles])

    @pl.when(step == pl.num_programs(0) - 1)
    def _():
        for i in chunks:
            at = block(i - first)
            total = jnp.sum(square_ref[at, :], axis=1, keepdims=True)
            row_ref[0:1, at] = jnp.broadcast_to(total, (LEN, LEN)).T[0:1]


def attention_kernel(chunks, q_ref, kv_ref, seg_row_ref, out_ref, lse_ref):
    scale = HEAD_DIM ** (-0.5) * LOG2E
    first = chunks[0]
    left_half = lane_iota() < HEAD_DIM
    zero = jnp.zeros((LEN, LEN), jnp.bfloat16)
    lse_ref[...] = jnp.zeros(lse_ref.shape, jnp.float32)
    for i in chunks:
        at = block(i - first)
        low = max(0, i - 2) * LEN
        span = (i + 1) * LEN - low
        allowed = jnp.concatenate([mask_ts(seg_row_ref, i, j) for j in range(low // LEN, i + 1)], axis=1)
        keys = kv_ref[low : low + span, :]
        swapped = pltpu.roll(keys.astype(jnp.float32), HEAD_DIM, 1).astype(jnp.bfloat16)
        for p in range(q_ref.shape[1] // LEN):
            queries = q_ref[block(i), block(p)]
            result = []
            for e in range(2):
                masked = jnp.where(left_half == (e == 0), queries, zero)
                scores = dot_nt(masked, keys if e == 0 else swapped) * scale
                scores = jnp.where(allowed, scores, hidden_bias)
                top = jnp.max(scores, axis=1, keepdims=True)
                weights = jnp.exp2(scores - top)
                total = jnp.sum(weights, axis=1, keepdims=True)
                probs = (weights * (1.0 / total)).astype(jnp.bfloat16)
                result.append(dot_nn(probs, swapped if e == 0 else keys))
                lse = jnp.broadcast_to(top + jnp.log(total) * LOG2E, (LEN, LEN))
                lse_ref[2 * p + e : 2 * p + e + 1, at] = lse.T[0:1]
            out_ref[at, block(p)] = jnp.where(left_half, result[0], result[1]).astype(jnp.bfloat16)


def attention_back_kernel(chunks, final, *refs):
    q_ref, kv_ref, do_ref, lse_ref, seg_row_ref, cos_ref, sin_ref = refs[:7]
    if final:
        dk_in_ref, dv_in_ref, dq_ref, dkv_ref, dk_ref, dv_ref, turned_ref, key_t_ref = refs[7:]
    else:
        dq_ref, dk_ref, dv_ref, turned_ref, key_t_ref = refs[7:]
    scale = HEAD_DIM ** (-0.5)
    blocks = q_ref.shape[0] // LEN
    first = chunks[0]
    left_half = lane_iota() < HEAD_DIM
    zero = jnp.zeros((LEN, LEN), jnp.bfloat16)
    for i in range(chunks[-1] + 1):
        kv = kv_ref[block(i), :].astype(jnp.float32)
        turned_ref[block(i), :] = pltpu.roll(kv, HEAD_DIM, 1).astype(jnp.bfloat16)
        key_t_ref[:, block(i)] = kv.T[:HEAD_DIM].astype(jnp.bfloat16)
    if final:
        dk_ref[...] = dk_in_ref[...]
        dv_ref[...] = dv_in_ref[...]
    else:
        dk_ref[...] = jnp.zeros(dk_ref.shape, jnp.float32)
        dv_ref[...] = jnp.zeros(dv_ref.shape, jnp.float32)
    for i in chunks:
        at = block(i - first)
        low = max(0, i - 2) * LEN
        span = (i + 1) * LEN - low
        window = slice(low, low + span)
        allowed = jnp.concatenate([mask_st(seg_row_ref, j, i) for j in range(low // LEN, i + 1)], axis=0)
        keys, swapped = kv_ref[window, :], turned_ref[window, :]
        for p in range(q_ref.shape[1] // LEN):
            queries, douts = q_ref[block(i), block(p)], do_ref[at, block(p)]
            back = []
            for e in range(2):
                side = left_half == (e == 0)
                q_half = jnp.where(side, queries, zero)
                do_half = jnp.where(side, douts, zero)
                h = 2 * p + e
                scores = dot_nt(keys if e == 0 else swapped, q_half) * (scale * LOG2E)
                probs = jnp.exp2(jnp.where(allowed, scores, hidden_bias) - lse_ref[h : h + 1, at])
                dprobs = dot_nt(swapped if e == 0 else keys, do_half)
                inner = jnp.sum(probs * dprobs, axis=0, keepdims=True)
                dscores = (probs * (dprobs - inner)).astype(jnp.bfloat16)
                dv_ref[window, :] = dv_ref[window, :] + dot_nn(probs.astype(jnp.bfloat16), do_half)
                dk_ref[window, :] = dk_ref[window, :] + dot_nn(dscores, q_half)
                back.append(dot_nn(key_t_ref[:, window], dscores))
            dq = jnp.concatenate(back, axis=0).T * scale
            dq_ref[at, block(p)] = rotate_tile(dq, cos_ref[block(i), :], -sin_ref[block(i), :]).astype(jnp.bfloat16)
    if not final:
        return
    for i in range(blocks):
        dk = dk_ref[block(i), :]
        dk = (dk + pltpu.roll(dk, HEAD_DIM, 1)) * scale
        dk = rotate_tile(dk, cos_ref[block(i), :], -sin_ref[block(i), :])
        dv = dv_ref[block(i), :]
        dv = dv + pltpu.roll(dv, HEAD_DIM, 1)
        dkv_ref[block(i), :] = jnp.where(left_half, dk, dv).astype(jnp.bfloat16)


def scan_back_kernel(
    chunks,
    heads,
    gmr_ref,
    gated_ref,
    square_a_ref,
    square_b_ref,
    dot_a_ref,
    dot_b_ref,
    table_ref,
    gate_ref,
    y_ref,
    x_ref,
    xb_ref,
    state_ref,
    lag_ref,
    cum_row_ref,
    seg_row_ref,
    select_ref,
    dgate_ref,
    gy_ref,
    dx_ref,
    p_ref,
    grad_in_ref,
    grad_out_ref,
    sums_ref,
    gyb_ref,
    wide_ref,
    cross_ref,
    bias_ref,
    dcross_ref,
    inv_wide_ref,
    dot_wide_ref,
    inner_ref,
    mix_ref,
):
    step = pl.program_id(0)
    first = chunks[0]
    sources = chunks[-1] + 1
    left_half = lane_iota() < HEAD_DIM
    zero = jnp.zeros((LEN, LEN), jnp.bfloat16)
    spans = [(j, max(j, first), min(j + 3, sources)) for j in range(sources)]
    pairs = [(j, i) for j, start, stop in spans for i in range(start, stop)]

    @pl.when(step == 0)
    def _():
        for i in chunks:
            at = block(i - first)
            square = (square_a_ref[:, at] + square_b_ref[:, at]) / DSSM
            inv = lax.rsqrt(square + norm_eps)
            inv_wide_ref[at, :] = jnp.broadcast_to(inv, (LEN, LEN)).T
            dot = (dot_a_ref[:, at] + dot_b_ref[:, at]) / DSSM
            dot_wide_ref[at, :] = jnp.broadcast_to(dot, (LEN, LEN)).T
        p_ref[...] = jnp.zeros(p_ref.shape, jnp.float32)
        for h in range(heads):
            wide_ref[h] = jnp.broadcast_to(lag_ref[: sources * LEN, h : h + 1], (sources * LEN, LEN))
        for j, start, stop in spans:
            cross = three_dots(dot_nt, state_ref[block(j), :LEN], state_ref[start * LEN : stop * LEN, LEN:])
            for n, (j2, i) in enumerate(pairs):
                if j2 == j:
                    cross_ref[n] = cross[:, block(i - start)]
                    allowed = mask_st(seg_row_ref, j, i)
                    bias_ref[n] = jnp.where(allowed, 0.0, hidden_bias)
                    dcross_ref[n] = jnp.zeros((LEN, LEN), jnp.float32)

    tiles = (
        gmr_ref,
        gated_ref,
        table_ref.at[6:7],
        gate_ref,
        y_ref,
        x_ref,
        xb_ref,
        table_ref.at[5:6],
        dgate_ref,
        gy_ref,
        dx_ref,
        sums_ref,
    )

    def head_pair(
        hp,
        select,
        gmr_ref,
        gated_ref,
        gain_ref,
        gate_ref,
        y_ref,
        x_ref,
        xb_ref,
        skip_ref,
        dgate_ref,
        gy_ref,
        dx_ref,
        sums_ref,
    ):
        skip = skip_ref[...]
        gain = gain_ref[...]
        skip_sum = jnp.zeros((1, LEN), jnp.float32)
        gain_sum = jnp.zeros((1, LEN), jnp.float32)
        for i in chunks:
            at = block(i - first)
            inv = inv_wide_ref[at, :]
            unit = gated_ref[at, :] * inv
            rows_grad = gmr_ref[at, :]
            grad = inv * (rows_grad * gain - unit * dot_wide_ref[at, :])
            gate = gate_ref[at, :]
            sig = sigmoid(gate)
            y = y_ref[at, :]
            x = x_ref[at, :]
            gy = grad * (gate * sig)
            dgate_ref[at, :] = (grad * (y + skip * x) * (sig * (1.0 + gate * (1.0 - sig)))).astype(jnp.bfloat16)
            gyb = gy.astype(jnp.bfloat16)
            gy_ref[at, :] = gy
            gyb_ref[at, :] = gyb
            high, rest = two_terms(gyb.astype(jnp.float32) * y)
            p_ref[:, at] = p_ref[:, at] + dot_nt(select, high) + dot_nt(select, rest)
            skip_sum = skip_sum + jnp.sum(gy * x, axis=0, keepdims=True)
            gain_sum = gain_sum + jnp.sum(rows_grad * unit, axis=0, keepdims=True)
        sums_ref[0:1, :] = skip_sum
        sums_ref[1:2, :] = gain_sum

        for j, start, stop in spans:
            x_pair = xb_ref[block(j), :]
            x_both = jnp.concatenate([jnp.where(left_half, x_pair, zero), jnp.where(left_half, zero, x_pair)], axis=0)
            wide = (stop - start) * LEN
            gy_rows = gyb_ref[(start - first) * LEN : (stop - first) * LEN, :]
            inner_ref[:, :wide] = dot_nt(x_both, gy_rows)
            for n, (j2, i) in enumerate(pairs):
                if j2 != j:
                    continue
                grown = dcross_ref[n]
                for e in range(2):
                    spread = cum_row_ref[2 * hp + e, :, block(i)] - wide_ref[2 * hp + e, block(j), :]
                    decay = jnp.exp2(spread + bias_ref[n])
                    grown = grown + inner_ref[block(e), block(i - start)] * decay
                    mix_ref[block(e), block(i - start)] = (decay * cross_ref[n]).astype(jnp.bfloat16)
                dcross_ref[n] = grown
            both = dot_nn(mix_ref[:, :wide], gy_rows)
            dx_ref[block(j), :] = jnp.where(left_half, both[:LEN], both[LEN:])

    for sub in range(GROUP):
        head_pair(GROUP * step + sub, select_ref[:, block(sub)], *[t.at[:, block(sub)] for t in tiles])

    @pl.when(step == pl.num_programs(0) - 1)
    def _():
        grad_out = {i: jnp.zeros((LEN, LEN), jnp.float32) for i in chunks}
        for j in range(sources):
            grad_in = jnp.zeros((LEN, LEN), jnp.float32)
            for n, (j2, i) in enumerate(pairs):
                if j2 != j:
                    continue
                high, rest = two_terms(dcross_ref[n])
                out_high, out_rest = two_terms(state_ref[block(i), LEN:])
                in_high, in_rest = two_terms(state_ref[block(j), :LEN])
                grad_in = grad_in + dot_nn(high, out_high) + dot_nn(high, out_rest) + dot_nn(rest, out_high)
                grad_out[i] = grad_out[i] + dot_tn(high, in_high) + dot_tn(high, in_rest) + dot_tn(rest, in_high)
            grad_in_ref[block(j), :] = grad_in
        for i in chunks:
            grad_out_ref[block(i - first), :] = grad_out[i]


def conv_back(grad_ref, value_ref, keep_ref, taps, out_ref, sum_ref, lanes, blocks):
    totals = [jnp.zeros((1, LEN), jnp.float32) for _ in range(5)]
    for i in range(blocks):
        here = grad_ref[i * LEN : (i + 1) * LEN, :]
        grad = taps[3:4] * here
        totals[4] = totals[4] + jnp.sum(here, axis=0, keepdims=True)
        totals[3] = totals[3] + jnp.sum(here * value_ref[8 + i * LEN : 8 + (i + 1) * LEN, :], axis=0, keepdims=True)
        for lag in (1, 2, 3):
            ahead = grad_ref[i * LEN + lag : (i + 1) * LEN + lag, :]
            grad = grad + taps[3 - lag : 4 - lag] * (ahead * keep_ref[lag - 1, i * LEN + lag : (i + 1) * LEN + lag, :])
            moved = value_ref[8 + i * LEN - lag : 8 + (i + 1) * LEN - lag, :]
            masked = here * keep_ref[lag - 1, i * LEN : (i + 1) * LEN, :]
            totals[3 - lag] = totals[3 - lag] + jnp.sum(masked * moved, axis=0, keepdims=True)
        out_ref[block(i), lanes] = grad.astype(jnp.bfloat16)
    for tap in range(5):
        sum_ref[tap : tap + 1, lanes] = totals[tap]


def scan_end_kernel(
    heads,
    gy_a_ref,
    gy_b_ref,
    dx_a_ref,
    dx_b_ref,
    p_a_ref,
    p_b_ref,
    in_a_ref,
    in_b_ref,
    out_a_ref,
    out_b_ref,
    xb_ref,
    slope_ref,
    state_slope_ref,
    conv_ref,
    small_ref,
    step_row_ref,
    sig_row_ref,
    seg_row_ref,
    select_ref,
    table_ref,
    params_ref,
    dconv_ref,
    dstate_ref,
    dstep_ref,
    conv_sum_ref,
    state_sum_ref,
    step_sum_ref,
    grad_pad_ref,
    value_pad_ref,
    wide_ref,
    q_ref,
    flow_ref,
):
    step = pl.program_id(0)
    rows = conv_ref.shape[0]
    blocks = rows // LEN
    half = rows // 2
    count = flow_ref.shape[0]

    @pl.when(step == 0)
    def _():
        value_pad_ref[0:8, :] = jnp.zeros((8, LEN), jnp.float32)
        grad_pad_ref[rows : rows + 8, :] = jnp.zeros((8, LEN), jnp.float32)
        widen(seg_row_ref, wide_ref, value_pad_ref)
        value_pad_ref[0:8, :] = jnp.zeros((8, LEN), jnp.float32)
        q_ref[...] = jnp.zeros(q_ref.shape, jnp.float32)
        for c in range(2):
            if c == 0:
                grad_pad_ref[0:half, :] = (in_a_ref[...] + in_b_ref[0:half, :]) * state_slope_ref[0:half, block(c)]
                grad_pad_ref[half:rows, :] = in_b_ref[half:rows, :] * state_slope_ref[half:rows, block(c)]
            else:
                grad_pad_ref[0:half, :] = out_a_ref[...] * state_slope_ref[0:half, block(c)]
                grad_pad_ref[half:rows, :] = out_b_ref[...] * state_slope_ref[half:rows, block(c)]
            value_pad_ref[8 : rows + 8, :] = small_ref[:, block(c)]
            conv_back(
                grad_pad_ref,
                value_pad_ref,
                wide_ref,
                params_ref[8:12, block(c)],
                dstate_ref,
                state_sum_ref,
                block(c),
                blocks,
            )

    tiles = (
        gy_a_ref,
        gy_b_ref,
        dx_a_ref,
        dx_b_ref,
        xb_ref,
        slope_ref,
        conv_ref,
        table_ref.at[5:6],
        dconv_ref,
        conv_sum_ref,
    )

    def head_pair(
        select,
        taps,
        gy_a_ref,
        gy_b_ref,
        dx_a_ref,
        dx_b_ref,
        xb_ref,
        slope_ref,
        conv_ref,
        skip_ref,
        dconv_ref,
        conv_sum_ref,
    ):
        for j in range(blocks):
            dx = dx_b_ref[block(j), :]
            if j < blocks // 2:
                dx = dx + dx_a_ref[block(j), :]
                gy = gy_a_ref[block(j), :]
            else:
                gy = gy_b_ref[block(j - blocks // 2), :]
            high, rest = two_terms(dx * xb_ref[block(j), :].astype(jnp.float32))
            q_ref[:, block(j)] = q_ref[:, block(j)] + dot_nt(select, high) + dot_nt(select, rest)
            grad_pad_ref[block(j), :] = (dx + gy * skip_ref[...]) * slope_ref[block(j), :]
        value_pad_ref[8 : rows + 8, :] = conv_ref[...]
        conv_back(
            grad_pad_ref, value_pad_ref, wide_ref, taps, dconv_ref, conv_sum_ref, slice(0, LEN), blocks
        )

    for sub in range(GROUP):
        head_pair(select_ref[:, block(sub)], table_ref[0:4, block(sub)], *[t.at[:, block(sub)] for t in tiles])

    @pl.when(step == pl.num_programs(0) - 1)
    def _():
        q = q_ref[...]
        flow_ref[:, 0:half] = p_a_ref[...] - q[:, 0:half]
        flow_ref[:, half:rows] = p_b_ref[...] - q[:, half:rows]
        rate = turned(params_ref[14:15, :LEN])[:count]
        bias_total = jnp.zeros((count, LEN), jnp.float32)
        decay_total = jnp.zeros((count, LEN), jnp.float32)
        for j in range(blocks):
            log_grad = jnp.zeros((count, LEN), jnp.float32)
            for i in range(j, min(j + 3, blocks)):
                chosen = jnp.where(mask_st(seg_row_ref, j, i), 1.0, 0.0).astype(jnp.bfloat16)
                high, rest = two_terms(flow_ref[:, block(i)])
                log_grad = log_grad + dot_nt(high, chosen) + dot_nt(rest, chosen)
            step = step_row_ref[:, block(j)]
            grad_step = jnp.where(step > 1e-30, q[:, block(j)] / step, 0.0) + log_grad * rate
            grad_arg = grad_step * sig_row_ref[:, block(j)]
            bias_total = bias_total + grad_arg
            decay_total = decay_total + log_grad * step
            tall = jnp.concatenate([grad_arg, jnp.zeros((LEN - count, LEN), jnp.float32)], axis=0)
            dstep_ref[block(j), :] = tall.T.astype(jnp.bfloat16)
        step_sum_ref[0:count, :] = jnp.broadcast_to(jnp.sum(bias_total, axis=1, keepdims=True), (count, LEN))
        step_sum_ref[count : 2 * count, :] = jnp.broadcast_to(
            jnp.sum(decay_total * rate, axis=1, keepdims=True), (count, LEN)
        )


def whole_block(shape):
    return pl.BlockSpec(shape, lambda step: (0,) * len(shape), pipeline_mode=pl.Buffered(1))


def tile(rows, row_block=0, first=0):
    return pl.BlockSpec((rows, GROUP * LEN), lambda step: (row_block, first + step))


def small_block(rows, width):
    return pl.BlockSpec((rows, width), lambda step: (0, 2), pipeline_mode=pl.Buffered(1))


def call(kernel, steps, out_shape, out_specs, scratch, operands, specs, flops):
    return pl.pallas_call(
        kernel,
        grid=(steps,),
        out_shape=out_shape,
        in_specs=[s or whole_block(o.shape) for o, s in zip(operands, specs)],
        out_specs=[s or whole_block(o.shape) for o, s in zip(out_shape, out_specs)],
        scratch_shapes=scratch,
        compiler_params=pltpu.CompilerParams(vmem_limit_bytes=VMEM_BYTES),
        cost_estimate=pl.CostEstimate(flops=flops, bytes_accessed=0, transcendentals=0),
    )(*operands)


def f32(*shape):
    return jax.ShapeDtypeStruct(shape, jnp.float32)


def b16(*shape):
    return jax.ShapeDtypeStruct(shape, jnp.bfloat16)


HEAD_ROWS = 16
GROUP = 3
VMEM_BYTES = 60 * 1024 * 1024


def scan_prep(width, wide_in, cosine, sine, seg_row, params):
    rows = wide_in.shape[0]
    steps = width // LEN // GROUP
    outs = [
        f32(rows, width),
        b16(rows, width),
        f32(rows, width),
        f32(rows, 2 * LEN),
        f32(rows, 2 * LEN),
        f32(rows, LEN),
        f32(rows, LEN),
        f32(HEAD_ROWS, 1, rows),
        f32(HEAD_ROWS, 1, rows),
        f32(HEAD_ROWS, rows),
        f32(HEAD_ROWS, rows),
        b16(rows, 2 * LEN),
        b16(rows, LEN),
    ]
    scratch = [pltpu.VMEM((rows + 8, LEN), jnp.float32), pltpu.VMEM((3, rows + 8, LEN), jnp.float32)]
    operands = (wide_in, wide_in, cosine, sine, seg_row, params, params)
    specs = [tile(rows, 0, steps), small_block(rows, width), None, None, None, tile(16), None]
    return call(prep_kernel, steps, outs, [tile(rows)] * 3 + [None] * 10, scratch, operands, specs, 0 * 10**9)


def scan_forward(chunks, heads, wide_in, x, xb, *rest):
    width = x.shape[1]
    rows = LEN * len(chunks)
    at = chunks[0] // len(chunks)
    count = sum(min(i, 2) + 1 for i in chunks)
    outs = [f32(rows, width), f32(rows, width), f32(1, rows)]
    scratch = [
        pltpu.VMEM((heads, rows, LEN), jnp.float32),
        pltpu.VMEM((count, LEN, LEN), jnp.float32),
        pltpu.VMEM((count, LEN, LEN), jnp.float32),
        pltpu.VMEM((len(chunks), 2 * LEN, 3 * LEN), jnp.bfloat16),
        pltpu.VMEM((rows, LEN), jnp.float32),
    ]
    specs = [tile(rows, at), tile(rows, at), tile((chunks[-1] + 1) * LEN)] + [None] * (len(rest) - 1) + [tile(16)]
    kernel = functools.partial(scan_kernel, chunks, heads)
    operands = (wide_in, x, xb, *rest)
    return call(kernel, heads // 2 // GROUP, outs, [tile(rows), tile(rows), None], scratch, operands, specs, (0 if chunks[0] else 30) * 10**9)


def attention_forward(chunks, q, kv, seg_row):
    rows = LEN * len(chunks)
    outs = [b16(rows, q.shape[1]), f32(8, rows)]
    kernel = functools.partial(attention_kernel, chunks)
    return call(kernel, 1, outs, [None] * 2, [], (q, kv, seg_row), [None] * 3, 0 * 10**9)


def attention_backward(chunks, final, *operands):
    q = operands[0]
    rows = q.shape[0]
    partial = [f32(rows, LEN), f32(rows, LEN)]
    sums = [pltpu.VMEM((rows, LEN), jnp.float32)] * 2
    outs = [b16(LEN * len(chunks), q.shape[1])] + ([b16(rows, LEN)] if final else partial)
    scratch = (sums if final else []) + [
        pltpu.VMEM((rows, LEN), jnp.bfloat16),
        pltpu.VMEM((HEAD_DIM, rows), jnp.bfloat16),
    ]
    kernel = functools.partial(attention_back_kernel, chunks, final)
    return call(kernel, 1, outs, [None] * len(outs), scratch, operands, [None] * len(operands), (0 if chunks[0] else 30) * 10**9)


def scan_backward(chunks, heads, *operands):
    rows, width = operands[0].shape
    at = chunks[0] // len(chunks)
    sources = (chunks[-1] + 1) * LEN
    count = sum(min(i, 2) + 1 for i in chunks)
    outs = [
        b16(rows, width),
        f32(rows, width),
        f32(sources, width),
        f32(HEAD_ROWS, rows),
        f32(sources, LEN),
        f32(rows, LEN),
        f32(8, width),
    ]
    scratch = [
        pltpu.VMEM((rows, LEN), jnp.bfloat16),
        pltpu.VMEM((heads, sources, LEN), jnp.float32),
        pltpu.VMEM((count, LEN, LEN), jnp.float32),
        pltpu.VMEM((count, LEN, LEN), jnp.float32),
        pltpu.VMEM((count, LEN, LEN), jnp.float32),
        pltpu.VMEM((rows, LEN), jnp.float32),
        pltpu.VMEM((rows, LEN), jnp.float32),
        pltpu.VMEM((2 * LEN, 3 * LEN), jnp.float32),
        pltpu.VMEM((2 * LEN, 3 * LEN), jnp.bfloat16),
    ]
    specs = [tile(rows), tile(rows), None, None, None, None, tile(16), tile(rows, at), tile(rows), tile(rows, at), tile(sources)]
    specs += [None, None, None, None, tile(HEAD_ROWS)]
    out_specs = [tile(rows), tile(rows), tile(sources), None, None, None, tile(8)]
    kernel = functools.partial(scan_back_kernel, chunks, heads)
    return call(kernel, heads // 2 // GROUP, outs, out_specs, scratch, operands, specs, 30 * 10**9)


def scan_end(heads, *operands):
    rows, width = 2 * operands[0].shape[0], operands[0].shape[1]
    steps = heads // 2 // GROUP
    outs = [
        b16(rows, width),
        b16(rows, 2 * LEN),
        b16(rows, LEN),
        f32(8, width),
        f32(8, 2 * LEN),
        f32(2 * HEAD_ROWS, LEN),
    ]
    scratch = [
        pltpu.VMEM((rows + 8, LEN), jnp.float32),
        pltpu.VMEM((rows + 8, LEN), jnp.float32),
        pltpu.VMEM((3, rows + 8, LEN), jnp.float32),
        pltpu.VMEM((HEAD_ROWS, rows), jnp.float32),
        pltpu.VMEM((HEAD_ROWS, rows), jnp.float32),
    ]
    half = rows // 2
    specs = [tile(half), tile(half), tile(half), tile(rows)] + [None] * 6 + [tile(rows), tile(rows), None]
    specs += [tile(rows, 0, steps), small_block(rows, width), None, None, None, tile(HEAD_ROWS), tile(16), None]
    out_specs = [tile(rows), None, None, tile(8), None, None]
    kernel = functools.partial(scan_end_kernel, heads)
    return call(kernel, steps, outs, out_specs, scratch, operands, specs, 30 * 10**9)


def inverse_rms(rows):
    return lax.rsqrt(jnp.mean(rows * rows, axis=-1, keepdims=True) + norm_eps)


def ffn_kernel(
    tokens_ref,
    part_ref,
    far_ref,
    gain_ref,
    gate_ref,
    up_ref,
    down_ref,
    cotangent_ref,
    hidden_ref,
    normed_ref,
    activated_ref,
    grad_gate_ref,
    grad_up_ref,
    back_ref,
    out_ref,
):
    @pl.when(pl.program_id(0) == 0)
    def _():
        hidden = tokens_ref[...].astype(jnp.float32) + (part_ref[...] + far_ref[...])
        hidden_ref[...] = hidden
        normed_ref[...] = (hidden * inverse_rms(hidden) * gain_ref[...]).astype(jnp.bfloat16)
        back_ref[...] = jnp.zeros(back_ref.shape, jnp.float32)
        out_ref[...] = jnp.zeros(out_ref.shape, jnp.float32)

    normed = normed_ref[...]
    gate = dot_nn(normed, gate_ref[...])
    up = dot_nn(normed, up_ref[...])
    sig = sigmoid(gate)
    act = gate * sig
    activated = (act * up).astype(jnp.bfloat16)
    activated_ref[...] = activated
    grad = dot_nt(cotangent_ref[...], down_ref[...])
    grad_gate = (grad * up * (sig * (1.0 + gate * (1.0 - sig)))).astype(jnp.bfloat16)
    grad_up = (grad * act).astype(jnp.bfloat16)
    grad_gate_ref[...] = grad_gate
    grad_up_ref[...] = grad_up
    back_ref[...] = back_ref[...] + (dot_nt(grad_gate, gate_ref[...]) + dot_nt(grad_up, up_ref[...]))
    out_ref[...] = out_ref[...] + dot_nn(activated, down_ref[...])


def ffn(chunks, tokens, part, far, gain, gate, up, down, cotangent):
    rows, model_width = part.shape
    at = chunks[0] // len(chunks)
    hidden_width = gate.shape[1]
    steps = hidden_width // 256
    outs = [f32(rows, model_width), b16(rows, model_width)] + [b16(rows, hidden_width)] * 3
    outs += [f32(rows, model_width)] * 2
    rows_of = pl.BlockSpec((rows, model_width), lambda step: (at, 0), pipeline_mode=pl.Buffered(1))
    columns = pl.BlockSpec((model_width, 256), lambda step: (0, step))
    tiles = pl.BlockSpec((rows, 256), lambda step: (0, step))
    specs = [rows_of, None, None, None, columns, columns]
    specs += [pl.BlockSpec((256, model_width), lambda step: (step, 0)), rows_of]
    operands = (tokens, part, far, gain, gate, up, down, cotangent)
    return call(ffn_kernel, steps, outs, [None, None, tiles, tiles, tiles, None, None], [], operands, specs, 0 * 10**9)


def middle_kernel(
    hidden_ref,
    part_ref,
    far_ref,
    cotangent_ref,
    gain_ref,
    gated_ref,
    square_a_ref,
    square_b_ref,
    params_ref,
    mixer_out_ref,
    attn_out_ref,
    grad_hidden_ref,
    grad_branch_ref,
    grad_rows_ref,
    grad_attended_ref,
    dot_ref,
    gain_sum_ref,
):
    hidden = hidden_ref[...]
    inv = inverse_rms(hidden)
    unit = hidden * inv
    grad_normed = part_ref[...] + far_ref[...]
    gain_sum_ref[0:1, :] = jnp.sum(grad_normed * unit, axis=0, keepdims=True)
    grad_unit = grad_normed * gain_ref[...]
    inner = jnp.mean(grad_unit * unit, axis=-1, keepdims=True)
    grad_hidden = cotangent_ref[...].astype(jnp.float32) + inv * (grad_unit - unit * inner)
    grad_hidden_ref[...] = grad_hidden
    grad_branch = grad_hidden.astype(jnp.bfloat16)
    grad_branch_ref[...] = grad_branch
    grad_rows = dot_nt(grad_branch, mixer_out_ref[...])
    grad_rows_ref[...] = grad_rows
    grad_attended_ref[...] = dot_nt(grad_branch, attn_out_ref[...]).astype(jnp.bfloat16)
    total = jnp.sum(grad_rows * params_ref[6:7, :] * gated_ref[...], axis=-1, keepdims=True)
    for i in range(hidden.shape[0] // LEN):
        at = block(i)
        inv_gated = lax.rsqrt((square_a_ref[:, at] + square_b_ref[:, at]) / DSSM + norm_eps)
        dot_ref[0:1, at] = jnp.broadcast_to(total[at], (LEN, LEN)).T[0:1] * inv_gated


def middle(chunks, hidden, part, far, cotangent, gain, gated, square_a, square_b, gated_gain, mixer_out, attn_out):
    rows, model_width = part.shape
    at = chunks[0] // len(chunks)
    width, inner = mixer_out.shape[0], attn_out.shape[0]
    outs = [
        f32(rows, model_width),
        b16(rows, model_width),
        f32(rows, width),
        b16(rows, inner),
        f32(1, rows),
        f32(8, model_width),
    ]
    rows_of = pl.BlockSpec((rows, model_width), lambda step: (at, 0), pipeline_mode=pl.Buffered(1))
    specs = [None, None, None, rows_of] + [None] * 7
    operands = (hidden, part, far, cotangent, gain, gated, square_a, square_b, gated_gain, mixer_out, attn_out)
    return call(middle_kernel, 1, outs, [None] * 6, [], operands, specs, (0 if chunks[0] else 90) * 10**9)


def core_call(kernel, steps, core, out_shape, out_spec, scratch, operands, specs, flops, aliases=None):
    return pl.pallas_call(
        kernel,
        grid_spec=pltpu.PrefetchScalarGridSpec(
            num_scalar_prefetch=1, grid=(steps,), in_specs=specs, out_specs=out_spec, scratch_shapes=scratch
        ),
        out_shape=out_shape,
        compiler_params=pltpu.CompilerParams(vmem_limit_bytes=VMEM_BYTES),
        cost_estimate=pl.CostEstimate(flops=flops, bytes_accessed=0, transcendentals=0),
        input_output_aliases=aliases or {},
    )(core, *operands)


def clip_tile(rows, columns, first, last):
    return pl.BlockSpec((rows, columns), lambda step, core_ref: (0, jnp.clip(step - first, 0, last - first - 1)))


def ffn_weights_kernel(add, core_ref, *refs):
    refs = list(refs)
    normed_a, normed_b, act_a, act_b, gate_a, gate_b, up_a, up_b, cot_a, cot_b = refs[:10]
    far_ref = refs[10] if add else None
    out_ref, left_ref = refs[-2:]
    step = pl.program_id(0)
    third = pl.num_programs(0) // 3
    half = normed_a.shape[0]

    def turn(first, second):
        left_ref[:, :half] = first[...].T
        left_ref[:, half:] = second[...].T

    @pl.when(step == 0)
    def _():
        turn(normed_a, normed_b)

    @pl.when(step == 2 * third)
    def _():
        turn(act_a, act_b)

    def product(first, second):
        result = dot_nn(left_ref[:, :half], first[...]) + dot_nn(left_ref[:, half:], second[...])
        out_ref[...] = result + far_ref[...] if add else result

    @pl.when(step < third)
    def _():
        product(gate_a, gate_b)

    @pl.when((step >= third) & (step < 2 * third))
    def _():
        product(up_a, up_b)

    @pl.when(step >= 2 * third)
    def _():
        product(cot_a, cot_b)


def ffn_weights(core, far, normed_a, normed_b, act_a, act_b, gate_a, gate_b, up_a, up_b, cotangent):
    half, columns = normed_a.shape
    kept = columns // 2
    tile_width = 512
    third = columns // tile_width
    left = pl.BlockSpec((half, kept), lambda step, core_ref: (0, core_ref[0]), pipeline_mode=pl.Buffered(1))
    specs = [left] * 4 + [clip_tile(half, tile_width, 0, third)] * 2
    specs += [clip_tile(half, tile_width, third, 2 * third)] * 2

    def cot_rows(at):
        return pl.BlockSpec(
            (half, tile_width), lambda step, core_ref: (at, jnp.clip(step - 2 * third, 0, third - 1))
        )

    specs += [cot_rows(0), cot_rows(1)]
    out = pl.BlockSpec((kept, tile_width), lambda step, core_ref: (0, step))
    operands = [normed_a, normed_b, act_a, act_b, gate_a, gate_b, up_a, up_b, cotangent, cotangent]
    if far is not None:
        operands.append(far)
        specs.append(out)
    return core_call(
        functools.partial(ffn_weights_kernel, far is not None),
        3 * third,
        core,
        f32(kept, (3 if far is None else 4) * columns),
        out,
        [pltpu.VMEM((kept, 2 * half), jnp.bfloat16)],
        operands,
        specs,
        0 * 10**9,
    )


def outer_weights_kernel(add, core_ref, *refs):
    refs = list(refs)
    rows_a, rows_b, edge_a, edge_b, att_a, att_b, branch_a, branch_b = refs[:8]
    out_ref, left_ref = refs[-2:]
    half = rows_a.shape[0]
    middle_row = left_ref.shape[0] // 2

    @pl.when((pl.program_id(0) == 0) & (core_ref[0] == 0))
    def _():
        left_ref[:, :half] = rows_a[...].T
        left_ref[:, half:] = rows_b[...].T

    @pl.when((pl.program_id(0) == 0) & (core_ref[0] == 1))
    def _():
        left_ref[:middle_row, :half] = edge_a[...].T
        left_ref[:middle_row, half:] = edge_b[...].T
        left_ref[middle_row:, :half] = att_a[...].T
        left_ref[middle_row:, half:] = att_b[...].T

    result = dot_nn(left_ref[:, :half], branch_a[...]) + dot_nn(left_ref[:, half:], branch_b[...])
    out_ref[...] = result + refs[8][...] if add else result


def outer_weights(core, far, buffer, rows_a, rows_b, att_a, att_b, branch_a, branch_b):
    half, width = rows_a.shape
    model_width = branch_a.shape[1]
    kept = model_width // 2
    tile_width = 512
    steps = model_width // tile_width

    def fixed(shape, column=0):
        return pl.BlockSpec(shape, lambda step, core_ref: (0, column), pipeline_mode=pl.Buffered(1))

    specs = [fixed((half, kept))] * 2
    specs += [fixed((half, width - kept), kept // (width - kept))] * 2
    specs += [fixed(att_a.shape)] * 2 + [clip_tile(half, tile_width, 0, steps)] * 2
    operands = [rows_a, rows_b, rows_a, rows_b, att_a, att_b, branch_a, branch_b]
    out = pl.BlockSpec((kept, tile_width), lambda step, core_ref: (0, step))
    columns, aliases = model_width, {}
    if far is not None:
        operands += [far, buffer]
        specs += [out, pl.BlockSpec(memory_space=pl.ANY)]
        columns = buffer.shape[1]
        first = columns // tile_width - steps
        out = pl.BlockSpec((kept, tile_width), lambda step, core_ref: (0, first + step))
        aliases = {len(operands): 0}
    return core_call(
        functools.partial(outer_weights_kernel, far is not None),
        steps,
        core,
        f32(kept, columns),
        out,
        [pltpu.VMEM((kept, 2 * half), jnp.bfloat16)],
        operands,
        specs,
        0,
        aliases,
    )


PARTS = ((0, 3), (3, 5), (5, 7), (7, 9))


def small_table(rows_ref, gain_ref, state_ref, step_ref, sums_a, sums_b, conv_ref, ffn_a, ffn_b, select_ref):
    kept = rows_ref.shape[1] // 2
    heads = 12
    rows_ref[...] = jnp.zeros(rows_ref.shape, jnp.float32)
    width = conv_ref.shape[1]
    states = state_ref.shape[1]
    rows_ref[0:1, :] = gain_ref[0:1, :]
    for tap in range(4):
        rows_ref[1:2, tap * states : (tap + 1) * states] = state_ref[tap : tap + 1, :]
    rows_ref[2:3, :states] = state_ref[4:5, :]
    sums = sums_a[...] + sums_b[...]
    high, rest = two_terms(sums)
    by_head = dot_nt(high, select_ref[...]) + dot_nt(rest, select_ref[...])
    count = by_head.shape[1]
    rows_ref[3:4, 0:count] = step_ref[0:count, :].T[0:1, :]
    rows_ref[3:4, LEN : LEN + count] = step_ref[count : 2 * count, :].T[0:1, :]
    rows_ref[3:4, 2 * LEN : 2 * LEN + count] = by_head[0:1, :]
    rows_ref[4:9, :width] = conv_ref[0:5, :]
    rows_ref[9:10, :width] = sums[1:2, :]
    rows_ref[10:11, :] = ffn_a[0:1, :] + ffn_b[0:1, :]
    stacked = []
    for index in range(11):
        stacked += [rows_ref[index : index + 1, :kept], rows_ref[index : index + 1, kept:]]
    before = jnp.zeros((heads, kept), jnp.float32)
    behind = jnp.zeros((LEN - heads - len(stacked), kept), jnp.float32)
    return jnp.concatenate([before, *stacked, behind], axis=0).T


def mixer_weights_kernel(add, core_ref, *refs):
    refs = list(refs)
    normed_ref, gate_a, gate_b, conv_ref, query_a, query_b, state_ref, pair_ref, step_ref = refs[:9]
    far_ref = refs[9] if add else None
    outs = refs[19:27] if add else refs[9:10]
    left_ref, result_ref = refs[-3:-1] if add else refs[-2:]
    step = pl.program_id(0)
    half = gate_a.shape[0]

    @pl.when(step == 0)
    def _():
        left_ref[...] = normed_ref[...].T

    def two(first, second):
        result_ref[...] = dot_nn(left_ref[:, :half], first[...]) + dot_nn(left_ref[:, half:], second[...])

    @pl.when(step < 3)
    def _():
        two(gate_a, gate_b)

    @pl.when((step >= 3) & (step < 6))
    def _():
        result_ref[...] = dot_nn(left_ref[...], conv_ref[...])

    @pl.when(step == 6)
    def _():
        two(query_a, query_b)

    @pl.when(step == 7)
    def _():
        result_ref[...] = dot_nn(left_ref[...], state_ref[...])

    @pl.when(step == 8)
    def _():
        result_ref[:, :LEN] = dot_nn(left_ref[...], pair_ref[...])
        steps = dot_nn(left_ref[...], step_ref[...])
        result_ref[:, LEN:] = steps + small_table(refs[-1], *refs[10:19]) if add else steps

    if not add:
        outs[0][...] = result_ref[...]
        return
    result_ref[...] = result_ref[...] + far_ref[...]
    for k, (first, last) in enumerate(PARTS):

        @pl.when((step >= first) & (step < last))
        def _():
            for side in range(2):
                out_ref = outs[2 * k + side]
                for q in range(2):
                    index = core_ref[1 + 4 * k + 2 * side + q]
                    if k < 2:
                        for y in range(4):
                            start = pl.multiple_of((4 * y + index) * 32, 32)
                            out_ref[(2 * y + q) * 32 : (2 * y + q + 1) * 32, :] = result_ref[pl.ds(start, 32), :]
                    else:
                        start = pl.multiple_of(index * LEN, LEN)
                        out_ref[q * LEN : (q + 1) * LEN, :] = result_ref[pl.ds(start, LEN), :]


def mixer_weights(core, far, smalls, normed, gate_a, gate_b, conv, query_a, query_b, state, pair, step):
    half = gate_a.shape[0]
    rows, model_width = normed.shape
    kept = model_width // 2
    tile_width = 256
    steps = 9

    def fixed(shape, column=0):
        return pl.BlockSpec(shape, lambda step, core_ref: (0, column), pipeline_mode=pl.Buffered(1))

    specs = [pl.BlockSpec((rows, kept), lambda step, core_ref: (0, core_ref[0]), pipeline_mode=pl.Buffered(1))]
    specs += [clip_tile(half, tile_width, 0, 3)] * 2 + [clip_tile(rows, tile_width, 3, 6)]
    specs += [fixed(query_a.shape)] * 2 + [fixed(state.shape), fixed(pair.shape), fixed(step.shape)]
    operands = [normed, gate_a, gate_b, conv, query_a, query_b, state, pair, step]
    out = pl.BlockSpec((kept, tile_width), lambda step, core_ref: (0, step))
    shape = f32(kept, steps * tile_width)
    if far is not None:
        operands += [far, *smalls]
        specs += [out] + [fixed(v.shape) for v in smalls]
        out, shape = [], []
        for first, last in PARTS:
            out += [clip_tile(kept // 2, tile_width, first, last)] * 2
            shape += [f32(kept // 2, (last - first) * tile_width)] * 2
    return core_call(
        functools.partial(mixer_weights_kernel, far is not None),
        steps,
        core,
        shape,
        out,
        [pltpu.VMEM((kept, rows), jnp.bfloat16), pltpu.VMEM((kept, tile_width), jnp.float32)]
        + ([pltpu.VMEM((16, model_width), jnp.float32)] if far is not None else []),
        operands,
        specs,
        30 * 10**9,
    )


def normed_back_kernel(
    gate_a,
    gate_b,
    conv_ref,
    query_a,
    query_b,
    state_ref,
    pair_ref,
    step_ref,
    wide_ref,
    small_ref,
    tokens_ref,
    whole_ref,
    *refs,
):
    outs, sum_ref, inv_ref = refs[:-2], refs[-2], refs[-1]


    @pl.when(pl.program_id(0) == 0)
    def _():
        inv_ref[...] = jnp.broadcast_to(inverse_rms(whole_ref[...].astype(jnp.float32)), inv_ref.shape)

    half, width = gate_a.shape
    query_width = query_a.shape[1]
    gate_w, conv_w = wide_ref[:, :width], wide_ref[:, width:]
    state_w = small_ref[:, : 2 * LEN]
    query_w = small_ref[:, 2 * LEN : 2 * LEN + query_width]
    pair_w = small_ref[:, 2 * LEN + query_width : 3 * LEN + query_width]
    step_w = small_ref[:, 3 * LEN + query_width :]
    total = jnp.zeros((1, sum_ref.shape[1]), jnp.float32)
    for k, (gate, query) in enumerate(((gate_a, query_a), (gate_b, query_b))):
        at = slice(k * half, (k + 1) * half)
        grad = dot_nt(gate[...], gate_w) + dot_nt(conv_ref[at, :], conv_w) + dot_nt(query[...], query_w)
        grad = grad + dot_nt(state_ref[at, :], state_w) + dot_nt(pair_ref[at, :], pair_w) + dot_nt(step_ref[at, :], step_w)
        for n in range(half // LEN):
            outs[k * (half // LEN) + n][...] = grad[block(n)]
        unit = tokens_ref[at, :].astype(jnp.float32) * jnp.concatenate([inv_ref[at, :]] * 2, axis=1)
        total = total + jnp.sum(grad * unit, axis=0, keepdims=True)
    sum_ref[0:1, :] = total


def normed_back(gate_a, gate_b, conv, query_a, query_b, state, pair, step, wide_proj, small_proj, tokens):
    rows, model_width = tokens.shape
    tile_width = 256
    operands = (gate_a, gate_b, conv, query_a, query_b, state, pair, step, wide_proj, small_proj, tokens, tokens)

    def weights(count):
        return pl.BlockSpec((tile_width, count), lambda step: (step, 0))

    columns = pl.BlockSpec((rows, tile_width), lambda step: (0, step))
    specs = [None] * 8 + [weights(wide_proj.shape[1]), weights(small_proj.shape[1]), columns, None]
    count = rows // LEN
    out_specs = [pl.BlockSpec((LEN, tile_width), lambda step: (0, step))] * count
    out_specs += [pl.BlockSpec((8, tile_width), lambda step: (0, step))]
    outs = [f32(LEN, model_width)] * count + [f32(8, model_width)]
    return call(
        normed_back_kernel,
        model_width // tile_width,
        outs,
        out_specs,
        [pltpu.VMEM((rows, LEN), jnp.float32)],
        operands,
        specs, 30 * 10**9)


def project_kernel(wide_steps, tokens_ref, gain_ref, wide_ref, small_ref, out_ref, normed_ref):
    step = pl.program_id(0)

    @pl.when(step == 0)
    def _():
        tokens = tokens_ref[...].astype(jnp.float32)
        normed_ref[...] = (tokens * inverse_rms(tokens) * gain_ref[...]).astype(jnp.bfloat16)

    @pl.when(step < wide_steps)
    def _():
        out_ref[...] = dot_nn(normed_ref[...], wide_ref[...])

    @pl.when(step >= wide_steps)
    def _():
        out_ref[...] = dot_nn(normed_ref[...], small_ref[...])


def project(tokens, gain, wide_proj, small_proj):
    rows, model_width = tokens.shape
    count = 768
    wide_steps = wide_proj.shape[1] // count
    steps = wide_steps + small_proj.shape[1] // count
    outs = [f32(rows, steps * count), b16(rows, model_width)]
    wide = pl.BlockSpec((model_width, count), lambda step: (0, jnp.minimum(step, wide_steps - 1)))
    small = pl.BlockSpec((model_width, count), lambda step: (0, jnp.maximum(step - wide_steps, 0)))
    out = pl.BlockSpec((rows, count), lambda step: (0, step))
    operands = (tokens, gain, wide_proj, small_proj)
    kernel = functools.partial(project_kernel, wide_steps)
    return call(kernel, steps, outs, [out, None], [], operands, [None, None, wide, small], 0)


def unpack_kernel(
    block_ref,
    step_ref,
    input_gain_ref,
    state_kernel_ref,
    state_bias_ref,
    step_bias_ref,
    decay_ref,
    skip_ref,
    conv_kernel_ref,
    conv_bias_ref,
    gated_gain_ref,
    ffn_gain_ref,
    turned_ref,
):
    heads = step_ref.shape[0]
    for i in range(block_ref.shape[0] // LEN):
        turned_ref[:, block(i)] = block_ref[block(i), :].T

    half = block_ref.shape[0] // 2

    def row(index, count, start=0):
        pieces = []
        for side in range(2):
            low, high = max(start, side * half), min(start + count, (side + 1) * half)
            if low < high:
                column, at = heads + 2 * index + side, low - side * half
                mine = turned_ref[column : column + 1, at : at + high - low]
                pieces.append(mine + turned_ref[column : column + 1, half + at : half + at + high - low])
        return (pieces[0] if len(pieces) == 1 else jnp.concatenate(pieces, axis=1))[0]

    step_ref[...] = turned_ref[0:heads, :]
    input_gain_ref[...] = row(0, input_gain_ref.shape[0])
    columns = state_kernel_ref.shape[1]
    for tap in range(4):
        state_kernel_ref[tap, :] = row(1, columns, tap * columns)
        conv_kernel_ref[tap, :] = row(4 + tap, conv_kernel_ref.shape[1])
    state_bias_ref[...] = row(2, columns)
    step_bias_ref[...] = row(3, heads)
    decay_ref[...] = row(3, heads, LEN)
    skip_ref[...] = row(3, heads, 2 * LEN)
    conv_bias_ref[...] = row(8, conv_bias_ref.shape[0])
    gated_gain_ref[...] = row(9, gated_gain_ref.shape[0])
    ffn_gain_ref[...] = row(10, ffn_gain_ref.shape[0])


def unpack(heads, width, states, values):
    rows = values.shape[0]
    outs = [f32(heads, rows), f32(rows), f32(4, states), f32(states), f32(heads), f32(heads), f32(heads)]
    outs += [f32(4, width), f32(width), f32(width), f32(rows)]
    scratch = [pltpu.VMEM((LEN, rows), jnp.float32)]
    return call(unpack_kernel, 1, outs, [None] * len(outs), scratch, (values,), [None], 0)


def assemble_kernel(source, mixer_proj_ref, query_ref, pair_ref, state_ref, step_ref):
    width = mixer_proj_ref.shape[2]
    start = 0
    mixer_proj_ref[:, 0, :] = source[:, start : start + width]
    start += width
    mixer_proj_ref[:, 1, :] = source[:, start : start + width]
    start += width
    query_ref[...] = source[:, start : start + query_ref.shape[1]]
    start += query_ref.shape[1]
    state_ref[...] = source[:, start : start + 2 * LEN]
    start += 2 * LEN
    pair_ref[:, 0, :] = source[:, start : start + LEN]
    step_ref[...] = source[:, start + LEN :]


def assemble(values, width, query_width):
    rows, columns = values.shape

    def plain(count):
        return pl.BlockSpec((LEN, count), lambda at: (at, 0))

    out_specs = [
        pl.BlockSpec((LEN, 2, width), lambda at: (at, 0, 0)),
        plain(query_width),
        pl.BlockSpec((LEN, 1, LEN), lambda at: (at, 0, 0)),
        plain(2 * LEN),
        plain(LEN),
    ]
    out_shape = [
        f32(rows, 2, width),
        f32(rows, query_width),
        f32(rows, 1, LEN),
        f32(rows, 2 * LEN),
        f32(rows, LEN),
    ]
    return call(assemble_kernel, rows // LEN, out_shape, out_specs, [], (values,), [plain(columns)], 0)


LINKS = {
    "A": [(0, 1), (1, 0), (2, 3), (3, 2)],
    "B": [(1, 2), (2, 1), (3, 0), (0, 3)],
}
ORDERS = (
    (("x", "A"), ("x", "B"), ("y", "A"), ("y", "B")),
    (("x", "B"), ("y", "A"), ("y", "B"), ("x", "A")),
    (("y", "A"), ("y", "B"), ("x", "A"), ("x", "B")),
    (("y", "B"), ("x", "A"), ("x", "B"), ("y", "A")),
)
AXIS = {"y": 0, "x": 1}


def take(values, index, axis):
    return lax.dynamic_slice_in_dim(values, index, 1, axis)


def halves(values, name, link, again):
    place, axis = lax.axis_index(name), AXIS[name]
    if again:
        index = place // 2 if link == "B" else place % 2
        return take(values, index, axis), take(values, 1 - index, axis)
    if link == "B":
        side = place // 2
        kept = lax.dynamic_slice_in_dim(values, 2 * side, 2, axis)
        return kept, lax.dynamic_slice_in_dim(values, 2 - 2 * side, 2, axis)
    side = ((place + 1) // 2) % 2
    kept = jnp.concatenate([take(values, side, axis), take(values, 3 - side, axis)], axis)
    return kept, jnp.concatenate([take(values, 1 - side, axis), take(values, 2 + side, axis)], axis)


def reduce_rows(pairs, steps):
    kept, sent, parts = [], [], pairs
    if steps[0] == 0:
        for k, (stays, goes) in enumerate(pairs):
            shape = (4, 2, 32, stays.shape[1]) if ORDERS[k][0][0] == "x" else (2, 4, 32, stays.shape[1])
            kept.append(stays.reshape(shape))
            sent.append(goes.reshape(shape))
    for step in steps:
        if step:
            kept, sent = [], []
            for k in range(4):
                name, link = ORDERS[k][step]
                again = name in [n for n, _ in ORDERS[k][:step]]
                stays, goes = halves(parts[k], name, link, again)
                kept.append(stays)
                sent.append(goes)
        sent = lax.optimization_barrier(tuple(sent))
        come = [lax.ppermute(sent[k], ORDERS[k][step][0], LINKS[ORDERS[k][step][1]]) for k in range(4)]
        come = lax.optimization_barrier(tuple(come))
        parts = [stays + more for stays, more in zip(kept, come)]
    return parts


def rope_tables(rows):
    half_size = HEAD_DIM // 2
    inverse = np.float32(rope_base) ** (-(2.0 * np.arange(half_size, dtype=np.float32)) / HEAD_DIM)
    angles = np.arange(rows, dtype=np.float32)[:, None] * inverse.astype(np.float32)[None, :]
    cosine, sine = np.cos(angles), np.sin(angles)
    return (
        np.concatenate([cosine] * 4, axis=1).astype(np.float32),
        np.concatenate([-sine, sine, -sine, sine], axis=1).astype(np.float32),
    )


def norm_backward(grad_unit, unit_rows, inv_rms):
    return inv_rms * (grad_unit - unit_rows * jnp.mean(grad_unit * unit_rows, axis=-1, keepdims=True))


def dot32(left, right):
    return jnp.dot(left, right, preferred_element_type=jnp.float32)


def after(value, *others):
    return lax.optimization_barrier((value, *others))[0]


def swap(values, name):
    return lax.ppermute(values, name, PAIR)


def exchange(values, name):
    return values + swap(values, name)


def core_rows(values, index):
    half = values.shape[1] // 2
    return lax.dynamic_slice_in_dim(values, index * half, half, 1)


def on_device(
    layer_input,
    segments,
    input_gain,
    mixer_proj,
    state_proj,
    step_proj,
    step_bias,
    decay_log,
    skip_gain,
    conv_kernel,
    conv_bias,
    state_kernel,
    state_bias,
    gated_gain,
    mixer_out,
    query_proj,
    key_value_weight,
    attn_out,
    ffn_gain,
    ffn_gate,
    ffn_up,
    ffn_down,
    cotangent,
):
    rows, model_width = layer_input.shape
    width = mixer_proj.shape[2]
    heads = step_proj.shape[1]
    state_size = state_proj.shape[1] // 2
    query_width = query_proj.shape[1]
    pair_width = key_value_weight.shape[2]
    place = lax.axis_index("core")
    zh = lax.axis_index("zh")
    core = place.astype(jnp.int32).reshape(1)
    far_core = 1 - core
    cosine, sine = rope_tables(rows)
    select = np.arange(HEAD_ROWS)[:, None] == np.arange(width)[None, :] // HEAD_DIM
    select = jnp.asarray(select.astype(np.float32)).astype(jnp.bfloat16)
    seg_row = segments
    pad_heads = ((0, 0), (0, LEN - heads))

    def padded(values):
        return jnp.pad(values, ((0, 0), (0, width - values.shape[1])))

    params = jnp.concatenate(
        [
            conv_kernel,
            conv_bias[None, :],
            jnp.repeat(skip_gain, HEAD_DIM)[None, :],
            gated_gain[None, :],
            jnp.zeros((1, width), jnp.float32),
            padded(state_kernel),
            padded(state_bias[None, :]),
            padded(step_bias[None, :]),
            padded(-jnp.exp(decay_log)[None, :]),
            jnp.zeros((1, width), jnp.float32),
        ],
        axis=0,
    )
    wide_proj = mixer_proj.reshape(model_width, 2 * width)
    small_proj = jnp.concatenate(
        [
            state_proj,
            query_proj,
            key_value_weight.reshape(model_width, pair_width),
            jnp.pad(step_proj, pad_heads),
        ],
        axis=1,
    )
    tokens = layer_input.astype(jnp.float32)
    wide_in, normed_input = project(layer_input, input_gain[None, :], wide_proj, small_proj)
    x, xb, slope, state, state_slope, cum, lag, cum_row, lag_row, step_row, sig_row, queries, pairs = scan_prep(
        width,
        wide_in,
        cosine,
        sine,
        seg_row,
        params,
    )

    blocks = rows // LEN
    late = tuple(range(blocks // 2, blocks))
    early = tuple(range(blocks // 2))
    half = {}
    ready = None
    for chunks in (late, early):
        h = {"span": slice(chunks[0] * LEN, (chunks[-1] + 1) * LEN)}
        lag_now = lag_row if ready is None else after(lag_row, ready)
        h["y"], h["gated"], h["square"] = scan_forward(
            chunks, heads, wide_in, x, xb, state, cum, lag_now, seg_row, params
        )
        h["square_far"] = swap(h["square"], "tensor")
        h["attended"], h["lse"] = attention_forward(chunks, after(queries, h["square"]), pairs, seg_row)
        tied = (h["lse"],) if chunks == late else (h["lse"], front_far)
        squares = h["square"] + after(h["square_far"], *tied)
        h["inv_gated"] = lax.rsqrt(squares.reshape(-1, 1) / DSSM + norm_eps)
        h["mixer_rows"] = (h["gated"] * h["inv_gated"] * gated_gain).astype(jnp.bfloat16)
        h["part"] = dot32(h["mixer_rows"], mixer_out) + dot32(h["attended"], attn_out)
        if chunks == late:
            front_far = swap(h["part"][:LEN], "tensor")
            ready = h["part"]
        else:
            rest_far = swap(after(half[late]["part"][LEN:], squares), "tensor")
            half[late]["branch_far"] = jnp.concatenate([front_far, rest_far], axis=0)
            h["branch_far"] = swap(after(h["part"], rest_far), "tensor")
        half[chunks] = h

    a, b = half[early], half[late]
    gain_ffn = ffn_gain[None, :]
    names = ("hidden", "normed", "activated", "grad_gate_rows", "grad_up_rows", "back", "down")
    for chunks in (late, early):
        h = half[chunks]
        far = h["branch_far"] if chunks == late else after(h["branch_far"], b["back"])
        operands = (layer_input, h["part"], far, gain_ffn, ffn_gate, ffn_up, ffn_down, cotangent)
        h.update(zip(names, ffn(chunks, *operands)))
        h["back_far"] = swap(h["back"], "tensor")

    for chunks in (late, early):
        h = half[chunks]
        far = h["back_far"] if chunks == late else after(h["back_far"], first)
        h["grad_hidden"], h["grad_branch"], h["grad_rows"], grad_attended, h["dot"], h["gain_sum"] = middle(
            chunks,
            h["hidden"],
            h["back"],
            far,
            cotangent,
            gain_ffn,
            h["gated"],
            h["square"],
            h["square_far"],
            params,
            mixer_out,
            attn_out,
        )
        if chunks == early:
            dots = jnp.concatenate([a["dot"], b["dot"]], axis=1)
            outer = (a["mixer_rows"], b["mixer_rows"], a["attended"], b["attended"])
            outer += (a["grad_branch"], b["grad_branch"])
            outer_sent = outer_weights(far_core, None, None, *outer)
            outer_far = swap(outer_sent, "core")
            first = ffn_weights(core, after(first_far, outer_sent), *sides)
            dots_far = swap(after(dots, first), "tensor")
            first = outer_weights(core, outer_far, first, *outer)
            first_sum = lax.psum_scatter(first, ("y", "x"), scatter_dimension=0, tiled=True)
            grad_attended = after(grad_attended, first)
        operands = (queries, pairs, grad_attended, h["lse"], seg_row, cosine, sine)
        if chunks == late:
            h["grad_queries"], grad_keys, grad_values = attention_backward(chunks, False, *operands)
            sides = (after(a["normed"], grad_keys), b["normed"], a["activated"], b["activated"])
            sides += (a["grad_gate_rows"], b["grad_gate_rows"], a["grad_up_rows"], b["grad_up_rows"], cotangent)
            first = ffn_weights(far_core, None, *sides)
            first_far = swap(first, "core")
        else:
            h["grad_queries"], grad_pairs = attention_backward(chunks, True, *operands, grad_keys, grad_values)
    dots_far = after(dots_far, grad_pairs)
    for chunks in (late, early):
        h = half[chunks]
        h["grad_gate"], h["gy"], h["dx"], h["p"], h["grad_in"], h["grad_out"], h["sums"] = scan_backward(
            chunks,
            heads,
            h["grad_rows"],
            h["gated"],
            h["square"],
            h["square_far"],
            h["dot"],
            dots_far[:, h["span"]],
            params,
            wide_in,
            h["y"],
            x,
            xb,
            state,
            lag,
            cum_row,
            seg_row,
            select,
        )
    pieces = [b["down"][:LEN], b["down"][LEN:], a["down"][:LEN], a["down"][LEN:]]
    pieces_far = [swap(after(piece, dots_far), "tensor") for piece in pieces[:3]]
    down = jnp.concatenate([a["down"], b["down"]], axis=0)
    ends = []
    for name in ("gy", "dx", "p", "grad_in", "grad_out"):
        ends += [a[name], b[name]]
    grad_conv, grad_state, grad_step, conv_sum, state_sum, step_sum = scan_end(
        heads,
        *ends,
        xb,
        slope,
        state_slope,
        wide_in,
        wide_in,
        step_row,
        sig_row,
        seg_row,
        select,
        params,
        params,
    )

    grads = (a["grad_gate"], b["grad_gate"], grad_conv, a["grad_queries"], b["grad_queries"])
    grads += (grad_state, grad_pairs, grad_step)
    tied = after(normed_input, pieces_far[0], pieces_far[1])
    second_far = swap(mixer_weights(far_core, None, None, tied, *grads), "core")
    *partial_normed, input_gain_sum = normed_back(*grads, wide_proj, small_proj, layer_input)

    smalls = (input_gain_sum, state_sum, step_sum, a["sums"], b["sums"], conv_sum, a["gain_sum"], b["gain_sum"], select)
    shared_end = heads + 6
    spots = [core]
    for name, link in [order[0] for order in ORDERS]:
        at = lax.axis_index(name).astype(jnp.int32)
        side = ((at + 1) // 2) % 2 if link == "A" else at // 2
        spots.append(jnp.stack([side, 3 - side, 1 - side, 2 + side] if link == "A" else [2 * side, 2 * side + 1, 2 - 2 * side, 3 - 2 * side]))
    second = mixer_weights(jnp.concatenate(spots), after(second_far, pieces_far[2]), smalls, normed_input, *grads)
    second = list(second)
    at_state = 2 * width + query_width
    normed_far = [swap(piece, "tensor") for piece in partial_normed]
    second[1] = after(second[1], normed_far[0])
    parts = reduce_rows([(second[2 * k], second[2 * k + 1]) for k in range(4)], (0,))
    parts[0] = after(parts[0], normed_far[1])
    first_own = exchange(after(first_sum, parts[0]), "zh")
    first_all = lax.all_gather(first_own, ("core", "y", "x"), axis=0, tiled=True)
    parts = reduce_rows(parts, (1,))
    parts[0] = after(parts[0], normed_far[2])
    parts = reduce_rows(parts, (2,))
    parts[0] = after(parts[0], normed_far[3])
    parts = reduce_rows(parts, (3,))
    second = jnp.concatenate([p.reshape(32, -1) for p in parts], axis=1)
    both = second[:, at_state:]
    lane = np.arange(both.shape[1])
    in_table = lane - 2 * state_size - pair_width
    is_shared = (lane < 2 * state_size) | ((in_table >= heads) & (in_table < shared_end))
    diagonal = [(0, 3), (3, 0), (1, 2), (2, 1)]
    more = swap(both, "tensor") + lax.ppermute(both, ("zh", "tensor"), diagonal)
    second = exchange(second, "zh")
    summed = second[:, at_state:] + jnp.where(is_shared[None, :], more, 0.0)
    second = jnp.concatenate([second[:, :at_state], summed], axis=1)
    second = after(second, first_all)
    pieces_far.append(swap(after(pieces[3], second), "tensor"))
    second = lax.all_gather(second, ("core", "y", "x"), axis=0, tiled=True)
    grad_mixer_proj, grad_query_proj, grad_keyval, grad_state_proj, step_block = assemble(second, width, query_width)

    def whole(name):
        return jnp.concatenate([a[name], b[name]], axis=0)

    grad_hidden = whole("grad_hidden")
    grad_normed = jnp.concatenate(partial_normed, axis=0) + jnp.concatenate(normed_far, axis=0)
    inv_rms_in = inverse_rms(tokens)
    unit_in = tokens * inv_rms_in
    input_grad = grad_hidden + norm_backward(grad_normed * input_gain, unit_in, inv_rms_in)
    down_far = jnp.concatenate([pieces_far[2], pieces_far[3], pieces_far[0], pieces_far[1]], axis=0)
    layer_output = (whole("hidden") + (down + down_far)).astype(jnp.bfloat16)

    smalls = unpack(heads, width, 2 * state_size, step_block)
    return (
        layer_output,
        input_grad,
        smalls[1],
        grad_mixer_proj,
        grad_state_proj,
        smalls[0].T,
        smalls[4],
        smalls[5],
        smalls[6],
        smalls[7],
        smalls[8],
        smalls[2],
        smalls[3],
        smalls[9],
        first_all[:width, 3 * model_width :],
        grad_query_proj,
        grad_keyval,
        first_all[width:, 3 * model_width :],
        smalls[10],
        first_all[:, :model_width],
        first_all[:, model_width : 2 * model_width],
        first_all[:, 2 * model_width : 3 * model_width],
    )


def solution(mesh):
    dp, whole_spec, columns = P(DP, None), P(), P(None, "tensor")
    per_channel, middle = P("tensor"), P(None, "tensor", None)
    last, by_rows = P(None, None, "tensor"), P("tensor", None)
    weights = (
        whole_spec,
        last,
        whole_spec,
        columns,
        per_channel,
        per_channel,
        per_channel,
        columns,
        per_channel,
        whole_spec,
        whole_spec,
        per_channel,
        by_rows,
        columns,
        middle,
        by_rows,
        whole_spec,
        columns,
        columns,
        by_rows,
    )
    mesh = jax.sharding.Mesh(mesh.devices.reshape(4, 2, 4, 2, 2), (*DP, "tensor"))
    return jax.shard_map(
        on_device, mesh=mesh, in_specs=(dp, dp, *weights, dp), out_specs=(dp, dp, *weights), check_vma=False
    )
```

```python
import functools

import jax
import jax.numpy as jnp
import numpy as np
from jax import lax
from jax.experimental import pallas as pl
from jax.experimental.pallas import tpu as pltpu
from jax.sharding import PartitionSpec as P

HEAD_DIM = 64
DSSM = 1536
DP = ("y", "zh", "x", "core")
PAIR = [(0, 1), (1, 0)]
LOG2E = 1.4426950408889634
hidden_bias = -1e30
norm_eps = 1e-05
rope_base = 10000.0
LEN = 128


def dot_nn(left, right):
    return lax.dot_general(
        left, right, (((1,), (0,)), ((), ())), preferred_element_type=jnp.float32
    )


def dot_nt(left, right):
    return lax.dot_general(
        left, right, (((1,), (1,)), ((), ())), preferred_element_type=jnp.float32
    )


def dot_tn(left, right):
    return lax.dot_general(
        left, right, (((0,), (0,)), ((), ())), preferred_element_type=jnp.float32
    )


def two_terms(v):
    high = v.astype(jnp.bfloat16)
    return high, (v - high.astype(jnp.float32)).astype(jnp.bfloat16)


def three_dots(dot, left, right):
    left_high, left_low = two_terms(left)
    right_high, right_low = two_terms(right)
    return dot(left_high, right_high) + dot(left_high, right_low) + dot(left_low, right_high)


def sigmoid(v):
    return 1.0 / (1.0 + jnp.exp(-v))


def block(index):
    return slice(index * LEN, (index + 1) * LEN)


def lane_iota(rows=LEN):
    return lax.broadcasted_iota(jnp.int32, (rows, LEN), 1)


def turned(row):
    return jnp.broadcast_to(row, (LEN, LEN)).T


def mask_ts(seg_row, i, j):
    same = turned(seg_row[:, block(i)].astype(jnp.float32)) == seg_row[:, block(j)].astype(jnp.float32)
    if i != j:
        return same
    down = lax.broadcasted_iota(jnp.int32, (LEN, LEN), 0)
    return same & (down >= lane_iota())


def mask_st(seg_row, j, i):
    same = turned(seg_row[:, block(j)].astype(jnp.float32)) == seg_row[:, block(i)].astype(jnp.float32)
    if i != j:
        return same
    down = lax.broadcasted_iota(jnp.int32, (LEN, LEN), 0)
    return same & (down <= lane_iota())


def conv_rows(pad_ref, keep_ref, kernel, bias, start, lanes):
    summed = bias + kernel[3:4] * pad_ref[8 + start : 8 + start + LEN, lanes]
    for lag in (1, 2, 3):
        moved = pad_ref[8 + start - lag : 8 + start - lag + LEN, lanes]
        summed = summed + kernel[3 - lag : 4 - lag] * (moved * keep_ref[lag - 1, start : start + LEN, :])
    return summed


def widen(seg_row_ref, wide_ref, pad_ref):
    rows = seg_row_ref.shape[1]
    pad_ref[0:8, :] = jnp.full((8, LEN), -1.0, jnp.float32)
    for i in range(rows // LEN):
        pad_ref[8 + i * LEN : 8 + (i + 1) * LEN, :] = turned(seg_row_ref[:, block(i)].astype(jnp.float32))
    for lag in (1, 2, 3):
        same = pad_ref[8 : rows + 8, :] == pad_ref[8 - lag : rows + 8 - lag, :]
        wide_ref[lag - 1, 0:rows, :] = jnp.where(same, 1.0, 0.0)
        wide_ref[lag - 1, rows : rows + 8, :] = jnp.zeros((8, LEN), jnp.float32)


def prep_kernel(
    conv_ref,
    small_ref,
    cos_ref,
    sin_ref,
    seg_row_ref,
    table_ref,
    params_ref,
    x_ref,
    xb_ref,
    slope_ref,
    state_ref,
    state_slope_ref,
    cum_ref,
    lag_ref,
    cum_row_ref,
    lag_row_ref,
    step_row_ref,
    sig_row_ref,
    q_ref,
    kv_ref,
    pad_ref,
    wide_ref,
):
    rows = conv_ref.shape[0]
    blocks = rows // LEN

    @pl.when(pl.program_id(0) == 0)
    def _():
        widen(seg_row_ref, wide_ref, pad_ref)
        pad_ref[0:8, :] = jnp.zeros((8, LEN), jnp.float32)
        for c in range(2):
            pad_ref[8 : rows + 8, :] = small_ref[:, block(c)]
            for i in range(blocks):
                pre = conv_rows(
                    pad_ref, wide_ref, params_ref[8:12, block(c)], params_ref[12:13, block(c)], i * LEN, slice(0, LEN)
                )
                sig = sigmoid(pre)
                state_ref[block(i), block(c)] = pre * sig
                state_slope_ref[block(i), block(c)] = sig * (1.0 + pre * (1.0 - sig))

    @pl.when(pl.program_id(0) == 1)
    def _():
        down = lax.broadcasted_iota(jnp.int32, (LEN, LEN), 0)
        lower = jnp.where(down >= lane_iota(), 1.0, 0.0).astype(jnp.bfloat16)
        left_half = lane_iota() < HEAD_DIM
        carry = jnp.zeros((1, LEN), jnp.float32)
        heads = cum_row_ref.shape[0]
        for i in range(blocks):
            argument = small_ref[block(i), block(5)] + params_ref[13:14, :LEN]
            tail = jnp.exp(-jnp.abs(argument))
            grown = jnp.where(tail < 1e-3, tail - 0.5 * tail * tail, jnp.log(1.0 + tail))
            step = jnp.maximum(argument, 0.0) + grown
            scaled = step * params_ref[14:15, :LEN] * LOG2E
            first, rest = two_terms(scaled)
            last = scaled - first.astype(jnp.float32) - rest.astype(jnp.float32)
            cum = dot_nn(lower, first) + dot_nn(lower, rest) + dot_nn(lower, last.astype(jnp.bfloat16)) + carry
            carry = cum[LEN - 1 : LEN, :]
            lag = cum - jnp.log(step) * LOG2E
            cum_ref[block(i), :] = cum
            lag_ref[block(i), :] = lag
            cum_t, lag_t = cum.T, lag.T
            step_row_ref[:, block(i)] = step.T[:heads]
            sig_row_ref[:, block(i)] = sigmoid(argument).T[:heads]
            for h in range(heads):
                cum_row_ref[h, :, block(i)] = cum_t[h : h + 1]
                lag_row_ref[h, :, block(i)] = lag_t[h : h + 1]
            cosine, sine = cos_ref[block(i), :], sin_ref[block(i), :]
            kv = small_ref[block(i), block(4)]
            kv_ref[block(i), :] = jnp.where(left_half, rotate_tile(kv, cosine, sine), kv).astype(jnp.bfloat16)
            for p in range(q_ref.shape[1] // LEN):
                q_ref[block(i), block(p)] = rotate_tile(small_ref[block(i), block(2 + p)], cosine, sine).astype(
                    jnp.bfloat16
                )

    for sub in range(GROUP):
        lanes = block(sub)
        pad_ref[8 : rows + 8, :] = conv_ref[:, lanes]
        for i in range(blocks):
            pre = conv_rows(pad_ref, wide_ref, table_ref[0:4, lanes], table_ref[4:5, lanes], i * LEN, slice(0, LEN))
            sig = sigmoid(pre)
            x = pre * sig
            x_ref[block(i), lanes] = x
            xb_ref[block(i), lanes] = x.astype(jnp.bfloat16)
            slope_ref[block(i), lanes] = sig * (1.0 + pre * (1.0 - sig))


def rotate_tile(v, cosine, sine):
    first = lax.rem(lane_iota(v.shape[0]), HEAD_DIM) < HEAD_DIM // 2
    swapped = jnp.where(first, pltpu.roll(v, LEN - HEAD_DIM // 2, 1), pltpu.roll(v, HEAD_DIM // 2, 1))
    return v * cosine + swapped * sine


def scan_kernel(
    chunks,
    heads,
    gate_ref,
    x_ref,
    xb_ref,
    state_ref,
    cum_ref,
    lag_row_ref,
    seg_row_ref,
    table_ref,
    y_ref,
    gated_ref,
    row_ref,
    wide_ref,
    cross_ref,
    bias_ref,
    mix_ref,
    square_ref,
):
    step = pl.program_id(0)
    first = chunks[0]
    pairs = [(i, j) for i in chunks for j in range(max(0, i - 2), i + 1)]
    left_half = lane_iota() < HEAD_DIM

    @pl.when(step == 0)
    def _():
        for h in range(heads):
            for i in chunks:
                wide_ref[h, block(i - first), :] = jnp.broadcast_to(cum_ref[block(i), h : h + 1], (LEN, LEN))
        for i in chunks:
            low = max(0, i - 2)
            cross = three_dots(dot_nt, state_ref[block(i), LEN:], state_ref[low * LEN : (i + 1) * LEN, :LEN])
            for n, (i2, j) in enumerate(pairs):
                if i2 == i:
                    cross_ref[n] = cross[:, block(j - low)]
                    allowed = mask_ts(seg_row_ref, i, j)
                    bias_ref[n] = jnp.where(allowed, 0.0, hidden_bias)
        square_ref[...] = jnp.zeros(square_ref.shape, jnp.float32)

    tiles = (gate_ref, x_ref, xb_ref, table_ref.at[5:6], y_ref, gated_ref)

    def head_pair(hp, gate_ref, x_ref, xb_ref, skip_ref, y_ref, gated_ref):
        for i in chunks:
            at = block(i - first)
            low = max(0, i - 2)
            for n, (i2, j) in enumerate(pairs):
                if i2 != i:
                    continue
                for e in range(2):
                    spread = wide_ref[2 * hp + e, at, :] - lag_row_ref[2 * hp + e, :, block(j)]
                    decay = jnp.exp2(spread + bias_ref[n])
                    mix_ref[i - first, block(e), block(j - low)] = (decay * cross_ref[n]).astype(jnp.bfloat16)
            both = dot_nn(mix_ref[i - first, :, : (i + 1 - low) * LEN], xb_ref[low * LEN : (i + 1) * LEN, :])
            y = jnp.where(left_half, both[:LEN], both[LEN:])
            y_ref[at, :] = y
            gate = gate_ref[at, :]
            gated = (y + skip_ref[...] * x_ref[at, :]) * (gate * sigmoid(gate))
            gated_ref[at, :] = gated
            square_ref[at, :] = square_ref[at, :] + gated * gated

    for sub in range(GROUP):
        head_pair(GROUP * step + sub, *[t.at[:, block(sub)] for t in tiles])

    @pl.when(step == pl.num_programs(0) - 1)
    def _():
        for i in chunks:
            at = block(i - first)
            total = jnp.sum(square_ref[at, :], axis=1, keepdims=True)
            row_ref[0:1, at] = jnp.broadcast_to(total, (LEN, LEN)).T[0:1]


def attention_kernel(chunks, q_ref, kv_ref, seg_row_ref, out_ref, lse_ref):
    scale = HEAD_DIM ** (-0.5) * LOG2E
    first = chunks[0]
    left_half = lane_iota() < HEAD_DIM
    zero = jnp.zeros((LEN, LEN), jnp.bfloat16)
    lse_ref[...] = jnp.zeros(lse_ref.shape, jnp.float32)
    for i in chunks:
        at = block(i - first)
        low = max(0, i - 2) * LEN
        span = (i + 1) * LEN - low
        allowed = jnp.concatenate([mask_ts(seg_row_ref, i, j) for j in range(low // LEN, i + 1)], axis=1)
        keys = kv_ref[low : low + span, :]
        swapped = pltpu.roll(keys.astype(jnp.float32), HEAD_DIM, 1).astype(jnp.bfloat16)
        for p in range(q_ref.shape[1] // LEN):
            queries = q_ref[block(i), block(p)]
            result = []
            for e in range(2):
                masked = jnp.where(left_half == (e == 0), queries, zero)
                scores = dot_nt(masked, keys if e == 0 else swapped) * scale
                scores = jnp.where(allowed, scores, hidden_bias)
                top = jnp.max(scores, axis=1, keepdims=True)
                weights = jnp.exp2(scores - top)
                total = jnp.sum(weights, axis=1, keepdims=True)
                probs = (weights * (1.0 / total)).astype(jnp.bfloat16)
                result.append(dot_nn(probs, swapped if e == 0 else keys))
                lse = jnp.broadcast_to(top + jnp.log(total) * LOG2E, (LEN, LEN))
                lse_ref[2 * p + e : 2 * p + e + 1, at] = lse.T[0:1]
            out_ref[at, block(p)] = jnp.where(left_half, result[0], result[1]).astype(jnp.bfloat16)


def attention_back_kernel(chunks, final, *refs):
    q_ref, kv_ref, do_ref, lse_ref, seg_row_ref, cos_ref, sin_ref = refs[:7]
    if final:
        dk_in_ref, dv_in_ref, dq_ref, dkv_ref, dk_ref, dv_ref, turned_ref, key_t_ref = refs[7:]
    else:
        dq_ref, dk_ref, dv_ref, turned_ref, key_t_ref = refs[7:]
    scale = HEAD_DIM ** (-0.5)
    blocks = q_ref.shape[0] // LEN
    first = chunks[0]
    left_half = lane_iota() < HEAD_DIM
    zero = jnp.zeros((LEN, LEN), jnp.bfloat16)
    for i in range(chunks[-1] + 1):
        kv = kv_ref[block(i), :].astype(jnp.float32)
        turned_ref[block(i), :] = pltpu.roll(kv, HEAD_DIM, 1).astype(jnp.bfloat16)
        key_t_ref[:, block(i)] = kv.T[:HEAD_DIM].astype(jnp.bfloat16)
    if final:
        dk_ref[...] = dk_in_ref[...]
        dv_ref[...] = dv_in_ref[...]
    else:
        dk_ref[...] = jnp.zeros(dk_ref.shape, jnp.float32)
        dv_ref[...] = jnp.zeros(dv_ref.shape, jnp.float32)
    for i in chunks:
        at = block(i - first)
        low = max(0, i - 2) * LEN
        span = (i + 1) * LEN - low
        window = slice(low, low + span)
        allowed = jnp.concatenate([mask_st(seg_row_ref, j, i) for j in range(low // LEN, i + 1)], axis=0)
        keys, swapped = kv_ref[window, :], turned_ref[window, :]
        for p in range(q_ref.shape[1] // LEN):
            queries, douts = q_ref[block(i), block(p)], do_ref[at, block(p)]
            back = []
            for e in range(2):
                side = left_half == (e == 0)
                q_half = jnp.where(side, queries, zero)
                do_half = jnp.where(side, douts, zero)
                h = 2 * p + e
                scores = dot_nt(keys if e == 0 else swapped, q_half) * (scale * LOG2E)
                probs = jnp.exp2(jnp.where(allowed, scores, hidden_bias) - lse_ref[h : h + 1, at])
                dprobs = dot_nt(swapped if e == 0 else keys, do_half)
                inner = jnp.sum(probs * dprobs, axis=0, keepdims=True)
                dscores = (probs * (dprobs - inner)).astype(jnp.bfloat16)
                dv_ref[window, :] = dv_ref[window, :] + dot_nn(probs.astype(jnp.bfloat16), do_half)
                dk_ref[window, :] = dk_ref[window, :] + dot_nn(dscores, q_half)
                back.append(dot_nn(key_t_ref[:, window], dscores))
            dq = jnp.concatenate(back, axis=0).T * scale
            dq_ref[at, block(p)] = rotate_tile(dq, cos_ref[block(i), :], -sin_ref[block(i), :]).astype(jnp.bfloat16)
    if not final:
        return
    for i in range(blocks):
        dk = dk_ref[block(i), :]
        dk = (dk + pltpu.roll(dk, HEAD_DIM, 1)) * scale
        dk = rotate_tile(dk, cos_ref[block(i), :], -sin_ref[block(i), :])
        dv = dv_ref[block(i), :]
        dv = dv + pltpu.roll(dv, HEAD_DIM, 1)
        dkv_ref[block(i), :] = jnp.where(left_half, dk, dv).astype(jnp.bfloat16)


def scan_back_kernel(
    chunks,
    heads,
    gmr_ref,
    gated_ref,
    square_a_ref,
    square_b_ref,
    dot_a_ref,
    dot_b_ref,
    table_ref,
    gate_ref,
    y_ref,
    x_ref,
    xb_ref,
    state_ref,
    lag_ref,
    cum_row_ref,
    seg_row_ref,
    select_ref,
    dgate_ref,
    gy_ref,
    dx_ref,
    p_ref,
    grad_in_ref,
    grad_out_ref,
    sums_ref,
    gyb_ref,
    wide_ref,
    cross_ref,
    bias_ref,
    dcross_ref,
    inv_wide_ref,
    dot_wide_ref,
    inner_ref,
    mix_ref,
):
    step = pl.program_id(0)
    first = chunks[0]
    sources = chunks[-1] + 1
    left_half = lane_iota() < HEAD_DIM
    zero = jnp.zeros((LEN, LEN), jnp.bfloat16)
    spans = [(j, max(j, first), min(j + 3, sources)) for j in range(sources)]
    pairs = [(j, i) for j, start, stop in spans for i in range(start, stop)]

    @pl.when(step == 0)
    def _():
        for i in chunks:
            at = block(i - first)
            square = (square_a_ref[:, at] + square_b_ref[:, at]) / DSSM
            inv = lax.rsqrt(square + norm_eps)
            inv_wide_ref[at, :] = jnp.broadcast_to(inv, (LEN, LEN)).T
            dot = (dot_a_ref[:, at] + dot_b_ref[:, at]) / DSSM
            dot_wide_ref[at, :] = jnp.broadcast_to(dot, (LEN, LEN)).T
        p_ref[...] = jnp.zeros(p_ref.shape, jnp.float32)
        for h in range(heads):
            wide_ref[h] = jnp.broadcast_to(lag_ref[: sources * LEN, h : h + 1], (sources * LEN, LEN))
        for j, start, stop in spans:
            cross = three_dots(dot_nt, state_ref[block(j), :LEN], state_ref[start * LEN : stop * LEN, LEN:])
            for n, (j2, i) in enumerate(pairs):
                if j2 == j:
                    cross_ref[n] = cross[:, block(i - start)]
                    allowed = mask_st(seg_row_ref, j, i)
                    bias_ref[n] = jnp.where(allowed, 0.0, hidden_bias)
                    dcross_ref[n] = jnp.zeros((LEN, LEN), jnp.float32)

    tiles = (
        gmr_ref,
        gated_ref,
        table_ref.at[6:7],
        gate_ref,
        y_ref,
        x_ref,
        xb_ref,
        table_ref.at[5:6],
        dgate_ref,
        gy_ref,
        dx_ref,
        sums_ref,
    )

    def head_pair(
        hp,
        select,
        gmr_ref,
        gated_ref,
        gain_ref,
        gate_ref,
        y_ref,
        x_ref,
        xb_ref,
        skip_ref,
        dgate_ref,
        gy_ref,
        dx_ref,
        sums_ref,
    ):
        skip = skip_ref[...]
        gain = gain_ref[...]
        skip_sum = jnp.zeros((1, LEN), jnp.float32)
        gain_sum = jnp.zeros((1, LEN), jnp.float32)
        for i in chunks:
            at = block(i - first)
            inv = inv_wide_ref[at, :]
            unit = gated_ref[at, :] * inv
            rows_grad = gmr_ref[at, :]
            grad = inv * (rows_grad * gain - unit * dot_wide_ref[at, :])
            gate = gate_ref[at, :]
            sig = sigmoid(gate)
            y = y_ref[at, :]
            x = x_ref[at, :]
            gy = grad * (gate * sig)
            dgate_ref[at, :] = (grad * (y + skip * x) * (sig * (1.0 + gate * (1.0 - sig)))).astype(jnp.bfloat16)
            gyb = gy.astype(jnp.bfloat16)
            gy_ref[at, :] = gy
            gyb_ref[at, :] = gyb
            high, rest = two_terms(gyb.astype(jnp.float32) * y)
            p_ref[:, at] = p_ref[:, at] + dot_nt(select, high) + dot_nt(select, rest)
            skip_sum = skip_sum + jnp.sum(gy * x, axis=0, keepdims=True)
            gain_sum = gain_sum + jnp.sum(rows_grad * unit, axis=0, keepdims=True)
        sums_ref[0:1, :] = skip_sum
        sums_ref[1:2, :] = gain_sum

        for j, start, stop in spans:
            x_pair = xb_ref[block(j), :]
            x_both = jnp.concatenate([jnp.where(left_half, x_pair, zero), jnp.where(left_half, zero, x_pair)], axis=0)
            wide = (stop - start) * LEN
            gy_rows = gyb_ref[(start - first) * LEN : (stop - first) * LEN, :]
            inner_ref[:, :wide] = dot_nt(x_both, gy_rows)
            for n, (j2, i) in enumerate(pairs):
                if j2 != j:
                    continue
                grown = dcross_ref[n]
                for e in range(2):
                    spread = cum_row_ref[2 * hp + e, :, block(i)] - wide_ref[2 * hp + e, block(j), :]
                    decay = jnp.exp2(spread + bias_ref[n])
                    grown = grown + inner_ref[block(e), block(i - start)] * decay
                    mix_ref[block(e), block(i - start)] = (decay * cross_ref[n]).astype(jnp.bfloat16)
                dcross_ref[n] = grown
            both = dot_nn(mix_ref[:, :wide], gy_rows)
            dx_ref[block(j), :] = jnp.where(left_half, both[:LEN], both[LEN:])

    for sub in range(GROUP):
        head_pair(GROUP * step + sub, select_ref[:, block(sub)], *[t.at[:, block(sub)] for t in tiles])

    @pl.when(step == pl.num_programs(0) - 1)
    def _():
        grad_out = {i: jnp.zeros((LEN, LEN), jnp.float32) for i in chunks}
        for j in range(sources):
            grad_in = jnp.zeros((LEN, LEN), jnp.float32)
            for n, (j2, i) in enumerate(pairs):
                if j2 != j:
                    continue
                high, rest = two_terms(dcross_ref[n])
                out_high, out_rest = two_terms(state_ref[block(i), LEN:])
                in_high, in_rest = two_terms(state_ref[block(j), :LEN])
                grad_in = grad_in + dot_nn(high, out_high) + dot_nn(high, out_rest) + dot_nn(rest, out_high)
                grad_out[i] = grad_out[i] + dot_tn(high, in_high) + dot_tn(high, in_rest) + dot_tn(rest, in_high)
            grad_in_ref[block(j), :] = grad_in
        for i in chunks:
            grad_out_ref[block(i - first), :] = grad_out[i]


def conv_back(grad_ref, value_ref, keep_ref, taps, out_ref, sum_ref, lanes, blocks):
    totals = [jnp.zeros((1, LEN), jnp.float32) for _ in range(5)]
    for i in range(blocks):
        here = grad_ref[i * LEN : (i + 1) * LEN, :]
        grad = taps[3:4] * here
        totals[4] = totals[4] + jnp.sum(here, axis=0, keepdims=True)
        totals[3] = totals[3] + jnp.sum(here * value_ref[8 + i * LEN : 8 + (i + 1) * LEN, :], axis=0, keepdims=True)
        for lag in (1, 2, 3):
            ahead = grad_ref[i * LEN + lag : (i + 1) * LEN + lag, :]
            grad = grad + taps[3 - lag : 4 - lag] * (ahead * keep_ref[lag - 1, i * LEN + lag : (i + 1) * LEN + lag, :])
            moved = value_ref[8 + i * LEN - lag : 8 + (i + 1) * LEN - lag, :]
            masked = here * keep_ref[lag - 1, i * LEN : (i + 1) * LEN, :]
            totals[3 - lag] = totals[3 - lag] + jnp.sum(masked * moved, axis=0, keepdims=True)
        out_ref[block(i), lanes] = grad.astype(jnp.bfloat16)
    for tap in range(5):
        sum_ref[tap : tap + 1, lanes] = totals[tap]


def scan_end_kernel(
    heads,
    gy_a_ref,
    gy_b_ref,
    dx_a_ref,
    dx_b_ref,
    p_a_ref,
    p_b_ref,
    in_a_ref,
    in_b_ref,
    out_a_ref,
    out_b_ref,
    xb_ref,
    slope_ref,
    state_slope_ref,
    conv_ref,
    small_ref,
    step_row_ref,
    sig_row_ref,
    seg_row_ref,
    select_ref,
    table_ref,
    params_ref,
    dconv_ref,
    dstate_ref,
    dstep_ref,
    conv_sum_ref,
    state_sum_ref,
    step_sum_ref,
    grad_pad_ref,
    value_pad_ref,
    wide_ref,
    q_ref,
    flow_ref,
):
    step = pl.program_id(0)
    rows = conv_ref.shape[0]
    blocks = rows // LEN
    half = rows // 2
    count = flow_ref.shape[0]

    @pl.when(step == 0)
    def _():
        value_pad_ref[0:8, :] = jnp.zeros((8, LEN), jnp.float32)
        grad_pad_ref[rows : rows + 8, :] = jnp.zeros((8, LEN), jnp.float32)
        widen(seg_row_ref, wide_ref, value_pad_ref)
        value_pad_ref[0:8, :] = jnp.zeros((8, LEN), jnp.float32)
        q_ref[...] = jnp.zeros(q_ref.shape, jnp.float32)
        for c in range(2):
            if c == 0:
                grad_pad_ref[0:half, :] = (in_a_ref[...] + in_b_ref[0:half, :]) * state_slope_ref[0:half, block(c)]
                grad_pad_ref[half:rows, :] = in_b_ref[half:rows, :] * state_slope_ref[half:rows, block(c)]
            else:
                grad_pad_ref[0:half, :] = out_a_ref[...] * state_slope_ref[0:half, block(c)]
                grad_pad_ref[half:rows, :] = out_b_ref[...] * state_slope_ref[half:rows, block(c)]
            value_pad_ref[8 : rows + 8, :] = small_ref[:, block(c)]
            conv_back(
                grad_pad_ref,
                value_pad_ref,
                wide_ref,
                params_ref[8:12, block(c)],
                dstate_ref,
                state_sum_ref,
                block(c),
                blocks,
            )

    tiles = (
        gy_a_ref,
        gy_b_ref,
        dx_a_ref,
        dx_b_ref,
        xb_ref,
        slope_ref,
        conv_ref,
        table_ref.at[5:6],
        dconv_ref,
        conv_sum_ref,
    )

    def head_pair(
        select,
        taps,
        gy_a_ref,
        gy_b_ref,
        dx_a_ref,
        dx_b_ref,
        xb_ref,
        slope_ref,
        conv_ref,
        skip_ref,
        dconv_ref,
        conv_sum_ref,
    ):
        for j in range(blocks):
            dx = dx_b_ref[block(j), :]
            if j < blocks // 2:
                dx = dx + dx_a_ref[block(j), :]
                gy = gy_a_ref[block(j), :]
            else:
                gy = gy_b_ref[block(j - blocks // 2), :]
            high, rest = two_terms(dx * xb_ref[block(j), :].astype(jnp.float32))
            q_ref[:, block(j)] = q_ref[:, block(j)] + dot_nt(select, high) + dot_nt(select, rest)
            grad_pad_ref[block(j), :] = (dx + gy * skip_ref[...]) * slope_ref[block(j), :]
        value_pad_ref[8 : rows + 8, :] = conv_ref[...]
        conv_back(
            grad_pad_ref, value_pad_ref, wide_ref, taps, dconv_ref, conv_sum_ref, slice(0, LEN), blocks
        )

    for sub in range(GROUP):
        head_pair(select_ref[:, block(sub)], table_ref[0:4, block(sub)], *[t.at[:, block(sub)] for t in tiles])

    @pl.when(step == pl.num_programs(0) - 1)
    def _():
        q = q_ref[...]
        flow_ref[:, 0:half] = p_a_ref[...] - q[:, 0:half]
        flow_ref[:, half:rows] = p_b_ref[...] - q[:, half:rows]
        rate = turned(params_ref[14:15, :LEN])[:count]
        bias_total = jnp.zeros((count, LEN), jnp.float32)
        decay_total = jnp.zeros((count, LEN), jnp.float32)
        for j in range(blocks):
            log_grad = jnp.zeros((count, LEN), jnp.float32)
            for i in range(j, min(j + 3, blocks)):
                chosen = jnp.where(mask_st(seg_row_ref, j, i), 1.0, 0.0).astype(jnp.bfloat16)
                high, rest = two_terms(flow_ref[:, block(i)])
                log_grad = log_grad + dot_nt(high, chosen) + dot_nt(rest, chosen)
            step = step_row_ref[:, block(j)]
            grad_step = jnp.where(step > 1e-30, q[:, block(j)] / step, 0.0) + log_grad * rate
            grad_arg = grad_step * sig_row_ref[:, block(j)]
            bias_total = bias_total + grad_arg
            decay_total = decay_total + log_grad * step
            tall = jnp.concatenate([grad_arg, jnp.zeros((LEN - count, LEN), jnp.float32)], axis=0)
            dstep_ref[block(j), :] = tall.T.astype(jnp.bfloat16)
        step_sum_ref[0:count, :] = jnp.broadcast_to(jnp.sum(bias_total, axis=1, keepdims=True), (count, LEN))
        step_sum_ref[count : 2 * count, :] = jnp.broadcast_to(
            jnp.sum(decay_total * rate, axis=1, keepdims=True), (count, LEN)
        )


def whole_block(shape):
    return pl.BlockSpec(shape, lambda step: (0,) * len(shape), pipeline_mode=pl.Buffered(1))


def tile(rows, row_block=0, first=0):
    return pl.BlockSpec((rows, GROUP * LEN), lambda step: (row_block, first + step))


def small_block(rows, width):
    return pl.BlockSpec((rows, width), lambda step: (0, 2), pipeline_mode=pl.Buffered(1))


def call(kernel, steps, out_shape, out_specs, scratch, operands, specs, flops):
    return pl.pallas_call(
        kernel,
        grid=(steps,),
        out_shape=out_shape,
        in_specs=[s or whole_block(o.shape) for o, s in zip(operands, specs)],
        out_specs=[s or whole_block(o.shape) for o, s in zip(out_shape, out_specs)],
        scratch_shapes=scratch,
        compiler_params=pltpu.CompilerParams(vmem_limit_bytes=VMEM_BYTES),
        cost_estimate=pl.CostEstimate(flops=flops, bytes_accessed=0, transcendentals=0),
    )(*operands)


def f32(*shape):
    return jax.ShapeDtypeStruct(shape, jnp.float32)


def b16(*shape):
    return jax.ShapeDtypeStruct(shape, jnp.bfloat16)


HEAD_ROWS = 16
GROUP = 3
VMEM_BYTES = 60 * 1024 * 1024


def scan_prep(width, wide_in, cosine, sine, seg_row, params):
    rows = wide_in.shape[0]
    steps = width // LEN // GROUP
    outs = [
        f32(rows, width),
        b16(rows, width),
        f32(rows, width),
        f32(rows, 2 * LEN),
        f32(rows, 2 * LEN),
        f32(rows, LEN),
        f32(rows, LEN),
        f32(HEAD_ROWS, 1, rows),
        f32(HEAD_ROWS, 1, rows),
        f32(HEAD_ROWS, rows),
        f32(HEAD_ROWS, rows),
        b16(rows, 2 * LEN),
        b16(rows, LEN),
    ]
    scratch = [pltpu.VMEM((rows + 8, LEN), jnp.float32), pltpu.VMEM((3, rows + 8, LEN), jnp.float32)]
    operands = (wide_in, wide_in, cosine, sine, seg_row, params, params)
    specs = [tile(rows, 0, steps), small_block(rows, width), None, None, None, tile(16), None]
    return call(prep_kernel, steps, outs, [tile(rows)] * 3 + [None] * 10, scratch, operands, specs, 0 * 10**9)


def scan_forward(chunks, heads, wide_in, x, xb, *rest):
    width = x.shape[1]
    rows = LEN * len(chunks)
    at = chunks[0] // len(chunks)
    count = sum(min(i, 2) + 1 for i in chunks)
    outs = [f32(rows, width), f32(rows, width), f32(1, rows)]
    scratch = [
        pltpu.VMEM((heads, rows, LEN), jnp.float32),
        pltpu.VMEM((count, LEN, LEN), jnp.float32),
        pltpu.VMEM((count, LEN, LEN), jnp.float32),
        pltpu.VMEM((len(chunks), 2 * LEN, 3 * LEN), jnp.bfloat16),
        pltpu.VMEM((rows, LEN), jnp.float32),
    ]
    specs = [tile(rows, at), tile(rows, at), tile((chunks[-1] + 1) * LEN)] + [None] * (len(rest) - 1) + [tile(16)]
    kernel = functools.partial(scan_kernel, chunks, heads)
    operands = (wide_in, x, xb, *rest)
    return call(kernel, heads // 2 // GROUP, outs, [tile(rows), tile(rows), None], scratch, operands, specs, 0 * 10**9)


def attention_forward(chunks, q, kv, seg_row):
    rows = LEN * len(chunks)
    outs = [b16(rows, q.shape[1]), f32(8, rows)]
    kernel = functools.partial(attention_kernel, chunks)
    return call(kernel, 1, outs, [None] * 2, [], (q, kv, seg_row), [None] * 3, 0 * 10**9)


def attention_backward(chunks, final, *operands):
    q = operands[0]
    rows = q.shape[0]
    partial = [f32(rows, LEN), f32(rows, LEN)]
    sums = [pltpu.VMEM((rows, LEN), jnp.float32)] * 2
    outs = [b16(LEN * len(chunks), q.shape[1])] + ([b16(rows, LEN)] if final else partial)
    scratch = (sums if final else []) + [
        pltpu.VMEM((rows, LEN), jnp.bfloat16),
        pltpu.VMEM((HEAD_DIM, rows), jnp.bfloat16),
    ]
    kernel = functools.partial(attention_back_kernel, chunks, final)
    return call(kernel, 1, outs, [None] * len(outs), scratch, operands, [None] * len(operands), (0 if chunks[0] else 30) * 10**9)


def scan_backward(chunks, heads, *operands):
    rows, width = operands[0].shape
    at = chunks[0] // len(chunks)
    sources = (chunks[-1] + 1) * LEN
    count = sum(min(i, 2) + 1 for i in chunks)
    outs = [
        b16(rows, width),
        f32(rows, width),
        f32(sources, width),
        f32(HEAD_ROWS, rows),
        f32(sources, LEN),
        f32(rows, LEN),
        f32(8, width),
    ]
    scratch = [
        pltpu.VMEM((rows, LEN), jnp.bfloat16),
        pltpu.VMEM((heads, sources, LEN), jnp.float32),
        pltpu.VMEM((count, LEN, LEN), jnp.float32),
        pltpu.VMEM((count, LEN, LEN), jnp.float32),
        pltpu.VMEM((count, LEN, LEN), jnp.float32),
        pltpu.VMEM((rows, LEN), jnp.float32),
        pltpu.VMEM((rows, LEN), jnp.float32),
        pltpu.VMEM((2 * LEN, 3 * LEN), jnp.float32),
        pltpu.VMEM((2 * LEN, 3 * LEN), jnp.bfloat16),
    ]
    specs = [tile(rows), tile(rows), None, None, None, None, tile(16), tile(rows, at), tile(rows), tile(rows, at), tile(sources)]
    specs += [None, None, None, None, tile(HEAD_ROWS)]
    out_specs = [tile(rows), tile(rows), tile(sources), None, None, None, tile(8)]
    kernel = functools.partial(scan_back_kernel, chunks, heads)
    return call(kernel, heads // 2 // GROUP, outs, out_specs, scratch, operands, specs, 30 * 10**9)


def scan_end(heads, *operands):
    rows, width = 2 * operands[0].shape[0], operands[0].shape[1]
    steps = heads // 2 // GROUP
    outs = [
        b16(rows, width),
        b16(rows, 2 * LEN),
        b16(rows, LEN),
        f32(8, width),
        f32(8, 2 * LEN),
        f32(2 * HEAD_ROWS, LEN),
    ]
    scratch = [
        pltpu.VMEM((rows + 8, LEN), jnp.float32),
        pltpu.VMEM((rows + 8, LEN), jnp.float32),
        pltpu.VMEM((3, rows + 8, LEN), jnp.float32),
        pltpu.VMEM((HEAD_ROWS, rows), jnp.float32),
        pltpu.VMEM((HEAD_ROWS, rows), jnp.float32),
    ]
    half = rows // 2
    specs = [tile(half), tile(half), tile(half), tile(rows)] + [None] * 6 + [tile(rows), tile(rows), None]
    specs += [tile(rows, 0, steps), small_block(rows, width), None, None, None, tile(HEAD_ROWS), tile(16), None]
    out_specs = [tile(rows), None, None, tile(8), None, None]
    kernel = functools.partial(scan_end_kernel, heads)
    return call(kernel, steps, outs, out_specs, scratch, operands, specs, 30 * 10**9)


def inverse_rms(rows):
    return lax.rsqrt(jnp.mean(rows * rows, axis=-1, keepdims=True) + norm_eps)


def ffn_kernel(
    tokens_ref,
    part_ref,
    far_ref,
    gain_ref,
    gate_ref,
    up_ref,
    down_ref,
    cotangent_ref,
    hidden_ref,
    normed_ref,
    activated_ref,
    grad_gate_ref,
    grad_up_ref,
    back_ref,
    out_ref,
):
    @pl.when(pl.program_id(0) == 0)
    def _():
        hidden = tokens_ref[...].astype(jnp.float32) + (part_ref[...] + far_ref[...])
        hidden_ref[...] = hidden
        normed_ref[...] = (hidden * inverse_rms(hidden) * gain_ref[...]).astype(jnp.bfloat16)
        back_ref[...] = jnp.zeros(back_ref.shape, jnp.float32)
        out_ref[...] = jnp.zeros(out_ref.shape, jnp.float32)

    normed = normed_ref[...]
    gate = dot_nn(normed, gate_ref[...])
    up = dot_nn(normed, up_ref[...])
    sig = sigmoid(gate)
    act = gate * sig
    activated = (act * up).astype(jnp.bfloat16)
    activated_ref[...] = activated
    grad = dot_nt(cotangent_ref[...], down_ref[...])
    grad_gate = (grad * up * (sig * (1.0 + gate * (1.0 - sig)))).astype(jnp.bfloat16)
    grad_up = (grad * act).astype(jnp.bfloat16)
    grad_gate_ref[...] = grad_gate
    grad_up_ref[...] = grad_up
    back_ref[...] = back_ref[...] + (dot_nt(grad_gate, gate_ref[...]) + dot_nt(grad_up, up_ref[...]))
    out_ref[...] = out_ref[...] + dot_nn(activated, down_ref[...])


def ffn(chunks, tokens, part, far, gain, gate, up, down, cotangent):
    rows, model_width = part.shape
    at = chunks[0] // len(chunks)
    hidden_width = gate.shape[1]
    steps = hidden_width // 256
    outs = [f32(rows, model_width), b16(rows, model_width)] + [b16(rows, hidden_width)] * 3
    outs += [f32(rows, model_width)] * 2
    rows_of = pl.BlockSpec((rows, model_width), lambda step: (at, 0), pipeline_mode=pl.Buffered(1))
    columns = pl.BlockSpec((model_width, 256), lambda step: (0, step))
    tiles = pl.BlockSpec((rows, 256), lambda step: (0, step))
    specs = [rows_of, None, None, None, columns, columns]
    specs += [pl.BlockSpec((256, model_width), lambda step: (step, 0)), rows_of]
    operands = (tokens, part, far, gain, gate, up, down, cotangent)
    return call(ffn_kernel, steps, outs, [None, None, tiles, tiles, tiles, None, None], [], operands, specs, 0 * 10**9)


def middle_kernel(
    hidden_ref,
    part_ref,
    far_ref,
    cotangent_ref,
    gain_ref,
    gated_ref,
    square_a_ref,
    square_b_ref,
    params_ref,
    mixer_out_ref,
    attn_out_ref,
    grad_hidden_ref,
    grad_branch_ref,
    grad_rows_ref,
    grad_attended_ref,
    dot_ref,
    gain_sum_ref,
):
    hidden = hidden_ref[...]
    inv = inverse_rms(hidden)
    unit = hidden * inv
    grad_normed = part_ref[...] + far_ref[...]
    gain_sum_ref[0:1, :] = jnp.sum(grad_normed * unit, axis=0, keepdims=True)
    grad_unit = grad_normed * gain_ref[...]
    inner = jnp.mean(grad_unit * unit, axis=-1, keepdims=True)
    grad_hidden = cotangent_ref[...].astype(jnp.float32) + inv * (grad_unit - unit * inner)
    grad_hidden_ref[...] = grad_hidden
    grad_branch = grad_hidden.astype(jnp.bfloat16)
    grad_branch_ref[...] = grad_branch
    grad_rows = dot_nt(grad_branch, mixer_out_ref[...])
    grad_rows_ref[...] = grad_rows
    grad_attended_ref[...] = dot_nt(grad_branch, attn_out_ref[...]).astype(jnp.bfloat16)
    total = jnp.sum(grad_rows * params_ref[6:7, :] * gated_ref[...], axis=-1, keepdims=True)
    for i in range(hidden.shape[0] // LEN):
        at = block(i)
        inv_gated = lax.rsqrt((square_a_ref[:, at] + square_b_ref[:, at]) / DSSM + norm_eps)
        dot_ref[0:1, at] = jnp.broadcast_to(total[at], (LEN, LEN)).T[0:1] * inv_gated


def middle(chunks, hidden, part, far, cotangent, gain, gated, square_a, square_b, gated_gain, mixer_out, attn_out):
    rows, model_width = part.shape
    at = chunks[0] // len(chunks)
    width, inner = mixer_out.shape[0], attn_out.shape[0]
    outs = [
        f32(rows, model_width),
        b16(rows, model_width),
        f32(rows, width),
        b16(rows, inner),
        f32(1, rows),
        f32(8, model_width),
    ]
    rows_of = pl.BlockSpec((rows, model_width), lambda step: (at, 0), pipeline_mode=pl.Buffered(1))
    specs = [None, None, None, rows_of] + [None] * 7
    operands = (hidden, part, far, cotangent, gain, gated, square_a, square_b, gated_gain, mixer_out, attn_out)
    return call(middle_kernel, 1, outs, [None] * 6, [], operands, specs, (0 if chunks[0] else 90) * 10**9)


def core_call(kernel, steps, core, out_shape, out_spec, scratch, operands, specs, flops, aliases=None):
    return pl.pallas_call(
        kernel,
        grid_spec=pltpu.PrefetchScalarGridSpec(
            num_scalar_prefetch=1, grid=(steps,), in_specs=specs, out_specs=out_spec, scratch_shapes=scratch
        ),
        out_shape=out_shape,
        compiler_params=pltpu.CompilerParams(vmem_limit_bytes=VMEM_BYTES),
        cost_estimate=pl.CostEstimate(flops=flops, bytes_accessed=0, transcendentals=0),
        input_output_aliases=aliases or {},
    )(core, *operands)


def clip_tile(rows, columns, first, last):
    return pl.BlockSpec((rows, columns), lambda step, core_ref: (0, jnp.clip(step - first, 0, last - first - 1)))


def ffn_weights_kernel(add, core_ref, *refs):
    refs = list(refs)
    normed_a, normed_b, act_a, act_b, gate_a, gate_b, up_a, up_b, cot_a, cot_b = refs[:10]
    far_ref = refs[10] if add else None
    out_ref, left_ref = refs[-2:]
    step = pl.program_id(0)
    third = pl.num_programs(0) // 3
    half = normed_a.shape[0]

    def turn(first, second):
        left_ref[:, :half] = first[...].T
        left_ref[:, half:] = second[...].T

    @pl.when(step == 0)
    def _():
        turn(normed_a, normed_b)

    @pl.when(step == 2 * third)
    def _():
        turn(act_a, act_b)

    def product(first, second):
        result = dot_nn(left_ref[:, :half], first[...]) + dot_nn(left_ref[:, half:], second[...])
        out_ref[...] = result + far_ref[...] if add else result

    @pl.when(step < third)
    def _():
        product(gate_a, gate_b)

    @pl.when((step >= third) & (step < 2 * third))
    def _():
        product(up_a, up_b)

    @pl.when(step >= 2 * third)
    def _():
        product(cot_a, cot_b)


def ffn_weights(core, far, normed_a, normed_b, act_a, act_b, gate_a, gate_b, up_a, up_b, cotangent):
    half, columns = normed_a.shape
    kept = columns // 2
    tile_width = 512
    third = columns // tile_width
    left = pl.BlockSpec((half, kept), lambda step, core_ref: (0, core_ref[0]), pipeline_mode=pl.Buffered(1))
    specs = [left] * 4 + [clip_tile(half, tile_width, 0, third)] * 2
    specs += [clip_tile(half, tile_width, third, 2 * third)] * 2

    def cot_rows(at):
        return pl.BlockSpec(
            (half, tile_width), lambda step, core_ref: (at, jnp.clip(step - 2 * third, 0, third - 1))
        )

    specs += [cot_rows(0), cot_rows(1)]
    out = pl.BlockSpec((kept, tile_width), lambda step, core_ref: (0, step))
    operands = [normed_a, normed_b, act_a, act_b, gate_a, gate_b, up_a, up_b, cotangent, cotangent]
    if far is not None:
        operands.append(far)
        specs.append(out)
    return core_call(
        functools.partial(ffn_weights_kernel, far is not None),
        3 * third,
        core,
        f32(kept, (3 if far is None else 4) * columns),
        out,
        [pltpu.VMEM((kept, 2 * half), jnp.bfloat16)],
        operands,
        specs,
        0 * 10**9,
    )


def outer_weights_kernel(add, core_ref, *refs):
    refs = list(refs)
    rows_a, rows_b, edge_a, edge_b, att_a, att_b, branch_a, branch_b = refs[:8]
    out_ref, left_ref = refs[-2:]
    half = rows_a.shape[0]
    middle_row = left_ref.shape[0] // 2

    @pl.when((pl.program_id(0) == 0) & (core_ref[0] == 0))
    def _():
        left_ref[:, :half] = rows_a[...].T
        left_ref[:, half:] = rows_b[...].T

    @pl.when((pl.program_id(0) == 0) & (core_ref[0] == 1))
    def _():
        left_ref[:middle_row, :half] = edge_a[...].T
        left_ref[:middle_row, half:] = edge_b[...].T
        left_ref[middle_row:, :half] = att_a[...].T
        left_ref[middle_row:, half:] = att_b[...].T

    result = dot_nn(left_ref[:, :half], branch_a[...]) + dot_nn(left_ref[:, half:], branch_b[...])
    out_ref[...] = result + refs[8][...] if add else result


def outer_weights(core, far, buffer, rows_a, rows_b, att_a, att_b, branch_a, branch_b):
    half, width = rows_a.shape
    model_width = branch_a.shape[1]
    kept = model_width // 2
    tile_width = 512
    steps = model_width // tile_width

    def fixed(shape, column=0):
        return pl.BlockSpec(shape, lambda step, core_ref: (0, column), pipeline_mode=pl.Buffered(1))

    specs = [fixed((half, kept))] * 2
    specs += [fixed((half, width - kept), kept // (width - kept))] * 2
    specs += [fixed(att_a.shape)] * 2 + [clip_tile(half, tile_width, 0, steps)] * 2
    operands = [rows_a, rows_b, rows_a, rows_b, att_a, att_b, branch_a, branch_b]
    out = pl.BlockSpec((kept, tile_width), lambda step, core_ref: (0, step))
    columns, aliases = model_width, {}
    if far is not None:
        operands += [far, buffer]
        specs += [out, pl.BlockSpec(memory_space=pl.ANY)]
        columns = buffer.shape[1]
        first = columns // tile_width - steps
        out = pl.BlockSpec((kept, tile_width), lambda step, core_ref: (0, first + step))
        aliases = {len(operands): 0}
    return core_call(
        functools.partial(outer_weights_kernel, far is not None),
        steps,
        core,
        f32(kept, columns),
        out,
        [pltpu.VMEM((kept, 2 * half), jnp.bfloat16)],
        operands,
        specs,
        0,
        aliases,
    )


PARTS = ((0, 3), (3, 5), (5, 7), (7, 9))


def small_table(rows_ref, gain_ref, state_ref, step_ref, sums_a, sums_b, conv_ref, ffn_a, ffn_b, select_ref):
    kept = rows_ref.shape[1] // 2
    heads = 12
    rows_ref[...] = jnp.zeros(rows_ref.shape, jnp.float32)
    width = conv_ref.shape[1]
    states = state_ref.shape[1]
    rows_ref[0:1, :] = gain_ref[0:1, :]
    for tap in range(4):
        rows_ref[1:2, tap * states : (tap + 1) * states] = state_ref[tap : tap + 1, :]
    rows_ref[2:3, :states] = state_ref[4:5, :]
    sums = sums_a[...] + sums_b[...]
    high, rest = two_terms(sums)
    by_head = dot_nt(high, select_ref[...]) + dot_nt(rest, select_ref[...])
    count = by_head.shape[1]
    rows_ref[3:4, 0:count] = step_ref[0:count, :].T[0:1, :]
    rows_ref[3:4, LEN : LEN + count] = step_ref[count : 2 * count, :].T[0:1, :]
    rows_ref[3:4, 2 * LEN : 2 * LEN + count] = by_head[0:1, :]
    rows_ref[4:9, :width] = conv_ref[0:5, :]
    rows_ref[9:10, :width] = sums[1:2, :]
    rows_ref[10:11, :] = ffn_a[0:1, :] + ffn_b[0:1, :]
    stacked = []
    for index in range(11):
        stacked += [rows_ref[index : index + 1, :kept], rows_ref[index : index + 1, kept:]]
    before = jnp.zeros((heads, kept), jnp.float32)
    behind = jnp.zeros((LEN - heads - len(stacked), kept), jnp.float32)
    return jnp.concatenate([before, *stacked, behind], axis=0).T


def mixer_weights_kernel(add, core_ref, *refs):
    refs = list(refs)
    normed_ref, gate_a, gate_b, conv_ref, query_a, query_b, state_ref, pair_ref, step_ref = refs[:9]
    far_ref = refs[9] if add else None
    outs = refs[19:27] if add else refs[9:10]
    left_ref, result_ref = refs[-3:-1] if add else refs[-2:]
    step = pl.program_id(0)
    half = gate_a.shape[0]

    @pl.when(step == 0)
    def _():
        left_ref[...] = normed_ref[...].T

    def two(first, second):
        result_ref[...] = dot_nn(left_ref[:, :half], first[...]) + dot_nn(left_ref[:, half:], second[...])

    @pl.when(step < 3)
    def _():
        two(gate_a, gate_b)

    @pl.when((step >= 3) & (step < 6))
    def _():
        result_ref[...] = dot_nn(left_ref[...], conv_ref[...])

    @pl.when(step == 6)
    def _():
        two(query_a, query_b)

    @pl.when(step == 7)
    def _():
        result_ref[...] = dot_nn(left_ref[...], state_ref[...])

    @pl.when(step == 8)
    def _():
        result_ref[:, :LEN] = dot_nn(left_ref[...], pair_ref[...])
        steps = dot_nn(left_ref[...], step_ref[...])
        result_ref[:, LEN:] = steps + small_table(refs[-1], *refs[10:19]) if add else steps

    if not add:
        outs[0][...] = result_ref[...]
        return
    result_ref[...] = result_ref[...] + far_ref[...]
    for k, (first, last) in enumerate(PARTS):

        @pl.when((step >= first) & (step < last))
        def _():
            for side in range(2):
                out_ref = outs[2 * k + side]
                for q in range(2):
                    index = core_ref[1 + 4 * k + 2 * side + q]
                    if k < 2:
                        for y in range(4):
                            start = pl.multiple_of((4 * y + index) * 32, 32)
                            out_ref[(2 * y + q) * 32 : (2 * y + q + 1) * 32, :] = result_ref[pl.ds(start, 32), :]
                    else:
                        start = pl.multiple_of(index * LEN, LEN)
                        out_ref[q * LEN : (q + 1) * LEN, :] = result_ref[pl.ds(start, LEN), :]


def mixer_weights(core, far, smalls, normed, gate_a, gate_b, conv, query_a, query_b, state, pair, step):
    half = gate_a.shape[0]
    rows, model_width = normed.shape
    kept = model_width // 2
    tile_width = 256
    steps = 9

    def fixed(shape, column=0):
        return pl.BlockSpec(shape, lambda step, core_ref: (0, column), pipeline_mode=pl.Buffered(1))

    specs = [pl.BlockSpec((rows, kept), lambda step, core_ref: (0, core_ref[0]), pipeline_mode=pl.Buffered(1))]
    specs += [clip_tile(half, tile_width, 0, 3)] * 2 + [clip_tile(rows, tile_width, 3, 6)]
    specs += [fixed(query_a.shape)] * 2 + [fixed(state.shape), fixed(pair.shape), fixed(step.shape)]
    operands = [normed, gate_a, gate_b, conv, query_a, query_b, state, pair, step]
    out = pl.BlockSpec((kept, tile_width), lambda step, core_ref: (0, step))
    shape = f32(kept, steps * tile_width)
    if far is not None:
        operands += [far, *smalls]
        specs += [out] + [fixed(v.shape) for v in smalls]
        out, shape = [], []
        for first, last in PARTS:
            out += [clip_tile(kept // 2, tile_width, first, last)] * 2
            shape += [f32(kept // 2, (last - first) * tile_width)] * 2
    return core_call(
        functools.partial(mixer_weights_kernel, far is not None),
        steps,
        core,
        shape,
        out,
        [pltpu.VMEM((kept, rows), jnp.bfloat16), pltpu.VMEM((kept, tile_width), jnp.float32)]
        + ([pltpu.VMEM((16, model_width), jnp.float32)] if far is not None else []),
        operands,
        specs,
        30 * 10**9,
    )


def normed_back_kernel(
    gate_a,
    gate_b,
    conv_ref,
    query_a,
    query_b,
    state_ref,
    pair_ref,
    step_ref,
    wide_ref,
    small_ref,
    tokens_ref,
    whole_ref,
    *refs,
):
    outs, sum_ref, inv_ref = refs[:-2], refs[-2], refs[-1]


    @pl.when(pl.program_id(0) == 0)
    def _():
        inv_ref[...] = jnp.broadcast_to(inverse_rms(whole_ref[...].astype(jnp.float32)), inv_ref.shape)

    half, width = gate_a.shape
    query_width = query_a.shape[1]
    gate_w, conv_w = wide_ref[:, :width], wide_ref[:, width:]
    state_w = small_ref[:, : 2 * LEN]
    query_w = small_ref[:, 2 * LEN : 2 * LEN + query_width]
    pair_w = small_ref[:, 2 * LEN + query_width : 3 * LEN + query_width]
    step_w = small_ref[:, 3 * LEN + query_width :]
    total = jnp.zeros((1, sum_ref.shape[1]), jnp.float32)
    for k, (gate, query) in enumerate(((gate_a, query_a), (gate_b, query_b))):
        at = slice(k * half, (k + 1) * half)
        grad = dot_nt(gate[...], gate_w) + dot_nt(conv_ref[at, :], conv_w) + dot_nt(query[...], query_w)
        grad = grad + dot_nt(state_ref[at, :], state_w) + dot_nt(pair_ref[at, :], pair_w) + dot_nt(step_ref[at, :], step_w)
        for n in range(half // LEN):
            outs[k * (half // LEN) + n][...] = grad[block(n)]
        unit = tokens_ref[at, :].astype(jnp.float32) * jnp.concatenate([inv_ref[at, :]] * 2, axis=1)
        total = total + jnp.sum(grad * unit, axis=0, keepdims=True)
    sum_ref[0:1, :] = total


def normed_back(gate_a, gate_b, conv, query_a, query_b, state, pair, step, wide_proj, small_proj, tokens):
    rows, model_width = tokens.shape
    tile_width = 256
    operands = (gate_a, gate_b, conv, query_a, query_b, state, pair, step, wide_proj, small_proj, tokens, tokens)

    def weights(count):
        return pl.BlockSpec((tile_width, count), lambda step: (step, 0))

    columns = pl.BlockSpec((rows, tile_width), lambda step: (0, step))
    specs = [None] * 8 + [weights(wide_proj.shape[1]), weights(small_proj.shape[1]), columns, None]
    count = rows // LEN
    out_specs = [pl.BlockSpec((LEN, tile_width), lambda step: (0, step))] * count
    out_specs += [pl.BlockSpec((8, tile_width), lambda step: (0, step))]
    outs = [f32(LEN, model_width)] * count + [f32(8, model_width)]
    return call(
        normed_back_kernel,
        model_width // tile_width,
        outs,
        out_specs,
        [pltpu.VMEM((rows, LEN), jnp.float32)],
        operands,
        specs, 30 * 10**9)


def project_kernel(wide_steps, tokens_ref, gain_ref, wide_ref, small_ref, out_ref, normed_ref):
    step = pl.program_id(0)

    @pl.when(step == 0)
    def _():
        tokens = tokens_ref[...].astype(jnp.float32)
        normed_ref[...] = (tokens * inverse_rms(tokens) * gain_ref[...]).astype(jnp.bfloat16)

    @pl.when(step < wide_steps)
    def _():
        out_ref[...] = dot_nn(normed_ref[...], wide_ref[...])

    @pl.when(step >= wide_steps)
    def _():
        out_ref[...] = dot_nn(normed_ref[...], small_ref[...])


def project(tokens, gain, wide_proj, small_proj):
    rows, model_width = tokens.shape
    count = 768
    wide_steps = wide_proj.shape[1] // count
    steps = wide_steps + small_proj.shape[1] // count
    outs = [f32(rows, steps * count), b16(rows, model_width)]
    wide = pl.BlockSpec((model_width, count), lambda step: (0, jnp.minimum(step, wide_steps - 1)))
    small = pl.BlockSpec((model_width, count), lambda step: (0, jnp.maximum(step - wide_steps, 0)))
    out = pl.BlockSpec((rows, count), lambda step: (0, step))
    operands = (tokens, gain, wide_proj, small_proj)
    kernel = functools.partial(project_kernel, wide_steps)
    return call(kernel, steps, outs, [out, None], [], operands, [None, None, wide, small], 0)


def unpack_kernel(
    block_ref,
    step_ref,
    input_gain_ref,
    state_kernel_ref,
    state_bias_ref,
    step_bias_ref,
    decay_ref,
    skip_ref,
    conv_kernel_ref,
    conv_bias_ref,
    gated_gain_ref,
    ffn_gain_ref,
    turned_ref,
):
    heads = step_ref.shape[0]
    for i in range(block_ref.shape[0] // LEN):
        turned_ref[:, block(i)] = block_ref[block(i), :].T

    half = block_ref.shape[0] // 2

    def row(index, count, start=0):
        pieces = []
        for side in range(2):
            low, high = max(start, side * half), min(start + count, (side + 1) * half)
            if low < high:
                column, at = heads + 2 * index + side, low - side * half
                mine = turned_ref[column : column + 1, at : at + high - low]
                pieces.append(mine + turned_ref[column : column + 1, half + at : half + at + high - low])
        return (pieces[0] if len(pieces) == 1 else jnp.concatenate(pieces, axis=1))[0]

    step_ref[...] = turned_ref[0:heads, :]
    input_gain_ref[...] = row(0, input_gain_ref.shape[0])
    columns = state_kernel_ref.shape[1]
    for tap in range(4):
        state_kernel_ref[tap, :] = row(1, columns, tap * columns)
        conv_kernel_ref[tap, :] = row(4 + tap, conv_kernel_ref.shape[1])
    state_bias_ref[...] = row(2, columns)
    step_bias_ref[...] = row(3, heads)
    decay_ref[...] = row(3, heads, LEN)
    skip_ref[...] = row(3, heads, 2 * LEN)
    conv_bias_ref[...] = row(8, conv_bias_ref.shape[0])
    gated_gain_ref[...] = row(9, gated_gain_ref.shape[0])
    ffn_gain_ref[...] = row(10, ffn_gain_ref.shape[0])


def unpack(heads, width, states, values):
    rows = values.shape[0]
    outs = [f32(heads, rows), f32(rows), f32(4, states), f32(states), f32(heads), f32(heads), f32(heads)]
    outs += [f32(4, width), f32(width), f32(width), f32(rows)]
    scratch = [pltpu.VMEM((LEN, rows), jnp.float32)]
    return call(unpack_kernel, 1, outs, [None] * len(outs), scratch, (values,), [None], 0)


def assemble_kernel(source, mixer_proj_ref, query_ref, pair_ref, state_ref, step_ref):
    width = mixer_proj_ref.shape[2]
    start = 0
    mixer_proj_ref[:, 0, :] = source[:, start : start + width]
    start += width
    mixer_proj_ref[:, 1, :] = source[:, start : start + width]
    start += width
    query_ref[...] = source[:, start : start + query_ref.shape[1]]
    start += query_ref.shape[1]
    state_ref[...] = source[:, start : start + 2 * LEN]
    start += 2 * LEN
    pair_ref[:, 0, :] = source[:, start : start + LEN]
    step_ref[...] = source[:, start + LEN :]


def assemble(values, width, query_width):
    rows, columns = values.shape

    def plain(count):
        return pl.BlockSpec((256, count), lambda at: (at, 0))

    out_specs = [
        pl.BlockSpec((256, 2, width), lambda at: (at, 0, 0)),
        plain(query_width),
        pl.BlockSpec((256, 1, LEN), lambda at: (at, 0, 0)),
        plain(2 * LEN),
        plain(LEN),
    ]
    out_shape = [
        f32(rows, 2, width),
        f32(rows, query_width),
        f32(rows, 1, LEN),
        f32(rows, 2 * LEN),
        f32(rows, LEN),
    ]
    return call(assemble_kernel, rows // 256, out_shape, out_specs, [], (values,), [plain(columns)], 0)


LINKS = {
    "A": [(0, 1), (1, 0), (2, 3), (3, 2)],
    "B": [(1, 2), (2, 1), (3, 0), (0, 3)],
}
ORDERS = (
    (("x", "A"), ("x", "B"), ("y", "A"), ("y", "B")),
    (("x", "B"), ("y", "A"), ("y", "B"), ("x", "A")),
    (("y", "A"), ("y", "B"), ("x", "A"), ("x", "B")),
    (("y", "B"), ("x", "A"), ("x", "B"), ("y", "A")),
)
AXIS = {"y": 0, "x": 1}


def take(values, index, axis):
    return lax.dynamic_slice_in_dim(values, index, 1, axis)


def halves(values, name, link, again):
    place, axis = lax.axis_index(name), AXIS[name]
    if again:
        index = place // 2 if link == "B" else place % 2
        return take(values, index, axis), take(values, 1 - index, axis)
    if link == "B":
        side = place // 2
        kept = lax.dynamic_slice_in_dim(values, 2 * side, 2, axis)
        return kept, lax.dynamic_slice_in_dim(values, 2 - 2 * side, 2, axis)
    side = ((place + 1) // 2) % 2
    kept = jnp.concatenate([take(values, side, axis), take(values, 3 - side, axis)], axis)
    return kept, jnp.concatenate([take(values, 1 - side, axis), take(values, 2 + side, axis)], axis)


def reduce_rows(pairs, steps):
    kept, sent, parts = [], [], pairs
    if steps[0] == 0:
        for k, (stays, goes) in enumerate(pairs):
            shape = (4, 2, 32, stays.shape[1]) if ORDERS[k][0][0] == "x" else (2, 4, 32, stays.shape[1])
            kept.append(stays.reshape(shape))
            sent.append(goes.reshape(shape))
    for step in steps:
        if step:
            kept, sent = [], []
            for k in range(4):
                name, link = ORDERS[k][step]
                again = name in [n for n, _ in ORDERS[k][:step]]
                stays, goes = halves(parts[k], name, link, again)
                kept.append(stays)
                sent.append(goes)
        sent = lax.optimization_barrier(tuple(sent))
        come = [lax.ppermute(sent[k], ORDERS[k][step][0], LINKS[ORDERS[k][step][1]]) for k in range(4)]
        come = lax.optimization_barrier(tuple(come))
        parts = [stays + more for stays, more in zip(kept, come)]
    return parts


def rope_tables(rows):
    half_size = HEAD_DIM // 2
    inverse = np.float32(rope_base) ** (-(2.0 * np.arange(half_size, dtype=np.float32)) / HEAD_DIM)
    angles = np.arange(rows, dtype=np.float32)[:, None] * inverse.astype(np.float32)[None, :]
    cosine, sine = np.cos(angles), np.sin(angles)
    return (
        np.concatenate([cosine] * 4, axis=1).astype(np.float32),
        np.concatenate([-sine, sine, -sine, sine], axis=1).astype(np.float32),
    )


def norm_backward(grad_unit, unit_rows, inv_rms):
    return inv_rms * (grad_unit - unit_rows * jnp.mean(grad_unit * unit_rows, axis=-1, keepdims=True))


def dot32(left, right):
    return jnp.dot(left, right, preferred_element_type=jnp.float32)


def after(value, *others):
    return lax.optimization_barrier((value, *others))[0]


def swap(values, name):
    return lax.ppermute(values, name, PAIR)


def exchange(values, name):
    return values + swap(values, name)


def core_rows(values, index):
    half = values.shape[1] // 2
    return lax.dynamic_slice_in_dim(values, index * half, half, 1)


def on_device(
    layer_input,
    segments,
    input_gain,
    mixer_proj,
    state_proj,
    step_proj,
    step_bias,
    decay_log,
    skip_gain,
    conv_kernel,
    conv_bias,
    state_kernel,
    state_bias,
    gated_gain,
    mixer_out,
    query_proj,
    key_value_weight,
    attn_out,
    ffn_gain,
    ffn_gate,
    ffn_up,
    ffn_down,
    cotangent,
):
    rows, model_width = layer_input.shape
    width = mixer_proj.shape[2]
    heads = step_proj.shape[1]
    state_size = state_proj.shape[1] // 2
    query_width = query_proj.shape[1]
    pair_width = key_value_weight.shape[2]
    place = lax.axis_index("core")
    zh = lax.axis_index("zh")
    core = place.astype(jnp.int32).reshape(1)
    far_core = 1 - core
    cosine, sine = rope_tables(rows)
    select = np.arange(HEAD_ROWS)[:, None] == np.arange(width)[None, :] // HEAD_DIM
    select = jnp.asarray(select.astype(np.float32)).astype(jnp.bfloat16)
    seg_row = segments
    pad_heads = ((0, 0), (0, LEN - heads))

    def padded(values):
        return jnp.pad(values, ((0, 0), (0, width - values.shape[1])))

    params = jnp.concatenate(
        [
            conv_kernel,
            conv_bias[None, :],
            jnp.repeat(skip_gain, HEAD_DIM)[None, :],
            gated_gain[None, :],
            jnp.zeros((1, width), jnp.float32),
            padded(state_kernel),
            padded(state_bias[None, :]),
            padded(step_bias[None, :]),
            padded(-jnp.exp(decay_log)[None, :]),
            jnp.zeros((1, width), jnp.float32),
        ],
        axis=0,
    )
    wide_proj = mixer_proj.reshape(model_width, 2 * width)
    small_proj = jnp.concatenate(
        [
            state_proj,
            query_proj,
            key_value_weight.reshape(model_width, pair_width),
            jnp.pad(step_proj, pad_heads),
        ],
        axis=1,
    )
    tokens = layer_input.astype(jnp.float32)
    wide_in, normed_input = project(layer_input, input_gain[None, :], wide_proj, small_proj)
    x, xb, slope, state, state_slope, cum, lag, cum_row, lag_row, step_row, sig_row, queries, pairs = scan_prep(
        width,
        wide_in,
        cosine,
        sine,
        seg_row,
        params,
    )

    blocks = rows // LEN
    late = tuple(range(blocks // 2, blocks))
    early = tuple(range(blocks // 2))
    half = {}
    for chunks in (late, early):
        h = {"span": slice(chunks[0] * LEN, (chunks[-1] + 1) * LEN)}
        h["y"], h["gated"], h["square"] = scan_forward(
            chunks, heads, wide_in, x, xb, state, cum, lag_row, seg_row, params
        )
        half[chunks] = h
    squares = jnp.concatenate([half[early]["square"], half[late]["square"]], axis=1)
    squares_far = swap(squares, "tensor")
    ready = squares
    for chunks in (late, early):
        h = half[chunks]
        h["attended"], h["lse"] = attention_forward(chunks, after(queries, ready), pairs, seg_row)
        if chunks == late:
            squares_far = after(squares_far, h["lse"])
            squares_all = squares + squares_far
        h["square"], h["square_far"] = squares[:, h["span"]], squares_far[:, h["span"]]
        h["inv_gated"] = lax.rsqrt(squares_all[:, h["span"]].reshape(-1, 1) / DSSM + norm_eps)
        h["mixer_rows"] = (h["gated"] * h["inv_gated"] * gated_gain).astype(jnp.bfloat16)
        h["part"] = dot32(h["mixer_rows"], mixer_out) + dot32(h["attended"], attn_out)
        h["branch_far"] = swap(h["part"], "tensor")
        ready = h["part"]

    a, b = half[early], half[late]
    gain_ffn = ffn_gain[None, :]
    names = ("hidden", "normed", "activated", "grad_gate_rows", "grad_up_rows", "back", "down")
    for chunks in (late, early):
        h = half[chunks]
        far = h["branch_far"] if chunks == late else after(h["branch_far"], b["back"])
        operands = (layer_input, h["part"], far, gain_ffn, ffn_gate, ffn_up, ffn_down, cotangent)
        h.update(zip(names, ffn(chunks, *operands)))
        h["back_far"] = swap(h["back"], "tensor")

    for chunks in (late, early):
        h = half[chunks]
        far = h["back_far"] if chunks == late else after(h["back_far"], first)
        h["grad_hidden"], h["grad_branch"], h["grad_rows"], grad_attended, h["dot"], h["gain_sum"] = middle(
            chunks,
            h["hidden"],
            h["back"],
            far,
            cotangent,
            gain_ffn,
            h["gated"],
            h["square"],
            h["square_far"],
            params,
            mixer_out,
            attn_out,
        )
        if chunks == early:
            dots = jnp.concatenate([a["dot"], b["dot"]], axis=1)
            outer = (a["mixer_rows"], b["mixer_rows"], a["attended"], b["attended"])
            outer += (a["grad_branch"], b["grad_branch"])
            outer_sent = outer_weights(far_core, None, None, *outer)
            outer_far = swap(outer_sent, "core")
            first = ffn_weights(core, after(first_far, outer_sent), *sides)
            dots_far = swap(after(dots, first), "tensor")
            first = outer_weights(core, outer_far, first, *outer)
            first_sum = lax.psum_scatter(first, ("y", "x"), scatter_dimension=0, tiled=True)
            grad_attended = after(grad_attended, first)
        operands = (queries, pairs, grad_attended, h["lse"], seg_row, cosine, sine)
        if chunks == late:
            h["grad_queries"], grad_keys, grad_values = attention_backward(chunks, False, *operands)
            sides = (after(a["normed"], grad_keys), b["normed"], a["activated"], b["activated"])
            sides += (a["grad_gate_rows"], b["grad_gate_rows"], a["grad_up_rows"], b["grad_up_rows"], cotangent)
            first = ffn_weights(far_core, None, *sides)
            first_far = swap(first, "core")
        else:
            h["grad_queries"], grad_pairs = attention_backward(chunks, True, *operands, grad_keys, grad_values)
    dots_far = after(dots_far, grad_pairs)
    for chunks in (late, early):
        h = half[chunks]
        h["grad_gate"], h["gy"], h["dx"], h["p"], h["grad_in"], h["grad_out"], h["sums"] = scan_backward(
            chunks,
            heads,
            h["grad_rows"],
            h["gated"],
            h["square"],
            h["square_far"],
            h["dot"],
            dots_far[:, h["span"]],
            params,
            wide_in,
            h["y"],
            x,
            xb,
            state,
            lag,
            cum_row,
            seg_row,
            select,
        )
    pieces = [b["down"][:LEN], b["down"][LEN:], a["down"][:LEN], a["down"][LEN:]]
    pieces_far = [swap(after(piece, dots_far), "tensor") for piece in pieces[:3]]
    down = jnp.concatenate([a["down"], b["down"]], axis=0)
    ends = []
    for name in ("gy", "dx", "p", "grad_in", "grad_out"):
        ends += [a[name], b[name]]
    grad_conv, grad_state, grad_step, conv_sum, state_sum, step_sum = scan_end(
        heads,
        *ends,
        xb,
        slope,
        state_slope,
        wide_in,
        wide_in,
        step_row,
        sig_row,
        seg_row,
        select,
        params,
        params,
    )

    grads = (a["grad_gate"], b["grad_gate"], grad_conv, a["grad_queries"], b["grad_queries"])
    grads += (grad_state, grad_pairs, grad_step)
    tied = after(normed_input, pieces_far[0], pieces_far[1])
    second_far = swap(mixer_weights(far_core, None, None, tied, *grads), "core")
    *partial_normed, input_gain_sum = normed_back(*grads, wide_proj, small_proj, layer_input)

    smalls = (input_gain_sum, state_sum, step_sum, a["sums"], b["sums"], conv_sum, a["gain_sum"], b["gain_sum"], select)
    shared_end = heads + 6
    spots = [core]
    for name, link in [order[0] for order in ORDERS]:
        at = lax.axis_index(name).astype(jnp.int32)
        side = ((at + 1) // 2) % 2 if link == "A" else at // 2
        spots.append(jnp.stack([side, 3 - side, 1 - side, 2 + side] if link == "A" else [2 * side, 2 * side + 1, 2 - 2 * side, 3 - 2 * side]))
    second = mixer_weights(jnp.concatenate(spots), after(second_far, pieces_far[2]), smalls, normed_input, *grads)
    second = list(second)
    at_state = 2 * width + query_width
    normed_far = [swap(piece, "tensor") for piece in partial_normed]
    second[1] = after(second[1], normed_far[0])
    parts = reduce_rows([(second[2 * k], second[2 * k + 1]) for k in range(4)], (0,))
    parts[0] = after(parts[0], normed_far[1])
    first_own = exchange(after(first_sum, parts[0]), "zh")
    first_all = lax.all_gather(first_own, ("core", "y", "x"), axis=0, tiled=True)
    parts = reduce_rows(parts, (1,))
    parts[0] = after(parts[0], normed_far[2])
    parts = reduce_rows(parts, (2,))
    parts[0] = after(parts[0], normed_far[3])
    parts = reduce_rows(parts, (3,))
    second = jnp.concatenate([p.reshape(32, -1) for p in parts], axis=1)
    both = second[:, at_state:]
    lane = np.arange(both.shape[1])
    in_table = lane - 2 * state_size - pair_width
    is_shared = (lane < 2 * state_size) | ((in_table >= heads) & (in_table < shared_end))
    diagonal = [(0, 3), (3, 0), (1, 2), (2, 1)]
    more = swap(both, "tensor") + lax.ppermute(both, ("zh", "tensor"), diagonal)
    second = exchange(second, "zh")
    summed = second[:, at_state:] + jnp.where(is_shared[None, :], more, 0.0)
    second = jnp.concatenate([second[:, :at_state], summed], axis=1)
    second = after(second, first_all)
    pieces_far.append(swap(after(pieces[3], second), "tensor"))
    second = lax.all_gather(second, ("core", "y", "x"), axis=0, tiled=True)
    grad_mixer_proj, grad_query_proj, grad_keyval, grad_state_proj, step_block = assemble(second, width, query_width)

    def whole(name):
        return jnp.concatenate([a[name], b[name]], axis=0)

    grad_hidden = whole("grad_hidden")
    grad_normed = jnp.concatenate(partial_normed, axis=0) + jnp.concatenate(normed_far, axis=0)
    inv_rms_in = inverse_rms(tokens)
    unit_in = tokens * inv_rms_in
    input_grad = grad_hidden + norm_backward(grad_normed * input_gain, unit_in, inv_rms_in)
    down_far = jnp.concatenate([pieces_far[2], pieces_far[3], pieces_far[0], pieces_far[1]], axis=0)
    layer_output = (whole("hidden") + (down + down_far)).astype(jnp.bfloat16)

    smalls = unpack(heads, width, 2 * state_size, step_block)
    return (
        layer_output,
        input_grad,
        smalls[1],
        grad_mixer_proj,
        grad_state_proj,
        smalls[0].T,
        smalls[4],
        smalls[5],
        smalls[6],
        smalls[7],
        smalls[8],
        smalls[2],
        smalls[3],
        smalls[9],
        first_all[:width, 3 * model_width :],
        grad_query_proj,
        grad_keyval,
        first_all[width:, 3 * model_width :],
        smalls[10],
        first_all[:, :model_width],
        first_all[:, model_width : 2 * model_width],
        first_all[:, 2 * model_width : 3 * model_width],
    )


def solution(mesh):
    dp, whole_spec, columns = P(DP, None), P(), P(None, "tensor")
    per_channel, middle = P("tensor"), P(None, "tensor", None)
    last, by_rows = P(None, None, "tensor"), P("tensor", None)
    weights = (
        whole_spec,
        last,
        whole_spec,
        columns,
        per_channel,
        per_channel,
        per_channel,
        columns,
        per_channel,
        whole_spec,
        whole_spec,
        per_channel,
        by_rows,
        columns,
        middle,
        by_rows,
        whole_spec,
        columns,
        columns,
        by_rows,
    )
    mesh = jax.sharding.Mesh(mesh.devices.reshape(4, 2, 4, 2, 2), (*DP, "tensor"))
    return jax.shard_map(
        on_device, mesh=mesh, in_specs=(dp, dp, *weights, dp), out_specs=(dp, dp, *weights), check_vma=False
    )
```
